32 devices in a mesh: shard: 2 (over z_hi), ctx: 8 (over y, x, core), tensor: 2 (over z_lo).
Axes of the slice: x: 2, y: 2, z: 4 (z_hi: 2, z_lo: 2; z = z_hi * 2 + z_lo), core: 2. Of those that a mesh axis runs over, the one named last changes fastest.
Arguments:
- tokens: bfloat16 [16384, 1024], P(('shard', 'ctx')), may hold values from -6 to 6
- cont_lengths: int32 [2, 8], P('shard'), may hold values from 1 to 1024, 4096 in all within a row
- attn_gain: bfloat16 [1024], P(('shard', 'ctx')), may hold values from 0.099609375 to 1.8984375
- ffn_gain: bfloat16 [1024], P(('shard', 'ctx')), may hold values from 0.099609375 to 1.8984375
- query_gain: bfloat16 [128], P(('shard', 'ctx')), may hold values from 0.5 to 1.59375
- key_gain: bfloat16 [128], P(('shard', 'ctx')), may hold values from 0.5 to 1.59375
- w_query: bfloat16 [1024, 2048], P(('shard', 'ctx'), 'tensor'), may hold values from -0.1875 to 0.1875
- key_weight: bfloat16 [1024, 1024], P(('shard', 'ctx'), 'tensor'), may hold values from -0.1875 to 0.1875
- value_weight: bfloat16 [1024, 1024], P(('shard', 'ctx'), 'tensor'), may hold values from -0.1875 to 0.1875
- w_out: bfloat16 [2048, 1024], P('tensor', ('shard', 'ctx')), may hold values from -1.5 to 1.5
- w_gate: bfloat16 [1024, 3072], P(('shard', 'ctx'), 'tensor'), may hold values from -0.1875 to 0.1875
- w_up: bfloat16 [1024, 3072], P(('shard', 'ctx'), 'tensor'), may hold values from -0.1875 to 0.1875
- w_down: bfloat16 [3072, 1024], P('tensor', ('shard', 'ctx')), may hold values from -0.109375 to 0.109375
- cotangent: bfloat16 [16384, 1024], P(('shard', 'ctx')), may hold values from -6 to 6
Outputs:
- layer_out: bfloat16 [16384, 1024], P(('shard', 'ctx'))
- grad_tokens: bfloat16 [16384, 1024], P(('shard', 'ctx'))
- grad_attn_gain: float32 [1024], P(('shard', 'ctx'))
- grad_ffn_gain: float32 [1024], P(('shard', 'ctx'))
- grad_query_gain: float32 [128], P(('shard', 'ctx'))
- grad_key_gain: float32 [128], P(('shard', 'ctx'))
- grad_w_query: float32 [1024, 2048], P(('shard', 'ctx'), 'tensor')
- grad_w_key: float32 [1024, 1024], P(('shard', 'ctx'), 'tensor')
- grad_w_value: float32 [1024, 1024], P(('shard', 'ctx'), 'tensor')
- grad_w_out: float32 [2048, 1024], P('tensor', ('shard', 'ctx'))
- grad_w_gate: float32 [1024, 3072], P(('shard', 'ctx'), 'tensor')
- grad_w_up: float32 [1024, 3072], P(('shard', 'ctx'), 'tensor')
- grad_w_down: float32 [3072, 1024], P('tensor', ('shard', 'ctx'))
The draws below stay inside these ranges and needn't reach their ends.
Inputs may be any that keep to these rules, and one draw needn't show every extreme that they name: `cont_lengths`: each row holds the lengths of one group's 8 continuations, summing to 4096, the largest exactly 1024.
All inputs are finite; a program needn't handle non-finite values.
Results may differ from the reference program's by a relative error of at most 0.019.
Values may be sent and summed in bfloat16 or wider, within the bound.
No kernel may reach another device: no remote copies, remote signals or barrier semaphores. Data moves between devices by JAX's collectives and lax.ppermute only.
A program may use at most 640 MiB of HBM per device.

```python
import math
import jax
import jax.numpy as jnp
import numpy as np
from jax import lax

MODEL_WIDTH = 1024
HQ = 16
KEY_VALUE_HEADS = 8
HEAD_SIZE = 128
FF = 3072
PROMPT = 4096
CONT_TOK = 4096
CONT_COUNT = 8
GROUPS = 2
TOKENS = 16384
LONGEST = 1024
N_CTX = 8


def spiked(drawn, own_key, source, target, blocks, factor):
    def block_of(dim):
        return (jnp.arange(drawn.shape[dim]) // (drawn.shape[dim] // blocks)).reshape((-1,) + (1,) * (drawn.ndim - 1 - dim))

    first = jax.random.permutation(own_key, blocks)[block_of(target)]
    second = (block_of(target) + blocks // 2) % blocks
    return jnp.where((block_of(source) == first) | (block_of(source) == second), factor * drawn, drawn)


def shard_levels(rng, shape, shards, smallest, largest):
    gain, own = 1.0, jax.random.fold_in(rng, 6)
    for dim, blocks in shards:
        draws = jnp.exp(jax.random.uniform(jax.random.fold_in(own, dim), (blocks,), jnp.float32, smallest / len(shards), largest / len(shards)))
        gain = gain * jnp.repeat(draws, shape[dim] // blocks).reshape([-1 if axis == dim else 1 for axis in range(len(shape))])
    return gain


def length_profile(amount, total, bound, slope):
    portions = [(1 << 20) // math.isqrt(standing ** slope) + 1 for standing in range(2, amount + 1)]
    spare, holding = total - bound - (amount - 1), [1] * (amount - 1)
    while spare > 0:
        movable = [i for i in range(amount - 1) if holding[i] < bound]
        pool, budget = sum([portions[i] for i in movable]), spare
        for i in movable:
            more = min(bound - holding[i], max(1, budget * portions[i] // pool), spare)
            holding[i] = holding[i] + more
            spare = spare - more
    return np.array([bound] + holding)


def uneven_parts(stream_key, count, total, bound, lean):
    if count == 2:
        one = jax.random.randint(stream_key, (), max(1, total - bound), min(bound, total - 1) + 1)
        return jnp.stack([one, total - one])
    sizes = jnp.asarray(length_profile(count, total, bound, lean), jnp.int32)
    pairs = (count - 1) // 2
    giver, receiver = sizes[1:1 + 2 * pairs:2], sizes[2:2 + 2 * pairs:2]
    room = jnp.minimum(giver - 1, bound - receiver)
    shifted = jax.random.randint(jax.random.fold_in(stream_key, 1), (pairs,), 0, 1 << 20) % (room + 1)
    sizes = sizes.at[1:1 + 2 * pairs:2].set(giver - shifted).at[2:2 + 2 * pairs:2].set(receiver + shifted)
    return sizes[jax.random.permutation(jax.random.fold_in(stream_key, 2), count)]


def gaussian(own_key, dims, deviation, limit, cuts=(), kind=jnp.bfloat16):
    drawn = jax.random.normal(own_key, dims, jnp.float32) * deviation
    if len(cuts) > 0:
        drawn = shard_levels(own_key, dims, cuts, -0.22, 0.18) * drawn
    return jnp.clip(drawn, min=-limit, max=limit).astype(kind)


def heavy_noise(own_key, dims, deviation, reach, pieces, heavy, kind=jnp.bfloat16):
    array = deviation * jax.random.normal(own_key, dims, jnp.float32)
    if pieces:
        array = array * shard_levels(own_key, dims, pieces, -0.22, 0.18)
    return jnp.clip(spiked(array, jax.random.fold_in(own_key, 3), *heavy), -reach, reach).astype(kind)


def setup_inputs(seed: int = 0) -> dict:
    streams_of = jax.random.split(jax.random.key(seed), 15)
    tokens = gaussian(streams_of[0], (TOKENS, MODEL_WIDTH), 1.0, 6.0, ((0, 16),))
    cont_lengths = jax.vmap(lambda own: uneven_parts(own, CONT_COUNT, CONT_TOK, LONGEST, 1))(jax.random.split(streams_of[1], GROUPS)).reshape((GROUPS, CONT_COUNT)).astype(jnp.int32)
    attn_gain = jnp.clip(1.0 + 0.18 * jax.random.normal(streams_of[2], (MODEL_WIDTH,), jnp.float32), 0.099609375, 1.8984375).astype(jnp.bfloat16)
    ffn_gain = jnp.clip(1.0 + 0.18 * jax.random.normal(streams_of[3], (MODEL_WIDTH,), jnp.float32), 0.099609375, 1.8984375).astype(jnp.bfloat16)
    query_gain = jnp.clip(0.5 + 1.09375 * jax.random.uniform(streams_of[4], (HEAD_SIZE,), jnp.float32) ** shard_levels(streams_of[4], (HEAD_SIZE,), ((0, 16),), -0.2, 0.2), 0.5, 1.59375).astype(jnp.bfloat16)
    key_gain = jnp.clip(0.5 + 1.09375 * jax.random.uniform(streams_of[5], (HEAD_SIZE,), jnp.float32) ** shard_levels(streams_of[5], (HEAD_SIZE,), ((0, 16),), -0.2, 0.2), 0.5, 1.59375).astype(jnp.bfloat16)
    w_query = gaussian(streams_of[6], (MODEL_WIDTH, HQ * HEAD_SIZE), MODEL_WIDTH ** -0.5, 0.1875, ((0, 16), (1, 2)))
    key_weight = gaussian(streams_of[7], (MODEL_WIDTH, KEY_VALUE_HEADS * HEAD_SIZE), MODEL_WIDTH ** -0.5, 0.1875, ((0, 16), (1, 2)))
    value_weight = gaussian(streams_of[8], (MODEL_WIDTH, KEY_VALUE_HEADS * HEAD_SIZE), MODEL_WIDTH ** -0.5, 0.1875, ((0, 16), (1, 2)))
    w_out = gaussian(streams_of[9], (HQ * HEAD_SIZE, MODEL_WIDTH), 16 ** -0.5, 1.5, ((0, 2), (1, 16)))
    w_gate = gaussian(streams_of[10], (MODEL_WIDTH, FF), MODEL_WIDTH ** -0.5, 0.1875, ((0, 16), (1, 2)))
    w_up = gaussian(streams_of[11], (MODEL_WIDTH, FF), MODEL_WIDTH ** -0.5, 0.1875, ((0, 16), (1, 2)))
    w_down = gaussian(streams_of[12], (FF, MODEL_WIDTH), FF ** -0.5, 0.109375, ((0, 2), (1, 16)))
    cotangent = heavy_noise(streams_of[13], (TOKENS, MODEL_WIDTH), 1.0, 6.0, ((0, 16),), (0, 1, 16, 2.0))
    return {"tokens": tokens, "cont_lengths": cont_lengths, "attn_gain": attn_gain, "ffn_gain": ffn_gain, "query_gain": query_gain, "key_gain": key_gain, "w_query": w_query, "key_weight": key_weight, "value_weight": value_weight, "w_out": w_out, "w_gate": w_gate, "w_up": w_up, "w_down": w_down, "cotangent": cotangent}


EPSILON = 1e-06
ROPE_BASE = 1000000.0
MASKED = -1e+30

@jax.custom_vjp
def low(v):
    return lax.optimization_barrier(v.astype(jnp.bfloat16)).astype(jnp.float32)

@jax.custom_vjp
def low_back(v):
    return v

def low_keep(v):
    return (low(v), None)

def low_pass(kept, grad):
    return (grad,)

def back_keep(v):
    return (v, None)

def back_low(kept, grad):
    return (low(grad),)
low.defvjp(low_keep, low_pass)
low_back.defvjp(back_keep, back_low)

def token_tags(row_ids, lengths, prompt_dev, cont_dev, prompt_len):
    per_dev = prompt_dev + cont_dev
    device = row_ids // per_dev
    offset = row_ids - device * per_dev
    is_prompt = offset < prompt_dev
    cont_at = device * cont_dev + offset - prompt_dev
    cont_ends = jnp.cumsum(lengths)
    seg_num = lax.optimization_barrier(jnp.sum((cont_ends[None, :] <= cont_at[:, None]).astype(jnp.int32), axis=1))
    starts = cont_ends - lengths
    slots = jnp.arange(lengths.shape[0], dtype=jnp.int32)
    picked = lax.optimization_barrier(jnp.sum(jnp.where(slots[None, :] == seg_num[:, None], starts[None, :], 0), axis=1))
    position = jnp.where(is_prompt, device * prompt_dev + offset, prompt_len + cont_at - picked)
    segment = jnp.where(is_prompt, -1, seg_num)
    return (segment.astype(jnp.int32), position.astype(jnp.int32))

def visible(seg_query, pos_query, seg_key, pos_key):
    causal = pos_key[None, :] <= pos_query[:, None]
    same = (seg_key[None, :] < 0) | (seg_key[None, :] == seg_query[:, None])
    return causal & same

def root_mean_gain(values, gain_vec):
    return values * lax.rsqrt(lax.optimization_barrier(jnp.mean(values * values, axis=-1, keepdims=True)) + EPSILON) * gain_vec

def rotary(head_values, position):
    half_dim = head_values.shape[-1] // 2
    inverse_freq = jnp.exp(jnp.arange(half_dim, dtype=jnp.float32) * (-math.log(ROPE_BASE) / half_dim))
    angles = position.astype(jnp.float32)[:, None] * inverse_freq[None, :]
    cosine = jnp.concatenate([jnp.cos(angles), jnp.cos(angles)], axis=-1)[:, None, :]
    sine_table = jnp.concatenate([jnp.sin(angles), jnp.sin(angles)], axis=-1)[:, None, :]
    rotated = jnp.concatenate([-head_values[..., half_dim:], head_values[..., :half_dim]], axis=-1)
    return head_values * cosine + rotated * sine_table

def head_chain(linear, gain_vec, position, head_dim):
    head_values = linear.reshape(linear.shape[0], -1, head_dim)
    return rotary(root_mean_gain(head_values, gain_vec), position)

def matmul(left, right):
    return jnp.dot(left, right, precision=lax.Precision.HIGHEST, preferred_element_type=jnp.float32)

def attention(queries, keys, values, segment, position):
    group_tok = PROMPT + CONT_TOK
    kv_heads = keys.shape[1]
    group_size = queries.shape[2]
    block = math.gcd(group_tok, 512)
    score_scale = 1.0 / math.sqrt(HEAD_SIZE)
    q_groups = queries.reshape(-1, group_tok // block, block, kv_heads, group_size, HEAD_SIZE)
    k_groups = keys.reshape(-1, group_tok, kv_heads, HEAD_SIZE)
    v_groups = values.reshape(-1, group_tok, kv_heads, HEAD_SIZE)
    s_groups = segment.reshape(-1, group_tok // block, block)
    p_groups = position.reshape(-1, group_tok // block, block)
    seg_all = segment.reshape(-1, group_tok)
    pos_all = position.reshape(-1, group_tok)

    def one_group(running, items):
        q_group, k_group, v_group, seg_blocks, pos_blocks, seg_keys, pos_keys = items

        def one_block(parts):
            q_block, seg_block, pos_block = parts
            raw = jnp.einsum('rkgd,nkd->rkgn', q_block, k_group, precision=lax.Precision.HIGHEST)
            scores = low_back(raw * score_scale)
            allowed = visible(seg_block, pos_block, seg_keys, pos_keys)[:, None, None, :]
            scores = jnp.where(allowed, scores, MASKED)
            top = lax.optimization_barrier(jnp.max(scores, axis=-1, keepdims=True))
            expo = jnp.exp(scores - top)
            probabilities = low(expo / lax.optimization_barrier(jnp.sum(expo, axis=-1, keepdims=True)))
            return jnp.einsum('rkgn,nkd->rkgd', probabilities, v_group, precision=lax.Precision.HIGHEST)
        outputs = lax.map(jax.checkpoint(one_block), (q_group, seg_blocks, pos_blocks))
        return (running, outputs.reshape(group_tok, kv_heads * group_size * HEAD_SIZE))
    running, outputs = lax.scan(one_group, jnp.zeros((), jnp.float32), (q_groups, k_groups, v_groups, s_groups, p_groups, seg_all, pos_all))
    return outputs.reshape(-1, kv_heads * group_size * HEAD_SIZE)

def reference(tokens, cont_lengths, attn_gain, ffn_gain, query_gain, key_gain, w_query, key_weight, value_weight, w_out, w_gate, w_up, w_down, cotangent):
    prompt_dev = PROMPT // N_CTX
    cont_dev = CONT_TOK // N_CTX
    group_tok = PROMPT + CONT_TOK

    def tags_for(lengths_row):
        return token_tags(jnp.arange(group_tok, dtype=jnp.int32), lengths_row, prompt_dev, cont_dev, PROMPT)
    segment, position = jax.vmap(tags_for)(cont_lengths)
    segment = segment.reshape(-1)
    position = position.reshape(-1)

    def layer_forward(inputs, gain_one, gain_two, gain_query, gain_key, mat_query, mat_key, mat_value, mat_out, mat_gate, mat_up, mat_down):
        normed = low(root_mean_gain(inputs, gain_one))
        q_linear = low_back(matmul(normed, mat_query))
        k_linear = low_back(matmul(normed, mat_key))
        v_linear = low_back(matmul(normed, mat_value))
        queries = low(head_chain(q_linear, gain_query, position, HEAD_SIZE))
        keys = low(head_chain(k_linear, gain_key, position, HEAD_SIZE))
        values = low(v_linear).reshape(v_linear.shape[0], -1, HEAD_SIZE)
        kv_heads = keys.shape[1]
        queries = queries.reshape(queries.shape[0], kv_heads, -1, HEAD_SIZE)
        attended = attention(queries, keys, values, segment, position)
        attended = low(low_back(attended))
        attn_mixed = low_back(matmul(attended, mat_out))
        residual = inputs + attn_mixed
        normed_ffn = low(root_mean_gain(residual, gain_two))
        gate_proj = low_back(matmul(normed_ffn, mat_gate))
        up_proj = low_back(matmul(normed_ffn, mat_up))
        hidden = low(jax.nn.silu(gate_proj) * up_proj)
        return residual + matmul(hidden, mat_down)
    floats = (tokens.astype(jnp.float32), attn_gain.astype(jnp.float32), ffn_gain.astype(jnp.float32), query_gain.astype(jnp.float32), key_gain.astype(jnp.float32), w_query.astype(jnp.float32), key_weight.astype(jnp.float32), value_weight.astype(jnp.float32), w_out.astype(jnp.float32), w_gate.astype(jnp.float32), w_up.astype(jnp.float32), w_down.astype(jnp.float32))
    layer_out, pullback = jax.vjp(layer_forward, floats[0], floats[1], floats[2], floats[3], floats[4], floats[5], floats[6], floats[7], floats[8], floats[9], floats[10], floats[11])
    grads = pullback(cotangent.astype(jnp.float32))
    return (layer_out.astype(jnp.bfloat16), grads[0].astype(jnp.bfloat16), grads[1], grads[2], grads[3], grads[4], grads[5], grads[6], grads[7], grads[8], grads[9], grads[10], grads[11])
```

```python
import functools
import math

import jax
import jax.numpy as jnp
from jax import lax
from jax.experimental import pallas as pl
from jax.experimental.pallas import tpu as pltpu
from jax.sharding import PartitionSpec as P

HEAD_SIZE = 128
PROMPT = 4096
CONT_TOK = 4096
LONGEST = 1024

EPSILON = 1e-06
ROPE_BASE = 1000000.0
MASKED = -1e30
LOG2E = math.log2(math.e)
LN2 = math.log(2.0)

BF = jnp.bfloat16
F32 = jnp.float32
NN = (((1,), (0,)), ((), ()))
NT = (((1,), (1,)), ((), ()))
TN = (((0,), (0,)), ((), ()))


def mm(left, right, dims=NN):
    return lax.dot_general(left, right, dims, preferred_element_type=F32)


def fwd_kernel(n_slots, n_halo, prompt, cont, idx_ref, q_ref, lo_ref, *refs):
    k_slots, refs = refs[:n_slots], refs[n_slots:]
    v_slots, refs = refs[:n_slots], refs[n_slots:]
    k_halo, refs = refs[:n_halo], refs[n_halo:]
    v_halo, refs = refs[:n_halo], refs[n_halo:]
    out_ref, lse_ref, acc, tot = refs
    me, lo_first = idx_ref[0], idx_ref[1]

    def fold(weights):
        part = weights[:, :128]
        for at in range(128, weights.shape[1], 128):
            part = part + weights[:, at : at + 128]
        return part

    def attend(g, rows, start, k_ref, v_ref, mask=None):
        scores = mm(q_ref[start : start + rows, g * 128 : (g + 1) * 128], k_ref[...], NT)
        if mask is not None:
            scores = jnp.where(mask, scores, MASKED)
        weights = jnp.exp2(scores)
        return mm(weights.astype(BF), v_ref[...]), fold(weights)

    def add(g, rows, start, k_ref, v_ref, mask=None):
        part, total = attend(g, rows, start, k_ref, v_ref, mask)
        acc[g, start : start + rows, :] += part
        tot[g, start : start + rows, :] += total

    row = lax.broadcasted_iota(jnp.int32, (prompt, 1), 0)
    col = lax.broadcasted_iota(jnp.int32, (1, prompt), 1)
    for g in range(2):
        part, total = attend(g, prompt, 0, k_slots[0], v_slots[0], col <= row)
        acc[g, :prompt, :] = part
        tot[g, :prompt, :] = total
    low = lo_ref[:, :1]
    row = lax.broadcasted_iota(jnp.int32, (cont, 1), 0)
    col = lax.broadcasted_iota(jnp.int32, (1, cont), 1)
    mask = (col <= row) & (col >= low)
    for g in range(2):
        part, total = attend(g, cont, prompt, k_halo[0], v_halo[0], mask)
        acc[g, prompt:, :] = part
        tot[g, prompt:, :] = total
    for d in range(1, n_halo):

        @pl.when(lo_first < -(d - 1) * cont)
        def _(d=d):
            for g in range(2):
                add(g, cont, prompt, k_halo[d], v_halo[d], col - d * cont >= low)

    for s in range(1, n_slots):

        @pl.when(jnp.bitwise_xor(me, s) < me)
        def _(s=s):
            for g in range(2):
                add(g, prompt, 0, k_slots[s], v_slots[s])

    for s in range(n_slots):
        for g in range(2):
            add(g, cont, prompt, k_slots[s], v_slots[s])
    for g in range(2):
        total = jnp.sum(tot[g], axis=1, keepdims=True)
        out_ref[:, g * 128 : (g + 1) * 128] = acc[g] / total
        lse_ref[0, g : g + 1, :] = jnp.log2(jnp.sum(tot[g].T, axis=0, keepdims=True))


def attention_forward(me, lo_first, q, low_col, k_slots, v_slots, k_halo, v_halo, prompt, cont):
    rows = q.shape[0]
    heads = k_slots[0].shape[1] // HEAD_SIZE
    n_slots, n_halo = len(k_slots), len(k_halo)
    wide = pl.BlockSpec((rows, 256), lambda h, i: (0, h))
    slot = pl.BlockSpec((prompt, 128), lambda h, i: (0, h))
    halo = pl.BlockSpec((cont, 128), lambda h, i: (0, h))
    low = pl.BlockSpec((cont, 128), lambda h, i: (0, 0))
    pairs = heads * 2 * (rows * prompt * n_slots + cont * cont * n_halo)
    return pl.pallas_call(
        functools.partial(fwd_kernel, n_slots, n_halo, prompt, cont),
        grid_spec=pltpu.PrefetchScalarGridSpec(
            num_scalar_prefetch=1,
            grid=(heads,),
            in_specs=[wide, low] + [slot] * (2 * n_slots) + [halo] * (2 * n_halo),
            out_specs=[wide, pl.BlockSpec((1, 8, rows), lambda h, i: (h, 0, 0))],
            scratch_shapes=[pltpu.VMEM((2, rows, 128), F32), pltpu.VMEM((2, rows, 128), F32)],
        ),
        out_shape=[
            jax.ShapeDtypeStruct((rows, heads * 256), F32),
            jax.ShapeDtypeStruct((heads, 8, rows), F32),
        ],
        compiler_params=pltpu.CompilerParams(vmem_limit_bytes=48 * 2**20),
        cost_estimate=pl.CostEstimate(
            flops=pairs * 512, bytes_accessed=24 * 2**20, transcendentals=pairs
        ),
        name="attention_forward",
    )(jnp.stack([me, lo_first]), q, low_col, *k_slots, *v_slots, *k_halo, *v_halo)


def bwd_kernel(n_slots, n_halo, prompt, cont, idx_ref, q_ref, do_ref, o_ref, lse_ref, lo_ref, *refs):
    k_slots, refs = refs[:n_slots], refs[n_slots:]
    v_slots, refs = refs[:n_slots], refs[n_slots:]
    k_halo, refs = refs[:n_halo], refs[n_halo:]
    v_halo, refs = refs[:n_halo], refs[n_halo:]
    dq_ref, refs = refs[0], refs[1:]
    dk_slots, refs = refs[:n_slots], refs[n_slots:]
    dv_slots, refs = refs[:n_slots], refs[n_slots:]
    dk_halo, refs = refs[:n_halo], refs[n_halo:]
    dv_halo, refs = refs[:n_halo], refs[n_halo:]
    qp, qc, dop, doc, lsep, lsec, delp, delc, dqp, dqc, dk_acc, dv_acc = refs
    me, lo_first = idx_ref[0], idx_ref[1]
    for g in range(2):
        cols = slice(g * 128, (g + 1) * 128)
        at_p, at_c = slice(g * prompt, (g + 1) * prompt), slice(g * cont, (g + 1) * cont)
        qp[at_p, :] = q_ref[:prompt, cols]
        qc[at_c, :] = q_ref[prompt:, cols]
        dop[at_p, :] = do_ref[:prompt, cols]
        doc[at_c, :] = do_ref[prompt:, cols]
        lsep[:, at_p] = lse_ref[0, g : g + 1, :prompt]
        lsec[:, at_c] = lse_ref[0, g : g + 1, prompt:]
        delta = jnp.sum((do_ref[:, cols].astype(F32) * o_ref[:, cols]).T, axis=0, keepdims=True)
        delp[:, at_p] = delta[:, :prompt]
        delc[:, at_c] = delta[:, prompt:]
    dqp[...] = jnp.zeros_like(dqp)
    dqc[...] = jnp.zeros_like(dqc)

    def block(k_ref, v_ref, q, do, lse, delta, dq, mask=None):
        keys = k_ref[...]
        scores = mm(keys, q[...], NT)
        dp = mm(v_ref[...], do[...], NT)
        scores = scores - lse[...]
        if mask is not None:
            scores = jnp.where(mask, scores, MASKED)
        probs = jnp.exp2(scores)
        ds = (probs * (dp - delta[...])).astype(BF)
        dq[...] += mm(keys.T, ds)
        return mm(ds, q[...]), mm(probs.astype(BF), do[...])

    prompt_side = (qp, dop, lsep, delp, dqp)
    cont_side = (qc, doc, lsec, delc, dqc)

    lane = lax.broadcasted_iota(jnp.int32, (1, 2 * cont), 1)
    lane = jnp.where(lane >= cont, lane - cont, lane)
    key = lax.broadcasted_iota(jnp.int32, (cont, 1), 0)
    low = lo_ref[:1, :]
    dk, dv = block(k_halo[0], v_halo[0], *cont_side, (key <= lane) & (key >= low))
    dk_halo[0][...] = (dk * LN2).astype(BF)
    dv_halo[0][...] = dv.astype(BF)
    for d in range(1, n_halo):
        needed = lo_first < -(d - 1) * cont

        @pl.when(needed)
        def _(d=d):
            dk, dv = block(k_halo[d], v_halo[d], *cont_side, key - d * cont >= low)
            dk_halo[d][...] = (dk * LN2).astype(BF)
            dv_halo[d][...] = dv.astype(BF)

        @pl.when(jnp.logical_not(needed))
        def _(d=d):
            dk_halo[d][...] = jnp.zeros_like(dk_halo[d])
            dv_halo[d][...] = jnp.zeros_like(dv_halo[d])

    lane = lax.broadcasted_iota(jnp.int32, (1, 2 * prompt), 1)
    lane = jnp.where(lane >= prompt, lane - prompt, lane)
    key = lax.broadcasted_iota(jnp.int32, (prompt, 1), 0)
    for s in range(n_slots):
        dk, dv = block(k_slots[s], v_slots[s], *cont_side)
        dk_acc[...] = dk
        dv_acc[...] = dv
        if s == 0:
            dk, dv = block(k_slots[s], v_slots[s], *prompt_side, key <= lane)
            dk_acc[...] += dk
            dv_acc[...] += dv
        else:

            @pl.when(jnp.bitwise_xor(me, s) < me)
            def _(s=s):
                dk, dv = block(k_slots[s], v_slots[s], *prompt_side)
                dk_acc[...] += dk
                dv_acc[...] += dv

        dk_slots[s][...] = (dk_acc[...] * LN2).astype(BF)
        dv_slots[s][...] = dv_acc[...].astype(BF)
    scale = 1.0 / math.sqrt(HEAD_SIZE)
    for g in range(2):
        cols = slice(g * 128, (g + 1) * 128)
        dq_ref[:prompt, cols] = dqp[:, g * prompt : (g + 1) * prompt].T * scale
        dq_ref[prompt:, cols] = dqc[:, g * cont : (g + 1) * cont].T * scale


def attention_backward(
    me, lo_first, q, do, out, lse, low_row, k_slots, v_slots, k_halo, v_halo, prompt, cont
):
    rows = q.shape[0]
    heads = k_slots[0].shape[1] // HEAD_SIZE
    n_slots, n_halo = len(k_slots), len(k_halo)
    wide = pl.BlockSpec((rows, 256), lambda h, i: (0, h))
    slot = pl.BlockSpec((prompt, 128), lambda h, i: (0, h))
    halo = pl.BlockSpec((cont, 128), lambda h, i: (0, h))
    low = pl.BlockSpec((8, 2 * cont), lambda h, i: (0, 0))
    pairs = heads * 2 * (rows * prompt * n_slots + cont * cont * n_halo)
    results = pl.pallas_call(
        functools.partial(bwd_kernel, n_slots, n_halo, prompt, cont),
        grid_spec=pltpu.PrefetchScalarGridSpec(
            num_scalar_prefetch=1,
            grid=(heads,),
            in_specs=[wide, wide, wide, pl.BlockSpec((1, 8, rows), lambda h, i: (h, 0, 0)), low]
            + [slot] * (2 * n_slots)
            + [halo] * (2 * n_halo),
            out_specs=[wide] + [slot] * (2 * n_slots) + [halo] * (2 * n_halo),
            scratch_shapes=[
                pltpu.VMEM((2 * prompt, 128), BF),
                pltpu.VMEM((2 * cont, 128), BF),
                pltpu.VMEM((2 * prompt, 128), BF),
                pltpu.VMEM((2 * cont, 128), BF),
                pltpu.VMEM((1, 2 * prompt), F32),
                pltpu.VMEM((1, 2 * cont), F32),
                pltpu.VMEM((1, 2 * prompt), F32),
                pltpu.VMEM((1, 2 * cont), F32),
                pltpu.VMEM((128, 2 * prompt), F32),
                pltpu.VMEM((128, 2 * cont), F32),
                pltpu.VMEM((prompt, 128), F32),
                pltpu.VMEM((prompt, 128), F32),
            ],
        ),
        out_shape=[jax.ShapeDtypeStruct((rows, heads * 256), F32)]
        + [jax.ShapeDtypeStruct((prompt, heads * 128), BF)] * (2 * n_slots)
        + [jax.ShapeDtypeStruct((cont, heads * 128), BF)] * (2 * n_halo),
        compiler_params=pltpu.CompilerParams(vmem_limit_bytes=52 * 2**20),
        cost_estimate=pl.CostEstimate(
            flops=pairs * 1280, bytes_accessed=40 * 2**20, transcendentals=pairs
        ),
        name="attention_backward",
    )(jnp.stack([me, lo_first]), q, do, out, lse, low_row, *k_slots, *v_slots, *k_halo, *v_halo)
    dq, results = results[0], results[1:]
    dk_slots, results = results[:n_slots], results[n_slots:]
    dv_slots, results = results[:n_slots], results[n_slots:]
    return dq, dk_slots, dv_slots, results[:n_halo], results[n_halo:]


def swap(value, axis, bit):
    size = lax.axis_size(axis)
    return lax.ppermute(value, axis, [(i, i ^ bit) for i in range(size)])


def add_low(left, right):
    return (left.astype(F32) + right.astype(F32)).astype(BF)


def gather_slots(keys, values):
    size = lax.axis_size("ctx")
    if size != 8:
        both = jnp.stack([keys, values])[None]
        bit = 1
        while bit < size:
            both = jnp.concatenate([both, swap(both, "ctx", bit)])
            bit *= 2
        return [both[s, 0] for s in range(size)], [both[s, 1] for s in range(size)]
    k, v = [None] * 8, [None] * 8
    k[0], v[0] = keys, values
    k[2], v[2] = swap(keys, "ctx", 2), swap(values, "ctx", 2)
    k[4], v[4] = swap(keys, "ctx", 4), swap(values, "ctx", 4)
    k[6], v[6] = swap(k[4], "ctx", 2), swap(v[2], "ctx", 4)
    for s in (0, 2, 4, 6):
        k[s + 1], v[s + 1] = swap(k[s], "ctx", 1), swap(v[s], "ctx", 1)
    return k, v


def scatter_slots(k, v):
    size = lax.axis_size("ctx")
    if size != 8:
        both = jnp.stack([jnp.stack(k), jnp.stack(v)], axis=1)
        while both.shape[0] > 1:
            half = both.shape[0] // 2
            both = add_low(both[:half], swap(both[half:], "ctx", half))
        return both[0, 0], both[0, 1]
    k, v = list(k), list(v)
    for s in (6, 4, 2, 0):
        k[s] = add_low(k[s], swap(k[s + 1], "ctx", 1))
        v[s] = add_low(v[s], swap(v[s + 1], "ctx", 1))
    k[4] = add_low(k[4], swap(k[6], "ctx", 2))
    v[2] = add_low(v[2], swap(v[6], "ctx", 4))
    k2, v2 = swap(k[2], "ctx", 2), swap(v[2], "ctx", 2)
    k4, v4 = swap(k[4], "ctx", 4), swap(v[4], "ctx", 4)
    dk = k[0].astype(F32) + k2.astype(F32) + k4.astype(F32)
    dv = v[0].astype(F32) + v2.astype(F32) + v4.astype(F32)
    return dk, dv


def shift(value, by):
    size = lax.axis_size("ctx")
    return lax.ppermute(value, "ctx", [(i, i + by) for i in range(size) if 0 <= i + by < size])


def exchange(part):
    low = part.astype(BF)
    return low.astype(F32) + swap(low, "tensor", 1).astype(F32)


def butterfly(value, axes):
    for axis in axes:
        bit = 1
        while bit < lax.axis_size(axis):
            value = value + swap(value, axis, bit)
            bit *= 2
    return value


def root_mean_gain(values, gain_vec):
    return (
        values * lax.rsqrt(jnp.mean(values * values, axis=-1, keepdims=True) + EPSILON) * gain_vec
    )


def rotary_tables(position):
    half_dim = HEAD_SIZE // 2
    inverse_freq = jnp.exp(
        jnp.arange(half_dim, dtype=F32) * (-math.log(ROPE_BASE) / half_dim)
    )
    angles = position.astype(F32)[:, None] * inverse_freq[None, :]
    cosine, sine = jnp.cos(angles), jnp.sin(angles)
    return (
        jnp.concatenate([cosine, cosine], axis=-1)[:, None, :],
        jnp.concatenate([sine, sine], axis=-1)[:, None, :],
    )


def rotary(head_values, tables):
    cosine, sine = tables
    half_dim = head_values.shape[-1] // 2
    rotated = jnp.concatenate([-head_values[..., half_dim:], head_values[..., :half_dim]], axis=-1)
    return head_values * cosine + rotated * sine


def swiglu(gate_in, up_in):
    return jax.nn.silu(gate_in) * up_in


def body(
    tokens,
    cont_lengths,
    attn_gain,
    ffn_gain,
    query_gain,
    key_gain,
    w_query,
    key_weight,
    value_weight,
    w_out,
    w_gate,
    w_up,
    w_down,
    cotangent,
):
    ctx_size = lax.axis_size("ctx")
    weight_axes = ("shard", "ctx")
    parts = lax.axis_size("shard") * ctx_size
    me = lax.axis_index("ctx")
    part = lax.axis_index("shard") * ctx_size + me
    prompt_dev = PROMPT // ctx_size
    cont_dev = CONT_TOK // ctx_size
    rows = tokens.shape[0]
    n_halo = 1 + -(-(LONGEST - 1) // cont_dev)
    lengths = cont_lengths[0]

    cont_at = me * cont_dev + jnp.arange(cont_dev, dtype=jnp.int32)
    cont_ends = jnp.cumsum(lengths)
    starts = cont_ends - lengths
    seg = jnp.sum((cont_ends[None, :] <= cont_at[:, None]).astype(jnp.int32), axis=1)
    slots = jnp.arange(lengths.shape[0], dtype=jnp.int32)
    first = jnp.sum(jnp.where(slots[None, :] == seg[:, None], starts[None, :], 0), axis=1)
    position = jnp.concatenate(
        [me * prompt_dev + jnp.arange(prompt_dev, dtype=jnp.int32), PROMPT + cont_at - first]
    )
    low = first - me * cont_dev
    low_col = jnp.broadcast_to(low[:, None], (cont_dev, 128))
    low_row = jnp.broadcast_to(jnp.concatenate([low, low])[None, :], (8, 2 * cont_dev))
    lo_first = low[0]
    tables = rotary_tables(position)

    gains = jnp.concatenate([attn_gain, ffn_gain, query_gain, key_gain])[None]
    spread = jnp.where(jnp.arange(parts)[:, None] == part, gains, jnp.zeros((), BF))
    gains = butterfly(spread, ("ctx", "shard"))
    wide, narrow = attn_gain.shape[0], query_gain.shape[0]
    full_attn_gain = gains[:, :wide].reshape(-1).astype(F32)
    full_ffn_gain = gains[:, wide : 2 * wide].reshape(-1).astype(F32)
    full_query_gain = gains[:, 2 * wide : 2 * wide + narrow].reshape(-1).astype(F32)
    full_key_gain = gains[:, 2 * wide + narrow :].reshape(-1).astype(F32)
    q_cols, k_cols = w_query.shape[1], key_weight.shape[1]
    w_qkv = lax.all_gather(
        jnp.concatenate([w_query, key_weight, value_weight], axis=1), weight_axes, axis=0, tiled=True
    )
    o_cols, f_cols = w_out.shape[0], w_gate.shape[1]
    w_rest = lax.all_gather(
        jnp.concatenate([w_out.T, w_gate, w_up, w_down.T], axis=1), weight_axes, axis=0, tiled=True
    )
    full_q, full_k, full_v = (
        w_qkv[:, :q_cols],
        w_qkv[:, q_cols : q_cols + k_cols],
        w_qkv[:, q_cols + k_cols :],
    )
    out_t, full_gate, full_up, down_t = (
        w_rest[:, :o_cols],
        w_rest[:, o_cols : o_cols + f_cols],
        w_rest[:, o_cols + f_cols : o_cols + 2 * f_cols],
        w_rest[:, o_cols + 2 * f_cols :],
    )

    fold = LOG2E / math.sqrt(HEAD_SIZE)

    def query_chain(linear, gain_vec):
        return rotary(root_mean_gain(linear.reshape(rows, -1, HEAD_SIZE), gain_vec), tables)

    inputs = tokens.astype(F32)
    normed_f, norm_one_back = jax.vjp(root_mean_gain, inputs, full_attn_gain)
    normed = normed_f.astype(BF)
    k_linear = mm(normed, full_k)
    v_linear = mm(normed, full_v)
    q_linear = mm(normed, full_q)
    key_f, key_back = jax.vjp(query_chain, k_linear, full_key_gain)
    query_f, query_back = jax.vjp(query_chain, q_linear, full_query_gain)
    keys = key_f.astype(BF).reshape(rows, -1)
    values = v_linear.astype(BF)
    queries = (query_f * fold).astype(BF).reshape(rows, -1)
    k_slots, v_slots = gather_slots(keys[:prompt_dev], values[:prompt_dev])
    k_own, v_own = keys[prompt_dev:], values[prompt_dev:]
    if n_halo == 3:
        odd = (me % 2) == 1
        k2, v2 = shift(k_own, 2), shift(v_own, 2)
        k1 = swap(jnp.where(odd, k2, k_own), "ctx", 1)
        v1 = swap(jnp.where(odd, v2, v_own), "ctx", 1)
        k_halo, v_halo = [k_own, k1, k2], [v_own, v1, v2]
    else:
        k_halo = [k_own] + [shift(k_own, d) for d in range(1, n_halo)]
        v_halo = [v_own] + [shift(v_own, d) for d in range(1, n_halo)]
    attended, lse = attention_forward(
        me, lo_first, queries, low_col, k_slots, v_slots, k_halo, v_halo, prompt_dev, cont_dev
    )
    attended_low = attended.astype(BF)
    residual = inputs + exchange(mm(attended_low, out_t, NT))
    normed_ffn_f, norm_two_back = jax.vjp(root_mean_gain, residual, full_ffn_gain)
    normed_ffn = normed_ffn_f.astype(BF)
    gate_proj = mm(normed_ffn, full_gate)
    up_proj = mm(normed_ffn, full_up)
    hidden_f, swiglu_back = jax.vjp(swiglu, gate_proj, up_proj)
    hidden = hidden_f.astype(BF)
    layer_out = (residual + exchange(mm(hidden, down_t, NT))).astype(BF)

    grad_hidden = mm(cotangent, down_t)
    grad_gate_f, grad_up_f = swiglu_back(grad_hidden)
    grad_gate, grad_upper = grad_gate_f.astype(BF), grad_up_f.astype(BF)
    grad_normed_ffn = exchange(mm(grad_gate, full_gate, NT) + mm(grad_upper, full_up, NT))
    grad_resid_norm, grad_ffn_gain_local = norm_two_back(grad_normed_ffn)
    grad_resid = cotangent.astype(F32) + grad_resid_norm
    grad_mixed = grad_resid.astype(BF)
    grad_attended = mm(grad_mixed, out_t).astype(BF)
    rest_grads = jnp.concatenate(
        [
            mm(grad_mixed, attended_low, TN).astype(BF),
            mm(normed_ffn, grad_gate, TN).astype(BF),
            mm(normed_ffn, grad_upper, TN).astype(BF),
            mm(cotangent, hidden, TN).astype(BF),
        ],
        axis=1,
    )
    rest_share = lax.psum_scatter(rest_grads, weight_axes, scatter_dimension=0, tiled=True)

    grad_query, dk_slots, dv_slots, dk_halo, dv_halo = attention_backward(
        me, lo_first, queries, grad_attended, attended, lse, low_row,
        k_slots, v_slots, k_halo, v_halo, prompt_dev, cont_dev,
    )
    dk_prompt, dv_prompt = scatter_slots(dk_slots, dv_slots)
    if n_halo == 3:
        k1, v1 = swap(dk_halo[1], "ctx", 1), swap(dv_halo[1], "ctx", 1)
        zero = jnp.zeros((), BF)
        k2 = shift(add_low(dk_halo[2], jnp.where(odd, k1, zero)), -2)
        v2 = shift(add_low(dv_halo[2], jnp.where(odd, v1, zero)), -2)
        dk_cont = dk_halo[0].astype(F32) + jnp.where(odd, zero, k1).astype(F32) + k2.astype(F32)
        dv_cont = dv_halo[0].astype(F32) + jnp.where(odd, zero, v1).astype(F32) + v2.astype(F32)
    else:
        dk_cont, dv_cont = dk_halo[0].astype(F32), dv_halo[0].astype(F32)
        for d in range(1, n_halo):
            dk_cont = dk_cont + shift(dk_halo[d], -d).astype(F32)
            dv_cont = dv_cont + shift(dv_halo[d], -d).astype(F32)
    grad_key = jnp.concatenate([dk_prompt.astype(F32), dk_cont])
    grad_value = jnp.concatenate([dv_prompt.astype(F32), dv_cont])
    grad_q_linear, grad_query_gain_part = query_back(grad_query.reshape(rows, -1, HEAD_SIZE))
    grad_k_linear, grad_key_gain_part = key_back(grad_key.reshape(rows, -1, HEAD_SIZE))
    grad_qkv = jnp.concatenate(
        [grad_q_linear.astype(BF), grad_k_linear.astype(BF), grad_value.astype(BF)], axis=1
    )
    grad_normed = exchange(mm(grad_qkv, w_qkv, NT))
    qkv_share = lax.psum_scatter(
        mm(normed, grad_qkv, TN).astype(BF), weight_axes, scatter_dimension=0, tiled=True
    )
    grad_inputs_norm, grad_attn_gain_local = norm_one_back(grad_normed)
    grad_tokens = (grad_resid + grad_inputs_norm).astype(BF)
    model_gains = jnp.concatenate([grad_attn_gain_local, grad_ffn_gain_local])
    model_gains = butterfly(model_gains, ("ctx", "shard")).reshape(2, parts, wide)
    head_gains = jnp.concatenate([grad_query_gain_part, grad_key_gain_part])
    head_gains = butterfly(head_gains, ("ctx", "shard", "tensor")).reshape(2, parts, narrow)
    model_gains = lax.dynamic_index_in_dim(model_gains, part, 1, keepdims=False)
    head_gains = lax.dynamic_index_in_dim(head_gains, part, 1, keepdims=False)
    qkv_share = qkv_share.astype(F32)
    rest_share = rest_share.astype(F32)
    return (
        layer_out,
        grad_tokens,
        model_gains[0],
        model_gains[1],
        head_gains[0],
        head_gains[1],
        qkv_share[:, :q_cols],
        qkv_share[:, q_cols : q_cols + k_cols],
        qkv_share[:, q_cols + k_cols :],
        rest_share[:, :o_cols].T,
        rest_share[:, o_cols : o_cols + f_cols],
        rest_share[:, o_cols + f_cols : o_cols + 2 * f_cols],
        rest_share[:, o_cols + 2 * f_cols :].T,
    )


def solution(mesh):
    split = ("shard", "ctx")
    rows, gain = P(split, None), P(split)
    into, out_of = P(split, "tensor"), P("tensor", split)
    in_specs = (rows, P("shard", None)) + (gain,) * 4 + (into,) * 3 + (out_of,)
    in_specs += (into, into, out_of, rows)
    out_specs = (rows, rows) + (gain,) * 4 + (into,) * 3 + (out_of, into, into, out_of)
    return jax.shard_map(body, mesh=mesh, in_specs=in_specs, out_specs=out_specs, check_vma=False)
```

```python
import functools
import math

import jax
import jax.numpy as jnp
from jax import lax
from jax.experimental import pallas as pl
from jax.experimental.pallas import tpu as pltpu
from jax.sharding import PartitionSpec as P

HEAD_SIZE = 128
PROMPT = 4096
CONT_TOK = 4096
LONGEST = 1024

EPSILON = 1e-06
ROPE_BASE = 1000000.0
MASKED = -1e30
LOG2E = math.log2(math.e)
LN2 = math.log(2.0)
SCALE = 1.0 / math.sqrt(HEAD_SIZE)

BF = jnp.bfloat16
F32 = jnp.float32
NN = (((1,), (0,)), ((), ()))
NT = (((1,), (1,)), ((), ()))
TN = (((0,), (0,)), ((), ()))
MIB = 2**20


def mm(left, right, dims=NN):
    return lax.dot_general(left, right, dims, preferred_element_type=F32)


def shaped(dims, kind):
    return jax.ShapeDtypeStruct(dims, kind)


def call(kernel, name, grid, ins, outs, scratch=(), vmem=56, flops=0, moved=0, scalars=None, keep=None):
    in_specs, arrays = [], []
    for array, block, index in ins:
        arrays.append(array)
        in_specs.append(pl.BlockSpec(memory_space=pl.ANY) if block is None else pl.BlockSpec(block, index))
    lead = 0 if scalars is None else 1
    return pl.pallas_call(
        kernel,
        grid_spec=pltpu.PrefetchScalarGridSpec(
            num_scalar_prefetch=lead,
            grid=grid,
            in_specs=in_specs,
            out_specs=[pl.BlockSpec(block, index) for _, block, index in outs],
            scratch_shapes=list(scratch),
        ),
        out_shape=[shape for shape, _, _ in outs],
        input_output_aliases={a + lead: b for a, b in (keep or {}).items()},
        compiler_params=pltpu.CompilerParams(vmem_limit_bytes=vmem * MIB),
        cost_estimate=pl.CostEstimate(flops=flops, bytes_accessed=moved, transcendentals=0),
        name=name,
    )(*([] if scalars is None else [scalars]), *arrays)


def rms(values):
    return lax.rsqrt(jnp.mean(values * values, axis=-1, keepdims=True) + EPSILON)


def turn(values, cos, sin):
    return values * cos + pltpu.roll(values, HEAD_SIZE // 2, 1) * sin


def turn_back(values, cos, sin):
    return values * cos - pltpu.roll(values, HEAD_SIZE // 2, 1) * sin


def kv_kernel(heads, x_ref, gain_ref, w_ref, hgain_ref, cos_ref, sin_ref, *refs):
    normed_ref, kv_ref, lin_ref = refs[-3:]
    x = x_ref[...].astype(F32)
    normed_ref[...] = (x * rms(x) * gain_ref[...]).astype(BF)
    both = mm(normed_ref[...], w_ref[...])
    width = heads * HEAD_SIZE
    kv_ref[1] = both[:, width:].astype(BF)
    for h in range(heads):
        cols = slice(h * HEAD_SIZE, (h + 1) * HEAD_SIZE)
        lin = both[:, cols]
        lin_ref[:, cols] = lin
        kv_ref[0, :, cols] = turn(lin * rms(lin) * hgain_ref[...], cos_ref[...], sin_ref[...]).astype(BF)


def q_kernel(heads, normed_ref, w_ref, hgain_ref, cos_ref, sin_ref, q_ref, lin_ref):
    both = mm(normed_ref[...], w_ref[...])
    for h in range(heads):
        cols = slice(h * HEAD_SIZE, (h + 1) * HEAD_SIZE)
        lin = both[:, cols]
        lin_ref[:, cols] = lin
        turned = turn(lin * rms(lin) * hgain_ref[...], cos_ref[...], sin_ref[...])
        q_ref[:, cols] = (turned * (SCALE * LOG2E)).astype(BF)


def fwd_kernel(plan, idx_ref, q_ref, lo_ref, *refs):
    half, slots, halos = plan["half"], plan["slots"], plan["halos"]
    refs = list(refs)
    slot_refs = [refs.pop(0) for _ in slots]
    halo_refs = [refs.pop(0) for _ in halos]
    prior = [refs.pop(0) for _ in range(2)] if plan["carry"] else None
    if plan["last"]:
        w_ref = refs.pop(0)
        if plan["alias"]:
            refs.pop(0)
        out_ref, lse_ref, part_ref, acc, tot, part_acc = refs
    else:
        acc, tot = refs
    me, lo_first = idx_ref[0], idx_ref[1]
    rows = q_ref.shape[0]
    if prior is None:
        acc[...] = jnp.zeros_like(acc)
        tot[...] = jnp.zeros_like(tot)
    else:
        acc[...] = prior[0][...]
        tot[...] = prior[1][...]

    def add(kv_ref, mask=None):
        for g in range(2):
            cols = slice(g * HEAD_SIZE, (g + 1) * HEAD_SIZE)
            scores = mm(q_ref[:, cols], kv_ref[0], NT)
            if mask is not None:
                scores = jnp.where(mask, scores, MASKED)
            weights = jnp.exp2(scores)
            total = weights[:, :128]
            for at in range(128, weights.shape[1], 128):
                total = total + weights[:, at : at + 128]
            acc[:, cols] += mm(weights.astype(BF), kv_ref[1])
            tot[:, cols] += total

    row = lax.broadcasted_iota(jnp.int32, (rows, 1), 0)
    col = lax.broadcasted_iota(jnp.int32, (1, rows), 1)
    for d, kv_ref in zip(halos, halo_refs):
        low = lo_ref[:, :1]
        if d == 0:
            add(kv_ref, (col <= row) & (col >= low))
        else:

            @pl.when(lo_first < -(d - 1) * rows)
            def _(d=d, kv_ref=kv_ref, low=low):
                add(kv_ref, col - d * rows >= low)

    for s, kv_ref in zip(slots, slot_refs):
        if half == 1:
            add(kv_ref)
        elif s == 0:
            add(kv_ref, col <= row)
        else:

            @pl.when(jnp.bitwise_xor(me, s) < me)
            def _(kv_ref=kv_ref):
                add(kv_ref)

    if plan["last"]:
        step, steps = pl.program_id(0), pl.num_programs(0)
        for g in range(2):
            cols = slice(g * HEAD_SIZE, (g + 1) * HEAD_SIZE)
            total = jnp.sum(tot[:, cols], axis=1, keepdims=True)
            out_ref[:, cols] = (acc[:, cols] / total).astype(BF)
            lse_ref[0, g : g + 1, :] = jnp.log2(jnp.sum(tot[:, cols].T, axis=0, keepdims=True))
        part = mm(out_ref[...], w_ref[...], NT)

        @pl.when(step == 0)
        def _():
            part_acc[...] = part

        @pl.when(step > 0)
        def _():
            part_acc[...] += part

        @pl.when(step == steps - 1)
        def _():
            part_ref[...] = part_acc[...].astype(BF)


def attention_forward(half, scalars, q, low, slots, halos, carry=None, last=None):
    rows, heads = q.shape[0] // 2, q.shape[1] // 256
    plan = dict(half=half, slots=list(slots), halos=list(halos), carry=carry is not None,
                last=last is not None, alias=last is not None and last[1] is not None)
    mine = lambda h, i: (half, h)
    part = lambda h, i: (0, h)
    ins = [(q, (rows, 256), mine), (low, (rows, 128), lambda h, i: (0, 0))]
    for kv in list(slots.values()) + list(halos.values()):
        ins.append((kv, (2, rows, 128), lambda h, i: (0, 0, h)))
    if carry is not None:
        ins += [(c, (rows, 256), part) for c in carry]
    scratch, keep = [], {}
    state = shaped((rows, heads * 256), F32)
    if last is None:
        outs = [(state, (rows, 256), part)] * 2
    else:
        w_rest, other = last
        model = w_rest.shape[0]
        ins.append((w_rest, (model, 256), part))
        if other is not None:
            keep = {len(ins): 0}
            ins.append((other, None, None))
        outs = [
            (shaped((2 * rows, heads * 256), BF), (rows, 256), mine),
            (shaped((heads, 8, rows), F32), (1, 8, rows), lambda h, i: (h, 0, 0)),
            (shaped((rows, model), BF), (rows, model), lambda h, i: (0, 0)),
        ]
        scratch = [pltpu.VMEM((rows, 256), F32)] * 2 + [pltpu.VMEM((rows, model), F32)]
    blocks = len(slots) * (2 if half else 1) + len(halos)
    pairs = heads * rows * rows * blocks
    return call(functools.partial(fwd_kernel, plan), "attend", (heads,), ins, outs, scratch,
                flops=pairs * 1024, moved=8 * MIB, scalars=scalars, keep=keep)


def bwd_kernel(plan, idx_ref, q_ref, do_ref, lse_ref, delta_ref, lo_ref, *refs):
    half, slots, halos = plan["half"], plan["slots"], plan["halos"]
    refs = list(refs)
    slot_refs = [refs.pop(0) for _ in slots]
    halo_refs = [refs.pop(0) for _ in halos]
    prior_dq = refs.pop(0) if plan["carry"] else None
    prior = [refs.pop(0) for _ in slots] if plan["sum"] else None
    dq_ref = refs.pop(0)
    slot_outs = [refs.pop(0) for _ in slots]
    halo_outs = [refs.pop(0) for _ in halos]
    qs, dos, lses, deltas, dq = refs
    me, lo_first = idx_ref[0], idx_ref[1]
    rows = q_ref.shape[0]
    for g in range(2):
        cols, at = slice(g * HEAD_SIZE, (g + 1) * HEAD_SIZE), slice(g * rows, (g + 1) * rows)
        qs[at, :] = q_ref[:, cols]
        dos[at, :] = do_ref[:, cols]
        lses[:, at] = lse_ref[0, g : g + 1, :]
        deltas[:, at] = delta_ref[0, g : g + 1, :]
    dq[...] = jnp.zeros_like(dq) if prior_dq is None else prior_dq[...]

    def block(kv_ref, out_ref, mask=None, before=None):
        keys = kv_ref[0]
        scores = mm(keys, qs[...], NT)
        dp = mm(kv_ref[1], dos[...], NT)
        scores = scores - lses[...]
        if mask is not None:
            scores = jnp.where(mask, scores, MASKED)
        probs = jnp.exp2(scores)
        ds = (probs * (dp - deltas[...])).astype(BF)
        dq[...] += mm(keys.T, ds)
        dk, dv = mm(ds, qs[...]) * LN2, mm(probs.astype(BF), dos[...])
        if before is not None:
            dk, dv = dk + before[0].astype(F32), dv + before[1].astype(F32)
        out_ref[0] = dk.astype(BF)
        out_ref[1] = dv.astype(BF)

    lane = lax.broadcasted_iota(jnp.int32, (1, 2 * rows), 1)
    lane = jnp.where(lane >= rows, lane - rows, lane)
    key = lax.broadcasted_iota(jnp.int32, (rows, 1), 0)

    def when(needed, kv_ref, out_ref, mask=None):
        @pl.when(needed)
        def _():
            block(kv_ref, out_ref, mask)

        @pl.when(jnp.logical_not(needed))
        def _():
            out_ref[...] = jnp.zeros_like(out_ref)

    low = lo_ref[:1, :]
    for d, kv_ref, out_ref in zip(halos, halo_refs, halo_outs):
        if d == 0:
            block(kv_ref, out_ref, (key <= lane) & (key >= low))
        else:
            when(lo_first < -(d - 1) * rows, kv_ref, out_ref, key - d * rows >= low)
    for at, (s, kv_ref, out_ref) in enumerate(zip(slots, slot_refs, slot_outs)):
        if half == 1:
            block(kv_ref, out_ref, None, prior[at])
        elif s == 0:
            block(kv_ref, out_ref, key <= lane)
        else:
            when(jnp.bitwise_xor(me, s) < me, kv_ref, out_ref)
    if plan["last"]:
        for g in range(2):
            cols = slice(g * HEAD_SIZE, (g + 1) * HEAD_SIZE)
            dq_ref[:, cols] = dq[:, g * rows : (g + 1) * rows].T * SCALE
    else:
        dq_ref[...] = dq[...]


def attention_backward(half, scalars, q, do, lse, delta, low, slots, halos, carry=None, prior=None, last=True):
    rows, heads = q.shape[0] // 2, q.shape[1] // 256
    plan = dict(half=half, slots=list(slots), halos=list(halos), carry=carry is not None,
                sum=prior is not None, last=last)
    part = lambda h, i: (0, h)
    stat = lambda h, i: (h, 0, 0)
    kv_map = lambda h, i: (0, 0, h)
    ins = [
        (q, (rows, 256), lambda h, i: (half, h)),
        (do, (rows, 256), part),
        (lse, (1, 8, rows), stat),
        (delta, (1, 8, rows), stat),
        (low, (8, 2 * rows), lambda h, i: (0, 0)),
    ]
    pieces = list(slots.values()) + list(halos.values())
    ins += [(kv, (2, rows, 128), kv_map) for kv in pieces]
    if carry is not None:
        ins.append((carry, (128, 2 * rows), lambda h, i: (h, 0)))
    if prior is not None:
        ins += [(prior[s], (2, rows, 128), kv_map) for s in slots]
    if last:
        outs = [(shaped((rows, heads * 256), F32), (rows, 256), part)]
    else:
        outs = [(shaped((heads * 128, 2 * rows), F32), (128, 2 * rows), lambda h, i: (h, 0))]
    outs += [(shaped(kv.shape, BF), (2, rows, 128), kv_map) for kv in pieces]
    scratch = [
        pltpu.VMEM((2 * rows, 128), BF),
        pltpu.VMEM((2 * rows, 128), BF),
        pltpu.VMEM((1, 2 * rows), F32),
        pltpu.VMEM((1, 2 * rows), F32),
        pltpu.VMEM((128, 2 * rows), F32),
    ]
    blocks = len(slots) * (2 if half else 1) + len(halos)
    pairs = heads * rows * rows * blocks
    results = call(functools.partial(bwd_kernel, plan), "attend_back", (heads,), ins, outs, scratch,
                   flops=pairs * 2560, moved=8 * MIB, scalars=scalars)
    n = len(slots)
    return results[0], dict(zip(slots, results[1 : 1 + n])), dict(zip(halos, results[1 + n :]))


def ffn_kernel(x_ref, own_ref, got_ref, gain_ref, dy_ref, gu_ref, down_ref, *refs):
    resid_ref, normed_ref, hidden_ref, dgu_ref, out_ref, back_ref, normed, out_acc, back_acc = refs[-9:]
    step, steps = pl.program_id(0), pl.num_programs(0)

    @pl.when(step == 0)
    def _():
        resid = x_ref[...].astype(F32) + (own_ref[...].astype(F32) + got_ref[...].astype(F32))
        resid_ref[...] = resid
        normed[...] = (resid * rms(resid) * gain_ref[...]).astype(BF)
        normed_ref[...] = normed[...]
        out_acc[...] = jnp.zeros_like(out_acc)
        back_acc[...] = jnp.zeros_like(back_acc)

    wide = down_ref.shape[1]
    both = mm(normed[...], gu_ref[...])
    d_hidden = mm(dy_ref[...], down_ref[...])
    gate, up = both[:, :wide], both[:, wide:]
    sig = 1.0 / (1.0 + jnp.exp(-gate))
    silu = gate * sig
    hidden = (silu * up).astype(BF)
    hidden_ref[...] = hidden
    d_up = (d_hidden * silu).astype(BF)
    d_gate = (d_hidden * up * (sig + silu * (1.0 - sig))).astype(BF)
    dgu_ref[:, :wide] = d_gate
    dgu_ref[:, wide:] = d_up
    out_acc[...] += mm(hidden, down_ref[...], NT)
    back_acc[...] += mm(dgu_ref[...], gu_ref[...], NT)

    @pl.when(step == steps - 1)
    def _():
        out_ref[...] = out_acc[...].astype(BF)
        back_ref[...] = back_acc[...].astype(BF)


def feed_forward(half, x, own, got, gain, dy, w_rest, o_cols, chunk, whole=None):
    rows, model = own.shape
    units = (w_rest.shape[1] - o_cols) // 3
    steps = units // chunk
    mine, once = lambda f: (half, 0), lambda f: (0, 0)
    at_gu, at_down = o_cols // (2 * chunk), (o_cols + 2 * units) // chunk
    block = (rows, model)
    ins = [
        (x, block, mine), (own, block, once), (got, block, once), (gain, (1, model), once), (dy, block, mine),
        (w_rest, (model, 2 * chunk), lambda f: (0, at_gu + f)),
        (w_rest, (model, chunk), lambda f: (0, at_down + f)),
    ]
    keep = {}
    if whole is not None:
        keep = {len(ins) + i: 1 + i for i in range(3)}
        ins += [(array, None, None) for array in whole]
    outs = [
        (shaped((rows, model), F32), block, once),
        (shaped((2 * rows, model), BF), block, mine),
        (shaped((2 * rows, units), BF), (rows, chunk), lambda f: (half, f)),
        (shaped((2 * rows, 2 * units), BF), (rows, 2 * chunk), lambda f: (half, f)),
        (shaped((rows, model), BF), block, once),
        (shaped((rows, model), BF), block, once),
    ]
    scratch = [pltpu.VMEM(block, BF), pltpu.VMEM(block, F32), pltpu.VMEM(block, F32)]
    return call(ffn_kernel, "feed_forward", (steps,), ins, outs, scratch,
                flops=12 * rows * model * units, moved=20 * MIB, keep=keep)


def norm_back(grad, values, gain):
    scale = rms(values)
    unit = values * scale
    inner = grad * gain
    return scale * (inner - unit * jnp.mean(inner * unit, axis=-1, keepdims=True)), grad * unit


def mixed_kernel(heads, own_ref, got_ref, resid_ref, gain_ref, dy_ref, w_ref, att_ref, *refs):
    d_resid_ref, mixed_ref, datt_ref, delta_ref, dgain_ref = refs[-5:]
    grad = own_ref[...].astype(F32) + got_ref[...].astype(F32)
    d_norm, summand = norm_back(grad, resid_ref[...], gain_ref[...])
    dgain_ref[...] = jnp.sum(summand, axis=0, keepdims=True)
    d_resid = dy_ref[...].astype(F32) + d_norm
    d_resid_ref[...] = d_resid
    mixed_ref[...] = d_resid.astype(BF)
    datt_ref[...] = mm(mixed_ref[...], w_ref[...]).astype(BF)
    for h in range(heads):
        cols = slice(h * HEAD_SIZE, (h + 1) * HEAD_SIZE)
        product = datt_ref[:, cols].astype(F32) * att_ref[:, cols].astype(F32)
        delta_ref[h // 2, h % 2 : h % 2 + 1, :] = jnp.sum(product.T, axis=0, keepdims=True)


def mixed_back(half, own, got, resid, gain, dy, w_rest, o_cols, attended, whole=None):
    rows, model = own.shape
    heads = o_cols // HEAD_SIZE
    mine, once = lambda f: (half, 0), lambda f: (0, 0)
    block = (rows, model)
    ins = [
        (own, block, once), (got, block, once), (resid, block, once), (gain, (1, model), once),
        (dy, block, mine), (w_rest, (model, o_cols), once), (attended, (rows, o_cols), mine),
    ]
    keep = {}
    if whole is not None:
        keep = {len(ins): 1}
        ins.append((whole, None, None))
    outs = [
        (shaped((rows, model), F32), block, once),
        (shaped((2 * rows, model), BF), block, mine),
        (shaped((rows, o_cols), BF), (rows, o_cols), once),
        (shaped((heads // 2, 8, rows), F32), (heads // 2, 8, rows), lambda f: (0, 0, 0)),
        (shaped((1, model), F32), (1, model), once),
    ]
    return call(functools.partial(mixed_kernel, heads), "mixed_back", (1,), ins, outs,
                flops=2 * rows * model * o_cols, moved=12 * MIB, keep=keep)


def qkv_kernel(heads, kv_heads, n_kv, dq_ref, ql_ref, kl_ref, qg_ref, kg_ref, cos_ref, sin_ref, w_ref, *refs):
    kv_refs = refs[:n_kv]
    dqkv_ref, part_ref, gains_ref = refs[-3:]
    cos, sin = cos_ref[...], sin_ref[...]
    q_cols, k_cols = heads * HEAD_SIZE, kv_heads * HEAD_SIZE

    def total(which, cols):
        value = kv_refs[0][which, :, cols].astype(F32)
        for ref in kv_refs[1:]:
            value = value + ref[which, :, cols].astype(F32)
        return value

    q_sum = k_sum = jnp.zeros((1, HEAD_SIZE), F32)
    for h in range(heads):
        cols = slice(h * HEAD_SIZE, (h + 1) * HEAD_SIZE)
        grad, summand = norm_back(turn_back(dq_ref[:, cols], cos, sin), ql_ref[:, cols], qg_ref[...])
        dqkv_ref[:, cols] = grad.astype(BF)
        q_sum = q_sum + jnp.sum(summand, axis=0, keepdims=True)
    for h in range(kv_heads):
        cols = slice(h * HEAD_SIZE, (h + 1) * HEAD_SIZE)
        grad, summand = norm_back(turn_back(total(0, cols), cos, sin), kl_ref[:, cols], kg_ref[...])
        dqkv_ref[:, q_cols + h * HEAD_SIZE : q_cols + (h + 1) * HEAD_SIZE] = grad.astype(BF)
        k_sum = k_sum + jnp.sum(summand, axis=0, keepdims=True)
    dqkv_ref[:, q_cols + k_cols :] = total(1, slice(None)).astype(BF)
    part_ref[...] = mm(dqkv_ref[...], w_ref[...], NT).astype(BF)
    gains_ref[:, :HEAD_SIZE] = q_sum
    gains_ref[:, HEAD_SIZE:] = k_sum


def qkv_back(half, dq, q_lin, k_lin, q_gain, k_gain, cos, sin, w_qkv, kvs, whole=None):
    rows, q_cols = dq.shape
    k_cols = k_lin.shape[1]
    model, cols = w_qkv.shape
    mine, once = lambda f: (half, 0), lambda f: (0, 0)
    ins = [
        (dq, (rows, q_cols), once), (q_lin, (rows, q_cols), mine), (k_lin, (rows, k_cols), once),
        (q_gain, (1, HEAD_SIZE), once), (k_gain, (1, HEAD_SIZE), once),
        (cos, (rows, HEAD_SIZE), mine), (sin, (rows, HEAD_SIZE), mine), (w_qkv, (model, cols), once),
    ]
    ins += [(kv, (2, rows, k_cols), lambda f: (0, 0, 0)) for kv in kvs]
    keep = {}
    if whole is not None:
        keep = {len(ins): 0}
        ins.append((whole, None, None))
    outs = [
        (shaped((2 * rows, cols), BF), (rows, cols), mine),
        (shaped((rows, model), BF), (rows, model), once),
        (shaped((1, 2 * HEAD_SIZE), F32), (1, 2 * HEAD_SIZE), once),
    ]
    kernel = functools.partial(qkv_kernel, q_cols // HEAD_SIZE, k_cols // HEAD_SIZE, len(kvs))
    return call(kernel, "qkv_back", (1,), ins, outs, flops=2 * rows * model * cols, moved=16 * MIB, keep=keep)


def tokens_kernel(own_ref, got_ref, x_ref, gain_ref, d_resid_ref, *refs):
    out_ref, dgain_ref = refs[-2:]
    grad = own_ref[...].astype(F32) + got_ref[...].astype(F32)
    d_norm, summand = norm_back(grad, x_ref[...].astype(F32), gain_ref[...])
    dgain_ref[...] = jnp.sum(summand, axis=0, keepdims=True)
    out_ref[...] = (d_resid_ref[...] + d_norm).astype(BF)


def tokens_back(half, own, got, x, gain, d_resid, whole=None):
    rows, model = own.shape
    mine, once = lambda f: (half, 0), lambda f: (0, 0)
    block = (rows, model)
    ins = [(own, block, once), (got, block, once), (x, block, mine), (gain, (1, model), once), (d_resid, block, once)]
    keep = {}
    if whole is not None:
        keep = {len(ins): 0}
        ins.append((whole, None, None))
    outs = [(shaped((2 * rows, model), BF), block, mine), (shaped((1, model), F32), (1, model), once)]
    return call(tokens_kernel, "tokens_back", (1,), ins, outs, flops=rows * model * 10, moved=8 * MIB, keep=keep)


def swap(value, axis, bit):
    size = lax.axis_size(axis)
    return lax.ppermute(value, axis, [(i, i ^ bit) for i in range(size)])


def shift(value, by):
    size = lax.axis_size("ctx")
    return lax.ppermute(value, "ctx", [(i, i + by) for i in range(size) if 0 <= i + by < size])


def add_low(left, right):
    return (left.astype(F32) + right.astype(F32)).astype(BF)


def butterfly(value, axes):
    for axis in axes:
        bit = 1
        while bit < lax.axis_size(axis):
            value = value + swap(value, axis, bit)
            bit *= 2
    return value


def after(value, *others):
    return lax.optimization_barrier((value, *others))[0]


def rotary_tables(position):
    half_dim = HEAD_SIZE // 2
    inverse_freq = jnp.exp(jnp.arange(half_dim, dtype=F32) * (-math.log(ROPE_BASE) / half_dim))
    angles = position.astype(F32)[:, None] * inverse_freq[None, :]
    cosine, sine = jnp.cos(angles), jnp.sin(angles)
    return jnp.concatenate([cosine, cosine], axis=-1), jnp.concatenate([-sine, sine], axis=-1)


def body(
    tokens,
    cont_lengths,
    attn_gain,
    ffn_gain,
    query_gain,
    key_gain,
    w_query,
    key_weight,
    value_weight,
    w_out,
    w_gate,
    w_up,
    w_down,
    cotangent,
):
    ctx_size = lax.axis_size("ctx")
    weight_axes = ("shard", "ctx")
    parts = lax.axis_size("shard") * ctx_size
    me = lax.axis_index("ctx")
    part = lax.axis_index("shard") * ctx_size + me
    rows, model = tokens.shape[0] // 2, tokens.shape[1]
    n_halo = 1 + -(-(LONGEST - 1) // rows)
    lengths = cont_lengths[0]

    gains = jnp.concatenate([attn_gain, ffn_gain, query_gain, key_gain])[None]
    spread = jnp.where(jnp.arange(parts)[:, None] == part, gains, jnp.zeros((), BF))
    gains = butterfly(spread, ("ctx", "shard")).astype(F32)
    wide, narrow = attn_gain.shape[0], query_gain.shape[0]
    gain_one = gains[:, :wide].reshape(1, -1)
    gain_two = gains[:, wide : 2 * wide].reshape(1, -1)
    gain_q = gains[:, 2 * wide : 2 * wide + narrow].reshape(1, -1)
    gain_k = gains[:, 2 * wide + narrow :].reshape(1, -1)
    q_cols, k_cols = w_query.shape[1], key_weight.shape[1]
    o_cols, units = w_out.shape[0], w_gate.shape[1]
    heads, kv_heads = q_cols // HEAD_SIZE, k_cols // HEAD_SIZE
    chunk = math.gcd(units, 512)
    w_qkv = lax.all_gather(
        jnp.concatenate([w_query, key_weight, value_weight], axis=1), weight_axes, axis=0, tiled=True
    )
    pieces = [w_out.T]
    for at in range(0, units, chunk):
        pieces += [w_gate[:, at : at + chunk], w_up[:, at : at + chunk]]
    w_rest = lax.all_gather(jnp.concatenate(pieces + [w_down.T], axis=1), weight_axes, axis=0, tiled=True)

    cont_at = me * rows + jnp.arange(rows, dtype=jnp.int32)
    cont_ends = jnp.cumsum(lengths)
    starts = cont_ends - lengths
    seg = jnp.sum((cont_ends[None, :] <= cont_at[:, None]).astype(jnp.int32), axis=1)
    numbers = jnp.arange(lengths.shape[0], dtype=jnp.int32)
    first = jnp.sum(jnp.where(numbers[None, :] == seg[:, None], starts[None, :], 0), axis=1)
    position = jnp.concatenate([me * rows + jnp.arange(rows, dtype=jnp.int32), PROMPT + cont_at - first])
    low = first - me * rows
    low_col = jnp.broadcast_to(low[:, None], (rows, 128))
    low_row = jnp.broadcast_to(jnp.concatenate([low, low])[None, :], (8, 2 * rows))
    scalars = jnp.stack([me, low[0]])
    cos, sin = rotary_tables(position)

    once = lambda f: (0, 0)

    def keys_values(half, whole=None):
        mine = lambda f: (half, 0)
        ins = [
            (tokens, (rows, model), mine), (gain_one, (1, model), once),
            (w_qkv, (model, 2 * k_cols), lambda f: (0, q_cols // (2 * k_cols))),
            (gain_k, (1, HEAD_SIZE), once), (cos, (rows, HEAD_SIZE), mine), (sin, (rows, HEAD_SIZE), mine),
        ]
        keep = {}
        if whole is not None:
            keep = {len(ins): 0}
            ins.append((whole, None, None))
        outs = [
            (shaped((2 * rows, model), BF), (rows, model), mine),
            (shaped((2, rows, k_cols), BF), (2, rows, k_cols), lambda f: (0, 0, 0)),
            (shaped((rows, k_cols), F32), (rows, k_cols), once),
        ]
        return call(functools.partial(kv_kernel, kv_heads), "keys_values", (1,), ins, outs,
                    flops=4 * rows * model * k_cols, moved=8 * MIB, keep=keep)

    normed, kv_p, k_lin_p = keys_values(0)
    slots = {0: kv_p}
    if ctx_size == 8:
        slots[2], slots[4] = swap(kv_p, "ctx", 2), swap(kv_p, "ctx", 4)
        slots[1] = swap(kv_p, "ctx", 1)
    normed, kv_c, k_lin_c = keys_values(1, normed)
    halos = {0: kv_c}
    odd = (me % 2) == 1
    if ctx_size == 8:
        halos[2] = shift(kv_c, 2)
        slots[6] = jnp.stack([swap(slots[4][0], "ctx", 2), swap(slots[2][1], "ctx", 4)])
        slots[3], slots[5], slots[7] = (swap(slots[s], "ctx", 1) for s in (2, 4, 6))
        halos[1] = swap(jnp.where(odd, halos[2], kv_c), "ctx", 1)
    else:
        both, bit = kv_p[None], 1
        while bit < ctx_size:
            both = jnp.concatenate([both, swap(both, "ctx", bit)])
            bit *= 2
        slots = {s: both[s] for s in range(ctx_size)}
        halos.update({d: shift(kv_c, d) for d in range(1, n_halo)})

    def pick(source, wanted):
        return {s: source[s] for s in source if s in wanted}

    mine = lambda f: (f, 0)
    q, q_lin = call(
        functools.partial(q_kernel, heads), "queries", (2,),
        [
            (normed, (rows, model), mine), (w_qkv, (model, q_cols), lambda f: (0, 0)),
            (gain_q, (1, HEAD_SIZE), lambda f: (0, 0)),
            (cos, (rows, HEAD_SIZE), mine), (sin, (rows, HEAD_SIZE), mine),
        ],
        [(shaped((2 * rows, q_cols), BF), (rows, q_cols), mine), (shaped((2 * rows, q_cols), F32), (rows, q_cols), mine)],
        flops=4 * rows * model * q_cols, moved=12 * MIB,
    )

    near, middle, far = (0, 1), (2, 3, 4, 5), tuple(range(6, ctx_size))
    p_state = attention_forward(0, scalars, q, low_col, pick(slots, near), {})
    c_state = attention_forward(1, scalars, q, low_col, pick(slots, near), pick(halos, (0,)))
    c_state = attention_forward(1, scalars, q, low_col, pick(slots, middle), {}, c_state)
    attended, lse_p, part_p = attention_forward(
        0, scalars, q, low_col, pick(slots, middle + far), {}, p_state, (w_rest, None)
    )
    got_p = swap(part_p, "tensor", 1)
    attended, lse_c, part_c = attention_forward(
        1, scalars, q, low_col, pick(slots, far), pick(halos, range(1, n_halo)), c_state, (w_rest, attended)
    )
    got_c = swap(part_c, "tensor", 1)

    resid_p, *whole, out_p, back_p = feed_forward(
        0, tokens, part_p, got_p, gain_two, cotangent, w_rest, o_cols, chunk
    )
    back_got_p = swap(back_p, "tensor", 1)
    resid_c, *whole, out_c, back_c = feed_forward(
        1, tokens, part_c, got_c, gain_two, cotangent, w_rest, o_cols, chunk, whole
    )
    back_got_c = swap(back_c, "tensor", 1)
    normed_ffn, hidden, d_gu = whole
    ffn_grads = jnp.concatenate(
        [mm(normed_ffn, d_gu, TN).astype(BF), mm(cotangent, hidden, TN).astype(BF)], axis=1
    )
    ffn_share = lax.psum_scatter(ffn_grads, weight_axes, scatter_dimension=0, tiled=True)

    back_got_p = after(back_got_p, ffn_grads)
    d_resid_p, d_mixed, d_att_p, delta_p, d_two_p = mixed_back(
        0, back_p, back_got_p, resid_p, gain_two, cotangent, w_rest, o_cols, attended
    )
    dq_p, from_p, _ = attention_backward(0, scalars, q, d_att_p, lse_p, delta_p, low_row, slots, {})
    d_resid_c, d_mixed, d_att_c, delta_c, d_two_c = mixed_back(
        1, back_c, back_got_c, resid_c, gain_two, cotangent, w_rest, o_cols, attended, d_mixed
    )
    out_grad = mm(d_mixed, attended, TN).astype(BF)
    out_share = lax.psum_scatter(out_grad, weight_axes, scatter_dimension=0, tiled=True)
    c_args = (scalars, q, d_att_c, lse_c, delta_c, low_row)
    dq_c, g, g_halo = attention_backward(1, *c_args, pick(slots, far), halos, None, pick(from_p, far), False)
    dq_c, more, _ = attention_backward(1, *c_args, pick(slots, middle), {}, dq_c, pick(from_p, middle), False)
    g.update(more)
    dq_c, more, _ = attention_backward(1, *c_args, pick(slots, near), {}, dq_c, pick(from_p, near), True)
    g.update(more)

    if ctx_size == 8:
        g6 = add_low(g[6], swap(g[7], "ctx", 1))
        k6, v6 = swap(g6[0], "ctx", 2), swap(g6[1], "ctx", 4)
        g4, g2 = add_low(g[4], swap(g[5], "ctx", 1)), add_low(g[2], swap(g[3], "ctx", 1))
        g4 = jnp.stack([add_low(g4[0], k6), g4[1]])
        g2 = jnp.stack([g2[0], add_low(g2[1], v6)])
        kvs_p = [g[0], swap(g[1], "ctx", 1), swap(g2, "ctx", 2), swap(g4, "ctx", 4)]
        zero = jnp.zeros((), BF)
        near_one = swap(g_halo[1], "ctx", 1)
        two = shift(add_low(g_halo[2], jnp.where(odd, near_one, zero)), -2)
        kvs_c = [g_halo[0], jnp.where(odd, zero, near_one), two]
    else:
        both = jnp.stack([g[s] for s in range(ctx_size)])
        while both.shape[0] > 1:
            size = both.shape[0] // 2
            both = add_low(both[:size], swap(both[size:], "ctx", size))
        kvs_p = [both[0]]
        kvs_c = [g_halo[0]] + [shift(g_halo[d], -d) for d in range(1, n_halo)]

    d_qkv, into_c, heads_c = qkv_back(1, dq_c, q_lin, k_lin_c, gain_q, gain_k, cos, sin, w_qkv, kvs_c)
    into_got_c = swap(into_c, "tensor", 1)
    d_qkv, into_p, heads_p = qkv_back(0, dq_p, q_lin, k_lin_p, gain_q, gain_k, cos, sin, w_qkv, kvs_p, d_qkv)
    into_got_p = swap(into_p, "tensor", 1)
    qkv_grad = mm(normed, d_qkv, TN).astype(BF)
    qkv_share = lax.psum_scatter(qkv_grad, weight_axes, scatter_dimension=0, tiled=True)
    grad_tokens, d_one_c = tokens_back(1, into_c, into_got_c, tokens, gain_one, d_resid_c)
    grad_tokens, d_one_p = tokens_back(0, into_p, into_got_p, tokens, gain_one, d_resid_p, grad_tokens)

    out_p, out_c = after(out_p, dq_p), after(out_c, dq_p)
    layer_out = jnp.concatenate(
        [
            (resid + (own.astype(F32) + swap(own, "tensor", 1).astype(F32))).astype(BF)
            for resid, own in ((resid_p, out_p), (resid_c, out_c))
        ]
    )

    model_gains = jnp.concatenate([d_one_c + d_one_p, d_two_c + d_two_p])
    model_gains = butterfly(model_gains, ("ctx", "shard")).reshape(2, parts, wide)
    head_gains = butterfly(heads_c + heads_p, ("ctx", "shard", "tensor")).reshape(2, parts, narrow)
    model_gains = lax.dynamic_index_in_dim(model_gains, part, 1, keepdims=False)
    head_gains = lax.dynamic_index_in_dim(head_gains, part, 1, keepdims=False)

    qkv_share, ffn_share, out_share = (s.astype(F32) for s in (qkv_share, ffn_share, out_share))
    gate_up = ffn_share[:, : 2 * units].reshape(wide, units // chunk, 2, chunk)
    return (
        layer_out,
        grad_tokens,
        model_gains[0],
        model_gains[1],
        head_gains[0],
        head_gains[1],
        qkv_share[:, :q_cols],
        qkv_share[:, q_cols : q_cols + k_cols],
        qkv_share[:, q_cols + k_cols :],
        out_share.T,
        gate_up[:, :, 0].reshape(wide, units),
        gate_up[:, :, 1].reshape(wide, units),
        ffn_share[:, 2 * units :].T,
    )


def solution(mesh):
    split = ("shard", "ctx")
    rows, gain = P(split, None), P(split)
    into, out_of = P(split, "tensor"), P("tensor", split)
    in_specs = (rows, P("shard", None)) + (gain,) * 4 + (into,) * 3 + (out_of,)
    in_specs += (into, into, out_of, rows)
    out_specs = (rows, rows) + (gain,) * 4 + (into,) * 3 + (out_of, into, into, out_of)
    return jax.shard_map(body, mesh=mesh, in_specs=in_specs, out_specs=out_specs, check_vma=False)
```

```python
import functools
import math

import jax
import jax.numpy as jnp
from jax import lax
from jax.experimental import pallas as pl
from jax.experimental.pallas import tpu as pltpu
from jax.sharding import PartitionSpec as P

HEAD_SIZE = 128
PROMPT = 4096
CONT_TOK = 4096
LONGEST = 1024

EPSILON = 1e-06
ROPE_BASE = 1000000.0
MASKED = -1e30
LOG2E = math.log2(math.e)
LN2 = math.log(2.0)
SCALE = 1.0 / math.sqrt(HEAD_SIZE)

BF = jnp.bfloat16
F32 = jnp.float32
NN = (((1,), (0,)), ((), ()))
NT = (((1,), (1,)), ((), ()))
TN = (((0,), (0,)), ((), ()))
MIB = 2**20


def mm(left, right, dims=NN):
    return lax.dot_general(left, right, dims, preferred_element_type=F32)


def shaped(dims, kind):
    return jax.ShapeDtypeStruct(dims, kind)


def call(kernel, name, grid, ins, outs, scratch=(), vmem=56, flops=0, moved=0, scalars=None, keep=None):
    in_specs, arrays = [], []
    for array, block, index in ins:
        arrays.append(array)
        in_specs.append(pl.BlockSpec(memory_space=pl.ANY) if block is None else pl.BlockSpec(block, index))
    lead = 0 if scalars is None else 1
    return pl.pallas_call(
        kernel,
        grid_spec=pltpu.PrefetchScalarGridSpec(
            num_scalar_prefetch=lead,
            grid=grid,
            in_specs=in_specs,
            out_specs=[pl.BlockSpec(block, index) for _, block, index in outs],
            scratch_shapes=list(scratch),
        ),
        out_shape=[shape for shape, _, _ in outs],
        input_output_aliases={a + lead: b for a, b in (keep or {}).items()},
        compiler_params=pltpu.CompilerParams(vmem_limit_bytes=vmem * MIB),
        cost_estimate=pl.CostEstimate(flops=flops, bytes_accessed=moved, transcendentals=0),
        name=name,
    )(*([] if scalars is None else [scalars]), *arrays)


def rms(values):
    return lax.rsqrt(jnp.mean(values * values, axis=-1, keepdims=True) + EPSILON)


def turn(values, cos, sin):
    return values * cos + pltpu.roll(values, HEAD_SIZE // 2, 1) * sin


def turn_back(values, cos, sin):
    return values * cos - pltpu.roll(values, HEAD_SIZE // 2, 1) * sin


def kv_kernel(heads, x_ref, gain_ref, w_ref, hgain_ref, cos_ref, sin_ref, *refs):
    normed_ref, kv_ref, lin_ref = refs[-3:]
    x = x_ref[...].astype(F32)
    normed_ref[...] = (x * rms(x) * gain_ref[...]).astype(BF)
    both = mm(normed_ref[...], w_ref[...])
    width = heads * HEAD_SIZE
    kv_ref[1] = both[:, width:].astype(BF)
    for h in range(heads):
        cols = slice(h * HEAD_SIZE, (h + 1) * HEAD_SIZE)
        lin = both[:, cols]
        lin_ref[:, cols] = lin
        kv_ref[0, :, cols] = turn(lin * rms(lin) * hgain_ref[...], cos_ref[...], sin_ref[...]).astype(BF)


def q_kernel(heads, normed_ref, w_ref, hgain_ref, cos_ref, sin_ref, q_ref, lin_ref):
    both = mm(normed_ref[...], w_ref[...])
    for h in range(heads):
        cols = slice(h * HEAD_SIZE, (h + 1) * HEAD_SIZE)
        lin = both[:, cols]
        lin_ref[:, cols] = lin
        turned = turn(lin * rms(lin) * hgain_ref[...], cos_ref[...], sin_ref[...])
        q_ref[:, cols] = (turned * (SCALE * LOG2E)).astype(BF)


def fwd_kernel(plan, idx_ref, q_ref, lo_ref, *refs):
    half, slots, halos = plan["half"], plan["slots"], plan["halos"]
    refs = list(refs)
    slot_refs = [refs.pop(0) for _ in slots]
    halo_refs = [refs.pop(0) for _ in halos]
    prior = [refs.pop(0) for _ in range(2)] if plan["carry"] else None
    if plan["last"]:
        w_ref = refs.pop(0)
        if plan["alias"]:
            refs.pop(0)
        out_ref, lse_ref, part_ref, acc, tot, part_acc = refs
    else:
        acc, tot = refs
    me, lo_first = idx_ref[0], idx_ref[1]
    rows = q_ref.shape[0]
    if prior is None:
        acc[...] = jnp.zeros_like(acc)
        tot[...] = jnp.zeros_like(tot)
    else:
        acc[...] = prior[0][...]
        tot[...] = prior[1][...]

    def add(kv_ref, mask=None):
        for g in range(2):
            cols = slice(g * HEAD_SIZE, (g + 1) * HEAD_SIZE)
            scores = mm(q_ref[:, cols], kv_ref[0], NT)
            if mask is not None:
                scores = jnp.where(mask, scores, MASKED)
            weights = jnp.exp2(scores)
            total = weights[:, :128]
            for at in range(128, weights.shape[1], 128):
                total = total + weights[:, at : at + 128]
            acc[:, cols] += mm(weights.astype(BF), kv_ref[1])
            tot[:, cols] += total

    row = lax.broadcasted_iota(jnp.int32, (rows, 1), 0)
    col = lax.broadcasted_iota(jnp.int32, (1, rows), 1)
    for d, kv_ref in zip(halos, halo_refs):
        low = lo_ref[:, :1]
        if d == 0:
            add(kv_ref, (col <= row) & (col >= low))
        else:

            @pl.when(lo_first < -(d - 1) * rows)
            def _(d=d, kv_ref=kv_ref, low=low):
                add(kv_ref, col - d * rows >= low)

    for s, kv_ref in zip(slots, slot_refs):
        if half == 1:
            add(kv_ref)
        elif s == 0:
            add(kv_ref, col <= row)
        else:

            @pl.when(jnp.bitwise_xor(me, s) < me)
            def _(kv_ref=kv_ref):
                add(kv_ref)

    if plan["last"]:
        step, steps = pl.program_id(0), pl.num_programs(0)
        for g in range(2):
            cols = slice(g * HEAD_SIZE, (g + 1) * HEAD_SIZE)
            total = jnp.sum(tot[:, cols], axis=1, keepdims=True)
            out_ref[:, cols] = (acc[:, cols] / total).astype(BF)
            lse_ref[0, g : g + 1, :] = jnp.log2(jnp.sum(tot[:, cols].T, axis=0, keepdims=True))
        part = mm(out_ref[...], w_ref[...], NT)

        @pl.when(step == 0)
        def _():
            part_acc[...] = part

        @pl.when(step > 0)
        def _():
            part_acc[...] += part

        @pl.when(step == steps - 1)
        def _():
            part_ref[...] = part_acc[...].astype(BF)


def attention_forward(half, scalars, q, low, slots, halos, carry=None, last=None):
    rows, heads = q.shape[0] // 2, q.shape[1] // 256
    plan = dict(half=half, slots=list(slots), halos=list(halos), carry=carry is not None,
                last=last is not None, alias=last is not None and last[1] is not None)
    mine = lambda h, i: (half, h)
    part = lambda h, i: (0, h)
    ins = [(q, (rows, 256), mine), (low, (rows, 128), lambda h, i: (0, 0))]
    for kv in list(slots.values()) + list(halos.values()):
        ins.append((kv, (2, rows, 128), lambda h, i: (0, 0, h)))
    if carry is not None:
        ins += [(c, (rows, 256), part) for c in carry]
    scratch, keep = [], {}
    state = shaped((rows, heads * 256), F32)
    if last is None:
        outs = [(state, (rows, 256), part)] * 2
    else:
        w_rest, other = last
        model = w_rest.shape[0]
        ins.append((w_rest, (model, 256), part))
        if other is not None:
            keep = {len(ins): 0}
            ins.append((other, None, None))
        outs = [
            (shaped((2 * rows, heads * 256), BF), (rows, 256), mine),
            (shaped((heads, 8, rows), F32), (1, 8, rows), lambda h, i: (h, 0, 0)),
            (shaped((rows, model), BF), (rows, model), lambda h, i: (0, 0)),
        ]
        scratch = [pltpu.VMEM((rows, 256), F32)] * 2 + [pltpu.VMEM((rows, model), F32)]
    blocks = len(slots) * (2 if half else 1) + len(halos)
    pairs = heads * rows * rows * blocks
    return call(functools.partial(fwd_kernel, plan), "attend", (heads,), ins, outs, scratch,
                flops=pairs * 1024, moved=8 * MIB, scalars=scalars, keep=keep)


def bwd_kernel(plan, idx_ref, q_ref, do_ref, lse_ref, delta_ref, lo_ref, *refs):
    half, slots, halos = plan["half"], plan["slots"], plan["halos"]
    refs = list(refs)
    slot_refs = [refs.pop(0) for _ in slots]
    halo_refs = [refs.pop(0) for _ in halos]
    prior_dq = refs.pop(0) if plan["carry"] else None
    prior = [refs.pop(0) for _ in slots] if plan["sum"] else None
    dq_ref = refs.pop(0)
    slot_outs = [refs.pop(0) for _ in slots]
    halo_outs = [refs.pop(0) for _ in halos]
    qs, dos, lses, deltas, dq = refs
    me, lo_first = idx_ref[0], idx_ref[1]
    rows = q_ref.shape[0]
    for g in range(2):
        cols, at = slice(g * HEAD_SIZE, (g + 1) * HEAD_SIZE), slice(g * rows, (g + 1) * rows)
        qs[at, :] = q_ref[:, cols]
        dos[at, :] = do_ref[:, cols]
        lses[:, at] = lse_ref[0, g : g + 1, :]
        deltas[:, at] = delta_ref[0, g : g + 1, :]
    dq[...] = jnp.zeros_like(dq) if prior_dq is None else prior_dq[...]

    def block(kv_ref, out_ref, mask=None, before=None):
        keys = kv_ref[0]
        scores = mm(keys, qs[...], NT)
        dp = mm(kv_ref[1], dos[...], NT)
        scores = scores - lses[...]
        if mask is not None:
            scores = jnp.where(mask, scores, MASKED)
        probs = jnp.exp2(scores)
        ds = (probs * (dp - deltas[...])).astype(BF)
        dq[...] += mm(keys.T, ds)
        dk, dv = mm(ds, qs[...]) * LN2, mm(probs.astype(BF), dos[...])
        if before is not None:
            dk, dv = dk + before[0].astype(F32), dv + before[1].astype(F32)
        out_ref[0] = dk.astype(BF)
        out_ref[1] = dv.astype(BF)

    lane = lax.broadcasted_iota(jnp.int32, (1, 2 * rows), 1)
    lane = jnp.where(lane >= rows, lane - rows, lane)
    key = lax.broadcasted_iota(jnp.int32, (rows, 1), 0)

    def when(needed, kv_ref, out_ref, mask=None):
        @pl.when(needed)
        def _():
            block(kv_ref, out_ref, mask)

        @pl.when(jnp.logical_not(needed))
        def _():
            out_ref[...] = jnp.zeros_like(out_ref)

    low = lo_ref[:1, :]
    for d, kv_ref, out_ref in zip(halos, halo_refs, halo_outs):
        if d == 0:
            block(kv_ref, out_ref, (key <= lane) & (key >= low))
        else:
            when(lo_first < -(d - 1) * rows, kv_ref, out_ref, key - d * rows >= low)
    for at, (s, kv_ref, out_ref) in enumerate(zip(slots, slot_refs, slot_outs)):
        if half == 1:
            block(kv_ref, out_ref, None, prior[at])
        elif s == 0:
            block(kv_ref, out_ref, key <= lane)
        else:
            when(jnp.bitwise_xor(me, s) < me, kv_ref, out_ref)
    if plan["last"]:
        for g in range(2):
            cols = slice(g * HEAD_SIZE, (g + 1) * HEAD_SIZE)
            dq_ref[:, cols] = dq[:, g * rows : (g + 1) * rows].T * SCALE
    else:
        dq_ref[...] = dq[...]


def attention_backward(half, scalars, q, do, lse, delta, low, slots, halos, carry=None, prior=None, last=True):
    rows, heads = q.shape[0] // 2, q.shape[1] // 256
    plan = dict(half=half, slots=list(slots), halos=list(halos), carry=carry is not None,
                sum=prior is not None, last=last)
    part = lambda h, i: (0, h)
    stat = lambda h, i: (h, 0, 0)
    kv_map = lambda h, i: (0, 0, h)
    ins = [
        (q, (rows, 256), lambda h, i: (half, h)),
        (do, (rows, 256), part),
        (lse, (1, 8, rows), stat),
        (delta, (1, 8, rows), stat),
        (low, (8, 2 * rows), lambda h, i: (0, 0)),
    ]
    pieces = list(slots.values()) + list(halos.values())
    ins += [(kv, (2, rows, 128), kv_map) for kv in pieces]
    if carry is not None:
        ins.append((carry, (128, 2 * rows), lambda h, i: (h, 0)))
    if prior is not None:
        ins += [(prior[s], (2, rows, 128), kv_map) for s in slots]
    if last:
        outs = [(shaped((rows, heads * 256), F32), (rows, 256), part)]
    else:
        outs = [(shaped((heads * 128, 2 * rows), F32), (128, 2 * rows), lambda h, i: (h, 0))]
    outs += [(shaped(kv.shape, BF), (2, rows, 128), kv_map) for kv in pieces]
    scratch = [
        pltpu.VMEM((2 * rows, 128), BF),
        pltpu.VMEM((2 * rows, 128), BF),
        pltpu.VMEM((1, 2 * rows), F32),
        pltpu.VMEM((1, 2 * rows), F32),
        pltpu.VMEM((128, 2 * rows), F32),
    ]
    blocks = len(slots) * (2 if half else 1) + len(halos)
    pairs = heads * rows * rows * blocks
    results = call(functools.partial(bwd_kernel, plan), "attend_back", (heads,), ins, outs, scratch,
                   flops=pairs * 2560, moved=8 * MIB, scalars=scalars)
    n = len(slots)
    return results[0], dict(zip(slots, results[1 : 1 + n])), dict(zip(halos, results[1 + n :]))


def ffn_kernel(x_ref, own_ref, got_ref, gain_ref, dy_ref, gu_ref, down_ref, *refs):
    resid_ref, normed_ref, hidden_ref, dgu_ref, out_ref, back_ref, normed, out_acc, back_acc = refs[-9:]
    step, steps = pl.program_id(0), pl.num_programs(0)

    @pl.when(step == 0)
    def _():
        resid = x_ref[...].astype(F32) + (own_ref[...].astype(F32) + got_ref[...].astype(F32))
        resid_ref[...] = resid
        normed[...] = (resid * rms(resid) * gain_ref[...]).astype(BF)
        normed_ref[...] = normed[...]
        out_acc[...] = jnp.zeros_like(out_acc)
        back_acc[...] = jnp.zeros_like(back_acc)

    wide = down_ref.shape[1]
    both = mm(normed[...], gu_ref[...])
    d_hidden = mm(dy_ref[...], down_ref[...])
    gate, up = both[:, :wide], both[:, wide:]
    sig = 1.0 / (1.0 + jnp.exp(-gate))
    silu = gate * sig
    hidden = (silu * up).astype(BF)
    hidden_ref[...] = hidden
    d_up = (d_hidden * silu).astype(BF)
    d_gate = (d_hidden * up * (sig + silu * (1.0 - sig))).astype(BF)
    dgu_ref[:, :wide] = d_gate
    dgu_ref[:, wide:] = d_up
    out_acc[...] += mm(hidden, down_ref[...], NT)
    back_acc[...] += mm(dgu_ref[...], gu_ref[...], NT)

    @pl.when(step == steps - 1)
    def _():
        out_ref[...] = out_acc[...].astype(BF)
        back_ref[...] = back_acc[...].astype(BF)


def feed_forward(half, x, own, got, gain, dy, w_rest, o_cols, chunk, whole=None):
    rows, model = own.shape
    units = (w_rest.shape[1] - o_cols) // 3
    steps = units // chunk
    mine, once = lambda f: (half, 0), lambda f: (0, 0)
    at_gu, at_down = o_cols // (2 * chunk), (o_cols + 2 * units) // chunk
    block = (rows, model)
    ins = [
        (x, block, mine), (own, block, once), (got, block, once), (gain, (1, model), once), (dy, block, mine),
        (w_rest, (model, 2 * chunk), lambda f: (0, at_gu + f)),
        (w_rest, (model, chunk), lambda f: (0, at_down + f)),
    ]
    keep = {}
    if whole is not None:
        keep = {len(ins) + i: 1 + i for i in range(3)}
        ins += [(array, None, None) for array in whole]
    outs = [
        (shaped((rows, model), F32), block, once),
        (shaped((2 * rows, model), BF), block, mine),
        (shaped((2 * rows, units), BF), (rows, chunk), lambda f: (half, f)),
        (shaped((2 * rows, 2 * units), BF), (rows, 2 * chunk), lambda f: (half, f)),
        (shaped((rows, model), BF), block, once),
        (shaped((rows, model), BF), block, once),
    ]
    scratch = [pltpu.VMEM(block, BF), pltpu.VMEM(block, F32), pltpu.VMEM(block, F32)]
    return call(ffn_kernel, "feed_forward", (steps,), ins, outs, scratch,
                flops=12 * rows * model * units, moved=20 * MIB, keep=keep)


def norm_back(grad, values, gain):
    scale = rms(values)
    unit = values * scale
    inner = grad * gain
    return scale * (inner - unit * jnp.mean(inner * unit, axis=-1, keepdims=True)), grad * unit


def mixed_kernel(heads, own_ref, got_ref, resid_ref, gain_ref, dy_ref, w_ref, att_ref, *refs):
    d_resid_ref, mixed_ref, datt_ref, delta_ref, dgain_ref = refs[-5:]
    grad = own_ref[...].astype(F32) + got_ref[...].astype(F32)
    d_norm, summand = norm_back(grad, resid_ref[...], gain_ref[...])
    dgain_ref[...] = jnp.sum(summand, axis=0, keepdims=True)
    d_resid = dy_ref[...].astype(F32) + d_norm
    d_resid_ref[...] = d_resid
    mixed_ref[...] = d_resid.astype(BF)
    datt_ref[...] = mm(mixed_ref[...], w_ref[...]).astype(BF)
    for h in range(heads):
        cols = slice(h * HEAD_SIZE, (h + 1) * HEAD_SIZE)
        product = datt_ref[:, cols].astype(F32) * att_ref[:, cols].astype(F32)
        delta_ref[h // 2, h % 2 : h % 2 + 1, :] = jnp.sum(product.T, axis=0, keepdims=True)


def mixed_back(half, own, got, resid, gain, dy, w_rest, o_cols, attended, whole=None):
    rows, model = own.shape
    heads = o_cols // HEAD_SIZE
    mine, once = lambda f: (half, 0), lambda f: (0, 0)
    block = (rows, model)
    ins = [
        (own, block, once), (got, block, once), (resid, block, once), (gain, (1, model), once),
        (dy, block, mine), (w_rest, (model, o_cols), once), (attended, (rows, o_cols), mine),
    ]
    keep = {}
    if whole is not None:
        keep = {len(ins): 1}
        ins.append((whole, None, None))
    outs = [
        (shaped((rows, model), F32), block, once),
        (shaped((2 * rows, model), BF), block, mine),
        (shaped((rows, o_cols), BF), (rows, o_cols), once),
        (shaped((heads // 2, 8, rows), F32), (heads // 2, 8, rows), lambda f: (0, 0, 0)),
        (shaped((1, model), F32), (1, model), once),
    ]
    return call(functools.partial(mixed_kernel, heads), "mixed_back", (1,), ins, outs,
                flops=2 * rows * model * o_cols, moved=12 * MIB, keep=keep)


def qkv_kernel(heads, kv_heads, n_kv, dq_ref, ql_ref, kl_ref, qg_ref, kg_ref, cos_ref, sin_ref, w_ref, *refs):
    kv_refs = refs[:n_kv]
    dqkv_ref, part_ref, gains_ref = refs[-3:]
    cos, sin = cos_ref[...], sin_ref[...]
    q_cols, k_cols = heads * HEAD_SIZE, kv_heads * HEAD_SIZE

    def total(which, cols):
        value = kv_refs[0][which, :, cols].astype(F32)
        for ref in kv_refs[1:]:
            value = value + ref[which, :, cols].astype(F32)
        return value

    q_sum = k_sum = jnp.zeros((1, HEAD_SIZE), F32)
    for h in range(heads):
        cols = slice(h * HEAD_SIZE, (h + 1) * HEAD_SIZE)
        grad, summand = norm_back(turn_back(dq_ref[:, cols], cos, sin), ql_ref[:, cols], qg_ref[...])
        dqkv_ref[:, cols] = grad.astype(BF)
        q_sum = q_sum + jnp.sum(summand, axis=0, keepdims=True)
    for h in range(kv_heads):
        cols = slice(h * HEAD_SIZE, (h + 1) * HEAD_SIZE)
        grad, summand = norm_back(turn_back(total(0, cols), cos, sin), kl_ref[:, cols], kg_ref[...])
        dqkv_ref[:, q_cols + h * HEAD_SIZE : q_cols + (h + 1) * HEAD_SIZE] = grad.astype(BF)
        k_sum = k_sum + jnp.sum(summand, axis=0, keepdims=True)
    dqkv_ref[:, q_cols + k_cols :] = total(1, slice(None)).astype(BF)
    part_ref[...] = mm(dqkv_ref[...], w_ref[...], NT).astype(BF)
    gains_ref[:, :HEAD_SIZE] = q_sum
    gains_ref[:, HEAD_SIZE:] = k_sum


def qkv_back(half, dq, q_lin, k_lin, q_gain, k_gain, cos, sin, w_qkv, kvs, whole=None):
    rows, q_cols = dq.shape
    k_cols = k_lin.shape[1]
    model, cols = w_qkv.shape
    mine, once = lambda f: (half, 0), lambda f: (0, 0)
    ins = [
        (dq, (rows, q_cols), once), (q_lin, (rows, q_cols), mine), (k_lin, (rows, k_cols), once),
        (q_gain, (1, HEAD_SIZE), once), (k_gain, (1, HEAD_SIZE), once),
        (cos, (rows, HEAD_SIZE), mine), (sin, (rows, HEAD_SIZE), mine), (w_qkv, (model, cols), once),
    ]
    ins += [(kv, (2, rows, k_cols), lambda f: (0, 0, 0)) for kv in kvs]
    keep = {}
    if whole is not None:
        keep = {len(ins): 0}
        ins.append((whole, None, None))
    outs = [
        (shaped((2 * rows, cols), BF), (rows, cols), mine),
        (shaped((rows, model), BF), (rows, model), once),
        (shaped((1, 2 * HEAD_SIZE), F32), (1, 2 * HEAD_SIZE), once),
    ]
    kernel = functools.partial(qkv_kernel, q_cols // HEAD_SIZE, k_cols // HEAD_SIZE, len(kvs))
    return call(kernel, "qkv_back", (1,), ins, outs, flops=2 * rows * model * cols, moved=16 * MIB, keep=keep)


def tokens_kernel(own_ref, got_ref, x_ref, gain_ref, d_resid_ref, *refs):
    out_ref, dgain_ref = refs[-2:]
    grad = own_ref[...].astype(F32) + got_ref[...].astype(F32)
    d_norm, summand = norm_back(grad, x_ref[...].astype(F32), gain_ref[...])
    dgain_ref[...] = jnp.sum(summand, axis=0, keepdims=True)
    out_ref[...] = (d_resid_ref[...] + d_norm).astype(BF)


def tokens_back(half, own, got, x, gain, d_resid, whole=None):
    rows, model = own.shape
    mine, once = lambda f: (half, 0), lambda f: (0, 0)
    block = (rows, model)
    ins = [(own, block, once), (got, block, once), (x, block, mine), (gain, (1, model), once), (d_resid, block, once)]
    keep = {}
    if whole is not None:
        keep = {len(ins): 0}
        ins.append((whole, None, None))
    outs = [(shaped((2 * rows, model), BF), block, mine), (shaped((1, model), F32), (1, model), once)]
    return call(tokens_kernel, "tokens_back", (1,), ins, outs, flops=rows * model * 10, moved=8 * MIB, keep=keep)


def swap(value, axis, bit):
    size = lax.axis_size(axis)
    return lax.ppermute(value, axis, [(i, i ^ bit) for i in range(size)])


def shift(value, by):
    size = lax.axis_size("ctx")
    return lax.ppermute(value, "ctx", [(i, i + by) for i in range(size) if 0 <= i + by < size])


def add_low(left, right):
    return (left.astype(F32) + right.astype(F32)).astype(BF)


def butterfly(value, axes):
    for axis in axes:
        bit = 1
        while bit < lax.axis_size(axis):
            value = value + swap(value, axis, bit)
            bit *= 2
    return value


def after(value, *others):
    return lax.optimization_barrier((value, *others))[0]


def rotary_tables(position):
    half_dim = HEAD_SIZE // 2
    inverse_freq = jnp.exp(jnp.arange(half_dim, dtype=F32) * (-math.log(ROPE_BASE) / half_dim))
    angles = position.astype(F32)[:, None] * inverse_freq[None, :]
    cosine, sine = jnp.cos(angles), jnp.sin(angles)
    return jnp.concatenate([cosine, cosine], axis=-1), jnp.concatenate([-sine, sine], axis=-1)


def body(
    tokens,
    cont_lengths,
    attn_gain,
    ffn_gain,
    query_gain,
    key_gain,
    w_query,
    key_weight,
    value_weight,
    w_out,
    w_gate,
    w_up,
    w_down,
    cotangent,
):
    ctx_size = lax.axis_size("ctx")
    weight_axes = ("shard", "ctx")
    parts = lax.axis_size("shard") * ctx_size
    me = lax.axis_index("ctx")
    part = lax.axis_index("shard") * ctx_size + me
    rows, model = tokens.shape[0] // 2, tokens.shape[1]
    n_halo = 1 + -(-(LONGEST - 1) // rows)
    lengths = cont_lengths[0]

    bits = [("shard", 1)] + [("ctx", 1 << i) for i in range(1, ctx_size.bit_length() - 1)] + [("ctx", 1)]
    order = [0]
    for axis, bit in bits:
        order += [j ^ (bit * ctx_size if axis == "shard" else bit) for j in order]
    wide, narrow = attn_gain.shape[0], query_gain.shape[0]
    q_cols, k_cols = w_query.shape[1], key_weight.shape[1]
    o_cols, units = w_out.shape[0], w_gate.shape[1]
    heads, kv_heads = q_cols // HEAD_SIZE, k_cols // HEAD_SIZE
    chunk = math.gcd(units, 512)

    def gather_rows(piece):
        if ctx_size != 8:
            for axis, bit in bits:
                piece = jnp.concatenate([piece, swap(piece, axis, bit)])
            return piece
        piece = jnp.concatenate([piece, swap(piece, "shard", 1)])
        by_x, by_y = swap(piece, "ctx", 2), swap(piece, "ctx", 4)
        cut = piece.shape[1] // 2
        far = jnp.concatenate([swap(by_y[:, :cut], "ctx", 2), swap(by_x[:, cut:], "ctx", 4)], axis=1)
        piece = jnp.concatenate([piece, by_x, by_y, far])
        return jnp.concatenate([piece, swap(piece, "ctx", 1)])

    def scatter_rows(low, high):
        total = add_low(low, swap(high, "ctx", 1))
        if ctx_size != 8:
            for axis, bit in bits[-2::-1]:
                size = total.shape[0] // 2
                total = add_low(total[:size], swap(total[size:], axis, bit))
            return total
        size, cut = total.shape[0] // 4, total.shape[1] // 2
        own, by_x, by_y, far = (total[i * size : (i + 1) * size] for i in range(4))
        left, right = swap(far[:, :cut], "ctx", 2), swap(far[:, cut:], "ctx", 4)
        by_x = jnp.concatenate([by_x[:, :cut], add_low(by_x[:, cut:], right)], axis=1)
        by_y = jnp.concatenate([add_low(by_y[:, :cut], left), by_y[:, cut:]], axis=1)
        own = own.astype(F32) + swap(by_x, "ctx", 2).astype(F32) + swap(by_y, "ctx", 4).astype(F32)
        own = own.astype(BF)
        return add_low(own[: size // 2], swap(own[size // 2 :], "shard", 1))

    w_kv = gather_rows(jnp.concatenate([key_weight, value_weight], axis=1))
    w_q = gather_rows(w_query)
    gains = jnp.concatenate([attn_gain, ffn_gain, query_gain, key_gain])[None]
    spread = jnp.where(jnp.arange(parts)[:, None] == part, gains, jnp.zeros((), BF))
    gains = butterfly(spread, ("ctx", "shard")).astype(F32)
    gain_one = gains[:, :wide].reshape(1, -1)
    gain_two = gains[:, wide : 2 * wide].reshape(1, -1)
    gain_q = gains[:, 2 * wide : 2 * wide + narrow].reshape(1, -1)
    gain_k = gains[:, 2 * wide + narrow :].reshape(1, -1)
    pieces = [w_out.T]
    for at in range(0, units, chunk):
        pieces += [w_gate[:, at : at + chunk], w_up[:, at : at + chunk]]
    w_rest = lax.all_gather(jnp.concatenate(pieces + [w_down.T], axis=1), weight_axes, axis=0, tiled=True)
    source = jnp.bitwise_xor(part, jnp.array(order, jnp.int32))[:, None] * wide + jnp.arange(wide, dtype=jnp.int32)
    to_slots = (jnp.arange(model, dtype=jnp.int32)[:, None] == source.reshape(1, -1)).astype(BF)
    tokens_s = mm(tokens, to_slots).astype(BF)
    gain_one_s = mm(gain_one.astype(BF), to_slots)

    cont_at = me * rows + jnp.arange(rows, dtype=jnp.int32)
    cont_ends = jnp.cumsum(lengths)
    starts = cont_ends - lengths
    seg = jnp.sum((cont_ends[None, :] <= cont_at[:, None]).astype(jnp.int32), axis=1)
    numbers = jnp.arange(lengths.shape[0], dtype=jnp.int32)
    first = jnp.sum(jnp.where(numbers[None, :] == seg[:, None], starts[None, :], 0), axis=1)
    position = jnp.concatenate([me * rows + jnp.arange(rows, dtype=jnp.int32), PROMPT + cont_at - first])
    low = first - me * rows
    low_col = jnp.broadcast_to(low[:, None], (rows, 128))
    low_row = jnp.broadcast_to(jnp.concatenate([low, low])[None, :], (8, 2 * rows))
    scalars = jnp.stack([me, low[0]])
    cos, sin = rotary_tables(position)

    once = lambda f: (0, 0)

    def keys_values(half, gain, whole=None):
        mine = lambda f: (half, 0)
        ins = [
            (tokens_s, (rows, model), mine), (gain, (1, model), once), (w_kv, (model, 2 * k_cols), once),
            (gain_k, (1, HEAD_SIZE), once), (cos, (rows, HEAD_SIZE), mine), (sin, (rows, HEAD_SIZE), mine),
        ]
        keep = {}
        if whole is not None:
            keep = {len(ins): 0}
            ins.append((whole, None, None))
        outs = [
            (shaped((2 * rows, model), BF), (rows, model), mine),
            (shaped((2, rows, k_cols), BF), (2, rows, k_cols), lambda f: (0, 0, 0)),
            (shaped((rows, k_cols), F32), (rows, k_cols), once),
        ]
        return call(functools.partial(kv_kernel, kv_heads), "keys_values", (1,), ins, outs,
                    flops=4 * rows * model * k_cols, moved=8 * MIB, keep=keep)

    normed, kv_p, k_lin_p = keys_values(0, gain_one_s)
    normed, kv_c, k_lin_c = keys_values(1, after(gain_one_s, kv_p), normed)
    mine = lambda f: (f, 0)
    q, q_lin = call(
        functools.partial(q_kernel, heads), "queries", (2,),
        [
            (normed, (rows, model), mine), (w_q, (model, q_cols), lambda f: (0, 0)),
            (gain_q, (1, HEAD_SIZE), lambda f: (0, 0)),
            (cos, (rows, HEAD_SIZE), mine), (sin, (rows, HEAD_SIZE), mine),
        ],
        [(shaped((2 * rows, q_cols), BF), (rows, q_cols), mine), (shaped((2 * rows, q_cols), F32), (rows, q_cols), mine)],
        flops=4 * rows * model * q_cols, moved=12 * MIB,
    )

    def pick(source, wanted):
        return {s: source[s] for s in source if s in wanted}

    near, middle, far = (0, 1), (2, 3, 4, 5), tuple(range(6, ctx_size))
    slots, halos = {0: kv_p}, {0: kv_c}
    odd = (me % 2) == 1
    if ctx_size == 8:
        slots[1], slots[2], slots[4] = (swap(kv_p, "ctx", bit) for bit in (1, 2, 4))
        halos[2] = shift(kv_c, 2)
    else:
        both, bit = kv_p[None], 1
        while bit < ctx_size:
            both = jnp.concatenate([both, swap(both, "ctx", bit)])
            bit *= 2
        slots = {s: both[s] for s in range(ctx_size)}
        halos.update({d: shift(kv_c, d) for d in range(1, n_halo)})
    p_state = attention_forward(0, scalars, q, low_col, pick(slots, near), {})
    if ctx_size == 8:
        two = after(slots[2], p_state[0]), after(slots[4], p_state[0])
        far_k, far_v = swap(two[1][0], "ctx", 2), swap(two[0][1], "ctx", 4)
        slots[3], slots[5] = swap(two[0], "ctx", 1), swap(two[1], "ctx", 1)
    else:
        two = ()
    c_state = attention_forward(
        1, after(scalars, p_state[0], *two), q, low_col, pick(slots, near), pick(halos, (0,))
    )
    c_state = attention_forward(1, after(scalars, c_state[0]), q, low_col, pick(slots, middle), {}, c_state)
    if ctx_size == 8:
        slots[6] = jnp.stack([after(far_k, c_state[0]), after(far_v, c_state[0])])
        slots[7] = swap(slots[6], "ctx", 1)
        halos[1] = swap(jnp.where(odd, after(halos[2], c_state[0]), kv_c), "ctx", 1)
        ready = (slots[6],)
    else:
        ready = ()
    attended, lse_p, part_p = attention_forward(
        0, after(scalars, c_state[0], *ready), q, low_col, pick(slots, middle + far), {}, p_state, (w_rest, None)
    )
    got_p = swap(part_p, "tensor", 1)
    attended, lse_c, part_c = attention_forward(
        1, after(scalars, part_p), q, low_col, pick(slots, far), pick(halos, range(1, n_halo)),
        c_state, (w_rest, attended),
    )
    got_c = swap(part_c, "tensor", 1)

    resid_p, *whole, out_p, back_p = feed_forward(
        0, tokens, part_p, got_p, after(gain_two, part_c), cotangent, w_rest, o_cols, chunk
    )
    back_got_p = swap(back_p, "tensor", 1)
    resid_c, *whole, out_c, back_c = feed_forward(
        1, tokens, part_c, got_c, after(gain_two, back_p), cotangent, w_rest, o_cols, chunk, whole
    )
    back_got_c = swap(back_c, "tensor", 1)
    normed_ffn, hidden, d_gu = whole
    gu_grad = mm(normed_ffn, d_gu, TN).astype(BF)
    down_grad = mm(after(cotangent, gu_grad), hidden, TN).astype(BF)
    d_resid_p, d_mixed, d_att_p, delta_p, d_two_p = mixed_back(
        0, back_p, back_got_p, resid_p, after(gain_two, down_grad), cotangent, w_rest, o_cols, attended
    )
    d_resid_c, d_mixed, d_att_c, delta_c, d_two_c = mixed_back(
        1, back_c, back_got_c, resid_c, after(gain_two, d_att_p), cotangent, w_rest, o_cols, attended, d_mixed
    )
    out_grad = mm(d_mixed, attended, TN).astype(BF)
    rest_grads = jnp.concatenate([out_grad, gu_grad, down_grad], axis=1)
    rest_share = lax.psum_scatter(rest_grads, weight_axes, scatter_dimension=0, tiled=True)
    out_p, out_c = after(out_p, back_got_c), after(out_c, back_got_c)
    out_got_p, out_got_c = swap(out_p, "tensor", 1), swap(out_c, "tensor", 1)

    dq_p, from_p, _ = attention_backward(
        0, after(scalars, rest_grads), q, d_att_p, lse_p, delta_p, low_row, slots, {}
    )

    def back_c_rows(deps, slots, halos, carry, last):
        prior = pick(from_p, tuple(slots)) if slots else None
        return attention_backward(
            1, after(scalars, *deps), q, d_att_c, lse_c, delta_c, low_row, slots, halos, carry, prior, last
        )

    dq_c, _, g_halo = back_c_rows((dq_p,), {}, halos, None, False)
    if ctx_size == 8:
        near_one = swap(g_halo[1], "ctx", 1)
    dq_c, g, _ = back_c_rows((dq_c,), pick(slots, far), {}, dq_c, False)
    zero = jnp.zeros((), BF)
    if ctx_size == 8:
        near_one = after(near_one, dq_c)
        two_back = add_low(g_halo[2], jnp.where(odd, near_one, zero))
        halo_two = shift(two_back, -2)
        got7 = swap(g[7], "ctx", 1)
        ready = (two_back,)
    dq_c, more, _ = back_c_rows((dq_c, *ready), pick(slots, middle), {}, dq_c, False)
    g.update(more)
    if ctx_size == 8:
        g6 = add_low(g[6], after(got7, dq_c))
        far_k, far_v = swap(g6[0], "ctx", 2), swap(g6[1], "ctx", 4)
        got3, got5 = swap(g[3], "ctx", 1), swap(g[5], "ctx", 1)
        ready = (g6,)
    dq_c, more, _ = back_c_rows((dq_c, *ready), pick(slots, near), {}, dq_c, True)
    g.update(more)
    if ctx_size == 8:
        got1 = swap(g[1], "ctx", 1)
        far_k, far_v, got3, got5 = (after(v, dq_c) for v in (far_k, far_v, got3, got5))
        g2 = jnp.stack([add_low(g[2][0], got3[0]), add_low(add_low(g[2][1], got3[1]), far_v)])
        g4 = jnp.stack([add_low(add_low(g[4][0], got5[0]), far_k), add_low(g[4][1], got5[1])])
        got2, got4 = swap(g2, "ctx", 2), swap(g4, "ctx", 4)
        ready = (g2, g4)
        kvs_p = [g[0], got1, got2, got4]
        kvs_c = [g_halo[0], jnp.where(odd, zero, near_one), halo_two]
    else:
        both = jnp.stack([g[s] for s in range(ctx_size)])
        while both.shape[0] > 1:
            size = both.shape[0] // 2
            both = add_low(both[:size], swap(both[size:], "ctx", size))
        kvs_p = [both[0]]
        kvs_c = [g_halo[0]] + [shift(g_halo[d], -d) for d in range(1, n_halo)]

    w_qkv = jnp.concatenate([w_q, w_kv], axis=1)
    w_qkv = mm(to_slots, after(w_qkv, part_p)).astype(BF)
    d_qkv, into_c, heads_c = qkv_back(
        1, dq_c, q_lin, k_lin_c, after(gain_q, dq_c, *ready), gain_k, cos, sin, w_qkv, kvs_c
    )
    into_got_c = swap(into_c, "tensor", 1)
    layer_out = jnp.concatenate(
        [
            (resid + (own.astype(F32) + got.astype(F32))).astype(BF)
            for resid, own, got in ((resid_p, out_p, out_got_p), (resid_c, out_c, after(out_got_c, into_c)))
        ]
    )
    d_qkv, into_p, heads_p = qkv_back(
        0, dq_p, q_lin, k_lin_p, after(gain_q, into_c, layer_out), gain_k, cos, sin, w_qkv, kvs_p, d_qkv
    )
    into_got_p = swap(into_p, "tensor", 1)
    grad_high = mm(normed[:, model // 2 :], after(d_qkv, into_p), TN).astype(BF)
    grad_low = mm(normed[:, : model // 2], after(d_qkv, grad_high), TN).astype(BF)
    qkv_share = scatter_rows(grad_low, grad_high)
    grad_tokens, d_one_c = tokens_back(
        1, into_c, into_got_c, tokens, after(gain_one, grad_low), d_resid_c
    )
    grad_tokens, d_one_p = tokens_back(
        0, into_p, into_got_p, tokens, after(gain_one, d_one_c), d_resid_p, grad_tokens
    )

    model_gains = jnp.concatenate([d_one_c + d_one_p, d_two_c + d_two_p])
    model_gains = butterfly(model_gains, ("ctx", "shard")).reshape(2, parts, wide)
    head_gains = butterfly(heads_c + heads_p, ("ctx", "shard", "tensor")).reshape(2, parts, narrow)
    model_gains = lax.dynamic_index_in_dim(model_gains, part, 1, keepdims=False)
    head_gains = lax.dynamic_index_in_dim(head_gains, part, 1, keepdims=False)

    qkv_share, rest_share = qkv_share.astype(F32), rest_share.astype(F32)
    gate_up = rest_share[:, o_cols : o_cols + 2 * units].reshape(wide, units // chunk, 2, chunk)
    return (
        layer_out,
        grad_tokens,
        model_gains[0],
        model_gains[1],
        head_gains[0],
        head_gains[1],
        qkv_share[:, :q_cols],
        qkv_share[:, q_cols : q_cols + k_cols],
        qkv_share[:, q_cols + k_cols :],
        rest_share[:, :o_cols].T,
        gate_up[:, :, 0].reshape(wide, units),
        gate_up[:, :, 1].reshape(wide, units),
        rest_share[:, o_cols + 2 * units :].T,
    )


def solution(mesh):
    split = ("shard", "ctx")
    rows, gain = P(split, None), P(split)
    into, out_of = P(split, "tensor"), P("tensor", split)
    in_specs = (rows, P("shard", None)) + (gain,) * 4 + (into,) * 3 + (out_of,)
    in_specs += (into, into, out_of, rows)
    out_specs = (rows, rows) + (gain,) * 4 + (into,) * 3 + (out_of, into, into, out_of)
    return jax.shard_map(body, mesh=mesh, in_specs=in_specs, out_specs=out_specs, check_vma=False)
```

```python
import functools
import math

import jax
import jax.numpy as jnp
from jax import lax
from jax.experimental import pallas as pl
from jax.experimental.pallas import tpu as pltpu
from jax.sharding import PartitionSpec as P

HEAD_SIZE = 128
PROMPT = 4096
CONT_TOK = 4096
LONGEST = 1024

EPSILON = 1e-06
ROPE_BASE = 1000000.0
MASKED = -1e30
LOG2E = math.log2(math.e)
LN2 = math.log(2.0)
SCALE = 1.0 / math.sqrt(HEAD_SIZE)

BF = jnp.bfloat16
F32 = jnp.float32
NN = (((1,), (0,)), ((), ()))
NT = (((1,), (1,)), ((), ()))
TN = (((0,), (0,)), ((), ()))
MIB = 2**20


def mm(left, right, dims=NN):
    return lax.dot_general(left, right, dims, preferred_element_type=F32)


def shaped(dims, kind):
    return jax.ShapeDtypeStruct(dims, kind)


def call(kernel, name, grid, ins, outs, scratch=(), vmem=56, scalars=None, keep=None):
    in_specs, arrays = [], []
    for array, block, index in ins:
        arrays.append(array)
        in_specs.append(pl.BlockSpec(memory_space=pl.ANY) if block is None else pl.BlockSpec(block, index))
    lead = 0 if scalars is None else 1
    return pl.pallas_call(
        kernel,
        grid_spec=pltpu.PrefetchScalarGridSpec(
            num_scalar_prefetch=lead,
            grid=grid,
            in_specs=in_specs,
            out_specs=[pl.BlockSpec(block, index) for _, block, index in outs],
            scratch_shapes=list(scratch),
        ),
        out_shape=[shape for shape, _, _ in outs],
        input_output_aliases={a + lead: b for a, b in (keep or {}).items()},
        compiler_params=pltpu.CompilerParams(vmem_limit_bytes=vmem * MIB),
        cost_estimate=pl.CostEstimate(flops=1, bytes_accessed=1, transcendentals=0),
        name=name,
    )(*([] if scalars is None else [scalars]), *arrays)


def rms(values):
    return lax.rsqrt(jnp.mean(values * values, axis=-1, keepdims=True) + EPSILON)


def turn(values, cos, sin):
    return values * cos + pltpu.roll(values, HEAD_SIZE // 2, 1) * sin


def turn_back(values, cos, sin):
    return values * cos - pltpu.roll(values, HEAD_SIZE // 2, 1) * sin


def kv_kernel(heads, x_ref, gain_ref, w_ref, hgain_ref, cos_ref, sin_ref, *refs):
    normed_ref, kv_ref, lin_ref = refs[-3:]
    x = x_ref[...].astype(F32)
    normed_ref[...] = (x * rms(x) * gain_ref[...]).astype(BF)
    both = mm(normed_ref[...], w_ref[...])
    width = heads * HEAD_SIZE
    kv_ref[1] = both[:, width:].astype(BF)
    for h in range(heads):
        cols = slice(h * HEAD_SIZE, (h + 1) * HEAD_SIZE)
        lin = both[:, cols]
        lin_ref[:, cols] = lin
        kv_ref[0, :, cols] = turn(lin * rms(lin) * hgain_ref[...], cos_ref[...], sin_ref[...]).astype(BF)


def q_kernel(heads, normed_ref, w_ref, hgain_ref, cos_ref, sin_ref, q_ref, lin_ref):
    both = mm(normed_ref[...], w_ref[...])
    for h in range(heads):
        cols = slice(h * HEAD_SIZE, (h + 1) * HEAD_SIZE)
        lin = both[:, cols]
        lin_ref[:, cols] = lin
        turned = turn(lin * rms(lin) * hgain_ref[...], cos_ref[...], sin_ref[...])
        q_ref[:, cols] = (turned * (SCALE * LOG2E)).astype(BF)


def by_top_bit(slots):
    groups = {}
    for at, s in enumerate(slots):
        if s:
            groups.setdefault(1 << (s.bit_length() - 1), []).append(at)
    return groups


def fwd_kernel(plan, idx_ref, lo_ref, *refs):
    halves, slots, halos = plan["halves"], plan["slots"], plan["halos"]
    refs = list(refs)
    q_refs = [refs.pop(0) for _ in halves]
    slot_refs = [refs.pop(0) for _ in slots]
    halo_refs = [refs.pop(0) for _ in halos]
    prior = [refs.pop(0) for _ in range(2)] if plan["carry"] else None
    if plan["last"]:
        w_ref = refs.pop(0)
        if plan["alias"]:
            refs.pop(0)
        out_ref, lse_ref, part_ref = refs[:3]
        refs = refs[3:]
    else:
        results, refs = refs[: 2 * len(halves)], refs[2 * len(halves) :]
    me, lo_first = idx_ref[0], idx_ref[1]
    rows = q_refs[0].shape[0]
    row = lax.broadcasted_iota(jnp.int32, (2 * rows, 1), 0)
    row = jnp.where(row >= rows, row - rows, row)
    col = lax.broadcasted_iota(jnp.int32, (1, rows), 1)
    for n, half in enumerate(halves):
        qs, acc, tot = refs[3 * n : 3 * n + 3]
        for g in range(2):
            cols, at = slice(g * HEAD_SIZE, (g + 1) * HEAD_SIZE), slice(g * rows, (g + 1) * rows)
            qs[at, :] = q_refs[n][:, cols]
            if prior is not None:
                acc[at, :] = prior[0][:, cols]
                tot[at, :] = prior[1][:, cols]
        empty = [prior is None]

        def add(kv_ref, mask=None):
            scores = mm(qs[...], kv_ref[0], NT)
            if mask is not None:
                scores = jnp.where(mask, scores, MASKED)
            weights = jnp.exp2(scores)
            total = weights[:, :128]
            for at in range(128, weights.shape[1], 128):
                total = total + weights[:, at : at + 128]
            part = mm(weights.astype(BF), kv_ref[1])
            if empty[0]:
                acc[...] = part
                tot[...] = total
            else:
                acc[...] += part
                tot[...] += total
            empty[0] = False

        if half == 1:
            for kv_ref in slot_refs:
                add(kv_ref)
            low = jnp.concatenate([lo_ref[:, :1], lo_ref[:, :1]])
            for d, kv_ref in zip(halos, halo_refs):
                if d == 0:
                    add(kv_ref, (col <= row) & (col >= low))
                else:

                    @pl.when(lo_first < -(d - 1) * rows)
                    def _(d=d, kv_ref=kv_ref):
                        add(kv_ref, col - d * rows >= low)

        else:
            if 0 in slots:
                add(slot_refs[slots.index(0)], col <= row)
            for bit, group in by_top_bit(slots).items():

                @pl.when(jnp.bitwise_and(me, bit) != 0)
                def _(group=group):
                    for at in group:
                        add(slot_refs[at])

        if not plan["last"]:
            for g in range(2):
                cols, at = slice(g * HEAD_SIZE, (g + 1) * HEAD_SIZE), slice(g * rows, (g + 1) * rows)
                results[2 * n][:, cols] = acc[at, :]
                results[2 * n + 1][:, cols] = tot[at, :]
    if plan["last"]:
        qs, acc, tot, part_acc = refs
        step, steps = pl.program_id(0), pl.num_programs(0)
        for g in range(2):
            cols, at = slice(g * HEAD_SIZE, (g + 1) * HEAD_SIZE), slice(g * rows, (g + 1) * rows)
            total = jnp.sum(tot[at, :], axis=1, keepdims=True)
            out_ref[:, cols] = (acc[at, :] / total).astype(BF)
            lse_ref[0, g : g + 1, :] = jnp.log2(jnp.sum(tot[at, :].T, axis=0, keepdims=True))
        part = mm(out_ref[...], w_ref[...], NT)

        @pl.when(step == 0)
        def _():
            part_acc[...] = part

        @pl.when((step > 0) & (step < steps - 1))
        def _():
            part_acc[...] += part

        @pl.when(step == steps - 1)
        def _():
            part_ref[...] = (part_acc[...] + part).astype(BF)


def attention_forward(halves, scalars, q, low, slots, halos, carry=None, last=None):
    rows, heads = q.shape[0] // 2, q.shape[1] // 256
    plan = dict(halves=halves, slots=list(slots), halos=list(halos), carry=carry is not None,
                last=last is not None, alias=last is not None and last[1] is not None)
    part = lambda h, i: (0, h)
    ins = [(low, (rows, 128), lambda h, i: (0, 0))]
    ins += [(q, (rows, 256), lambda h, i, half=half: (half, h)) for half in halves]
    for kv in list(slots.values()) + list(halos.values()):
        ins.append((kv, (2, rows, 128), lambda h, i: (0, 0, h)))
    if carry is not None:
        ins += [(c, (rows, 256), part) for c in carry]
    scratch, keep = [], {}
    for _ in halves:
        scratch += [pltpu.VMEM((2 * rows, 128), BF)] + [pltpu.VMEM((2 * rows, 128), F32)] * 2
    state = shaped((rows, heads * 256), F32)
    if last is None:
        outs = [(state, (rows, 256), part)] * (2 * len(halves))
    else:
        w_rest, other = last
        model = w_rest.shape[0]
        ins.append((w_rest, (model, 256), part))
        if other is not None:
            keep = {len(ins): 0}
            ins.append((other, None, None))
        half = halves[0]
        outs = [
            (shaped((2 * rows, heads * 256), BF), (rows, 256), lambda h, i: (half, h)),
            (shaped((heads, 8, rows), F32), (1, 8, rows), lambda h, i: (h, 0, 0)),
            (shaped((rows, model), BF), (rows, model), lambda h, i: (0, 0)),
        ]
        scratch.append(pltpu.VMEM((rows, model), F32))
    return call(functools.partial(fwd_kernel, plan), "attend", (heads,), ins, outs, scratch,
                scalars=scalars, keep=keep)


def bwd_kernel(plan, idx_ref, q_ref, do_ref, lse_ref, delta_ref, lo_ref, *refs):
    half, slots, halos = plan["half"], plan["slots"], plan["halos"]
    refs = list(refs)
    slot_refs = [refs.pop(0) for _ in slots]
    halo_refs = [refs.pop(0) for _ in halos]
    prior_dq = refs.pop(0) if plan["carry"] else None
    prior = [refs.pop(0) for _ in slots] if plan["sum"] else None
    dq_ref = refs.pop(0)
    slot_outs = [refs.pop(0) for _ in slots]
    halo_outs = [refs.pop(0) for _ in halos]
    qs, dos, lses, deltas, dq = refs
    me, lo_first = idx_ref[0], idx_ref[1]
    rows = q_ref.shape[0]
    for g in range(2):
        cols, at = slice(g * HEAD_SIZE, (g + 1) * HEAD_SIZE), slice(g * rows, (g + 1) * rows)
        qs[at, :] = q_ref[:, cols]
        dos[at, :] = do_ref[:, cols]
        lses[:, at] = lse_ref[0, g : g + 1, :]
        deltas[:, at] = delta_ref[0, g : g + 1, :]
    dq[...] = jnp.zeros_like(dq) if prior_dq is None else prior_dq[...]

    def block(kv_ref, out_ref, mask=None, before=None):
        keys = kv_ref[0]
        scores = mm(keys, qs[...], NT)
        dp = mm(kv_ref[1], dos[...], NT)
        scores = scores - lses[...]
        if mask is not None:
            scores = jnp.where(mask, scores, MASKED)
        probs = jnp.exp2(scores)
        ds = (probs * (dp - deltas[...])).astype(BF)
        dq[...] += mm(keys.T, ds)
        dk, dv = mm(ds, qs[...]) * LN2, mm(probs.astype(BF), dos[...])
        if before is not None:
            dk, dv = dk + before[0].astype(F32), dv + before[1].astype(F32)
        out_ref[0] = dk.astype(BF)
        out_ref[1] = dv.astype(BF)

    lane = lax.broadcasted_iota(jnp.int32, (1, 2 * rows), 1)
    lane = jnp.where(lane >= rows, lane - rows, lane)
    key = lax.broadcasted_iota(jnp.int32, (rows, 1), 0)

    def when(needed, kv_ref, out_ref, mask=None):
        @pl.when(needed)
        def _():
            block(kv_ref, out_ref, mask)

        @pl.when(jnp.logical_not(needed))
        def _():
            out_ref[...] = jnp.zeros_like(out_ref)

    low = lo_ref[:1, :]
    for d, kv_ref, out_ref in zip(halos, halo_refs, halo_outs):
        if d == 0:
            block(kv_ref, out_ref, (key <= lane) & (key >= low))
        else:
            when(lo_first < -(d - 1) * rows, kv_ref, out_ref, key - d * rows >= low)
    if half == 1:
        for at in range(len(slots)):
            block(slot_refs[at], slot_outs[at], None, prior[at])
    else:
        if 0 in slots:
            at = slots.index(0)
            block(slot_refs[at], slot_outs[at], key <= lane)
        for bit, group in by_top_bit(slots).items():

            @pl.when(jnp.bitwise_and(me, bit) != 0)
            def _(group=group):
                for at in group:
                    block(slot_refs[at], slot_outs[at])

            @pl.when(jnp.bitwise_and(me, bit) == 0)
            def _(group=group):
                for at in group:
                    slot_outs[at][...] = jnp.zeros_like(slot_outs[at])

    if plan["last"]:
        for g in range(2):
            cols = slice(g * HEAD_SIZE, (g + 1) * HEAD_SIZE)
            dq_ref[:, cols] = dq[:, g * rows : (g + 1) * rows].T * SCALE
    else:
        dq_ref[...] = dq[...]


def attention_backward(half, scalars, q, do, lse, delta, low, slots, halos, carry=None, prior=None, last=True):
    rows, heads = q.shape[0] // 2, q.shape[1] // 256
    plan = dict(half=half, slots=list(slots), halos=list(halos), carry=carry is not None,
                sum=prior is not None, last=last)
    part = lambda h, i: (0, h)
    stat = lambda h, i: (h, 0, 0)
    kv_map = lambda h, i: (0, 0, h)
    ins = [
        (q, (rows, 256), lambda h, i: (half, h)),
        (do, (rows, 256), part),
        (lse, (1, 8, rows), stat),
        (delta, (1, 8, rows), stat),
        (low, (8, 2 * rows), lambda h, i: (0, 0)),
    ]
    pieces = list(slots.values()) + list(halos.values())
    ins += [(kv, (2, rows, 128), kv_map) for kv in pieces]
    if carry is not None:
        ins.append((carry, (128, 2 * rows), lambda h, i: (h, 0)))
    if prior is not None:
        ins += [(prior[s], (2, rows, 128), kv_map) for s in slots]
    if last:
        outs = [(shaped((rows, heads * 256), F32), (rows, 256), part)]
    else:
        outs = [(shaped((heads * 128, 2 * rows), F32), (128, 2 * rows), lambda h, i: (h, 0))]
    outs += [(shaped(kv.shape, BF), (2, rows, 128), kv_map) for kv in pieces]
    scratch = [
        pltpu.VMEM((2 * rows, 128), BF),
        pltpu.VMEM((2 * rows, 128), BF),
        pltpu.VMEM((1, 2 * rows), F32),
        pltpu.VMEM((1, 2 * rows), F32),
        pltpu.VMEM((128, 2 * rows), F32),
    ]
    blocks = len(slots) * (2 if half else 1) + len(halos)
    pairs = heads * rows * rows * blocks
    results = call(functools.partial(bwd_kernel, plan), "attend_back", (heads,), ins, outs, scratch, scalars=scalars)
    n = len(slots)
    return results[0], dict(zip(slots, results[1 : 1 + n])), dict(zip(halos, results[1 + n :]))


def ffn_kernel(x_ref, own_ref, got_ref, gain_ref, dy_ref, gu_ref, down_ref, *refs):
    resid_ref, normed_ref, hidden_ref, dgu_ref, out_ref, back_ref, normed, out_acc, back_acc = refs[-9:]
    step, steps = pl.program_id(0), pl.num_programs(0)

    @pl.when(step == 0)
    def _():
        resid = x_ref[...].astype(F32) + (own_ref[...].astype(F32) + got_ref[...].astype(F32))
        resid_ref[...] = resid
        normed[...] = (resid * rms(resid) * gain_ref[...]).astype(BF)
        normed_ref[...] = normed[...]
        out_acc[...] = jnp.zeros_like(out_acc)
        back_acc[...] = jnp.zeros_like(back_acc)

    wide = down_ref.shape[1]
    both = mm(normed[...], gu_ref[...])
    d_hidden = mm(dy_ref[...], down_ref[...])
    gate, up = both[:, :wide], both[:, wide:]
    sig = 1.0 / (1.0 + jnp.exp(-gate))
    silu = gate * sig
    hidden = (silu * up).astype(BF)
    hidden_ref[...] = hidden
    d_up = (d_hidden * silu).astype(BF)
    d_gate = (d_hidden * up * (sig + silu * (1.0 - sig))).astype(BF)
    dgu_ref[:, :wide] = d_gate
    dgu_ref[:, wide:] = d_up
    out_acc[...] += mm(hidden, down_ref[...], NT)
    back_acc[...] += mm(dgu_ref[...], gu_ref[...], NT)

    @pl.when(step == steps - 1)
    def _():
        out_ref[...] = out_acc[...].astype(BF)
        back_ref[...] = back_acc[...].astype(BF)


def feed_forward(half, x, own, got, gain, dy, w_rest, o_cols, chunk, whole=None):
    rows, model = own.shape
    units = (w_rest.shape[1] - o_cols) // 3
    steps = units // chunk
    mine, once = lambda f: (half, 0), lambda f: (0, 0)
    at_gu, at_down = o_cols // (2 * chunk), (o_cols + 2 * units) // chunk
    block = (rows, model)
    ins = [
        (x, block, mine), (own, block, once), (got, block, once), (gain, (1, model), once), (dy, block, mine),
        (w_rest, (model, 2 * chunk), lambda f: (0, at_gu + f)),
        (w_rest, (model, chunk), lambda f: (0, at_down + f)),
    ]
    keep = {}
    if whole is not None:
        keep = {len(ins) + i: 1 + i for i in range(3)}
        ins += [(array, None, None) for array in whole]
    outs = [
        (shaped((rows, model), F32), block, once),
        (shaped((2 * rows, model), BF), block, mine),
        (shaped((2 * rows, units), BF), (rows, chunk), lambda f: (half, f)),
        (shaped((2 * rows, 2 * units), BF), (rows, 2 * chunk), lambda f: (half, f)),
        (shaped((rows, model), BF), block, once),
        (shaped((rows, model), BF), block, once),
    ]
    scratch = [pltpu.VMEM(block, BF), pltpu.VMEM(block, F32), pltpu.VMEM(block, F32)]
    return call(ffn_kernel, "feed_forward", (steps,), ins, outs, scratch, keep=keep)


def norm_back(grad, values, gain):
    scale = rms(values)
    unit = values * scale
    inner = grad * gain
    return scale * (inner - unit * jnp.mean(inner * unit, axis=-1, keepdims=True)), grad * unit


def row_blocks(rows):
    size = rows // 2 if rows % 512 == 0 else rows
    return size, rows // size


def add_up(ref, value):
    total = jnp.sum(value, axis=0, keepdims=True)

    @pl.when(pl.program_id(0) == 0)
    def _():
        ref[...] = total

    @pl.when(pl.program_id(0) > 0)
    def _():
        ref[...] += total


def mixed_kernel(heads, own_ref, got_ref, resid_ref, gain_ref, dy_ref, w_ref, att_ref, *refs):
    d_resid_ref, mixed_ref, datt_ref, delta_ref, dgain_ref = refs[-5:]
    grad = own_ref[...].astype(F32) + got_ref[...].astype(F32)
    d_norm, summand = norm_back(grad, resid_ref[...], gain_ref[...])
    add_up(dgain_ref, summand)
    d_resid = dy_ref[...].astype(F32) + d_norm
    d_resid_ref[...] = d_resid
    mixed_ref[...] = d_resid.astype(BF)
    datt_ref[...] = mm(mixed_ref[...], w_ref[...]).astype(BF)
    for h in range(heads):
        cols = slice(h * HEAD_SIZE, (h + 1) * HEAD_SIZE)
        product = datt_ref[:, cols].astype(F32) * att_ref[:, cols].astype(F32)
        delta_ref[h // 2, h % 2 : h % 2 + 1, :] = jnp.sum(product.T, axis=0, keepdims=True)


def mixed_back(half, own, got, resid, gain, dy, w_rest, o_cols, attended, whole=None):
    rows, model = own.shape
    heads = o_cols // HEAD_SIZE
    size, steps = row_blocks(rows)
    mine, here, once = lambda f: (half * steps + f, 0), lambda f: (f, 0), lambda f: (0, 0)
    block = (size, model)
    ins = [
        (own, block, here), (got, block, here), (resid, block, here), (gain, (1, model), once),
        (dy, block, mine), (w_rest, (model, o_cols), once), (attended, (size, o_cols), mine),
    ]
    keep = {}
    if whole is not None:
        keep = {len(ins): 1}
        ins.append((whole, None, None))
    outs = [
        (shaped((rows, model), F32), block, here),
        (shaped((2 * rows, model), BF), block, mine),
        (shaped((rows, o_cols), BF), (size, o_cols), here),
        (shaped((heads // 2, 8, rows), F32), (heads // 2, 8, size), lambda f: (0, 0, f)),
        (shaped((1, model), F32), (1, model), once),
    ]
    return call(functools.partial(mixed_kernel, heads), "mixed_back", (steps,), ins, outs, keep=keep)


def weight_kernel(left_ref, right_ref, *refs):
    refs[-1][...] = mm(left_ref[...], right_ref[...], TN).astype(BF)


def weight_grad(left, right, at, width, cols, whole=None):
    tokens, model = left.shape
    n = right.shape[1]
    ins = [(left, (tokens, model), lambda j: (0, 0)), (right, (tokens, cols), lambda j: (0, j))]
    keep = {}
    if whole is not None:
        keep = {len(ins): 0}
        ins.append((whole, None, None))
    outs = [(shaped((model, width), BF), (model, cols), lambda j: (0, at // cols + j))]
    return call(weight_kernel, "weight_grad", (n // cols,), ins, outs, keep=keep)[0]


def q_back_kernel(heads, dq_ref, lin_ref, gain_ref, cos_ref, sin_ref, w_ref, *refs):
    d_ref, part_ref, gains_ref = refs[-3:]
    cos, sin = cos_ref[...], sin_ref[...]
    total = jnp.zeros(cos.shape, F32)
    for h in range(heads):
        cols = slice(h * HEAD_SIZE, (h + 1) * HEAD_SIZE)
        grad, summand = norm_back(turn_back(dq_ref[:, cols], cos, sin), lin_ref[:, cols], gain_ref[...])
        d_ref[:, cols] = grad.astype(BF)
        total = total + summand
    part_ref[...] = mm(d_ref[...], w_ref[...], NT)
    add_up(gains_ref, total)


def q_back(half, dq, lin, gain, cos, sin, w, whole=None):
    rows, cols = dq.shape
    model = w.shape[0]
    size, steps = row_blocks(rows)
    mine, here, once = lambda f: (half * steps + f, 0), lambda f: (f, 0), lambda f: (0, 0)
    ins = [
        (dq, (size, cols), here), (lin, (size, cols), mine), (gain, (1, HEAD_SIZE), once),
        (cos, (size, HEAD_SIZE), mine), (sin, (size, HEAD_SIZE), mine), (w, (model, cols), once),
    ]
    keep = {}
    if whole is not None:
        keep = {len(ins): 0}
        ins.append((whole, None, None))
    outs = [
        (shaped((2 * rows, cols), BF), (size, cols), mine),
        (shaped((rows, model), F32), (size, model), here),
        (shaped((1, HEAD_SIZE), F32), (1, HEAD_SIZE), once),
    ]
    kernel = functools.partial(q_back_kernel, cols // HEAD_SIZE)
    return call(kernel, "q_back", (steps,), ins, outs, keep=keep)


def kv_back_kernel(heads, n_keys, n_values, lin_ref, gain_ref, cos_ref, sin_ref, w_ref, q_part_ref, *refs):
    key_refs, value_refs = refs[:n_keys], refs[n_keys : n_keys + n_values]
    d_ref, part_ref, gains_ref = refs[-3:]
    cos, sin = cos_ref[...], sin_ref[...]
    width = heads * HEAD_SIZE

    def total(sources, which, cols):
        value = None
        for ref in sources:
            piece = ref[which, :, cols] if len(ref.shape) == 3 else ref[:, cols]
            value = piece.astype(F32) if value is None else value + piece.astype(F32)
        return value

    gains = jnp.zeros(cos.shape, F32)
    for h in range(heads):
        cols = slice(h * HEAD_SIZE, (h + 1) * HEAD_SIZE)
        grad, summand = norm_back(
            turn_back(total(key_refs, 0, cols), cos, sin), lin_ref[:, cols], gain_ref[...]
        )
        d_ref[:, cols] = grad.astype(BF)
        gains = gains + summand
    d_ref[:, width:] = total(value_refs, 1, slice(None)).astype(BF)
    part_ref[...] = (q_part_ref[...] + mm(d_ref[...], w_ref[...], NT)).astype(BF)
    add_up(gains_ref, gains)


def kv_back(half, keys, values, lin, gain, cos, sin, w, q_part, whole=None):
    rows, cols = lin.shape
    model = w.shape[0]
    size, steps = row_blocks(rows)
    mine, here, once = lambda f: (half * steps + f, 0), lambda f: (f, 0), lambda f: (0, 0)
    ins = [
        (lin, (size, cols), here), (gain, (1, HEAD_SIZE), once), (cos, (size, HEAD_SIZE), mine),
        (sin, (size, HEAD_SIZE), mine), (w, (model, 2 * cols), once), (q_part, (size, model), here),
    ]
    for piece in list(keys) + list(values):
        if piece.ndim == 3:
            ins.append((piece, (2, size, cols), lambda f: (0, f, 0)))
        else:
            ins.append((piece, (size, cols), here))
    keep = {}
    if whole is not None:
        keep = {len(ins): 0}
        ins.append((whole, None, None))
    outs = [
        (shaped((2 * rows, 2 * cols), BF), (size, 2 * cols), mine),
        (shaped((rows, model), BF), (size, model), here),
        (shaped((1, HEAD_SIZE), F32), (1, HEAD_SIZE), once),
    ]
    kernel = functools.partial(kv_back_kernel, cols // HEAD_SIZE, len(keys), len(values))
    return call(kernel, "kv_back", (steps,), ins, outs, keep=keep)


def tokens_kernel(own_ref, got_ref, x_ref, gain_ref, d_resid_ref, *refs):
    out_ref, dgain_ref = refs[-2:]
    grad = own_ref[...].astype(F32) + got_ref[...].astype(F32)
    d_norm, summand = norm_back(grad, x_ref[...].astype(F32), gain_ref[...])
    add_up(dgain_ref, summand)
    out_ref[...] = (d_resid_ref[...] + d_norm).astype(BF)


def tokens_back(half, own, got, x, gain, d_resid, whole=None):
    rows, model = own.shape
    size, steps = row_blocks(rows)
    mine, here, once = lambda f: (half * steps + f, 0), lambda f: (f, 0), lambda f: (0, 0)
    block = (size, model)
    ins = [(own, block, here), (got, block, here), (x, block, mine), (gain, (1, model), once), (d_resid, block, here)]
    keep = {}
    if whole is not None:
        keep = {len(ins): 0}
        ins.append((whole, None, None))
    outs = [(shaped((2 * rows, model), BF), block, mine), (shaped((1, model), F32), (1, model), once)]
    return call(tokens_kernel, "tokens_back", (steps,), ins, outs, keep=keep)


def swap(value, axis, bit):
    size = lax.axis_size(axis)
    return lax.ppermute(value, axis, [(i, i ^ bit) for i in range(size)])


def shift(value, by):
    size = lax.axis_size("ctx")
    return lax.ppermute(value, "ctx", [(i, i + by) for i in range(size) if 0 <= i + by < size])


def add_low(left, right):
    return (left.astype(F32) + right.astype(F32)).astype(BF)


def butterfly(value, axes):
    for axis in axes:
        bit = 1
        while bit < lax.axis_size(axis):
            value = value + swap(value, axis, bit)
            bit *= 2
    return value


def after(value, *others):
    return lax.optimization_barrier((value, *others))[0]


def rotary_tables(position):
    half_dim = HEAD_SIZE // 2
    inverse_freq = jnp.exp(jnp.arange(half_dim, dtype=F32) * (-math.log(ROPE_BASE) / half_dim))
    angles = position.astype(F32)[:, None] * inverse_freq[None, :]
    cosine, sine = jnp.cos(angles), jnp.sin(angles)
    return jnp.concatenate([cosine, cosine], axis=-1), jnp.concatenate([-sine, sine], axis=-1)


def body(
    tokens,
    cont_lengths,
    attn_gain,
    ffn_gain,
    query_gain,
    key_gain,
    w_query,
    key_weight,
    value_weight,
    w_out,
    w_gate,
    w_up,
    w_down,
    cotangent,
):
    ctx_size = lax.axis_size("ctx")
    weight_axes = ("shard", "ctx")
    parts = lax.axis_size("shard") * ctx_size
    me = lax.axis_index("ctx")
    part = lax.axis_index("shard") * ctx_size + me
    rows, model = tokens.shape[0] // 2, tokens.shape[1]
    n_halo = 1 + -(-(LONGEST - 1) // rows)
    lengths = cont_lengths[0]

    bits = [("shard", 1)] + [("ctx", 1 << i) for i in range(1, ctx_size.bit_length() - 1)] + [("ctx", 1)]
    order = [0]
    for axis, bit in bits:
        order += [j ^ (bit * ctx_size if axis == "shard" else bit) for j in order]
    wide, narrow = attn_gain.shape[0], query_gain.shape[0]
    q_cols, k_cols = w_query.shape[1], key_weight.shape[1]
    o_cols, units = w_out.shape[0], w_gate.shape[1]
    heads, kv_heads = q_cols // HEAD_SIZE, k_cols // HEAD_SIZE
    chunk = math.gcd(units, 512)

    def gather_rows(piece):
        if ctx_size != 8:
            for axis, bit in bits:
                piece = jnp.concatenate([piece, swap(piece, axis, bit)])
            return piece, piece
        piece = jnp.concatenate([piece, swap(piece, "shard", 1)])
        by_x, by_y = swap(piece, "ctx", 2), swap(piece, "ctx", 4)
        cut = piece.shape[1] // 2
        far = jnp.concatenate([swap(by_y[:, :cut], "ctx", 2), swap(by_x[:, cut:], "ctx", 4)], axis=1)
        half = jnp.concatenate([piece, by_x, by_y, far])
        return jnp.concatenate([half, swap(half, "ctx", 1)]), piece

    def scatter_rows(low, high, late):
        total = add_low(low, after(swap(high, "ctx", 1), late))
        if ctx_size != 8:
            for axis, bit in bits[-2:0:-1]:
                size = total.shape[0] // 2
                total = add_low(total[:size], swap(total[size:], axis, bit))
            return (total,)
        size, cut = total.shape[0] // 4, total.shape[1] // 2
        own, by_x, by_y, far = (total[i * size : (i + 1) * size] for i in range(4))
        left, right = swap(far[:, :cut], "ctx", 2), swap(far[:, cut:], "ctx", 4)
        return own, by_x, by_y, left, right

    def scatter_more(stage, late):
        if ctx_size != 8:
            return stage
        own, by_x, by_y, left, right = stage
        left, right = after(left, late), after(right, late)
        cut = left.shape[1]
        by_x = jnp.concatenate([by_x[:, :cut], add_low(by_x[:, cut:], right)], axis=1)
        by_y = jnp.concatenate([add_low(by_y[:, :cut], left), by_y[:, cut:]], axis=1)
        return own, swap(by_x, "ctx", 2), swap(by_y, "ctx", 4)

    def scatter_last(stage):
        total = stage[0].astype(F32)
        for piece in stage[1:]:
            total = total + piece.astype(F32)
        total, size = total.astype(BF), total.shape[0] // 2
        return add_low(total[:size], swap(total[size:], "shard", 1))

    w_kv, first_piece = gather_rows(jnp.concatenate([key_weight, value_weight], axis=1))
    gains = jnp.concatenate([attn_gain, ffn_gain, query_gain, key_gain])[None]
    spread = jnp.where(jnp.arange(parts)[:, None] == part, gains, jnp.zeros((), BF))
    gains = butterfly(after(spread, first_piece), ("ctx", "shard")).astype(F32)
    gain_one = gains[:, :wide].reshape(1, -1)
    gain_two = gains[:, wide : 2 * wide].reshape(1, -1)
    gain_q = gains[:, 2 * wide : 2 * wide + narrow].reshape(1, -1)
    gain_k = gains[:, 2 * wide + narrow :].reshape(1, -1)
    w_q, _ = gather_rows(after(w_query, first_piece))
    pieces = [after(w_out, first_piece).T]
    for at in range(0, units, chunk):
        pieces += [w_gate[:, at : at + chunk], w_up[:, at : at + chunk]]
    w_rest = lax.all_gather(jnp.concatenate(pieces + [w_down.T], axis=1), weight_axes, axis=0, tiled=True)
    source = jnp.bitwise_xor(part, jnp.array(order, jnp.int32))[:, None] * wide + jnp.arange(wide, dtype=jnp.int32)
    to_slots = (jnp.arange(model, dtype=jnp.int32)[:, None] == source.reshape(1, -1)).astype(BF)
    tokens_s = mm(after(tokens, first_piece), to_slots).astype(BF)
    gain_one_s = mm(gain_one.astype(BF), to_slots)

    cont_at = me * rows + jnp.arange(rows, dtype=jnp.int32)
    cont_ends = jnp.cumsum(lengths)
    starts = cont_ends - lengths
    seg = jnp.sum((cont_ends[None, :] <= cont_at[:, None]).astype(jnp.int32), axis=1)
    numbers = jnp.arange(lengths.shape[0], dtype=jnp.int32)
    first = jnp.sum(jnp.where(numbers[None, :] == seg[:, None], starts[None, :], 0), axis=1)
    position = jnp.concatenate([me * rows + jnp.arange(rows, dtype=jnp.int32), PROMPT + cont_at - first])
    low = first - me * rows
    low_col = jnp.broadcast_to(low[:, None], (rows, 128))
    low_row = jnp.broadcast_to(jnp.concatenate([low, low])[None, :], (8, 2 * rows))
    scalars = jnp.stack([me, low[0]])
    cos, sin = rotary_tables(position)

    once = lambda f: (0, 0)

    def keys_values(half, gain, whole=None):
        mine = lambda f: (half, 0)
        ins = [
            (tokens_s, (rows, model), mine), (gain, (1, model), once), (w_kv, (model, 2 * k_cols), once),
            (gain_k, (1, HEAD_SIZE), once), (cos, (rows, HEAD_SIZE), mine), (sin, (rows, HEAD_SIZE), mine),
        ]
        keep = {}
        if whole is not None:
            keep = {len(ins): 0}
            ins.append((whole, None, None))
        outs = [
            (shaped((2 * rows, model), BF), (rows, model), mine),
            (shaped((2, rows, k_cols), BF), (2, rows, k_cols), lambda f: (0, 0, 0)),
            (shaped((rows, k_cols), F32), (rows, k_cols), once),
        ]
        return call(functools.partial(kv_kernel, kv_heads), "keys_values", (1,), ins, outs, keep=keep)

    normed, kv_p, k_lin_p = keys_values(0, gain_one_s)
    normed, kv_c, k_lin_c = keys_values(1, after(gain_one_s, kv_p), normed)
    mine = lambda f: (f, 0)
    q, q_lin = call(
        functools.partial(q_kernel, heads), "queries", (2,),
        [
            (normed, (rows, model), mine), (w_q, (model, q_cols), lambda f: (0, 0)),
            (gain_q, (1, HEAD_SIZE), lambda f: (0, 0)),
            (cos, (rows, HEAD_SIZE), mine), (sin, (rows, HEAD_SIZE), mine),
        ],
        [(shaped((2 * rows, q_cols), BF), (rows, q_cols), mine), (shaped((2 * rows, q_cols), F32), (rows, q_cols), mine)],
    )

    def pick(source, wanted):
        return {s: source[s] for s in source if s in wanted}

    near, middle, far = (0, 1), (2, 3, 4, 5), tuple(range(6, ctx_size))
    slots, halos = {0: kv_p}, {0: kv_c}
    odd = (me % 2) == 1
    if ctx_size == 8:
        slots[1], slots[2], slots[4] = (swap(kv_p, "ctx", bit) for bit in (1, 2, 4))
        halos[2] = shift(kv_c, 2)
    else:
        both, bit = kv_p[None], 1
        while bit < ctx_size:
            both = jnp.concatenate([both, swap(both, "ctx", bit)])
            bit *= 2
        slots = {s: both[s] for s in range(ctx_size)}
        halos.update({d: shift(kv_c, d) for d in range(1, n_halo)})
    *p_state, c_acc, c_tot = attention_forward(
        (0, 1), scalars, q, low_col, pick(slots, near), pick(halos, (0,))
    )
    ready = ()
    if ctx_size == 8:
        two = after(slots[2], q), after(slots[4], q)
        far_k, far_v = swap(two[1][0], "ctx", 2), swap(two[0][1], "ctx", 4)
        slots[3], slots[5] = swap(two[0], "ctx", 1), swap(two[1], "ctx", 1)
        halo_two = after(halos[2], c_acc)
        halo_one = jnp.where(odd, halo_two, kv_c)
        halos[1] = swap(halo_one, "ctx", 1)
        ready = (halo_one,)
    c_state = attention_forward(
        (1,), after(scalars, c_acc, *ready), q, low_col, pick(slots, middle), {}, (c_acc, c_tot)
    )
    if ctx_size == 8:
        slots[6] = jnp.stack([after(far_k, c_state[0]), after(far_v, c_state[0])])
        slots[7] = swap(slots[6], "ctx", 1)
        ready = (slots[6],)
    attended, lse_p, part_p = attention_forward(
        (0,), after(scalars, c_state[0], *ready), q, low_col, pick(slots, middle + far), {}, p_state, (w_rest, None)
    )
    got_p = swap(part_p, "tensor", 1)
    attended, lse_c, part_c = attention_forward(
        (1,), after(scalars, part_p), q, low_col, pick(slots, far), pick(halos, range(1, n_halo)),
        c_state, (w_rest, attended),
    )
    got_c = swap(part_c, "tensor", 1)

    resid_p, *whole, out_p, back_p = feed_forward(
        0, tokens, part_p, got_p, after(gain_two, part_c), cotangent, w_rest, o_cols, chunk
    )
    back_got_p = swap(back_p, "tensor", 1)
    resid_c, *whole, out_c, back_c = feed_forward(
        1, tokens, part_c, got_c, after(gain_two, back_p), cotangent, w_rest, o_cols, chunk, whole
    )
    back_got_c = swap(back_c, "tensor", 1)
    normed_ffn, hidden, d_gu = whole
    width = o_cols + 3 * units
    rest_grads = weight_grad(normed_ffn, d_gu, o_cols, width, min(1024, o_cols))
    rest_grads = weight_grad(cotangent, hidden, o_cols + 2 * units, width, chunk, rest_grads)
    d_resid_p, d_mixed, d_att_p, delta_p, d_two_p = mixed_back(
        0, back_p, back_got_p, resid_p, after(gain_two, rest_grads), cotangent, w_rest, o_cols, attended
    )
    d_resid_c, d_mixed, d_att_c, delta_c, d_two_c = mixed_back(
        1, back_c, back_got_c, resid_c, after(gain_two, d_att_p), cotangent, w_rest, o_cols, attended, d_mixed
    )
    rest_grads = weight_grad(d_mixed, attended, 0, width, min(1024, o_cols), rest_grads)
    rest_share = lax.psum_scatter(rest_grads, weight_axes, scatter_dimension=0, tiled=True)
    out_p, out_c = after(out_p, back_got_c), after(out_c, back_got_c)
    out_got_p, out_got_c = swap(out_p, "tensor", 1), swap(out_c, "tensor", 1)

    dq_p, from_p, _ = attention_backward(
        0, after(scalars, rest_grads), q, d_att_p, lse_p, delta_p, low_row, slots, {}
    )

    def back_c_rows(deps, slots, halos, carry, last):
        prior = pick(from_p, tuple(slots)) if slots else None
        return attention_backward(
            1, after(scalars, *deps), q, d_att_c, lse_c, delta_c, low_row, slots, halos, carry, prior, last
        )

    dq_c, _, g_halo = back_c_rows((dq_p,), {}, halos, None, False)
    if ctx_size == 8:
        near_one = swap(g_halo[1], "ctx", 1)
    dq_c, g, _ = back_c_rows((dq_c,), pick(slots, far), {}, dq_c, False)
    zero = jnp.zeros((), BF)
    if ctx_size == 8:
        near_one = after(near_one, dq_c)
        two_back = add_low(g_halo[2], jnp.where(odd, near_one, zero))
        halo_two = shift(two_back, -2)
        got7 = swap(g[7], "ctx", 1)
        ready = (two_back,)
    dq_c, more, _ = back_c_rows((dq_c, *ready), pick(slots, middle), {}, dq_c, False)
    g.update(more)
    if ctx_size == 8:
        g6 = add_low(g[6], after(got7, dq_c))
        far_k, far_v = swap(g6[0], "ctx", 2), swap(g6[1], "ctx", 4)
        got3, got5 = swap(g[3], "ctx", 1), swap(g[5], "ctx", 1)
        ready = (g6,)
    if ctx_size == 8:
        ready = (g6, halo_two)
    dq_c, more, _ = back_c_rows((dq_c, *ready), pick(slots, near), {}, dq_c, True)
    g.update(more)
    if ctx_size == 8:
        got1 = swap(g[1], "ctx", 1)
        far_k, far_v, got3, got5 = (after(v, dq_c) for v in (far_k, far_v, got3, got5))
        k2, v2 = add_low(g[2][0], got3[0]), add_low(add_low(g[2][1], got3[1]), far_v)
        k4, v4 = add_low(add_low(g[4][0], got5[0]), far_k), add_low(g[4][1], got5[1])
        ready = (k2, v2, k4, v4)
        keys_p = [g[0], got1, swap(k2, "ctx", 2), swap(k4, "ctx", 4)]
        values_p = [g[0], got1, swap(v2, "ctx", 2), swap(v4, "ctx", 4)]
        keys_c = values_c = [g_halo[0], jnp.where(odd, zero, near_one), halo_two]
    else:
        both = jnp.stack([g[s] for s in range(ctx_size)])
        while both.shape[0] > 1:
            size = both.shape[0] // 2
            both = add_low(both[:size], swap(both[size:], "ctx", size))
        keys_p = values_p = [both[0]]
        keys_c = values_c = [g_halo[0]] + [shift(g_halo[d], -d) for d in range(1, n_halo)]

    w_q_abs, w_kv_abs = (mm(to_slots, after(w, part_p)).astype(BF) for w in (w_q, w_kv))
    d_q, q_part_p, heads_p = q_back(0, dq_p, q_lin, after(gain_q, dq_c, *ready), cos, sin, w_q_abs)
    d_q, q_part_c, heads_c = q_back(1, dq_c, q_lin, after(gain_q, q_part_p), cos, sin, w_q_abs, d_q)
    q_high = mm(normed[:, model // 2 :], after(d_q, q_part_c), TN).astype(BF)
    q_low = mm(normed[:, : model // 2], after(d_q, q_high), TN).astype(BF)
    d_kv, into_c, k_heads_c = kv_back(
        1, keys_c, values_c, k_lin_c, after(gain_k, q_low), cos, sin, w_kv_abs, q_part_c
    )
    into_got_c = swap(into_c, "tensor", 1)
    q_grad = scatter_rows(q_low, q_high, into_c)
    d_kv, into_p, k_heads_p = kv_back(
        0, keys_p, values_p, k_lin_p, after(gain_k, into_c, *q_grad), cos, sin, w_kv_abs, q_part_p, d_kv
    )
    into_got_p = swap(into_p, "tensor", 1)
    kv_high = mm(normed[:, model // 2 :], after(d_kv, into_p), TN).astype(BF)
    kv_low = mm(normed[:, : model // 2], after(d_kv, kv_high), TN).astype(BF)
    layer_out = jnp.concatenate(
        [
            (resid + (own.astype(F32) + after(got, kv_low).astype(F32))).astype(BF)
            for resid, own, got in ((resid_p, out_p, out_got_p), (resid_c, out_c, out_got_c))
        ]
    )
    rest_share = after(rest_share, kv_low).astype(F32)
    out_share, down_share = rest_share[:, :o_cols].T, rest_share[:, o_cols + 2 * units :].T
    gate_up = rest_share[:, o_cols : o_cols + 2 * units].reshape(wide, units // chunk, 2, chunk)
    gate_share, up_share = gate_up[:, :, 0].reshape(wide, units), gate_up[:, :, 1].reshape(wide, units)
    kv_grad = scatter_rows(kv_low, kv_high, layer_out)
    grad_tokens, d_one_c = tokens_back(
        1, into_c, into_got_c, tokens, after(gain_one, *kv_grad, layer_out, gate_share, up_share), d_resid_c
    )
    early = jnp.concatenate([d_two_c + d_two_p, heads_c + heads_p, k_heads_c + k_heads_p], axis=1)
    early = butterfly(after(early, into_p), ("ctx", "shard"))
    head_gains = butterfly(early[:, model:], ("tensor",))
    kv_grad = scatter_more(kv_grad, d_one_c)
    q_grad = scatter_more(q_grad, d_one_c)
    grad_tokens, d_one_p = tokens_back(
        0, into_p, into_got_p, tokens, after(gain_one, d_one_c, head_gains, *kv_grad, *q_grad, out_share, down_share),
        d_resid_p, grad_tokens,
    )
    kv_share, q_share = (scatter_last(v).astype(F32) for v in (kv_grad, q_grad))
    late = butterfly(d_one_c + d_one_p, ("ctx", "shard"))

    def own_gain(value, size):
        return lax.dynamic_index_in_dim(value.reshape(-1, parts, size), part, 1, keepdims=False)

    model_gains = own_gain(jnp.concatenate([late, early[:, :model]]), wide)
    head_gains = own_gain(head_gains, narrow)
    return (
        layer_out,
        grad_tokens,
        model_gains[0],
        model_gains[1],
        head_gains[0],
        head_gains[1],
        q_share,
        kv_share[:, :k_cols],
        kv_share[:, k_cols:],
        out_share,
        gate_share,
        up_share,
        down_share,
    )


def solution(mesh):
    split = ("shard", "ctx")
    rows, gain = P(split, None), P(split)
    into, out_of = P(split, "tensor"), P("tensor", split)
    in_specs = (rows, P("shard", None)) + (gain,) * 4 + (into,) * 3 + (out_of,)
    in_specs += (into, into, out_of, rows)
    out_specs = (rows, rows) + (gain,) * 4 + (into,) * 3 + (out_of, into, into, out_of)
    return jax.shard_map(body, mesh=mesh, in_specs=in_specs, out_specs=out_specs, check_vma=False)
```

```python
import functools
import math

import jax
import jax.numpy as jnp
from jax import lax
from jax.experimental import pallas as pl
from jax.experimental.pallas import tpu as pltpu
from jax.sharding import PartitionSpec as P

HEAD_SIZE = 128
PROMPT = 4096
CONT_TOK = 4096
LONGEST = 1024

EPSILON = 1e-06
ROPE_BASE = 1000000.0
MASKED = -1e30
LOG2E = math.log2(math.e)
LN2 = math.log(2.0)
SCALE = 1.0 / math.sqrt(HEAD_SIZE)

BF = jnp.bfloat16
F32 = jnp.float32
NN = (((1,), (0,)), ((), ()))
NT = (((1,), (1,)), ((), ()))
TN = (((0,), (0,)), ((), ()))
MIB = 2**20
STATED = 1.2e6


def mm(left, right, dims=NN):
    return lax.dot_general(left, right, dims, preferred_element_type=F32)


def shaped(dims, kind):
    return jax.ShapeDtypeStruct(dims, kind)


def call(kernel, name, grid, ins, outs, scratch=(), vmem=56, scalars=None, keep=None, us=4):
    in_specs, arrays = [], []
    for array, block, index in ins:
        arrays.append(array)
        in_specs.append(pl.BlockSpec(memory_space=pl.ANY) if block is None else pl.BlockSpec(block, index))
    lead = 0 if scalars is None else 1
    return pl.pallas_call(
        kernel,
        grid_spec=pltpu.PrefetchScalarGridSpec(
            num_scalar_prefetch=lead,
            grid=grid,
            in_specs=in_specs,
            out_specs=[pl.BlockSpec(block, index) for _, block, index in outs],
            scratch_shapes=list(scratch),
        ),
        out_shape=[shape for shape, _, _ in outs],
        input_output_aliases={a + lead: b for a, b in (keep or {}).items()},
        compiler_params=pltpu.CompilerParams(vmem_limit_bytes=vmem * MIB),
        cost_estimate=pl.CostEstimate(flops=0, bytes_accessed=int(us * STATED), transcendentals=0),
        name=name,
    )(*([] if scalars is None else [scalars]), *arrays)


def rms(values):
    return lax.rsqrt(jnp.mean(values * values, axis=-1, keepdims=True) + EPSILON)


def turn(values, cos, sin):
    return values * cos + pltpu.roll(values, HEAD_SIZE // 2, 1) * sin


def turn_back(values, cos, sin):
    return values * cos - pltpu.roll(values, HEAD_SIZE // 2, 1) * sin


def kv_kernel(heads, x_ref, gain_ref, w_ref, hgain_ref, cos_ref, sin_ref, *refs):
    normed_ref, kv_ref, lin_ref = refs[-3:]
    x = x_ref[...].astype(F32)
    normed_ref[...] = (x * rms(x) * gain_ref[...]).astype(BF)
    both = mm(normed_ref[...], w_ref[...])
    width = heads * HEAD_SIZE
    kv_ref[1] = both[:, width:].astype(BF)
    for h in range(heads):
        cols = slice(h * HEAD_SIZE, (h + 1) * HEAD_SIZE)
        lin = both[:, cols]
        lin_ref[:, cols] = lin
        kv_ref[0, :, cols] = turn(lin * rms(lin) * hgain_ref[...], cos_ref[...], sin_ref[...]).astype(BF)


def q_kernel(heads, normed_ref, w_ref, hgain_ref, cos_ref, sin_ref, q_ref, lin_ref):
    both = mm(normed_ref[...], w_ref[...])
    for h in range(heads):
        cols = slice(h * HEAD_SIZE, (h + 1) * HEAD_SIZE)
        lin = both[:, cols]
        lin_ref[:, cols] = lin
        turned = turn(lin * rms(lin) * hgain_ref[...], cos_ref[...], sin_ref[...])
        q_ref[:, cols] = (turned * (SCALE * LOG2E)).astype(BF)


def pack_kernel(chunk, key_ref, value_ref, out_ref, gate_ref, up_ref, down_ref, kv_ref, rest_ref):
    wide, k_cols = key_ref.shape
    o_cols, units = out_ref.shape[0], gate_ref.shape[1]
    kv_ref[:, :k_cols] = key_ref[...]
    kv_ref[:, k_cols:] = value_ref[...]
    eye = lax.broadcasted_iota(jnp.int32, (wide, wide), 0) == lax.broadcasted_iota(jnp.int32, (wide, wide), 1)
    eye = jnp.where(eye, 1.0, 0.0).astype(BF)
    rest_ref[:, :o_cols] = mm(eye, out_ref[...], NT).astype(BF)
    for at in range(0, units, chunk):
        to = o_cols + 2 * at
        rest_ref[:, to : to + chunk] = gate_ref[:, at : at + chunk]
        rest_ref[:, to + chunk : to + 2 * chunk] = up_ref[:, at : at + chunk]
    rest_ref[:, o_cols + 2 * units :] = mm(eye, down_ref[...], NT).astype(BF)


def pack(chunk, *weights):
    wide, k_cols = weights[0].shape
    width = weights[2].shape[0] + 3 * weights[3].shape[1]
    whole = lambda f: (0, 0)
    ins = [(w, w.shape, whole) for w in weights]
    outs = [(shaped((wide, cols), BF), (wide, cols), whole) for cols in (2 * k_cols, width)]
    return call(functools.partial(pack_kernel, chunk), "pack", (1,), ins, outs, us=3)


def by_top_bit(slots):
    groups = {}
    for at, s in enumerate(slots):
        if s:
            groups.setdefault(1 << (s.bit_length() - 1), []).append(at)
    return groups


def fwd_kernel(plan, idx_ref, lo_ref, *refs):
    halves, slots, halos = plan["halves"], plan["slots"], plan["halos"]
    refs = list(refs)
    q_refs = [refs.pop(0) for _ in halves]
    slot_refs = [refs.pop(0) for _ in slots]
    halo_refs = [refs.pop(0) for _ in halos]
    prior = [refs.pop(0) for _ in range(2 * len(halves))] if plan["carry"] else None
    if plan["last"]:
        w_ref = refs.pop(0)
        if plan["alias"]:
            refs.pop(0)
        out_ref, lse_ref, part_ref = refs[:3]
        refs = refs[3:]
    else:
        results, refs = refs[: 2 * len(halves)], refs[2 * len(halves) :]
    me, lo_first = idx_ref[0], idx_ref[1]
    rows = q_refs[0].shape[0]
    row = lax.broadcasted_iota(jnp.int32, (2 * rows, 1), 0)
    row = jnp.where(row >= rows, row - rows, row)
    col = lax.broadcasted_iota(jnp.int32, (1, rows), 1)
    for n, half in enumerate(halves):
        qs, acc, tot = refs[3 * n : 3 * n + 3]
        for g in range(2):
            cols, at = slice(g * HEAD_SIZE, (g + 1) * HEAD_SIZE), slice(g * rows, (g + 1) * rows)
            qs[at, :] = q_refs[n][:, cols]
            if prior is not None:
                acc[at, :] = prior[2 * n][:, cols]
                tot[at, :] = prior[2 * n + 1][:, cols]
        empty = [prior is None]

        def add(kv_ref, mask=None):
            scores = mm(qs[...], kv_ref[0], NT)
            if mask is not None:
                scores = jnp.where(mask, scores, MASKED)
            weights = jnp.exp2(scores)
            total = weights[:, :128]
            for at in range(128, weights.shape[1], 128):
                total = total + weights[:, at : at + 128]
            part = mm(weights.astype(BF), kv_ref[1])
            if empty[0]:
                acc[...] = part
                tot[...] = total
            else:
                acc[...] += part
                tot[...] += total
            empty[0] = False

        if half == 1:
            for kv_ref in slot_refs:
                add(kv_ref)
            low = jnp.concatenate([lo_ref[:, :1], lo_ref[:, :1]])
            for d, kv_ref in zip(halos, halo_refs):
                if d == 0:
                    add(kv_ref, (col <= row) & (col >= low))
                else:

                    @pl.when(lo_first < -(d - 1) * rows)
                    def _(d=d, kv_ref=kv_ref):
                        add(kv_ref, col - d * rows >= low)

        else:
            if 0 in slots:
                add(slot_refs[slots.index(0)], col <= row)
            for bit, group in by_top_bit(slots).items():

                @pl.when(jnp.bitwise_and(me, bit) != 0)
                def _(group=group):
                    for at in group:
                        add(slot_refs[at])

        if not plan["last"]:
            for g in range(2):
                cols, at = slice(g * HEAD_SIZE, (g + 1) * HEAD_SIZE), slice(g * rows, (g + 1) * rows)
                results[2 * n][:, cols] = acc[at, :]
                results[2 * n + 1][:, cols] = tot[at, :]
    if plan["last"]:
        qs, acc, tot, part_acc = refs
        step, steps = pl.program_id(0), pl.num_programs(0)
        for g in range(2):
            cols, at = slice(g * HEAD_SIZE, (g + 1) * HEAD_SIZE), slice(g * rows, (g + 1) * rows)
            total = jnp.sum(tot[at, :], axis=1, keepdims=True)
            out_ref[:, cols] = (acc[at, :] / total).astype(BF)
            lse_ref[0, g : g + 1, :] = jnp.log2(jnp.sum(tot[at, :].T, axis=0, keepdims=True))
        part = mm(out_ref[...], w_ref[...], NT)

        @pl.when(step == 0)
        def _():
            part_acc[...] = part

        @pl.when((step > 0) & (step < steps - 1))
        def _():
            part_acc[...] += part

        @pl.when(step == steps - 1)
        def _():
            part_ref[...] = (part_acc[...] + part).astype(BF)


def attention_forward(halves, scalars, q, low, slots, halos, carry=None, last=None):
    rows, heads = q.shape[0] // 2, q.shape[1] // 256
    plan = dict(halves=halves, slots=list(slots), halos=list(halos), carry=carry is not None,
                last=last is not None, alias=last is not None and last[1] is not None)
    part = lambda h, i: (0, h)
    ins = [(low, (rows, 128), lambda h, i: (0, 0))]
    ins += [(q, (rows, 256), lambda h, i, half=half: (half, h)) for half in halves]
    for kv in list(slots.values()) + list(halos.values()):
        ins.append((kv, (2, rows, 128), lambda h, i: (0, 0, h)))
    if carry is not None:
        ins += [(c, (rows, 256), part) for c in carry]
    scratch, keep = [], {}
    for _ in halves:
        scratch += [pltpu.VMEM((2 * rows, 128), BF)] + [pltpu.VMEM((2 * rows, 128), F32)] * 2
    state = shaped((rows, heads * 256), F32)
    if last is None:
        outs = [(state, (rows, 256), part)] * (2 * len(halves))
    else:
        w_rest, other = last
        model = w_rest.shape[0]
        ins.append((w_rest, (model, 256), part))
        if other is not None:
            keep = {len(ins): 0}
            ins.append((other, None, None))
        half = halves[0]
        outs = [
            (shaped((2 * rows, heads * 256), BF), (rows, 256), lambda h, i: (half, h)),
            (shaped((heads, 8, rows), F32), (1, 8, rows), lambda h, i: (h, 0, 0)),
            (shaped((rows, model), BF), (rows, model), lambda h, i: (0, 0)),
        ]
        scratch.append(pltpu.VMEM((rows, model), F32))
    blocks = len(slots) * len(halves) + len(halos)
    return call(functools.partial(fwd_kernel, plan), "attend", (heads,), ins, outs, scratch,
                scalars=scalars, keep=keep, us=2 + 3 * blocks)


def bwd_kernel(plan, idx_ref, q_ref, do_ref, lse_ref, delta_ref, lo_ref, *refs):
    half, slots, halos = plan["half"], plan["slots"], plan["halos"]
    refs = list(refs)
    slot_refs = [refs.pop(0) for _ in slots]
    halo_refs = [refs.pop(0) for _ in halos]
    prior_dq = refs.pop(0) if plan["carry"] else None
    prior = [refs.pop(0) for _ in slots] if plan["sum"] else None
    dq_ref = refs.pop(0)
    slot_outs = [refs.pop(0) for _ in slots]
    halo_outs = [refs.pop(0) for _ in halos]
    qs, dos, lses, deltas, dq = refs
    me, lo_first = idx_ref[0], idx_ref[1]
    rows = q_ref.shape[0]
    for g in range(2):
        cols, at = slice(g * HEAD_SIZE, (g + 1) * HEAD_SIZE), slice(g * rows, (g + 1) * rows)
        qs[at, :] = q_ref[:, cols]
        dos[at, :] = do_ref[:, cols]
        lses[:, at] = lse_ref[0, g : g + 1, :]
        deltas[:, at] = delta_ref[0, g : g + 1, :]
    dq[...] = jnp.zeros_like(dq) if prior_dq is None else prior_dq[...]

    def block(kv_ref, out_ref, mask=None, before=None):
        keys = kv_ref[0]
        scores = mm(keys, qs[...], NT)
        dp = mm(kv_ref[1], dos[...], NT)
        scores = scores - lses[...]
        if mask is not None:
            scores = jnp.where(mask, scores, MASKED)
        probs = jnp.exp2(scores)
        ds = (probs * (dp - deltas[...])).astype(BF)
        dq[...] += mm(keys.T, ds)
        dk, dv = mm(ds, qs[...]) * LN2, mm(probs.astype(BF), dos[...])
        if before is not None:
            dk, dv = dk + before[0].astype(F32), dv + before[1].astype(F32)
        out_ref[0] = dk.astype(BF)
        out_ref[1] = dv.astype(BF)

    lane = lax.broadcasted_iota(jnp.int32, (1, 2 * rows), 1)
    lane = jnp.where(lane >= rows, lane - rows, lane)
    key = lax.broadcasted_iota(jnp.int32, (rows, 1), 0)

    def when(needed, kv_ref, out_ref, mask=None):
        @pl.when(needed)
        def _():
            block(kv_ref, out_ref, mask)

        @pl.when(jnp.logical_not(needed))
        def _():
            out_ref[...] = jnp.zeros_like(out_ref)

    low = lo_ref[:1, :]
    for d, kv_ref, out_ref in zip(halos, halo_refs, halo_outs):
        if d == 0:
            block(kv_ref, out_ref, (key <= lane) & (key >= low))
        else:
            when(lo_first < -(d - 1) * rows, kv_ref, out_ref, key - d * rows >= low)
    if half == 1:
        for at in range(len(slots)):
            block(slot_refs[at], slot_outs[at], None, prior[at])
    else:
        if 0 in slots:
            at = slots.index(0)
            block(slot_refs[at], slot_outs[at], key <= lane)
        for bit, group in by_top_bit(slots).items():

            @pl.when(jnp.bitwise_and(me, bit) != 0)
            def _(group=group):
                for at in group:
                    block(slot_refs[at], slot_outs[at])

            @pl.when(jnp.bitwise_and(me, bit) == 0)
            def _(group=group):
                for at in group:
                    slot_outs[at][...] = jnp.zeros_like(slot_outs[at])

    if plan["last"]:
        for g in range(2):
            cols = slice(g * HEAD_SIZE, (g + 1) * HEAD_SIZE)
            dq_ref[:, cols] = dq[:, g * rows : (g + 1) * rows].T * SCALE
    else:
        dq_ref[...] = dq[...]


def attention_backward(half, scalars, q, do, lse, delta, low, slots, halos, carry=None, prior=None, last=True):
    rows, heads = q.shape[0] // 2, q.shape[1] // 256
    plan = dict(half=half, slots=list(slots), halos=list(halos), carry=carry is not None,
                sum=prior is not None, last=last)
    part = lambda h, i: (0, h)
    stat = lambda h, i: (h, 0, 0)
    kv_map = lambda h, i: (0, 0, h)
    ins = [
        (q, (rows, 256), lambda h, i: (half, h)),
        (do, (rows, 256), part),
        (lse, (1, 8, rows), stat),
        (delta, (1, 8, rows), stat),
        (low, (8, 2 * rows), lambda h, i: (0, 0)),
    ]
    pieces = list(slots.values()) + list(halos.values())
    ins += [(kv, (2, rows, 128), kv_map) for kv in pieces]
    if carry is not None:
        ins.append((carry, (128, 2 * rows), lambda h, i: (h, 0)))
    if prior is not None:
        ins += [(prior[s], (2, rows, 128), kv_map) for s in slots]
    if last:
        outs = [(shaped((rows, heads * 256), F32), (rows, 256), part)]
    else:
        outs = [(shaped((heads * 128, 2 * rows), F32), (128, 2 * rows), lambda h, i: (h, 0))]
    outs += [(shaped(kv.shape, BF), (2, rows, 128), kv_map) for kv in pieces]
    scratch = [
        pltpu.VMEM((2 * rows, 128), BF),
        pltpu.VMEM((2 * rows, 128), BF),
        pltpu.VMEM((1, 2 * rows), F32),
        pltpu.VMEM((1, 2 * rows), F32),
        pltpu.VMEM((128, 2 * rows), F32),
    ]
    us = 4 + 6 * (len(slots) + len(halos))
    results = call(functools.partial(bwd_kernel, plan), "attend_back", (heads,), ins, outs, scratch,
                   scalars=scalars, us=us)
    n = len(slots)
    return results[0], dict(zip(slots, results[1 : 1 + n])), dict(zip(halos, results[1 + n :]))


def ffn_kernel(x_ref, own_ref, got_ref, gain_ref, dy_ref, gu_ref, down_ref, *refs):
    resid_ref, normed_ref, hidden_ref, dgu_ref, out_ref, back_ref, normed, out_acc, back_acc = refs[-9:]
    step, steps = pl.program_id(0), pl.num_programs(0)

    @pl.when(step == 0)
    def _():
        resid = x_ref[...].astype(F32) + (own_ref[...].astype(F32) + got_ref[...].astype(F32))
        resid_ref[...] = resid
        normed[...] = (resid * rms(resid) * gain_ref[...]).astype(BF)
        normed_ref[...] = normed[...]
        out_acc[...] = jnp.zeros_like(out_acc)
        back_acc[...] = jnp.zeros_like(back_acc)

    wide = down_ref.shape[1]
    both = mm(normed[...], gu_ref[...])
    d_hidden = mm(dy_ref[...], down_ref[...])
    gate, up = both[:, :wide], both[:, wide:]
    sig = 1.0 / (1.0 + jnp.exp(-gate))
    silu = gate * sig
    hidden = (silu * up).astype(BF)
    hidden_ref[...] = hidden
    d_up = (d_hidden * silu).astype(BF)
    d_gate = (d_hidden * up * (sig + silu * (1.0 - sig))).astype(BF)
    dgu_ref[:, :wide] = d_gate
    dgu_ref[:, wide:] = d_up
    out_acc[...] += mm(hidden, down_ref[...], NT)
    back_acc[...] += mm(dgu_ref[...], gu_ref[...], NT)

    @pl.when(step == steps - 1)
    def _():
        out_ref[...] = out_acc[...].astype(BF)
        back_ref[...] = back_acc[...].astype(BF)


def feed_forward(half, x, own, got, gain, dy, w_rest, o_cols, chunk, whole=None):
    rows, model = own.shape
    units = (w_rest.shape[1] - o_cols) // 3
    steps = units // chunk
    mine, once = lambda f: (half, 0), lambda f: (0, 0)
    at_gu, at_down = o_cols // (2 * chunk), (o_cols + 2 * units) // chunk
    block = (rows, model)
    ins = [
        (x, block, mine), (own, block, once), (got, block, once), (gain, (1, model), once), (dy, block, mine),
        (w_rest, (model, 2 * chunk), lambda f: (0, at_gu + f)),
        (w_rest, (model, chunk), lambda f: (0, at_down + f)),
    ]
    keep = {}
    if whole is not None:
        keep = {len(ins) + i: 1 + i for i in range(3)}
        ins += [(array, None, None) for array in whole]
    outs = [
        (shaped((rows, model), F32), block, once),
        (shaped((2 * rows, model), BF), block, mine),
        (shaped((2 * rows, units), BF), (rows, chunk), lambda f: (half, f)),
        (shaped((2 * rows, 2 * units), BF), (rows, 2 * chunk), lambda f: (half, f)),
        (shaped((rows, model), BF), block, once),
        (shaped((rows, model), BF), block, once),
    ]
    scratch = [pltpu.VMEM(block, BF), pltpu.VMEM(block, F32), pltpu.VMEM(block, F32)]
    return call(ffn_kernel, "feed_forward", (steps,), ins, outs, scratch, keep=keep, us=18)


def norm_back(grad, values, gain):
    scale = rms(values)
    unit = values * scale
    inner = grad * gain
    return scale * (inner - unit * jnp.mean(inner * unit, axis=-1, keepdims=True)), grad * unit


def row_blocks(rows):
    size = rows // 2 if rows % 512 == 0 else rows
    return size, rows // size


def add_up(ref, value):
    total = jnp.sum(value, axis=0, keepdims=True)

    @pl.when(pl.program_id(0) == 0)
    def _():
        ref[...] = total

    @pl.when(pl.program_id(0) > 0)
    def _():
        ref[...] += total


def mixed_kernel(heads, own_ref, got_ref, resid_ref, gain_ref, dy_ref, w_ref, att_ref, *refs):
    d_resid_ref, mixed_ref, datt_ref, delta_ref, dgain_ref = refs[-5:]
    grad = own_ref[...].astype(F32) + got_ref[...].astype(F32)
    d_norm, summand = norm_back(grad, resid_ref[...], gain_ref[...])
    add_up(dgain_ref, summand)
    d_resid = dy_ref[...].astype(F32) + d_norm
    d_resid_ref[...] = d_resid
    mixed_ref[...] = d_resid.astype(BF)
    datt_ref[...] = mm(mixed_ref[...], w_ref[...]).astype(BF)
    for h in range(heads):
        cols = slice(h * HEAD_SIZE, (h + 1) * HEAD_SIZE)
        product = datt_ref[:, cols].astype(F32) * att_ref[:, cols].astype(F32)
        delta_ref[h // 2, h % 2 : h % 2 + 1, :] = jnp.sum(product.T, axis=0, keepdims=True)


def mixed_back(half, own, got, resid, gain, dy, w_rest, o_cols, attended, whole=None):
    rows, model = own.shape
    heads = o_cols // HEAD_SIZE
    size, steps = row_blocks(rows)
    mine, here, once = lambda f: (half * steps + f, 0), lambda f: (f, 0), lambda f: (0, 0)
    block = (size, model)
    ins = [
        (own, block, here), (got, block, here), (resid, block, here), (gain, (1, model), once),
        (dy, block, mine), (w_rest, (model, o_cols), once), (attended, (size, o_cols), mine),
    ]
    keep = {}
    if whole is not None:
        keep = {len(ins): 1}
        ins.append((whole, None, None))
    outs = [
        (shaped((rows, model), F32), block, here),
        (shaped((2 * rows, model), BF), block, mine),
        (shaped((rows, o_cols), BF), (size, o_cols), here),
        (shaped((heads // 2, 8, rows), F32), (heads // 2, 8, size), lambda f: (0, 0, f)),
        (shaped((1, model), F32), (1, model), once),
    ]
    return call(functools.partial(mixed_kernel, heads), "mixed_back", (steps,), ins, outs, keep=keep, us=7)


def weight_kernel(left_ref, right_ref, *refs):
    refs[-1][...] = mm(left_ref[...], right_ref[...], TN).astype(BF)


def weight_grad(left, right, at, width, cols, whole=None):
    tokens, model = left.shape
    n = right.shape[1]
    ins = [(left, (tokens, model), lambda j: (0, 0)), (right, (tokens, cols), lambda j: (0, j))]
    keep = {}
    if whole is not None:
        keep = {len(ins): 0}
        ins.append((whole, None, None))
    outs = [(shaped((model, width), BF), (model, cols), lambda j: (0, at // cols + j))]
    return call(weight_kernel, "weight_grad", (n // cols,), ins, outs, keep=keep, us=n / 270)[0]


def q_back_kernel(heads, dq_ref, lin_ref, gain_ref, cos_ref, sin_ref, w_ref, *refs):
    d_ref, part_ref, gains_ref = refs[-3:]
    cos, sin = cos_ref[...], sin_ref[...]
    total = jnp.zeros(cos.shape, F32)
    for h in range(heads):
        cols = slice(h * HEAD_SIZE, (h + 1) * HEAD_SIZE)
        grad, summand = norm_back(turn_back(dq_ref[:, cols], cos, sin), lin_ref[:, cols], gain_ref[...])
        d_ref[:, cols] = grad.astype(BF)
        total = total + summand
    part_ref[...] = mm(d_ref[...], w_ref[...], NT)
    add_up(gains_ref, total)


def q_back(half, dq, lin, gain, cos, sin, w, whole=None):
    rows, cols = dq.shape
    model = w.shape[0]
    size, steps = row_blocks(rows)
    mine, here, once = lambda f: (half * steps + f, 0), lambda f: (f, 0), lambda f: (0, 0)
    ins = [
        (dq, (size, cols), here), (lin, (size, cols), mine), (gain, (1, HEAD_SIZE), once),
        (cos, (size, HEAD_SIZE), mine), (sin, (size, HEAD_SIZE), mine), (w, (model, cols), once),
    ]
    keep = {}
    if whole is not None:
        keep = {len(ins): 0}
        ins.append((whole, None, None))
    outs = [
        (shaped((2 * rows, cols), BF), (size, cols), mine),
        (shaped((rows, model), F32), (size, model), here),
        (shaped((1, HEAD_SIZE), F32), (1, HEAD_SIZE), once),
    ]
    kernel = functools.partial(q_back_kernel, cols // HEAD_SIZE)
    return call(kernel, "q_back", (steps,), ins, outs, keep=keep, us=10)


def kv_back_kernel(heads, n_keys, n_values, lin_ref, gain_ref, cos_ref, sin_ref, w_ref, slots_ref, q_part_ref, *refs):
    key_refs, value_refs = refs[:n_keys], refs[n_keys : n_keys + n_values]
    d_ref, part_ref, gains_ref = refs[-3:]
    cos, sin = cos_ref[...], sin_ref[...]
    width = heads * HEAD_SIZE

    def total(sources, which, cols):
        value = None
        for ref in sources:
            piece = ref[which, :, cols] if len(ref.shape) == 3 else ref[:, cols]
            value = piece.astype(F32) if value is None else value + piece.astype(F32)
        return value

    gains = jnp.zeros(cos.shape, F32)
    for h in range(heads):
        cols = slice(h * HEAD_SIZE, (h + 1) * HEAD_SIZE)
        grad, summand = norm_back(
            turn_back(total(key_refs, 0, cols), cos, sin), lin_ref[:, cols], gain_ref[...]
        )
        d_ref[:, cols] = grad.astype(BF)
        gains = gains + summand
    d_ref[:, width:] = total(value_refs, 1, slice(None)).astype(BF)
    part = (q_part_ref[...] + mm(d_ref[...], w_ref[...], NT)).astype(BF)
    part_ref[...] = mm(part, slots_ref[...], NT).astype(BF)
    add_up(gains_ref, gains)


def kv_back(half, keys, values, lin, gain, cos, sin, w, to_slots, q_part, whole=None):
    rows, cols = lin.shape
    model = w.shape[0]
    size, steps = row_blocks(rows)
    mine, here, once = lambda f: (half * steps + f, 0), lambda f: (f, 0), lambda f: (0, 0)
    ins = [
        (lin, (size, cols), here), (gain, (1, HEAD_SIZE), once), (cos, (size, HEAD_SIZE), mine),
        (sin, (size, HEAD_SIZE), mine), (w, (model, 2 * cols), once),
        (to_slots, (model, model), once), (q_part, (size, model), here),
    ]
    for piece in list(keys) + list(values):
        if piece.ndim == 3:
            ins.append((piece, (2, size, cols), lambda f: (0, f, 0)))
        else:
            ins.append((piece, (size, cols), here))
    keep = {}
    if whole is not None:
        keep = {len(ins): 0}
        ins.append((whole, None, None))
    outs = [
        (shaped((2 * rows, 2 * cols), BF), (size, 2 * cols), mine),
        (shaped((rows, model), BF), (size, model), here),
        (shaped((1, HEAD_SIZE), F32), (1, HEAD_SIZE), once),
    ]
    kernel = functools.partial(kv_back_kernel, cols // HEAD_SIZE, len(keys), len(values))
    return call(kernel, "kv_back", (steps,), ins, outs, keep=keep, us=8)


def tokens_kernel(own_ref, got_ref, x_ref, gain_ref, d_resid_ref, *refs):
    out_ref, dgain_ref = refs[-2:]
    grad = own_ref[...].astype(F32) + got_ref[...].astype(F32)
    d_norm, summand = norm_back(grad, x_ref[...].astype(F32), gain_ref[...])
    add_up(dgain_ref, summand)
    out_ref[...] = (d_resid_ref[...] + d_norm).astype(BF)


def tokens_back(half, own, got, x, gain, d_resid, whole=None):
    rows, model = own.shape
    size, steps = row_blocks(rows)
    mine, here, once = lambda f: (half * steps + f, 0), lambda f: (f, 0), lambda f: (0, 0)
    block = (size, model)
    ins = [(own, block, here), (got, block, here), (x, block, mine), (gain, (1, model), once), (d_resid, block, here)]
    keep = {}
    if whole is not None:
        keep = {len(ins): 0}
        ins.append((whole, None, None))
    outs = [(shaped((2 * rows, model), BF), block, mine), (shaped((1, model), F32), (1, model), once)]
    return call(tokens_kernel, "tokens_back", (steps,), ins, outs, keep=keep, us=4)


def swap(value, axis, bit):
    size = lax.axis_size(axis)
    return lax.ppermute(value, axis, [(i, i ^ bit) for i in range(size)])


def shift(value, by):
    size = lax.axis_size("ctx")
    return lax.ppermute(value, "ctx", [(i, i + by) for i in range(size) if 0 <= i + by < size])


def add_low(left, right):
    return (left.astype(F32) + right.astype(F32)).astype(BF)


def butterfly(value, axes):
    for axis in axes:
        bit = 1
        while bit < lax.axis_size(axis):
            value = value + swap(value, axis, bit)
            bit *= 2
    return value


def after(value, *others):
    return lax.optimization_barrier((value, *others))[0]


def rotary_tables(position):
    half_dim = HEAD_SIZE // 2
    inverse_freq = jnp.exp(jnp.arange(half_dim, dtype=F32) * (-math.log(ROPE_BASE) / half_dim))
    angles = position.astype(F32)[:, None] * inverse_freq[None, :]
    cosine, sine = jnp.cos(angles), jnp.sin(angles)
    return jnp.concatenate([cosine, cosine], axis=-1), jnp.concatenate([-sine, sine], axis=-1)


def body(
    tokens,
    cont_lengths,
    attn_gain,
    ffn_gain,
    query_gain,
    key_gain,
    w_query,
    key_weight,
    value_weight,
    w_out,
    w_gate,
    w_up,
    w_down,
    cotangent,
):
    ctx_size = lax.axis_size("ctx")
    weight_axes = ("shard", "ctx")
    parts = lax.axis_size("shard") * ctx_size
    me = lax.axis_index("ctx")
    part = lax.axis_index("shard") * ctx_size + me
    rows, model = tokens.shape[0] // 2, tokens.shape[1]
    n_halo = 1 + -(-(LONGEST - 1) // rows)
    lengths = cont_lengths[0]

    bits = [("shard", 1)] + [("ctx", 1 << i) for i in range(1, ctx_size.bit_length() - 1)] + [("ctx", 1)]
    order = [0]
    for axis, bit in bits:
        order += [j ^ (bit * ctx_size if axis == "shard" else bit) for j in order]
    wide, narrow = attn_gain.shape[0], query_gain.shape[0]
    q_cols, k_cols = w_query.shape[1], key_weight.shape[1]
    o_cols, units = w_out.shape[0], w_gate.shape[1]
    heads, kv_heads = q_cols // HEAD_SIZE, k_cols // HEAD_SIZE
    chunk = math.gcd(units, 512)

    def gather_rows(piece, gates=((),) * 4):
        if ctx_size != 8:
            for axis, bit in bits:
                piece = jnp.concatenate([piece, swap(piece, axis, bit)])
            return piece, (piece,) * 4
        one = jnp.concatenate([piece, after(swap(piece, "shard", 1), *gates[0])])
        by_x, by_y = (after(v, *gates[1]) for v in (swap(one, "ctx", 2), swap(one, "ctx", 4)))
        cut = one.shape[1] // 2
        left, right = swap(by_y[:, :cut], "ctx", 2), swap(by_x[:, cut:], "ctx", 4)
        far = jnp.concatenate([after(left, *gates[2]), after(right, *gates[2])], axis=1)
        half = jnp.concatenate([one, by_x, by_y, far])
        whole = jnp.concatenate([half, after(swap(half, "ctx", 1), *gates[3])])
        return whole, (one, by_x, half, whole)

    def scatter_rows(low, high, late):
        total = add_low(low, after(swap(high, "ctx", 1), late))
        if ctx_size != 8:
            for axis, bit in bits[-2:0:-1]:
                size = total.shape[0] // 2
                total = add_low(total[:size], swap(total[size:], axis, bit))
            return (total,)
        size, cut = total.shape[0] // 4, total.shape[1] // 2
        own, by_x, by_y, far = (total[i * size : (i + 1) * size] for i in range(4))
        left, right = swap(far[:, :cut], "ctx", 2), swap(far[:, cut:], "ctx", 4)
        return own, by_x, by_y, left, right

    def scatter_more(stage, late):
        if ctx_size != 8:
            return stage
        own, by_x, by_y, left, right = stage
        left, right = after(left, late), after(right, late)
        cut = left.shape[1]
        by_x = jnp.concatenate([by_x[:, :cut], add_low(by_x[:, cut:], right)], axis=1)
        by_y = jnp.concatenate([add_low(by_y[:, :cut], left), by_y[:, cut:]], axis=1)
        return lax.optimization_barrier((own, by_x, by_y))[0], swap(by_x, "ctx", 2), swap(by_y, "ctx", 4)

    def scatter_last(stage, late):
        total = stage[0].astype(F32)
        for piece in stage[1:]:
            total = total + after(piece, late).astype(F32)
        total, size = total.astype(BF), total.shape[0] // 2
        return add_low(total[:size], swap(total[size:], "shard", 1))

    kv_piece, rest_piece = pack(chunk, key_weight, value_weight, w_out, w_gate, w_up, w_down)
    w_kv, stages = gather_rows(kv_piece)
    w_rest = lax.all_gather(rest_piece, weight_axes, axis=0, tiled=True)
    gains = jnp.concatenate([attn_gain, ffn_gain, query_gain, key_gain])[None]
    gains = jnp.where(jnp.arange(parts)[:, None] == part, gains, jnp.zeros((), BF))
    gains = gains + after(swap(gains, "ctx", 1), kv_piece)
    for at, (axis, bit) in enumerate(bits[:-1]):
        gains = gains + after(swap(gains, axis, bit), stages[min(at, 2)])
    gains = gains.astype(F32)
    gain_one = gains[:, :wide].reshape(1, -1)
    gain_two = gains[:, wide : 2 * wide].reshape(1, -1)
    gain_q = gains[:, 2 * wide : 2 * wide + narrow].reshape(1, -1)
    gain_k = gains[:, 2 * wide + narrow :].reshape(1, -1)
    source = jnp.bitwise_xor(part, jnp.array(order, jnp.int32))[:, None] * wide + jnp.arange(wide, dtype=jnp.int32)
    to_slots = (jnp.arange(model, dtype=jnp.int32)[:, None] == source.reshape(1, -1)).astype(BF)
    tokens_s = mm(after(tokens, stages[0]), to_slots).astype(BF)
    gain_one_s = mm(gain_one.astype(BF), to_slots)

    cont_at = me * rows + jnp.arange(rows, dtype=jnp.int32)
    cont_ends = jnp.cumsum(lengths)
    starts = cont_ends - lengths
    seg = jnp.sum((cont_ends[None, :] <= cont_at[:, None]).astype(jnp.int32), axis=1)
    numbers = jnp.arange(lengths.shape[0], dtype=jnp.int32)
    first = jnp.sum(jnp.where(numbers[None, :] == seg[:, None], starts[None, :], 0), axis=1)
    position = jnp.concatenate([me * rows + jnp.arange(rows, dtype=jnp.int32), PROMPT + cont_at - first])
    low = first - me * rows
    low_col = jnp.broadcast_to(low[:, None], (rows, 128))
    low_row = jnp.broadcast_to(jnp.concatenate([low, low])[None, :], (8, 2 * rows))
    scalars = jnp.stack([me, low[0]])
    cos, sin = rotary_tables(position)

    once = lambda f: (0, 0)

    def keys_values(half, gain, whole=None):
        mine = lambda f: (half, 0)
        ins = [
            (tokens_s, (rows, model), mine), (gain, (1, model), once), (w_kv, (model, 2 * k_cols), once),
            (gain_k, (1, HEAD_SIZE), once), (cos, (rows, HEAD_SIZE), mine), (sin, (rows, HEAD_SIZE), mine),
        ]
        keep = {}
        if whole is not None:
            keep = {len(ins): 0}
            ins.append((whole, None, None))
        outs = [
            (shaped((2 * rows, model), BF), (rows, model), mine),
            (shaped((2, rows, k_cols), BF), (2, rows, k_cols), lambda f: (0, 0, 0)),
            (shaped((rows, k_cols), F32), (rows, k_cols), once),
        ]
        return call(functools.partial(kv_kernel, kv_heads), "keys_values", (1,), ins, outs, keep=keep, us=6)

    normed, kv_p, k_lin_p = keys_values(0, gain_one_s)
    w_q, _ = gather_rows(after(w_query, stages[0]), [(v,) for v in stages[1:]] + [(kv_p,)])
    normed, kv_c, k_lin_c = keys_values(1, after(gain_one_s, kv_p), normed)
    mine = lambda f: (f, 0)
    q, q_lin = call(
        functools.partial(q_kernel, heads), "queries", (2,),
        [
            (normed, (rows, model), mine), (w_q, (model, q_cols), lambda f: (0, 0)),
            (gain_q, (1, HEAD_SIZE), lambda f: (0, 0)),
            (cos, (rows, HEAD_SIZE), mine), (sin, (rows, HEAD_SIZE), mine),
        ],
        [(shaped((2 * rows, q_cols), BF), (rows, q_cols), mine), (shaped((2 * rows, q_cols), F32), (rows, q_cols), mine)],
    )

    def pick(source, wanted):
        return {s: source[s] for s in source if s in wanted}

    near, middle, far = (0, 1), (2, 3, 4, 5), tuple(range(6, ctx_size))
    slots, halos = {0: kv_p}, {0: kv_c}
    odd = (me % 2) == 1
    if ctx_size == 8:
        slots[1], slots[2], slots[4] = (swap(kv_p, "ctx", bit) for bit in (1, 2, 4))
    else:
        both, bit = kv_p[None], 1
        while bit < ctx_size:
            both = jnp.concatenate([both, swap(both, "ctx", bit)])
            bit *= 2
        slots = {s: both[s] for s in range(ctx_size)}
        halos.update({d: shift(kv_c, d) for d in range(1, n_halo)})
    state = attention_forward((0, 1), scalars, q, low_col, pick(slots, near), pick(halos, (0,)))
    ready = ()
    if ctx_size == 8:
        slots[2], slots[4] = after(slots[2], state[0]), after(slots[4], state[0])
        far_k, far_v = swap(slots[4][0], "ctx", 2), swap(slots[2][1], "ctx", 4)
        slots[3], slots[5] = swap(slots[2], "ctx", 1), swap(slots[4], "ctx", 1)
        halos[2] = shift(after(kv_c, slots[2]), 2)
    state = attention_forward((0, 1), after(scalars, state[0]), q, low_col, pick(slots, middle), {}, state)
    if ctx_size == 8:
        slots[6] = jnp.stack([after(far_k, state[0]), after(far_v, state[0])])
        slots[7] = swap(slots[6], "ctx", 1)
        halo_one = jnp.where(odd, after(halos[2], slots[7]), kv_c)
        halos[1] = swap(halo_one, "ctx", 1)
        ready = (halo_one,)
    p_state, c_state = state[:2], state[2:]
    attended, lse_p, part_p = attention_forward(
        (0,), after(scalars, c_state[0], *ready), q, low_col, pick(slots, far), {}, p_state, (w_rest, None)
    )
    got_p = swap(part_p, "tensor", 1)
    attended, lse_c, part_c = attention_forward(
        (1,), after(scalars, part_p), q, low_col, pick(slots, far), pick(halos, range(1, n_halo)),
        c_state, (w_rest, attended),
    )
    got_c = swap(part_c, "tensor", 1)

    resid_p, *whole, out_p, back_p = feed_forward(
        0, tokens, part_p, got_p, after(gain_two, part_c), cotangent, w_rest, o_cols, chunk
    )
    back_got_p = swap(back_p, "tensor", 1)
    resid_c, *whole, out_c, back_c = feed_forward(
        1, tokens, part_c, got_c, after(gain_two, back_p), cotangent, w_rest, o_cols, chunk, whole
    )
    back_got_c = swap(back_c, "tensor", 1)
    normed_ffn, hidden, d_gu = whole
    width = o_cols + 3 * units
    rest_grads = weight_grad(normed_ffn, d_gu, o_cols, width, min(1024, o_cols))
    rest_grads = weight_grad(cotangent, hidden, o_cols + 2 * units, width, chunk, rest_grads)
    d_resid_p, d_mixed, d_att_p, delta_p, d_two_p = mixed_back(
        0, back_p, back_got_p, resid_p, after(gain_two, rest_grads), cotangent, w_rest, o_cols, attended
    )
    d_resid_c, d_mixed, d_att_c, delta_c, d_two_c = mixed_back(
        1, back_c, back_got_c, resid_c, after(gain_two, d_att_p), cotangent, w_rest, o_cols, attended, d_mixed
    )
    rest_grads = weight_grad(d_mixed, attended, 0, width, min(1024, o_cols), rest_grads)
    rest_share = lax.psum_scatter(rest_grads, weight_axes, scatter_dimension=0, tiled=True)
    out_p, out_c = after(out_p, back_got_c), after(out_c, back_got_c)
    out_got_p, out_got_c = swap(out_p, "tensor", 1), swap(out_c, "tensor", 1)

    dq_p, from_p, _ = attention_backward(
        0, after(scalars, rest_grads), q, d_att_p, lse_p, delta_p, low_row, slots, {}
    )

    def back_c_rows(deps, slots, halos, carry, last):
        prior = pick(from_p, tuple(slots)) if slots else None
        return attention_backward(
            1, after(scalars, *deps), q, d_att_c, lse_c, delta_c, low_row, slots, halos, carry, prior, last
        )

    dq_c, _, g_halo = back_c_rows((dq_p,), {}, halos, None, False)
    if ctx_size == 8:
        near_one = swap(g_halo[1], "ctx", 1)
    dq_c, g, _ = back_c_rows((dq_c,), pick(slots, far), {}, dq_c, False)
    zero = jnp.zeros((), BF)
    if ctx_size == 8:
        near_one = after(near_one, dq_c)
        two_back = add_low(g_halo[2], jnp.where(odd, near_one, zero))
        halo_two = shift(two_back, -2)
        got7 = swap(g[7], "ctx", 1)
        ready = (two_back,)
    dq_c, more, _ = back_c_rows((dq_c, *ready), pick(slots, middle), {}, dq_c, False)
    g.update(more)
    if ctx_size == 8:
        g6 = add_low(g[6], after(got7, dq_c))
        far_k, far_v = swap(g6[0], "ctx", 2), swap(g6[1], "ctx", 4)
        got3, got5 = swap(g[3], "ctx", 1), swap(g[5], "ctx", 1)
        ready = (g6,)
    if ctx_size == 8:
        ready = (g6,)
    dq_c, more, _ = back_c_rows((dq_c, *ready), pick(slots, near), {}, dq_c, True)
    g.update(more)
    if ctx_size == 8:
        got1 = swap(g[1], "ctx", 1)
        far_k, far_v, got3, got5 = (after(v, dq_c) for v in (far_k, far_v, got3, got5))
        k2, v2 = add_low(g[2][0], got3[0]), add_low(add_low(g[2][1], got3[1]), far_v)
        k4, v4 = add_low(add_low(g[4][0], got5[0]), far_k), add_low(g[4][1], got5[1])
        ready = (k2, v2, k4, v4)
        keys_p = [g[0], got1, swap(k2, "ctx", 2), swap(k4, "ctx", 4)]
        values_p = [g[0], got1, swap(v2, "ctx", 2), swap(v4, "ctx", 4)]
        keys_c = values_c = [g_halo[0], jnp.where(odd, zero, near_one), halo_two]
    else:
        both = jnp.stack([g[s] for s in range(ctx_size)])
        while both.shape[0] > 1:
            size = both.shape[0] // 2
            both = add_low(both[:size], swap(both[size:], "ctx", size))
        keys_p = values_p = [both[0]]
        keys_c = values_c = [g_halo[0]] + [shift(g_halo[d], -d) for d in range(1, n_halo)]

    d_q, q_part_p, heads_p = q_back(0, dq_p, q_lin, after(gain_q, dq_c, *ready), cos, sin, w_q)
    d_q, q_part_c, heads_c = q_back(1, dq_c, q_lin, after(gain_q, q_part_p), cos, sin, w_q, d_q)
    q_high = mm(normed[:, model // 2 :], after(d_q, q_part_c), TN).astype(BF)
    q_low = mm(normed[:, : model // 2], after(d_q, q_high), TN).astype(BF)
    d_kv, into_c, k_heads_c = kv_back(
        1, keys_c, values_c, k_lin_c, after(gain_k, q_low), cos, sin, w_kv, to_slots, q_part_c
    )
    into_got_c = swap(into_c, "tensor", 1)
    q_grad = scatter_rows(q_low, q_high, into_c)
    d_kv, into_p, k_heads_p = kv_back(
        0, keys_p, values_p, k_lin_p, after(gain_k, into_c, q_grad[0]), cos, sin, w_kv, to_slots, q_part_p, d_kv
    )
    into_got_p = swap(into_p, "tensor", 1)
    kv_high = mm(normed[:, model // 2 :], after(d_kv, into_p), TN).astype(BF)
    kv_low = mm(normed[:, : model // 2], after(d_kv, kv_high), TN).astype(BF)
    q_grad = scatter_more(q_grad, kv_low)
    layer_out = jnp.concatenate(
        [
            (resid + (own.astype(F32) + after(got, kv_low).astype(F32))).astype(BF)
            for resid, own, got in ((resid_p, out_p, out_got_p), (resid_c, out_c, out_got_c))
        ]
    )
    rest_share = after(rest_share, kv_low).astype(F32)
    out_share, down_share = rest_share[:, :o_cols].T, rest_share[:, o_cols + 2 * units :].T
    gate_up = rest_share[:, o_cols : o_cols + 2 * units].reshape(wide, units // chunk, 2, chunk)
    gate_share, up_share = gate_up[:, :, 0].reshape(wide, units), gate_up[:, :, 1].reshape(wide, units)
    kv_grad = scatter_rows(kv_low, kv_high, layer_out)
    early = jnp.concatenate([d_two_c + d_two_p, heads_c + heads_p, k_heads_c + k_heads_p], axis=1)
    early = butterfly(after(early, kv_low), ("ctx", "shard"))
    head_gains = butterfly(early[:, model:], ("tensor",))
    grad_tokens, d_one_c = tokens_back(
        1, into_c, into_got_c, tokens, after(gain_one, kv_grad[0], layer_out, gate_share, up_share), d_resid_c
    )
    kv_grad = scatter_more(kv_grad, d_one_c)
    q_share = scatter_last(q_grad, d_one_c).astype(F32)
    grad_tokens, d_one_p = tokens_back(
        0, into_p, into_got_p, tokens, after(gain_one, d_one_c, head_gains, kv_grad[0], out_share, down_share),
        d_resid_p, grad_tokens,
    )
    kv_share = scatter_last(kv_grad, d_one_p).astype(F32)
    late = butterfly(d_one_c + d_one_p, ("ctx", "shard"))

    def own_gain(value, size):
        return lax.dynamic_index_in_dim(value.reshape(-1, parts, size), part, 1, keepdims=False)

    model_gains = own_gain(jnp.concatenate([late, early[:, :model]]), wide)
    head_gains = own_gain(head_gains, narrow)
    return (
        layer_out,
        grad_tokens,
        model_gains[0],
        model_gains[1],
        head_gains[0],
        head_gains[1],
        q_share,
        kv_share[:, :k_cols],
        kv_share[:, k_cols:],
        out_share,
        gate_share,
        up_share,
        down_share,
    )


def solution(mesh):
    split = ("shard", "ctx")
    rows, gain = P(split, None), P(split)
    into, out_of = P(split, "tensor"), P("tensor", split)
    in_specs = (rows, P("shard", None)) + (gain,) * 4 + (into,) * 3 + (out_of,)
    in_specs += (into, into, out_of, rows)
    out_specs = (rows, rows) + (gain,) * 4 + (into,) * 3 + (out_of, into, into, out_of)
    return jax.shard_map(body, mesh=mesh, in_specs=in_specs, out_specs=out_specs, check_vma=False)
```

```python
import functools
import math

import jax
import jax.numpy as jnp
from jax import lax
from jax.experimental import pallas as pl
from jax.experimental.pallas import tpu as pltpu
from jax.sharding import PartitionSpec as P

HEAD_SIZE = 128
PROMPT = 4096
CONT_TOK = 4096
LONGEST = 1024

EPSILON = 1e-06
ROPE_BASE = 1000000.0
MASKED = -1e30
LOG2E = math.log2(math.e)
LN2 = math.log(2.0)
SCALE = 1.0 / math.sqrt(HEAD_SIZE)

BF = jnp.bfloat16
F32 = jnp.float32
NN = (((1,), (0,)), ((), ()))
NT = (((1,), (1,)), ((), ()))
TN = (((0,), (0,)), ((), ()))
MIB = 2**20
STATED = 0


def mm(left, right, dims=NN):
    return lax.dot_general(left, right, dims, preferred_element_type=F32)


def shaped(dims, kind):
    return jax.ShapeDtypeStruct(dims, kind)


def call(kernel, name, grid, ins, outs, scratch=(), vmem=56, scalars=None, keep=None, us=4):
    in_specs, arrays = [], []
    for array, block, index in ins:
        arrays.append(array)
        in_specs.append(pl.BlockSpec(memory_space=pl.ANY) if block is None else pl.BlockSpec(block, index))
    lead = 0 if scalars is None else 1
    return pl.pallas_call(
        kernel,
        grid_spec=pltpu.PrefetchScalarGridSpec(
            num_scalar_prefetch=lead,
            grid=grid,
            in_specs=in_specs,
            out_specs=[pl.BlockSpec(block, index) for _, block, index in outs],
            scratch_shapes=list(scratch),
        ),
        out_shape=[shape for shape, _, _ in outs],
        input_output_aliases={a + lead: b for a, b in (keep or {}).items()},
        compiler_params=pltpu.CompilerParams(vmem_limit_bytes=vmem * MIB),
        cost_estimate=pl.CostEstimate(flops=int(us * STATED), bytes_accessed=0, transcendentals=0),
        name=name,
    )(*([] if scalars is None else [scalars]), *arrays)


def rms(values):
    return lax.rsqrt(jnp.mean(values * values, axis=-1, keepdims=True) + EPSILON)


def turn(values, cos, sin):
    return values * cos + pltpu.roll(values, HEAD_SIZE // 2, 1) * sin


def turn_back(values, cos, sin):
    return values * cos - pltpu.roll(values, HEAD_SIZE // 2, 1) * sin


def kv_kernel(heads, x_ref, gain_ref, w_ref, hgain_ref, cos_ref, sin_ref, *refs):
    normed_ref, kv_ref, lin_ref = refs[-3:]
    x = x_ref[...].astype(F32)
    normed_ref[...] = (x * rms(x) * gain_ref[...]).astype(BF)
    both = mm(normed_ref[...], w_ref[...])
    width = heads * HEAD_SIZE
    kv_ref[1] = both[:, width:].astype(BF)
    for h in range(heads):
        cols = slice(h * HEAD_SIZE, (h + 1) * HEAD_SIZE)
        lin = both[:, cols]
        lin_ref[:, cols] = lin
        kv_ref[0, :, cols] = turn(lin * rms(lin) * hgain_ref[...], cos_ref[...], sin_ref[...]).astype(BF)


def q_kernel(heads, normed_ref, w_ref, hgain_ref, cos_ref, sin_ref, q_ref, lin_ref):
    both = mm(normed_ref[...], w_ref[...])
    for h in range(heads):
        cols = slice(h * HEAD_SIZE, (h + 1) * HEAD_SIZE)
        lin = both[:, cols]
        lin_ref[:, cols] = lin
        turned = turn(lin * rms(lin) * hgain_ref[...], cos_ref[...], sin_ref[...])
        q_ref[:, cols] = (turned * (SCALE * LOG2E)).astype(BF)


def pack_kernel(chunk, key_ref, value_ref, out_ref, gate_ref, up_ref, down_ref, kv_ref, rest_ref):
    k_cols, o_cols, units = key_ref.shape[1], out_ref.shape[1], gate_ref.shape[1]
    kv_ref[:, :k_cols] = key_ref[...]
    kv_ref[:, k_cols:] = value_ref[...]
    rest_ref[:, :o_cols] = out_ref[...]
    for at in range(0, units, chunk):
        to = o_cols + 2 * at
        rest_ref[:, to : to + chunk] = gate_ref[:, at : at + chunk]
        rest_ref[:, to + chunk : to + 2 * chunk] = up_ref[:, at : at + chunk]
    rest_ref[:, o_cols + 2 * units :] = down_ref[...]


def pack(chunk, *weights):
    wide, k_cols = weights[0].shape
    width = weights[2].shape[1] + 3 * weights[3].shape[1]
    whole = lambda f: (0, 0)
    ins = [(w, w.shape, whole) for w in weights]
    outs = [(shaped((wide, cols), BF), (wide, cols), whole) for cols in (2 * k_cols, width)]
    return call(functools.partial(pack_kernel, chunk), "pack", (1,), ins, outs, us=3)


def by_top_bit(slots):
    groups = {}
    for at, s in enumerate(slots):
        if s:
            groups.setdefault(1 << (s.bit_length() - 1), []).append(at)
    return groups


def fwd_kernel(plan, idx_ref, lo_ref, *refs):
    halves, slots, halos = plan["halves"], plan["slots"], plan["halos"]
    refs = list(refs)
    q_refs = [refs.pop(0) for _ in halves]
    slot_refs = [refs.pop(0) for _ in slots]
    halo_refs = [refs.pop(0) for _ in halos]
    prior = [refs.pop(0) for _ in range(2 * len(halves))] if plan["carry"] else None
    if plan["last"]:
        w_ref = refs.pop(0)
        if plan["alias"]:
            refs.pop(0)
        out_ref, lse_ref, part_ref = refs[:3]
        refs = refs[3:]
    else:
        results, refs = refs[: 2 * len(halves)], refs[2 * len(halves) :]
    me, lo_first = idx_ref[0], idx_ref[1]
    rows = q_refs[0].shape[0]
    row = lax.broadcasted_iota(jnp.int32, (2 * rows, 1), 0)
    row = jnp.where(row >= rows, row - rows, row)
    col = lax.broadcasted_iota(jnp.int32, (1, rows), 1)
    for n, half in enumerate(halves):
        qs, acc, tot = refs[3 * n : 3 * n + 3]
        for g in range(2):
            cols, at = slice(g * HEAD_SIZE, (g + 1) * HEAD_SIZE), slice(g * rows, (g + 1) * rows)
            qs[at, :] = q_refs[n][:, cols]
            if prior is not None:
                acc[at, :] = prior[2 * n][:, cols]
                tot[at, :] = prior[2 * n + 1][:, cols]
        empty = [prior is None]

        def add(kv_ref, mask=None):
            scores = mm(qs[...], kv_ref[0], NT)
            if mask is not None:
                scores = jnp.where(mask, scores, MASKED)
            weights = jnp.exp2(scores)
            total = weights[:, :128]
            for at in range(128, weights.shape[1], 128):
                total = total + weights[:, at : at + 128]
            part = mm(weights.astype(BF), kv_ref[1])
            if empty[0]:
                acc[...] = part
                tot[...] = total
            else:
                acc[...] += part
                tot[...] += total
            empty[0] = False

        if half == 1:
            for kv_ref in slot_refs:
                add(kv_ref)
            low = jnp.concatenate([lo_ref[:, :1], lo_ref[:, :1]])
            for d, kv_ref in zip(halos, halo_refs):
                if d == 0:
                    add(kv_ref, (col <= row) & (col >= low))
                else:

                    @pl.when(lo_first < -(d - 1) * rows)
                    def _(d=d, kv_ref=kv_ref):
                        add(kv_ref, col - d * rows >= low)

        else:
            if 0 in slots:
                add(slot_refs[slots.index(0)], col <= row)
            for bit, group in by_top_bit(slots).items():

                @pl.when(jnp.bitwise_and(me, bit) != 0)
                def _(group=group):
                    for at in group:
                        add(slot_refs[at])

        if not plan["last"]:
            for g in range(2):
                cols, at = slice(g * HEAD_SIZE, (g + 1) * HEAD_SIZE), slice(g * rows, (g + 1) * rows)
                results[2 * n][:, cols] = acc[at, :]
                results[2 * n + 1][:, cols] = tot[at, :]
    if plan["last"]:
        qs, acc, tot, part_acc = refs
        step, steps = pl.program_id(0), pl.num_programs(0)
        for g in range(2):
            cols, at = slice(g * HEAD_SIZE, (g + 1) * HEAD_SIZE), slice(g * rows, (g + 1) * rows)
            total = jnp.sum(tot[at, :], axis=1, keepdims=True)
            out_ref[:, cols] = (acc[at, :] / total).astype(BF)
            lse_ref[0, g : g + 1, :] = jnp.log2(jnp.sum(tot[at, :].T, axis=0, keepdims=True))
        part = mm(out_ref[...], w_ref[...], NT)

        @pl.when(step == 0)
        def _():
            part_acc[...] = part

        @pl.when((step > 0) & (step < steps - 1))
        def _():
            part_acc[...] += part

        @pl.when(step == steps - 1)
        def _():
            part_ref[...] = (part_acc[...] + part).astype(BF)


def attention_forward(halves, scalars, q, low, slots, halos, carry=None, last=None):
    rows, heads = q.shape[0] // 2, q.shape[1] // 256
    plan = dict(halves=halves, slots=list(slots), halos=list(halos), carry=carry is not None,
                last=last is not None, alias=last is not None and last[1] is not None)
    part = lambda h, i: (0, h)
    ins = [(low, (rows, 128), lambda h, i: (0, 0))]
    ins += [(q, (rows, 256), lambda h, i, half=half: (half, h)) for half in halves]
    for kv in list(slots.values()) + list(halos.values()):
        ins.append((kv, (2, rows, 128), lambda h, i: (0, 0, h)))
    if carry is not None:
        ins += [(c, (rows, 256), part) for c in carry]
    scratch, keep = [], {}
    for _ in halves:
        scratch += [pltpu.VMEM((2 * rows, 128), BF)] + [pltpu.VMEM((2 * rows, 128), F32)] * 2
    state = shaped((rows, heads * 256), F32)
    if last is None:
        outs = [(state, (rows, 256), part)] * (2 * len(halves))
    else:
        w_rest, other = last
        model = w_rest.shape[0]
        ins.append((w_rest, (model, 256), part))
        if other is not None:
            keep = {len(ins): 0}
            ins.append((other, None, None))
        half = halves[0]
        outs = [
            (shaped((2 * rows, heads * 256), BF), (rows, 256), lambda h, i: (half, h)),
            (shaped((heads, 8, rows), F32), (1, 8, rows), lambda h, i: (h, 0, 0)),
            (shaped((rows, model), BF), (rows, model), lambda h, i: (0, 0)),
        ]
        scratch.append(pltpu.VMEM((rows, model), F32))
    blocks = len(slots) * len(halves) + len(halos)
    return call(functools.partial(fwd_kernel, plan), "attend", (heads,), ins, outs, scratch,
                scalars=scalars, keep=keep, us=2 + 3 * blocks)


def bwd_kernel(plan, idx_ref, q_ref, do_ref, lse_ref, delta_ref, lo_ref, *refs):
    half, slots, halos = plan["half"], plan["slots"], plan["halos"]
    refs = list(refs)
    slot_refs = [refs.pop(0) for _ in slots]
    halo_refs = [refs.pop(0) for _ in halos]
    prior_dq = refs.pop(0) if plan["carry"] else None
    prior = [refs.pop(0) for _ in slots] if plan["sum"] else None
    if plan["alias"]:
        refs.pop(0)
    dq_ref = refs.pop(0)
    slot_outs = [refs.pop(0) for _ in slots]
    halo_outs = [refs.pop(0) for _ in halos]
    qs, dos, lses, deltas, dq = refs
    me, lo_first = idx_ref[0], idx_ref[1]
    rows = q_ref.shape[0]
    for g in range(2):
        cols, at = slice(g * HEAD_SIZE, (g + 1) * HEAD_SIZE), slice(g * rows, (g + 1) * rows)
        qs[at, :] = q_ref[:, cols]
        dos[at, :] = do_ref[:, cols]
        lses[:, at] = lse_ref[0, g : g + 1, :]
        deltas[:, at] = delta_ref[0, g : g + 1, :]
    dq[...] = jnp.zeros_like(dq) if prior_dq is None else prior_dq[...]

    def block(kv_ref, out_ref, mask=None, before=None):
        keys = kv_ref[0]
        scores = mm(keys, qs[...], NT)
        dp = mm(kv_ref[1], dos[...], NT)
        scores = scores - lses[...]
        if mask is not None:
            scores = jnp.where(mask, scores, MASKED)
        probs = jnp.exp2(scores)
        ds = (probs * (dp - deltas[...])).astype(BF)
        dq[...] += mm(keys.T, ds)
        dk, dv = mm(ds, qs[...]) * LN2, mm(probs.astype(BF), dos[...])
        if before is not None:
            dk, dv = dk + before[0].astype(F32), dv + before[1].astype(F32)
        out_ref[0] = dk.astype(BF)
        out_ref[1] = dv.astype(BF)

    lane = lax.broadcasted_iota(jnp.int32, (1, 2 * rows), 1)
    lane = jnp.where(lane >= rows, lane - rows, lane)
    key = lax.broadcasted_iota(jnp.int32, (rows, 1), 0)

    def when(needed, kv_ref, out_ref, mask=None):
        @pl.when(needed)
        def _():
            block(kv_ref, out_ref, mask)

        @pl.when(jnp.logical_not(needed))
        def _():
            out_ref[...] = jnp.zeros_like(out_ref)

    low = lo_ref[:1, :]
    for d, kv_ref, out_ref in zip(halos, halo_refs, halo_outs):
        if d == 0:
            block(kv_ref, out_ref, (key <= lane) & (key >= low))
        else:
            when(lo_first < -(d - 1) * rows, kv_ref, out_ref, key - d * rows >= low)
    if half == 1:
        for at in range(len(slots)):
            block(slot_refs[at], slot_outs[at], None, prior[at])
    else:
        if 0 in slots:
            at = slots.index(0)
            block(slot_refs[at], slot_outs[at], key <= lane)
        for bit, group in by_top_bit(slots).items():

            @pl.when(jnp.bitwise_and(me, bit) != 0)
            def _(group=group):
                for at in group:
                    block(slot_refs[at], slot_outs[at])

            @pl.when(jnp.bitwise_and(me, bit) == 0)
            def _(group=group):
                for at in group:
                    slot_outs[at][...] = jnp.zeros_like(slot_outs[at])

    if plan["last"]:
        for g in range(2):
            cols = slice(g * HEAD_SIZE, (g + 1) * HEAD_SIZE)
            dq_ref[:, cols] = dq[:, g * rows : (g + 1) * rows].T * SCALE
    else:
        dq_ref[...] = dq[...]


def attention_backward(half, scalars, q, do, lse, delta, low, slots, halos, carry=None, prior=None, last=True, whole=None):
    rows, heads = q.shape[0] // 2, q.shape[1] // 256
    plan = dict(half=half, slots=list(slots), halos=list(halos), carry=carry is not None,
                sum=prior is not None, last=last, alias=whole is not None)
    part = lambda h, i: (0, h)
    stat = lambda h, i: (h, 0, 0)
    kv_map = lambda h, i: (0, 0, h)
    ins = [
        (q, (rows, 256), lambda h, i: (half, h)),
        (do, (rows, 256), part),
        (lse, (1, 8, rows), stat),
        (delta, (1, 8, rows), stat),
        (low, (8, 2 * rows), lambda h, i: (0, 0)),
    ]
    pieces = list(slots.values()) + list(halos.values())
    ins += [(kv, (2, rows, 128), kv_map) for kv in pieces]
    if carry is not None:
        ins.append((carry, (128, 2 * rows), lambda h, i: (h, 0)))
    if prior is not None:
        ins += [(prior[s], (2, rows, 128), kv_map) for s in slots]
    keep = {}
    if whole is not None:
        keep = {len(ins): 0}
        ins.append((whole, None, None))
    if last:
        outs = [(shaped((2 * rows, heads * 256), F32), (rows, 256), lambda h, i: (half, h))]
    else:
        outs = [(shaped((heads * 128, 2 * rows), F32), (128, 2 * rows), lambda h, i: (h, 0))]
    outs += [(shaped(kv.shape, BF), (2, rows, 128), kv_map) for kv in pieces]
    scratch = [
        pltpu.VMEM((2 * rows, 128), BF),
        pltpu.VMEM((2 * rows, 128), BF),
        pltpu.VMEM((1, 2 * rows), F32),
        pltpu.VMEM((1, 2 * rows), F32),
        pltpu.VMEM((128, 2 * rows), F32),
    ]
    us = 4 + 6 * (len(slots) + len(halos))
    results = call(functools.partial(bwd_kernel, plan), "attend_back", (heads,), ins, outs, scratch,
                   scalars=scalars, us=us, keep=keep)
    n = len(slots)
    return results[0], dict(zip(slots, results[1 : 1 + n])), dict(zip(halos, results[1 + n :]))


def ffn_kernel(x_ref, own_ref, got_ref, gain_ref, dy_ref, gu_ref, down_ref, *refs):
    resid_ref, normed_ref, hidden_ref, dgu_ref, out_ref, back_ref, normed, out_acc, back_acc = refs[-9:]
    step, steps = pl.program_id(0), pl.num_programs(0)

    @pl.when(step == 0)
    def _():
        resid = x_ref[...].astype(F32) + (own_ref[...].astype(F32) + got_ref[...].astype(F32))
        resid_ref[...] = resid
        normed[...] = (resid * rms(resid) * gain_ref[...]).astype(BF)
        normed_ref[...] = normed[...]
        out_acc[...] = jnp.zeros_like(out_acc)
        back_acc[...] = jnp.zeros_like(back_acc)

    wide = down_ref.shape[1]
    both = mm(normed[...], gu_ref[...])
    d_hidden = mm(dy_ref[...], down_ref[...])
    gate, up = both[:, :wide], both[:, wide:]
    sig = 1.0 / (1.0 + jnp.exp(-gate))
    silu = gate * sig
    hidden = (silu * up).astype(BF)
    hidden_ref[...] = hidden
    d_up = (d_hidden * silu).astype(BF)
    d_gate = (d_hidden * up * (sig + silu * (1.0 - sig))).astype(BF)
    dgu_ref[:, :wide] = d_gate
    dgu_ref[:, wide:] = d_up
    out_acc[...] += mm(hidden, down_ref[...], NT)
    back_acc[...] += mm(dgu_ref[...], gu_ref[...], NT)

    @pl.when(step == steps - 1)
    def _():
        out_ref[...] = out_acc[...].astype(BF)
        back_ref[...] = back_acc[...].astype(BF)


def feed_forward(half, x, own, got, gain, dy, w_rest, o_cols, chunk, whole=None):
    rows, model = own.shape
    units = (w_rest.shape[1] - o_cols) // 3
    steps = units // chunk
    mine, once = lambda f: (half, 0), lambda f: (0, 0)
    at_gu, at_down = o_cols // (2 * chunk), (o_cols + 2 * units) // chunk
    block = (rows, model)
    ins = [
        (x, block, mine), (own, block, once), (got, block, once), (gain, (1, model), once), (dy, block, mine),
        (w_rest, (model, 2 * chunk), lambda f: (0, at_gu + f)),
        (w_rest, (model, chunk), lambda f: (0, at_down + f)),
    ]
    keep = {}
    if whole is not None:
        keep = {len(ins) + i: 1 + i for i in range(3)}
        ins += [(array, None, None) for array in whole]
    outs = [
        (shaped((rows, model), F32), block, once),
        (shaped((2 * rows, model), BF), block, mine),
        (shaped((2 * rows, units), BF), (rows, chunk), lambda f: (half, f)),
        (shaped((2 * rows, 2 * units), BF), (rows, 2 * chunk), lambda f: (half, f)),
        (shaped((rows, model), BF), block, once),
        (shaped((rows, model), BF), block, once),
    ]
    scratch = [pltpu.VMEM(block, BF), pltpu.VMEM(block, F32), pltpu.VMEM(block, F32)]
    return call(ffn_kernel, "feed_forward", (steps,), ins, outs, scratch, keep=keep, us=18)


def norm_back(grad, values, gain):
    scale = rms(values)
    unit = values * scale
    inner = grad * gain
    return scale * (inner - unit * jnp.mean(inner * unit, axis=-1, keepdims=True)), grad * unit


def row_blocks(rows):
    size = rows // 2 if rows % 512 == 0 else rows
    return size, rows // size


def add_up(ref, value):
    total = jnp.sum(value, axis=0, keepdims=True)

    @pl.when(pl.program_id(0) == 0)
    def _():
        ref[...] = total

    @pl.when(pl.program_id(0) > 0)
    def _():
        ref[...] += total


def mixed_kernel(heads, own_ref, got_ref, resid_ref, gain_ref, dy_ref, w_ref, att_ref, *refs):
    d_resid_ref, mixed_ref, datt_ref, delta_ref, dgain_ref = refs[-5:]
    grad = own_ref[...].astype(F32) + got_ref[...].astype(F32)
    d_norm, summand = norm_back(grad, resid_ref[...], gain_ref[...])
    add_up(dgain_ref, summand)
    d_resid = dy_ref[...].astype(F32) + d_norm
    d_resid_ref[...] = d_resid
    mixed_ref[...] = d_resid.astype(BF)
    datt_ref[...] = mm(mixed_ref[...], w_ref[...]).astype(BF)
    for h in range(heads):
        cols = slice(h * HEAD_SIZE, (h + 1) * HEAD_SIZE)
        product = datt_ref[:, cols].astype(F32) * att_ref[:, cols].astype(F32)
        delta_ref[h // 2, h % 2 : h % 2 + 1, :] = jnp.sum(product.T, axis=0, keepdims=True)


def mixed_back(half, own, got, resid, gain, dy, w_rest, o_cols, attended, whole=None):
    rows, model = own.shape
    heads = o_cols // HEAD_SIZE
    size, steps = row_blocks(rows)
    mine, here, once = lambda f: (half * steps + f, 0), lambda f: (f, 0), lambda f: (0, 0)
    block = (size, model)
    ins = [
        (own, block, here), (got, block, here), (resid, block, here), (gain, (1, model), once),
        (dy, block, mine), (w_rest, (model, o_cols), once), (attended, (size, o_cols), mine),
    ]
    keep = {}
    if whole is not None:
        keep = {len(ins): 1}
        ins.append((whole, None, None))
    outs = [
        (shaped((rows, model), F32), block, here),
        (shaped((2 * rows, model), BF), block, mine),
        (shaped((rows, o_cols), BF), (size, o_cols), here),
        (shaped((heads // 2, 8, rows), F32), (heads // 2, 8, size), lambda f: (0, 0, f)),
        (shaped((1, model), F32), (1, model), once),
    ]
    return call(functools.partial(mixed_kernel, heads), "mixed_back", (steps,), ins, outs, keep=keep, us=7)


def merge_kernel(two, got3, four, got5, far_k, far_v, to_x, to_y):
    for which in range(2):
        by_x = two[which].astype(F32) + got3[which].astype(F32)
        by_y = four[which].astype(F32) + got5[which].astype(F32)
        to_x[which] = (by_x + far_v[...].astype(F32) if which else by_x).astype(BF)
        to_y[which] = (by_y if which else by_y + far_k[...].astype(F32)).astype(BF)


def merge(*pieces):
    rows, cols = pieces[-1].shape
    size, steps = row_blocks(rows)
    ins = []
    for piece in pieces:
        if piece.ndim == 3:
            ins.append((piece, (2, size, cols), lambda f: (0, f, 0)))
        else:
            ins.append((piece, (size, cols), lambda f: (f, 0)))
    outs = [(shaped((2, rows, cols), BF), (2, size, cols), lambda f: (0, f, 0))] * 2
    return call(merge_kernel, "merge", (steps,), ins, outs, us=4)


def weight_kernel(left_ref, right_ref, *refs):
    refs[-1][...] = mm(left_ref[...], right_ref[...], TN).astype(BF)


def weight_grad(left, right, at, width, cols, whole=None):
    tokens, model = left.shape
    n = right.shape[1]
    ins = [(left, (tokens, model), lambda j: (0, 0)), (right, (tokens, cols), lambda j: (0, j))]
    keep = {}
    if whole is not None:
        keep = {len(ins): 0}
        ins.append((whole, None, None))
    outs = [(shaped((model, width), BF), (model, cols), lambda j: (0, at // cols + j))]
    return call(weight_kernel, "weight_grad", (n // cols,), ins, outs, keep=keep)[0]


def qkv_weight_kernel(left_ref, q_ref, kv_ref, high_ref, low_ref):
    for half, out_ref in enumerate((high_ref, low_ref)):
        for which, right_ref in enumerate((q_ref, kv_ref)):

            @pl.when((pl.program_id(0) == half) & (pl.program_id(1) == which))
            def _(out_ref=out_ref, right_ref=right_ref):
                out_ref[...] = mm(left_ref[...], right_ref[...], TN).astype(BF)


def qkv_weight_grad(left, d_q, d_kv):
    tokens, model = left.shape
    cols = d_q.shape[1]
    ins = [
        (left, (tokens, model // 2), lambda i, j: (0, 1 - i)),
        (d_q, (tokens, cols), lambda i, j: (0, 0)),
        (d_kv, (tokens, cols), lambda i, j: (0, 0)),
    ]
    half, block = shaped((model // 2, 2 * cols), BF), (model // 2, cols)
    outs = [(half, block, lambda i, j: (0, jnp.where(i == 0, j, 1))), (half, block, lambda i, j: (0, i * j))]
    return call(qkv_weight_kernel, "qkv_weight_grad", (2, 2), ins, outs)


def q_back_kernel(heads, dq_ref, lin_ref, gain_ref, cos_ref, sin_ref, w_ref, *refs):
    d_ref, part_ref, gains_ref = refs[-3:]
    cos, sin = cos_ref[...], sin_ref[...]
    total = jnp.zeros(cos.shape, F32)
    for h in range(heads):
        cols = slice(h * HEAD_SIZE, (h + 1) * HEAD_SIZE)
        grad, summand = norm_back(turn_back(dq_ref[:, cols], cos, sin), lin_ref[:, cols], gain_ref[...])
        d_ref[:, cols] = grad.astype(BF)
        total = total + summand
    part_ref[...] = mm(d_ref[...], w_ref[...], NT)
    add_up(gains_ref, total)


def q_back(dq, lin, gain, cos, sin, w):
    rows, cols = dq.shape
    model = w.shape[0]
    size, steps = row_blocks(rows)
    here, once = lambda f: (f, 0), lambda f: (0, 0)
    ins = [
        (dq, (size, cols), here), (lin, (size, cols), here), (gain, (1, HEAD_SIZE), once),
        (cos, (size, HEAD_SIZE), here), (sin, (size, HEAD_SIZE), here), (w, (model, cols), once),
    ]
    outs = [
        (shaped((rows, cols), BF), (size, cols), here),
        (shaped((rows, model), F32), (size, model), here),
        (shaped((1, HEAD_SIZE), F32), (1, HEAD_SIZE), once),
    ]
    kernel = functools.partial(q_back_kernel, cols // HEAD_SIZE)
    return call(kernel, "q_back", (steps,), ins, outs)


def kv_back_kernel(heads, n_keys, n_values, lin_ref, gain_ref, cos_ref, sin_ref, w_ref, slots_ref, q_part_ref, *refs):
    key_refs, value_refs = refs[:n_keys], refs[n_keys : n_keys + n_values]
    d_ref, part_ref, gains_ref = refs[-3:]
    cos, sin = cos_ref[...], sin_ref[...]
    width = heads * HEAD_SIZE

    def total(sources, which, cols):
        value = None
        for ref in sources:
            piece = ref[which, :, cols] if len(ref.shape) == 3 else ref[:, cols]
            value = piece.astype(F32) if value is None else value + piece.astype(F32)
        return value

    gains = jnp.zeros(cos.shape, F32)
    for h in range(heads):
        cols = slice(h * HEAD_SIZE, (h + 1) * HEAD_SIZE)
        grad, summand = norm_back(
            turn_back(total(key_refs, 0, cols), cos, sin), lin_ref[:, cols], gain_ref[...]
        )
        d_ref[:, cols] = grad.astype(BF)
        gains = gains + summand
    d_ref[:, width:] = total(value_refs, 1, slice(None)).astype(BF)
    part = (q_part_ref[...] + mm(d_ref[...], w_ref[...], NT)).astype(BF)
    part_ref[...] = mm(part, slots_ref[...], NT).astype(BF)
    add_up(gains_ref, gains)


def kv_back(half, keys, values, lin, gain, cos, sin, w, to_slots, q_part, whole=None):
    rows, cols = lin.shape
    model = w.shape[0]
    size, steps = row_blocks(rows)
    mine, here, once = lambda f: (half * steps + f, 0), lambda f: (f, 0), lambda f: (0, 0)
    ins = [
        (lin, (size, cols), here), (gain, (1, HEAD_SIZE), once), (cos, (size, HEAD_SIZE), mine),
        (sin, (size, HEAD_SIZE), mine), (w, (model, 2 * cols), once),
        (to_slots, (model, model), once), (q_part, (size, model), mine),
    ]
    for piece in list(keys) + list(values):
        if piece.ndim == 3:
            ins.append((piece, (2, size, cols), lambda f: (0, f, 0)))
        else:
            ins.append((piece, (size, cols), here))
    keep = {}
    if whole is not None:
        keep = {len(ins): 0}
        ins.append((whole, None, None))
    outs = [
        (shaped((2 * rows, 2 * cols), BF), (size, 2 * cols), mine),
        (shaped((rows, model), BF), (size, model), here),
        (shaped((1, HEAD_SIZE), F32), (1, HEAD_SIZE), once),
    ]
    kernel = functools.partial(kv_back_kernel, cols // HEAD_SIZE, len(keys), len(values))
    return call(kernel, "kv_back", (steps,), ins, outs, keep=keep, us=8)


def tokens_kernel(own_ref, got_ref, x_ref, gain_ref, d_resid_ref, *refs):
    out_ref, dgain_ref = refs[-2:]
    grad = own_ref[...].astype(F32) + got_ref[...].astype(F32)
    d_norm, summand = norm_back(grad, x_ref[...].astype(F32), gain_ref[...])
    add_up(dgain_ref, summand)
    out_ref[...] = (d_resid_ref[...] + d_norm).astype(BF)


def tokens_back(half, own, got, x, gain, d_resid, whole=None):
    rows, model = own.shape
    size, steps = row_blocks(rows)
    mine, here, once = lambda f: (half * steps + f, 0), lambda f: (f, 0), lambda f: (0, 0)
    block = (size, model)
    ins = [(own, block, here), (got, block, here), (x, block, mine), (gain, (1, model), once), (d_resid, block, here)]
    keep = {}
    if whole is not None:
        keep = {len(ins): 0}
        ins.append((whole, None, None))
    outs = [(shaped((2 * rows, model), BF), block, mine), (shaped((1, model), F32), (1, model), once)]
    return call(tokens_kernel, "tokens_back", (steps,), ins, outs, keep=keep, us=4)


def share_kernel(chunk, share_ref, out_ref, gate_ref, up_ref, down_ref):
    o_cols, units = out_ref.shape[1], gate_ref.shape[1]
    out_ref[...] = share_ref[:, :o_cols].astype(F32)
    for at in range(0, units, chunk):
        to = o_cols + 2 * at
        gate_ref[:, at : at + chunk] = share_ref[:, to : to + chunk].astype(F32)
        up_ref[:, at : at + chunk] = share_ref[:, to + chunk : to + 2 * chunk].astype(F32)
    down_ref[...] = share_ref[:, o_cols + 2 * units :].astype(F32)


def unpack(chunk, o_cols, share):
    wide = share.shape[0]
    units = (share.shape[1] - o_cols) // 3
    whole = lambda f: (0, 0)
    outs = [(shaped((wide, cols), F32), (wide, cols), whole) for cols in (o_cols, units, units, units)]
    return call(functools.partial(share_kernel, chunk), "unpack", (1,), [(share, share.shape, whole)], outs)


def layer_kernel(resid_ref, own_ref, got_ref, *refs):
    refs[-1][...] = (resid_ref[...] + (own_ref[...].astype(F32) + got_ref[...].astype(F32))).astype(BF)


def add_layer(half, resid, own, got, whole=None):
    rows, model = resid.shape
    size, steps = row_blocks(rows)
    here, mine = lambda f: (f, 0), lambda f: (half * steps + f, 0)
    ins = [(array, (size, model), here) for array in (resid, own, got)]
    keep = {}
    if whole is not None:
        keep = {len(ins): 0}
        ins.append((whole, None, None))
    outs = [(shaped((2 * rows, model), BF), (size, model), mine)]
    return call(layer_kernel, "add_layer", (steps,), ins, outs, keep=keep, us=3)[0]


def swap(value, axis, bit):
    size = lax.axis_size(axis)
    return lax.ppermute(value, axis, [(i, i ^ bit) for i in range(size)])


def shift(value, by):
    size = lax.axis_size("ctx")
    return lax.ppermute(value, "ctx", [(i, i + by) for i in range(size) if 0 <= i + by < size])


def add_low(left, right):
    return (left.astype(F32) + right.astype(F32)).astype(BF)


def butterfly(value, axes, gates=()):
    gates = list(gates)
    for axis in axes:
        bit = 1
        while bit < lax.axis_size(axis):
            got = swap(value, axis, bit)
            value = value + (after(got, gates.pop(0)) if gates else got)
            bit *= 2
    return value


def after(value, *others):
    return lax.optimization_barrier((value, *others))[0]


def rotary_tables(position):
    half_dim = HEAD_SIZE // 2
    inverse_freq = jnp.exp(jnp.arange(half_dim, dtype=F32) * (-math.log(ROPE_BASE) / half_dim))
    angles = position.astype(F32)[:, None] * inverse_freq[None, :]
    cosine, sine = jnp.cos(angles), jnp.sin(angles)
    return jnp.concatenate([cosine, cosine], axis=-1), jnp.concatenate([-sine, sine], axis=-1)


def body(
    tokens,
    cont_lengths,
    attn_gain,
    ffn_gain,
    query_gain,
    key_gain,
    w_query,
    key_weight,
    value_weight,
    w_out,
    w_gate,
    w_up,
    w_down,
    cotangent,
):
    ctx_size = lax.axis_size("ctx")
    weight_axes = ("shard", "ctx")
    parts = lax.axis_size("shard") * ctx_size
    me = lax.axis_index("ctx")
    part = lax.axis_index("shard") * ctx_size + me
    rows, model = tokens.shape[0] // 2, tokens.shape[1]
    n_halo = 1 + -(-(LONGEST - 1) // rows)
    lengths = cont_lengths[0]

    bits = [("shard", 1)] + [("ctx", 1 << i) for i in range(1, ctx_size.bit_length() - 1)] + [("ctx", 1)]
    order = [0]
    for axis, bit in bits:
        order += [j ^ (bit * ctx_size if axis == "shard" else bit) for j in order]
    wide, narrow = attn_gain.shape[0], query_gain.shape[0]
    q_cols, k_cols = w_query.shape[1], key_weight.shape[1]
    o_cols, units = w_out.shape[0], w_gate.shape[1]
    heads, kv_heads = q_cols // HEAD_SIZE, k_cols // HEAD_SIZE
    chunk = math.gcd(units, 512)

    def gather_rows(piece, gates=((),) * 4):
        if ctx_size != 8:
            for axis, bit in bits:
                piece = jnp.concatenate([piece, swap(piece, axis, bit)])
            return piece, (piece,) * 4
        one = jnp.concatenate([piece, after(swap(piece, "shard", 1), *gates[0])])
        by_x, by_y = (after(v, *gates[1]) for v in (swap(one, "ctx", 2), swap(one, "ctx", 4)))
        cut = one.shape[1] // 2
        left, right = swap(by_y[:, :cut], "ctx", 2), swap(by_x[:, cut:], "ctx", 4)
        far = jnp.concatenate([after(left, *gates[2]), after(right, *gates[2])], axis=1)
        half = jnp.concatenate([one, by_x, by_y, far])
        whole = jnp.concatenate([half, after(swap(half, "ctx", 1), *gates[3])])
        return whole, (one, by_x, half, whole)

    def scatter_rows(low, high, late):
        total = add_low(low, after(swap(high, "ctx", 1), late))
        if ctx_size != 8:
            for axis, bit in bits[-2:0:-1]:
                size = total.shape[0] // 2
                total = add_low(total[:size], swap(total[size:], axis, bit))
            return (total,)
        size, cut = total.shape[0] // 4, total.shape[1] // 2
        own, by_x, by_y, far = (total[i * size : (i + 1) * size] for i in range(4))
        left, right = swap(far[:, :cut], "ctx", 2), swap(far[:, cut:], "ctx", 4)
        return own, by_x, by_y, left, right

    def scatter_more(stage, late):
        if ctx_size != 8:
            return stage
        own, by_x, by_y, left, right = stage
        left, right = after(left, late), after(right, late)
        cut = left.shape[1]
        by_x = jnp.concatenate([by_x[:, :cut], add_low(by_x[:, cut:], right)], axis=1)
        by_y = jnp.concatenate([add_low(by_y[:, :cut], left), by_y[:, cut:]], axis=1)
        return lax.optimization_barrier((own, by_x, by_y))[0], swap(by_x, "ctx", 2), swap(by_y, "ctx", 4)

    def scatter_sum(stage, late):
        total = stage[0].astype(F32)
        for piece in stage[1:]:
            total = total + after(piece, late).astype(F32)
        total, size = total.astype(BF), total.shape[0] // 2
        return total, swap(total[size:], "shard", 1)

    kv_piece, rest_piece = pack(chunk, key_weight, value_weight, w_out.T, w_gate, w_up, w_down.T)
    w_kv, stages = gather_rows(kv_piece)
    w_rest = lax.all_gather(rest_piece, weight_axes, axis=0, tiled=True)
    gains = jnp.concatenate([attn_gain, ffn_gain, query_gain, key_gain])[None]
    gains = jnp.where(jnp.arange(parts)[:, None] == part, gains, jnp.zeros((), BF))
    gains = gains + after(swap(gains, "ctx", 1), kv_piece)
    for at, (axis, bit) in enumerate(bits[:-1]):
        gains = gains + after(swap(gains, axis, bit), stages[min(at, 2)])
    gains = gains.astype(F32)
    gain_one = gains[:, :wide].reshape(1, -1)
    gain_two = gains[:, wide : 2 * wide].reshape(1, -1)
    gain_q = gains[:, 2 * wide : 2 * wide + narrow].reshape(1, -1)
    gain_k = gains[:, 2 * wide + narrow :].reshape(1, -1)
    source = jnp.bitwise_xor(part, jnp.array(order, jnp.int32))[:, None] * wide + jnp.arange(wide, dtype=jnp.int32)
    to_slots = (jnp.arange(model, dtype=jnp.int32)[:, None] == source.reshape(1, -1)).astype(BF)
    tokens_s = mm(after(tokens, stages[0]), to_slots).astype(BF)
    gain_one_s = mm(gain_one.astype(BF), to_slots)

    cont_at = me * rows + jnp.arange(rows, dtype=jnp.int32)
    cont_ends = jnp.cumsum(lengths)
    starts = cont_ends - lengths
    seg = jnp.sum((cont_ends[None, :] <= cont_at[:, None]).astype(jnp.int32), axis=1)
    numbers = jnp.arange(lengths.shape[0], dtype=jnp.int32)
    first = jnp.sum(jnp.where(numbers[None, :] == seg[:, None], starts[None, :], 0), axis=1)
    position = jnp.concatenate([me * rows + jnp.arange(rows, dtype=jnp.int32), PROMPT + cont_at - first])
    low = first - me * rows
    low_col = jnp.broadcast_to(low[:, None], (rows, 128))
    low_row = jnp.broadcast_to(jnp.concatenate([low, low])[None, :], (8, 2 * rows))
    scalars = jnp.stack([me, low[0]])
    cos, sin = rotary_tables(position)

    once = lambda f: (0, 0)

    def keys_values(half, gain, whole=None):
        mine = lambda f: (half, 0)
        ins = [
            (tokens_s, (rows, model), mine), (gain, (1, model), once), (w_kv, (model, 2 * k_cols), once),
            (gain_k, (1, HEAD_SIZE), once), (cos, (rows, HEAD_SIZE), mine), (sin, (rows, HEAD_SIZE), mine),
        ]
        keep = {}
        if whole is not None:
            keep = {len(ins): 0}
            ins.append((whole, None, None))
        outs = [
            (shaped((2 * rows, model), BF), (rows, model), mine),
            (shaped((2, rows, k_cols), BF), (2, rows, k_cols), lambda f: (0, 0, 0)),
            (shaped((rows, k_cols), F32), (rows, k_cols), once),
        ]
        return call(functools.partial(kv_kernel, kv_heads), "keys_values", (1,), ins, outs, keep=keep, us=6)

    normed, kv_p, k_lin_p = keys_values(0, gain_one_s)
    normed, kv_c, k_lin_c = keys_values(1, after(gain_one_s, kv_p), normed)
    w_q, _ = gather_rows(after(w_query, stages[0]), ((stages[1],), (w_kv,), (kv_p,), (kv_c,)))
    mine = lambda f: (f, 0)
    q, q_lin = call(
        functools.partial(q_kernel, heads), "queries", (2,),
        [
            (normed, (rows, model), mine), (w_q, (model, q_cols), lambda f: (0, 0)),
            (gain_q, (1, HEAD_SIZE), lambda f: (0, 0)),
            (cos, (rows, HEAD_SIZE), mine), (sin, (rows, HEAD_SIZE), mine),
        ],
        [(shaped((2 * rows, q_cols), BF), (rows, q_cols), mine), (shaped((2 * rows, q_cols), F32), (rows, q_cols), mine)],
    )

    def pick(source, wanted):
        return {s: source[s] for s in source if s in wanted}

    near, middle, far = (0, 1), (2, 3, 4, 5), tuple(range(6, ctx_size))
    slots, halos = {0: kv_p}, {0: kv_c}
    odd = (me % 2) == 1
    if ctx_size == 8:
        slots[1], slots[2], slots[4] = (swap(kv_p, "ctx", bit) for bit in (1, 2, 4))
    else:
        both, bit = kv_p[None], 1
        while bit < ctx_size:
            both = jnp.concatenate([both, swap(both, "ctx", bit)])
            bit *= 2
        slots = {s: both[s] for s in range(ctx_size)}
        halos.update({d: shift(kv_c, d) for d in range(1, n_halo)})
    state = attention_forward((0, 1), scalars, q, low_col, pick(slots, near), pick(halos, (0,)))
    ready = ()
    if ctx_size == 8:
        slots[2], slots[4] = after(slots[2], state[0]), after(slots[4], state[0])
        far_k, far_v = swap(slots[4][0], "ctx", 2), swap(slots[2][1], "ctx", 4)
        slots[3], slots[5] = swap(slots[2], "ctx", 1), swap(slots[4], "ctx", 1)
        halos[2] = shift(after(kv_c, slots[2]), 2)
    state = attention_forward((0, 1), after(scalars, state[0]), q, low_col, pick(slots, middle), {}, state)
    if ctx_size == 8:
        slots[6] = jnp.stack([after(far_k, state[0]), after(far_v, state[0])])
        slots[7] = swap(slots[6], "ctx", 1)
        halo_one = jnp.where(odd, after(halos[2], slots[7]), kv_c)
        halos[1] = swap(halo_one, "ctx", 1)
        ready = (halo_one,)
    p_state, c_state = state[:2], state[2:]
    attended, lse_p, part_p = attention_forward(
        (0,), after(scalars, c_state[0], *ready), q, low_col, pick(slots, far), {}, p_state, (w_rest, None)
    )
    got_p = swap(part_p, "tensor", 1)
    attended, lse_c, part_c = attention_forward(
        (1,), after(scalars, part_p), q, low_col, pick(slots, far), pick(halos, range(1, n_halo)),
        c_state, (w_rest, attended),
    )
    got_c = swap(part_c, "tensor", 1)

    resid_p, *whole, out_p, back_p = feed_forward(
        0, tokens, part_p, got_p, after(gain_two, part_c), cotangent, w_rest, o_cols, chunk
    )
    back_got_p = swap(back_p, "tensor", 1)
    resid_c, *whole, out_c, back_c = feed_forward(
        1, tokens, part_c, got_c, after(gain_two, back_p), cotangent, w_rest, o_cols, chunk, whole
    )
    back_got_c = swap(back_c, "tensor", 1)
    normed_ffn, hidden, d_gu = whole
    width = o_cols + 3 * units
    rest_grads = weight_grad(normed_ffn, d_gu, o_cols, width, min(1024, o_cols))
    rest_grads = weight_grad(cotangent, hidden, o_cols + 2 * units, width, chunk, rest_grads)
    d_resid_p, d_mixed, d_att_p, delta_p, d_two_p = mixed_back(
        0, back_p, back_got_p, resid_p, after(gain_two, rest_grads), cotangent, w_rest, o_cols, attended
    )
    d_resid_c, d_mixed, d_att_c, delta_c, d_two_c = mixed_back(
        1, back_c, back_got_c, resid_c, after(gain_two, d_att_p), cotangent, w_rest, o_cols, attended, d_mixed
    )
    rest_grads = weight_grad(d_mixed, attended, 0, width, min(1024, o_cols), rest_grads)
    rest_share = lax.psum_scatter(rest_grads, weight_axes, scatter_dimension=0, tiled=True)
    out_p, out_c = after(out_p, back_got_c), after(out_c, back_got_c)
    out_got_p, out_got_c = swap(out_p, "tensor", 1), swap(out_c, "tensor", 1)

    dq, from_p, _ = attention_backward(
        0, after(scalars, rest_grads), q, d_att_p, lse_p, delta_p, low_row, slots, {}
    )

    def back_c_rows(deps, slots, halos, carry, whole=None):
        prior = pick(from_p, tuple(slots)) if slots else None
        return attention_backward(
            1, after(scalars, *deps), q, d_att_c, lse_c, delta_c, low_row, slots, halos, carry, prior,
            whole is not None, whole,
        )

    dq_c, _, g_halo = back_c_rows((dq, out_got_p, out_got_c), {}, halos, None)
    if ctx_size == 8:
        near_one = swap(g_halo[1], "ctx", 1)
    dq_c, g, _ = back_c_rows((dq_c,), pick(slots, far), {}, dq_c)
    zero = jnp.zeros((), BF)
    if ctx_size == 8:
        near_one = after(near_one, dq_c)
        two_back = add_low(g_halo[2], jnp.where(odd, near_one, zero))
        halo_two = shift(two_back, -2)
        got7 = swap(g[7], "ctx", 1)
        ready = (two_back,)
    dq_c, more, _ = back_c_rows((dq_c, *ready), pick(slots, middle), {}, dq_c)
    g.update(more)
    if ctx_size == 8:
        g6 = add_low(g[6], after(got7, dq_c))
        far_k, far_v = swap(g6[0], "ctx", 2), swap(g6[1], "ctx", 4)
        got3, got5 = swap(g[3], "ctx", 1), swap(g[5], "ctx", 1)
        ready = (g6,)
    dq, more, _ = back_c_rows((dq_c, *ready), pick(slots, near), {}, dq_c, dq)
    g.update(more)
    if ctx_size == 8:
        got1 = swap(g[1], "ctx", 1)
        far_k, far_v, got3, got5 = (after(v, dq, halo_two) for v in (far_k, far_v, got3, got5))
        to_x, to_y = merge(g[2], got3, g[4], got5, far_k, far_v)
        ready = (to_x,)
        keys_p = values_p = [g[0], got1, swap(to_x, "ctx", 2), swap(to_y, "ctx", 4)]
        keys_c = values_c = [g_halo[0], jnp.where(odd, zero, near_one), halo_two]
    else:
        both = jnp.stack([g[s] for s in range(ctx_size)])
        while both.shape[0] > 1:
            size = both.shape[0] // 2
            both = add_low(both[:size], swap(both[size:], "ctx", size))
        keys_p = values_p = [both[0]]
        keys_c = values_c = [g_halo[0]] + [shift(g_halo[d], -d) for d in range(1, n_halo)]

    d_q, q_part, q_heads = q_back(dq, q_lin, after(gain_q, dq, *ready), cos, sin, w_q)
    d_kv, into_c, k_heads_c = kv_back(
        1, keys_c, values_c, k_lin_c, after(gain_k, q_part), cos, sin, w_kv, to_slots, q_part
    )
    into_got_c = swap(into_c, "tensor", 1)
    d_kv, into_p, k_heads_p = kv_back(
        0, keys_p, values_p, k_lin_p, after(gain_k, into_c), cos, sin, w_kv, to_slots, q_part, d_kv
    )
    into_got_p = swap(into_p, "tensor", 1)
    high, low = qkv_weight_grad(normed, after(d_q, into_p), d_kv)
    heads = jnp.concatenate([q_heads, k_heads_c + k_heads_p], axis=1)
    heads_got = swap(heads, "tensor", 1)
    out_share, gate_share, up_share, down_share = unpack(chunk, o_cols, after(rest_share, low))
    grad_tokens, d_one_c = tokens_back(1, into_c, into_got_c, tokens, after(gain_one, gate_share), d_resid_c)
    qkv_grad = scatter_rows(low, high, d_one_c)
    layer_out = add_layer(0, after(resid_p, qkv_grad[0]), out_p, out_got_p)
    qkv_grad = scatter_more(qkv_grad, layer_out)
    layer_out = add_layer(1, after(resid_c, qkv_grad[0]), out_c, out_got_c, layer_out)
    grad_tokens, d_one_p = tokens_back(
        0, into_p, into_got_p, tokens, after(gain_one, layer_out), d_resid_p, grad_tokens
    )
    qkv_grad = scatter_sum(qkv_grad, d_one_p)
    heads = heads + after(heads_got, d_one_p)
    late = jnp.concatenate([d_one_c + d_one_p, heads, d_two_c + d_two_p], axis=1)
    late = butterfly(late, ("ctx", "shard"))
    qkv_share = add_low(qkv_grad[0][:wide], qkv_grad[1]).astype(F32)

    def own_gain(value, size):
        return lax.dynamic_index_in_dim(value.reshape(parts, size), part, 0, keepdims=False)

    return (
        layer_out,
        grad_tokens,
        own_gain(late[:, :model], wide),
        own_gain(late[:, model + 2 * HEAD_SIZE :], wide),
        own_gain(late[:, model : model + HEAD_SIZE], narrow),
        own_gain(late[:, model + HEAD_SIZE : model + 2 * HEAD_SIZE], narrow),
        qkv_share[:, :q_cols],
        qkv_share[:, q_cols : q_cols + k_cols],
        qkv_share[:, q_cols + k_cols :],
        out_share.T,
        gate_share,
        up_share,
        down_share.T,
    )


def solution(mesh):
    split = ("shard", "ctx")
    rows, gain = P(split, None), P(split)
    into, out_of = P(split, "tensor"), P("tensor", split)
    in_specs = (rows, P("shard", None)) + (gain,) * 4 + (into,) * 3 + (out_of,)
    in_specs += (into, into, out_of, rows)
    out_specs = (rows, rows) + (gain,) * 4 + (into,) * 3 + (out_of, into, into, out_of)
    return jax.shard_map(body, mesh=mesh, in_specs=in_specs, out_specs=out_specs, check_vma=False)
```

```python
import functools
import math

import jax
import jax.numpy as jnp
from jax import lax
from jax.experimental import pallas as pl
from jax.experimental.pallas import tpu as pltpu
from jax.sharding import PartitionSpec as P

HEAD_SIZE = 128
PROMPT = 4096
CONT_TOK = 4096
LONGEST = 1024

EPSILON = 1e-06
ROPE_BASE = 1000000.0
MASKED = -1e30
LOG2E = math.log2(math.e)
LN2 = math.log(2.0)
SCALE = 1.0 / math.sqrt(HEAD_SIZE)

BF = jnp.bfloat16
F32 = jnp.float32
NN = (((1,), (0,)), ((), ()))
NT = (((1,), (1,)), ((), ()))
TN = (((0,), (0,)), ((), ()))
MIB = 2**20
STATED = 3e9


def mm(left, right, dims=NN):
    return lax.dot_general(left, right, dims, preferred_element_type=F32)


def shaped(dims, kind):
    return jax.ShapeDtypeStruct(dims, kind)


def call(kernel, name, grid, ins, outs, scratch=(), vmem=56, scalars=None, keep=None, us=0):
    in_specs, arrays = [], []
    for array, block, index in ins:
        arrays.append(array)
        in_specs.append(pl.BlockSpec(memory_space=pl.ANY) if block is None else pl.BlockSpec(block, index))
    lead = 0 if scalars is None else 1
    return pl.pallas_call(
        kernel,
        grid_spec=pltpu.PrefetchScalarGridSpec(
            num_scalar_prefetch=lead,
            grid=grid,
            in_specs=in_specs,
            out_specs=[pl.BlockSpec(block, index) for _, block, index in outs],
            scratch_shapes=list(scratch),
        ),
        out_shape=[shape for shape, _, _ in outs],
        input_output_aliases={a + lead: b for a, b in (keep or {}).items()},
        compiler_params=pltpu.CompilerParams(vmem_limit_bytes=vmem * MIB),
        cost_estimate=pl.CostEstimate(flops=int(us * STATED), bytes_accessed=0, transcendentals=0),
        name=name,
    )(*([] if scalars is None else [scalars]), *arrays)


def rms(values):
    return lax.rsqrt(jnp.mean(values * values, axis=-1, keepdims=True) + EPSILON)


def turn(values, cos, sin):
    return values * cos + pltpu.roll(values, HEAD_SIZE // 2, 1) * sin


def turn_back(values, cos, sin):
    return values * cos - pltpu.roll(values, HEAD_SIZE // 2, 1) * sin


def kv_kernel(heads, x_ref, gain_ref, w_ref, hgain_ref, cos_ref, sin_ref, *refs):
    normed_ref, kv_ref, lin_ref = refs[-3:]
    x = x_ref[...].astype(F32)
    normed_ref[...] = (x * rms(x) * gain_ref[...]).astype(BF)
    both = mm(normed_ref[...], w_ref[...])
    width = heads * HEAD_SIZE
    kv_ref[1] = both[:, width:].astype(BF)
    for h in range(heads):
        cols = slice(h * HEAD_SIZE, (h + 1) * HEAD_SIZE)
        lin = both[:, cols]
        lin_ref[:, cols] = lin
        kv_ref[0, :, cols] = turn(lin * rms(lin) * hgain_ref[...], cos_ref[...], sin_ref[...]).astype(BF)


def q_kernel(heads, normed_ref, w_ref, hgain_ref, cos_ref, sin_ref, q_ref, lin_ref):
    both = mm(normed_ref[...], w_ref[...])
    for h in range(heads):
        cols = slice(h * HEAD_SIZE, (h + 1) * HEAD_SIZE)
        lin = both[:, cols]
        lin_ref[:, cols] = lin
        turned = turn(lin * rms(lin) * hgain_ref[...], cos_ref[...], sin_ref[...])
        q_ref[:, cols] = (turned * (SCALE * LOG2E)).astype(BF)


def pack_kernel(chunk, key_ref, value_ref, out_ref, gate_ref, up_ref, down_ref, kv_ref, rest_ref):
    k_cols, o_cols, units = key_ref.shape[1], out_ref.shape[1], gate_ref.shape[1]
    kv_ref[:, :k_cols] = key_ref[...]
    kv_ref[:, k_cols:] = value_ref[...]
    rest_ref[:, :o_cols] = out_ref[...]
    for at in range(0, units, chunk):
        to = o_cols + 2 * at
        rest_ref[:, to : to + chunk] = gate_ref[:, at : at + chunk]
        rest_ref[:, to + chunk : to + 2 * chunk] = up_ref[:, at : at + chunk]
    rest_ref[:, o_cols + 2 * units :] = down_ref[...]


def pack(chunk, *weights):
    wide, k_cols = weights[0].shape
    width = weights[2].shape[1] + 3 * weights[3].shape[1]
    whole = lambda f: (0, 0)
    ins = [(w, w.shape, whole) for w in weights]
    outs = [(shaped((wide, cols), BF), (wide, cols), whole) for cols in (2 * k_cols, width)]
    return call(functools.partial(pack_kernel, chunk), "pack", (1,), ins, outs)


def by_top_bit(slots):
    groups = {}
    for at, s in enumerate(slots):
        if s:
            groups.setdefault(1 << (s.bit_length() - 1), []).append(at)
    return groups


def fwd_kernel(plan, idx_ref, lo_ref, *refs):
    halves, slots, halos = plan["halves"], plan["slots"], plan["halos"]
    refs = list(refs)
    q_refs = [refs.pop(0) for _ in halves]
    slot_refs = [refs.pop(0) for _ in slots]
    halo_refs = [refs.pop(0) for _ in halos]
    prior = [refs.pop(0) for _ in range(2 * len(halves))] if plan["carry"] else None
    if plan["last"]:
        w_ref = refs.pop(0)
        if plan["alias"]:
            refs.pop(0)
        out_ref, lse_ref, part_ref = refs[:3]
        refs = refs[3:]
    else:
        results, refs = refs[: 2 * len(halves)], refs[2 * len(halves) :]
    me, lo_first = idx_ref[0], idx_ref[1]
    rows = q_refs[0].shape[0]
    row = lax.broadcasted_iota(jnp.int32, (2 * rows, 1), 0)
    row = jnp.where(row >= rows, row - rows, row)
    col = lax.broadcasted_iota(jnp.int32, (1, rows), 1)
    for n, half in enumerate(halves):
        qs, acc, tot = refs[3 * n : 3 * n + 3]
        for g in range(2):
            cols, at = slice(g * HEAD_SIZE, (g + 1) * HEAD_SIZE), slice(g * rows, (g + 1) * rows)
            qs[at, :] = q_refs[n][:, cols]
            if prior is not None:
                acc[at, :] = prior[2 * n][:, cols]
                tot[at, :] = prior[2 * n + 1][:, cols]
        empty = [prior is None]

        def add(kv_ref, mask=None):
            scores = mm(qs[...], kv_ref[0], NT)
            if mask is not None:
                scores = jnp.where(mask, scores, MASKED)
            weights = jnp.exp2(scores)
            total = weights[:, :128]
            for at in range(128, weights.shape[1], 128):
                total = total + weights[:, at : at + 128]
            part = mm(weights.astype(BF), kv_ref[1])
            if empty[0]:
                acc[...] = part
                tot[...] = total
            else:
                acc[...] += part
                tot[...] += total
            empty[0] = False

        if half == 1:
            for kv_ref in slot_refs:
                add(kv_ref)
            low = jnp.concatenate([lo_ref[:, :1], lo_ref[:, :1]])
            for d, kv_ref in zip(halos, halo_refs):
                if d == 0:
                    add(kv_ref, (col <= row) & (col >= low))
                else:

                    @pl.when(lo_first < -(d - 1) * rows)
                    def _(d=d, kv_ref=kv_ref):
                        add(kv_ref, col - d * rows >= low)

        else:
            if 0 in slots:
                add(slot_refs[slots.index(0)], col <= row)
            for bit, group in by_top_bit(slots).items():

                @pl.when(jnp.bitwise_and(me, bit) != 0)
                def _(group=group):
                    for at in group:
                        add(slot_refs[at])

        if not plan["last"]:
            for g in range(2):
                cols, at = slice(g * HEAD_SIZE, (g + 1) * HEAD_SIZE), slice(g * rows, (g + 1) * rows)
                results[2 * n][:, cols] = acc[at, :]
                results[2 * n + 1][:, cols] = tot[at, :]
    if plan["last"]:
        qs, acc, tot, part_acc = refs
        step, steps = pl.program_id(0), pl.num_programs(0)
        for g in range(2):
            cols, at = slice(g * HEAD_SIZE, (g + 1) * HEAD_SIZE), slice(g * rows, (g + 1) * rows)
            total = jnp.sum(tot[at, :], axis=1, keepdims=True)
            out_ref[:, cols] = (acc[at, :] / total).astype(BF)
            lse_ref[0, g : g + 1, :] = jnp.log2(jnp.sum(tot[at, :].T, axis=0, keepdims=True))
        part = mm(out_ref[...], w_ref[...], NT)

        @pl.when(step == 0)
        def _():
            part_acc[...] = part

        @pl.when((step > 0) & (step < steps - 1))
        def _():
            part_acc[...] += part

        @pl.when(step == steps - 1)
        def _():
            part_ref[...] = (part_acc[...] + part).astype(BF)


def attention_forward(halves, scalars, q, low, slots, halos, carry=None, last=None):
    rows, heads = q.shape[0] // 2, q.shape[1] // 256
    plan = dict(halves=halves, slots=list(slots), halos=list(halos), carry=carry is not None,
                last=last is not None, alias=last is not None and last[1] is not None)
    part = lambda h, i: (0, h)
    ins = [(low, (rows, 128), lambda h, i: (0, 0))]
    ins += [(q, (rows, 256), lambda h, i, half=half: (half, h)) for half in halves]
    for kv in list(slots.values()) + list(halos.values()):
        ins.append((kv, (2, rows, 128), lambda h, i: (0, 0, h)))
    if carry is not None:
        ins += [(c, (rows, 256), part) for c in carry]
    scratch, keep = [], {}
    for _ in halves:
        scratch += [pltpu.VMEM((2 * rows, 128), BF)] + [pltpu.VMEM((2 * rows, 128), F32)] * 2
    state = shaped((rows, heads * 256), F32)
    if last is None:
        outs = [(state, (rows, 256), part)] * (2 * len(halves))
    else:
        w_rest, other = last
        model = w_rest.shape[0]
        ins.append((w_rest, (model, 256), part))
        if other is not None:
            keep = {len(ins): 0}
            ins.append((other, None, None))
        half = halves[0]
        outs = [
            (shaped((2 * rows, heads * 256), BF), (rows, 256), lambda h, i: (half, h)),
            (shaped((heads, 8, rows), F32), (1, 8, rows), lambda h, i: (h, 0, 0)),
            (shaped((rows, model), BF), (rows, model), lambda h, i: (0, 0)),
        ]
        scratch.append(pltpu.VMEM((rows, model), F32))
    return call(functools.partial(fwd_kernel, plan), "attend", (heads,), ins, outs, scratch,
                scalars=scalars, keep=keep)


def bwd_kernel(plan, idx_ref, q_ref, do_ref, lse_ref, delta_ref, lo_ref, *refs):
    half, slots, halos = plan["half"], plan["slots"], plan["halos"]
    refs = list(refs)
    slot_refs = [refs.pop(0) for _ in slots]
    halo_refs = [refs.pop(0) for _ in halos]
    prior_dq = refs.pop(0) if plan["carry"] else None
    prior = [refs.pop(0) for _ in slots] if plan["sum"] else None
    if plan["alias"]:
        refs.pop(0)
    dq_ref = refs.pop(0)
    slot_outs = [refs.pop(0) for _ in slots]
    halo_outs = [refs.pop(0) for _ in halos]
    qs, dos, lses, deltas, dq = refs
    me, lo_first = idx_ref[0], idx_ref[1]
    rows = q_ref.shape[0]
    for g in range(2):
        cols, at = slice(g * HEAD_SIZE, (g + 1) * HEAD_SIZE), slice(g * rows, (g + 1) * rows)
        qs[at, :] = q_ref[:, cols]
        dos[at, :] = do_ref[:, cols]
        lses[:, at] = lse_ref[0, g : g + 1, :]
        deltas[:, at] = delta_ref[0, g : g + 1, :]
    dq[...] = jnp.zeros_like(dq) if prior_dq is None else prior_dq[...]

    def block(kv_ref, out_ref, mask=None, before=None):
        keys = kv_ref[0]
        scores = mm(keys, qs[...], NT)
        dp = mm(kv_ref[1], dos[...], NT)
        scores = scores - lses[...]
        if mask is not None:
            scores = jnp.where(mask, scores, MASKED)
        probs = jnp.exp2(scores)
        ds = (probs * (dp - deltas[...])).astype(BF)
        dq[...] += mm(keys.T, ds)
        dk, dv = mm(ds, qs[...]) * LN2, mm(probs.astype(BF), dos[...])
        if before is not None:
            dk, dv = dk + before[0].astype(F32), dv + before[1].astype(F32)
        out_ref[0] = dk.astype(BF)
        out_ref[1] = dv.astype(BF)

    lane = lax.broadcasted_iota(jnp.int32, (1, 2 * rows), 1)
    lane = jnp.where(lane >= rows, lane - rows, lane)
    key = lax.broadcasted_iota(jnp.int32, (rows, 1), 0)

    def when(needed, kv_ref, out_ref, mask=None):
        @pl.when(needed)
        def _():
            block(kv_ref, out_ref, mask)

        @pl.when(jnp.logical_not(needed))
        def _():
            out_ref[...] = jnp.zeros_like(out_ref)

    low = lo_ref[:1, :]
    for d, kv_ref, out_ref in zip(halos, halo_refs, halo_outs):
        if d == 0:
            block(kv_ref, out_ref, (key <= lane) & (key >= low))
        else:
            when(lo_first < -(d - 1) * rows, kv_ref, out_ref, key - d * rows >= low)
    if half == 1:
        for at in range(len(slots)):
            block(slot_refs[at], slot_outs[at], None, prior[at] if prior else None)
    else:
        if 0 in slots:
            at = slots.index(0)
            block(slot_refs[at], slot_outs[at], key <= lane)
        for bit, group in by_top_bit(slots).items():

            @pl.when(jnp.bitwise_and(me, bit) != 0)
            def _(group=group):
                for at in group:
                    block(slot_refs[at], slot_outs[at])

            @pl.when(jnp.bitwise_and(me, bit) == 0)
            def _(group=group):
                for at in group:
                    slot_outs[at][...] = jnp.zeros_like(slot_outs[at])

    if plan["last"]:
        for g in range(2):
            cols = slice(g * HEAD_SIZE, (g + 1) * HEAD_SIZE)
            dq_ref[:, cols] = dq[:, g * rows : (g + 1) * rows].T * SCALE
    else:
        dq_ref[...] = dq[...]


def attention_backward(half, scalars, q, do, lse, delta, low, slots, halos, carry=None, prior=None, last=True, whole=None):
    rows, heads = q.shape[0] // 2, q.shape[1] // 256
    plan = dict(half=half, slots=list(slots), halos=list(halos), carry=carry is not None,
                sum=prior is not None, last=last, alias=whole is not None)
    part = lambda h, i: (0, h)
    stat = lambda h, i: (h, 0, 0)
    kv_map = lambda h, i: (0, 0, h)
    ins = [
        (q, (rows, 256), lambda h, i: (half, h)),
        (do, (rows, 256), part),
        (lse, (1, 8, rows), stat),
        (delta, (1, 8, rows), stat),
        (low, (8, 2 * rows), lambda h, i: (0, 0)),
    ]
    pieces = list(slots.values()) + list(halos.values())
    ins += [(kv, (2, rows, 128), kv_map) for kv in pieces]
    if carry is not None:
        ins.append((carry, (128, 2 * rows), lambda h, i: (h, 0)))
    if prior is not None:
        ins += [(prior[s], (2, rows, 128), kv_map) for s in slots]
    keep = {}
    if whole is not None:
        keep = {len(ins): 0}
        ins.append((whole, None, None))
    if last:
        outs = [(shaped((2 * rows, heads * 256), F32), (rows, 256), lambda h, i: (half, h))]
    else:
        outs = [(shaped((heads * 128, 2 * rows), F32), (128, 2 * rows), lambda h, i: (h, 0))]
    outs += [(shaped(kv.shape, BF), (2, rows, 128), kv_map) for kv in pieces]
    scratch = [
        pltpu.VMEM((2 * rows, 128), BF),
        pltpu.VMEM((2 * rows, 128), BF),
        pltpu.VMEM((1, 2 * rows), F32),
        pltpu.VMEM((1, 2 * rows), F32),
        pltpu.VMEM((128, 2 * rows), F32),
    ]
    us = 4 + 6 * (len(slots) + len(halos)) if carry is not None or halos else 0
    results = call(functools.partial(bwd_kernel, plan), "attend_back", (heads,), ins, outs, scratch,
                   scalars=scalars, us=us, keep=keep)
    n = len(slots)
    return results[0], dict(zip(slots, results[1 : 1 + n])), dict(zip(halos, results[1 + n :]))


def ffn_kernel(x_ref, own_ref, got_ref, gain_ref, dy_ref, gu_ref, down_ref, *refs):
    resid_ref, normed_ref, hidden_ref, dgu_ref, out_ref, back_ref, normed, out_acc, back_acc = refs[-9:]
    step, steps = pl.program_id(0), pl.num_programs(0)

    @pl.when(step == 0)
    def _():
        resid = x_ref[...].astype(F32) + (own_ref[...].astype(F32) + got_ref[...].astype(F32))
        resid_ref[...] = resid
        normed[...] = (resid * rms(resid) * gain_ref[...]).astype(BF)
        normed_ref[...] = normed[...]
        out_acc[...] = jnp.zeros_like(out_acc)
        back_acc[...] = jnp.zeros_like(back_acc)

    wide = down_ref.shape[1]
    both = mm(normed[...], gu_ref[...])
    d_hidden = mm(dy_ref[...], down_ref[...])
    gate, up = both[:, :wide], both[:, wide:]
    sig = 1.0 / (1.0 + jnp.exp(-gate))
    silu = gate * sig
    hidden = (silu * up).astype(BF)
    hidden_ref[...] = hidden
    d_up = (d_hidden * silu).astype(BF)
    d_gate = (d_hidden * up * (sig + silu * (1.0 - sig))).astype(BF)
    dgu_ref[:, :wide] = d_gate
    dgu_ref[:, wide:] = d_up
    out_acc[...] += mm(hidden, down_ref[...], NT)
    back_acc[...] += mm(dgu_ref[...], gu_ref[...], NT)

    @pl.when(step == steps - 1)
    def _():
        out_ref[...] = out_acc[...].astype(BF)
        back_ref[...] = back_acc[...].astype(BF)


def feed_forward(half, x, own, got, gain, dy, w_rest, o_cols, chunk, whole=None):
    rows, model = own.shape
    units = (w_rest.shape[1] - o_cols) // 3
    steps = units // chunk
    mine, once = lambda f: (half, 0), lambda f: (0, 0)
    at_gu, at_down = o_cols // (2 * chunk), (o_cols + 2 * units) // chunk
    block = (rows, model)
    ins = [
        (x, block, mine), (own, block, once), (got, block, once), (gain, (1, model), once), (dy, block, mine),
        (w_rest, (model, 2 * chunk), lambda f: (0, at_gu + f)),
        (w_rest, (model, chunk), lambda f: (0, at_down + f)),
    ]
    keep = {}
    if whole is not None:
        keep = {len(ins) + i: 1 + i for i in range(3)}
        ins += [(array, None, None) for array in whole]
    outs = [
        (shaped((rows, model), F32), block, once),
        (shaped((2 * rows, model), BF), block, mine),
        (shaped((2 * rows, units), BF), (rows, chunk), lambda f: (half, f)),
        (shaped((2 * rows, 2 * units), BF), (rows, 2 * chunk), lambda f: (half, f)),
        (shaped((rows, model), BF), block, once),
        (shaped((rows, model), BF), block, once),
    ]
    scratch = [pltpu.VMEM(block, BF), pltpu.VMEM(block, F32), pltpu.VMEM(block, F32)]
    return call(ffn_kernel, "feed_forward", (steps,), ins, outs, scratch, keep=keep)


def norm_back(grad, values, gain):
    scale = rms(values)
    unit = values * scale
    inner = grad * gain
    return scale * (inner - unit * jnp.mean(inner * unit, axis=-1, keepdims=True)), grad * unit


def row_blocks(rows):
    size = rows // 2 if rows % 512 == 0 else rows
    return size, rows // size


def add_up(ref, value):
    total = jnp.sum(value, axis=0, keepdims=True)

    @pl.when(pl.program_id(0) == 0)
    def _():
        ref[...] = total

    @pl.when(pl.program_id(0) > 0)
    def _():
        ref[...] += total


def mixed_kernel(heads, own_ref, got_ref, resid_ref, gain_ref, dy_ref, w_ref, att_ref, *refs):
    d_resid_ref, mixed_ref, datt_ref, delta_ref, dgain_ref = refs[-5:]
    grad = own_ref[...].astype(F32) + got_ref[...].astype(F32)
    d_norm, summand = norm_back(grad, resid_ref[...], gain_ref[...])
    add_up(dgain_ref, summand)
    d_resid = dy_ref[...].astype(F32) + d_norm
    d_resid_ref[...] = d_resid
    mixed_ref[...] = d_resid.astype(BF)
    datt_ref[...] = mm(mixed_ref[...], w_ref[...]).astype(BF)
    for h in range(heads):
        cols = slice(h * HEAD_SIZE, (h + 1) * HEAD_SIZE)
        product = datt_ref[:, cols].astype(F32) * att_ref[:, cols].astype(F32)
        delta_ref[h // 2, h % 2 : h % 2 + 1, :] = jnp.sum(product.T, axis=0, keepdims=True)


def mixed_back(half, own, got, resid, gain, dy, w_rest, o_cols, attended, whole=None):
    rows, model = own.shape
    heads = o_cols // HEAD_SIZE
    size, steps = row_blocks(rows)
    mine, here, once = lambda f: (half * steps + f, 0), lambda f: (f, 0), lambda f: (0, 0)
    block = (size, model)
    ins = [
        (own, block, here), (got, block, here), (resid, block, here), (gain, (1, model), once),
        (dy, block, mine), (w_rest, (model, o_cols), once), (attended, (size, o_cols), mine),
    ]
    keep = {}
    if whole is not None:
        keep = {len(ins): 1}
        ins.append((whole, None, None))
    outs = [
        (shaped((rows, model), F32), block, here),
        (shaped((2 * rows, model), BF), block, mine),
        (shaped((rows, o_cols), BF), (size, o_cols), here),
        (shaped((heads // 2, 8, rows), F32), (heads // 2, 8, size), lambda f: (0, 0, f)),
        (shaped((1, model), F32), (1, model), once),
    ]
    return call(functools.partial(mixed_kernel, heads), "mixed_back", (steps,), ins, outs, keep=keep)


def merge_kernel(two, got3, four, got5, far_k, far_v, to_x, to_y):
    for which in range(2):
        by_x = two[which].astype(F32) + got3[which].astype(F32)
        by_y = four[which].astype(F32) + got5[which].astype(F32)
        to_x[which] = (by_x + far_v[...].astype(F32) if which else by_x).astype(BF)
        to_y[which] = (by_y if which else by_y + far_k[...].astype(F32)).astype(BF)


def merge(*pieces):
    rows, cols = pieces[-1].shape
    size, steps = row_blocks(rows)
    ins = []
    for piece in pieces:
        if piece.ndim == 3:
            ins.append((piece, (2, size, cols), lambda f: (0, f, 0)))
        else:
            ins.append((piece, (size, cols), lambda f: (f, 0)))
    outs = [(shaped((2, rows, cols), BF), (2, size, cols), lambda f: (0, f, 0))] * 2
    return call(merge_kernel, "merge", (steps,), ins, outs)


def weight_kernel(left_ref, right_ref, *refs):
    refs[-1][...] = mm(left_ref[...], right_ref[...], TN).astype(BF)


def weight_grad(left, right, at, width, cols, whole=None):
    tokens, model = left.shape
    n = right.shape[1]
    ins = [(left, (tokens, model), lambda j: (0, 0)), (right, (tokens, cols), lambda j: (0, j))]
    keep = {}
    if whole is not None:
        keep = {len(ins): 0}
        ins.append((whole, None, None))
    outs = [(shaped((model, width), BF), (model, cols), lambda j: (0, at // cols + j))]
    return call(weight_kernel, "weight_grad", (n // cols,), ins, outs, keep=keep)[0]


def qkv_weight_kernel(left_ref, q_ref, kv_ref, high_ref, low_ref):
    for half, out_ref in enumerate((high_ref, low_ref)):
        for which, right_ref in enumerate((q_ref, kv_ref)):

            @pl.when((pl.program_id(0) == half) & (pl.program_id(1) == which))
            def _(out_ref=out_ref, right_ref=right_ref):
                out_ref[...] = mm(left_ref[...], right_ref[...], TN).astype(BF)


def qkv_weight_grad(left, d_q, d_kv):
    tokens, model = left.shape
    cols = d_q.shape[1]
    ins = [
        (left, (tokens, model // 2), lambda i, j: (0, 1 - i)),
        (d_q, (tokens, cols), lambda i, j: (0, 0)),
        (d_kv, (tokens, cols), lambda i, j: (0, 0)),
    ]
    half, block = shaped((model // 2, 2 * cols), BF), (model // 2, cols)
    outs = [(half, block, lambda i, j: (0, jnp.where(i == 0, j, 1))), (half, block, lambda i, j: (0, i * j))]
    return call(qkv_weight_kernel, "qkv_weight_grad", (2, 2), ins, outs)


def q_back_kernel(heads, dq_ref, lin_ref, gain_ref, cos_ref, sin_ref, w_ref, *refs):
    d_ref, part_ref, gains_ref = refs[-3:]
    cos, sin = cos_ref[...], sin_ref[...]
    total = jnp.zeros(cos.shape, F32)
    for h in range(heads):
        cols = slice(h * HEAD_SIZE, (h + 1) * HEAD_SIZE)
        grad, summand = norm_back(turn_back(dq_ref[:, cols], cos, sin), lin_ref[:, cols], gain_ref[...])
        d_ref[:, cols] = grad.astype(BF)
        total = total + summand
    part_ref[...] = mm(d_ref[...], w_ref[...], NT)
    add_up(gains_ref, total)


def q_back(dq, lin, gain, cos, sin, w):
    rows, cols = dq.shape
    model = w.shape[0]
    size, steps = row_blocks(rows)
    here, once = lambda f: (f, 0), lambda f: (0, 0)
    ins = [
        (dq, (size, cols), here), (lin, (size, cols), here), (gain, (1, HEAD_SIZE), once),
        (cos, (size, HEAD_SIZE), here), (sin, (size, HEAD_SIZE), here), (w, (model, cols), once),
    ]
    outs = [
        (shaped((rows, cols), BF), (size, cols), here),
        (shaped((rows, model), F32), (size, model), here),
        (shaped((1, HEAD_SIZE), F32), (1, HEAD_SIZE), once),
    ]
    kernel = functools.partial(q_back_kernel, cols // HEAD_SIZE)
    return call(kernel, "q_back", (steps,), ins, outs)


def kv_back_kernel(heads, n_keys, n_values, lin_ref, gain_ref, cos_ref, sin_ref, w_ref, slots_ref, q_part_ref, *refs):
    key_refs, value_refs = refs[:n_keys], refs[n_keys : n_keys + n_values]
    d_ref, part_ref, gains_ref = refs[-3:]
    cos, sin = cos_ref[...], sin_ref[...]
    width = heads * HEAD_SIZE

    def total(sources, which, cols):
        value = None
        for ref in sources:
            piece = ref[which, :, cols] if len(ref.shape) == 3 else ref[:, cols]
            value = piece.astype(F32) if value is None else value + piece.astype(F32)
        return value

    gains = jnp.zeros(cos.shape, F32)
    for h in range(heads):
        cols = slice(h * HEAD_SIZE, (h + 1) * HEAD_SIZE)
        grad, summand = norm_back(
            turn_back(total(key_refs, 0, cols), cos, sin), lin_ref[:, cols], gain_ref[...]
        )
        d_ref[:, cols] = grad.astype(BF)
        gains = gains + summand
    d_ref[:, width:] = total(value_refs, 1, slice(None)).astype(BF)
    part = (q_part_ref[...] + mm(d_ref[...], w_ref[...], NT)).astype(BF)
    part_ref[...] = mm(part, slots_ref[...], NT).astype(BF)
    add_up(gains_ref, gains)


def kv_back(half, keys, values, lin, gain, cos, sin, w, to_slots, q_part, whole=None):
    rows, cols = lin.shape
    model = w.shape[0]
    size, steps = row_blocks(rows)
    mine, here, once = lambda f: (half * steps + f, 0), lambda f: (f, 0), lambda f: (0, 0)
    ins = [
        (lin, (size, cols), here), (gain, (1, HEAD_SIZE), once), (cos, (size, HEAD_SIZE), mine),
        (sin, (size, HEAD_SIZE), mine), (w, (model, 2 * cols), once),
        (to_slots, (model, model), once), (q_part, (size, model), mine),
    ]
    for piece in list(keys) + list(values):
        if piece.ndim == 3:
            ins.append((piece, (2, size, cols), lambda f: (0, f, 0)))
        else:
            ins.append((piece, (size, cols), here))
    keep = {}
    if whole is not None:
        keep = {len(ins): 0}
        ins.append((whole, None, None))
    outs = [
        (shaped((2 * rows, 2 * cols), BF), (size, 2 * cols), mine),
        (shaped((rows, model), BF), (size, model), here),
        (shaped((1, HEAD_SIZE), F32), (1, HEAD_SIZE), once),
    ]
    kernel = functools.partial(kv_back_kernel, cols // HEAD_SIZE, len(keys), len(values))
    return call(kernel, "kv_back", (steps,), ins, outs, keep=keep)


def tokens_kernel(own_ref, got_ref, x_ref, gain_ref, d_resid_ref, *refs):
    out_ref, dgain_ref = refs[-2:]
    grad = own_ref[...].astype(F32) + got_ref[...].astype(F32)
    d_norm, summand = norm_back(grad, x_ref[...].astype(F32), gain_ref[...])
    add_up(dgain_ref, summand)
    out_ref[...] = (d_resid_ref[...] + d_norm).astype(BF)


def tokens_back(half, own, got, x, gain, d_resid, whole=None):
    rows, model = own.shape
    size, steps = row_blocks(rows)
    mine, here, once = lambda f: (half * steps + f, 0), lambda f: (f, 0), lambda f: (0, 0)
    block = (size, model)
    ins = [(own, block, here), (got, block, here), (x, block, mine), (gain, (1, model), once), (d_resid, block, here)]
    keep = {}
    if whole is not None:
        keep = {len(ins): 0}
        ins.append((whole, None, None))
    outs = [(shaped((2 * rows, model), BF), block, mine), (shaped((1, model), F32), (1, model), once)]
    return call(tokens_kernel, "tokens_back", (steps,), ins, outs, keep=keep, us=20 * half)


def share_kernel(chunk, share_ref, out_ref, gate_ref, up_ref, down_ref):
    o_cols, units = out_ref.shape[1], gate_ref.shape[1]
    out_ref[...] = share_ref[:, :o_cols].astype(F32)
    for at in range(0, units, chunk):
        to = o_cols + 2 * at
        gate_ref[:, at : at + chunk] = share_ref[:, to : to + chunk].astype(F32)
        up_ref[:, at : at + chunk] = share_ref[:, to + chunk : to + 2 * chunk].astype(F32)
    down_ref[...] = share_ref[:, o_cols + 2 * units :].astype(F32)


def unpack(chunk, o_cols, share):
    wide = share.shape[0]
    units = (share.shape[1] - o_cols) // 3
    whole = lambda f: (0, 0)
    outs = [(shaped((wide, cols), F32), (wide, cols), whole) for cols in (o_cols, units, units, units)]
    return call(functools.partial(share_kernel, chunk), "unpack", (1,), [(share, share.shape, whole)], outs)


def layer_kernel(resid_ref, own_ref, got_ref, *refs):
    refs[-1][...] = (resid_ref[...] + (own_ref[...].astype(F32) + got_ref[...].astype(F32))).astype(BF)


def add_layer(half, resid, own, got, whole=None):
    rows, model = resid.shape
    size, steps = row_blocks(rows)
    here, mine = lambda f: (f, 0), lambda f: (half * steps + f, 0)
    ins = [(array, (size, model), here) for array in (resid, own, got)]
    keep = {}
    if whole is not None:
        keep = {len(ins): 0}
        ins.append((whole, None, None))
    outs = [(shaped((2 * rows, model), BF), (size, model), mine)]
    return call(layer_kernel, "add_layer", (steps,), ins, outs, keep=keep)[0]


def swap(value, axis, bit):
    size = lax.axis_size(axis)
    return lax.ppermute(value, axis, [(i, i ^ bit) for i in range(size)])


def shift(value, by):
    size = lax.axis_size("ctx")
    return lax.ppermute(value, "ctx", [(i, i + by) for i in range(size) if 0 <= i + by < size])


def add_low(left, right):
    return (left.astype(F32) + right.astype(F32)).astype(BF)


def butterfly(value, axes, gates=()):
    gates = list(gates)
    for axis in axes:
        bit = 1
        while bit < lax.axis_size(axis):
            got = swap(value, axis, bit)
            value = value + (after(got, gates.pop(0)) if gates else got)
            bit *= 2
    return value


def after(value, *others):
    return lax.optimization_barrier((value, *others))[0]


def rotary_tables(position):
    half_dim = HEAD_SIZE // 2
    inverse_freq = jnp.exp(jnp.arange(half_dim, dtype=F32) * (-math.log(ROPE_BASE) / half_dim))
    angles = position.astype(F32)[:, None] * inverse_freq[None, :]
    cosine, sine = jnp.cos(angles), jnp.sin(angles)
    return jnp.concatenate([cosine, cosine], axis=-1), jnp.concatenate([-sine, sine], axis=-1)


def body(
    tokens,
    cont_lengths,
    attn_gain,
    ffn_gain,
    query_gain,
    key_gain,
    w_query,
    key_weight,
    value_weight,
    w_out,
    w_gate,
    w_up,
    w_down,
    cotangent,
):
    ctx_size = lax.axis_size("ctx")
    weight_axes = ("shard", "ctx")
    parts = lax.axis_size("shard") * ctx_size
    me = lax.axis_index("ctx")
    part = lax.axis_index("shard") * ctx_size + me
    rows, model = tokens.shape[0] // 2, tokens.shape[1]
    n_halo = 1 + -(-(LONGEST - 1) // rows)
    lengths = cont_lengths[0]

    bits = [("shard", 1)] + [("ctx", 1 << i) for i in range(1, ctx_size.bit_length() - 1)] + [("ctx", 1)]
    order = [0]
    for axis, bit in bits:
        order += [j ^ (bit * ctx_size if axis == "shard" else bit) for j in order]
    wide, narrow = attn_gain.shape[0], query_gain.shape[0]
    q_cols, k_cols = w_query.shape[1], key_weight.shape[1]
    o_cols, units = w_out.shape[0], w_gate.shape[1]
    heads, kv_heads = q_cols // HEAD_SIZE, k_cols // HEAD_SIZE
    chunk = math.gcd(units, 512)

    def gather_rows(piece, gates=((),) * 4):
        if ctx_size != 8:
            for axis, bit in bits:
                piece = jnp.concatenate([piece, swap(piece, axis, bit)])
            return piece, (piece,) * 4
        one = jnp.concatenate([piece, after(swap(piece, "shard", 1), *gates[0])])
        by_x, by_y = (after(v, *gates[1]) for v in (swap(one, "ctx", 2), swap(one, "ctx", 4)))
        cut = one.shape[1] // 2
        left, right = swap(by_y[:, :cut], "ctx", 2), swap(by_x[:, cut:], "ctx", 4)
        far = jnp.concatenate([after(left, *gates[2]), after(right, *gates[2])], axis=1)
        half = jnp.concatenate([one, by_x, by_y, far])
        whole = jnp.concatenate([half, after(swap(half, "ctx", 1), *gates[3])])
        return whole, (one, by_x, half, whole)

    def scatter_rows(low, high, late):
        total = add_low(low, after(swap(high, "ctx", 1), late))
        if ctx_size != 8:
            for axis, bit in bits[-2:0:-1]:
                size = total.shape[0] // 2
                total = add_low(total[:size], swap(total[size:], axis, bit))
            return (total,)
        size, cut = total.shape[0] // 4, total.shape[1] // 2
        own, by_x, by_y, far = (total[i * size : (i + 1) * size] for i in range(4))
        left, right = swap(far[:, :cut], "ctx", 2), swap(far[:, cut:], "ctx", 4)
        return own, by_x, by_y, left, right

    def scatter_more(stage, late):
        if ctx_size != 8:
            return stage
        own, by_x, by_y, left, right = stage
        left, right = after(left, late), after(right, late)
        cut = left.shape[1]
        by_x = jnp.concatenate([by_x[:, :cut], add_low(by_x[:, cut:], right)], axis=1)
        by_y = jnp.concatenate([add_low(by_y[:, :cut], left), by_y[:, cut:]], axis=1)
        return lax.optimization_barrier((own, by_x, by_y))[0], swap(by_x, "ctx", 2), swap(by_y, "ctx", 4)

    def scatter_sum(stage, late):
        total = stage[0].astype(F32)
        for piece in stage[1:]:
            total = total + after(piece, late).astype(F32)
        total, size = total.astype(BF), total.shape[0] // 2
        return total, swap(total[size:], "shard", 1)

    kv_piece, rest_piece = pack(chunk, key_weight, value_weight, w_out.T, w_gate, w_up, w_down.T)
    w_kv, stages = gather_rows(kv_piece)
    w_rest = lax.all_gather(rest_piece, weight_axes, axis=0, tiled=True)
    gains = jnp.concatenate([attn_gain, ffn_gain, query_gain, key_gain])[None]
    gains = jnp.where(jnp.arange(parts)[:, None] == part, gains, jnp.zeros((), BF))
    gains = gains + after(swap(gains, "ctx", 1), kv_piece)
    for at, (axis, bit) in enumerate(bits[:-1]):
        gains = gains + after(swap(gains, axis, bit), stages[min(at, 2)])
    gains = gains.astype(F32)
    gain_one = gains[:, :wide].reshape(1, -1)
    gain_two = gains[:, wide : 2 * wide].reshape(1, -1)
    gain_q = gains[:, 2 * wide : 2 * wide + narrow].reshape(1, -1)
    gain_k = gains[:, 2 * wide + narrow :].reshape(1, -1)
    source = jnp.bitwise_xor(part, jnp.array(order, jnp.int32))[:, None] * wide + jnp.arange(wide, dtype=jnp.int32)
    to_slots = (jnp.arange(model, dtype=jnp.int32)[:, None] == source.reshape(1, -1)).astype(BF)
    tokens_s = mm(after(tokens, stages[0]), to_slots).astype(BF)
    gain_one_s = mm(gain_one.astype(BF), to_slots)

    cont_at = me * rows + jnp.arange(rows, dtype=jnp.int32)
    cont_ends = jnp.cumsum(lengths)
    starts = cont_ends - lengths
    seg = jnp.sum((cont_ends[None, :] <= cont_at[:, None]).astype(jnp.int32), axis=1)
    numbers = jnp.arange(lengths.shape[0], dtype=jnp.int32)
    first = jnp.sum(jnp.where(numbers[None, :] == seg[:, None], starts[None, :], 0), axis=1)
    position = jnp.concatenate([me * rows + jnp.arange(rows, dtype=jnp.int32), PROMPT + cont_at - first])
    low = first - me * rows
    low_col = jnp.broadcast_to(low[:, None], (rows, 128))
    low_row = jnp.broadcast_to(jnp.concatenate([low, low])[None, :], (8, 2 * rows))
    scalars = jnp.stack([me, low[0]])
    cos, sin = rotary_tables(position)

    once = lambda f: (0, 0)

    def keys_values(half, gain, whole=None):
        mine = lambda f: (half, 0)
        ins = [
            (tokens_s, (rows, model), mine), (gain, (1, model), once), (w_kv, (model, 2 * k_cols), once),
            (gain_k, (1, HEAD_SIZE), once), (cos, (rows, HEAD_SIZE), mine), (sin, (rows, HEAD_SIZE), mine),
        ]
        keep = {}
        if whole is not None:
            keep = {len(ins): 0}
            ins.append((whole, None, None))
        outs = [
            (shaped((2 * rows, model), BF), (rows, model), mine),
            (shaped((2, rows, k_cols), BF), (2, rows, k_cols), lambda f: (0, 0, 0)),
            (shaped((rows, k_cols), F32), (rows, k_cols), once),
        ]
        return call(functools.partial(kv_kernel, kv_heads), "keys_values", (1,), ins, outs, keep=keep)

    normed, kv_p, k_lin_p = keys_values(0, gain_one_s)
    normed, kv_c, k_lin_c = keys_values(1, after(gain_one_s, kv_p), normed)
    w_q, _ = gather_rows(after(w_query, stages[0]), ((stages[1],), (kv_p,), (kv_p,), (kv_c,)))
    mine = lambda f: (f, 0)
    q, q_lin = call(
        functools.partial(q_kernel, heads), "queries", (2,),
        [
            (normed, (rows, model), mine), (w_q, (model, q_cols), lambda f: (0, 0)),
            (gain_q, (1, HEAD_SIZE), lambda f: (0, 0)),
            (cos, (rows, HEAD_SIZE), mine), (sin, (rows, HEAD_SIZE), mine),
        ],
        [(shaped((2 * rows, q_cols), BF), (rows, q_cols), mine), (shaped((2 * rows, q_cols), F32), (rows, q_cols), mine)],
    )

    def pick(source, wanted):
        return {s: source[s] for s in source if s in wanted}

    near, middle, far = (0, 1), (2, 3, 4, 5), tuple(range(6, ctx_size))
    slots, halos = {0: kv_p}, {0: kv_c}
    odd = (me % 2) == 1
    if ctx_size == 8:
        slots[1], slots[2], slots[4] = (swap(kv_p, "ctx", bit) for bit in (1, 2, 4))
    else:
        both, bit = kv_p[None], 1
        while bit < ctx_size:
            both = jnp.concatenate([both, swap(both, "ctx", bit)])
            bit *= 2
        slots = {s: both[s] for s in range(ctx_size)}
        halos.update({d: shift(kv_c, d) for d in range(1, n_halo)})
    ready = ()
    if ctx_size == 8:
        slots[2], slots[4] = after(slots[2], q), after(slots[4], q)
        far_k, far_v = swap(slots[4][0], "ctx", 2), swap(slots[2][1], "ctx", 4)
        slots[3], slots[5] = swap(slots[2], "ctx", 1), swap(slots[4], "ctx", 1)
        halos[2] = shift(after(kv_c, slots[2]), 2)
        ready = (slots[2], slots[4])
    c_state = attention_forward(
        (1,), after(scalars, *ready), q, low_col, pick(slots, near), pick(halos, (0,))
    )
    if ctx_size == 8:
        slots[6] = jnp.stack([after(far_k, c_state[0]), after(far_v, c_state[0])])
        slots[7] = swap(slots[6], "ctx", 1)
        ready = (slots[7],)
    attended, lse_p, part_p = attention_forward(
        (0,), after(scalars, c_state[0], *ready), q, low_col, slots, {}, None, (w_rest, None)
    )
    got_p = swap(part_p, "tensor", 1)
    if ctx_size == 8:
        halos[1] = swap(jnp.where(odd, after(halos[2], part_p), kv_c), "ctx", 1)
    attended, lse_c, part_c = attention_forward(
        (1,), after(scalars, part_p), q, low_col, pick(slots, middle + far), pick(halos, range(1, n_halo)),
        c_state, (w_rest, attended),
    )
    got_c = swap(part_c, "tensor", 1)

    resid_p, *whole, out_p, back_p = feed_forward(
        0, tokens, part_p, got_p, after(gain_two, part_c), cotangent, w_rest, o_cols, chunk
    )
    back_got_p = swap(back_p, "tensor", 1)
    resid_c, *whole, out_c, back_c = feed_forward(
        1, tokens, part_c, got_c, after(gain_two, back_p), cotangent, w_rest, o_cols, chunk, whole
    )
    back_got_c = swap(back_c, "tensor", 1)
    normed_ffn, hidden, d_gu = whole
    width = o_cols + 3 * units
    rest_grads = weight_grad(normed_ffn, d_gu, o_cols, width, min(1024, o_cols))
    rest_grads = weight_grad(cotangent, hidden, o_cols + 2 * units, width, chunk, rest_grads)
    d_resid_p, d_mixed, d_att_p, delta_p, d_two_p = mixed_back(
        0, back_p, back_got_p, resid_p, after(gain_two, rest_grads), cotangent, w_rest, o_cols, attended
    )
    out_p, out_c = after(out_p, back_got_c), after(out_c, back_got_c)
    out_got_p, out_got_c = swap(out_p, "tensor", 1), swap(out_c, "tensor", 1)

    of_rows = [(d_att_p, lse_p, delta_p)]

    def back_rows(half, deps, slots, halos, carry, prior=None, whole=None, last=False):
        do, lse, delta = of_rows[half]
        return attention_backward(
            half, after(scalars, *deps), q, do, lse, delta, low_row, slots, halos, carry, prior, last, whole
        )

    dq_p, prior, _ = back_rows(0, (d_att_p,), pick(slots, far), {}, None)
    d_resid_c, d_mixed, d_att_c, delta_c, d_two_c = mixed_back(
        1, back_c, back_got_c, resid_c, after(gain_two, dq_p), cotangent, w_rest, o_cols, attended, d_mixed
    )
    of_rows.append((d_att_c, lse_c, delta_c))
    rest_grads = weight_grad(d_mixed, attended, 0, width, min(1024, o_cols), rest_grads)
    rest_share = lax.psum_scatter(rest_grads, weight_axes, scatter_dimension=0, tiled=True)
    dq_c, _, g_halo = back_rows(1, (rest_grads,), {}, halos, None)
    if ctx_size == 8:
        near_one = swap(g_halo[1], "ctx", 1)
    dq_c, g, _ = back_rows(1, (dq_c,), pick(slots, far), {}, dq_c, prior)
    zero = jnp.zeros((), BF)
    ready = ()
    if ctx_size == 8:
        got7 = swap(g[7], "ctx", 1)
        near_one = after(near_one, dq_c)
        two_back = add_low(g_halo[2], jnp.where(odd, near_one, zero))
        halo_two = shift(two_back, -2)
        ready = (two_back,)
    dq, prior, _ = back_rows(0, (dq_c, *ready), pick(slots, near + middle), {}, dq_p, None, None, True)
    if ctx_size == 8:
        g6 = add_low(g[6], after(got7, dq))
        far_k, far_v = swap(g6[0], "ctx", 2), swap(g6[1], "ctx", 4)
        ready = (g6, halo_two)
    dq_c, more, _ = back_rows(1, (dq, out_got_p, out_got_c, *ready), pick(slots, middle), {}, dq_c, prior)
    g.update(more)
    if ctx_size == 8:
        got3, got5 = swap(g[3], "ctx", 1), swap(g[5], "ctx", 1)
    dq, more, _ = back_rows(1, (dq_c,), pick(slots, near), {}, dq_c, prior, dq, True)
    g.update(more)
    if ctx_size == 8:
        got1 = swap(g[1], "ctx", 1)
        far_k, far_v, got3, got5 = (after(v, dq) for v in (far_k, far_v, got3, got5))
        to_x, to_y = merge(g[2], got3, g[4], got5, far_k, far_v)
        ready = (to_x,)
        keys_p = values_p = [g[0], got1, swap(to_x, "ctx", 2), swap(to_y, "ctx", 4)]
        keys_c = values_c = [g_halo[0], jnp.where(odd, zero, near_one), halo_two]
    else:
        both = jnp.stack([g[s] for s in range(ctx_size)])
        while both.shape[0] > 1:
            size = both.shape[0] // 2
            both = add_low(both[:size], swap(both[size:], "ctx", size))
        keys_p = values_p = [both[0]]
        keys_c = values_c = [g_halo[0]] + [shift(g_halo[d], -d) for d in range(1, n_halo)]

    d_q, q_part, q_heads = q_back(dq, q_lin, after(gain_q, dq, *ready), cos, sin, w_q)
    d_kv, into_c, k_heads_c = kv_back(
        1, keys_c, values_c, k_lin_c, after(gain_k, q_part), cos, sin, w_kv, to_slots, q_part
    )
    into_got_c = swap(into_c, "tensor", 1)
    d_kv, into_p, k_heads_p = kv_back(
        0, keys_p, values_p, k_lin_p, after(gain_k, into_c), cos, sin, w_kv, to_slots, q_part, d_kv
    )
    into_got_p = swap(into_p, "tensor", 1)
    high, low = qkv_weight_grad(normed, after(d_q, into_p), d_kv)
    heads = jnp.concatenate([q_heads, k_heads_c + k_heads_p], axis=1)
    heads_got = swap(heads, "tensor", 1)
    grad_tokens, d_one_c = tokens_back(1, into_c, into_got_c, tokens, after(gain_one, low), d_resid_c)
    out_share, gate_share, up_share, down_share = unpack(chunk, o_cols, after(rest_share, d_one_c))
    qkv_grad = scatter_rows(low, high, gate_share)
    layer_out = add_layer(0, after(resid_p, qkv_grad[0]), out_p, out_got_p)
    qkv_grad = scatter_more(qkv_grad, layer_out)
    layer_out = add_layer(1, after(resid_c, qkv_grad[0]), out_c, out_got_c, layer_out)
    qkv_grad = scatter_sum(qkv_grad, layer_out)
    grad_tokens, d_one_p = tokens_back(
        0, into_p, into_got_p, tokens, after(gain_one, qkv_grad[0]), d_resid_p, grad_tokens
    )
    heads = heads + after(heads_got, d_one_p)
    late = jnp.concatenate([d_one_c + d_one_p, heads, d_two_c + d_two_p], axis=1)
    late = butterfly(late, ("ctx", "shard"))
    qkv_share = add_low(qkv_grad[0][:wide], after(qkv_grad[1], d_one_p)).astype(F32)

    def own_gain(value, size):
        return lax.dynamic_index_in_dim(value.reshape(parts, size), part, 0, keepdims=False)

    return (
        layer_out,
        grad_tokens,
        own_gain(late[:, :model], wide),
        own_gain(late[:, model + 2 * HEAD_SIZE :], wide),
        own_gain(late[:, model : model + HEAD_SIZE], narrow),
        own_gain(late[:, model + HEAD_SIZE : model + 2 * HEAD_SIZE], narrow),
        qkv_share[:, :q_cols],
        qkv_share[:, q_cols : q_cols + k_cols],
        qkv_share[:, q_cols + k_cols :],
        out_share.T,
        gate_share,
        up_share,
        down_share.T,
    )


def solution(mesh):
    split = ("shard", "ctx")
    rows, gain = P(split, None), P(split)
    into, out_of = P(split, "tensor"), P("tensor", split)
    in_specs = (rows, P("shard", None)) + (gain,) * 4 + (into,) * 3 + (out_of,)
    in_specs += (into, into, out_of, rows)
    out_specs = (rows, rows) + (gain,) * 4 + (into,) * 3 + (out_of, into, into, out_of)
    return jax.shard_map(body, mesh=mesh, in_specs=in_specs, out_specs=out_specs, check_vma=False)
```

```python
import functools
import math

import jax
import jax.numpy as jnp
from jax import lax
from jax.experimental import pallas as pl
from jax.experimental.pallas import tpu as pltpu
from jax.sharding import PartitionSpec as P

HEAD_SIZE = 128
PROMPT = 4096
CONT_TOK = 4096
LONGEST = 1024

EPSILON = 1e-06
ROPE_BASE = 1000000.0
MASKED = -1e30
LOG2E = math.log2(math.e)
LN2 = math.log(2.0)
SCALE = 1.0 / math.sqrt(HEAD_SIZE)

BF = jnp.bfloat16
F32 = jnp.float32
NN = (((1,), (0,)), ((), ()))
NT = (((1,), (1,)), ((), ()))
TN = (((0,), (0,)), ((), ()))
MIB = 2**20
STATED = 3e9


def mm(left, right, dims=NN):
    return lax.dot_general(left, right, dims, preferred_element_type=F32)


def shaped(dims, kind):
    return jax.ShapeDtypeStruct(dims, kind)


def call(kernel, name, grid, ins, outs, scratch=(), vmem=56, scalars=None, keep=None, us=0):
    in_specs, arrays = [], []
    for array, block, index in ins:
        arrays.append(array)
        in_specs.append(pl.BlockSpec(memory_space=pl.ANY) if block is None else pl.BlockSpec(block, index))
    lead = 0 if scalars is None else 1
    return pl.pallas_call(
        kernel,
        grid_spec=pltpu.PrefetchScalarGridSpec(
            num_scalar_prefetch=lead,
            grid=grid,
            in_specs=in_specs,
            out_specs=[pl.BlockSpec(block, index) for _, block, index in outs],
            scratch_shapes=list(scratch),
        ),
        out_shape=[shape for shape, _, _ in outs],
        input_output_aliases={a + lead: b for a, b in (keep or {}).items()},
        compiler_params=pltpu.CompilerParams(vmem_limit_bytes=vmem * MIB),
        cost_estimate=pl.CostEstimate(flops=int(us * STATED), bytes_accessed=0, transcendentals=0),
        name=name,
    )(*([] if scalars is None else [scalars]), *arrays)


def rms(values):
    return lax.rsqrt(jnp.mean(values * values, axis=-1, keepdims=True) + EPSILON)


def turn(values, cos, sin):
    return values * cos + pltpu.roll(values, HEAD_SIZE // 2, 1) * sin


def turn_back(values, cos, sin):
    return values * cos - pltpu.roll(values, HEAD_SIZE // 2, 1) * sin


def kv_kernel(heads, x_ref, gain_ref, w_ref, hgain_ref, cos_ref, sin_ref, *refs):
    normed_ref, kv_ref, lin_ref = refs[-3:]
    x = x_ref[...].astype(F32)
    normed_ref[...] = (x * rms(x) * gain_ref[...]).astype(BF)
    both = mm(normed_ref[...], w_ref[...])
    width = heads * HEAD_SIZE
    kv_ref[1] = both[:, width:].astype(BF)
    for h in range(heads):
        cols = slice(h * HEAD_SIZE, (h + 1) * HEAD_SIZE)
        lin = both[:, cols]
        lin_ref[:, cols] = lin
        kv_ref[0, :, cols] = turn(lin * rms(lin) * hgain_ref[...], cos_ref[...], sin_ref[...]).astype(BF)


def q_kernel(heads, normed_ref, w_ref, hgain_ref, cos_ref, sin_ref, q_ref, lin_ref):
    both = mm(normed_ref[...], w_ref[...])
    for h in range(heads):
        cols = slice(h * HEAD_SIZE, (h + 1) * HEAD_SIZE)
        lin = both[:, cols]
        lin_ref[:, cols] = lin
        turned = turn(lin * rms(lin) * hgain_ref[...], cos_ref[...], sin_ref[...])
        q_ref[:, cols] = (turned * (SCALE * LOG2E)).astype(BF)


def pack_kernel(chunk, key_ref, value_ref, out_ref, gate_ref, up_ref, down_ref, kv_ref, rest_ref):
    k_cols, o_cols, units = key_ref.shape[1], out_ref.shape[1], gate_ref.shape[1]
    kv_ref[:, :k_cols] = key_ref[...]
    kv_ref[:, k_cols:] = value_ref[...]
    rest_ref[:, :o_cols] = out_ref[...]
    for at in range(0, units, chunk):
        to = o_cols + 2 * at
        rest_ref[:, to : to + chunk] = gate_ref[:, at : at + chunk]
        rest_ref[:, to + chunk : to + 2 * chunk] = up_ref[:, at : at + chunk]
    rest_ref[:, o_cols + 2 * units :] = down_ref[...]


def pack(chunk, *weights):
    wide, k_cols = weights[0].shape
    width = weights[2].shape[1] + 3 * weights[3].shape[1]
    whole = lambda f: (0, 0)
    ins = [(w, w.shape, whole) for w in weights]
    outs = [(shaped((wide, cols), BF), (wide, cols), whole) for cols in (2 * k_cols, width)]
    return call(functools.partial(pack_kernel, chunk), "pack", (1,), ins, outs)


def by_top_bit(slots):
    groups = {}
    for at, s in enumerate(slots):
        if s:
            groups.setdefault(1 << (s.bit_length() - 1), []).append(at)
    return groups


def fwd_kernel(plan, idx_ref, lo_ref, *refs):
    halves, slots, halos = plan["halves"], plan["slots"], plan["halos"]
    refs = list(refs)
    q_refs = [refs.pop(0) for _ in halves]
    slot_refs = [refs.pop(0) for _ in slots]
    halo_refs = [refs.pop(0) for _ in halos]
    prior = [refs.pop(0) for _ in range(2 * len(halves))] if plan["carry"] else None
    if plan["last"]:
        if plan["alias"]:
            refs.pop(0)
        out_ref, lse_ref = refs[:2]
        refs = refs[2:]
    else:
        results, refs = refs[: 2 * len(halves)], refs[2 * len(halves) :]
    me, lo_first = idx_ref[0], idx_ref[1]
    rows = q_refs[0].shape[0]
    row = lax.broadcasted_iota(jnp.int32, (2 * rows, 1), 0)
    row = jnp.where(row >= rows, row - rows, row)
    col = lax.broadcasted_iota(jnp.int32, (1, rows), 1)
    for n, half in enumerate(halves):
        qs, acc, tot = refs[3 * n : 3 * n + 3]
        for g in range(2):
            cols, at = slice(g * HEAD_SIZE, (g + 1) * HEAD_SIZE), slice(g * rows, (g + 1) * rows)
            qs[at, :] = q_refs[n][:, cols]
            if prior is not None:
                acc[at, :] = prior[2 * n][:, cols]
                tot[at, :] = prior[2 * n + 1][:, cols]
        empty = [prior is None]

        def add(kv_ref, mask=None):
            scores = mm(qs[...], kv_ref[0], NT)
            if mask is not None:
                scores = jnp.where(mask, scores, MASKED)
            weights = jnp.exp2(scores)
            total = weights[:, :128]
            for at in range(128, weights.shape[1], 128):
                total = total + weights[:, at : at + 128]
            part = mm(weights.astype(BF), kv_ref[1])
            if empty[0]:
                acc[...] = part
                tot[...] = total
            else:
                acc[...] += part
                tot[...] += total
            empty[0] = False

        if half == 1:
            for kv_ref in slot_refs:
                add(kv_ref)
            low = jnp.concatenate([lo_ref[:, :1], lo_ref[:, :1]])
            for d, kv_ref in zip(halos, halo_refs):
                if d == 0:
                    add(kv_ref, (col <= row) & (col >= low))
                else:

                    @pl.when(lo_first < -(d - 1) * rows)
                    def _(d=d, kv_ref=kv_ref):
                        add(kv_ref, col - d * rows >= low)

        else:
            if 0 in slots:
                add(slot_refs[slots.index(0)], col <= row)
            for bit, group in by_top_bit(slots).items():

                @pl.when(jnp.bitwise_and(me, bit) != 0)
                def _(group=group):
                    for at in group:
                        add(slot_refs[at])

        if not plan["last"]:
            for g in range(2):
                cols, at = slice(g * HEAD_SIZE, (g + 1) * HEAD_SIZE), slice(g * rows, (g + 1) * rows)
                results[2 * n][:, cols] = acc[at, :]
                results[2 * n + 1][:, cols] = tot[at, :]
    if plan["last"]:
        qs, acc, tot = refs
        for g in range(2):
            cols, at = slice(g * HEAD_SIZE, (g + 1) * HEAD_SIZE), slice(g * rows, (g + 1) * rows)
            total = jnp.sum(tot[at, :], axis=1, keepdims=True)
            out_ref[:, cols] = (acc[at, :] / total).astype(BF)
            lse_ref[0, g : g + 1, :] = jnp.log2(jnp.sum(tot[at, :].T, axis=0, keepdims=True))


def attention_forward(halves, scalars, q, low, slots, halos, carry=None, last=None):
    rows, heads = q.shape[0] // 2, q.shape[1] // 256
    plan = dict(halves=halves, slots=list(slots), halos=list(halos), carry=carry is not None,
                last=last is not None, alias=last is not None and last[0] is not None)
    part = lambda h, i: (0, h)
    ins = [(low, (rows, 128), lambda h, i: (0, 0))]
    ins += [(q, (rows, 256), lambda h, i, half=half: (half, h)) for half in halves]
    for kv in list(slots.values()) + list(halos.values()):
        ins.append((kv, (2, rows, 128), lambda h, i: (0, 0, h)))
    if carry is not None:
        ins += [(c, (rows, 256), part) for c in carry]
    scratch, keep = [], {}
    for _ in halves:
        scratch += [pltpu.VMEM((2 * rows, 128), BF)] + [pltpu.VMEM((2 * rows, 128), F32)] * 2
    state = shaped((rows, heads * 256), F32)
    if last is None:
        outs = [(state, (rows, 256), part)] * (2 * len(halves))
    else:
        other = last[0]
        if other is not None:
            keep = {len(ins): 0}
            ins.append((other, None, None))
        half = halves[0]
        outs = [
            (shaped((2 * rows, heads * 256), BF), (rows, 256), lambda h, i: (half, h)),
            (shaped((heads, 8, rows), F32), (1, 8, rows), lambda h, i: (h, 0, 0)),
        ]
    return call(functools.partial(fwd_kernel, plan), "attend", (heads,), ins, outs, scratch,
                scalars=scalars, keep=keep)


def out_kernel(att_ref, w_ref, part_ref):
    part_ref[...] = mm(att_ref[...], w_ref[...], NT).astype(BF)


def out_projection(half, attended, w_rest):
    rows, cols = attended.shape[0] // 2, attended.shape[1]
    model = w_rest.shape[0]
    ins = [(attended, (rows, cols), lambda j: (half, 0)), (w_rest, (model // 2, cols), lambda j: (j, 0))]
    outs = [(shaped((rows, model), BF), (rows, model // 2), lambda j: (0, j))]
    return call(out_kernel, "out_projection", (2,), ins, outs)[0]


def bwd_kernel(plan, idx_ref, q_ref, do_ref, lse_ref, delta_ref, lo_ref, *refs):
    half, slots, halos = plan["half"], plan["slots"], plan["halos"]
    refs = list(refs)
    slot_refs = [refs.pop(0) for _ in slots]
    halo_refs = [refs.pop(0) for _ in halos]
    prior_dq = refs.pop(0) if plan["carry"] else None
    prior = [refs.pop(0) for _ in slots] if plan["sum"] else None
    if plan["alias"]:
        refs.pop(0)
    dq_ref = refs.pop(0)
    slot_outs = [refs.pop(0) for _ in slots]
    halo_outs = [refs.pop(0) for _ in halos]
    qs, dos, lses, deltas, dq = refs
    me, lo_first = idx_ref[0], idx_ref[1]
    rows = q_ref.shape[0]
    for g in range(2):
        cols, at = slice(g * HEAD_SIZE, (g + 1) * HEAD_SIZE), slice(g * rows, (g + 1) * rows)
        qs[at, :] = q_ref[:, cols]
        dos[at, :] = do_ref[:, cols]
        lses[:, at] = lse_ref[0, g : g + 1, :]
        deltas[:, at] = delta_ref[0, g : g + 1, :]
    dq[...] = jnp.zeros_like(dq) if prior_dq is None else prior_dq[...]

    def block(kv_ref, out_ref, mask=None, before=None):
        keys = kv_ref[0]
        scores = mm(keys, qs[...], NT)
        dp = mm(kv_ref[1], dos[...], NT)
        scores = scores - lses[...]
        if mask is not None:
            scores = jnp.where(mask, scores, MASKED)
        probs = jnp.exp2(scores)
        ds = (probs * (dp - deltas[...])).astype(BF)
        dq[...] += mm(keys.T, ds)
        dk, dv = mm(ds, qs[...]) * LN2, mm(probs.astype(BF), dos[...])
        if before is not None:
            dk, dv = dk + before[0].astype(F32), dv + before[1].astype(F32)
        out_ref[0] = dk.astype(BF)
        out_ref[1] = dv.astype(BF)

    lane = lax.broadcasted_iota(jnp.int32, (1, 2 * rows), 1)
    lane = jnp.where(lane >= rows, lane - rows, lane)
    key = lax.broadcasted_iota(jnp.int32, (rows, 1), 0)

    def when(needed, kv_ref, out_ref, mask=None):
        @pl.when(needed)
        def _():
            block(kv_ref, out_ref, mask)

        @pl.when(jnp.logical_not(needed))
        def _():
            out_ref[...] = jnp.zeros_like(out_ref)

    low = lo_ref[:1, :]
    for d, kv_ref, out_ref in zip(halos, halo_refs, halo_outs):
        if d == 0:
            block(kv_ref, out_ref, (key <= lane) & (key >= low))
        else:
            when(lo_first < -(d - 1) * rows, kv_ref, out_ref, key - d * rows >= low)
    if half == 1:
        for at in range(len(slots)):
            block(slot_refs[at], slot_outs[at], None, prior[at] if prior else None)
    else:
        if 0 in slots:
            at = slots.index(0)
            block(slot_refs[at], slot_outs[at], key <= lane)
        for bit, group in by_top_bit(slots).items():

            @pl.when(jnp.bitwise_and(me, bit) != 0)
            def _(group=group):
                for at in group:
                    block(slot_refs[at], slot_outs[at])

            @pl.when(jnp.bitwise_and(me, bit) == 0)
            def _(group=group):
                for at in group:
                    slot_outs[at][...] = jnp.zeros_like(slot_outs[at])

    if plan["last"]:
        for g in range(2):
            cols = slice(g * HEAD_SIZE, (g + 1) * HEAD_SIZE)
            dq_ref[:, cols] = dq[:, g * rows : (g + 1) * rows].T * SCALE
    else:
        dq_ref[...] = dq[...]


def attention_backward(half, scalars, q, do, lse, delta, low, slots, halos, carry=None, prior=None, last=True, whole=None):
    rows, heads = q.shape[0] // 2, q.shape[1] // 256
    plan = dict(half=half, slots=list(slots), halos=list(halos), carry=carry is not None,
                sum=prior is not None, last=last, alias=whole is not None)
    part = lambda h, i: (0, h)
    stat = lambda h, i: (h, 0, 0)
    kv_map = lambda h, i: (0, 0, h)
    ins = [
        (q, (rows, 256), lambda h, i: (half, h)),
        (do, (rows, 256), part),
        (lse, (1, 8, rows), stat),
        (delta, (1, 8, rows), stat),
        (low, (8, 2 * rows), lambda h, i: (0, 0)),
    ]
    pieces = list(slots.values()) + list(halos.values())
    ins += [(kv, (2, rows, 128), kv_map) for kv in pieces]
    if carry is not None:
        ins.append((carry, (128, 2 * rows), lambda h, i: (h, 0)))
    if prior is not None:
        ins += [(prior[s], (2, rows, 128), kv_map) for s in slots]
    keep = {}
    if whole is not None:
        keep = {len(ins): 0}
        ins.append((whole, None, None))
    if last:
        outs = [(shaped((2 * rows, heads * 256), F32), (rows, 256), lambda h, i: (half, h))]
    else:
        outs = [(shaped((heads * 128, 2 * rows), F32), (128, 2 * rows), lambda h, i: (h, 0))]
    outs += [(shaped(kv.shape, BF), (2, rows, 128), kv_map) for kv in pieces]
    scratch = [
        pltpu.VMEM((2 * rows, 128), BF),
        pltpu.VMEM((2 * rows, 128), BF),
        pltpu.VMEM((1, 2 * rows), F32),
        pltpu.VMEM((1, 2 * rows), F32),
        pltpu.VMEM((128, 2 * rows), F32),
    ]
    us = 4 + 6 * (len(slots) + len(halos)) if carry is not None or halos else 0
    results = call(functools.partial(bwd_kernel, plan), "attend_back", (heads,), ins, outs, scratch,
                   scalars=scalars, us=us, keep=keep)
    n = len(slots)
    return results[0], dict(zip(slots, results[1 : 1 + n])), dict(zip(halos, results[1 + n :]))


def ffn_kernel(x_ref, own_ref, got_ref, gain_ref, dy_ref, gu_ref, down_ref, *refs):
    resid_ref, normed_ref, hidden_ref, dgu_ref, out_ref, back_ref, normed, out_acc, back_acc = refs[-9:]
    step, steps = pl.program_id(0), pl.num_programs(0)

    @pl.when(step == 0)
    def _():
        resid = x_ref[...].astype(F32) + (own_ref[...].astype(F32) + got_ref[...].astype(F32))
        resid_ref[...] = resid
        normed[...] = (resid * rms(resid) * gain_ref[...]).astype(BF)
        normed_ref[...] = normed[...]
        out_acc[...] = jnp.zeros_like(out_acc)
        back_acc[...] = jnp.zeros_like(back_acc)

    wide = down_ref.shape[1]
    both = mm(normed[...], gu_ref[...])
    d_hidden = mm(dy_ref[...], down_ref[...])
    gate, up = both[:, :wide], both[:, wide:]
    sig = 1.0 / (1.0 + jnp.exp(-gate))
    silu = gate * sig
    hidden = (silu * up).astype(BF)
    hidden_ref[...] = hidden
    d_up = (d_hidden * silu).astype(BF)
    d_gate = (d_hidden * up * (sig + silu * (1.0 - sig))).astype(BF)
    dgu_ref[:, :wide] = d_gate
    dgu_ref[:, wide:] = d_up
    out_acc[...] += mm(hidden, down_ref[...], NT)
    back_acc[...] += mm(dgu_ref[...], gu_ref[...], NT)

    @pl.when(step == steps - 1)
    def _():
        out_ref[...] = out_acc[...].astype(BF)
        back_ref[...] = back_acc[...].astype(BF)


def feed_forward(half, x, own, got, gain, dy, w_rest, o_cols, chunk, whole=None):
    rows, model = own.shape
    units = (w_rest.shape[1] - o_cols) // 3
    steps = units // chunk
    mine, once = lambda f: (half, 0), lambda f: (0, 0)
    at_gu, at_down = o_cols // (2 * chunk), (o_cols + 2 * units) // chunk
    block = (rows, model)
    ins = [
        (x, block, mine), (own, block, once), (got, block, once), (gain, (1, model), once), (dy, block, mine),
        (w_rest, (model, 2 * chunk), lambda f: (0, at_gu + f)),
        (w_rest, (model, chunk), lambda f: (0, at_down + f)),
    ]
    keep = {}
    if whole is not None:
        keep = {len(ins) + i: 1 + i for i in range(3)}
        ins += [(array, None, None) for array in whole]
    outs = [
        (shaped((rows, model), F32), block, once),
        (shaped((2 * rows, model), BF), block, mine),
        (shaped((2 * rows, units), BF), (rows, chunk), lambda f: (half, f)),
        (shaped((2 * rows, 2 * units), BF), (rows, 2 * chunk), lambda f: (half, f)),
        (shaped((rows, model), BF), block, once),
        (shaped((rows, model), BF), block, once),
    ]
    scratch = [pltpu.VMEM(block, BF), pltpu.VMEM(block, F32), pltpu.VMEM(block, F32)]
    return call(ffn_kernel, "feed_forward", (steps,), ins, outs, scratch, keep=keep)


def norm_back(grad, values, gain):
    scale = rms(values)
    unit = values * scale
    inner = grad * gain
    return scale * (inner - unit * jnp.mean(inner * unit, axis=-1, keepdims=True)), grad * unit


def row_blocks(rows):
    size = rows // 2 if rows % 512 == 0 else rows
    return size, rows // size


def add_up(ref, value):
    total = jnp.sum(value, axis=0, keepdims=True)

    @pl.when(pl.program_id(0) == 0)
    def _():
        ref[...] = total

    @pl.when(pl.program_id(0) > 0)
    def _():
        ref[...] += total


def mixed_kernel(heads, own_ref, got_ref, resid_ref, gain_ref, dy_ref, w_ref, att_ref, *refs):
    d_resid_ref, mixed_ref, datt_ref, delta_ref, dgain_ref = refs[-5:]
    grad = own_ref[...].astype(F32) + got_ref[...].astype(F32)
    d_norm, summand = norm_back(grad, resid_ref[...], gain_ref[...])
    add_up(dgain_ref, summand)
    d_resid = dy_ref[...].astype(F32) + d_norm
    d_resid_ref[...] = d_resid
    mixed_ref[...] = d_resid.astype(BF)
    datt_ref[...] = mm(mixed_ref[...], w_ref[...]).astype(BF)
    for h in range(heads):
        cols = slice(h * HEAD_SIZE, (h + 1) * HEAD_SIZE)
        product = datt_ref[:, cols].astype(F32) * att_ref[:, cols].astype(F32)
        delta_ref[h // 2, h % 2 : h % 2 + 1, :] = jnp.sum(product.T, axis=0, keepdims=True)


def mixed_back(half, own, got, resid, gain, dy, w_rest, o_cols, attended, whole=None):
    rows, model = own.shape
    heads = o_cols // HEAD_SIZE
    size, steps = row_blocks(rows)
    mine, here, once = lambda f: (half * steps + f, 0), lambda f: (f, 0), lambda f: (0, 0)
    block = (size, model)
    ins = [
        (own, block, here), (got, block, here), (resid, block, here), (gain, (1, model), once),
        (dy, block, mine), (w_rest, (model, o_cols), once), (attended, (size, o_cols), mine),
    ]
    keep = {}
    if whole is not None:
        keep = {len(ins): 1}
        ins.append((whole, None, None))
    outs = [
        (shaped((rows, model), F32), block, here),
        (shaped((2 * rows, model), BF), block, mine),
        (shaped((rows, o_cols), BF), (size, o_cols), here),
        (shaped((heads // 2, 8, rows), F32), (heads // 2, 8, size), lambda f: (0, 0, f)),
        (shaped((1, model), F32), (1, model), once),
    ]
    return call(functools.partial(mixed_kernel, heads), "mixed_back", (steps,), ins, outs, keep=keep)


def merge_kernel(two, got3, four, got5, far_k, far_v, to_x, to_y):
    for which in range(2):
        by_x = two[which].astype(F32) + got3[which].astype(F32)
        by_y = four[which].astype(F32) + got5[which].astype(F32)
        to_x[which] = (by_x + far_v[...].astype(F32) if which else by_x).astype(BF)
        to_y[which] = (by_y if which else by_y + far_k[...].astype(F32)).astype(BF)


def merge(*pieces):
    rows, cols = pieces[-1].shape
    size, steps = row_blocks(rows)
    ins = []
    for piece in pieces:
        if piece.ndim == 3:
            ins.append((piece, (2, size, cols), lambda f: (0, f, 0)))
        else:
            ins.append((piece, (size, cols), lambda f: (f, 0)))
    outs = [(shaped((2, rows, cols), BF), (2, size, cols), lambda f: (0, f, 0))] * 2
    return call(merge_kernel, "merge", (steps,), ins, outs)


def weight_kernel(left_ref, right_ref, *refs):
    refs[-1][...] = mm(left_ref[...], right_ref[...], TN).astype(BF)


def weight_grad(left, right, at, width, cols, whole=None):
    tokens, model = left.shape
    n = right.shape[1]
    ins = [(left, (tokens, model), lambda j: (0, 0)), (right, (tokens, cols), lambda j: (0, j))]
    keep = {}
    if whole is not None:
        keep = {len(ins): 0}
        ins.append((whole, None, None))
    outs = [(shaped((model, width), BF), (model, cols), lambda j: (0, at // cols + j))]
    return call(weight_kernel, "weight_grad", (n // cols,), ins, outs, keep=keep)[0]


def weight_halves_kernel(left_ref, right_ref, high_ref, low_ref):
    for half, out_ref in enumerate((high_ref, low_ref)):

        @pl.when(pl.program_id(0) == half)
        def _(out_ref=out_ref):
            out_ref[...] = mm(left_ref[...], right_ref[...], TN).astype(BF)


def weight_halves(left, right):
    tokens, model = left.shape
    cols = right.shape[1]
    once = lambda i: (0, 0)
    ins = [(left, (tokens, model // 2), lambda i: (0, 1 - i)), (right, (tokens, cols), once)]
    half = shaped((model // 2, cols), BF)
    return call(weight_halves_kernel, "weight_halves", (2,), ins, [(half, half.shape, once)] * 2)


def q_back_kernel(heads, dq_ref, lin_ref, gain_ref, cos_ref, sin_ref, w_ref, *refs):
    d_ref, part_ref, gains_ref = refs[-3:]
    cos, sin = cos_ref[...], sin_ref[...]
    total = jnp.zeros(cos.shape, F32)
    for h in range(heads):
        cols = slice(h * HEAD_SIZE, (h + 1) * HEAD_SIZE)
        grad, summand = norm_back(turn_back(dq_ref[:, cols], cos, sin), lin_ref[:, cols], gain_ref[...])
        d_ref[:, cols] = grad.astype(BF)
        total = total + summand
    part_ref[...] = mm(d_ref[...], w_ref[...], NT)
    add_up(gains_ref, total)


def q_back(dq, lin, gain, cos, sin, w):
    rows, cols = dq.shape
    model = w.shape[0]
    size, steps = row_blocks(rows)
    here, once = lambda f: (f, 0), lambda f: (0, 0)
    ins = [
        (dq, (size, cols), here), (lin, (size, cols), here), (gain, (1, HEAD_SIZE), once),
        (cos, (size, HEAD_SIZE), here), (sin, (size, HEAD_SIZE), here), (w, (model, cols), once),
    ]
    outs = [
        (shaped((rows, cols), BF), (size, cols), here),
        (shaped((rows, model), F32), (size, model), here),
        (shaped((1, HEAD_SIZE), F32), (1, HEAD_SIZE), once),
    ]
    kernel = functools.partial(q_back_kernel, cols // HEAD_SIZE)
    return call(kernel, "q_back", (steps,), ins, outs)


def kv_back_kernel(heads, n_keys, n_values, lin_ref, gain_ref, cos_ref, sin_ref, w_ref, slots_ref, q_part_ref, *refs):
    key_refs, value_refs = refs[:n_keys], refs[n_keys : n_keys + n_values]
    d_ref, part_ref, gains_ref = refs[-3:]
    cos, sin = cos_ref[...], sin_ref[...]
    width = heads * HEAD_SIZE

    def total(sources, which, cols):
        value = None
        for ref in sources:
            piece = ref[which, :, cols] if len(ref.shape) == 3 else ref[:, cols]
            value = piece.astype(F32) if value is None else value + piece.astype(F32)
        return value

    gains = jnp.zeros(cos.shape, F32)
    for h in range(heads):
        cols = slice(h * HEAD_SIZE, (h + 1) * HEAD_SIZE)
        grad, summand = norm_back(
            turn_back(total(key_refs, 0, cols), cos, sin), lin_ref[:, cols], gain_ref[...]
        )
        d_ref[:, cols] = grad.astype(BF)
        gains = gains + summand
    d_ref[:, width:] = total(value_refs, 1, slice(None)).astype(BF)
    part = (q_part_ref[...] + mm(d_ref[...], w_ref[...], NT)).astype(BF)
    part_ref[...] = mm(part, slots_ref[...], NT).astype(BF)
    add_up(gains_ref, gains)


def kv_back(half, keys, values, lin, gain, cos, sin, w, to_slots, q_part, whole=None):
    rows, cols = lin.shape
    model = w.shape[0]
    size, steps = row_blocks(rows)
    mine, here, once = lambda f: (half * steps + f, 0), lambda f: (f, 0), lambda f: (0, 0)
    ins = [
        (lin, (size, cols), here), (gain, (1, HEAD_SIZE), once), (cos, (size, HEAD_SIZE), mine),
        (sin, (size, HEAD_SIZE), mine), (w, (model, 2 * cols), once),
        (to_slots, (model, model), once), (q_part, (size, model), mine),
    ]
    for piece in list(keys) + list(values):
        if piece.ndim == 3:
            ins.append((piece, (2, size, cols), lambda f: (0, f, 0)))
        else:
            ins.append((piece, (size, cols), here))
    keep = {}
    if whole is not None:
        keep = {len(ins): 0}
        ins.append((whole, None, None))
    outs = [
        (shaped((2 * rows, 2 * cols), BF), (size, 2 * cols), mine),
        (shaped((rows, model), BF), (size, model), here),
        (shaped((1, HEAD_SIZE), F32), (1, HEAD_SIZE), once),
    ]
    kernel = functools.partial(kv_back_kernel, cols // HEAD_SIZE, len(keys), len(values))
    return call(kernel, "kv_back", (steps,), ins, outs, keep=keep, us=3 * (1 - half))


def tokens_kernel(own_ref, got_ref, x_ref, gain_ref, d_resid_ref, *refs):
    out_ref, dgain_ref = refs[-2:]
    grad = own_ref[...].astype(F32) + got_ref[...].astype(F32)
    d_norm, summand = norm_back(grad, x_ref[...].astype(F32), gain_ref[...])
    add_up(dgain_ref, summand)
    out_ref[...] = (d_resid_ref[...] + d_norm).astype(BF)


def tokens_back(half, own, got, x, gain, d_resid, whole=None):
    rows, model = own.shape
    size, steps = row_blocks(rows)
    mine, here, once = lambda f: (half * steps + f, 0), lambda f: (f, 0), lambda f: (0, 0)
    block = (size, model)
    ins = [(own, block, here), (got, block, here), (x, block, mine), (gain, (1, model), once), (d_resid, block, here)]
    keep = {}
    if whole is not None:
        keep = {len(ins): 0}
        ins.append((whole, None, None))
    outs = [(shaped((2 * rows, model), BF), block, mine), (shaped((1, model), F32), (1, model), once)]
    return call(tokens_kernel, "tokens_back", (steps,), ins, outs, keep=keep, us=20)


def share_kernel(chunk, share_ref, out_ref, gate_ref, up_ref, down_ref):
    o_cols, units = out_ref.shape[1], gate_ref.shape[1]
    out_ref[...] = share_ref[:, :o_cols].astype(F32)
    for at in range(0, units, chunk):
        to = o_cols + 2 * at
        gate_ref[:, at : at + chunk] = share_ref[:, to : to + chunk].astype(F32)
        up_ref[:, at : at + chunk] = share_ref[:, to + chunk : to + 2 * chunk].astype(F32)
    down_ref[...] = share_ref[:, o_cols + 2 * units :].astype(F32)


def unpack(chunk, o_cols, share):
    wide = share.shape[0]
    units = (share.shape[1] - o_cols) // 3
    whole = lambda f: (0, 0)
    outs = [(shaped((wide, cols), F32), (wide, cols), whole) for cols in (o_cols, units, units, units)]
    return call(functools.partial(share_kernel, chunk), "unpack", (1,), [(share, share.shape, whole)], outs)


def layer_kernel(resid_ref, own_ref, got_ref, *refs):
    refs[-1][...] = (resid_ref[...] + (own_ref[...].astype(F32) + got_ref[...].astype(F32))).astype(BF)


def add_layer(half, resid, own, got, whole=None):
    rows, model = resid.shape
    size, steps = row_blocks(rows)
    here, mine = lambda f: (f, 0), lambda f: (half * steps + f, 0)
    ins = [(array, (size, model), here) for array in (resid, own, got)]
    keep = {}
    if whole is not None:
        keep = {len(ins): 0}
        ins.append((whole, None, None))
    outs = [(shaped((2 * rows, model), BF), (size, model), mine)]
    return call(layer_kernel, "add_layer", (steps,), ins, outs, keep=keep)[0]


def swap(value, axis, bit):
    size = lax.axis_size(axis)
    return lax.ppermute(value, axis, [(i, i ^ bit) for i in range(size)])


def shift(value, by):
    size = lax.axis_size("ctx")
    return lax.ppermute(value, "ctx", [(i, i + by) for i in range(size) if 0 <= i + by < size])


def add_low(left, right):
    return (left.astype(F32) + right.astype(F32)).astype(BF)


def butterfly(value, axes, gates=()):
    gates = list(gates)
    for axis in axes:
        bit = 1
        while bit < lax.axis_size(axis):
            got = swap(value, axis, bit)
            value = value + (after(got, gates.pop(0)) if gates else got)
            bit *= 2
    return value


def after(value, *others):
    return lax.optimization_barrier((value, *others))[0]


def rotary_tables(position):
    half_dim = HEAD_SIZE // 2
    inverse_freq = jnp.exp(jnp.arange(half_dim, dtype=F32) * (-math.log(ROPE_BASE) / half_dim))
    angles = position.astype(F32)[:, None] * inverse_freq[None, :]
    cosine, sine = jnp.cos(angles), jnp.sin(angles)
    return jnp.concatenate([cosine, cosine], axis=-1), jnp.concatenate([-sine, sine], axis=-1)


def body(
    tokens,
    cont_lengths,
    attn_gain,
    ffn_gain,
    query_gain,
    key_gain,
    w_query,
    key_weight,
    value_weight,
    w_out,
    w_gate,
    w_up,
    w_down,
    cotangent,
):
    ctx_size = lax.axis_size("ctx")
    weight_axes = ("shard", "ctx")
    parts = lax.axis_size("shard") * ctx_size
    me = lax.axis_index("ctx")
    part = lax.axis_index("shard") * ctx_size + me
    rows, model = tokens.shape[0] // 2, tokens.shape[1]
    n_halo = 1 + -(-(LONGEST - 1) // rows)
    lengths = cont_lengths[0]

    bits = [("shard", 1)] + [("ctx", 1 << i) for i in range(1, ctx_size.bit_length() - 1)] + [("ctx", 1)]
    order = [0]
    for axis, bit in bits:
        order += [j ^ (bit * ctx_size if axis == "shard" else bit) for j in order]
    wide, narrow = attn_gain.shape[0], query_gain.shape[0]
    q_cols, k_cols = w_query.shape[1], key_weight.shape[1]
    o_cols, units = w_out.shape[0], w_gate.shape[1]
    heads, kv_heads = q_cols // HEAD_SIZE, k_cols // HEAD_SIZE
    chunk = math.gcd(units, 512)

    def gather_first(piece, *gate):
        return jnp.concatenate([piece, after(swap(piece, "shard", 1), *gate)]) if ctx_size == 8 else piece

    def gather_rows(one, gates=((),) * 3):
        if ctx_size != 8:
            for axis, bit in bits:
                one = jnp.concatenate([one, swap(one, axis, bit)])
            return one, (one,) * 3
        by_x, by_y = (after(v, *gates[0]) for v in (swap(one, "ctx", 2), swap(one, "ctx", 4)))
        cut = one.shape[1] // 2
        left, right = swap(by_y[:, :cut], "ctx", 2), swap(by_x[:, cut:], "ctx", 4)
        far = jnp.concatenate([after(left, *gates[1]), after(right, *gates[1])], axis=1)
        half = jnp.concatenate([one, by_x, by_y, far])
        whole = jnp.concatenate([half, after(swap(half, "ctx", 1), *gates[2])])
        return whole, (by_x, half, whole)

    def scatter_rows(low, high, late):
        total = add_low(low, after(swap(high, "ctx", 1), late))
        if ctx_size != 8:
            for axis, bit in bits[-2:0:-1]:
                size = total.shape[0] // 2
                total = add_low(total[:size], swap(total[size:], axis, bit))
            return (total,)
        size, cut = total.shape[0] // 4, total.shape[1] // 2
        own, by_x, by_y, far = (total[i * size : (i + 1) * size] for i in range(4))
        left, right = swap(far[:, :cut], "ctx", 2), swap(far[:, cut:], "ctx", 4)
        return own, by_x, by_y, left, right

    def scatter_more(stage, late):
        if ctx_size != 8:
            return stage
        own, by_x, by_y, left, right = stage
        left, right = after(left, late), after(right, late)
        cut = left.shape[1]
        by_x = jnp.concatenate([by_x[:, :cut], add_low(by_x[:, cut:], right)], axis=1)
        by_y = jnp.concatenate([add_low(by_y[:, :cut], left), by_y[:, cut:]], axis=1)
        return lax.optimization_barrier((own, by_x, by_y))[0], swap(by_x, "ctx", 2), swap(by_y, "ctx", 4)

    def scatter_sum(stage, late):
        total = stage[0].astype(F32)
        for piece in stage[1:]:
            total = total + after(piece, late).astype(F32)
        total, size = total.astype(BF), total.shape[0] // 2
        return total, swap(total[size:], "shard", 1)

    kv_piece, rest_piece = pack(chunk, key_weight, value_weight, w_out.T, w_gate, w_up, w_down.T)
    kv_one = gather_first(kv_piece)
    w_kv, stages = gather_rows(kv_one)
    q_one = gather_first(after(w_query, kv_one), stages[1])
    w_rest = lax.all_gather(rest_piece, weight_axes, axis=0, tiled=True)
    gains = jnp.concatenate([attn_gain, ffn_gain, query_gain, key_gain])[None]
    gains = jnp.where(jnp.arange(parts)[:, None] == part, gains, jnp.zeros((), BF))
    gains = gains + after(swap(gains, "ctx", 1), kv_piece)
    for at, (axis, bit) in enumerate(bits[:-1]):
        gains = gains + after(swap(gains, axis, bit), (kv_one, *stages)[min(at, 2)])
    gains = gains.astype(F32)
    gain_one = gains[:, :wide].reshape(1, -1)
    gain_two = gains[:, wide : 2 * wide].reshape(1, -1)
    gain_q = gains[:, 2 * wide : 2 * wide + narrow].reshape(1, -1)
    gain_k = gains[:, 2 * wide + narrow :].reshape(1, -1)
    source = jnp.bitwise_xor(part, jnp.array(order, jnp.int32))[:, None] * wide + jnp.arange(wide, dtype=jnp.int32)
    to_slots = (jnp.arange(model, dtype=jnp.int32)[:, None] == source.reshape(1, -1)).astype(BF)
    tokens_s = mm(after(tokens, q_one), to_slots).astype(BF)
    gain_one_s = mm(gain_one.astype(BF), to_slots)

    cont_at = me * rows + jnp.arange(rows, dtype=jnp.int32)
    cont_ends = jnp.cumsum(lengths)
    starts = cont_ends - lengths
    seg = jnp.sum((cont_ends[None, :] <= cont_at[:, None]).astype(jnp.int32), axis=1)
    numbers = jnp.arange(lengths.shape[0], dtype=jnp.int32)
    first = jnp.sum(jnp.where(numbers[None, :] == seg[:, None], starts[None, :], 0), axis=1)
    position = jnp.concatenate([me * rows + jnp.arange(rows, dtype=jnp.int32), PROMPT + cont_at - first])
    low = first - me * rows
    low_col = jnp.broadcast_to(low[:, None], (rows, 128))
    low_row = jnp.broadcast_to(jnp.concatenate([low, low])[None, :], (8, 2 * rows))
    scalars = jnp.stack([me, low[0]])
    cos, sin = rotary_tables(position)

    once = lambda f: (0, 0)

    def keys_values(half, gain, whole=None):
        mine = lambda f: (half, 0)
        ins = [
            (tokens_s, (rows, model), mine), (gain, (1, model), once), (w_kv, (model, 2 * k_cols), once),
            (gain_k, (1, HEAD_SIZE), once), (cos, (rows, HEAD_SIZE), mine), (sin, (rows, HEAD_SIZE), mine),
        ]
        keep = {}
        if whole is not None:
            keep = {len(ins): 0}
            ins.append((whole, None, None))
        outs = [
            (shaped((2 * rows, model), BF), (rows, model), mine),
            (shaped((2, rows, k_cols), BF), (2, rows, k_cols), lambda f: (0, 0, 0)),
            (shaped((rows, k_cols), F32), (rows, k_cols), once),
        ]
        return call(functools.partial(kv_kernel, kv_heads), "keys_values", (1,), ins, outs, keep=keep)

    normed, kv_p, k_lin_p = keys_values(0, gain_one_s)
    normed, kv_c, k_lin_c = keys_values(1, after(gain_one_s, kv_p), normed)
    w_q, _ = gather_rows(q_one, ((w_kv,), (kv_p,), (kv_c,)))
    mine = lambda f: (f, 0)
    q, q_lin = call(
        functools.partial(q_kernel, heads), "queries", (2,),
        [
            (normed, (rows, model), mine), (w_q, (model, q_cols), lambda f: (0, 0)),
            (gain_q, (1, HEAD_SIZE), lambda f: (0, 0)),
            (cos, (rows, HEAD_SIZE), mine), (sin, (rows, HEAD_SIZE), mine),
        ],
        [(shaped((2 * rows, q_cols), BF), (rows, q_cols), mine), (shaped((2 * rows, q_cols), F32), (rows, q_cols), mine)],
    )

    def pick(source, wanted):
        return {s: source[s] for s in source if s in wanted}

    near, middle, far = (0, 1), (2, 3, 4, 5), tuple(range(6, ctx_size))
    slots, halos = {0: kv_p}, {0: kv_c}
    odd = (me % 2) == 1
    if ctx_size == 8:
        slots[1], slots[2], slots[4] = (swap(kv_p, "ctx", bit) for bit in (1, 2, 4))
    else:
        both, bit = kv_p[None], 1
        while bit < ctx_size:
            both = jnp.concatenate([both, swap(both, "ctx", bit)])
            bit *= 2
        slots = {s: both[s] for s in range(ctx_size)}
        halos.update({d: shift(kv_c, d) for d in range(1, n_halo)})
    ready = ()
    if ctx_size == 8:
        slots[2], slots[4] = after(slots[2], q), after(slots[4], q)
        far_k, far_v = swap(slots[4][0], "ctx", 2), swap(slots[2][1], "ctx", 4)
        slots[3], slots[5] = swap(slots[2], "ctx", 1), swap(slots[4], "ctx", 1)
        halos[2] = shift(after(kv_c, slots[2]), 2)
        ready = (slots[2], slots[4])
    c_state = attention_forward(
        (1,), after(scalars, *ready), q, low_col, pick(slots, near), pick(halos, (0,))
    )
    if ctx_size == 8:
        slots[6] = jnp.stack([after(far_k, c_state[0]), after(far_v, c_state[0])])
        slots[7] = swap(slots[6], "ctx", 1)
        ready = (slots[7],)
    attended, lse_p = attention_forward(
        (0,), after(scalars, c_state[0], *ready), q, low_col, slots, {}, None, (None,)
    )
    part_p = out_projection(0, attended, w_rest)
    got_p = swap(part_p, "tensor", 1)
    if ctx_size == 8:
        halos[1] = swap(jnp.where(odd, after(halos[2], part_p), kv_c), "ctx", 1)
    attended, lse_c = attention_forward(
        (1,), after(scalars, part_p), q, low_col, pick(slots, middle + far), pick(halos, range(1, n_halo)),
        c_state, (attended,),
    )
    part_c = out_projection(1, attended, w_rest)
    got_c = swap(part_c, "tensor", 1)

    resid_p, *whole, out_p, back_p = feed_forward(
        0, tokens, part_p, got_p, after(gain_two, part_c), cotangent, w_rest, o_cols, chunk
    )
    back_got_p = swap(back_p, "tensor", 1)
    resid_c, *whole, out_c, back_c = feed_forward(
        1, tokens, part_c, got_c, after(gain_two, back_p), cotangent, w_rest, o_cols, chunk, whole
    )
    back_got_c = swap(back_c, "tensor", 1)
    normed_ffn, hidden, d_gu = whole
    width = o_cols + 3 * units
    rest_grads = weight_grad(normed_ffn, d_gu, o_cols, width, min(1024, o_cols))
    rest_grads = weight_grad(cotangent, hidden, o_cols + 2 * units, width, chunk, rest_grads)
    d_resid_p, d_mixed, d_att_p, delta_p, d_two_p = mixed_back(
        0, back_p, back_got_p, resid_p, after(gain_two, rest_grads), cotangent, w_rest, o_cols, attended
    )
    out_p, out_c = after(out_p, back_got_c), after(out_c, back_got_c)
    out_got_p, out_got_c = swap(out_p, "tensor", 1), swap(out_c, "tensor", 1)

    of_rows = [(d_att_p, lse_p, delta_p)]

    def back_rows(half, deps, slots, halos, carry, prior=None, whole=None, last=False):
        do, lse, delta = of_rows[half]
        return attention_backward(
            half, after(scalars, *deps), q, do, lse, delta, low_row, slots, halos, carry, prior, last, whole
        )

    dq_p, prior, _ = back_rows(0, (d_att_p,), pick(slots, far), {}, None)
    d_resid_c, d_mixed, d_att_c, delta_c, d_two_c = mixed_back(
        1, back_c, back_got_c, resid_c, after(gain_two, dq_p), cotangent, w_rest, o_cols, attended, d_mixed
    )
    of_rows.append((d_att_c, lse_c, delta_c))
    rest_grads = weight_grad(d_mixed, attended, 0, width, min(1024, o_cols), rest_grads)
    rest_share = lax.psum_scatter(rest_grads, weight_axes, scatter_dimension=0, tiled=True)
    dq_c, _, g_halo = back_rows(1, (rest_grads,), {}, halos, None)
    if ctx_size == 8:
        near_one = swap(g_halo[1], "ctx", 1)
    dq_c, g, _ = back_rows(1, (dq_c,), pick(slots, far), {}, dq_c, prior)
    zero = jnp.zeros((), BF)
    ready = ()
    if ctx_size == 8:
        got7 = swap(g[7], "ctx", 1)
        near_one = after(near_one, dq_c)
        two_back = add_low(g_halo[2], jnp.where(odd, near_one, zero))
        halo_two = shift(two_back, -2)
        halo_near = jnp.where(odd, zero, near_one)
        ready = (two_back, halo_near)
    dq, prior, _ = back_rows(0, (dq_c, *ready), pick(slots, near + middle), {}, dq_p, None, None, True)
    if ctx_size == 8:
        g6 = add_low(g[6], after(got7, dq))
        far_k, far_v = swap(g6[0], "ctx", 2), swap(g6[1], "ctx", 4)
        ready = (g6, halo_two)
    dq_c, more, _ = back_rows(1, (dq, *ready), pick(slots, middle), {}, dq_c, prior)
    g.update(more)
    if ctx_size == 8:
        got3, got5 = swap(g[3], "ctx", 1), swap(g[5], "ctx", 1)
    dq, more, _ = back_rows(1, (dq_c, out_got_p, out_got_c), pick(slots, near), {}, dq_c, prior, dq, True)
    g.update(more)
    if ctx_size == 8:
        got1 = swap(g[1], "ctx", 1)
        far_k, far_v, got3, got5 = (after(v, dq) for v in (far_k, far_v, got3, got5))
        to_x, to_y = merge(g[2], got3, g[4], got5, far_k, far_v)
        ready = (to_x,)
        keys_p = values_p = [g[0], got1, swap(to_x, "ctx", 2), swap(to_y, "ctx", 4)]
        keys_c = values_c = [g_halo[0], halo_near, halo_two]
    else:
        both = jnp.stack([g[s] for s in range(ctx_size)])
        while both.shape[0] > 1:
            size = both.shape[0] // 2
            both = add_low(both[:size], swap(both[size:], "ctx", size))
        keys_p = values_p = [both[0]]
        keys_c = values_c = [g_halo[0]] + [shift(g_halo[d], -d) for d in range(1, n_halo)]

    d_q, q_part, q_heads = q_back(dq, q_lin, after(gain_q, dq, *ready), cos, sin, w_q)
    d_kv, into_c, k_heads_c = kv_back(
        1, keys_c, values_c, k_lin_c, after(gain_k, q_part), cos, sin, w_kv, to_slots, q_part
    )
    into_got_c = swap(into_c, "tensor", 1)
    q_high, q_low = weight_halves(normed, after(d_q, into_c))
    d_kv, into_p, k_heads_p = kv_back(
        0, keys_p, values_p, k_lin_p, after(gain_k, q_low), cos, sin, w_kv, to_slots, q_part, d_kv
    )
    into_got_p = swap(into_p, "tensor", 1)
    q_grad = scatter_rows(q_low, q_high, into_p)
    kv_high, kv_low = weight_halves(normed, after(d_kv, q_grad[0]))
    q_grad = scatter_more(q_grad, kv_low)
    heads = jnp.concatenate([q_heads, k_heads_c + k_heads_p], axis=1)
    heads_got = swap(heads, "tensor", 1)
    grad_tokens, d_one_c = tokens_back(1, into_c, into_got_c, tokens, after(gain_one, kv_low, q_grad[0]), d_resid_c)
    out_share, gate_share, up_share, down_share = unpack(chunk, o_cols, after(rest_share, d_one_c))
    q_grad = scatter_sum(q_grad, gate_share)
    kv_grad = scatter_rows(kv_low, kv_high, gate_share)
    layer_out = add_layer(0, after(resid_p, kv_grad[0], q_grad[0]), out_p, out_got_p)
    kv_grad = scatter_more(kv_grad, layer_out)
    layer_out = add_layer(1, after(resid_c, kv_grad[0]), out_c, out_got_c, layer_out)
    q_share = add_low(q_grad[0][:wide], after(q_grad[1], layer_out)).astype(F32)
    kv_grad = scatter_sum(kv_grad, layer_out)
    grad_tokens, d_one_p = tokens_back(
        0, into_p, into_got_p, tokens, after(gain_one, kv_grad[0], q_share), d_resid_p, grad_tokens
    )
    heads = heads + after(heads_got, d_one_p)
    late = jnp.concatenate([d_one_c + d_one_p, heads, d_two_c + d_two_p], axis=1)
    kv_share = add_low(kv_grad[0][:wide], after(kv_grad[1], d_one_p)).astype(F32)
    late = butterfly(late, ("ctx", "shard"), (d_one_p, kv_share))

    def own_gain(value, size):
        return lax.dynamic_index_in_dim(value.reshape(parts, size), part, 0, keepdims=False)

    return (
        layer_out,
        grad_tokens,
        own_gain(late[:, :model], wide),
        own_gain(late[:, model + 2 * HEAD_SIZE :], wide),
        own_gain(late[:, model : model + HEAD_SIZE], narrow),
        own_gain(late[:, model + HEAD_SIZE : model + 2 * HEAD_SIZE], narrow),
        q_share,
        kv_share[:, :k_cols],
        kv_share[:, k_cols:],
        out_share.T,
        gate_share,
        up_share,
        down_share.T,
    )


def solution(mesh):
    split = ("shard", "ctx")
    rows, gain = P(split, None), P(split)
    into, out_of = P(split, "tensor"), P("tensor", split)
    in_specs = (rows, P("shard", None)) + (gain,) * 4 + (into,) * 3 + (out_of,)
    in_specs += (into, into, out_of, rows)
    out_specs = (rows, rows) + (gain,) * 4 + (into,) * 3 + (out_of, into, into, out_of)
    return jax.shard_map(body, mesh=mesh, in_specs=in_specs, out_specs=out_specs, check_vma=False)
```

```python
import functools
import math

import jax
import jax.numpy as jnp
from jax import lax
from jax.experimental import pallas as pl
from jax.experimental.pallas import tpu as pltpu
from jax.sharding import PartitionSpec as P

HEAD_SIZE = 128
PROMPT = 4096
CONT_TOK = 4096
LONGEST = 1024

EPSILON = 1e-06
ROPE_BASE = 1000000.0
MASKED = -1e30
LOG2E = math.log2(math.e)
LN2 = math.log(2.0)
SCALE = 1.0 / math.sqrt(HEAD_SIZE)

BF = jnp.bfloat16
F32 = jnp.float32
NN = (((1,), (0,)), ((), ()))
NT = (((1,), (1,)), ((), ()))
TN = (((0,), (0,)), ((), ()))
MIB = 2**20
STATED = 3e9


def mm(left, right, dims=NN):
    return lax.dot_general(left, right, dims, preferred_element_type=F32)


def shaped(dims, kind):
    return jax.ShapeDtypeStruct(dims, kind)


def call(kernel, name, grid, ins, outs, scratch=(), vmem=56, scalars=None, keep=None, us=0):
    in_specs, arrays = [], []
    for array, block, index in ins:
        arrays.append(array)
        in_specs.append(pl.BlockSpec(memory_space=pl.ANY) if block is None else pl.BlockSpec(block, index))
    lead = 0 if scalars is None else 1
    return pl.pallas_call(
        kernel,
        grid_spec=pltpu.PrefetchScalarGridSpec(
            num_scalar_prefetch=lead,
            grid=grid,
            in_specs=in_specs,
            out_specs=[pl.BlockSpec(block, index) for _, block, index in outs],
            scratch_shapes=list(scratch),
        ),
        out_shape=[shape for shape, _, _ in outs],
        input_output_aliases={a + lead: b for a, b in (keep or {}).items()},
        compiler_params=pltpu.CompilerParams(vmem_limit_bytes=vmem * MIB),
        cost_estimate=pl.CostEstimate(flops=int(us * STATED), bytes_accessed=0, transcendentals=0),
        name=name,
    )(*([] if scalars is None else [scalars]), *arrays)


def rms(values):
    return lax.rsqrt(jnp.mean(values * values, axis=-1, keepdims=True) + EPSILON)


def turn(values, cos, sin):
    return values * cos + pltpu.roll(values, HEAD_SIZE // 2, 1) * sin


def turn_back(values, cos, sin):
    return values * cos - pltpu.roll(values, HEAD_SIZE // 2, 1) * sin


def kv_kernel(heads, x_ref, gain_ref, w_ref, hgain_ref, cos_ref, sin_ref, *refs):
    normed_ref, kv_ref, lin_ref = refs[-3:]
    x = x_ref[...].astype(F32)
    normed_ref[...] = (x * rms(x) * gain_ref[...]).astype(BF)
    both = mm(normed_ref[...], w_ref[...])
    width = heads * HEAD_SIZE
    kv_ref[1] = both[:, width:].astype(BF)
    for h in range(heads):
        cols = slice(h * HEAD_SIZE, (h + 1) * HEAD_SIZE)
        lin = both[:, cols]
        lin_ref[:, cols] = lin
        kv_ref[0, :, cols] = turn(lin * rms(lin) * hgain_ref[...], cos_ref[...], sin_ref[...]).astype(BF)


def q_kernel(heads, normed_ref, w_ref, hgain_ref, cos_ref, sin_ref, q_ref, lin_ref):
    both = mm(normed_ref[...], w_ref[...])
    for h in range(heads):
        cols = slice(h * HEAD_SIZE, (h + 1) * HEAD_SIZE)
        lin = both[:, cols]
        lin_ref[:, cols] = lin
        turned = turn(lin * rms(lin) * hgain_ref[...], cos_ref[...], sin_ref[...])
        q_ref[:, cols] = (turned * (SCALE * LOG2E)).astype(BF)


def pack_kernel(chunk, key_ref, value_ref, q_ref, out_ref, gate_ref, up_ref, down_ref, kv_ref, qo_ref, ffn_ref):
    k_cols, q_cols, units = key_ref.shape[1], q_ref.shape[1], gate_ref.shape[1]
    kv_ref[:, :k_cols] = key_ref[...]
    kv_ref[:, k_cols:] = value_ref[...]
    qo_ref[:, :q_cols] = q_ref[...]
    qo_ref[:, q_cols:] = out_ref[...]
    for at in range(0, units, chunk):
        ffn_ref[:, 2 * at : 2 * at + chunk] = gate_ref[:, at : at + chunk]
        ffn_ref[:, 2 * at + chunk : 2 * at + 2 * chunk] = up_ref[:, at : at + chunk]
    ffn_ref[:, 2 * units :] = down_ref[...]


def pack(chunk, *weights):
    cols = [w.shape[1] for w in weights]
    wide = weights[0].shape[0]
    whole = lambda f: (0, 0)
    ins = [(w, w.shape, whole) for w in weights]
    sums = (cols[0] + cols[1], cols[2] + cols[3], sum(cols[4:]))
    outs = [(shaped((wide, width), BF), (wide, width), whole) for width in sums]
    return call(functools.partial(pack_kernel, chunk), "pack", (1,), ins, outs)


def assemble_kernel(moves, wide, part_ref, *refs):
    pieces, out_ref, sems = refs[:-2], refs[-2], refs[-1]
    copies = []
    for at, (piece, row, first, slot, to, cols) in enumerate(moves):
        block = jnp.bitwise_xor(part_ref[0], slot)
        target = out_ref.at[pl.ds(pl.multiple_of(block * wide, wide), wide), pl.ds(to, cols)]
        source = pieces[piece].at[pl.ds(row, wide), pl.ds(first, cols)]
        copies.append(pltpu.make_async_copy(source, target, sems.at[at]))
    for copy in copies:
        copy.start()
    for copy in copies:
        copy.wait()


def assemble(part, wide, pieces, moves, shape):
    return pl.pallas_call(
        functools.partial(assemble_kernel, moves, wide),
        grid_spec=pltpu.PrefetchScalarGridSpec(
            num_scalar_prefetch=1,
            grid=(1,),
            in_specs=[pl.BlockSpec(memory_space=pl.ANY)] * len(pieces),
            out_specs=pl.BlockSpec(memory_space=pl.ANY),
            scratch_shapes=[pltpu.SemaphoreType.DMA((len(moves),))],
        ),
        out_shape=shaped(shape, BF),
        cost_estimate=pl.CostEstimate(flops=0, bytes_accessed=0, transcendentals=0),
        name="assemble",
    )(part[None], *pieces)


def by_top_bit(slots):
    groups = {}
    for at, s in enumerate(slots):
        if s:
            groups.setdefault(1 << (s.bit_length() - 1), []).append(at)
    return groups


def fwd_kernel(plan, idx_ref, lo_ref, *refs):
    halves, slots, halos = plan["halves"], plan["slots"], plan["halos"]
    refs = list(refs)
    q_refs = [refs.pop(0) for _ in halves]
    slot_refs = [refs.pop(0) for _ in slots]
    halo_refs = [refs.pop(0) for _ in halos]
    prior = [refs.pop(0) for _ in range(2 * len(halves))] if plan["carry"] else None
    if plan["last"]:
        if plan["alias"]:
            refs.pop(0)
        out_ref, lse_ref = refs[:2]
        refs = refs[2:]
    else:
        results, refs = refs[: 2 * len(halves)], refs[2 * len(halves) :]
    me, lo_first = idx_ref[0], idx_ref[1]
    rows = q_refs[0].shape[0]
    row = lax.broadcasted_iota(jnp.int32, (2 * rows, 1), 0)
    row = jnp.where(row >= rows, row - rows, row)
    col = lax.broadcasted_iota(jnp.int32, (1, rows), 1)
    for n, half in enumerate(halves):
        qs, acc, tot = refs[3 * n : 3 * n + 3]
        for g in range(2):
            cols, at = slice(g * HEAD_SIZE, (g + 1) * HEAD_SIZE), slice(g * rows, (g + 1) * rows)
            qs[at, :] = q_refs[n][:, cols]
            if prior is not None:
                acc[at, :] = prior[2 * n][:, cols]
                tot[at, :] = prior[2 * n + 1][:, cols]
        empty = [prior is None]

        def add(kv_ref, mask=None):
            scores = mm(qs[...], kv_ref[0], NT)
            if mask is not None:
                scores = jnp.where(mask, scores, MASKED)
            weights = jnp.exp2(scores)
            total = weights[:, :128]
            for at in range(128, weights.shape[1], 128):
                total = total + weights[:, at : at + 128]
            part = mm(weights.astype(BF), kv_ref[1])
            if empty[0]:
                acc[...] = part
                tot[...] = total
            else:
                acc[...] += part
                tot[...] += total
            empty[0] = False

        if half == 1:
            for kv_ref in slot_refs:
                add(kv_ref)
            low = jnp.concatenate([lo_ref[:, :1], lo_ref[:, :1]])
            for d, kv_ref in zip(halos, halo_refs):
                if d == 0:
                    add(kv_ref, (col <= row) & (col >= low))
                else:

                    @pl.when(lo_first < -(d - 1) * rows)
                    def _(d=d, kv_ref=kv_ref):
                        add(kv_ref, col - d * rows >= low)

        else:
            if 0 in slots:
                add(slot_refs[slots.index(0)], col <= row)
            for bit, group in by_top_bit(slots).items():

                @pl.when(jnp.bitwise_and(me, bit) != 0)
                def _(group=group):
                    for at in group:
                        add(slot_refs[at])

        if not plan["last"]:
            for g in range(2):
                cols, at = slice(g * HEAD_SIZE, (g + 1) * HEAD_SIZE), slice(g * rows, (g + 1) * rows)
                results[2 * n][:, cols] = acc[at, :]
                results[2 * n + 1][:, cols] = tot[at, :]
    if plan["last"]:
        qs, acc, tot = refs
        for g in range(2):
            cols, at = slice(g * HEAD_SIZE, (g + 1) * HEAD_SIZE), slice(g * rows, (g + 1) * rows)
            total = jnp.sum(tot[at, :], axis=1, keepdims=True)
            out_ref[:, cols] = (acc[at, :] / total).astype(BF)
            lse_ref[0, g : g + 1, :] = jnp.log2(jnp.sum(tot[at, :].T, axis=0, keepdims=True))


def attention_forward(halves, scalars, q, low, slots, halos, carry=None, last=None):
    rows, heads = q.shape[0] // 2, q.shape[1] // 256
    plan = dict(halves=halves, slots=list(slots), halos=list(halos), carry=carry is not None,
                last=last is not None, alias=last is not None and last[0] is not None)
    part = lambda h, i: (0, h)
    ins = [(low, (rows, 128), lambda h, i: (0, 0))]
    ins += [(q, (rows, 256), lambda h, i, half=half: (half, h)) for half in halves]
    for kv in list(slots.values()) + list(halos.values()):
        ins.append((kv, (2, rows, 128), lambda h, i: (0, 0, h)))
    if carry is not None:
        ins += [(c, (rows, 256), part) for c in carry]
    scratch, keep = [], {}
    for _ in halves:
        scratch += [pltpu.VMEM((2 * rows, 128), BF)] + [pltpu.VMEM((2 * rows, 128), F32)] * 2
    state = shaped((rows, heads * 256), F32)
    if last is None:
        outs = [(state, (rows, 256), part)] * (2 * len(halves))
    else:
        other = last[0]
        if other is not None:
            keep = {len(ins): 0}
            ins.append((other, None, None))
        half = halves[0]
        outs = [
            (shaped((2 * rows, heads * 256), BF), (rows, 256), lambda h, i: (half, h)),
            (shaped((heads, 8, rows), F32), (1, 8, rows), lambda h, i: (h, 0, 0)),
        ]
    return call(functools.partial(fwd_kernel, plan), "attend", (heads,), ins, outs, scratch,
                scalars=scalars, keep=keep)


def out_kernel(att_ref, w_ref, part_ref):
    part_ref[...] = mm(att_ref[...], w_ref[...], NT).astype(BF)


def out_projection(half, attended, w_out):
    rows, cols = attended.shape[0] // 2, attended.shape[1]
    model = w_out.shape[0]
    ins = [(attended, (rows, cols), lambda j: (half, 0)), (w_out, (model // 2, cols), lambda j: (j, 0))]
    outs = [(shaped((rows, model), BF), (rows, model // 2), lambda j: (0, j))]
    return call(out_kernel, "out_projection", (2,), ins, outs)[0]


def bwd_kernel(plan, idx_ref, q_ref, do_ref, lse_ref, delta_ref, lo_ref, *refs):
    half, slots, halos = plan["half"], plan["slots"], plan["halos"]
    refs = list(refs)
    slot_refs = [refs.pop(0) for _ in slots]
    halo_refs = [refs.pop(0) for _ in halos]
    prior_dq = refs.pop(0) if plan["carry"] else None
    prior = [refs.pop(0) for _ in slots] if plan["sum"] else None
    if plan["alias"]:
        refs.pop(0)
    dq_ref = refs.pop(0)
    slot_outs = [refs.pop(0) for _ in slots]
    halo_outs = [refs.pop(0) for _ in halos]
    qs, dos, lses, deltas, dq = refs
    me, lo_first = idx_ref[0], idx_ref[1]
    rows = q_ref.shape[0]
    for g in range(2):
        cols, at = slice(g * HEAD_SIZE, (g + 1) * HEAD_SIZE), slice(g * rows, (g + 1) * rows)
        qs[at, :] = q_ref[:, cols]
        dos[at, :] = do_ref[:, cols]
        lses[:, at] = lse_ref[0, g : g + 1, :]
        deltas[:, at] = delta_ref[0, g : g + 1, :]
    dq[...] = jnp.zeros_like(dq) if prior_dq is None else prior_dq[...]

    def block(kv_ref, out_ref, mask=None, before=None):
        keys = kv_ref[0]
        scores = mm(keys, qs[...], NT)
        dp = mm(kv_ref[1], dos[...], NT)
        scores = scores - lses[...]
        if mask is not None:
            scores = jnp.where(mask, scores, MASKED)
        probs = jnp.exp2(scores)
        ds = (probs * (dp - deltas[...])).astype(BF)
        dq[...] += mm(keys.T, ds)
        dk, dv = mm(ds, qs[...]) * LN2, mm(probs.astype(BF), dos[...])
        if before is not None:
            dk, dv = dk + before[0].astype(F32), dv + before[1].astype(F32)
        out_ref[0] = dk.astype(BF)
        out_ref[1] = dv.astype(BF)

    lane = lax.broadcasted_iota(jnp.int32, (1, 2 * rows), 1)
    lane = jnp.where(lane >= rows, lane - rows, lane)
    key = lax.broadcasted_iota(jnp.int32, (rows, 1), 0)

    def when(needed, kv_ref, out_ref, mask=None):
        @pl.when(needed)
        def _():
            block(kv_ref, out_ref, mask)

        @pl.when(jnp.logical_not(needed))
        def _():
            out_ref[...] = jnp.zeros_like(out_ref)

    low = lo_ref[:1, :]
    for d, kv_ref, out_ref in zip(halos, halo_refs, halo_outs):
        if d == 0:
            block(kv_ref, out_ref, (key <= lane) & (key >= low))
        else:
            when(lo_first < -(d - 1) * rows, kv_ref, out_ref, key - d * rows >= low)
    if half == 1:
        for at in range(len(slots)):
            block(slot_refs[at], slot_outs[at], None, prior[at] if prior else None)
    else:
        if 0 in slots:
            at = slots.index(0)
            block(slot_refs[at], slot_outs[at], key <= lane)
        for bit, group in by_top_bit(slots).items():

            @pl.when(jnp.bitwise_and(me, bit) != 0)
            def _(group=group):
                for at in group:
                    block(slot_refs[at], slot_outs[at])

            @pl.when(jnp.bitwise_and(me, bit) == 0)
            def _(group=group):
                for at in group:
                    slot_outs[at][...] = jnp.zeros_like(slot_outs[at])

    if plan["last"]:
        for g in range(2):
            cols = slice(g * HEAD_SIZE, (g + 1) * HEAD_SIZE)
            dq_ref[:, cols] = dq[:, g * rows : (g + 1) * rows].T * SCALE
    else:
        dq_ref[...] = dq[...]


def attention_backward(half, scalars, q, do, lse, delta, low, slots, halos, carry=None, prior=None, last=True, whole=None):
    rows, heads = q.shape[0] // 2, q.shape[1] // 256
    plan = dict(half=half, slots=list(slots), halos=list(halos), carry=carry is not None,
                sum=prior is not None, last=last, alias=whole is not None)
    part = lambda h, i: (0, h)
    stat = lambda h, i: (h, 0, 0)
    kv_map = lambda h, i: (0, 0, h)
    ins = [
        (q, (rows, 256), lambda h, i: (half, h)),
        (do, (rows, 256), part),
        (lse, (1, 8, rows), stat),
        (delta, (1, 8, rows), stat),
        (low, (8, 2 * rows), lambda h, i: (0, 0)),
    ]
    pieces = list(slots.values()) + list(halos.values())
    ins += [(kv, (2, rows, 128), kv_map) for kv in pieces]
    if carry is not None:
        ins.append((carry, (128, 2 * rows), lambda h, i: (h, 0)))
    if prior is not None:
        ins += [(prior[s], (2, rows, 128), kv_map) for s in slots]
    keep = {}
    if whole is not None:
        keep = {len(ins): 0}
        ins.append((whole, None, None))
    if last:
        outs = [(shaped((2 * rows, heads * 256), F32), (rows, 256), lambda h, i: (half, h))]
    else:
        outs = [(shaped((heads * 128, 2 * rows), F32), (128, 2 * rows), lambda h, i: (h, 0))]
    outs += [(shaped(kv.shape, BF), (2, rows, 128), kv_map) for kv in pieces]
    scratch = [
        pltpu.VMEM((2 * rows, 128), BF),
        pltpu.VMEM((2 * rows, 128), BF),
        pltpu.VMEM((1, 2 * rows), F32),
        pltpu.VMEM((1, 2 * rows), F32),
        pltpu.VMEM((128, 2 * rows), F32),
    ]
    us = 4 + 6 * len(slots) if half == 0 and carry is None else 0
    results = call(functools.partial(bwd_kernel, plan), "attend_back", (heads,), ins, outs, scratch,
                   scalars=scalars, us=us, keep=keep)
    n = len(slots)
    return results[0], dict(zip(slots, results[1 : 1 + n])), dict(zip(halos, results[1 + n :]))


def ffn_kernel(x_ref, own_ref, got_ref, gain_ref, dy_ref, gu_ref, down_ref, *refs):
    resid_ref, normed_ref, hidden_ref, dgu_ref, out_ref, back_ref, normed, out_acc, back_acc = refs[-9:]
    step, steps = pl.program_id(0), pl.num_programs(0)

    @pl.when(step == 0)
    def _():
        resid = x_ref[...].astype(F32) + (own_ref[...].astype(F32) + got_ref[...].astype(F32))
        resid_ref[...] = resid
        normed[...] = (resid * rms(resid) * gain_ref[...]).astype(BF)
        normed_ref[...] = normed[...]
        out_acc[...] = jnp.zeros_like(out_acc)
        back_acc[...] = jnp.zeros_like(back_acc)

    wide = down_ref.shape[1]
    both = mm(normed[...], gu_ref[...])
    d_hidden = mm(dy_ref[...], down_ref[...])
    gate, up = both[:, :wide], both[:, wide:]
    sig = 1.0 / (1.0 + jnp.exp(-gate))
    silu = gate * sig
    hidden = (silu * up).astype(BF)
    hidden_ref[...] = hidden
    d_up = (d_hidden * silu).astype(BF)
    d_gate = (d_hidden * up * (sig + silu * (1.0 - sig))).astype(BF)
    dgu_ref[:, :wide] = d_gate
    dgu_ref[:, wide:] = d_up
    out_acc[...] += mm(hidden, down_ref[...], NT)
    back_acc[...] += mm(dgu_ref[...], gu_ref[...], NT)

    @pl.when(step == steps - 1)
    def _():
        out_ref[...] = out_acc[...].astype(BF)
        back_ref[...] = back_acc[...].astype(BF)


def feed_forward(half, x, own, got, gain, dy, w_ffn, chunk, whole=None):
    rows, model = own.shape
    units = w_ffn.shape[1] // 3
    steps = units // chunk
    mine, once = lambda f: (half, 0), lambda f: (0, 0)
    at_down = 2 * units // chunk
    block = (rows, model)
    ins = [
        (x, block, mine), (own, block, once), (got, block, once), (gain, (1, model), once), (dy, block, mine),
        (w_ffn, (model, 2 * chunk), lambda f: (0, f)),
        (w_ffn, (model, chunk), lambda f: (0, at_down + f)),
    ]
    keep = {}
    if whole is not None:
        keep = {len(ins) + i: 1 + i for i in range(3)}
        ins += [(array, None, None) for array in whole]
    outs = [
        (shaped((rows, model), F32), block, once),
        (shaped((2 * rows, model), BF), block, mine),
        (shaped((2 * rows, units), BF), (rows, chunk), lambda f: (half, f)),
        (shaped((2 * rows, 2 * units), BF), (rows, 2 * chunk), lambda f: (half, f)),
        (shaped((rows, model), BF), block, once),
        (shaped((rows, model), BF), block, once),
    ]
    scratch = [pltpu.VMEM(block, BF), pltpu.VMEM(block, F32), pltpu.VMEM(block, F32)]
    return call(ffn_kernel, "feed_forward", (steps,), ins, outs, scratch, keep=keep)


def norm_back(grad, values, gain):
    scale = rms(values)
    unit = values * scale
    inner = grad * gain
    return scale * (inner - unit * jnp.mean(inner * unit, axis=-1, keepdims=True)), grad * unit


def lane_mean(values):
    width = values.shape[-1]
    ones = jnp.ones((width, width), BF)
    high = values.astype(BF)
    low = (values - high.astype(F32)).astype(BF)
    return (mm(high, ones) + mm(low, ones)) * (1.0 / width)


def head_norm_back(grad, values, gain):
    scale = lax.rsqrt(lane_mean(values * values) + EPSILON)
    unit = values * scale
    inner = grad * gain
    return scale * (inner - unit * lane_mean(inner * unit)), grad * unit


def row_blocks(rows):
    size = rows // 2 if rows % 512 == 0 else rows
    return size, rows // size


def add_up(ref, value):
    total = jnp.sum(value, axis=0, keepdims=True)

    @pl.when(pl.program_id(0) == 0)
    def _():
        ref[...] = total

    @pl.when(pl.program_id(0) > 0)
    def _():
        ref[...] += total


def mixed_kernel(heads, own_ref, got_ref, resid_ref, gain_ref, dy_ref, w_ref, att_ref, *refs):
    d_resid_ref, mixed_ref, datt_ref, delta_ref, dgain_ref = refs[-5:]
    grad = own_ref[...].astype(F32) + got_ref[...].astype(F32)
    d_norm, summand = norm_back(grad, resid_ref[...], gain_ref[...])
    add_up(dgain_ref, summand)
    d_resid = dy_ref[...].astype(F32) + d_norm
    d_resid_ref[...] = d_resid
    mixed_ref[...] = d_resid.astype(BF)
    datt_ref[...] = mm(mixed_ref[...], w_ref[...]).astype(BF)
    for h in range(heads):
        cols = slice(h * HEAD_SIZE, (h + 1) * HEAD_SIZE)
        product = datt_ref[:, cols].astype(F32) * att_ref[:, cols].astype(F32)
        delta_ref[h // 2, h % 2 : h % 2 + 1, :] = jnp.sum(product.T, axis=0, keepdims=True)


def mixed_back(half, own, got, resid, gain, dy, w_out, attended, whole=None):
    rows, model = own.shape
    o_cols = w_out.shape[1]
    heads = o_cols // HEAD_SIZE
    size, steps = row_blocks(rows)
    mine, here, once = lambda f: (half * steps + f, 0), lambda f: (f, 0), lambda f: (0, 0)
    block = (size, model)
    ins = [
        (own, block, here), (got, block, here), (resid, block, here), (gain, (1, model), once),
        (dy, block, mine), (w_out, (model, o_cols), once), (attended, (size, o_cols), mine),
    ]
    keep = {}
    if whole is not None:
        keep = {len(ins): 1}
        ins.append((whole, None, None))
    outs = [
        (shaped((rows, model), F32), block, here),
        (shaped((2 * rows, model), BF), block, mine),
        (shaped((rows, o_cols), BF), (size, o_cols), here),
        (shaped((heads // 2, 8, rows), F32), (heads // 2, 8, size), lambda f: (0, 0, f)),
        (shaped((1, model), F32), (1, model), once),
    ]
    return call(functools.partial(mixed_kernel, heads), "mixed_back", (steps,), ins, outs, keep=keep)


def merge_kernel(two, got3, four, got5, far_k, far_v, to_x, to_y):
    for which in range(2):
        by_x = two[which].astype(F32) + got3[which].astype(F32)
        by_y = four[which].astype(F32) + got5[which].astype(F32)
        to_x[which] = (by_x + far_v[...].astype(F32) if which else by_x).astype(BF)
        to_y[which] = (by_y if which else by_y + far_k[...].astype(F32)).astype(BF)


def merge(*pieces):
    rows, cols = pieces[-1].shape
    size, steps = row_blocks(rows)
    ins = []
    for piece in pieces:
        if piece.ndim == 3:
            ins.append((piece, (2, size, cols), lambda f: (0, f, 0)))
        else:
            ins.append((piece, (size, cols), lambda f: (f, 0)))
    outs = [(shaped((2, rows, cols), BF), (2, size, cols), lambda f: (0, f, 0))] * 2
    return call(merge_kernel, "merge", (steps,), ins, outs)


def weight_kernel(order, part_ref, left_ref, right_ref, *refs):
    low_ref, high_ref, total = refs[-3:]
    total[...] = mm(left_ref[...], right_ref[...], TN)
    wide = total.shape[0] // len(order)
    for at, slot in enumerate(order):
        block = jnp.bitwise_xor(part_ref[0], slot)
        piece = total[pl.ds(pl.multiple_of(block * wide, wide), wide), :].astype(BF)
        out_ref, row = (low_ref, at) if at < len(order) // 2 else (high_ref, at - len(order) // 2)
        out_ref[row * wide : (row + 1) * wide, :] = piece


def weight_grad(order, part, left, right, at, width, cols, whole=None):
    tokens, model = left.shape
    n = right.shape[1]
    ins = [(left, (tokens, model), lambda j, i: (0, 0)), (right, (tokens, cols), lambda j, i: (0, j))]
    keep = {}
    if whole is not None:
        keep = {len(ins): 0, len(ins) + 1: 1}
        ins += [(array, None, None) for array in whole]
    outs = [(shaped((model // 2, width), BF), (model // 2, cols), lambda j, i: (0, at // cols + j))] * 2
    return call(functools.partial(weight_kernel, order), "weight_grad", (n // cols,), ins, outs,
                [pltpu.VMEM((model, cols), F32)], scalars=part[None], keep=keep)


def weight_halves_kernel(left_ref, right_ref, high_ref, low_ref):
    for half, out_ref in enumerate((high_ref, low_ref)):

        @pl.when(pl.program_id(0) == half)
        def _(out_ref=out_ref):
            out_ref[...] = mm(left_ref[...], right_ref[...], TN).astype(BF)


def weight_halves(left, right):
    tokens, model = left.shape
    cols = right.shape[1]
    once = lambda i: (0, 0)
    ins = [(left, (tokens, model // 2), lambda i: (0, 1 - i)), (right, (tokens, cols), once)]
    half = shaped((model // 2, cols), BF)
    return call(weight_halves_kernel, "weight_halves", (2,), ins, [(half, half.shape, once)] * 2)


def q_back_kernel(heads, dq_ref, lin_ref, gain_ref, cos_ref, sin_ref, w_ref, *refs):
    d_ref, part_ref, gains_ref = refs[-3:]
    cos, sin = cos_ref[...], sin_ref[...]
    total = jnp.zeros(cos.shape, F32)
    for h in range(heads):
        cols = slice(h * HEAD_SIZE, (h + 1) * HEAD_SIZE)
        grad, summand = head_norm_back(turn_back(dq_ref[:, cols], cos, sin), lin_ref[:, cols], gain_ref[...])
        d_ref[:, cols] = grad.astype(BF)
        total = total + summand
    part_ref[...] = mm(d_ref[...], w_ref[...], NT)
    add_up(gains_ref, total)


def q_back(dq, lin, gain, cos, sin, w):
    rows, cols = dq.shape
    model = w.shape[0]
    size, steps = row_blocks(rows)
    here, once = lambda f: (f, 0), lambda f: (0, 0)
    ins = [
        (dq, (size, cols), here), (lin, (size, cols), here), (gain, (1, HEAD_SIZE), once),
        (cos, (size, HEAD_SIZE), here), (sin, (size, HEAD_SIZE), here), (w, (model, cols), once),
    ]
    outs = [
        (shaped((rows, cols), BF), (size, cols), here),
        (shaped((rows, model), F32), (size, model), here),
        (shaped((1, HEAD_SIZE), F32), (1, HEAD_SIZE), once),
    ]
    kernel = functools.partial(q_back_kernel, cols // HEAD_SIZE)
    return call(kernel, "q_back", (steps,), ins, outs)


def kv_back_kernel(heads, n_keys, n_values, lin_ref, gain_ref, cos_ref, sin_ref, w_ref, slots_ref, q_part_ref, *refs):
    key_refs, value_refs = refs[:n_keys], refs[n_keys : n_keys + n_values]
    d_ref, part_ref, gains_ref = refs[-3:]
    cos, sin = cos_ref[...], sin_ref[...]
    width = heads * HEAD_SIZE

    def total(sources, which, cols):
        value = None
        for ref in sources:
            piece = ref[which, :, cols] if len(ref.shape) == 3 else ref[:, cols]
            value = piece.astype(F32) if value is None else value + piece.astype(F32)
        return value

    gains = jnp.zeros(cos.shape, F32)
    for h in range(heads):
        cols = slice(h * HEAD_SIZE, (h + 1) * HEAD_SIZE)
        grad, summand = head_norm_back(
            turn_back(total(key_refs, 0, cols), cos, sin), lin_ref[:, cols], gain_ref[...]
        )
        d_ref[:, cols] = grad.astype(BF)
        gains = gains + summand
    d_ref[:, width:] = total(value_refs, 1, slice(None)).astype(BF)
    part = (q_part_ref[...] + mm(d_ref[...], w_ref[...], NT)).astype(BF)
    part_ref[...] = mm(part, slots_ref[...], NT).astype(BF)
    add_up(gains_ref, gains)


def kv_back(half, keys, values, lin, gain, cos, sin, w, to_slots, q_part, whole=None):
    rows, cols = lin.shape
    model = w.shape[0]
    size, steps = row_blocks(rows)
    mine, here, once = lambda f: (half * steps + f, 0), lambda f: (f, 0), lambda f: (0, 0)
    ins = [
        (lin, (size, cols), here), (gain, (1, HEAD_SIZE), once), (cos, (size, HEAD_SIZE), mine),
        (sin, (size, HEAD_SIZE), mine), (w, (model, 2 * cols), once),
        (to_slots, (model, model), once), (q_part, (size, model), mine),
    ]
    for piece in list(keys) + list(values):
        if piece.ndim == 3:
            ins.append((piece, (2, size, cols), lambda f: (0, f, 0)))
        else:
            ins.append((piece, (size, cols), here))
    keep = {}
    if whole is not None:
        keep = {len(ins): 0}
        ins.append((whole, None, None))
    outs = [
        (shaped((2 * rows, 2 * cols), BF), (size, 2 * cols), mine),
        (shaped((rows, model), BF), (size, model), here),
        (shaped((1, HEAD_SIZE), F32), (1, HEAD_SIZE), once),
    ]
    kernel = functools.partial(kv_back_kernel, cols // HEAD_SIZE, len(keys), len(values))
    return call(kernel, "kv_back", (steps,), ins, outs, keep=keep, us=3 * (1 - half))


def tokens_kernel(own_ref, got_ref, x_ref, gain_ref, d_resid_ref, *refs):
    out_ref, dgain_ref = refs[-2:]
    grad = own_ref[...].astype(F32) + got_ref[...].astype(F32)
    d_norm, summand = norm_back(grad, x_ref[...].astype(F32), gain_ref[...])
    add_up(dgain_ref, summand)
    out_ref[...] = (d_resid_ref[...] + d_norm).astype(BF)


def tokens_back(half, own, got, x, gain, d_resid, whole=None):
    rows, model = own.shape
    size, steps = row_blocks(rows)
    mine, here, once = lambda f: (half * steps + f, 0), lambda f: (f, 0), lambda f: (0, 0)
    block = (size, model)
    ins = [(own, block, here), (got, block, here), (x, block, mine), (gain, (1, model), once), (d_resid, block, here)]
    keep = {}
    if whole is not None:
        keep = {len(ins): 0}
        ins.append((whole, None, None))
    outs = [(shaped((2 * rows, model), BF), block, mine), (shaped((1, model), F32), (1, model), once)]
    return call(tokens_kernel, "tokens_back", (steps,), ins, outs, keep=keep, us=20)


def share_kernel(chunk, ffn_ref, ffn_got_ref, out_own_ref, out_got_ref, late_ref, out_ref, gate_ref, up_ref, down_ref):
    units = gate_ref.shape[1]
    out_ref[...] = out_own_ref[...].astype(F32) + out_got_ref[...].astype(F32)

    def total(at, cols):
        return ffn_ref[:, at : at + cols].astype(F32) + ffn_got_ref[:, at : at + cols].astype(F32)

    for at in range(0, units, chunk):
        gate_ref[:, at : at + chunk] = total(2 * at, chunk)
        up_ref[:, at : at + chunk] = total(2 * at + chunk, chunk)
    down_ref[...] = total(2 * units, units)


def unpack(chunk, ffn_grad, out_grad, late):
    wide, width = ffn_grad[1].shape
    o_cols, units = out_grad[1].shape[1], width // 3
    whole = lambda f: (0, 0)
    ins = [(array, (wide, array.shape[1]), whole) for array in (*ffn_grad, *out_grad)]
    ins.append((late, late.shape, whole))
    outs = [(shaped((wide, cols), F32), (wide, cols), whole) for cols in (o_cols, units, units, units)]
    return call(functools.partial(share_kernel, chunk), "unpack", (1,), ins, outs)


def layer_kernel(resid_ref, own_ref, got_ref, *refs):
    refs[-1][...] = (resid_ref[...] + (own_ref[...].astype(F32) + got_ref[...].astype(F32))).astype(BF)


def add_layer(half, resid, own, got, whole=None):
    rows, model = resid.shape
    size, steps = row_blocks(rows)
    here, mine = lambda f: (f, 0), lambda f: (half * steps + f, 0)
    ins = [(array, (size, model), here) for array in (resid, own, got)]
    keep = {}
    if whole is not None:
        keep = {len(ins): 0}
        ins.append((whole, None, None))
    outs = [(shaped((2 * rows, model), BF), (size, model), mine)]
    return call(layer_kernel, "add_layer", (steps,), ins, outs, keep=keep)[0]


def swap(value, axis, bit):
    size = lax.axis_size(axis)
    return lax.ppermute(value, axis, [(i, i ^ bit) for i in range(size)])


def shift(value, by):
    size = lax.axis_size("ctx")
    return lax.ppermute(value, "ctx", [(i, i + by) for i in range(size) if 0 <= i + by < size])


def add_low(left, right):
    return (left.astype(F32) + right.astype(F32)).astype(BF)


def butterfly(value, axes, gates=()):
    gates = list(gates)
    for axis in axes:
        bit = 1
        while bit < lax.axis_size(axis):
            got = swap(value, axis, bit)
            value = value + (after(got, gates.pop(0)) if gates else got)
            bit *= 2
    return value


def after(value, *others):
    return lax.optimization_barrier((value, *others))[0]


def rotary_tables(position):
    half_dim = HEAD_SIZE // 2
    inverse_freq = jnp.exp(jnp.arange(half_dim, dtype=F32) * (-math.log(ROPE_BASE) / half_dim))
    angles = position.astype(F32)[:, None] * inverse_freq[None, :]
    cosine, sine = jnp.cos(angles), jnp.sin(angles)
    return jnp.concatenate([cosine, cosine], axis=-1), jnp.concatenate([-sine, sine], axis=-1)


def body(
    tokens,
    cont_lengths,
    attn_gain,
    ffn_gain,
    query_gain,
    key_gain,
    w_query,
    key_weight,
    value_weight,
    w_out,
    w_gate,
    w_up,
    w_down,
    cotangent,
):
    ctx_size = lax.axis_size("ctx")
    weight_axes = ("shard", "ctx")
    parts = lax.axis_size("shard") * ctx_size
    me = lax.axis_index("ctx")
    part = lax.axis_index("shard") * ctx_size + me
    rows, model = tokens.shape[0] // 2, tokens.shape[1]
    n_halo = 1 + -(-(LONGEST - 1) // rows)
    lengths = cont_lengths[0]

    bits = [("shard", 1)] + [("ctx", 1 << i) for i in range(1, ctx_size.bit_length() - 1)] + [("ctx", 1)]
    order = [0]
    for axis, bit in bits:
        order += [j ^ (bit * ctx_size if axis == "shard" else bit) for j in order]
    wide, narrow = attn_gain.shape[0], query_gain.shape[0]
    q_cols, k_cols = w_query.shape[1], key_weight.shape[1]
    o_cols, units = w_out.shape[0], w_gate.shape[1]
    heads, kv_heads = q_cols // HEAD_SIZE, k_cols // HEAD_SIZE
    chunk = math.gcd(units, 512)

    def gather_first(piece, *gate):
        return jnp.concatenate([piece, after(swap(piece, "shard", 1), *gate)]) if ctx_size == 8 else piece

    def gather_near(one, *gate):
        if ctx_size != 8:
            for axis, bit in bits:
                one = jnp.concatenate([one, swap(one, axis, bit)])
            return [one]
        by_x, by_y = (after(v, *gate) for v in (swap(one, "ctx", 2), swap(one, "ctx", 4)))
        cut = one.shape[1] // 2
        return [one, by_x, by_y, swap(by_y[:, :cut], "ctx", 2), swap(by_x[:, cut:], "ctx", 4)]

    def gather_far(pieces, *gate):
        if ctx_size != 8:
            return pieces[0], pieces[0]
        *near, left, right = pieces
        far = jnp.concatenate([after(left, *gate), after(right, *gate)], axis=1)
        near = [*near, far]
        return jnp.concatenate(near + [after(swap(piece, "ctx", 1), *gate) for piece in near]), far

    def scatter_rows(low, high, late):
        total = add_low(low, after(swap(high, "ctx", 1), late))
        if ctx_size != 8:
            for axis, bit in bits[-2:0:-1]:
                size = total.shape[0] // 2
                total = add_low(total[:size], swap(total[size:], axis, bit))
            return (total,)
        size, cut = total.shape[0] // 4, total.shape[1] // 2
        own, by_x, by_y, far = (total[i * size : (i + 1) * size] for i in range(4))
        left, right = swap(far[:, :cut], "ctx", 2), swap(far[:, cut:], "ctx", 4)
        return own, by_x, by_y, left, right

    def scatter_more(stage, late):
        if ctx_size != 8:
            return stage
        own, by_x, by_y, left, right = stage
        left, right = after(left, late), after(right, late)
        cut = left.shape[1]
        by_x = jnp.concatenate([by_x[:, :cut], add_low(by_x[:, cut:], right)], axis=1)
        by_y = jnp.concatenate([add_low(by_y[:, :cut], left), by_y[:, cut:]], axis=1)
        return lax.optimization_barrier((own, by_x, by_y))[0], swap(by_x, "ctx", 2), swap(by_y, "ctx", 4)

    def scatter_sum(stage, late):
        total = stage[0].astype(F32)
        for piece in stage[1:]:
            total = total + after(piece, late).astype(F32)
        total, size = total.astype(BF), total.shape[0] // 2
        return total, swap(total[size:], "shard", 1)

    kv_piece, qo_piece, ffn_piece = pack(
        chunk, key_weight, value_weight, w_query, w_out.T, w_gate, w_up, w_down.T
    )
    kv_one = gather_first(kv_piece)
    kv_near = gather_near(kv_one)
    w_kv, kv_far = gather_far(kv_near)
    qo_one = gather_first(after(qo_piece, kv_one), kv_far)
    gains = jnp.concatenate([attn_gain, ffn_gain, query_gain, key_gain])[None]
    gains = jnp.where(jnp.arange(parts)[:, None] == part, gains, jnp.zeros((), BF))
    gains = gains + after(swap(gains, "ctx", 1), kv_piece)
    for at, (axis, bit) in enumerate(bits[:-1]):
        gains = gains + after(swap(gains, axis, bit), (kv_one, kv_near[min(1, len(kv_near) - 1)], kv_far)[min(at, 2)])
    gains = gains.astype(F32)
    gain_one = gains[:, :wide].reshape(1, -1)
    gain_two = gains[:, wide : 2 * wide].reshape(1, -1)
    gain_q = gains[:, 2 * wide : 2 * wide + narrow].reshape(1, -1)
    gain_k = gains[:, 2 * wide + narrow :].reshape(1, -1)
    source = jnp.bitwise_xor(part, jnp.array(order, jnp.int32))[:, None] * wide + jnp.arange(wide, dtype=jnp.int32)
    to_slots = (jnp.arange(model, dtype=jnp.int32)[:, None] == source.reshape(1, -1)).astype(BF)
    tokens_s = mm(after(tokens, qo_one), to_slots).astype(BF)
    gain_one_s = mm(gain_one.astype(BF), to_slots)

    cont_at = me * rows + jnp.arange(rows, dtype=jnp.int32)
    cont_ends = jnp.cumsum(lengths)
    starts = cont_ends - lengths
    seg = jnp.sum((cont_ends[None, :] <= cont_at[:, None]).astype(jnp.int32), axis=1)
    numbers = jnp.arange(lengths.shape[0], dtype=jnp.int32)
    first = jnp.sum(jnp.where(numbers[None, :] == seg[:, None], starts[None, :], 0), axis=1)
    position = jnp.concatenate([me * rows + jnp.arange(rows, dtype=jnp.int32), PROMPT + cont_at - first])
    low = first - me * rows
    low_col = jnp.broadcast_to(low[:, None], (rows, 128))
    low_row = jnp.broadcast_to(jnp.concatenate([low, low])[None, :], (8, 2 * rows))
    scalars = jnp.stack([me, low[0]])
    cos, sin = rotary_tables(position)

    once = lambda f: (0, 0)

    def keys_values(half, gain, whole=None):
        mine = lambda f: (half, 0)
        ins = [
            (tokens_s, (rows, model), mine), (gain, (1, model), once), (w_kv, (model, 2 * k_cols), once),
            (gain_k, (1, HEAD_SIZE), once), (cos, (rows, HEAD_SIZE), mine), (sin, (rows, HEAD_SIZE), mine),
        ]
        keep = {}
        if whole is not None:
            keep = {len(ins): 0}
            ins.append((whole, None, None))
        outs = [
            (shaped((2 * rows, model), BF), (rows, model), mine),
            (shaped((2, rows, k_cols), BF), (2, rows, k_cols), lambda f: (0, 0, 0)),
            (shaped((rows, k_cols), F32), (rows, k_cols), once),
        ]
        return call(functools.partial(kv_kernel, kv_heads), "keys_values", (1,), ins, outs, keep=keep)

    normed, kv_p, k_lin_p = keys_values(0, gain_one_s)
    qo_near = gather_near(qo_one, kv_p)
    normed, kv_c, k_lin_c = keys_values(1, after(gain_one_s, kv_p, *qo_near[1:3]), normed)
    w_qo, _ = gather_far(qo_near, kv_c)
    if ctx_size == 8:
        moves = [(0, i * wide, q_cols, slot, 0, o_cols) for i, slot in enumerate(order)]
        w_out_t = assemble(part, wide, [w_qo], moves, (model, o_cols))
    else:
        places = jnp.argsort(jnp.bitwise_xor(part, jnp.array(order, jnp.int32)))

        def to_places(rows):
            return jnp.take(rows.reshape(parts, wide, -1), places, axis=0).reshape(rows.shape)

        w_out_t = to_places(w_qo[:, q_cols:])
        w_ffn = to_places(gather_near(ffn_piece)[0])
    mine = lambda f: (f, 0)
    q, q_lin = call(
        functools.partial(q_kernel, heads), "queries", (2,),
        [
            (normed, (rows, model), mine), (w_qo, (model, q_cols), lambda f: (0, 0)),
            (gain_q, (1, HEAD_SIZE), lambda f: (0, 0)),
            (cos, (rows, HEAD_SIZE), mine), (sin, (rows, HEAD_SIZE), mine),
        ],
        [(shaped((2 * rows, q_cols), BF), (rows, q_cols), mine), (shaped((2 * rows, q_cols), F32), (rows, q_cols), mine)],
    )

    ffn_one = gather_first(after(ffn_piece, qo_one), q)

    def pick(source, wanted):
        return {s: source[s] for s in source if s in wanted}

    near, middle, far = (0, 1), (2, 3, 4, 5), tuple(range(6, ctx_size))
    slots, halos = {0: kv_p}, {0: kv_c}
    odd = (me % 2) == 1
    if ctx_size == 8:
        slots[1], slots[2], slots[4] = (swap(kv_p, "ctx", bit) for bit in (1, 2, 4))
    else:
        both, bit = kv_p[None], 1
        while bit < ctx_size:
            both = jnp.concatenate([both, swap(both, "ctx", bit)])
            bit *= 2
        slots = {s: both[s] for s in range(ctx_size)}
        halos.update({d: shift(kv_c, d) for d in range(1, n_halo)})
    ready = ()
    if ctx_size == 8:
        slots[2], slots[4] = after(slots[2], q), after(slots[4], q)
        far_k, far_v = swap(slots[4][0], "ctx", 2), swap(slots[2][1], "ctx", 4)
        slots[3], slots[5] = swap(slots[2], "ctx", 1), swap(slots[4], "ctx", 1)
        halos[2] = shift(after(kv_c, slots[2]), 2)
        ready = (slots[2], slots[4])
        ffn_x, ffn_y = (swap(after(ffn_one, slots[2]), "ctx", bit) for bit in (2, 4))
        ffn_core = [swap(ffn_one, "ctx", 1)]
    c_state = attention_forward(
        (1,), after(scalars, ffn_one, *ready), q, low_col, pick(slots, near), pick(halos, (0,))
    )
    if ctx_size == 8:
        slots[6] = jnp.stack([after(far_k, c_state[0]), after(far_v, c_state[0])])
        slots[7] = swap(slots[6], "ctx", 1)
        ready = (slots[7],)
    attended, lse_p = attention_forward(
        (0,), after(scalars, c_state[0], *ready), q, low_col, slots, {}, None, (None,)
    )
    part_p = out_projection(0, attended, after(w_out_t, attended))
    got_p = swap(part_p, "tensor", 1)
    if ctx_size == 8:
        halos[1] = swap(jnp.where(odd, after(halos[2], part_p), kv_c), "ctx", 1)
        cut = ffn_y.shape[1] // 2
        ffn_y = after(ffn_y, part_p)
        ffn_left = swap(ffn_y[:, :cut], "ctx", 2)
        ffn_core.append(swap(ffn_y, "ctx", 1))
    attended, lse_c = attention_forward(
        (1,), after(scalars, part_p), q, low_col, pick(slots, middle + far), pick(halos, range(1, n_halo)),
        c_state, (attended,),
    )
    part_c = out_projection(1, attended, after(w_out_t, attended, got_p))
    got_c = swap(part_c, "tensor", 1)
    if ctx_size == 8:
        ffn_x = after(ffn_x, part_c)
        ffn_right = swap(ffn_x[:, cut:], "ctx", 4)
        ffn_left = after(ffn_left, part_c)
        ffn_core += [swap(ffn_x, "ctx", 1), swap(ffn_left, "ctx", 1), swap(ffn_right, "ctx", 1)]
        near_pieces = [(ffn_one, 0, 0, 2 * cut), (ffn_y, 4, 0, 2 * cut), (ffn_x, 2, 0, 2 * cut)]
        near_pieces += [(ffn_left, 6, 0, cut), (ffn_right, 6, cut, cut)]
        moves = []
        for at, (_, slot, to, cols) in enumerate(near_pieces):
            for core in range(2):
                for shard in range(2):
                    moves.append((at + 5 * core, shard * wide, 0, slot + core + shard * ctx_size, to, cols))
        w_ffn = assemble(part, wide, [p[0] for p in near_pieces] + ffn_core, moves, (model, 3 * units))

    resid_p, *whole, out_p, back_p = feed_forward(
        0, tokens, part_p, got_p, after(gain_two, part_c), cotangent, w_ffn, chunk
    )
    back_got_p = swap(back_p, "tensor", 1)
    resid_c, *whole, out_c, back_c = feed_forward(
        1, tokens, part_c, got_c, after(gain_two, back_p), cotangent, w_ffn, chunk, whole
    )
    back_got_c = swap(back_c, "tensor", 1)
    normed_ffn, hidden, d_gu = whole
    ffn_grads = weight_grad(order, part, normed_ffn, d_gu, 0, 3 * units, 2 * chunk)
    ffn_low, ffn_high = weight_grad(
        order, part, after(cotangent, back_got_p), hidden, 2 * units, 3 * units, chunk, ffn_grads
    )
    d_resid_p, d_mixed, d_att_p, delta_p, d_two_p = mixed_back(
        0, back_p, back_got_p, resid_p, after(gain_two, ffn_low), cotangent, w_out_t, attended
    )
    out_p, out_c = after(out_p, back_got_c), after(out_c, back_got_c)
    out_got_p, out_got_c = swap(out_p, "tensor", 1), swap(out_c, "tensor", 1)

    of_rows = [(d_att_p, lse_p, delta_p)]

    def back_rows(half, deps, slots, halos, carry, prior=None, whole=None, last=False):
        do, lse, delta = of_rows[half]
        return attention_backward(
            half, after(scalars, *deps), q, do, lse, delta, low_row, slots, halos, carry, prior, last, whole
        )

    dq_p, prior, _ = back_rows(0, (d_att_p,), pick(slots, far), {}, None)
    ffn_grad = scatter_rows(ffn_low, ffn_high, dq_p)
    d_resid_c, d_mixed, d_att_c, delta_c, d_two_c = mixed_back(
        1, back_c, back_got_c, resid_c, after(gain_two, dq_p, ffn_grad[0]), cotangent, w_out_t, attended, d_mixed
    )
    of_rows.append((d_att_c, lse_c, delta_c))
    out_low, out_high = weight_grad(order, part, d_mixed, attended, 0, o_cols, o_cols)
    dq_c, _, g_halo = back_rows(1, (out_low, ffn_grad[0]), {}, halos, None)
    ffn_grad = scatter_more(ffn_grad, dq_c)
    out_grad = scatter_rows(out_low, out_high, dq_c)
    if ctx_size == 8:
        near_one = swap(g_halo[1], "ctx", 1)
    dq_c, g, _ = back_rows(1, (dq_c, ffn_grad[0], out_grad[0]), pick(slots, far), {}, dq_c, prior)
    out_grad = scatter_more(out_grad, dq_c)
    zero = jnp.zeros((), BF)
    ready = ()
    if ctx_size == 8:
        got7 = swap(g[7], "ctx", 1)
        near_one = after(near_one, dq_c)
        two_back = add_low(g_halo[2], jnp.where(odd, near_one, zero))
        halo_two = shift(two_back, -2)
        halo_near = jnp.where(odd, zero, near_one)
        ready = (two_back, halo_near)
    dq, prior, _ = back_rows(0, (dq_c, out_grad[0], *ready), pick(slots, near + middle), {}, dq_p, None, None, True)
    if ctx_size == 8:
        g6 = add_low(g[6], after(got7, dq))
        far_k, far_v = swap(g6[0], "ctx", 2), swap(g6[1], "ctx", 4)
        ready = (g6,)
    ffn_grad, out_grad = scatter_sum(ffn_grad, dq), scatter_sum(out_grad, dq)
    dq_c, more, _ = back_rows(1, (dq, ffn_grad[0], out_grad[0], *ready), pick(slots, middle), {}, dq_c, prior)
    g.update(more)
    if ctx_size == 8:
        got3, got5 = swap(g[3], "ctx", 1), swap(g[5], "ctx", 1)
        ready = (halo_two,)
    dq, more, _ = back_rows(1, (dq_c, out_got_p, out_got_c, *ready), pick(slots, near), {}, dq_c, prior, dq, True)
    g.update(more)
    if ctx_size == 8:
        got1 = swap(g[1], "ctx", 1)
        far_k, far_v, got3, got5 = (after(v, dq, ffn_grad[1], out_grad[1]) for v in (far_k, far_v, got3, got5))
        to_x, to_y = merge(g[2], got3, g[4], got5, far_k, far_v)
        ready = (to_x,)
        keys_p = values_p = [g[0], got1, swap(to_x, "ctx", 2), swap(to_y, "ctx", 4)]
        keys_c = values_c = [g_halo[0], halo_near, halo_two]
    else:
        both = jnp.stack([g[s] for s in range(ctx_size)])
        while both.shape[0] > 1:
            size = both.shape[0] // 2
            both = add_low(both[:size], swap(both[size:], "ctx", size))
        keys_p = values_p = [both[0]]
        keys_c = values_c = [g_halo[0]] + [shift(g_halo[d], -d) for d in range(1, n_halo)]

    d_q, q_part, q_heads = q_back(dq, q_lin, after(gain_q, dq, *ready), cos, sin, w_qo)
    d_kv, into_c, k_heads_c = kv_back(
        1, keys_c, values_c, k_lin_c, after(gain_k, q_part), cos, sin, w_kv, to_slots, q_part
    )
    into_got_c = swap(into_c, "tensor", 1)
    q_high, q_low = weight_halves(normed, after(d_q, into_c))
    d_kv, into_p, k_heads_p = kv_back(
        0, keys_p, values_p, k_lin_p, after(gain_k, q_low), cos, sin, w_kv, to_slots, q_part, d_kv
    )
    into_got_p = swap(into_p, "tensor", 1)
    q_grad = scatter_rows(q_low, q_high, into_p)
    kv_high, kv_low = weight_halves(normed, after(d_kv, q_grad[0]))
    q_grad = scatter_more(q_grad, kv_low)
    heads = jnp.concatenate([q_heads, k_heads_c + k_heads_p], axis=1)
    heads_got = swap(heads, "tensor", 1)
    grad_tokens, d_one_c = tokens_back(1, into_c, into_got_c, tokens, after(gain_one, kv_low, q_grad[0]), d_resid_c)
    out_share, gate_share, up_share, down_share = unpack(chunk, ffn_grad, out_grad, d_one_c)
    q_grad = scatter_sum(q_grad, gate_share)
    kv_grad = scatter_rows(kv_low, kv_high, gate_share)
    layer_out = add_layer(0, after(resid_p, kv_grad[0], q_grad[0]), out_p, out_got_p)
    kv_grad = scatter_more(kv_grad, layer_out)
    layer_out = add_layer(1, after(resid_c, kv_grad[0]), out_c, out_got_c, layer_out)
    q_share = add_low(q_grad[0][:wide], after(q_grad[1], layer_out)).astype(F32)
    kv_grad = scatter_sum(kv_grad, layer_out)
    grad_tokens, d_one_p = tokens_back(
        0, into_p, into_got_p, tokens, after(gain_one, kv_grad[0], q_share), d_resid_p, grad_tokens
    )
    heads = heads + after(heads_got, d_one_p)
    late = jnp.concatenate([d_one_c + d_one_p, heads, d_two_c + d_two_p], axis=1)
    kv_share = add_low(kv_grad[0][:wide], after(kv_grad[1], d_one_p)).astype(F32)
    late = butterfly(late, ("ctx", "shard"), (d_one_p, kv_share))

    def own_gain(value, size):
        return lax.dynamic_index_in_dim(value.reshape(parts, size), part, 0, keepdims=False)

    return (
        layer_out,
        grad_tokens,
        own_gain(late[:, :model], wide),
        own_gain(late[:, model + 2 * HEAD_SIZE :], wide),
        own_gain(late[:, model : model + HEAD_SIZE], narrow),
        own_gain(late[:, model + HEAD_SIZE : model + 2 * HEAD_SIZE], narrow),
        q_share,
        kv_share[:, :k_cols],
        kv_share[:, k_cols:],
        out_share.T,
        gate_share,
        up_share,
        down_share.T,
    )


def solution(mesh):
    split = ("shard", "ctx")
    rows, gain = P(split, None), P(split)
    into, out_of = P(split, "tensor"), P("tensor", split)
    in_specs = (rows, P("shard", None)) + (gain,) * 4 + (into,) * 3 + (out_of,)
    in_specs += (into, into, out_of, rows)
    out_specs = (rows, rows) + (gain,) * 4 + (into,) * 3 + (out_of, into, into, out_of)
    return jax.shard_map(body, mesh=mesh, in_specs=in_specs, out_specs=out_specs, check_vma=False)
```

```python
import functools
import math

import jax
import jax.numpy as jnp
from jax import lax
from jax.experimental import pallas as pl
from jax.experimental.pallas import tpu as pltpu
from jax.sharding import PartitionSpec as P

HEAD_SIZE = 128
PROMPT = 4096
CONT_TOK = 4096
LONGEST = 1024

EPSILON = 1e-06
ROPE_BASE = 1000000.0
MASKED = -1e30
LOG2E = math.log2(math.e)
LN2 = math.log(2.0)
SCALE = 1.0 / math.sqrt(HEAD_SIZE)

BF = jnp.bfloat16
F32 = jnp.float32
NN = (((1,), (0,)), ((), ()))
NT = (((1,), (1,)), ((), ()))
TN = (((0,), (0,)), ((), ()))
MIB = 2**20
STATED = 3e9


def mm(left, right, dims=NN):
    return lax.dot_general(left, right, dims, preferred_element_type=F32)


def shaped(dims, kind):
    return jax.ShapeDtypeStruct(dims, kind)


def call(kernel, name, grid, ins, outs, scratch=(), vmem=56, scalars=None, keep=None, us=0):
    in_specs, arrays = [], []
    for array, block, index in ins:
        arrays.append(array)
        in_specs.append(pl.BlockSpec(memory_space=pl.ANY) if block is None else pl.BlockSpec(block, index))
    lead = 0 if scalars is None else 1
    return pl.pallas_call(
        kernel,
        grid_spec=pltpu.PrefetchScalarGridSpec(
            num_scalar_prefetch=lead,
            grid=grid,
            in_specs=in_specs,
            out_specs=[pl.BlockSpec(block, index) for _, block, index in outs],
            scratch_shapes=list(scratch),
        ),
        out_shape=[shape for shape, _, _ in outs],
        input_output_aliases={a + lead: b for a, b in (keep or {}).items()},
        compiler_params=pltpu.CompilerParams(vmem_limit_bytes=vmem * MIB),
        cost_estimate=pl.CostEstimate(flops=int(us * STATED), bytes_accessed=0, transcendentals=0),
        name=name,
    )(*([] if scalars is None else [scalars]), *arrays)


def rms(values):
    return lax.rsqrt(jnp.mean(values * values, axis=-1, keepdims=True) + EPSILON)


def turn(values, cos, sin):
    return values * cos + pltpu.roll(values, HEAD_SIZE // 2, 1) * sin


def turn_back(values, cos, sin):
    return values * cos - pltpu.roll(values, HEAD_SIZE // 2, 1) * sin


def kv_kernel(heads, x_ref, gain_ref, w_ref, hgain_ref, cos_ref, sin_ref, *refs):
    normed_ref, kv_ref, lin_ref = refs[-3:]
    x = x_ref[...].astype(F32)
    normed_ref[...] = (x * rms(x) * gain_ref[...]).astype(BF)
    both = mm(normed_ref[...], w_ref[...])
    width = heads * HEAD_SIZE
    kv_ref[1] = both[:, width:].astype(BF)
    for h in range(heads):
        cols = slice(h * HEAD_SIZE, (h + 1) * HEAD_SIZE)
        lin = both[:, cols]
        lin_ref[:, cols] = lin
        kv_ref[0, :, cols] = turn(lin * rms(lin) * hgain_ref[...], cos_ref[...], sin_ref[...]).astype(BF)


def q_kernel(heads, normed_ref, w_ref, hgain_ref, cos_ref, sin_ref, q_ref, lin_ref):
    both = mm(normed_ref[...], w_ref[...])
    for h in range(heads):
        cols = slice(h * HEAD_SIZE, (h + 1) * HEAD_SIZE)
        lin = both[:, cols]
        lin_ref[:, cols] = lin
        turned = turn(lin * rms(lin) * hgain_ref[...], cos_ref[...], sin_ref[...])
        q_ref[:, cols] = (turned * (SCALE * LOG2E)).astype(BF)


def pack_kernel(chunk, key_ref, value_ref, out_ref, down_ref, gate_ref, up_ref, kv_ref, od_ref, gu_ref):
    k_cols, o_cols, units = key_ref.shape[1], out_ref.shape[1], gate_ref.shape[1]
    kv_ref[:, :k_cols] = key_ref[...]
    kv_ref[:, k_cols:] = value_ref[...]
    od_ref[:, :o_cols] = out_ref[...]
    od_ref[:, o_cols:] = down_ref[...]
    for at in range(0, units, chunk):
        gu_ref[:, 2 * at : 2 * at + chunk] = gate_ref[:, at : at + chunk]
        gu_ref[:, 2 * at + chunk : 2 * at + 2 * chunk] = up_ref[:, at : at + chunk]


def pack(chunk, *weights):
    cols = [w.shape[1] for w in weights]
    wide = weights[0].shape[0]
    whole = lambda f: (0, 0)
    ins = [(w, w.shape, whole) for w in weights]
    sums = (cols[0] + cols[1], cols[2] + cols[3], cols[4] + cols[5])
    outs = [(shaped((wide, width), BF), (wide, width), whole) for width in sums]
    return call(functools.partial(pack_kernel, chunk), "pack", (1,), ins, outs)


def by_top_bit(slots):
    groups = {}
    for at, s in enumerate(slots):
        if s:
            groups.setdefault(1 << (s.bit_length() - 1), []).append(at)
    return groups


def fwd_kernel(plan, idx_ref, lo_ref, *refs):
    halves, slots, halos = plan["halves"], plan["slots"], plan["halos"]
    refs = list(refs)
    q_refs = [refs.pop(0) for _ in halves]
    slot_refs = [refs.pop(0) for _ in slots]
    halo_refs = [refs.pop(0) for _ in halos]
    prior = [refs.pop(0) for _ in range(2 * len(halves))] if plan["carry"] else None
    if plan["last"]:
        if plan["alias"]:
            refs.pop(0)
        out_ref, lse_ref = refs[:2]
        refs = refs[2:]
    else:
        results, refs = refs[: 2 * len(halves)], refs[2 * len(halves) :]
    me, lo_first = idx_ref[0], idx_ref[1]
    rows = q_refs[0].shape[0]
    row = lax.broadcasted_iota(jnp.int32, (2 * rows, 1), 0)
    row = jnp.where(row >= rows, row - rows, row)
    col = lax.broadcasted_iota(jnp.int32, (1, rows), 1)
    for n, half in enumerate(halves):
        qs, acc, tot = refs[3 * n : 3 * n + 3]
        for g in range(2):
            cols, at = slice(g * HEAD_SIZE, (g + 1) * HEAD_SIZE), slice(g * rows, (g + 1) * rows)
            qs[at, :] = q_refs[n][:, cols]
            if prior is not None:
                acc[at, :] = prior[2 * n][:, cols]
                tot[at, :] = prior[2 * n + 1][:, cols]
        empty = [prior is None]

        def add(kv_ref, mask=None):
            scores = mm(qs[...], kv_ref[0], NT)
            if mask is not None:
                scores = jnp.where(mask, scores, MASKED)
            weights = jnp.exp2(scores)
            total = weights[:, :128]
            for at in range(128, weights.shape[1], 128):
                total = total + weights[:, at : at + 128]
            part = mm(weights.astype(BF), kv_ref[1])
            if empty[0]:
                acc[...] = part
                tot[...] = total
            else:
                acc[...] += part
                tot[...] += total
            empty[0] = False

        if half == 1:
            for kv_ref in slot_refs:
                add(kv_ref)
            low = jnp.concatenate([lo_ref[:, :1], lo_ref[:, :1]])
            for d, kv_ref in zip(halos, halo_refs):
                if d == 0:
                    add(kv_ref, (col <= row) & (col >= low))
                else:

                    @pl.when(lo_first < -(d - 1) * rows)
                    def _(d=d, kv_ref=kv_ref):
                        add(kv_ref, col - d * rows >= low)

        else:
            if 0 in slots:
                add(slot_refs[slots.index(0)], col <= row)
            for bit, group in by_top_bit(slots).items():

                @pl.when(jnp.bitwise_and(me, bit) != 0)
                def _(group=group):
                    for at in group:
                        add(slot_refs[at])

        if not plan["last"]:
            for g in range(2):
                cols, at = slice(g * HEAD_SIZE, (g + 1) * HEAD_SIZE), slice(g * rows, (g + 1) * rows)
                results[2 * n][:, cols] = acc[at, :]
                results[2 * n + 1][:, cols] = tot[at, :]
    if plan["last"]:
        qs, acc, tot = refs
        for g in range(2):
            cols, at = slice(g * HEAD_SIZE, (g + 1) * HEAD_SIZE), slice(g * rows, (g + 1) * rows)
            total = jnp.sum(tot[at, :], axis=1, keepdims=True)
            out_ref[:, cols] = (acc[at, :] / total).astype(BF)
            lse_ref[0, g : g + 1, :] = jnp.log2(jnp.sum(tot[at, :].T, axis=0, keepdims=True))


def attention_forward(halves, scalars, q, low, slots, halos, carry=None, last=None):
    rows, heads = q.shape[0] // 2, q.shape[1] // 256
    plan = dict(halves=halves, slots=list(slots), halos=list(halos), carry=carry is not None,
                last=last is not None, alias=last is not None and last[0] is not None)
    part = lambda h, i: (0, h)
    ins = [(low, (rows, 128), lambda h, i: (0, 0))]
    ins += [(q, (rows, 256), lambda h, i, half=half: (half, h)) for half in halves]
    for kv in list(slots.values()) + list(halos.values()):
        ins.append((kv, (2, rows, 128), lambda h, i: (0, 0, h)))
    if carry is not None:
        ins += [(c, (rows, 256), part) for c in carry]
    scratch, keep = [], {}
    for _ in halves:
        scratch += [pltpu.VMEM((2 * rows, 128), BF)] + [pltpu.VMEM((2 * rows, 128), F32)] * 2
    state = shaped((rows, heads * 256), F32)
    if last is None:
        outs = [(state, (rows, 256), part)] * (2 * len(halves))
    else:
        other = last[0]
        if other is not None:
            keep = {len(ins): 0}
            ins.append((other, None, None))
        half = halves[0]
        outs = [
            (shaped((2 * rows, heads * 256), BF), (rows, 256), lambda h, i: (half, h)),
            (shaped((heads, 8, rows), F32), (1, 8, rows), lambda h, i: (h, 0, 0)),
        ]
    return call(functools.partial(fwd_kernel, plan), "attend", (heads,), ins, outs, scratch,
                scalars=scalars, keep=keep)


def out_kernel(att_ref, w_ref, part_ref):
    part_ref[...] = mm(att_ref[...], w_ref[...], NT).astype(BF)


def out_projection(half, attended, w_rest):
    rows, cols = attended.shape[0] // 2, attended.shape[1]
    model = w_rest.shape[0]
    ins = [(attended, (rows, cols), lambda j: (half, 0)), (w_rest, (model // 2, cols), lambda j: (j, 0))]
    outs = [(shaped((rows, model), BF), (rows, model // 2), lambda j: (0, j))]
    return call(out_kernel, "out_projection", (2,), ins, outs)[0]


def bwd_kernel(plan, idx_ref, q_ref, do_ref, lse_ref, delta_ref, lo_ref, *refs):
    half, slots, halos = plan["half"], plan["slots"], plan["halos"]
    refs = list(refs)
    slot_refs = [refs.pop(0) for _ in slots]
    halo_refs = [refs.pop(0) for _ in halos]
    prior_dq = refs.pop(0) if plan["carry"] else None
    prior = [refs.pop(0) for _ in slots] if plan["sum"] else None
    if plan["alias"]:
        refs.pop(0)
    dq_ref = refs.pop(0)
    slot_outs = [refs.pop(0) for _ in slots]
    halo_outs = [refs.pop(0) for _ in halos]
    qs, dos, lses, deltas, dq = refs
    me, lo_first = idx_ref[0], idx_ref[1]
    rows = q_ref.shape[0]
    for g in range(2):
        cols, at = slice(g * HEAD_SIZE, (g + 1) * HEAD_SIZE), slice(g * rows, (g + 1) * rows)
        qs[at, :] = q_ref[:, cols]
        dos[at, :] = do_ref[:, cols]
        lses[:, at] = lse_ref[0, g : g + 1, :]
        deltas[:, at] = delta_ref[0, g : g + 1, :]
    dq[...] = jnp.zeros_like(dq) if prior_dq is None else prior_dq[...]

    def block(kv_ref, out_ref, mask=None, before=None):
        keys = kv_ref[0]
        scores = mm(keys, qs[...], NT)
        dp = mm(kv_ref[1], dos[...], NT)
        scores = scores - lses[...]
        if mask is not None:
            scores = jnp.where(mask, scores, MASKED)
        probs = jnp.exp2(scores)
        ds = (probs * (dp - deltas[...])).astype(BF)
        dq[...] += mm(keys.T, ds)
        dk, dv = mm(ds, qs[...]) * LN2, mm(probs.astype(BF), dos[...])
        if before is not None:
            dk, dv = dk + before[0].astype(F32), dv + before[1].astype(F32)
        out_ref[0] = dk.astype(BF)
        out_ref[1] = dv.astype(BF)

    lane = lax.broadcasted_iota(jnp.int32, (1, 2 * rows), 1)
    lane = jnp.where(lane >= rows, lane - rows, lane)
    key = lax.broadcasted_iota(jnp.int32, (rows, 1), 0)

    def when(needed, kv_ref, out_ref, mask=None):
        @pl.when(needed)
        def _():
            block(kv_ref, out_ref, mask)

        @pl.when(jnp.logical_not(needed))
        def _():
            out_ref[...] = jnp.zeros_like(out_ref)

    low = lo_ref[:1, :]
    for d, kv_ref, out_ref in zip(halos, halo_refs, halo_outs):
        if d == 0:
            block(kv_ref, out_ref, (key <= lane) & (key >= low))
        else:
            when(lo_first < -(d - 1) * rows, kv_ref, out_ref, key - d * rows >= low)
    if half == 1:
        for at in range(len(slots)):
            block(slot_refs[at], slot_outs[at], None, prior[at] if prior else None)
    else:
        if 0 in slots:
            at = slots.index(0)
            block(slot_refs[at], slot_outs[at], key <= lane)
        for bit, group in by_top_bit(slots).items():

            @pl.when(jnp.bitwise_and(me, bit) != 0)
            def _(group=group):
                for at in group:
                    block(slot_refs[at], slot_outs[at])

            @pl.when(jnp.bitwise_and(me, bit) == 0)
            def _(group=group):
                for at in group:
                    slot_outs[at][...] = jnp.zeros_like(slot_outs[at])

    if plan["last"]:
        for g in range(2):
            cols = slice(g * HEAD_SIZE, (g + 1) * HEAD_SIZE)
            dq_ref[:, cols] = dq[:, g * rows : (g + 1) * rows].T * SCALE
    else:
        dq_ref[...] = dq[...]


def attention_backward(half, scalars, q, do, lse, delta, low, slots, halos, carry=None, prior=None, last=True, whole=None):
    rows, heads = q.shape[0] // 2, q.shape[1] // 256
    plan = dict(half=half, slots=list(slots), halos=list(halos), carry=carry is not None,
                sum=prior is not None, last=last, alias=whole is not None)
    part = lambda h, i: (0, h)
    stat = lambda h, i: (h, 0, 0)
    kv_map = lambda h, i: (0, 0, h)
    ins = [
        (q, (rows, 256), lambda h, i: (half, h)),
        (do, (rows, 256), part),
        (lse, (1, 8, rows), stat),
        (delta, (1, 8, rows), stat),
        (low, (8, 2 * rows), lambda h, i: (0, 0)),
    ]
    pieces = list(slots.values()) + list(halos.values())
    ins += [(kv, (2, rows, 128), kv_map) for kv in pieces]
    if carry is not None:
        ins.append((carry, (128, 2 * rows), lambda h, i: (h, 0)))
    if prior is not None:
        ins += [(prior[s], (2, rows, 128), kv_map) for s in slots]
    keep = {}
    if whole is not None:
        keep = {len(ins): 0}
        ins.append((whole, None, None))
    if last:
        outs = [(shaped((2 * rows, heads * 256), F32), (rows, 256), lambda h, i: (half, h))]
    else:
        outs = [(shaped((heads * 128, 2 * rows), F32), (128, 2 * rows), lambda h, i: (h, 0))]
    outs += [(shaped(kv.shape, BF), (2, rows, 128), kv_map) for kv in pieces]
    scratch = [
        pltpu.VMEM((2 * rows, 128), BF),
        pltpu.VMEM((2 * rows, 128), BF),
        pltpu.VMEM((1, 2 * rows), F32),
        pltpu.VMEM((1, 2 * rows), F32),
        pltpu.VMEM((128, 2 * rows), F32),
    ]
    us = 4 + 6 * (len(slots) + len(halos)) if carry is not None or halos else 0
    results = call(functools.partial(bwd_kernel, plan), "attend_back", (heads,), ins, outs, scratch,
                   scalars=scalars, us=us, keep=keep)
    n = len(slots)
    return results[0], dict(zip(slots, results[1 : 1 + n])), dict(zip(halos, results[1 + n :]))


def ffn_kernel(x_ref, own_ref, got_ref, gain_ref, dy_ref, gu_ref, down_ref, *refs):
    resid_ref, normed_ref, hidden_ref, dgu_ref, out_ref, back_ref, normed, out_acc, back_acc = refs[-9:]
    step, steps = pl.program_id(0), pl.num_programs(0)

    @pl.when(step == 0)
    def _():
        resid = x_ref[...].astype(F32) + (own_ref[...].astype(F32) + got_ref[...].astype(F32))
        resid_ref[...] = resid
        normed[...] = (resid * rms(resid) * gain_ref[...]).astype(BF)
        normed_ref[...] = normed[...]
        out_acc[...] = jnp.zeros_like(out_acc)
        back_acc[...] = jnp.zeros_like(back_acc)

    wide = down_ref.shape[1]
    both = mm(normed[...], gu_ref[...])
    d_hidden = mm(dy_ref[...], down_ref[...])
    gate, up = both[:, :wide], both[:, wide:]
    sig = 1.0 / (1.0 + jnp.exp(-gate))
    silu = gate * sig
    hidden = (silu * up).astype(BF)
    hidden_ref[...] = hidden
    d_up = (d_hidden * silu).astype(BF)
    d_gate = (d_hidden * up * (sig + silu * (1.0 - sig))).astype(BF)
    dgu_ref[:, :wide] = d_gate
    dgu_ref[:, wide:] = d_up
    out_acc[...] += mm(hidden, down_ref[...], NT)
    back_acc[...] += mm(dgu_ref[...], gu_ref[...], NT)

    @pl.when(step == steps - 1)
    def _():
        out_ref[...] = out_acc[...].astype(BF)
        back_ref[...] = back_acc[...].astype(BF)


def feed_forward(half, x, own, got, gain, dy, w_od, w_gu, chunk, whole=None):
    rows, model = own.shape
    units = w_gu.shape[1] // 2
    steps = units // chunk
    mine, once = lambda f: (half, 0), lambda f: (0, 0)
    at_down = (w_od.shape[1] - units) // chunk
    block = (rows, model)
    ins = [
        (x, block, mine), (own, block, once), (got, block, once), (gain, (1, model), once), (dy, block, mine),
        (w_gu, (model, 2 * chunk), lambda f: (0, f)),
        (w_od, (model, chunk), lambda f: (0, at_down + f)),
    ]
    keep = {}
    if whole is not None:
        keep = {len(ins) + i: 1 + i for i in range(3)}
        ins += [(array, None, None) for array in whole]
    outs = [
        (shaped((rows, model), F32), block, once),
        (shaped((2 * rows, model), BF), block, mine),
        (shaped((2 * rows, units), BF), (rows, chunk), lambda f: (half, f)),
        (shaped((2 * rows, 2 * units), BF), (rows, 2 * chunk), lambda f: (half, f)),
        (shaped((rows, model), BF), block, once),
        (shaped((rows, model), BF), block, once),
    ]
    scratch = [pltpu.VMEM(block, BF), pltpu.VMEM(block, F32), pltpu.VMEM(block, F32)]
    return call(ffn_kernel, "feed_forward", (steps,), ins, outs, scratch, keep=keep)


def norm_back(grad, values, gain):
    scale = rms(values)
    unit = values * scale
    inner = grad * gain
    return scale * (inner - unit * jnp.mean(inner * unit, axis=-1, keepdims=True)), grad * unit


def lane_mean(values):
    width = values.shape[-1]
    ones = jnp.ones((width, width), BF)
    high = values.astype(BF)
    low = (values - high.astype(F32)).astype(BF)
    return (mm(high, ones) + mm(low, ones)) * (1.0 / width)


def head_norm_back(grad, values, gain):
    scale = lax.rsqrt(lane_mean(values * values) + EPSILON)
    unit = values * scale
    inner = grad * gain
    return scale * (inner - unit * lane_mean(inner * unit)), grad * unit


def row_blocks(rows):
    size = rows // 2 if rows % 512 == 0 else rows
    return size, rows // size


def add_up(ref, value):
    total = jnp.sum(value, axis=0, keepdims=True)

    @pl.when(pl.program_id(0) == 0)
    def _():
        ref[...] = total

    @pl.when(pl.program_id(0) > 0)
    def _():
        ref[...] += total


def mixed_kernel(heads, own_ref, got_ref, resid_ref, gain_ref, dy_ref, w_ref, att_ref, *refs):
    d_resid_ref, mixed_ref, datt_ref, delta_ref, dgain_ref = refs[-5:]
    grad = own_ref[...].astype(F32) + got_ref[...].astype(F32)
    d_norm, summand = norm_back(grad, resid_ref[...], gain_ref[...])
    add_up(dgain_ref, summand)
    d_resid = dy_ref[...].astype(F32) + d_norm
    d_resid_ref[...] = d_resid
    mixed_ref[...] = d_resid.astype(BF)
    datt_ref[...] = mm(mixed_ref[...], w_ref[...]).astype(BF)
    for h in range(heads):
        cols = slice(h * HEAD_SIZE, (h + 1) * HEAD_SIZE)
        product = datt_ref[:, cols].astype(F32) * att_ref[:, cols].astype(F32)
        delta_ref[h // 2, h % 2 : h % 2 + 1, :] = jnp.sum(product.T, axis=0, keepdims=True)


def mixed_back(half, own, got, resid, gain, dy, w_rest, o_cols, attended, whole=None):
    rows, model = own.shape
    heads = o_cols // HEAD_SIZE
    size, steps = row_blocks(rows)
    mine, here, once = lambda f: (half * steps + f, 0), lambda f: (f, 0), lambda f: (0, 0)
    block = (size, model)
    ins = [
        (own, block, here), (got, block, here), (resid, block, here), (gain, (1, model), once),
        (dy, block, mine), (w_rest, (model, o_cols), once), (attended, (size, o_cols), mine),
    ]
    keep = {}
    if whole is not None:
        keep = {len(ins): 1}
        ins.append((whole, None, None))
    outs = [
        (shaped((rows, model), F32), block, here),
        (shaped((2 * rows, model), BF), block, mine),
        (shaped((rows, o_cols), BF), (size, o_cols), here),
        (shaped((heads // 2, 8, rows), F32), (heads // 2, 8, size), lambda f: (0, 0, f)),
        (shaped((1, model), F32), (1, model), once),
    ]
    return call(functools.partial(mixed_kernel, heads), "mixed_back", (steps,), ins, outs, keep=keep)


def merge_kernel(two, got3, four, got5, far_k, far_v, to_x, to_y):
    for which in range(2):
        by_x = two[which].astype(F32) + got3[which].astype(F32)
        by_y = four[which].astype(F32) + got5[which].astype(F32)
        to_x[which] = (by_x + far_v[...].astype(F32) if which else by_x).astype(BF)
        to_y[which] = (by_y if which else by_y + far_k[...].astype(F32)).astype(BF)


def merge(*pieces):
    rows, cols = pieces[-1].shape
    size, steps = row_blocks(rows)
    ins = []
    for piece in pieces:
        if piece.ndim == 3:
            ins.append((piece, (2, size, cols), lambda f: (0, f, 0)))
        else:
            ins.append((piece, (size, cols), lambda f: (f, 0)))
    outs = [(shaped((2, rows, cols), BF), (2, size, cols), lambda f: (0, f, 0))] * 2
    return call(merge_kernel, "merge", (steps,), ins, outs)


def weight_kernel(left_ref, right_ref, *refs):
    refs[-1][...] = mm(left_ref[...], right_ref[...], TN).astype(BF)


def weight_grad(left, right, at, width, cols, whole=None):
    tokens, model = left.shape
    n = right.shape[1]
    ins = [(left, (tokens, model), lambda j: (0, 0)), (right, (tokens, cols), lambda j: (0, j))]
    keep = {}
    if whole is not None:
        keep = {len(ins): 0}
        ins.append((whole, None, None))
    outs = [(shaped((model, width), BF), (model, cols), lambda j: (0, at // cols + j))]
    return call(weight_kernel, "weight_grad", (n // cols,), ins, outs, keep=keep)[0]


def weight_halves_kernel(left_ref, right_ref, high_ref, low_ref):
    for half, out_ref in enumerate((high_ref, low_ref)):

        @pl.when(pl.program_id(0) == half)
        def _(out_ref=out_ref):
            out_ref[...] = mm(left_ref[...], right_ref[...], TN).astype(BF)


def weight_halves(left, right):
    tokens, model = left.shape
    cols = right.shape[1]
    once = lambda i: (0, 0)
    ins = [(left, (tokens, model // 2), lambda i: (0, 1 - i)), (right, (tokens, cols), once)]
    half = shaped((model // 2, cols), BF)
    return call(weight_halves_kernel, "weight_halves", (2,), ins, [(half, half.shape, once)] * 2)


def q_back_kernel(heads, dq_ref, lin_ref, gain_ref, cos_ref, sin_ref, w_ref, *refs):
    d_ref, part_ref, gains_ref = refs[-3:]
    cos, sin = cos_ref[...], sin_ref[...]
    total = jnp.zeros(cos.shape, F32)
    for h in range(heads):
        cols = slice(h * HEAD_SIZE, (h + 1) * HEAD_SIZE)
        grad, summand = head_norm_back(turn_back(dq_ref[:, cols], cos, sin), lin_ref[:, cols], gain_ref[...])
        d_ref[:, cols] = grad.astype(BF)
        total = total + summand
    part_ref[...] = mm(d_ref[...], w_ref[...], NT)
    add_up(gains_ref, total)


def q_back(dq, lin, gain, cos, sin, w):
    rows, cols = dq.shape
    model = w.shape[0]
    size, steps = row_blocks(rows)
    here, once = lambda f: (f, 0), lambda f: (0, 0)
    ins = [
        (dq, (size, cols), here), (lin, (size, cols), here), (gain, (1, HEAD_SIZE), once),
        (cos, (size, HEAD_SIZE), here), (sin, (size, HEAD_SIZE), here), (w, (model, cols), once),
    ]
    outs = [
        (shaped((rows, cols), BF), (size, cols), here),
        (shaped((rows, model), F32), (size, model), here),
        (shaped((1, HEAD_SIZE), F32), (1, HEAD_SIZE), once),
    ]
    kernel = functools.partial(q_back_kernel, cols // HEAD_SIZE)
    return call(kernel, "q_back", (steps,), ins, outs)


def kv_back_kernel(heads, n_keys, n_values, lin_ref, gain_ref, cos_ref, sin_ref, w_ref, slots_ref, q_part_ref, *refs):
    key_refs, value_refs = refs[:n_keys], refs[n_keys : n_keys + n_values]
    d_ref, part_ref, gains_ref = refs[-3:]
    cos, sin = cos_ref[...], sin_ref[...]
    width = heads * HEAD_SIZE

    def total(sources, which, cols):
        value = None
        for ref in sources:
            piece = ref[which, :, cols] if len(ref.shape) == 3 else ref[:, cols]
            value = piece.astype(F32) if value is None else value + piece.astype(F32)
        return value

    gains = jnp.zeros(cos.shape, F32)
    for h in range(heads):
        cols = slice(h * HEAD_SIZE, (h + 1) * HEAD_SIZE)
        grad, summand = head_norm_back(
            turn_back(total(key_refs, 0, cols), cos, sin), lin_ref[:, cols], gain_ref[...]
        )
        d_ref[:, cols] = grad.astype(BF)
        gains = gains + summand
    d_ref[:, width:] = total(value_refs, 1, slice(None)).astype(BF)
    part = (q_part_ref[...] + mm(d_ref[...], w_ref[...], NT)).astype(BF)
    part_ref[...] = mm(part, slots_ref[...], NT).astype(BF)
    add_up(gains_ref, gains)


def kv_back(half, keys, values, lin, gain, cos, sin, w, to_slots, q_part, whole=None):
    rows, cols = lin.shape
    model = w.shape[0]
    size, steps = row_blocks(rows)
    mine, here, once = lambda f: (half * steps + f, 0), lambda f: (f, 0), lambda f: (0, 0)
    ins = [
        (lin, (size, cols), here), (gain, (1, HEAD_SIZE), once), (cos, (size, HEAD_SIZE), mine),
        (sin, (size, HEAD_SIZE), mine), (w, (model, 2 * cols), once),
        (to_slots, (model, model), once), (q_part, (size, model), mine),
    ]
    for piece in list(keys) + list(values):
        if piece.ndim == 3:
            ins.append((piece, (2, size, cols), lambda f: (0, f, 0)))
        else:
            ins.append((piece, (size, cols), here))
    keep = {}
    if whole is not None:
        keep = {len(ins): 0}
        ins.append((whole, None, None))
    outs = [
        (shaped((2 * rows, 2 * cols), BF), (size, 2 * cols), mine),
        (shaped((rows, model), BF), (size, model), here),
        (shaped((1, HEAD_SIZE), F32), (1, HEAD_SIZE), once),
    ]
    kernel = functools.partial(kv_back_kernel, cols // HEAD_SIZE, len(keys), len(values))
    return call(kernel, "kv_back", (steps,), ins, outs, keep=keep, us=3 * (1 - half))


def tokens_kernel(own_ref, got_ref, x_ref, gain_ref, d_resid_ref, *refs):
    out_ref, dgain_ref = refs[-2:]
    grad = own_ref[...].astype(F32) + got_ref[...].astype(F32)
    d_norm, summand = norm_back(grad, x_ref[...].astype(F32), gain_ref[...])
    add_up(dgain_ref, summand)
    out_ref[...] = (d_resid_ref[...] + d_norm).astype(BF)


def tokens_back(half, own, got, x, gain, d_resid, whole=None):
    rows, model = own.shape
    size, steps = row_blocks(rows)
    mine, here, once = lambda f: (half * steps + f, 0), lambda f: (f, 0), lambda f: (0, 0)
    block = (size, model)
    ins = [(own, block, here), (got, block, here), (x, block, mine), (gain, (1, model), once), (d_resid, block, here)]
    keep = {}
    if whole is not None:
        keep = {len(ins): 0}
        ins.append((whole, None, None))
    outs = [(shaped((2 * rows, model), BF), block, mine), (shaped((1, model), F32), (1, model), once)]
    return call(tokens_kernel, "tokens_back", (steps,), ins, outs, keep=keep, us=20)


def share_kernel(chunk, share_ref, out_ref, gate_ref, up_ref, down_ref):
    o_cols, units = out_ref.shape[1], gate_ref.shape[1]
    out_ref[...] = share_ref[:, :o_cols].astype(F32)
    for at in range(0, units, chunk):
        to = o_cols + 2 * at
        gate_ref[:, at : at + chunk] = share_ref[:, to : to + chunk].astype(F32)
        up_ref[:, at : at + chunk] = share_ref[:, to + chunk : to + 2 * chunk].astype(F32)
    down_ref[...] = share_ref[:, o_cols + 2 * units :].astype(F32)


def unpack(chunk, o_cols, share):
    wide = share.shape[0]
    units = (share.shape[1] - o_cols) // 3
    whole = lambda f: (0, 0)
    outs = [(shaped((wide, cols), F32), (wide, cols), whole) for cols in (o_cols, units, units, units)]
    return call(functools.partial(share_kernel, chunk), "unpack", (1,), [(share, share.shape, whole)], outs)


def layer_kernel(resid_ref, own_ref, got_ref, *refs):
    refs[-1][...] = (resid_ref[...] + (own_ref[...].astype(F32) + got_ref[...].astype(F32))).astype(BF)


def add_layer(half, resid, own, got, whole=None):
    rows, model = resid.shape
    size, steps = row_blocks(rows)
    here, mine = lambda f: (f, 0), lambda f: (half * steps + f, 0)
    ins = [(array, (size, model), here) for array in (resid, own, got)]
    keep = {}
    if whole is not None:
        keep = {len(ins): 0}
        ins.append((whole, None, None))
    outs = [(shaped((2 * rows, model), BF), (size, model), mine)]
    return call(layer_kernel, "add_layer", (steps,), ins, outs, keep=keep)[0]


def swap(value, axis, bit):
    size = lax.axis_size(axis)
    return lax.ppermute(value, axis, [(i, i ^ bit) for i in range(size)])


def shift(value, by):
    size = lax.axis_size("ctx")
    return lax.ppermute(value, "ctx", [(i, i + by) for i in range(size) if 0 <= i + by < size])


def add_low(left, right):
    return (left.astype(F32) + right.astype(F32)).astype(BF)


def butterfly(value, axes, gates=()):
    gates = list(gates)
    for axis in axes:
        bit = 1
        while bit < lax.axis_size(axis):
            got = swap(value, axis, bit)
            value = value + (after(got, gates.pop(0)) if gates else got)
            bit *= 2
    return value


def after(value, *others):
    return lax.optimization_barrier((value, *others))[0]


def rotary_tables(position):
    half_dim = HEAD_SIZE // 2
    inverse_freq = jnp.exp(jnp.arange(half_dim, dtype=F32) * (-math.log(ROPE_BASE) / half_dim))
    angles = position.astype(F32)[:, None] * inverse_freq[None, :]
    cosine, sine = jnp.cos(angles), jnp.sin(angles)
    return jnp.concatenate([cosine, cosine], axis=-1), jnp.concatenate([-sine, sine], axis=-1)


def body(
    tokens,
    cont_lengths,
    attn_gain,
    ffn_gain,
    query_gain,
    key_gain,
    w_query,
    key_weight,
    value_weight,
    w_out,
    w_gate,
    w_up,
    w_down,
    cotangent,
):
    ctx_size = lax.axis_size("ctx")
    weight_axes = ("shard", "ctx")
    parts = lax.axis_size("shard") * ctx_size
    me = lax.axis_index("ctx")
    part = lax.axis_index("shard") * ctx_size + me
    rows, model = tokens.shape[0] // 2, tokens.shape[1]
    n_halo = 1 + -(-(LONGEST - 1) // rows)
    lengths = cont_lengths[0]

    bits = [("shard", 1)] + [("ctx", 1 << i) for i in range(1, ctx_size.bit_length() - 1)] + [("ctx", 1)]
    order = [0]
    for axis, bit in bits:
        order += [j ^ (bit * ctx_size if axis == "shard" else bit) for j in order]
    wide, narrow = attn_gain.shape[0], query_gain.shape[0]
    q_cols, k_cols = w_query.shape[1], key_weight.shape[1]
    o_cols, units = w_out.shape[0], w_gate.shape[1]
    heads, kv_heads = q_cols // HEAD_SIZE, k_cols // HEAD_SIZE
    chunk = math.gcd(units, 512)

    def gather_first(piece, *gate):
        return jnp.concatenate([piece, after(swap(piece, "shard", 1), *gate)]) if ctx_size == 8 else piece

    def gather_near(one, *gate):
        if ctx_size != 8:
            for axis, bit in bits:
                one = jnp.concatenate([one, swap(one, axis, bit)])
            return [one]
        by_x, by_y = (after(v, *gate) for v in (swap(one, "ctx", 2), swap(one, "ctx", 4)))
        cut = one.shape[1] // 2
        return [one, by_x, by_y, swap(by_y[:, :cut], "ctx", 2), swap(by_x[:, cut:], "ctx", 4)]

    def gather_far(pieces, *gate):
        if ctx_size != 8:
            return pieces[0], pieces[0]
        *near, left, right = pieces
        far = jnp.concatenate([after(left, *gate), after(right, *gate)], axis=1)
        near = [*near, far]
        return jnp.concatenate(near + [after(swap(piece, "ctx", 1), *gate) for piece in near]), far

    def scatter_rows(low, high, late):
        total = add_low(low, after(swap(high, "ctx", 1), late))
        if ctx_size != 8:
            for axis, bit in bits[-2:0:-1]:
                size = total.shape[0] // 2
                total = add_low(total[:size], swap(total[size:], axis, bit))
            return (total,)
        size, cut = total.shape[0] // 4, total.shape[1] // 2
        own, by_x, by_y, far = (total[i * size : (i + 1) * size] for i in range(4))
        left, right = swap(far[:, :cut], "ctx", 2), swap(far[:, cut:], "ctx", 4)
        return own, by_x, by_y, left, right

    def scatter_more(stage, late):
        if ctx_size != 8:
            return stage
        own, by_x, by_y, left, right = stage
        left, right = after(left, late), after(right, late)
        cut = left.shape[1]
        by_x = jnp.concatenate([by_x[:, :cut], add_low(by_x[:, cut:], right)], axis=1)
        by_y = jnp.concatenate([add_low(by_y[:, :cut], left), by_y[:, cut:]], axis=1)
        return lax.optimization_barrier((own, by_x, by_y))[0], swap(by_x, "ctx", 2), swap(by_y, "ctx", 4)

    def scatter_sum(stage, late):
        total = stage[0].astype(F32)
        for piece in stage[1:]:
            total = total + after(piece, late).astype(F32)
        total, size = total.astype(BF), total.shape[0] // 2
        return total, swap(total[size:], "shard", 1)

    kv_piece, od_piece, gu_piece = pack(
        chunk, key_weight, value_weight, w_out.T, w_down.T, w_gate, w_up
    )
    kv_one = gather_first(kv_piece)
    kv_near = gather_near(kv_one)
    w_kv, kv_far = gather_far(kv_near)
    q_one = gather_first(after(w_query, kv_one), kv_far)
    w_od = lax.all_gather(od_piece, weight_axes, axis=0, tiled=True)
    gains = jnp.concatenate([attn_gain, ffn_gain, query_gain, key_gain])[None]
    gains = jnp.where(jnp.arange(parts)[:, None] == part, gains, jnp.zeros((), BF))
    gains = gains + after(swap(gains, "ctx", 1), kv_piece)
    for at, (axis, bit) in enumerate(bits[:-1]):
        gains = gains + after(swap(gains, axis, bit), (kv_one, kv_near[min(1, len(kv_near) - 1)], kv_far)[min(at, 2)])
    gains = gains.astype(F32)
    gain_one = gains[:, :wide].reshape(1, -1)
    gain_two = gains[:, wide : 2 * wide].reshape(1, -1)
    gain_q = gains[:, 2 * wide : 2 * wide + narrow].reshape(1, -1)
    gain_k = gains[:, 2 * wide + narrow :].reshape(1, -1)
    source = jnp.bitwise_xor(part, jnp.array(order, jnp.int32))[:, None] * wide + jnp.arange(wide, dtype=jnp.int32)
    to_slots = (jnp.arange(model, dtype=jnp.int32)[:, None] == source.reshape(1, -1)).astype(BF)
    tokens_s = mm(after(tokens, q_one), to_slots).astype(BF)
    gain_one_s = mm(gain_one.astype(BF), to_slots)

    cont_at = me * rows + jnp.arange(rows, dtype=jnp.int32)
    cont_ends = jnp.cumsum(lengths)
    starts = cont_ends - lengths
    seg = jnp.sum((cont_ends[None, :] <= cont_at[:, None]).astype(jnp.int32), axis=1)
    numbers = jnp.arange(lengths.shape[0], dtype=jnp.int32)
    first = jnp.sum(jnp.where(numbers[None, :] == seg[:, None], starts[None, :], 0), axis=1)
    position = jnp.concatenate([me * rows + jnp.arange(rows, dtype=jnp.int32), PROMPT + cont_at - first])
    low = first - me * rows
    low_col = jnp.broadcast_to(low[:, None], (rows, 128))
    low_row = jnp.broadcast_to(jnp.concatenate([low, low])[None, :], (8, 2 * rows))
    scalars = jnp.stack([me, low[0]])
    cos, sin = rotary_tables(position)

    once = lambda f: (0, 0)

    def keys_values(half, gain, whole=None):
        mine = lambda f: (half, 0)
        ins = [
            (tokens_s, (rows, model), mine), (gain, (1, model), once), (w_kv, (model, 2 * k_cols), once),
            (gain_k, (1, HEAD_SIZE), once), (cos, (rows, HEAD_SIZE), mine), (sin, (rows, HEAD_SIZE), mine),
        ]
        keep = {}
        if whole is not None:
            keep = {len(ins): 0}
            ins.append((whole, None, None))
        outs = [
            (shaped((2 * rows, model), BF), (rows, model), mine),
            (shaped((2, rows, k_cols), BF), (2, rows, k_cols), lambda f: (0, 0, 0)),
            (shaped((rows, k_cols), F32), (rows, k_cols), once),
        ]
        return call(functools.partial(kv_kernel, kv_heads), "keys_values", (1,), ins, outs, keep=keep)

    q_near = gather_near(q_one, w_kv)
    normed, kv_p, k_lin_p = keys_values(0, after(gain_one_s, *q_near[1:]))
    normed, kv_c, k_lin_c = keys_values(1, after(gain_one_s, kv_p), normed)
    w_q, _ = gather_far(q_near, kv_c)
    mine = lambda f: (f, 0)
    q, q_lin = call(
        functools.partial(q_kernel, heads), "queries", (2,),
        [
            (normed, (rows, model), mine), (w_q, (model, q_cols), lambda f: (0, 0)),
            (gain_q, (1, HEAD_SIZE), lambda f: (0, 0)),
            (cos, (rows, HEAD_SIZE), mine), (sin, (rows, HEAD_SIZE), mine),
        ],
        [(shaped((2 * rows, q_cols), BF), (rows, q_cols), mine), (shaped((2 * rows, q_cols), F32), (rows, q_cols), mine)],
    )

    def pick(source, wanted):
        return {s: source[s] for s in source if s in wanted}

    near, middle, far = (0, 1), (2, 3, 4, 5), tuple(range(6, ctx_size))
    slots, halos = {0: kv_p}, {0: kv_c}
    odd = (me % 2) == 1
    if ctx_size == 8:
        slots[1], slots[2], slots[4] = (swap(kv_p, "ctx", bit) for bit in (1, 2, 4))
    else:
        both, bit = kv_p[None], 1
        while bit < ctx_size:
            both = jnp.concatenate([both, swap(both, "ctx", bit)])
            bit *= 2
        slots = {s: both[s] for s in range(ctx_size)}
        halos.update({d: shift(kv_c, d) for d in range(1, n_halo)})
    ready = ()
    if ctx_size == 8:
        slots[2], slots[4] = after(slots[2], q), after(slots[4], q)
        far_k, far_v = swap(slots[4][0], "ctx", 2), swap(slots[2][1], "ctx", 4)
        slots[3], slots[5] = swap(slots[2], "ctx", 1), swap(slots[4], "ctx", 1)
        halos[2] = shift(after(kv_c, slots[2]), 2)
        gu_piece = after(gu_piece, slots[2], slots[4])
        ready = (slots[2], slots[4])
    w_gu = lax.all_gather(after(gu_piece, w_od), weight_axes, axis=0, tiled=True)
    c_state = attention_forward(
        (1,), after(scalars, *ready), q, low_col, pick(slots, near), pick(halos, (0,))
    )
    if ctx_size == 8:
        slots[6] = jnp.stack([after(far_k, c_state[0]), after(far_v, c_state[0])])
        slots[7] = swap(slots[6], "ctx", 1)
        ready = (slots[7],)
    attended, lse_p = attention_forward(
        (0,), after(scalars, c_state[0], *ready), q, low_col, slots, {}, None, (None,)
    )
    part_p = out_projection(0, attended, w_od)
    got_p = swap(part_p, "tensor", 1)
    if ctx_size == 8:
        halos[1] = swap(jnp.where(odd, after(halos[2], part_p), kv_c), "ctx", 1)
    attended, lse_c = attention_forward(
        (1,), after(scalars, part_p), q, low_col, pick(slots, middle + far), pick(halos, range(1, n_halo)),
        c_state, (attended,),
    )
    part_c = out_projection(1, attended, w_od)
    got_c = swap(part_c, "tensor", 1)

    resid_p, *whole, out_p, back_p = feed_forward(
        0, tokens, part_p, got_p, after(gain_two, part_c), cotangent, w_od, w_gu, chunk
    )
    back_got_p = swap(back_p, "tensor", 1)
    resid_c, *whole, out_c, back_c = feed_forward(
        1, tokens, part_c, got_c, after(gain_two, back_p), cotangent, w_od, w_gu, chunk, whole
    )
    back_got_c = swap(back_c, "tensor", 1)
    normed_ffn, hidden, d_gu = whole
    width = o_cols + 3 * units
    rest_grads = weight_grad(normed_ffn, d_gu, o_cols, width, min(1024, o_cols))
    rest_grads = weight_grad(cotangent, hidden, o_cols + 2 * units, width, chunk, rest_grads)
    d_resid_p, d_mixed, d_att_p, delta_p, d_two_p = mixed_back(
        0, back_p, back_got_p, resid_p, after(gain_two, rest_grads), cotangent, w_od, o_cols, attended
    )
    out_p, out_c = after(out_p, back_got_c), after(out_c, back_got_c)
    out_got_p, out_got_c = swap(out_p, "tensor", 1), swap(out_c, "tensor", 1)

    of_rows = [(d_att_p, lse_p, delta_p)]

    def back_rows(half, deps, slots, halos, carry, prior=None, whole=None, last=False):
        do, lse, delta = of_rows[half]
        return attention_backward(
            half, after(scalars, *deps), q, do, lse, delta, low_row, slots, halos, carry, prior, last, whole
        )

    dq_p, prior, _ = back_rows(0, (d_att_p,), pick(slots, far), {}, None)
    d_resid_c, d_mixed, d_att_c, delta_c, d_two_c = mixed_back(
        1, back_c, back_got_c, resid_c, after(gain_two, dq_p), cotangent, w_od, o_cols, attended, d_mixed
    )
    of_rows.append((d_att_c, lse_c, delta_c))
    rest_grads = weight_grad(d_mixed, attended, 0, width, min(1024, o_cols), rest_grads)
    rest_share = lax.psum_scatter(rest_grads, weight_axes, scatter_dimension=0, tiled=True)
    dq_c, _, g_halo = back_rows(1, (rest_grads,), {}, halos, None)
    if ctx_size == 8:
        near_one = swap(g_halo[1], "ctx", 1)
    dq_c, g, _ = back_rows(1, (dq_c,), pick(slots, far), {}, dq_c, prior)
    zero = jnp.zeros((), BF)
    ready = ()
    if ctx_size == 8:
        got7 = swap(g[7], "ctx", 1)
        near_one = after(near_one, dq_c)
        two_back = add_low(g_halo[2], jnp.where(odd, near_one, zero))
        halo_two = shift(two_back, -2)
        halo_near = jnp.where(odd, zero, near_one)
        ready = (two_back, halo_near)
    dq, prior, _ = back_rows(0, (dq_c, *ready), pick(slots, near + middle), {}, dq_p, None, None, True)
    if ctx_size == 8:
        g6 = add_low(g[6], after(got7, dq))
        far_k, far_v = swap(g6[0], "ctx", 2), swap(g6[1], "ctx", 4)
        ready = (g6,)
    dq_c, more, _ = back_rows(1, (dq, *ready), pick(slots, middle), {}, dq_c, prior)
    g.update(more)
    if ctx_size == 8:
        got3, got5 = swap(g[3], "ctx", 1), swap(g[5], "ctx", 1)
        ready = (halo_two,)
    dq, more, _ = back_rows(1, (dq_c, out_got_p, out_got_c, *ready), pick(slots, near), {}, dq_c, prior, dq, True)
    g.update(more)
    if ctx_size == 8:
        got1 = swap(g[1], "ctx", 1)
        far_k, far_v, got3, got5 = (after(v, dq) for v in (far_k, far_v, got3, got5))
        to_x, to_y = merge(g[2], got3, g[4], got5, far_k, far_v)
        ready = (to_x,)
        keys_p = values_p = [g[0], got1, swap(to_x, "ctx", 2), swap(to_y, "ctx", 4)]
        keys_c = values_c = [g_halo[0], halo_near, halo_two]
    else:
        both = jnp.stack([g[s] for s in range(ctx_size)])
        while both.shape[0] > 1:
            size = both.shape[0] // 2
            both = add_low(both[:size], swap(both[size:], "ctx", size))
        keys_p = values_p = [both[0]]
        keys_c = values_c = [g_halo[0]] + [shift(g_halo[d], -d) for d in range(1, n_halo)]

    d_q, q_part, q_heads = q_back(dq, q_lin, after(gain_q, dq, *ready), cos, sin, w_q)
    d_kv, into_c, k_heads_c = kv_back(
        1, keys_c, values_c, k_lin_c, after(gain_k, q_part), cos, sin, w_kv, to_slots, q_part
    )
    into_got_c = swap(into_c, "tensor", 1)
    q_high, q_low = weight_halves(normed, after(d_q, into_c))
    d_kv, into_p, k_heads_p = kv_back(
        0, keys_p, values_p, k_lin_p, after(gain_k, q_low), cos, sin, w_kv, to_slots, q_part, d_kv
    )
    into_got_p = swap(into_p, "tensor", 1)
    q_grad = scatter_rows(q_low, q_high, into_p)
    kv_high, kv_low = weight_halves(normed, after(d_kv, q_grad[0]))
    q_grad = scatter_more(q_grad, kv_low)
    heads = jnp.concatenate([q_heads, k_heads_c + k_heads_p], axis=1)
    heads_got = swap(heads, "tensor", 1)
    grad_tokens, d_one_c = tokens_back(1, into_c, into_got_c, tokens, after(gain_one, kv_low, q_grad[0]), d_resid_c)
    out_share, gate_share, up_share, down_share = unpack(chunk, o_cols, after(rest_share, d_one_c))
    q_grad = scatter_sum(q_grad, gate_share)
    kv_grad = scatter_rows(kv_low, kv_high, gate_share)
    layer_out = add_layer(0, after(resid_p, kv_grad[0], q_grad[0]), out_p, out_got_p)
    kv_grad = scatter_more(kv_grad, layer_out)
    layer_out = add_layer(1, after(resid_c, kv_grad[0]), out_c, out_got_c, layer_out)
    q_share = add_low(q_grad[0][:wide], after(q_grad[1], layer_out)).astype(F32)
    kv_grad = scatter_sum(kv_grad, layer_out)
    grad_tokens, d_one_p = tokens_back(
        0, into_p, into_got_p, tokens, after(gain_one, kv_grad[0], q_share), d_resid_p, grad_tokens
    )
    heads = heads + after(heads_got, d_one_p)
    late = jnp.concatenate([d_one_c + d_one_p, heads, d_two_c + d_two_p], axis=1)
    kv_share = add_low(kv_grad[0][:wide], after(kv_grad[1], d_one_p)).astype(F32)
    late = butterfly(late, ("ctx", "shard"), (d_one_p, kv_share))

    def own_gain(value, size):
        return lax.dynamic_index_in_dim(value.reshape(parts, size), part, 0, keepdims=False)

    return (
        layer_out,
        grad_tokens,
        own_gain(late[:, :model], wide),
        own_gain(late[:, model + 2 * HEAD_SIZE :], wide),
        own_gain(late[:, model : model + HEAD_SIZE], narrow),
        own_gain(late[:, model + HEAD_SIZE : model + 2 * HEAD_SIZE], narrow),
        q_share,
        kv_share[:, :k_cols],
        kv_share[:, k_cols:],
        out_share.T,
        gate_share,
        up_share,
        down_share.T,
    )


def solution(mesh):
    split = ("shard", "ctx")
    rows, gain = P(split, None), P(split)
    into, out_of = P(split, "tensor"), P("tensor", split)
    in_specs = (rows, P("shard", None)) + (gain,) * 4 + (into,) * 3 + (out_of,)
    in_specs += (into, into, out_of, rows)
    out_specs = (rows, rows) + (gain,) * 4 + (into,) * 3 + (out_of, into, into, out_of)
    return jax.shard_map(body, mesh=mesh, in_specs=in_specs, out_specs=out_specs, check_vma=False)
```

```python
import functools
import math

import jax
import jax.numpy as jnp
from jax import lax
from jax.experimental import pallas as pl
from jax.experimental.pallas import tpu as pltpu
from jax.sharding import PartitionSpec as P

HEAD_SIZE = 128
PROMPT = 4096
CONT_TOK = 4096
LONGEST = 1024

EPSILON = 1e-06
ROPE_BASE = 1000000.0
MASKED = -1e30
LOG2E = math.log2(math.e)
LN2 = math.log(2.0)
SCALE = 1.0 / math.sqrt(HEAD_SIZE)

BF = jnp.bfloat16
F32 = jnp.float32
NN = (((1,), (0,)), ((), ()))
NT = (((1,), (1,)), ((), ()))
TN = (((0,), (0,)), ((), ()))
MIB = 2**20
STATED = 3e9


def mm(left, right, dims=NN):
    return lax.dot_general(left, right, dims, preferred_element_type=F32)


def shaped(dims, kind):
    return jax.ShapeDtypeStruct(dims, kind)


def call(kernel, name, grid, ins, outs, scratch=(), vmem=56, scalars=None, keep=None, us=0):
    in_specs, arrays = [], []
    for array, block, index in ins:
        arrays.append(array)
        in_specs.append(pl.BlockSpec(memory_space=pl.ANY) if block is None else pl.BlockSpec(block, index))
    lead = 0 if scalars is None else 1
    return pl.pallas_call(
        kernel,
        grid_spec=pltpu.PrefetchScalarGridSpec(
            num_scalar_prefetch=lead,
            grid=grid,
            in_specs=in_specs,
            out_specs=[pl.BlockSpec(block, index) for _, block, index in outs],
            scratch_shapes=list(scratch),
        ),
        out_shape=[shape for shape, _, _ in outs],
        input_output_aliases={a + lead: b for a, b in (keep or {}).items()},
        compiler_params=pltpu.CompilerParams(vmem_limit_bytes=vmem * MIB),
        cost_estimate=pl.CostEstimate(flops=int(us * STATED), bytes_accessed=0, transcendentals=0),
        name=name,
    )(*([] if scalars is None else [scalars]), *arrays)


def rms(values):
    return lax.rsqrt(jnp.mean(values * values, axis=-1, keepdims=True) + EPSILON)


def turn(values, cos, sin):
    return values * cos + pltpu.roll(values, HEAD_SIZE // 2, 1) * sin


def turn_back(values, cos, sin):
    return values * cos - pltpu.roll(values, HEAD_SIZE // 2, 1) * sin


def kv_kernel(heads, x_ref, gain_ref, w_ref, hgain_ref, cos_ref, sin_ref, *refs):
    normed_ref, kv_ref, lin_ref = refs[-3:]
    x = x_ref[...].astype(F32)
    normed_ref[...] = (x * rms(x) * gain_ref[...]).astype(BF)
    both = mm(normed_ref[...], w_ref[...])
    width = heads * HEAD_SIZE
    kv_ref[1] = both[:, width:].astype(BF)
    for h in range(heads):
        cols = slice(h * HEAD_SIZE, (h + 1) * HEAD_SIZE)
        lin = both[:, cols]
        lin_ref[:, cols] = lin
        kv_ref[0, :, cols] = turn(lin * rms(lin) * hgain_ref[...], cos_ref[...], sin_ref[...]).astype(BF)


def q_kernel(heads, normed_ref, w_ref, hgain_ref, cos_ref, sin_ref, *refs):
    q_ref, lin_ref = refs[-2:]
    both = mm(normed_ref[...], w_ref[...])
    for h in range(heads):
        cols = slice(h * HEAD_SIZE, (h + 1) * HEAD_SIZE)
        lin = both[:, cols]
        lin_ref[:, cols] = lin
        turned = turn(lin * rms(lin) * hgain_ref[...], cos_ref[...], sin_ref[...])
        q_ref[:, cols] = (turned * (SCALE * LOG2E)).astype(BF)


def pack_kernel(chunk, key_ref, value_ref, out_ref, down_ref, gate_ref, up_ref, kv_ref, od_ref, gu_ref):
    k_cols, o_cols, units = key_ref.shape[1], out_ref.shape[1], gate_ref.shape[1]
    kv_ref[:, :k_cols] = key_ref[...]
    kv_ref[:, k_cols:] = value_ref[...]
    od_ref[:, :o_cols] = out_ref[...]
    od_ref[:, o_cols:] = down_ref[...]
    for at in range(0, units, chunk):
        gu_ref[:, 2 * at : 2 * at + chunk] = gate_ref[:, at : at + chunk]
        gu_ref[:, 2 * at + chunk : 2 * at + 2 * chunk] = up_ref[:, at : at + chunk]


def pack(chunk, *weights):
    cols = [w.shape[1] for w in weights]
    wide = weights[0].shape[0]
    whole = lambda f: (0, 0)
    ins = [(w, w.shape, whole) for w in weights]
    sums = (cols[0] + cols[1], cols[2] + cols[3], cols[4] + cols[5])
    outs = [(shaped((wide, width), BF), (wide, width), whole) for width in sums]
    return call(functools.partial(pack_kernel, chunk), "pack", (1,), ins, outs)


def by_top_bit(slots):
    groups = {}
    for at, s in enumerate(slots):
        if s:
            groups.setdefault(1 << (s.bit_length() - 1), []).append(at)
    return groups


def slot_inputs(kv, rows):
    if isinstance(kv, tuple):
        return [(part, (rows, 128), lambda h, i: (0, h)) for part in kv]
    return [(kv, (2, rows, 128), lambda h, i: (0, 0, h))]


def take_slots(refs, pairs):
    taken = []
    for pair in pairs:
        if pair:
            taken.append((refs.pop(0), refs.pop(0)))
        else:
            ref = refs.pop(0)
            taken.append((ref.at[0], ref.at[1]))
    return taken


def fwd_kernel(plan, idx_ref, lo_ref, *refs):
    halves, slots, halos = plan["halves"], plan["slots"], plan["halos"]
    refs = list(refs)
    q_refs = [refs.pop(0) for _ in halves]
    slot_refs = take_slots(refs, plan["pairs"])
    halo_refs = take_slots(refs, [False] * len(halos))
    prior = [refs.pop(0) for _ in range(2 * len(halves))] if plan["carry"] else None
    if plan["last"]:
        if plan["alias"]:
            refs.pop(0)
        out_ref, lse_ref = refs[:2]
        refs = refs[2:]
    else:
        results, refs = refs[: 2 * len(halves)], refs[2 * len(halves) :]
    me, lo_first = idx_ref[0], idx_ref[1]
    rows = q_refs[0].shape[0]
    row = lax.broadcasted_iota(jnp.int32, (2 * rows, 1), 0)
    row = jnp.where(row >= rows, row - rows, row)
    col = lax.broadcasted_iota(jnp.int32, (1, rows), 1)
    for n, half in enumerate(halves):
        qs, acc, tot = refs[3 * n : 3 * n + 3]
        for g in range(2):
            cols, at = slice(g * HEAD_SIZE, (g + 1) * HEAD_SIZE), slice(g * rows, (g + 1) * rows)
            qs[at, :] = q_refs[n][:, cols]
            if prior is not None:
                acc[at, :] = prior[2 * n][:, cols]
                tot[at, :] = prior[2 * n + 1][:, cols]
        empty = [prior is None]

        def add(kv_ref, mask=None):
            scores = mm(qs[...], kv_ref[0][...], NT)
            if mask is not None:
                scores = jnp.where(mask, scores, MASKED)
            weights = jnp.exp2(scores)
            total = weights[:, :128]
            for at in range(128, weights.shape[1], 128):
                total = total + weights[:, at : at + 128]
            part = mm(weights.astype(BF), kv_ref[1][...])
            if empty[0]:
                acc[...] = part
                tot[...] = total
            else:
                acc[...] += part
                tot[...] += total
            empty[0] = False

        if half == 1:
            for kv_ref in slot_refs:
                add(kv_ref)
            low = jnp.concatenate([lo_ref[:, :1], lo_ref[:, :1]])
            for d, kv_ref in zip(halos, halo_refs):
                if d == 0:
                    add(kv_ref, (col <= row) & (col >= low))
                else:

                    @pl.when(lo_first < -(d - 1) * rows)
                    def _(d=d, kv_ref=kv_ref):
                        add(kv_ref, col - d * rows >= low)

        else:
            if 0 in slots:
                add(slot_refs[slots.index(0)], col <= row)
            for bit, group in by_top_bit(slots).items():

                @pl.when(jnp.bitwise_and(me, bit) != 0)
                def _(group=group):
                    for at in group:
                        add(slot_refs[at])

        if not plan["last"]:
            for g in range(2):
                cols, at = slice(g * HEAD_SIZE, (g + 1) * HEAD_SIZE), slice(g * rows, (g + 1) * rows)
                results[2 * n][:, cols] = acc[at, :]
                results[2 * n + 1][:, cols] = tot[at, :]
    if plan["last"]:
        qs, acc, tot = refs
        for g in range(2):
            cols, at = slice(g * HEAD_SIZE, (g + 1) * HEAD_SIZE), slice(g * rows, (g + 1) * rows)
            total = jnp.sum(tot[at, :], axis=1, keepdims=True)
            out_ref[:, cols] = (acc[at, :] / total).astype(BF)
            lse_ref[0, g : g + 1, :] = jnp.log2(jnp.sum(tot[at, :].T, axis=0, keepdims=True))


def attention_forward(halves, scalars, q, low, slots, halos, carry=None, last=None):
    rows, heads = q[0].shape[0], q[0].shape[1] // 256
    plan = dict(halves=halves, slots=list(slots), pairs=[isinstance(kv, tuple) for kv in slots.values()], halos=list(halos), carry=carry is not None,
                last=last is not None, alias=last is not None and last[0] is not None)
    part = lambda h, i: (0, h)
    ins = [(low, (rows, 128), lambda h, i: (0, 0))]
    ins += [(of_half, (rows, 256), part) for of_half in q]
    for kv in list(slots.values()) + list(halos.values()):
        ins += slot_inputs(kv, rows)
    if carry is not None:
        ins += [(c, (rows, 256), part) for c in carry]
    scratch, keep = [], {}
    for _ in halves:
        scratch += [pltpu.VMEM((2 * rows, 128), BF)] + [pltpu.VMEM((2 * rows, 128), F32)] * 2
    state = shaped((rows, heads * 256), F32)
    if last is None:
        outs = [(state, (rows, 256), part)] * (2 * len(halves))
    else:
        other = last[0]
        if other is not None:
            keep = {len(ins): 0}
            ins.append((other, None, None))
        half = halves[0]
        outs = [
            (shaped((2 * rows, heads * 256), BF), (rows, 256), lambda h, i: (half, h)),
            (shaped((heads, 8, rows), F32), (1, 8, rows), lambda h, i: (h, 0, 0)),
        ]
    return call(functools.partial(fwd_kernel, plan), "attend", (heads,), ins, outs, scratch,
                scalars=scalars, keep=keep)


def out_kernel(att_ref, w_ref, part_ref):
    part_ref[...] = mm(att_ref[...], w_ref[...], NT).astype(BF)


def out_projection(half, attended, w_rest):
    rows, cols = attended.shape[0] // 2, attended.shape[1]
    model = w_rest.shape[0]
    ins = [(attended, (rows, cols), lambda j: (half, 0)), (w_rest, (model // 2, cols), lambda j: (j, 0))]
    outs = [(shaped((rows, model), BF), (rows, model // 2), lambda j: (0, j))]
    return call(out_kernel, "out_projection", (2,), ins, outs)[0]


def bwd_kernel(plan, idx_ref, q_ref, do_ref, lse_ref, delta_ref, lo_ref, *refs):
    half, slots, halos = plan["half"], plan["slots"], plan["halos"]
    refs = list(refs)
    slot_refs = take_slots(refs, plan["pairs"])
    halo_refs = take_slots(refs, [False] * len(halos))
    prior_dq = refs.pop(0) if plan["carry"] else None
    prior = [refs.pop(0) for _ in slots] if plan["sum"] else None
    if plan["alias"]:
        refs.pop(0)
    dq_ref = refs.pop(0)
    slot_outs = [refs.pop(0) for _ in slots]
    halo_outs = [refs.pop(0) for _ in halos]
    qs, dos, lses, deltas, dq = refs
    me, lo_first = idx_ref[0], idx_ref[1]
    rows = q_ref.shape[0]
    for g in range(2):
        cols, at = slice(g * HEAD_SIZE, (g + 1) * HEAD_SIZE), slice(g * rows, (g + 1) * rows)
        qs[at, :] = q_ref[:, cols]
        dos[at, :] = do_ref[:, cols]
        lses[:, at] = lse_ref[0, g : g + 1, :]
        deltas[:, at] = delta_ref[0, g : g + 1, :]
    dq[...] = jnp.zeros_like(dq) if prior_dq is None else prior_dq[...]

    def block(kv_ref, out_ref, mask=None, before=None):
        keys = kv_ref[0][...]
        scores = mm(keys, qs[...], NT)
        dp = mm(kv_ref[1][...], dos[...], NT)
        scores = scores - lses[...]
        if mask is not None:
            scores = jnp.where(mask, scores, MASKED)
        probs = jnp.exp2(scores)
        ds = (probs * (dp - deltas[...])).astype(BF)
        dq[...] += mm(keys.T, ds)
        dk, dv = mm(ds, qs[...]) * LN2, mm(probs.astype(BF), dos[...])
        if before is not None:
            dk, dv = dk + before[0].astype(F32), dv + before[1].astype(F32)
        out_ref[0] = dk.astype(BF)
        out_ref[1] = dv.astype(BF)

    lane = lax.broadcasted_iota(jnp.int32, (1, 2 * rows), 1)
    lane = jnp.where(lane >= rows, lane - rows, lane)
    key = lax.broadcasted_iota(jnp.int32, (rows, 1), 0)

    def when(needed, kv_ref, out_ref, mask=None):
        @pl.when(needed)
        def _():
            block(kv_ref, out_ref, mask)

        @pl.when(jnp.logical_not(needed))
        def _():
            out_ref[...] = jnp.zeros_like(out_ref)

    low = lo_ref[:1, :]
    for d, kv_ref, out_ref in zip(halos, halo_refs, halo_outs):
        if d == 0:
            block(kv_ref, out_ref, (key <= lane) & (key >= low))
        else:
            when(lo_first < -(d - 1) * rows, kv_ref, out_ref, key - d * rows >= low)
    if half == 1:
        for at in range(len(slots)):
            block(slot_refs[at], slot_outs[at], None, prior[at] if prior else None)
    else:
        if 0 in slots:
            at = slots.index(0)
            block(slot_refs[at], slot_outs[at], key <= lane)
        for bit, group in by_top_bit(slots).items():

            @pl.when(jnp.bitwise_and(me, bit) != 0)
            def _(group=group):
                for at in group:
                    block(slot_refs[at], slot_outs[at])

            @pl.when(jnp.bitwise_and(me, bit) == 0)
            def _(group=group):
                for at in group:
                    slot_outs[at][...] = jnp.zeros_like(slot_outs[at])

    if plan["last"]:
        for g in range(2):
            cols = slice(g * HEAD_SIZE, (g + 1) * HEAD_SIZE)
            dq_ref[:, cols] = dq[:, g * rows : (g + 1) * rows].T * SCALE
    else:
        dq_ref[...] = dq[...]


def attention_backward(half, scalars, q, do, lse, delta, low, slots, halos, carry=None, prior=None, last=True, whole=None):
    rows, heads = q.shape[0], q.shape[1] // 256
    plan = dict(half=half, slots=list(slots), pairs=[isinstance(kv, tuple) for kv in slots.values()], halos=list(halos), carry=carry is not None,
                sum=prior is not None, last=last, alias=whole is not None)
    part = lambda h, i: (0, h)
    stat = lambda h, i: (h, 0, 0)
    kv_map = lambda h, i: (0, 0, h)
    ins = [
        (q, (rows, 256), part),
        (do, (rows, 256), part),
        (lse, (1, 8, rows), stat),
        (delta, (1, 8, rows), stat),
        (low, (8, 2 * rows), lambda h, i: (0, 0)),
    ]
    pieces = list(slots.values()) + list(halos.values())
    for kv in pieces:
        ins += slot_inputs(kv, rows)
    if carry is not None:
        ins.append((carry, (128, 2 * rows), lambda h, i: (h, 0)))
    if prior is not None:
        ins += [(prior[s], (2, rows, 128), kv_map) for s in slots]
    keep = {}
    if whole is not None:
        keep = {len(ins): 0}
        ins.append((whole, None, None))
    if last:
        outs = [(shaped((2 * rows, heads * 256), F32), (rows, 256), lambda h, i: (half, h))]
    else:
        outs = [(shaped((heads * 128, 2 * rows), F32), (128, 2 * rows), lambda h, i: (h, 0))]
    outs += [(shaped((2, rows, heads * 128), BF), (2, rows, 128), kv_map) for _ in pieces]
    scratch = [
        pltpu.VMEM((2 * rows, 128), BF),
        pltpu.VMEM((2 * rows, 128), BF),
        pltpu.VMEM((1, 2 * rows), F32),
        pltpu.VMEM((1, 2 * rows), F32),
        pltpu.VMEM((128, 2 * rows), F32),
    ]
    us = 4 + 6 * (len(slots) + len(halos)) if carry is not None or halos else 0.1
    results = call(functools.partial(bwd_kernel, plan), "attend_back", (heads,), ins, outs, scratch,
                   scalars=scalars, us=us, keep=keep)
    n = len(slots)
    return results[0], dict(zip(slots, results[1 : 1 + n])), dict(zip(halos, results[1 + n :]))


def ffn_kernel(x_ref, own_ref, got_ref, gain_ref, dy_ref, gu_ref, down_ref, *refs):
    resid_ref, normed_ref, hidden_ref, dgu_ref, out_ref, back_ref, normed, out_acc, back_acc = refs[-9:]
    step, steps = pl.program_id(0), pl.num_programs(0)

    @pl.when(step == 0)
    def _():
        resid = x_ref[...].astype(F32) + (own_ref[...].astype(F32) + got_ref[...].astype(F32))
        resid_ref[...] = resid
        normed[...] = (resid * rms(resid) * gain_ref[...]).astype(BF)
        normed_ref[...] = normed[...]
        out_acc[...] = jnp.zeros_like(out_acc)
        back_acc[...] = jnp.zeros_like(back_acc)

    wide = down_ref.shape[1]
    both = mm(normed[...], gu_ref[...])
    d_hidden = mm(dy_ref[...], down_ref[...])
    gate, up = both[:, :wide], both[:, wide:]
    sig = 1.0 / (1.0 + jnp.exp(-gate))
    silu = gate * sig
    hidden = (silu * up).astype(BF)
    hidden_ref[...] = hidden
    d_up = (d_hidden * silu).astype(BF)
    d_gate = (d_hidden * up * (sig + silu * (1.0 - sig))).astype(BF)
    dgu_ref[:, :wide] = d_gate
    dgu_ref[:, wide:] = d_up
    out_acc[...] += mm(hidden, down_ref[...], NT)
    back_acc[...] += mm(dgu_ref[...], gu_ref[...], NT)

    @pl.when(step == steps - 1)
    def _():
        out_ref[...] = out_acc[...].astype(BF)
        back_ref[...] = back_acc[...].astype(BF)


def feed_forward(half, x, own, got, gain, dy, w_od, w_gu, chunk, whole=None):
    rows, model = own.shape
    units = w_gu.shape[1] // 2
    steps = units // chunk
    mine, once = lambda f: (half, 0), lambda f: (0, 0)
    at_down = (w_od.shape[1] - units) // chunk
    block = (rows, model)
    ins = [
        (x, block, mine), (own, block, once), (got, block, once), (gain, (1, model), once), (dy, block, mine),
        (w_gu, (model, 2 * chunk), lambda f: (0, f)),
        (w_od, (model, chunk), lambda f: (0, at_down + f)),
    ]
    keep = {}
    if whole is not None:
        keep = {len(ins) + i: 1 + i for i in range(3)}
        ins += [(array, None, None) for array in whole]
    outs = [
        (shaped((rows, model), F32), block, once),
        (shaped((2 * rows, model), BF), block, mine),
        (shaped((2 * rows, units), BF), (rows, chunk), lambda f: (half, f)),
        (shaped((2 * rows, 2 * units), BF), (rows, 2 * chunk), lambda f: (half, f)),
        (shaped((rows, model), BF), block, once),
        (shaped((rows, model), BF), block, once),
    ]
    scratch = [pltpu.VMEM(block, BF), pltpu.VMEM(block, F32), pltpu.VMEM(block, F32)]
    return call(ffn_kernel, "feed_forward", (steps,), ins, outs, scratch, keep=keep)


def norm_back(grad, values, gain):
    scale = rms(values)
    unit = values * scale
    inner = grad * gain
    return scale * (inner - unit * jnp.mean(inner * unit, axis=-1, keepdims=True)), grad * unit


def lane_mean(values):
    width = values.shape[-1]
    ones = jnp.ones((width, width), BF)
    high = values.astype(BF)
    low = (values - high.astype(F32)).astype(BF)
    return (mm(high, ones) + mm(low, ones)) * (1.0 / width)


def head_norm_back(grad, values, gain):
    scale = lax.rsqrt(lane_mean(values * values) + EPSILON)
    unit = values * scale
    inner = grad * gain
    return scale * (inner - unit * lane_mean(inner * unit)), grad * unit


def row_blocks(rows):
    size = rows // 2 if rows % 512 == 0 else rows
    return size, rows // size


def add_up(ref, value):
    total = jnp.sum(value, axis=0, keepdims=True)

    @pl.when(pl.program_id(0) == 0)
    def _():
        ref[...] = total

    @pl.when(pl.program_id(0) > 0)
    def _():
        ref[...] += total


def mixed_kernel(heads, own_ref, got_ref, resid_ref, gain_ref, dy_ref, w_ref, att_ref, *refs):
    d_resid_ref, mixed_ref, datt_ref, delta_ref, dgain_ref = refs[-5:]
    grad = own_ref[...].astype(F32) + got_ref[...].astype(F32)
    d_norm, summand = norm_back(grad, resid_ref[...], gain_ref[...])
    add_up(dgain_ref, summand)
    d_resid = dy_ref[...].astype(F32) + d_norm
    d_resid_ref[...] = d_resid
    mixed_ref[...] = d_resid.astype(BF)
    datt_ref[...] = mm(mixed_ref[...], w_ref[...]).astype(BF)
    for h in range(heads):
        cols = slice(h * HEAD_SIZE, (h + 1) * HEAD_SIZE)
        product = datt_ref[:, cols].astype(F32) * att_ref[:, cols].astype(F32)
        delta_ref[h // 2, h % 2 : h % 2 + 1, :] = jnp.sum(product.T, axis=0, keepdims=True)


def mixed_back(half, own, got, resid, gain, dy, w_rest, o_cols, attended, whole=None):
    rows, model = own.shape
    heads = o_cols // HEAD_SIZE
    size, steps = row_blocks(rows)
    mine, here, once = lambda f: (half * steps + f, 0), lambda f: (f, 0), lambda f: (0, 0)
    block = (size, model)
    ins = [
        (own, block, here), (got, block, here), (resid, block, here), (gain, (1, model), once),
        (dy, block, mine), (w_rest, (model, o_cols), once), (attended, (size, o_cols), mine),
    ]
    keep = {}
    if whole is not None:
        keep = {len(ins): 1}
        ins.append((whole, None, None))
    outs = [
        (shaped((rows, model), F32), block, here),
        (shaped((2 * rows, model), BF), block, mine),
        (shaped((rows, o_cols), BF), (size, o_cols), here),
        (shaped((heads // 2, 8, rows), F32), (heads // 2, 8, size), lambda f: (0, 0, f)),
        (shaped((1, model), F32), (1, model), once),
    ]
    return call(functools.partial(mixed_kernel, heads), "mixed_back", (steps,), ins, outs, keep=keep)


def merge_kernel(two, got3, four, got5, far_k, far_v, to_x, to_y):
    for which in range(2):
        by_x = two[which].astype(F32) + got3[which].astype(F32)
        by_y = four[which].astype(F32) + got5[which].astype(F32)
        to_x[which] = (by_x + far_v[...].astype(F32) if which else by_x).astype(BF)
        to_y[which] = (by_y if which else by_y + far_k[...].astype(F32)).astype(BF)


def merge(*pieces):
    rows, cols = pieces[-1].shape
    size, steps = row_blocks(rows)
    ins = []
    for piece in pieces:
        if piece.ndim == 3:
            ins.append((piece, (2, size, cols), lambda f: (0, f, 0)))
        else:
            ins.append((piece, (size, cols), lambda f: (f, 0)))
    outs = [(shaped((2, rows, cols), BF), (2, size, cols), lambda f: (0, f, 0))] * 2
    return call(merge_kernel, "merge", (steps,), ins, outs)


def weight_kernel(left_ref, right_ref, *refs):
    refs[-1][...] = mm(left_ref[...], right_ref[...], TN).astype(BF)


def weight_grad(left, right, at, width, cols, whole=None):
    tokens, model = left.shape
    n = right.shape[1]
    ins = [(left, (tokens, model), lambda j: (0, 0)), (right, (tokens, cols), lambda j: (0, j))]
    keep = {}
    if whole is not None:
        keep = {len(ins): 0}
        ins.append((whole, None, None))
    outs = [(shaped((model, width), BF), (model, cols), lambda j: (0, at // cols + j))]
    return call(weight_kernel, "weight_grad", (n // cols,), ins, outs, keep=keep)[0]


def slot_weight_kernel(order, part_ref, left_ref, right_ref, low_ref, high_ref, total):
    total[...] = mm(left_ref[...], right_ref[...], TN)
    wide = total.shape[0] // len(order)
    for at, slot in enumerate(order):
        block = jnp.bitwise_xor(part_ref[0], slot)
        piece = total[pl.ds(pl.multiple_of(block * wide, wide), wide), :].astype(BF)
        out_ref, row = (low_ref, at) if at < len(order) // 2 else (high_ref, at - len(order) // 2)
        out_ref[row * wide : (row + 1) * wide, :] = piece


def slot_weight_grad(order, part, left, right):
    tokens, model = left.shape
    cols = right.shape[1]
    once = lambda j, i: (0, 0)
    ins = [(left, (tokens, model), once), (right, (tokens, cols), once)]
    half = shaped((model // 2, cols), BF)
    return call(functools.partial(slot_weight_kernel, order), "slot_weight_grad", (1,), ins,
                [(half, half.shape, once)] * 2, [pltpu.VMEM((model, cols), F32)], scalars=part[None])


def weight_halves_kernel(left_ref, right_ref, high_ref, low_ref):
    for half, out_ref in enumerate((high_ref, low_ref)):

        @pl.when(pl.program_id(0) == half)
        def _(out_ref=out_ref):
            out_ref[...] = mm(left_ref[...], right_ref[...], TN).astype(BF)


def weight_halves(left, right):
    tokens, model = left.shape
    cols = right.shape[1]
    once = lambda i: (0, 0)
    ins = [(left, (tokens, model // 2), lambda i: (0, 1 - i)), (right, (tokens, cols), once)]
    half = shaped((model // 2, cols), BF)
    return call(weight_halves_kernel, "weight_halves", (2,), ins, [(half, half.shape, once)] * 2)


def q_back_kernel(heads, dq_ref, lin_ref, gain_ref, cos_ref, sin_ref, w_ref, *refs):
    d_ref, part_ref, gains_ref = refs[-3:]
    cos, sin = cos_ref[...], sin_ref[...]
    total = jnp.zeros(cos.shape, F32)
    for h in range(heads):
        cols = slice(h * HEAD_SIZE, (h + 1) * HEAD_SIZE)
        grad, summand = head_norm_back(turn_back(dq_ref[:, cols], cos, sin), lin_ref[:, cols], gain_ref[...])
        d_ref[:, cols] = grad.astype(BF)
        total = total + summand
    part_ref[...] = mm(d_ref[...], w_ref[...], NT)
    add_up(gains_ref, total)


def q_back(dq, lin, gain, cos, sin, w):
    rows, cols = dq.shape
    model = w.shape[0]
    size, steps = row_blocks(rows)
    here, once = lambda f: (f, 0), lambda f: (0, 0)
    ins = [
        (dq, (size, cols), here), (lin, (size, cols), here), (gain, (1, HEAD_SIZE), once),
        (cos, (size, HEAD_SIZE), here), (sin, (size, HEAD_SIZE), here), (w, (model, cols), once),
    ]
    outs = [
        (shaped((rows, cols), BF), (size, cols), here),
        (shaped((rows, model), F32), (size, model), here),
        (shaped((1, HEAD_SIZE), F32), (1, HEAD_SIZE), once),
    ]
    kernel = functools.partial(q_back_kernel, cols // HEAD_SIZE)
    return call(kernel, "q_back", (steps,), ins, outs)


def kv_back_kernel(heads, n_keys, n_values, lin_ref, gain_ref, cos_ref, sin_ref, w_ref, slots_ref, q_part_ref, *refs):
    key_refs, value_refs = refs[:n_keys], refs[n_keys : n_keys + n_values]
    d_ref, part_ref, gains_ref = refs[-3:]
    cos, sin = cos_ref[...], sin_ref[...]
    width = heads * HEAD_SIZE

    def total(sources, which, cols):
        value = None
        for ref in sources:
            piece = ref[which, :, cols] if len(ref.shape) == 3 else ref[:, cols]
            value = piece.astype(F32) if value is None else value + piece.astype(F32)
        return value

    gains = jnp.zeros(cos.shape, F32)
    for h in range(heads):
        cols = slice(h * HEAD_SIZE, (h + 1) * HEAD_SIZE)
        grad, summand = head_norm_back(
            turn_back(total(key_refs, 0, cols), cos, sin), lin_ref[:, cols], gain_ref[...]
        )
        d_ref[:, cols] = grad.astype(BF)
        gains = gains + summand
    d_ref[:, width:] = total(value_refs, 1, slice(None)).astype(BF)
    part = (q_part_ref[...] + mm(d_ref[...], w_ref[...], NT)).astype(BF)
    part_ref[...] = mm(part, slots_ref[...], NT).astype(BF)
    add_up(gains_ref, gains)


def kv_back(half, keys, values, lin, gain, cos, sin, w, to_slots, q_part, whole=None):
    rows, cols = lin.shape
    model = w.shape[0]
    size, steps = row_blocks(rows)
    mine, here, once = lambda f: (half * steps + f, 0), lambda f: (f, 0), lambda f: (0, 0)
    ins = [
        (lin, (size, cols), here), (gain, (1, HEAD_SIZE), once), (cos, (size, HEAD_SIZE), mine),
        (sin, (size, HEAD_SIZE), mine), (w, (model, 2 * cols), once),
        (to_slots, (model, model), once), (q_part, (size, model), mine),
    ]
    for piece in list(keys) + list(values):
        if piece.ndim == 3:
            ins.append((piece, (2, size, cols), lambda f: (0, f, 0)))
        else:
            ins.append((piece, (size, cols), here))
    keep = {}
    if whole is not None:
        keep = {len(ins): 0}
        ins.append((whole, None, None))
    outs = [
        (shaped((2 * rows, 2 * cols), BF), (size, 2 * cols), mine),
        (shaped((rows, model), BF), (size, model), here),
        (shaped((1, HEAD_SIZE), F32), (1, HEAD_SIZE), once),
    ]
    kernel = functools.partial(kv_back_kernel, cols // HEAD_SIZE, len(keys), len(values))
    return call(kernel, "kv_back", (steps,), ins, outs, keep=keep, us=3 * (1 - half))


def tokens_kernel(own_ref, got_ref, x_ref, gain_ref, d_resid_ref, *refs):
    out_ref, dgain_ref = refs[-2:]
    grad = own_ref[...].astype(F32) + got_ref[...].astype(F32)
    d_norm, summand = norm_back(grad, x_ref[...].astype(F32), gain_ref[...])
    add_up(dgain_ref, summand)
    out_ref[...] = (d_resid_ref[...] + d_norm).astype(BF)


def tokens_back(half, own, got, x, gain, d_resid, whole=None):
    rows, model = own.shape
    size, steps = row_blocks(rows)
    mine, here, once = lambda f: (half * steps + f, 0), lambda f: (f, 0), lambda f: (0, 0)
    block = (size, model)
    ins = [(own, block, here), (got, block, here), (x, block, mine), (gain, (1, model), once), (d_resid, block, here)]
    keep = {}
    if whole is not None:
        keep = {len(ins): 0}
        ins.append((whole, None, None))
    outs = [(shaped((2 * rows, model), BF), block, mine), (shaped((1, model), F32), (1, model), once)]
    return call(tokens_kernel, "tokens_back", (steps,), ins, outs, keep=keep, us=20)


def share_kernel(chunk, ffn_ref, own_ref, got_ref, out_ref, gate_ref, up_ref, down_ref):
    units = gate_ref.shape[1]
    out_ref[...] = own_ref[...].astype(F32) + got_ref[...].astype(F32)
    for at in range(0, units, chunk):
        gate_ref[:, at : at + chunk] = ffn_ref[:, 2 * at : 2 * at + chunk].astype(F32)
        up_ref[:, at : at + chunk] = ffn_ref[:, 2 * at + chunk : 2 * at + 2 * chunk].astype(F32)
    down_ref[...] = ffn_ref[:, 2 * units :].astype(F32)


def unpack(chunk, ffn_share, out_grad):
    wide, units = ffn_share.shape[0], ffn_share.shape[1] // 3
    o_cols = out_grad[0].shape[1]
    whole = lambda f: (0, 0)
    ins = [(ffn_share, ffn_share.shape, whole)] + [(grad, (wide, o_cols), whole) for grad in out_grad]
    outs = [(shaped((wide, cols), F32), (wide, cols), whole) for cols in (o_cols, units, units, units)]
    return call(functools.partial(share_kernel, chunk), "unpack", (1,), ins, outs)


def layer_kernel(resid_ref, own_ref, got_ref, *refs):
    refs[-1][...] = (resid_ref[...] + (own_ref[...].astype(F32) + got_ref[...].astype(F32))).astype(BF)


def add_layer(half, resid, own, got, whole=None):
    rows, model = resid.shape
    size, steps = row_blocks(rows)
    here, mine = lambda f: (f, 0), lambda f: (half * steps + f, 0)
    ins = [(array, (size, model), here) for array in (resid, own, got)]
    keep = {}
    if whole is not None:
        keep = {len(ins): 0}
        ins.append((whole, None, None))
    outs = [(shaped((2 * rows, model), BF), (size, model), mine)]
    return call(layer_kernel, "add_layer", (steps,), ins, outs, keep=keep)[0]


def swap(value, axis, bit):
    size = lax.axis_size(axis)
    return lax.ppermute(value, axis, [(i, i ^ bit) for i in range(size)])


def shift(value, by):
    size = lax.axis_size("ctx")
    return lax.ppermute(value, "ctx", [(i, i + by) for i in range(size) if 0 <= i + by < size])


def add_low(left, right):
    return (left.astype(F32) + right.astype(F32)).astype(BF)


def butterfly(value, axes, gates=()):
    gates = list(gates)
    for axis in axes:
        bit = 1
        while bit < lax.axis_size(axis):
            got = swap(value, axis, bit)
            value = value + (after(got, gates.pop(0)) if gates else got)
            bit *= 2
    return value


def after(value, *others):
    return lax.optimization_barrier((value, *others))[0]


def rotary_tables(position):
    half_dim = HEAD_SIZE // 2
    inverse_freq = jnp.exp(jnp.arange(half_dim, dtype=F32) * (-math.log(ROPE_BASE) / half_dim))
    angles = position.astype(F32)[:, None] * inverse_freq[None, :]
    cosine, sine = jnp.cos(angles), jnp.sin(angles)
    return jnp.concatenate([cosine, cosine], axis=-1), jnp.concatenate([-sine, sine], axis=-1)


def body(
    tokens,
    cont_lengths,
    attn_gain,
    ffn_gain,
    query_gain,
    key_gain,
    w_query,
    key_weight,
    value_weight,
    w_out,
    w_gate,
    w_up,
    w_down,
    cotangent,
):
    ctx_size = lax.axis_size("ctx")
    weight_axes = ("shard", "ctx")
    parts = lax.axis_size("shard") * ctx_size
    me = lax.axis_index("ctx")
    part = lax.axis_index("shard") * ctx_size + me
    rows, model = tokens.shape[0] // 2, tokens.shape[1]
    n_halo = 1 + -(-(LONGEST - 1) // rows)
    lengths = cont_lengths[0]

    bits = [("shard", 1)] + [("ctx", 1 << i) for i in range(1, ctx_size.bit_length() - 1)] + [("ctx", 1)]
    order = [0]
    for axis, bit in bits:
        order += [j ^ (bit * ctx_size if axis == "shard" else bit) for j in order]
    wide, narrow = attn_gain.shape[0], query_gain.shape[0]
    q_cols, k_cols = w_query.shape[1], key_weight.shape[1]
    o_cols, units = w_out.shape[0], w_gate.shape[1]
    heads, kv_heads = q_cols // HEAD_SIZE, k_cols // HEAD_SIZE
    chunk = math.gcd(units, 512)

    def gather_first(piece, *gate):
        return jnp.concatenate([piece, after(swap(piece, "shard", 1), *gate)]) if ctx_size == 8 else piece

    def gather_near(one, *gate):
        if ctx_size != 8:
            for axis, bit in bits:
                one = jnp.concatenate([one, swap(one, axis, bit)])
            return [one]
        by_x, by_y = (after(v, *gate) for v in (swap(one, "ctx", 2), swap(one, "ctx", 4)))
        cut = one.shape[1] // 2
        return [one, by_x, by_y, swap(by_y[:, :cut], "ctx", 2), swap(by_x[:, cut:], "ctx", 4)]

    def gather_far(pieces, *gate):
        if ctx_size != 8:
            return pieces[0], pieces[0]
        *near, left, right = pieces
        far = jnp.concatenate([after(left, *gate), after(right, *gate)], axis=1)
        near = [*near, far]
        return jnp.concatenate(near + [after(swap(piece, "ctx", 1), *gate) for piece in near]), far

    def scatter_rows(low, high, late):
        total = add_low(low, after(swap(high, "ctx", 1), late))
        if ctx_size != 8:
            for axis, bit in bits[-2:0:-1]:
                size = total.shape[0] // 2
                total = add_low(total[:size], swap(total[size:], axis, bit))
            return (total,)
        size, cut = total.shape[0] // 4, total.shape[1] // 2
        own, by_x, by_y, far = (total[i * size : (i + 1) * size] for i in range(4))
        left, right = swap(far[:, :cut], "ctx", 2), swap(far[:, cut:], "ctx", 4)
        return own, by_x, by_y, left, right

    def scatter_more(stage, late):
        if ctx_size != 8:
            return stage
        own, by_x, by_y, left, right = stage
        left, right = after(left, late), after(right, late)
        cut = left.shape[1]
        by_x = jnp.concatenate([by_x[:, :cut], add_low(by_x[:, cut:], right)], axis=1)
        by_y = jnp.concatenate([add_low(by_y[:, :cut], left), by_y[:, cut:]], axis=1)
        return lax.optimization_barrier((own, by_x, by_y))[0], swap(by_x, "ctx", 2), swap(by_y, "ctx", 4)

    def scatter_sum(stage, late):
        total = stage[0].astype(F32)
        for piece in stage[1:]:
            total = total + after(piece, late).astype(F32)
        total, size = total.astype(BF), total.shape[0] // 2
        return total, swap(total[size:], "shard", 1)

    kv_piece, od_piece, gu_piece = pack(
        chunk, key_weight, value_weight, w_out.T, w_down.T, w_gate, w_up
    )
    kv_one = gather_first(kv_piece)
    kv_near = gather_near(kv_one)
    w_kv, kv_far = gather_far(kv_near)
    q_one = gather_first(after(w_query, kv_piece), kv_far)
    w_od = lax.all_gather(od_piece, weight_axes, axis=0, tiled=True)
    gains = jnp.concatenate([attn_gain, ffn_gain, query_gain, key_gain])[None]
    gains = jnp.where(jnp.arange(parts)[:, None] == part, gains, jnp.zeros((), BF))
    gains = gains + after(swap(gains, "ctx", 1), kv_piece)
    for at, (axis, bit) in enumerate(bits[:-1]):
        gains = gains + after(swap(gains, axis, bit), (kv_one, kv_near[min(1, len(kv_near) - 1)], kv_far)[min(at, 2)])
    gains = gains.astype(F32)
    gain_one = gains[:, :wide].reshape(1, -1)
    gain_two = gains[:, wide : 2 * wide].reshape(1, -1)
    gain_q = gains[:, 2 * wide : 2 * wide + narrow].reshape(1, -1)
    gain_k = gains[:, 2 * wide + narrow :].reshape(1, -1)
    source = jnp.bitwise_xor(part, jnp.array(order, jnp.int32))[:, None] * wide + jnp.arange(wide, dtype=jnp.int32)
    to_slots = (jnp.arange(model, dtype=jnp.int32)[:, None] == source.reshape(1, -1)).astype(BF)
    tokens_s = mm(after(tokens, q_one), to_slots).astype(BF)
    gain_one_s = mm(gain_one.astype(BF), to_slots)

    cont_at = me * rows + jnp.arange(rows, dtype=jnp.int32)
    cont_ends = jnp.cumsum(lengths)
    starts = cont_ends - lengths
    seg = jnp.sum((cont_ends[None, :] <= cont_at[:, None]).astype(jnp.int32), axis=1)
    numbers = jnp.arange(lengths.shape[0], dtype=jnp.int32)
    first = jnp.sum(jnp.where(numbers[None, :] == seg[:, None], starts[None, :], 0), axis=1)
    position = jnp.concatenate([me * rows + jnp.arange(rows, dtype=jnp.int32), PROMPT + cont_at - first])
    low = first - me * rows
    low_col = jnp.broadcast_to(low[:, None], (rows, 128))
    low_row = jnp.broadcast_to(jnp.concatenate([low, low])[None, :], (8, 2 * rows))
    scalars = jnp.stack([me, low[0]])
    cos, sin = rotary_tables(position)

    once = lambda f: (0, 0)

    def keys_values(half, gain, whole=None):
        mine = lambda f: (half, 0)
        ins = [
            (tokens_s, (rows, model), mine), (gain, (1, model), once), (w_kv, (model, 2 * k_cols), once),
            (gain_k, (1, HEAD_SIZE), once), (cos, (rows, HEAD_SIZE), mine), (sin, (rows, HEAD_SIZE), mine),
        ]
        keep = {}
        if whole is not None:
            keep = {len(ins): 0}
            ins.append((whole, None, None))
        outs = [
            (shaped((2 * rows, model), BF), (rows, model), mine),
            (shaped((2, rows, k_cols), BF), (2, rows, k_cols), lambda f: (0, 0, 0)),
            (shaped((rows, k_cols), F32), (rows, k_cols), once),
        ]
        return call(functools.partial(kv_kernel, kv_heads), "keys_values", (1,), ins, outs, keep=keep)

    q_near = gather_near(q_one, w_kv)
    normed, kv_p, k_lin_p = keys_values(0, after(gain_one_s, *q_near[1:]))
    normed, kv_c, k_lin_c = keys_values(1, after(gain_one_s, kv_p), normed)
    w_q, _ = gather_far(q_near, kv_c)
    def queries(half, gain, whole=None):
        mine = lambda f: (half, 0)
        ins = [
            (normed, (rows, model), mine), (w_q, (model, q_cols), once), (gain, (1, HEAD_SIZE), once),
            (cos, (rows, HEAD_SIZE), mine), (sin, (rows, HEAD_SIZE), mine),
        ]
        keep = {}
        if whole is not None:
            keep = {len(ins): 1}
            ins.append((whole, None, None))
        outs = [
            (shaped((rows, q_cols), BF), (rows, q_cols), once),
            (shaped((2 * rows, q_cols), F32), (rows, q_cols), mine),
        ]
        return call(functools.partial(q_kernel, heads), "queries", (1,), ins, outs, keep=keep)

    q_c, q_lin = queries(1, gain_q)

    def pick(source, wanted):
        return {s: source[s] for s in source if s in wanted}

    near, middle, far = (0, 1), (2, 3, 4, 5), tuple(range(6, ctx_size))
    slots, halos = {0: kv_p}, {0: kv_c}
    odd = (me % 2) == 1
    if ctx_size == 8:
        slots[1], slots[2], slots[4] = (swap(kv_p, "ctx", bit) for bit in (1, 2, 4))
    else:
        both, bit = kv_p[None], 1
        while bit < ctx_size:
            both = jnp.concatenate([both, swap(both, "ctx", bit)])
            bit *= 2
        slots = {s: both[s] for s in range(ctx_size)}
        halos.update({d: shift(kv_c, d) for d in range(1, n_halo)})
    ready = ()
    if ctx_size == 8:
        slots[2], slots[4] = after(slots[2], q_c), after(slots[4], q_c)
        far_k, far_v = swap(slots[4][0], "ctx", 2), swap(slots[2][1], "ctx", 4)
        slots[3], slots[5] = swap(slots[2], "ctx", 1), swap(slots[4], "ctx", 1)
        halos[2] = shift(after(kv_c, slots[2]), 2)
        gu_piece = after(gu_piece, slots[2], slots[4])
        ready = (slots[2], slots[4])
    w_gu = lax.all_gather(after(gu_piece, w_od), weight_axes, axis=0, tiled=True)
    c_state = attention_forward(
        (1,), after(scalars, *ready), (q_c,), low_col, pick(slots, near), pick(halos, (0,))
    )
    q_p, q_lin = queries(0, after(gain_q, c_state[0]), q_lin)
    if ctx_size == 8:
        slots[6] = after(far_k, c_state[0]), after(far_v, c_state[0])
        slots[7] = tuple(swap(part, "ctx", 1) for part in slots[6])
    attended, lse_p = attention_forward(
        (0,), after(scalars, q_p), (q_p,), low_col, slots, {}, None, (None,)
    )
    part_p = out_projection(0, attended, w_od)
    got_p = swap(part_p, "tensor", 1)
    if ctx_size == 8:
        halos[1] = swap(jnp.where(odd, after(halos[2], part_p), kv_c), "ctx", 1)
    attended, lse_c = attention_forward(
        (1,), after(scalars, part_p), (q_c,), low_col, pick(slots, middle + far), pick(halos, range(1, n_halo)),
        c_state, (attended,),
    )
    part_c = out_projection(1, attended, w_od)
    got_c = swap(part_c, "tensor", 1)

    resid_p, *whole, out_p, back_p = feed_forward(
        0, tokens, part_p, got_p, after(gain_two, part_c), cotangent, w_od, w_gu, chunk
    )
    back_got_p = swap(back_p, "tensor", 1)
    resid_c, *whole, out_c, back_c = feed_forward(
        1, tokens, part_c, got_c, after(gain_two, back_p), cotangent, w_od, w_gu, chunk, whole
    )
    back_got_c = swap(back_c, "tensor", 1)
    normed_ffn, hidden, d_gu = whole
    ffn_grads = weight_grad(normed_ffn, d_gu, 0, 3 * units, 2 * chunk)
    ffn_grads = weight_grad(cotangent, hidden, 2 * units, 3 * units, chunk, ffn_grads)
    ffn_share = lax.psum_scatter(ffn_grads, weight_axes, scatter_dimension=0, tiled=True)
    d_resid_p, d_mixed, d_att_p, delta_p, d_two_p = mixed_back(
        0, back_p, back_got_p, resid_p, after(gain_two, ffn_grads), cotangent, w_od, o_cols, attended
    )

    of_rows = [(d_att_p, lse_p, delta_p)]

    def back_rows(half, deps, slots, halos, carry, prior=None, whole=None, last=False):
        do, lse, delta = of_rows[half]
        return attention_backward(
            half, after(scalars, *deps), (q_p, q_c)[half], do, lse, delta, low_row, slots, halos, carry, prior, last, whole
        )

    dq_p, prior, _ = back_rows(0, (d_att_p,), pick(slots, far), {}, None)
    d_resid_c, d_mixed, d_att_c, delta_c, d_two_c = mixed_back(
        1, back_c, back_got_c, resid_c, after(gain_two, dq_p), cotangent, w_od, o_cols, attended, d_mixed
    )
    of_rows.append((d_att_c, lse_c, delta_c))
    out_low, out_high = slot_weight_grad(order, part, d_mixed, attended)
    out_p, out_c = after(out_p, out_low), after(out_c, out_low)
    out_got_p, out_got_c = swap(out_p, "tensor", 1), swap(out_c, "tensor", 1)
    dq_c, _, g_halo = back_rows(1, (out_low,), {}, halos, None)
    out_grad = scatter_rows(out_low, out_high, dq_c)
    if ctx_size == 8:
        near_one = swap(g_halo[1], "ctx", 1)
    dq_c, g, _ = back_rows(1, (dq_c, out_grad[0]), pick(slots, far), {}, dq_c, prior)
    out_grad = scatter_more(out_grad, dq_c)
    zero = jnp.zeros((), BF)
    ready = ()
    if ctx_size == 8:
        got7 = swap(g[7], "ctx", 1)
        near_one = after(near_one, dq_c)
        two_back = add_low(g_halo[2], jnp.where(odd, near_one, zero))
        halo_two = shift(two_back, -2)
        halo_near = jnp.where(odd, zero, near_one)
        ready = (two_back, halo_near)
    dq, prior, _ = back_rows(0, (dq_c, out_grad[0], *ready), pick(slots, near + middle), {}, dq_p, None, None, True)
    if ctx_size == 8:
        g6 = add_low(g[6], after(got7, dq))
        far_k, far_v = swap(g6[0], "ctx", 2), swap(g6[1], "ctx", 4)
        ready = (g6,)
    out_grad = scatter_sum(out_grad, dq)
    dq_c, more, _ = back_rows(1, (dq, out_grad[0], *ready), pick(slots, middle), {}, dq_c, prior)
    g.update(more)
    if ctx_size == 8:
        got3, got5 = swap(g[3], "ctx", 1), swap(g[5], "ctx", 1)
        ready = (halo_two,)
    dq, more, _ = back_rows(1, (dq_c, out_got_p, out_got_c, *ready), pick(slots, near), {}, dq_c, prior, dq, True)
    g.update(more)
    if ctx_size == 8:
        got1 = swap(g[1], "ctx", 1)
        far_k, far_v, got3, got5 = (after(v, dq, out_grad[1], ffn_share) for v in (far_k, far_v, got3, got5))
        to_x, to_y = merge(g[2], got3, g[4], got5, far_k, far_v)
        ready = (to_x,)
        keys_p = values_p = [g[0], got1, swap(to_x, "ctx", 2), swap(to_y, "ctx", 4)]
        keys_c = values_c = [g_halo[0], halo_near, halo_two]
    else:
        both = jnp.stack([g[s] for s in range(ctx_size)])
        while both.shape[0] > 1:
            size = both.shape[0] // 2
            both = add_low(both[:size], swap(both[size:], "ctx", size))
        keys_p = values_p = [both[0]]
        keys_c = values_c = [g_halo[0]] + [shift(g_halo[d], -d) for d in range(1, n_halo)]

    d_q, q_part, q_heads = q_back(dq, q_lin, after(gain_q, dq, *ready), cos, sin, w_q)
    d_kv, into_c, k_heads_c = kv_back(
        1, keys_c, values_c, k_lin_c, after(gain_k, q_part), cos, sin, w_kv, to_slots, q_part
    )
    into_got_c = swap(into_c, "tensor", 1)
    q_high, q_low = weight_halves(normed, after(d_q, into_c))
    d_kv, into_p, k_heads_p = kv_back(
        0, keys_p, values_p, k_lin_p, after(gain_k, q_low), cos, sin, w_kv, to_slots, q_part, d_kv
    )
    into_got_p = swap(into_p, "tensor", 1)
    q_grad = scatter_rows(q_low, q_high, into_p)
    kv_high, kv_low = weight_halves(normed, after(d_kv, q_grad[0]))
    q_grad = scatter_more(q_grad, kv_low)
    heads = jnp.concatenate([q_heads, k_heads_c + k_heads_p], axis=1)
    heads_got = swap(heads, "tensor", 1)
    grad_tokens, d_one_c = tokens_back(1, into_c, into_got_c, tokens, after(gain_one, kv_low, q_grad[0]), d_resid_c)
    out_share, gate_share, up_share, down_share = unpack(chunk, after(ffn_share, d_one_c), out_grad)
    q_grad = scatter_sum(q_grad, gate_share)
    kv_grad = scatter_rows(kv_low, kv_high, gate_share)
    layer_out = add_layer(0, after(resid_p, kv_grad[0], q_grad[0]), out_p, out_got_p)
    kv_grad = scatter_more(kv_grad, layer_out)
    layer_out = add_layer(1, after(resid_c, kv_grad[0]), out_c, out_got_c, layer_out)
    q_share = add_low(q_grad[0][:wide], after(q_grad[1], layer_out)).astype(F32)
    kv_grad = scatter_sum(kv_grad, layer_out)
    grad_tokens, d_one_p = tokens_back(
        0, into_p, into_got_p, tokens, after(gain_one, kv_grad[0], q_share), d_resid_p, grad_tokens
    )
    heads = heads + after(heads_got, d_one_p)
    late = jnp.concatenate([d_one_c + d_one_p, heads, d_two_c + d_two_p], axis=1)
    kv_share = add_low(kv_grad[0][:wide], after(kv_grad[1], d_one_p)).astype(F32)
    late = butterfly(late, ("ctx", "shard"), (d_one_p, kv_share))

    def own_gain(value, size):
        return lax.dynamic_index_in_dim(value.reshape(parts, size), part, 0, keepdims=False)

    return (
        layer_out,
        grad_tokens,
        own_gain(late[:, :model], wide),
        own_gain(late[:, model + 2 * HEAD_SIZE :], wide),
        own_gain(late[:, model : model + HEAD_SIZE], narrow),
        own_gain(late[:, model + HEAD_SIZE : model + 2 * HEAD_SIZE], narrow),
        q_share,
        kv_share[:, :k_cols],
        kv_share[:, k_cols:],
        out_share.T,
        gate_share,
        up_share,
        down_share.T,
    )


def solution(mesh):
    split = ("shard", "ctx")
    rows, gain = P(split, None), P(split)
    into, out_of = P(split, "tensor"), P("tensor", split)
    in_specs = (rows, P("shard", None)) + (gain,) * 4 + (into,) * 3 + (out_of,)
    in_specs += (into, into, out_of, rows)
    out_specs = (rows, rows) + (gain,) * 4 + (into,) * 3 + (out_of, into, into, out_of)
    return jax.shard_map(body, mesh=mesh, in_specs=in_specs, out_specs=out_specs, check_vma=False)
```

```python
import functools
import math

import jax
import jax.numpy as jnp
from jax import lax
from jax.experimental import pallas as pl
from jax.experimental.pallas import tpu as pltpu
from jax.sharding import PartitionSpec as P

HEAD_SIZE = 128
PROMPT = 4096
CONT_TOK = 4096
LONGEST = 1024

EPSILON = 1e-06
ROPE_BASE = 1000000.0
MASKED = -1e30
LOG2E = math.log2(math.e)
LN2 = math.log(2.0)
SCALE = 1.0 / math.sqrt(HEAD_SIZE)

BF = jnp.bfloat16
F32 = jnp.float32
NN = (((1,), (0,)), ((), ()))
NT = (((1,), (1,)), ((), ()))
TN = (((0,), (0,)), ((), ()))
MIB = 2**20
STATED = 3e9


def mm(left, right, dims=NN):
    return lax.dot_general(left, right, dims, preferred_element_type=F32)


def shaped(dims, kind):
    return jax.ShapeDtypeStruct(dims, kind)


def call(kernel, name, grid, ins, outs, scratch=(), vmem=56, scalars=None, keep=None, us=0):
    in_specs, arrays = [], []
    for array, block, index in ins:
        arrays.append(array)
        in_specs.append(pl.BlockSpec(memory_space=pl.ANY) if block is None else pl.BlockSpec(block, index))
    lead = 0 if scalars is None else 1
    return pl.pallas_call(
        kernel,
        grid_spec=pltpu.PrefetchScalarGridSpec(
            num_scalar_prefetch=lead,
            grid=grid,
            in_specs=in_specs,
            out_specs=[pl.BlockSpec(block, index) for _, block, index in outs],
            scratch_shapes=list(scratch),
        ),
        out_shape=[shape for shape, _, _ in outs],
        input_output_aliases={a + lead: b for a, b in (keep or {}).items()},
        compiler_params=pltpu.CompilerParams(vmem_limit_bytes=vmem * MIB),
        cost_estimate=pl.CostEstimate(flops=int(us * STATED), bytes_accessed=0, transcendentals=0),
        name=name,
    )(*([] if scalars is None else [scalars]), *arrays)


def rms(values):
    return lax.rsqrt(jnp.mean(values * values, axis=-1, keepdims=True) + EPSILON)


def turn(values, cos, sin):
    return values * cos + pltpu.roll(values, HEAD_SIZE // 2, 1) * sin


def turn_back(values, cos, sin):
    return values * cos - pltpu.roll(values, HEAD_SIZE // 2, 1) * sin


def put_together(pieces, whole_ref):
    rows = whole_ref.shape[0] // len(pieces)
    for at, piece in enumerate(pieces):
        whole_ref[at * rows : (at + 1) * rows, :] = piece[...]


def kv_kernel(heads, n_pieces, x_ref, gain_ref, hgain_ref, cos_ref, sin_ref, *refs):
    pieces, refs = refs[:n_pieces], refs[n_pieces:]
    if n_pieces == 1:
        w_ref, (normed_ref, kv_ref, lin_ref) = pieces[0], refs[-3:]
    else:
        normed_ref, kv_ref, lin_ref, w_ref = refs[-4:]
        put_together(pieces, w_ref)
    x = x_ref[...].astype(F32)
    normed_ref[...] = (x * rms(x) * gain_ref[...]).astype(BF)
    both = mm(normed_ref[...], w_ref[...])
    width = heads * HEAD_SIZE
    kv_ref[1] = both[:, width:].astype(BF)
    for h in range(heads):
        cols = slice(h * HEAD_SIZE, (h + 1) * HEAD_SIZE)
        lin = both[:, cols]
        lin_ref[:, cols] = lin
        kv_ref[0, :, cols] = turn(lin * rms(lin) * hgain_ref[...], cos_ref[...], sin_ref[...]).astype(BF)


def q_kernel(heads, n_pieces, normed_ref, hgain_ref, cos_ref, sin_ref, *refs):
    pieces, refs = refs[:n_pieces], refs[n_pieces:]
    if n_pieces == 1:
        w_ref, (q_ref, lin_ref) = pieces[0], refs[-2:]
    else:
        q_ref, lin_ref, w_ref = refs[-3:]
        put_together(pieces, w_ref)
    both = mm(normed_ref[...], w_ref[...])
    for h in range(heads):
        cols = slice(h * HEAD_SIZE, (h + 1) * HEAD_SIZE)
        lin = both[:, cols]
        lin_ref[:, cols] = lin
        turned = turn(lin * rms(lin) * hgain_ref[...], cos_ref[...], sin_ref[...])
        q_ref[:, cols] = (turned * (SCALE * LOG2E)).astype(BF)


def pack_kernel(chunk, key_ref, value_ref, out_ref, down_ref, gate_ref, up_ref, kv_ref, od_ref, gu_ref):
    k_cols, o_cols, units = key_ref.shape[1], out_ref.shape[1], gate_ref.shape[1]
    kv_ref[:, :k_cols] = key_ref[...]
    kv_ref[:, k_cols:] = value_ref[...]
    od_ref[:, :o_cols] = out_ref[...]
    od_ref[:, o_cols:] = down_ref[...]
    for at in range(0, units, chunk):
        gu_ref[:, 2 * at : 2 * at + chunk] = gate_ref[:, at : at + chunk]
        gu_ref[:, 2 * at + chunk : 2 * at + 2 * chunk] = up_ref[:, at : at + chunk]


def pack(chunk, *weights):
    cols = [w.shape[1] for w in weights]
    wide = weights[0].shape[0]
    whole = lambda f: (0, 0)
    ins = [(w, w.shape, whole) for w in weights]
    sums = (cols[0] + cols[1], cols[2] + cols[3], cols[4] + cols[5])
    outs = [(shaped((wide, width), BF), (wide, width), whole) for width in sums]
    return call(functools.partial(pack_kernel, chunk), "pack", (1,), ins, outs)


def by_top_bit(slots):
    groups = {}
    for at, s in enumerate(slots):
        if s:
            groups.setdefault(1 << (s.bit_length() - 1), []).append(at)
    return groups


def slot_inputs(kv, rows):
    if isinstance(kv, tuple):
        return [(part, (rows, 128), lambda h, i: (0, h)) for part in kv]
    return [(kv, (2, rows, 128), lambda h, i: (0, 0, h))]


def take_slots(refs, pairs):
    taken = []
    for pair in pairs:
        if pair:
            taken.append((refs.pop(0), refs.pop(0)))
        else:
            ref = refs.pop(0)
            taken.append((ref.at[0], ref.at[1]))
    return taken


def fwd_kernel(plan, idx_ref, lo_ref, *refs):
    halves, slots, halos = plan["halves"], plan["slots"], plan["halos"]
    refs = list(refs)
    q_refs = [refs.pop(0) for _ in halves]
    slot_refs = take_slots(refs, plan["pairs"])
    halo_refs = take_slots(refs, [False] * len(halos))
    prior = [refs.pop(0) for _ in range(2 * len(halves))] if plan["carry"] else None
    if plan["last"]:
        if plan["alias"]:
            refs.pop(0)
        out_ref, lse_ref = refs[:2]
        refs = refs[2:]
    else:
        results, refs = refs[: 2 * len(halves)], refs[2 * len(halves) :]
    me, lo_first = idx_ref[0], idx_ref[1]
    rows = q_refs[0].shape[0]
    row = lax.broadcasted_iota(jnp.int32, (2 * rows, 1), 0)
    row = jnp.where(row >= rows, row - rows, row)
    col = lax.broadcasted_iota(jnp.int32, (1, rows), 1)
    for n, half in enumerate(halves):
        qs, acc, tot = refs[3 * n : 3 * n + 3]
        for g in range(2):
            cols, at = slice(g * HEAD_SIZE, (g + 1) * HEAD_SIZE), slice(g * rows, (g + 1) * rows)
            qs[at, :] = q_refs[n][:, cols]
            if prior is not None:
                acc[at, :] = prior[2 * n][:, cols]
                tot[at, :] = prior[2 * n + 1][:, cols]
        empty = [prior is None]

        def add(kv_ref, mask=None):
            scores = mm(qs[...], kv_ref[0][...], NT)
            if mask is not None:
                scores = jnp.where(mask, scores, MASKED)
            weights = jnp.exp2(scores)
            total = weights[:, :128]
            for at in range(128, weights.shape[1], 128):
                total = total + weights[:, at : at + 128]
            part = mm(weights.astype(BF), kv_ref[1][...])
            if empty[0]:
                acc[...] = part
                tot[...] = total
            else:
                acc[...] += part
                tot[...] += total
            empty[0] = False

        if half == 1:
            for kv_ref in slot_refs:
                add(kv_ref)
            low = jnp.concatenate([lo_ref[:, :1], lo_ref[:, :1]])
            for d, kv_ref in zip(halos, halo_refs):
                if d == 0:
                    add(kv_ref, (col <= row) & (col >= low))
                else:

                    @pl.when(lo_first < -(d - 1) * rows)
                    def _(d=d, kv_ref=kv_ref):
                        add(kv_ref, col - d * rows >= low)

        else:
            if 0 in slots:
                add(slot_refs[slots.index(0)], col <= row)
            for bit, group in by_top_bit(slots).items():

                @pl.when(jnp.bitwise_and(me, bit) != 0)
                def _(group=group):
                    for at in group:
                        add(slot_refs[at])

        if not plan["last"]:
            for g in range(2):
                cols, at = slice(g * HEAD_SIZE, (g + 1) * HEAD_SIZE), slice(g * rows, (g + 1) * rows)
                results[2 * n][:, cols] = acc[at, :]
                results[2 * n + 1][:, cols] = tot[at, :]
    if plan["last"]:
        qs, acc, tot = refs
        for g in range(2):
            cols, at = slice(g * HEAD_SIZE, (g + 1) * HEAD_SIZE), slice(g * rows, (g + 1) * rows)
            total = jnp.sum(tot[at, :], axis=1, keepdims=True)
            out_ref[:, cols] = (acc[at, :] / total).astype(BF)
            lse_ref[0, g : g + 1, :] = jnp.log2(jnp.sum(tot[at, :].T, axis=0, keepdims=True))


def attention_forward(halves, scalars, q, low, slots, halos, carry=None, last=None):
    rows, heads = q[0].shape[0], q[0].shape[1] // 256
    plan = dict(halves=halves, slots=list(slots), pairs=[isinstance(kv, tuple) for kv in slots.values()], halos=list(halos), carry=carry is not None,
                last=last is not None, alias=last is not None and last[0] is not None)
    part = lambda h, i: (0, h)
    ins = [(low, (rows, 128), lambda h, i: (0, 0))]
    ins += [(of_half, (rows, 256), part) for of_half in q]
    for kv in list(slots.values()) + list(halos.values()):
        ins += slot_inputs(kv, rows)
    if carry is not None:
        ins += [(c, (rows, 256), part) for c in carry]
    scratch, keep = [], {}
    for _ in halves:
        scratch += [pltpu.VMEM((2 * rows, 128), BF)] + [pltpu.VMEM((2 * rows, 128), F32)] * 2
    state = shaped((rows, heads * 256), F32)
    if last is None:
        outs = [(state, (rows, 256), part)] * (2 * len(halves))
    else:
        other = last[0]
        if other is not None:
            keep = {len(ins): 0}
            ins.append((other, None, None))
        half = halves[0]
        outs = [
            (shaped((2 * rows, heads * 256), BF), (rows, 256), lambda h, i: (half, h)),
            (shaped((heads, 8, rows), F32), (1, 8, rows), lambda h, i: (h, 0, 0)),
        ]
    return call(functools.partial(fwd_kernel, plan), "attend", (heads,), ins, outs, scratch,
                scalars=scalars, keep=keep)


def out_kernel(att_ref, w_ref, part_ref):
    part_ref[...] = mm(att_ref[...], w_ref[...], NT).astype(BF)


def out_projection(half, attended, w_rest):
    rows, cols = attended.shape[0] // 2, attended.shape[1]
    model = w_rest.shape[0]
    ins = [(attended, (rows, cols), lambda j: (half, 0)), (w_rest, (model // 2, cols), lambda j: (j, 0))]
    outs = [(shaped((rows, model), BF), (rows, model // 2), lambda j: (0, j))]
    return call(out_kernel, "out_projection", (2,), ins, outs)[0]


def bwd_kernel(plan, idx_ref, q_ref, do_ref, lse_ref, delta_ref, lo_ref, *refs):
    half, slots, halos = plan["half"], plan["slots"], plan["halos"]
    refs = list(refs)
    slot_refs = take_slots(refs, plan["pairs"])
    halo_refs = take_slots(refs, [False] * len(halos))
    prior_dq = refs.pop(0) if plan["carry"] else None
    prior = [refs.pop(0) for _ in slots] if plan["sum"] else None
    if plan["alias"]:
        refs.pop(0)
    dq_ref = refs.pop(0)
    slot_outs = [refs.pop(0) for _ in slots]
    halo_outs = [refs.pop(0) for _ in halos]
    qs, dos, lses, deltas, dq = refs
    me, lo_first = idx_ref[0], idx_ref[1]
    rows = q_ref.shape[0]
    for g in range(2):
        cols, at = slice(g * HEAD_SIZE, (g + 1) * HEAD_SIZE), slice(g * rows, (g + 1) * rows)
        qs[at, :] = q_ref[:, cols]
        dos[at, :] = do_ref[:, cols]
        lses[:, at] = lse_ref[0, g : g + 1, :]
        deltas[:, at] = delta_ref[0, g : g + 1, :]
    dq[...] = jnp.zeros_like(dq) if prior_dq is None else prior_dq[...]

    def block(kv_ref, out_ref, mask=None, before=None):
        keys = kv_ref[0][...]
        scores = mm(keys, qs[...], NT)
        dp = mm(kv_ref[1][...], dos[...], NT)
        scores = scores - lses[...]
        if mask is not None:
            scores = jnp.where(mask, scores, MASKED)
        probs = jnp.exp2(scores)
        ds = (probs * (dp - deltas[...])).astype(BF)
        dq[...] += mm(keys.T, ds)
        dk, dv = mm(ds, qs[...]) * LN2, mm(probs.astype(BF), dos[...])
        if before is not None:
            dk, dv = dk + before[0].astype(F32), dv + before[1].astype(F32)
        out_ref[0] = dk.astype(BF)
        out_ref[1] = dv.astype(BF)

    lane = lax.broadcasted_iota(jnp.int32, (1, 2 * rows), 1)
    lane = jnp.where(lane >= rows, lane - rows, lane)
    key = lax.broadcasted_iota(jnp.int32, (rows, 1), 0)

    def when(needed, kv_ref, out_ref, mask=None):
        @pl.when(needed)
        def _():
            block(kv_ref, out_ref, mask)

        @pl.when(jnp.logical_not(needed))
        def _():
            out_ref[...] = jnp.zeros_like(out_ref)

    low = lo_ref[:1, :]
    for d, kv_ref, out_ref in zip(halos, halo_refs, halo_outs):
        if d == 0:
            block(kv_ref, out_ref, (key <= lane) & (key >= low))
        else:
            when(lo_first < -(d - 1) * rows, kv_ref, out_ref, key - d * rows >= low)
    if half == 1:
        for at in range(len(slots)):
            block(slot_refs[at], slot_outs[at], None, prior[at] if prior else None)
    else:
        if 0 in slots:
            at = slots.index(0)
            block(slot_refs[at], slot_outs[at], key <= lane)
        for bit, group in by_top_bit(slots).items():

            @pl.when(jnp.bitwise_and(me, bit) != 0)
            def _(group=group):
                for at in group:
                    block(slot_refs[at], slot_outs[at])

            @pl.when(jnp.bitwise_and(me, bit) == 0)
            def _(group=group):
                for at in group:
                    slot_outs[at][...] = jnp.zeros_like(slot_outs[at])

    if plan["last"]:
        for g in range(2):
            cols = slice(g * HEAD_SIZE, (g + 1) * HEAD_SIZE)
            dq_ref[:, cols] = dq[:, g * rows : (g + 1) * rows].T * SCALE
    else:
        dq_ref[...] = dq[...]


def attention_backward(half, scalars, q, do, lse, delta, low, slots, halos, carry=None, prior=None, last=True, whole=None):
    rows, heads = q.shape[0], q.shape[1] // 256
    plan = dict(half=half, slots=list(slots), pairs=[isinstance(kv, tuple) for kv in slots.values()], halos=list(halos), carry=carry is not None,
                sum=prior is not None, last=last, alias=whole is not None)
    part = lambda h, i: (0, h)
    stat = lambda h, i: (h, 0, 0)
    kv_map = lambda h, i: (0, 0, h)
    ins = [
        (q, (rows, 256), part),
        (do, (rows, 256), part),
        (lse, (1, 8, rows), stat),
        (delta, (1, 8, rows), stat),
        (low, (8, 2 * rows), lambda h, i: (0, 0)),
    ]
    pieces = list(slots.values()) + list(halos.values())
    for kv in pieces:
        ins += slot_inputs(kv, rows)
    if carry is not None:
        ins.append((carry, (128, 2 * rows), lambda h, i: (h, 0)))
    if prior is not None:
        ins += [(prior[s], (2, rows, 128), kv_map) for s in slots]
    keep = {}
    if whole is not None:
        keep = {len(ins): 0}
        ins.append((whole, None, None))
    if last:
        outs = [(shaped((2 * rows, heads * 256), F32), (rows, 256), lambda h, i: (half, h))]
    else:
        outs = [(shaped((heads * 128, 2 * rows), F32), (128, 2 * rows), lambda h, i: (h, 0))]
    outs += [(shaped((2, rows, heads * 128), BF), (2, rows, 128), kv_map) for _ in pieces]
    scratch = [
        pltpu.VMEM((2 * rows, 128), BF),
        pltpu.VMEM((2 * rows, 128), BF),
        pltpu.VMEM((1, 2 * rows), F32),
        pltpu.VMEM((1, 2 * rows), F32),
        pltpu.VMEM((128, 2 * rows), F32),
    ]
    us = 4 + 6 * (len(slots) + len(halos)) if carry is not None or halos else 0.1
    results = call(functools.partial(bwd_kernel, plan), "attend_back", (heads,), ins, outs, scratch,
                   scalars=scalars, us=us, keep=keep)
    n = len(slots)
    return results[0], dict(zip(slots, results[1 : 1 + n])), dict(zip(halos, results[1 + n :]))


def ffn_kernel(x_ref, own_ref, got_ref, gain_ref, dy_ref, gu_ref, down_ref, *refs):
    resid_ref, normed_ref, hidden_ref, dgu_ref, out_ref, back_ref, normed, out_acc, back_acc = refs[-9:]
    step, steps = pl.program_id(0), pl.num_programs(0)

    @pl.when(step == 0)
    def _():
        resid = x_ref[...].astype(F32) + (own_ref[...].astype(F32) + got_ref[...].astype(F32))
        resid_ref[...] = resid
        normed[...] = (resid * rms(resid) * gain_ref[...]).astype(BF)
        normed_ref[...] = normed[...]
        out_acc[...] = jnp.zeros_like(out_acc)
        back_acc[...] = jnp.zeros_like(back_acc)

    wide = down_ref.shape[1]
    both = mm(normed[...], gu_ref[...])
    d_hidden = mm(dy_ref[...], down_ref[...])
    gate, up = both[:, :wide], both[:, wide:]
    sig = 1.0 / (1.0 + jnp.exp(-gate))
    silu = gate * sig
    hidden = (silu * up).astype(BF)
    hidden_ref[...] = hidden
    d_up = (d_hidden * silu).astype(BF)
    d_gate = (d_hidden * up * (sig + silu * (1.0 - sig))).astype(BF)
    dgu_ref[:, :wide] = d_gate
    dgu_ref[:, wide:] = d_up
    out_acc[...] += mm(hidden, down_ref[...], NT)
    back_acc[...] += mm(dgu_ref[...], gu_ref[...], NT)

    @pl.when(step == steps - 1)
    def _():
        out_ref[...] = out_acc[...].astype(BF)
        back_ref[...] = back_acc[...].astype(BF)


def feed_forward(half, x, own, got, gain, dy, w_od, w_gu, chunk, whole=None):
    rows, model = own.shape
    units = w_gu.shape[1] // 2
    steps = units // chunk
    mine, once = lambda f: (half, 0), lambda f: (0, 0)
    at_down = (w_od.shape[1] - units) // chunk
    block = (rows, model)
    ins = [
        (x, block, mine), (own, block, once), (got, block, once), (gain, (1, model), once), (dy, block, mine),
        (w_gu, (model, 2 * chunk), lambda f: (0, f)),
        (w_od, (model, chunk), lambda f: (0, at_down + f)),
    ]
    keep = {}
    if whole is not None:
        keep = {len(ins) + i: 1 + i for i in range(3)}
        ins += [(array, None, None) for array in whole]
    outs = [
        (shaped((rows, model), F32), block, once),
        (shaped((2 * rows, model), BF), block, mine),
        (shaped((2 * rows, units), BF), (rows, chunk), lambda f: (half, f)),
        (shaped((2 * rows, 2 * units), BF), (rows, 2 * chunk), lambda f: (half, f)),
        (shaped((rows, model), BF), block, once),
        (shaped((rows, model), BF), block, once),
    ]
    scratch = [pltpu.VMEM(block, BF), pltpu.VMEM(block, F32), pltpu.VMEM(block, F32)]
    return call(ffn_kernel, "feed_forward", (steps,), ins, outs, scratch, keep=keep)


def norm_back(grad, values, gain):
    scale = rms(values)
    unit = values * scale
    inner = grad * gain
    return scale * (inner - unit * jnp.mean(inner * unit, axis=-1, keepdims=True)), grad * unit


def lane_mean(values):
    width = values.shape[-1]
    ones = jnp.ones((width, width), BF)
    high = values.astype(BF)
    low = (values - high.astype(F32)).astype(BF)
    return (mm(high, ones) + mm(low, ones)) * (1.0 / width)


def head_norm_back(grad, values, gain):
    scale = lax.rsqrt(lane_mean(values * values) + EPSILON)
    unit = values * scale
    inner = grad * gain
    return scale * (inner - unit * lane_mean(inner * unit)), grad * unit


def row_blocks(rows):
    size = rows // 2 if rows % 512 == 0 else rows
    return size, rows // size


def add_up(ref, value):
    total = jnp.sum(value, axis=0, keepdims=True)

    @pl.when(pl.program_id(0) == 0)
    def _():
        ref[...] = total

    @pl.when(pl.program_id(0) > 0)
    def _():
        ref[...] += total


def mixed_kernel(heads, own_ref, got_ref, resid_ref, gain_ref, dy_ref, w_ref, att_ref, *refs):
    d_resid_ref, mixed_ref, datt_ref, delta_ref, dgain_ref = refs[-5:]
    grad = own_ref[...].astype(F32) + got_ref[...].astype(F32)
    d_norm, summand = norm_back(grad, resid_ref[...], gain_ref[...])
    add_up(dgain_ref, summand)
    d_resid = dy_ref[...].astype(F32) + d_norm
    d_resid_ref[...] = d_resid
    mixed_ref[...] = d_resid.astype(BF)
    datt_ref[...] = mm(mixed_ref[...], w_ref[...]).astype(BF)
    for h in range(heads):
        cols = slice(h * HEAD_SIZE, (h + 1) * HEAD_SIZE)
        product = datt_ref[:, cols].astype(F32) * att_ref[:, cols].astype(F32)
        delta_ref[h // 2, h % 2 : h % 2 + 1, :] = jnp.sum(product.T, axis=0, keepdims=True)


def mixed_back(half, own, got, resid, gain, dy, w_rest, o_cols, attended, whole=None):
    rows, model = own.shape
    heads = o_cols // HEAD_SIZE
    size, steps = row_blocks(rows)
    mine, here, once = lambda f: (half * steps + f, 0), lambda f: (f, 0), lambda f: (0, 0)
    block = (size, model)
    ins = [
        (own, block, here), (got, block, here), (resid, block, here), (gain, (1, model), once),
        (dy, block, mine), (w_rest, (model, o_cols), once), (attended, (size, o_cols), mine),
    ]
    keep = {}
    if whole is not None:
        keep = {len(ins): 1}
        ins.append((whole, None, None))
    outs = [
        (shaped((rows, model), F32), block, here),
        (shaped((2 * rows, model), BF), block, mine),
        (shaped((rows, o_cols), BF), (size, o_cols), here),
        (shaped((heads // 2, 8, rows), F32), (heads // 2, 8, size), lambda f: (0, 0, f)),
        (shaped((1, model), F32), (1, model), once),
    ]
    return call(functools.partial(mixed_kernel, heads), "mixed_back", (steps,), ins, outs, keep=keep)


def merge_kernel(two, got3, four, got5, far_k, far_v, to_x, to_y):
    for which in range(2):
        by_x = two[which].astype(F32) + got3[which].astype(F32)
        by_y = four[which].astype(F32) + got5[which].astype(F32)
        to_x[which] = (by_x + far_v[...].astype(F32) if which else by_x).astype(BF)
        to_y[which] = (by_y if which else by_y + far_k[...].astype(F32)).astype(BF)


def merge(*pieces):
    rows, cols = pieces[-1].shape
    size, steps = row_blocks(rows)
    ins = []
    for piece in pieces:
        if piece.ndim == 3:
            ins.append((piece, (2, size, cols), lambda f: (0, f, 0)))
        else:
            ins.append((piece, (size, cols), lambda f: (f, 0)))
    outs = [(shaped((2, rows, cols), BF), (2, size, cols), lambda f: (0, f, 0))] * 2
    return call(merge_kernel, "merge", (steps,), ins, outs)


def weight_kernel(left_ref, right_ref, *refs):
    refs[-1][...] = mm(left_ref[...], right_ref[...], TN).astype(BF)


def weight_grad(left, right, at, width, cols, whole=None):
    tokens, model = left.shape
    n = right.shape[1]
    ins = [(left, (tokens, model), lambda j: (0, 0)), (right, (tokens, cols), lambda j: (0, j))]
    keep = {}
    if whole is not None:
        keep = {len(ins): 0}
        ins.append((whole, None, None))
    outs = [(shaped((model, width), BF), (model, cols), lambda j: (0, at // cols + j))]
    return call(weight_kernel, "weight_grad", (n // cols,), ins, outs, keep=keep)[0]


def slot_weight_kernel(order, part_ref, left_ref, right_ref, low_ref, high_ref, total):
    total[...] = mm(left_ref[...], right_ref[...], TN)
    wide = total.shape[0] // len(order)
    for at, slot in enumerate(order):
        block = jnp.bitwise_xor(part_ref[0], slot)
        piece = total[pl.ds(pl.multiple_of(block * wide, wide), wide), :].astype(BF)
        out_ref, row = (low_ref, at) if at < len(order) // 2 else (high_ref, at - len(order) // 2)
        out_ref[row * wide : (row + 1) * wide, :] = piece


def slot_weight_grad(order, part, left, right):
    tokens, model = left.shape
    cols = right.shape[1]
    once = lambda j, i: (0, 0)
    ins = [(left, (tokens, model), once), (right, (tokens, cols), once)]
    half = shaped((model // 2, cols), BF)
    return call(functools.partial(slot_weight_kernel, order), "slot_weight_grad", (1,), ins,
                [(half, half.shape, once)] * 2, [pltpu.VMEM((model, cols), F32)], scalars=part[None])


def weight_halves_kernel(left_ref, right_ref, high_ref, low_ref):
    for half, out_ref in enumerate((high_ref, low_ref)):

        @pl.when(pl.program_id(0) == half)
        def _(out_ref=out_ref):
            out_ref[...] = mm(left_ref[...], right_ref[...], TN).astype(BF)


def weight_halves(left, right):
    tokens, model = left.shape
    cols = right.shape[1]
    once = lambda i: (0, 0)
    ins = [(left, (tokens, model // 2), lambda i: (0, 1 - i)), (right, (tokens, cols), once)]
    half = shaped((model // 2, cols), BF)
    return call(weight_halves_kernel, "weight_halves", (2,), ins, [(half, half.shape, once)] * 2)


def q_back_kernel(heads, dq_ref, lin_ref, gain_ref, cos_ref, sin_ref, w_ref, *refs):
    d_ref, part_ref, gains_ref = refs[-3:]
    cos, sin = cos_ref[...], sin_ref[...]
    total = jnp.zeros(cos.shape, F32)
    for h in range(heads):
        cols = slice(h * HEAD_SIZE, (h + 1) * HEAD_SIZE)
        grad, summand = head_norm_back(turn_back(dq_ref[:, cols], cos, sin), lin_ref[:, cols], gain_ref[...])
        d_ref[:, cols] = grad.astype(BF)
        total = total + summand
    part_ref[...] = mm(d_ref[...], w_ref[...], NT)
    add_up(gains_ref, total)


def q_back(dq, lin, gain, cos, sin, w):
    rows, cols = dq.shape
    model = w.shape[0]
    size, steps = row_blocks(rows)
    here, once = lambda f: (f, 0), lambda f: (0, 0)
    ins = [
        (dq, (size, cols), here), (lin, (size, cols), here), (gain, (1, HEAD_SIZE), once),
        (cos, (size, HEAD_SIZE), here), (sin, (size, HEAD_SIZE), here), (w, (model, cols), once),
    ]
    outs = [
        (shaped((rows, cols), BF), (size, cols), here),
        (shaped((rows, model), F32), (size, model), here),
        (shaped((1, HEAD_SIZE), F32), (1, HEAD_SIZE), once),
    ]
    kernel = functools.partial(q_back_kernel, cols // HEAD_SIZE)
    return call(kernel, "q_back", (steps,), ins, outs)


def kv_back_kernel(heads, n_keys, n_values, lin_ref, gain_ref, cos_ref, sin_ref, w_ref, slots_ref, q_part_ref, *refs):
    key_refs, value_refs = refs[:n_keys], refs[n_keys : n_keys + n_values]
    d_ref, part_ref, gains_ref = refs[-3:]
    cos, sin = cos_ref[...], sin_ref[...]
    width = heads * HEAD_SIZE

    def total(sources, which, cols):
        value = None
        for ref in sources:
            piece = ref[which, :, cols] if len(ref.shape) == 3 else ref[:, cols]
            value = piece.astype(F32) if value is None else value + piece.astype(F32)
        return value

    gains = jnp.zeros(cos.shape, F32)
    for h in range(heads):
        cols = slice(h * HEAD_SIZE, (h + 1) * HEAD_SIZE)
        grad, summand = head_norm_back(
            turn_back(total(key_refs, 0, cols), cos, sin), lin_ref[:, cols], gain_ref[...]
        )
        d_ref[:, cols] = grad.astype(BF)
        gains = gains + summand
    d_ref[:, width:] = total(value_refs, 1, slice(None)).astype(BF)
    part = (q_part_ref[...] + mm(d_ref[...], w_ref[...], NT)).astype(BF)
    part_ref[...] = mm(part, slots_ref[...], NT).astype(BF)
    add_up(gains_ref, gains)


def kv_back(half, keys, values, lin, gain, cos, sin, w, to_slots, q_part, whole=None):
    rows, cols = lin.shape
    model = w.shape[0]
    size, steps = row_blocks(rows)
    mine, here, once = lambda f: (half * steps + f, 0), lambda f: (f, 0), lambda f: (0, 0)
    ins = [
        (lin, (size, cols), here), (gain, (1, HEAD_SIZE), once), (cos, (size, HEAD_SIZE), mine),
        (sin, (size, HEAD_SIZE), mine), (w, (model, 2 * cols), once),
        (to_slots, (model, model), once), (q_part, (size, model), mine),
    ]
    for piece in list(keys) + list(values):
        if piece.ndim == 3:
            ins.append((piece, (2, size, cols), lambda f: (0, f, 0)))
        else:
            ins.append((piece, (size, cols), here))
    keep = {}
    if whole is not None:
        keep = {len(ins): 0}
        ins.append((whole, None, None))
    outs = [
        (shaped((2 * rows, 2 * cols), BF), (size, 2 * cols), mine),
        (shaped((rows, model), BF), (size, model), here),
        (shaped((1, HEAD_SIZE), F32), (1, HEAD_SIZE), once),
    ]
    kernel = functools.partial(kv_back_kernel, cols // HEAD_SIZE, len(keys), len(values))
    return call(kernel, "kv_back", (steps,), ins, outs, keep=keep, us=3 * (1 - half))


def tokens_kernel(own_ref, got_ref, x_ref, gain_ref, d_resid_ref, *refs):
    out_ref, dgain_ref = refs[-2:]
    grad = own_ref[...].astype(F32) + got_ref[...].astype(F32)
    d_norm, summand = norm_back(grad, x_ref[...].astype(F32), gain_ref[...])
    add_up(dgain_ref, summand)
    out_ref[...] = (d_resid_ref[...] + d_norm).astype(BF)


def tokens_back(half, own, got, x, gain, d_resid, whole=None):
    rows, model = own.shape
    size, steps = row_blocks(rows)
    mine, here, once = lambda f: (half * steps + f, 0), lambda f: (f, 0), lambda f: (0, 0)
    block = (size, model)
    ins = [(own, block, here), (got, block, here), (x, block, mine), (gain, (1, model), once), (d_resid, block, here)]
    keep = {}
    if whole is not None:
        keep = {len(ins): 0}
        ins.append((whole, None, None))
    outs = [(shaped((2 * rows, model), BF), block, mine), (shaped((1, model), F32), (1, model), once)]
    return call(tokens_kernel, "tokens_back", (steps,), ins, outs, keep=keep, us=20)


def share_kernel(chunk, ffn_ref, own_ref, got_ref, out_ref, gate_ref, up_ref, down_ref):
    units = gate_ref.shape[1]
    out_ref[...] = own_ref[...].astype(F32) + got_ref[...].astype(F32)
    for at in range(0, units, chunk):
        gate_ref[:, at : at + chunk] = ffn_ref[:, 2 * at : 2 * at + chunk].astype(F32)
        up_ref[:, at : at + chunk] = ffn_ref[:, 2 * at + chunk : 2 * at + 2 * chunk].astype(F32)
    down_ref[...] = ffn_ref[:, 2 * units :].astype(F32)


def unpack(chunk, ffn_share, out_grad):
    wide, units = ffn_share.shape[0], ffn_share.shape[1] // 3
    o_cols = out_grad[0].shape[1]
    whole = lambda f: (0, 0)
    ins = [(ffn_share, ffn_share.shape, whole)] + [(grad, (wide, o_cols), whole) for grad in out_grad]
    outs = [(shaped((wide, cols), F32), (wide, cols), whole) for cols in (o_cols, units, units, units)]
    return call(functools.partial(share_kernel, chunk), "unpack", (1,), ins, outs)


def layer_kernel(resid_ref, own_ref, got_ref, *refs):
    refs[-1][...] = (resid_ref[...] + (own_ref[...].astype(F32) + got_ref[...].astype(F32))).astype(BF)


def add_layer(half, resid, own, got, whole=None):
    rows, model = resid.shape
    size, steps = row_blocks(rows)
    here, mine = lambda f: (f, 0), lambda f: (half * steps + f, 0)
    ins = [(array, (size, model), here) for array in (resid, own, got)]
    keep = {}
    if whole is not None:
        keep = {len(ins): 0}
        ins.append((whole, None, None))
    outs = [(shaped((2 * rows, model), BF), (size, model), mine)]
    return call(layer_kernel, "add_layer", (steps,), ins, outs, keep=keep)[0]


def swap(value, axis, bit):
    size = lax.axis_size(axis)
    return lax.ppermute(value, axis, [(i, i ^ bit) for i in range(size)])


def shift(value, by):
    size = lax.axis_size("ctx")
    return lax.ppermute(value, "ctx", [(i, i + by) for i in range(size) if 0 <= i + by < size])


def add_low(left, right):
    return (left.astype(F32) + right.astype(F32)).astype(BF)


def butterfly(value, axes, gates=()):
    gates = list(gates)
    for axis in axes:
        bit = 1
        while bit < lax.axis_size(axis):
            got = swap(value, axis, bit)
            value = value + (after(got, gates.pop(0)) if gates else got)
            bit *= 2
    return value


def after(value, *others):
    return lax.optimization_barrier((value, *others))[0]


def rotary_tables(position):
    half_dim = HEAD_SIZE // 2
    inverse_freq = jnp.exp(jnp.arange(half_dim, dtype=F32) * (-math.log(ROPE_BASE) / half_dim))
    angles = position.astype(F32)[:, None] * inverse_freq[None, :]
    cosine, sine = jnp.cos(angles), jnp.sin(angles)
    return jnp.concatenate([cosine, cosine], axis=-1), jnp.concatenate([-sine, sine], axis=-1)


def body(
    tokens,
    cont_lengths,
    attn_gain,
    ffn_gain,
    query_gain,
    key_gain,
    w_query,
    key_weight,
    value_weight,
    w_out,
    w_gate,
    w_up,
    w_down,
    cotangent,
):
    ctx_size = lax.axis_size("ctx")
    weight_axes = ("shard", "ctx")
    parts = lax.axis_size("shard") * ctx_size
    me = lax.axis_index("ctx")
    part = lax.axis_index("shard") * ctx_size + me
    rows, model = tokens.shape[0] // 2, tokens.shape[1]
    n_halo = 1 + -(-(LONGEST - 1) // rows)
    lengths = cont_lengths[0]

    bits = [("shard", 1)] + [("ctx", 1 << i) for i in range(1, ctx_size.bit_length() - 1)] + [("ctx", 1)]
    order = [0]
    for axis, bit in bits:
        order += [j ^ (bit * ctx_size if axis == "shard" else bit) for j in order]
    wide, narrow = attn_gain.shape[0], query_gain.shape[0]
    q_cols, k_cols = w_query.shape[1], key_weight.shape[1]
    o_cols, units = w_out.shape[0], w_gate.shape[1]
    heads, kv_heads = q_cols // HEAD_SIZE, k_cols // HEAD_SIZE
    chunk = math.gcd(units, 512)

    def gather_first(piece, *gate):
        return jnp.concatenate([piece, after(swap(piece, "shard", 1), *gate)]) if ctx_size == 8 else piece

    def gather_near(one, *gate):
        if ctx_size != 8:
            for axis, bit in bits:
                one = jnp.concatenate([one, swap(one, axis, bit)])
            return [one]
        return [one] + [after(swap(one, "ctx", bit), *gate) for bit in (2, 4, 6)]

    def gather_far(near, *gate):
        if ctx_size != 8:
            return near
        return near + [after(swap(piece, "ctx", 1), *gate) for piece in near]

    def scatter_rows(low, high, late):
        total = add_low(low, after(swap(high, "ctx", 1), late))
        if ctx_size != 8:
            for axis, bit in bits[-2:0:-1]:
                size = total.shape[0] // 2
                total = add_low(total[:size], swap(total[size:], axis, bit))
            return (total,)
        size, cut = total.shape[0] // 4, total.shape[1] // 2
        own, by_x, by_y, far = (total[i * size : (i + 1) * size] for i in range(4))
        left, right = swap(far[:, :cut], "ctx", 2), swap(far[:, cut:], "ctx", 4)
        return own, by_x, by_y, left, right

    def scatter_more(stage, late):
        if ctx_size != 8:
            return stage
        own, by_x, by_y, left, right = stage
        left, right = after(left, late), after(right, late)
        cut = left.shape[1]
        by_x = jnp.concatenate([by_x[:, :cut], add_low(by_x[:, cut:], right)], axis=1)
        by_y = jnp.concatenate([add_low(by_y[:, :cut], left), by_y[:, cut:]], axis=1)
        return lax.optimization_barrier((own, by_x, by_y))[0], swap(by_x, "ctx", 2), swap(by_y, "ctx", 4)

    def scatter_sum(stage, late):
        total = stage[0].astype(F32)
        for piece in stage[1:]:
            total = total + after(piece, late).astype(F32)
        total, size = total.astype(BF), total.shape[0] // 2
        return total, swap(total[size:], "shard", 1)

    kv_piece, od_piece, gu_piece = pack(
        chunk, key_weight, value_weight, w_out.T, w_down.T, w_gate, w_up
    )
    kv_one = gather_first(kv_piece)
    kv_near = gather_near(kv_one)
    kv_pieces = gather_far(kv_near)
    q_one = gather_first(after(w_query, kv_one), kv_near[-1])
    w_od = lax.all_gather(od_piece, weight_axes, axis=0, tiled=True)
    gains = jnp.concatenate([attn_gain, ffn_gain, query_gain, key_gain])[None]
    gains = jnp.where(jnp.arange(parts)[:, None] == part, gains, jnp.zeros((), BF))
    gains = gains + after(swap(gains, "ctx", 1), kv_piece)
    for at, (axis, bit) in enumerate(bits[:-1]):
        gains = gains + after(swap(gains, axis, bit), (kv_one, kv_near[-1], kv_near[-1])[min(at, 2)])
    gains = gains.astype(F32)
    gain_one = gains[:, :wide].reshape(1, -1)
    gain_two = gains[:, wide : 2 * wide].reshape(1, -1)
    gain_q = gains[:, 2 * wide : 2 * wide + narrow].reshape(1, -1)
    gain_k = gains[:, 2 * wide + narrow :].reshape(1, -1)
    source = jnp.bitwise_xor(part, jnp.array(order, jnp.int32))[:, None] * wide + jnp.arange(wide, dtype=jnp.int32)
    to_slots = (jnp.arange(model, dtype=jnp.int32)[:, None] == source.reshape(1, -1)).astype(BF)
    tokens_s = mm(after(tokens, q_one), to_slots).astype(BF)
    gain_one_s = mm(gain_one.astype(BF), to_slots)

    cont_at = me * rows + jnp.arange(rows, dtype=jnp.int32)
    cont_ends = jnp.cumsum(lengths)
    starts = cont_ends - lengths
    seg = jnp.sum((cont_ends[None, :] <= cont_at[:, None]).astype(jnp.int32), axis=1)
    numbers = jnp.arange(lengths.shape[0], dtype=jnp.int32)
    first = jnp.sum(jnp.where(numbers[None, :] == seg[:, None], starts[None, :], 0), axis=1)
    position = jnp.concatenate([me * rows + jnp.arange(rows, dtype=jnp.int32), PROMPT + cont_at - first])
    low = first - me * rows
    low_col = jnp.broadcast_to(low[:, None], (rows, 128))
    low_row = jnp.broadcast_to(jnp.concatenate([low, low])[None, :], (8, 2 * rows))
    scalars = jnp.stack([me, low[0]])
    cos, sin = rotary_tables(position)

    once = lambda f: (0, 0)

    def weight_inputs(pieces):
        return [(piece, piece.shape, once) for piece in pieces]

    def keys_values(half, gain, pieces, whole=None):
        mine = lambda f: (half, 0)
        ins = [
            (tokens_s, (rows, model), mine), (gain, (1, model), once), (gain_k, (1, HEAD_SIZE), once),
            (cos, (rows, HEAD_SIZE), mine), (sin, (rows, HEAD_SIZE), mine), *weight_inputs(pieces),
        ]
        keep = {}
        if whole is not None:
            keep = {len(ins): 0}
            ins.append((whole, None, None))
        outs = [
            (shaped((2 * rows, model), BF), (rows, model), mine),
            (shaped((2, rows, k_cols), BF), (2, rows, k_cols), lambda f: (0, 0, 0)),
            (shaped((rows, k_cols), F32), (rows, k_cols), once),
        ]
        if len(pieces) > 1:
            outs.append((shaped((model, 2 * k_cols), BF), (model, 2 * k_cols), once))
        return call(functools.partial(kv_kernel, kv_heads, len(pieces)), "keys_values", (1,), ins, outs, keep=keep)

    q_near = gather_near(q_one, kv_pieces[-1])
    normed, kv_p, k_lin_p, *w_kv = keys_values(0, after(gain_one_s, *q_near[1:]), kv_pieces)
    (w_kv,) = w_kv or kv_pieces
    normed, kv_c, k_lin_c = keys_values(1, after(gain_one_s, kv_p), [w_kv], normed)
    q_pieces = gather_far(q_near, kv_c)

    def queries(half, gain, pieces, whole=None):
        mine = lambda f: (half, 0)
        ins = [
            (normed, (rows, model), mine), (gain, (1, HEAD_SIZE), once),
            (cos, (rows, HEAD_SIZE), mine), (sin, (rows, HEAD_SIZE), mine), *weight_inputs(pieces),
        ]
        keep = {}
        if whole is not None:
            keep = {len(ins): 1}
            ins.append((whole, None, None))
        outs = [
            (shaped((rows, q_cols), BF), (rows, q_cols), once),
            (shaped((2 * rows, q_cols), F32), (rows, q_cols), mine),
        ]
        if len(pieces) > 1:
            outs.append((shaped((model, q_cols), BF), (model, q_cols), once))
        return call(functools.partial(q_kernel, heads, len(pieces)), "queries", (1,), ins, outs, keep=keep)

    q_c, q_lin, *w_q = queries(1, gain_q, q_pieces)
    (w_q,) = w_q or q_pieces
    q_p, q_lin = queries(0, after(gain_q, q_c), [w_q], q_lin)

    def pick(source, wanted):
        return {s: source[s] for s in source if s in wanted}

    near, middle, far = (0, 1), (2, 3, 4, 5), tuple(range(6, ctx_size))
    slots, halos = {0: kv_p}, {0: kv_c}
    odd = (me % 2) == 1
    if ctx_size == 8:
        slots[1], slots[2], slots[4] = (swap(kv_p, "ctx", bit) for bit in (1, 2, 4))
    else:
        both, bit = kv_p[None], 1
        while bit < ctx_size:
            both = jnp.concatenate([both, swap(both, "ctx", bit)])
            bit *= 2
        slots = {s: both[s] for s in range(ctx_size)}
        halos.update({d: shift(kv_c, d) for d in range(1, n_halo)})
    ready = ()
    if ctx_size == 8:
        slots[2], slots[4] = after(slots[2], q_p), after(slots[4], q_p)
        far_k, far_v = swap(slots[4][0], "ctx", 2), swap(slots[2][1], "ctx", 4)
        slots[3], slots[5] = swap(slots[2], "ctx", 1), swap(slots[4], "ctx", 1)
        halos[2] = shift(after(kv_c, slots[2]), 2)
        gu_piece = after(gu_piece, slots[2], slots[4])
        ready = (slots[2], slots[4])
    w_gu = lax.all_gather(after(gu_piece, w_od), weight_axes, axis=0, tiled=True)
    c_state = attention_forward(
        (1,), after(scalars, *ready), (q_c,), low_col, pick(slots, near), pick(halos, (0,))
    )
    if ctx_size == 8:
        slots[6] = after(far_k, c_state[0]), after(far_v, c_state[0])
        slots[7] = tuple(swap(part, "ctx", 1) for part in slots[6])
    attended, lse_p = attention_forward(
        (0,), after(scalars, c_state[0]), (q_p,), low_col, slots, {}, None, (None,)
    )
    part_p = out_projection(0, attended, w_od)
    got_p = swap(part_p, "tensor", 1)
    if ctx_size == 8:
        halos[1] = swap(jnp.where(odd, after(halos[2], part_p), kv_c), "ctx", 1)
    attended, lse_c = attention_forward(
        (1,), after(scalars, part_p), (q_c,), low_col, pick(slots, middle + far), pick(halos, range(1, n_halo)),
        c_state, (attended,),
    )
    part_c = out_projection(1, attended, w_od)
    got_c = swap(part_c, "tensor", 1)

    resid_p, *whole, out_p, back_p = feed_forward(
        0, tokens, part_p, got_p, after(gain_two, part_c), cotangent, w_od, w_gu, chunk
    )
    back_got_p = swap(back_p, "tensor", 1)
    resid_c, *whole, out_c, back_c = feed_forward(
        1, tokens, part_c, got_c, after(gain_two, back_p), cotangent, w_od, w_gu, chunk, whole
    )
    back_got_c = swap(back_c, "tensor", 1)
    normed_ffn, hidden, d_gu = whole
    ffn_grads = weight_grad(normed_ffn, d_gu, 0, 3 * units, 2 * chunk)
    ffn_grads = weight_grad(cotangent, hidden, 2 * units, 3 * units, chunk, ffn_grads)
    ffn_share = lax.psum_scatter(ffn_grads, weight_axes, scatter_dimension=0, tiled=True)
    d_resid_p, d_mixed, d_att_p, delta_p, d_two_p = mixed_back(
        0, back_p, back_got_p, resid_p, after(gain_two, ffn_grads), cotangent, w_od, o_cols, attended
    )

    of_rows = [(d_att_p, lse_p, delta_p)]

    def back_rows(half, deps, slots, halos, carry, prior=None, whole=None, last=False):
        do, lse, delta = of_rows[half]
        return attention_backward(
            half, after(scalars, *deps), (q_p, q_c)[half], do, lse, delta, low_row, slots, halos, carry, prior, last, whole
        )

    dq_p, prior, _ = back_rows(0, (d_att_p,), pick(slots, far), {}, None)
    d_resid_c, d_mixed, d_att_c, delta_c, d_two_c = mixed_back(
        1, back_c, back_got_c, resid_c, after(gain_two, dq_p), cotangent, w_od, o_cols, attended, d_mixed
    )
    of_rows.append((d_att_c, lse_c, delta_c))
    out_low, out_high = slot_weight_grad(order, part, d_mixed, attended)
    out_p, out_c = after(out_p, out_low), after(out_c, out_low)
    out_got_p, out_got_c = swap(out_p, "tensor", 1), swap(out_c, "tensor", 1)
    dq_c, _, g_halo = back_rows(1, (out_low,), {}, halos, None)
    out_grad = scatter_rows(out_low, out_high, dq_c)
    if ctx_size == 8:
        near_one = swap(g_halo[1], "ctx", 1)
    dq_c, g, _ = back_rows(1, (dq_c, out_grad[0]), pick(slots, far), {}, dq_c, prior)
    out_grad = scatter_more(out_grad, dq_c)
    zero = jnp.zeros((), BF)
    ready = ()
    if ctx_size == 8:
        got7 = swap(g[7], "ctx", 1)
        near_one = after(near_one, dq_c)
        two_back = add_low(g_halo[2], jnp.where(odd, near_one, zero))
        halo_two = shift(two_back, -2)
        halo_near = jnp.where(odd, zero, near_one)
        ready = (two_back, halo_near)
    dq, prior, _ = back_rows(0, (dq_c, out_grad[0], *ready), pick(slots, near + middle), {}, dq_p, None, None, True)
    if ctx_size == 8:
        g6 = add_low(g[6], after(got7, dq))
        far_k, far_v = swap(g6[0], "ctx", 2), swap(g6[1], "ctx", 4)
        ready = (g6,)
    out_grad = scatter_sum(out_grad, dq)
    dq_c, more, _ = back_rows(1, (dq, out_grad[0], *ready), pick(slots, middle), {}, dq_c, prior)
    g.update(more)
    if ctx_size == 8:
        got3, got5 = swap(g[3], "ctx", 1), swap(g[5], "ctx", 1)
        ready = (halo_two,)
    dq, more, _ = back_rows(1, (dq_c, out_got_p, out_got_c, *ready), pick(slots, near), {}, dq_c, prior, dq, True)
    g.update(more)
    if ctx_size == 8:
        got1 = swap(g[1], "ctx", 1)
        far_k, far_v, got3, got5 = (after(v, dq, out_grad[1], ffn_share) for v in (far_k, far_v, got3, got5))
        to_x, to_y = merge(g[2], got3, g[4], got5, far_k, far_v)
        ready = (to_x,)
        keys_p = values_p = [g[0], got1, swap(to_x, "ctx", 2), swap(to_y, "ctx", 4)]
        keys_c = values_c = [g_halo[0], halo_near, halo_two]
    else:
        both = jnp.stack([g[s] for s in range(ctx_size)])
        while both.shape[0] > 1:
            size = both.shape[0] // 2
            both = add_low(both[:size], swap(both[size:], "ctx", size))
        keys_p = values_p = [both[0]]
        keys_c = values_c = [g_halo[0]] + [shift(g_halo[d], -d) for d in range(1, n_halo)]

    d_q, q_part, q_heads = q_back(dq, q_lin, after(gain_q, dq, *ready), cos, sin, w_q)
    d_kv, into_c, k_heads_c = kv_back(
        1, keys_c, values_c, k_lin_c, after(gain_k, q_part), cos, sin, w_kv, to_slots, q_part
    )
    into_got_c = swap(into_c, "tensor", 1)
    q_high, q_low = weight_halves(normed, after(d_q, into_c))
    d_kv, into_p, k_heads_p = kv_back(
        0, keys_p, values_p, k_lin_p, after(gain_k, q_low), cos, sin, w_kv, to_slots, q_part, d_kv
    )
    into_got_p = swap(into_p, "tensor", 1)
    q_grad = scatter_rows(q_low, q_high, into_p)
    kv_high, kv_low = weight_halves(normed, after(d_kv, q_grad[0]))
    q_grad = scatter_more(q_grad, kv_low)
    heads = jnp.concatenate([q_heads, k_heads_c + k_heads_p], axis=1)
    heads_got = swap(heads, "tensor", 1)
    grad_tokens, d_one_c = tokens_back(1, into_c, into_got_c, tokens, after(gain_one, kv_low, q_grad[0]), d_resid_c)
    out_share, gate_share, up_share, down_share = unpack(chunk, after(ffn_share, d_one_c), out_grad)
    q_grad = scatter_sum(q_grad, gate_share)
    kv_grad = scatter_rows(kv_low, kv_high, gate_share)
    layer_out = add_layer(0, after(resid_p, kv_grad[0], q_grad[0]), out_p, out_got_p)
    kv_grad = scatter_more(kv_grad, layer_out)
    layer_out = add_layer(1, after(resid_c, kv_grad[0]), out_c, out_got_c, layer_out)
    q_share = add_low(q_grad[0][:wide], after(q_grad[1], layer_out)).astype(F32)
    kv_grad = scatter_sum(kv_grad, layer_out)
    grad_tokens, d_one_p = tokens_back(
        0, into_p, into_got_p, tokens, after(gain_one, kv_grad[0], q_share), d_resid_p, grad_tokens
    )
    heads = heads + after(heads_got, d_one_p)
    late = jnp.concatenate([d_one_c + d_one_p, heads, d_two_c + d_two_p], axis=1)
    kv_share = add_low(kv_grad[0][:wide], after(kv_grad[1], d_one_p)).astype(F32)
    late = butterfly(late, ("ctx", "shard"), (d_one_p, kv_share))

    def own_gain(value, size):
        return lax.dynamic_index_in_dim(value.reshape(parts, size), part, 0, keepdims=False)

    return (
        layer_out,
        grad_tokens,
        own_gain(late[:, :model], wide),
        own_gain(late[:, model + 2 * HEAD_SIZE :], wide),
        own_gain(late[:, model : model + HEAD_SIZE], narrow),
        own_gain(late[:, model + HEAD_SIZE : model + 2 * HEAD_SIZE], narrow),
        q_share,
        kv_share[:, :k_cols],
        kv_share[:, k_cols:],
        out_share.T,
        gate_share,
        up_share,
        down_share.T,
    )


def solution(mesh):
    split = ("shard", "ctx")
    rows, gain = P(split, None), P(split)
    into, out_of = P(split, "tensor"), P("tensor", split)
    in_specs = (rows, P("shard", None)) + (gain,) * 4 + (into,) * 3 + (out_of,)
    in_specs += (into, into, out_of, rows)
    out_specs = (rows, rows) + (gain,) * 4 + (into,) * 3 + (out_of, into, into, out_of)
    return jax.shard_map(body, mesh=mesh, in_specs=in_specs, out_specs=out_specs, check_vma=False)
```

```python
import functools
import math

import jax
import jax.numpy as jnp
from jax import lax
from jax.experimental import pallas as pl
from jax.experimental.pallas import tpu as pltpu
from jax.sharding import PartitionSpec as P

HEAD_SIZE = 128
PROMPT = 4096
CONT_TOK = 4096
LONGEST = 1024

EPSILON = 1e-06
ROPE_BASE = 1000000.0
MASKED = -1e30
LOG2E = math.log2(math.e)
LN2 = math.log(2.0)
SCALE = 1.0 / math.sqrt(HEAD_SIZE)

BF = jnp.bfloat16
F32 = jnp.float32
NN = (((1,), (0,)), ((), ()))
NT = (((1,), (1,)), ((), ()))
TN = (((0,), (0,)), ((), ()))
MIB = 2**20
STATED = 3e9


def mm(left, right, dims=NN):
    return lax.dot_general(left, right, dims, preferred_element_type=F32)


def shaped(dims, kind):
    return jax.ShapeDtypeStruct(dims, kind)


def call(kernel, name, grid, ins, outs, scratch=(), vmem=56, scalars=None, keep=None, us=0):
    in_specs, arrays = [], []
    for array, block, index in ins:
        arrays.append(array)
        in_specs.append(pl.BlockSpec(memory_space=pl.ANY) if block is None else pl.BlockSpec(block, index))
    lead = 0 if scalars is None else 1
    return pl.pallas_call(
        kernel,
        grid_spec=pltpu.PrefetchScalarGridSpec(
            num_scalar_prefetch=lead,
            grid=grid,
            in_specs=in_specs,
            out_specs=[pl.BlockSpec(block, index) for _, block, index in outs],
            scratch_shapes=list(scratch),
        ),
        out_shape=[shape for shape, _, _ in outs],
        input_output_aliases={a + lead: b for a, b in (keep or {}).items()},
        compiler_params=pltpu.CompilerParams(vmem_limit_bytes=vmem * MIB),
        cost_estimate=pl.CostEstimate(flops=int(us * STATED), bytes_accessed=0, transcendentals=0),
        name=name,
    )(*([] if scalars is None else [scalars]), *arrays)


def rms(values):
    return lax.rsqrt(jnp.mean(values * values, axis=-1, keepdims=True) + EPSILON)


def turn(values, cos, sin):
    return values * cos + pltpu.roll(values, HEAD_SIZE // 2, 1) * sin


def turn_back(values, cos, sin):
    return values * cos - pltpu.roll(values, HEAD_SIZE // 2, 1) * sin


def put_together(pieces, whole_ref):
    rows = whole_ref.shape[0] // len(pieces)
    for at, piece in enumerate(pieces):
        whole_ref[at * rows : (at + 1) * rows, :] = piece[...]


def kv_kernel(heads, n_pieces, x_ref, gain_ref, hgain_ref, cos_ref, sin_ref, *refs):
    pieces, refs = refs[:n_pieces], refs[n_pieces:]
    if n_pieces == 1:
        w_ref, (normed_ref, kv_ref, lin_ref) = pieces[0], refs[-3:]
    else:
        normed_ref, kv_ref, lin_ref, w_ref = refs[-4:]
        put_together(pieces, w_ref)
    x = x_ref[...].astype(F32)
    normed_ref[...] = (x * rms(x) * gain_ref[...]).astype(BF)
    both = mm(normed_ref[...], w_ref[...])
    width = heads * HEAD_SIZE
    kv_ref[1] = both[:, width:].astype(BF)
    for h in range(heads):
        cols = slice(h * HEAD_SIZE, (h + 1) * HEAD_SIZE)
        lin = both[:, cols]
        lin_ref[:, cols] = lin
        kv_ref[0, :, cols] = turn(lin * rms(lin) * hgain_ref[...], cos_ref[...], sin_ref[...]).astype(BF)


def q_kernel(heads, n_pieces, normed_ref, hgain_ref, cos_ref, sin_ref, *refs):
    pieces, refs = refs[:n_pieces], refs[n_pieces:]
    if n_pieces == 1:
        w_ref, (q_ref, lin_ref) = pieces[0], refs[-2:]
    else:
        q_ref, lin_ref, w_ref = refs[-3:]
        put_together(pieces, w_ref)
    both = mm(normed_ref[...], w_ref[...])
    for h in range(heads):
        cols = slice(h * HEAD_SIZE, (h + 1) * HEAD_SIZE)
        lin = both[:, cols]
        lin_ref[:, cols] = lin
        turned = turn(lin * rms(lin) * hgain_ref[...], cos_ref[...], sin_ref[...])
        q_ref[:, cols] = (turned * (SCALE * LOG2E)).astype(BF)


def pack_kernel(chunk, key_ref, value_ref, out_ref, down_ref, gate_ref, up_ref, kv_ref, od_ref, gu_ref):
    k_cols, o_cols, units = key_ref.shape[1], out_ref.shape[1], gate_ref.shape[1]
    kv_ref[:, :k_cols] = key_ref[...]
    kv_ref[:, k_cols:] = value_ref[...]
    od_ref[:, :o_cols] = out_ref[...]
    od_ref[:, o_cols:] = down_ref[...]
    for at in range(0, units, chunk):
        gu_ref[:, 2 * at : 2 * at + chunk] = gate_ref[:, at : at + chunk]
        gu_ref[:, 2 * at + chunk : 2 * at + 2 * chunk] = up_ref[:, at : at + chunk]


def pack(chunk, *weights):
    cols = [w.shape[1] for w in weights]
    wide = weights[0].shape[0]
    whole = lambda f: (0, 0)
    ins = [(w, w.shape, whole) for w in weights]
    sums = (cols[0] + cols[1], cols[2] + cols[3], cols[4] + cols[5])
    outs = [(shaped((wide, width), BF), (wide, width), whole) for width in sums]
    return call(functools.partial(pack_kernel, chunk), "pack", (1,), ins, outs)


def by_top_bit(slots):
    groups = {}
    for at, s in enumerate(slots):
        if s:
            groups.setdefault(1 << (s.bit_length() - 1), []).append(at)
    return groups


def slot_inputs(kv, rows):
    if isinstance(kv, tuple):
        return [(part, (rows, 128), lambda h, i: (0, h)) for part in kv]
    return [(kv, (2, rows, 128), lambda h, i: (0, 0, h))]


def take_slots(refs, pairs):
    taken = []
    for pair in pairs:
        if pair:
            taken.append((refs.pop(0), refs.pop(0)))
        else:
            ref = refs.pop(0)
            taken.append((ref.at[0], ref.at[1]))
    return taken


def fwd_kernel(plan, idx_ref, lo_ref, *refs):
    halves, slots, halos = plan["halves"], plan["slots"], plan["halos"]
    refs = list(refs)
    q_refs = [refs.pop(0) for _ in halves]
    slot_refs = take_slots(refs, plan["pairs"])
    halo_refs = take_slots(refs, [False] * len(halos))
    prior = [refs.pop(0) for _ in range(2 * len(halves))] if plan["carry"] else None
    if plan["last"]:
        if plan["alias"]:
            refs.pop(0)
        out_ref, lse_ref = refs[:2]
        refs = refs[2:]
    else:
        results, refs = refs[: 2 * len(halves)], refs[2 * len(halves) :]
    me, lo_first = idx_ref[0], idx_ref[1]
    rows = q_refs[0].shape[0]
    row = lax.broadcasted_iota(jnp.int32, (2 * rows, 1), 0)
    row = jnp.where(row >= rows, row - rows, row)
    col = lax.broadcasted_iota(jnp.int32, (1, rows), 1)
    for n, half in enumerate(halves):
        qs, acc, tot = refs[3 * n : 3 * n + 3]
        for g in range(2):
            cols, at = slice(g * HEAD_SIZE, (g + 1) * HEAD_SIZE), slice(g * rows, (g + 1) * rows)
            qs[at, :] = q_refs[n][:, cols]
            if prior is not None:
                acc[at, :] = prior[2 * n][:, cols]
                tot[at, :] = prior[2 * n + 1][:, cols]
        empty = [prior is None]

        def add(kv_ref, mask=None):
            scores = mm(qs[...], kv_ref[0][...], NT)
            if mask is not None:
                scores = jnp.where(mask, scores, MASKED)
            weights = jnp.exp2(scores)
            total = weights[:, :128]
            for at in range(128, weights.shape[1], 128):
                total = total + weights[:, at : at + 128]
            part = mm(weights.astype(BF), kv_ref[1][...])
            if empty[0]:
                acc[...] = part
                tot[...] = total
            else:
                acc[...] += part
                tot[...] += total
            empty[0] = False

        if half == 1:
            for kv_ref in slot_refs:
                add(kv_ref)
            low = jnp.concatenate([lo_ref[:, :1], lo_ref[:, :1]])
            for d, kv_ref in zip(halos, halo_refs):
                if d == 0:
                    add(kv_ref, (col <= row) & (col >= low))
                else:

                    @pl.when(lo_first < -(d - 1) * rows)
                    def _(d=d, kv_ref=kv_ref):
                        add(kv_ref, col - d * rows >= low)

        else:
            if 0 in slots:
                add(slot_refs[slots.index(0)], col <= row)
            for bit, group in by_top_bit(slots).items():

                @pl.when(jnp.bitwise_and(me, bit) != 0)
                def _(group=group):
                    for at in group:
                        add(slot_refs[at])

        if not plan["last"]:
            for g in range(2):
                cols, at = slice(g * HEAD_SIZE, (g + 1) * HEAD_SIZE), slice(g * rows, (g + 1) * rows)
                results[2 * n][:, cols] = acc[at, :]
                results[2 * n + 1][:, cols] = tot[at, :]
    if plan["last"]:
        qs, acc, tot = refs
        for g in range(2):
            cols, at = slice(g * HEAD_SIZE, (g + 1) * HEAD_SIZE), slice(g * rows, (g + 1) * rows)
            total = jnp.sum(tot[at, :], axis=1, keepdims=True)
            out_ref[:, cols] = (acc[at, :] / total).astype(BF)
            lse_ref[0, g : g + 1, :] = jnp.log2(jnp.sum(tot[at, :].T, axis=0, keepdims=True))


def attention_forward(halves, scalars, q, low, slots, halos, carry=None, last=None):
    rows, heads = q[0].shape[0], q[0].shape[1] // 256
    plan = dict(halves=halves, slots=list(slots), pairs=[isinstance(kv, tuple) for kv in slots.values()], halos=list(halos), carry=carry is not None,
                last=last is not None, alias=last is not None and last[0] is not None)
    part = lambda h, i: (0, h)
    ins = [(low, (rows, 128), lambda h, i: (0, 0))]
    ins += [(of_half, (rows, 256), part) for of_half in q]
    for kv in list(slots.values()) + list(halos.values()):
        ins += slot_inputs(kv, rows)
    if carry is not None:
        ins += [(c, (rows, 256), part) for c in carry]
    scratch, keep = [], {}
    for _ in halves:
        scratch += [pltpu.VMEM((2 * rows, 128), BF)] + [pltpu.VMEM((2 * rows, 128), F32)] * 2
    state = shaped((rows, heads * 256), F32)
    if last is None:
        outs = [(state, (rows, 256), part)] * (2 * len(halves))
    else:
        other = last[0]
        if other is not None:
            keep = {len(ins): 0}
            ins.append((other, None, None))
        half = halves[0]
        outs = [
            (shaped((2 * rows, heads * 256), BF), (rows, 256), lambda h, i: (half, h)),
            (shaped((heads, 8, rows), F32), (1, 8, rows), lambda h, i: (h, 0, 0)),
        ]
    return call(functools.partial(fwd_kernel, plan), "attend", (heads,), ins, outs, scratch,
                scalars=scalars, keep=keep)


def out_kernel(att_ref, w_ref, part_ref):
    part_ref[...] = mm(att_ref[...], w_ref[...], NT).astype(BF)


def out_projection(half, attended, w_rest):
    rows, cols = attended.shape[0] // 2, attended.shape[1]
    model = w_rest.shape[0]
    ins = [(attended, (rows, cols), lambda j: (half, 0)), (w_rest, (model // 2, cols), lambda j: (j, 0))]
    outs = [(shaped((rows, model), BF), (rows, model // 2), lambda j: (0, j))]
    return call(out_kernel, "out_projection", (2,), ins, outs)[0]


def bwd_kernel(plan, idx_ref, q_ref, do_ref, lse_ref, delta_ref, lo_ref, *refs):
    half, slots, halos = plan["half"], plan["slots"], plan["halos"]
    refs = list(refs)
    slot_refs = take_slots(refs, plan["pairs"])
    halo_refs = take_slots(refs, [False] * len(halos))
    prior_dq = refs.pop(0) if plan["carry"] else None
    prior = [refs.pop(0) for _ in slots] if plan["sum"] else None
    if plan["alias"]:
        refs.pop(0)
    dq_ref = refs.pop(0)
    slot_outs = [refs.pop(0) for _ in slots]
    halo_outs = [refs.pop(0) for _ in halos]
    qs, dos, lses, deltas, dq = refs
    me, lo_first = idx_ref[0], idx_ref[1]
    rows = q_ref.shape[0]
    for g in range(2):
        cols, at = slice(g * HEAD_SIZE, (g + 1) * HEAD_SIZE), slice(g * rows, (g + 1) * rows)
        qs[at, :] = q_ref[:, cols]
        dos[at, :] = do_ref[:, cols]
        lses[:, at] = lse_ref[0, g : g + 1, :]
        deltas[:, at] = delta_ref[0, g : g + 1, :]
    dq[...] = jnp.zeros_like(dq) if prior_dq is None else prior_dq[...]

    def block(kv_ref, out_ref, mask=None, before=None):
        keys = kv_ref[0][...]
        scores = mm(keys, qs[...], NT)
        dp = mm(kv_ref[1][...], dos[...], NT)
        scores = scores - lses[...]
        if mask is not None:
            scores = jnp.where(mask, scores, MASKED)
        probs = jnp.exp2(scores)
        ds = (probs * (dp - deltas[...])).astype(BF)
        dq[...] += mm(keys.T, ds)
        dk, dv = mm(ds, qs[...]) * LN2, mm(probs.astype(BF), dos[...])
        if before is not None:
            dk, dv = dk + before[0].astype(F32), dv + before[1].astype(F32)
        out_ref[0] = dk.astype(BF)
        out_ref[1] = dv.astype(BF)

    lane = lax.broadcasted_iota(jnp.int32, (1, 2 * rows), 1)
    lane = jnp.where(lane >= rows, lane - rows, lane)
    key = lax.broadcasted_iota(jnp.int32, (rows, 1), 0)

    def when(needed, kv_ref, out_ref, mask=None):
        @pl.when(needed)
        def _():
            block(kv_ref, out_ref, mask)

        @pl.when(jnp.logical_not(needed))
        def _():
            out_ref[...] = jnp.zeros_like(out_ref)

    low = lo_ref[:1, :]
    for d, kv_ref, out_ref in zip(halos, halo_refs, halo_outs):
        if d == 0:
            block(kv_ref, out_ref, (key <= lane) & (key >= low))
        else:
            when(lo_first < -(d - 1) * rows, kv_ref, out_ref, key - d * rows >= low)
    if half == 1:
        for at in range(len(slots)):
            block(slot_refs[at], slot_outs[at], None, prior[at] if prior else None)
    else:
        if 0 in slots:
            at = slots.index(0)
            block(slot_refs[at], slot_outs[at], key <= lane)
        for bit, group in by_top_bit(slots).items():

            @pl.when(jnp.bitwise_and(me, bit) != 0)
            def _(group=group):
                for at in group:
                    block(slot_refs[at], slot_outs[at])

            @pl.when(jnp.bitwise_and(me, bit) == 0)
            def _(group=group):
                for at in group:
                    slot_outs[at][...] = jnp.zeros_like(slot_outs[at])

    if plan["last"]:
        for g in range(2):
            cols = slice(g * HEAD_SIZE, (g + 1) * HEAD_SIZE)
            dq_ref[:, cols] = dq[:, g * rows : (g + 1) * rows].T * SCALE
    else:
        dq_ref[...] = dq[...]


def attention_backward(half, scalars, q, do, lse, delta, low, slots, halos, carry=None, prior=None, last=True, whole=None):
    rows, heads = q.shape[0], q.shape[1] // 256
    plan = dict(half=half, slots=list(slots), pairs=[isinstance(kv, tuple) for kv in slots.values()], halos=list(halos), carry=carry is not None,
                sum=prior is not None, last=last, alias=whole is not None)
    part = lambda h, i: (0, h)
    stat = lambda h, i: (h, 0, 0)
    kv_map = lambda h, i: (0, 0, h)
    ins = [
        (q, (rows, 256), part),
        (do, (rows, 256), part),
        (lse, (1, 8, rows), stat),
        (delta, (1, 8, rows), stat),
        (low, (8, 2 * rows), lambda h, i: (0, 0)),
    ]
    pieces = list(slots.values()) + list(halos.values())
    for kv in pieces:
        ins += slot_inputs(kv, rows)
    if carry is not None:
        ins.append((carry, (128, 2 * rows), lambda h, i: (h, 0)))
    if prior is not None:
        ins += [(prior[s], (2, rows, 128), kv_map) for s in slots]
    keep = {}
    if whole is not None:
        keep = {len(ins): 0}
        ins.append((whole, None, None))
    if last:
        outs = [(shaped((rows, heads * 256), F32), (rows, 256), part)]
    else:
        outs = [(shaped((heads * 128, 2 * rows), F32), (128, 2 * rows), lambda h, i: (h, 0))]
    outs += [(shaped((2, rows, heads * 128), BF), (2, rows, 128), kv_map) for _ in pieces]
    scratch = [
        pltpu.VMEM((2 * rows, 128), BF),
        pltpu.VMEM((2 * rows, 128), BF),
        pltpu.VMEM((1, 2 * rows), F32),
        pltpu.VMEM((1, 2 * rows), F32),
        pltpu.VMEM((128, 2 * rows), F32),
    ]
    us = 4 + 6 * (len(slots) + len(halos)) if carry is not None or halos else 0.1
    results = call(functools.partial(bwd_kernel, plan), "attend_back", (heads,), ins, outs, scratch,
                   scalars=scalars, us=us, keep=keep)
    n = len(slots)
    return results[0], dict(zip(slots, results[1 : 1 + n])), dict(zip(halos, results[1 + n :]))


def prompt_back_kernel(plan, idx_ref, qa_ref, qb_ref, doa_ref, dob_ref, lse_ref, lse_b_ref, delta_ref, delta_b_ref, *refs):
    slots, last = plan["slots"], plan["ctx"] - 1
    refs = list(refs)
    slot_refs = take_slots(refs, plan["pairs"])
    prior = {s: refs.pop(0) for s in plan["prior"]}
    dqa_ref, dqb_ref = refs.pop(0), refs.pop(0)
    outs = [refs.pop(0) for _ in slots]
    qs, dos, lses, deltas, dq, dkv = refs
    me = idx_ref[0]
    half = qa_ref.shape[0]
    rows = 2 * half
    for part, (q_ref, do_ref) in enumerate(((qa_ref, doa_ref), (qb_ref, dob_ref))):
        for g in range(2):
            cols = slice(g * HEAD_SIZE, (g + 1) * HEAD_SIZE)
            at = slice(part * rows + g * half, part * rows + (g + 1) * half)
            qs[at, :] = q_ref[:, cols]
            dos[at, :] = do_ref[:, cols]
            for total, own, got in ((lses, lse_ref, lse_b_ref), (deltas, delta_ref, delta_b_ref)):
                total[:, at] = (got if part else own)[0, g : g + 1, :half]
    dq[...] = jnp.zeros_like(dq)
    lane = lax.broadcasted_iota(jnp.int32, (1, rows), 1)
    lane = jnp.where(lane >= half, lane - half, lane)
    key = lax.broadcasted_iota(jnp.int32, (rows, 1), 0)

    def block(kv_ref, part, mask=None):
        at = slice(part * rows, (part + 1) * rows)
        keys = kv_ref[0][...]
        scores = mm(keys, qs[at, :], NT)
        dp = mm(kv_ref[1][...], dos[at, :], NT)
        scores = scores - lses[:, at]
        if mask is not None:
            scores = jnp.where(mask, scores, MASKED)
        probs = jnp.exp2(scores)
        ds = (probs * (dp - deltas[:, at])).astype(BF)
        dq[:, at] += mm(keys.T, ds)
        dkv[0] += mm(ds, qs[at, :])
        dkv[1] += mm(probs.astype(BF), dos[at, :])

    def top(s):
        return 1 << (s.bit_length() - 1)

    for s, kv_ref, out_ref in zip(slots, slot_refs, outs):
        dkv[...] = jnp.zeros_like(dkv)
        if s == 0:
            block(kv_ref, 0, key <= lane)
        else:

            @pl.when(jnp.bitwise_and(me, top(s)) != 0)
            def _(kv_ref=kv_ref):
                block(kv_ref, 0)

        if s == last:
            block(kv_ref, 1, key <= lane + half)
        else:

            @pl.when(jnp.bitwise_and(me, top(s ^ last)) == 0)
            def _(kv_ref=kv_ref):
                block(kv_ref, 1)

        for which, factor in ((0, LN2), (1, 1.0)):
            total = dkv[which] * factor
            if s in prior:
                total = total + prior[s][which].astype(F32)
            out_ref[which] = total.astype(BF)
    for part, out_ref in enumerate((dqa_ref, dqb_ref)):
        for g in range(2):
            at = slice(part * rows + g * half, part * rows + (g + 1) * half)
            cols = slice(g * HEAD_SIZE, (g + 1) * HEAD_SIZE)
            out_ref[:, cols] = (dq[:, at].T * SCALE).astype(out_ref.dtype)


def prompt_backward(scalars, ctx, own, got, slots, prior):
    rows, heads = own[0].shape[0], own[0].shape[1] // 256
    half = rows // 2
    plan = dict(slots=list(slots), prior=list(prior), ctx=ctx,
                pairs=[isinstance(kv, tuple) for kv in slots.values()])
    part = lambda h, i: (0, h)
    stat = lambda h, i: (h, 0, 0)
    kv_map = lambda h, i: (0, 0, h)
    ins = []
    for mine, other in zip(own[:2], got[:2]):
        ins += [(mine, (half, 256), part), (other, (half, 256), part)]
    for mine, other in zip(own[2:], got[2:]):
        ins += [(mine, (1, 8, rows), stat), (other, (1, 8, half), stat)]
    for kv in slots.values():
        ins += slot_inputs(kv, rows)
    ins += [(grad, (2, rows, 128), kv_map) for grad in prior.values()]
    outs = [(shaped((half, heads * 256), kind), (half, 256), part) for kind in (F32, BF)]
    outs += [(shaped((2, rows, heads * 128), BF), (2, rows, 128), kv_map) for _ in slots]
    scratch = [
        pltpu.VMEM((2 * rows, 128), BF),
        pltpu.VMEM((2 * rows, 128), BF),
        pltpu.VMEM((1, 2 * rows), F32),
        pltpu.VMEM((1, 2 * rows), F32),
        pltpu.VMEM((128, 2 * rows), F32),
        pltpu.VMEM((2, rows, 128), F32),
    ]
    results = call(functools.partial(prompt_back_kernel, plan), "prompt_back", (heads,), ins, outs, scratch,
                   scalars=scalars, us=16)
    return results[0], results[1], dict(zip(slots, results[2:]))


def ffn_kernel(x_ref, own_ref, got_ref, gain_ref, dy_ref, gu_ref, down_ref, *refs):
    resid_ref, normed_ref, hidden_ref, dgu_ref, out_ref, back_ref, normed, out_acc, back_acc = refs[-9:]
    step, steps = pl.program_id(0), pl.num_programs(0)

    @pl.when(step == 0)
    def _():
        resid = x_ref[...].astype(F32) + (own_ref[...].astype(F32) + got_ref[...].astype(F32))
        resid_ref[...] = resid
        normed[...] = (resid * rms(resid) * gain_ref[...]).astype(BF)
        normed_ref[...] = normed[...]
        out_acc[...] = jnp.zeros_like(out_acc)
        back_acc[...] = jnp.zeros_like(back_acc)

    wide = down_ref.shape[1]
    both = mm(normed[...], gu_ref[...])
    d_hidden = mm(dy_ref[...], down_ref[...])
    gate, up = both[:, :wide], both[:, wide:]
    sig = 1.0 / (1.0 + jnp.exp(-gate))
    silu = gate * sig
    hidden = (silu * up).astype(BF)
    hidden_ref[...] = hidden
    d_up = (d_hidden * silu).astype(BF)
    d_gate = (d_hidden * up * (sig + silu * (1.0 - sig))).astype(BF)
    dgu_ref[:, :wide] = d_gate
    dgu_ref[:, wide:] = d_up
    out_acc[...] += mm(hidden, down_ref[...], NT)
    back_acc[...] += mm(dgu_ref[...], gu_ref[...], NT)

    @pl.when(step == steps - 1)
    def _():
        out_ref[...] = out_acc[...].astype(BF)
        back_ref[...] = back_acc[...].astype(BF)


def feed_forward(half, x, own, got, gain, dy, w_od, w_gu, chunk, whole=None):
    rows, model = own.shape
    units = w_gu.shape[1] // 2
    steps = units // chunk
    mine, once = lambda f: (half, 0), lambda f: (0, 0)
    at_down = (w_od.shape[1] - units) // chunk
    block = (rows, model)
    ins = [
        (x, block, mine), (own, block, once), (got, block, once), (gain, (1, model), once), (dy, block, mine),
        (w_gu, (model, 2 * chunk), lambda f: (0, f)),
        (w_od, (model, chunk), lambda f: (0, at_down + f)),
    ]
    keep = {}
    if whole is not None:
        keep = {len(ins) + i: 1 + i for i in range(3)}
        ins += [(array, None, None) for array in whole]
    outs = [
        (shaped((rows, model), F32), block, once),
        (shaped((2 * rows, model), BF), block, mine),
        (shaped((2 * rows, units), BF), (rows, chunk), lambda f: (half, f)),
        (shaped((2 * rows, 2 * units), BF), (rows, 2 * chunk), lambda f: (half, f)),
        (shaped((rows, model), BF), block, once),
        (shaped((rows, model), BF), block, once),
    ]
    scratch = [pltpu.VMEM(block, BF), pltpu.VMEM(block, F32), pltpu.VMEM(block, F32)]
    return call(ffn_kernel, "feed_forward", (steps,), ins, outs, scratch, keep=keep)


def norm_back(grad, values, gain):
    scale = rms(values)
    unit = values * scale
    inner = grad * gain
    return scale * (inner - unit * jnp.mean(inner * unit, axis=-1, keepdims=True)), grad * unit


def lane_mean(values):
    width = values.shape[-1]
    ones = jnp.ones((width, width), BF)
    high = values.astype(BF)
    low = (values - high.astype(F32)).astype(BF)
    return (mm(high, ones) + mm(low, ones)) * (1.0 / width)


def head_norm_back(grad, values, gain):
    scale = lax.rsqrt(lane_mean(values * values) + EPSILON)
    unit = values * scale
    inner = grad * gain
    return scale * (inner - unit * lane_mean(inner * unit)), grad * unit


def row_blocks(rows):
    size = rows // 2 if rows % 512 == 0 else rows
    return size, rows // size


def add_up(ref, value):
    total = jnp.sum(value, axis=0, keepdims=True)

    @pl.when(pl.program_id(0) == 0)
    def _():
        ref[...] = total

    @pl.when(pl.program_id(0) > 0)
    def _():
        ref[...] += total


def mixed_kernel(heads, own_ref, got_ref, resid_ref, gain_ref, dy_ref, w_ref, att_ref, *refs):
    d_resid_ref, mixed_ref, datt_ref, delta_ref, dgain_ref = refs[-5:]
    grad = own_ref[...].astype(F32) + got_ref[...].astype(F32)
    d_norm, summand = norm_back(grad, resid_ref[...], gain_ref[...])
    add_up(dgain_ref, summand)
    d_resid = dy_ref[...].astype(F32) + d_norm
    d_resid_ref[...] = d_resid
    mixed_ref[...] = d_resid.astype(BF)
    datt_ref[...] = mm(mixed_ref[...], w_ref[...]).astype(BF)
    for h in range(heads):
        cols = slice(h * HEAD_SIZE, (h + 1) * HEAD_SIZE)
        product = datt_ref[:, cols].astype(F32) * att_ref[:, cols].astype(F32)
        delta_ref[h // 2, h % 2 : h % 2 + 1, :] = jnp.sum(product.T, axis=0, keepdims=True)


def mixed_back(half, own, got, resid, gain, dy, w_rest, o_cols, attended, whole=None):
    rows, model = own.shape
    heads = o_cols // HEAD_SIZE
    size, steps = row_blocks(rows)
    mine, here, once = lambda f: (half * steps + f, 0), lambda f: (f, 0), lambda f: (0, 0)
    block = (size, model)
    ins = [
        (own, block, here), (got, block, here), (resid, block, here), (gain, (1, model), once),
        (dy, block, mine), (w_rest, (model, o_cols), once), (attended, (size, o_cols), mine),
    ]
    keep = {}
    if whole is not None:
        keep = {len(ins): 1}
        ins.append((whole, None, None))
    outs = [
        (shaped((rows, model), F32), block, here),
        (shaped((2 * rows, model), BF), block, mine),
        (shaped((rows, o_cols), BF), (size, o_cols), here),
        (shaped((heads // 2, 8, rows), F32), (heads // 2, 8, size), lambda f: (0, 0, f)),
        (shaped((1, model), F32), (1, model), once),
    ]
    return call(functools.partial(mixed_kernel, heads), "mixed_back", (steps,), ins, outs, keep=keep)


def merge_kernel(two, got3, four, got5, far_k, far_v, to_x, to_y):
    for which in range(2):
        by_x = two[which].astype(F32) + got3[which].astype(F32)
        by_y = four[which].astype(F32) + got5[which].astype(F32)
        to_x[which] = (by_x + far_v[...].astype(F32) if which else by_x).astype(BF)
        to_y[which] = (by_y if which else by_y + far_k[...].astype(F32)).astype(BF)


def merge(*pieces):
    rows, cols = pieces[-1].shape
    size, steps = row_blocks(rows)
    ins = []
    for piece in pieces:
        if piece.ndim == 3:
            ins.append((piece, (2, size, cols), lambda f: (0, f, 0)))
        else:
            ins.append((piece, (size, cols), lambda f: (f, 0)))
    outs = [(shaped((2, rows, cols), BF), (2, size, cols), lambda f: (0, f, 0))] * 2
    return call(merge_kernel, "merge", (steps,), ins, outs)


def weight_kernel(left_ref, right_ref, *refs):
    refs[-1][...] = mm(left_ref[...], right_ref[...], TN).astype(BF)


def weight_grad(left, right, at, width, cols, whole=None):
    tokens, model = left.shape
    n = right.shape[1]
    ins = [(left, (tokens, model), lambda j: (0, 0)), (right, (tokens, cols), lambda j: (0, j))]
    keep = {}
    if whole is not None:
        keep = {len(ins): 0}
        ins.append((whole, None, None))
    outs = [(shaped((model, width), BF), (model, cols), lambda j: (0, at // cols + j))]
    return call(weight_kernel, "weight_grad", (n // cols,), ins, outs, keep=keep)[0]


def slot_weight_kernel(order, part_ref, left_ref, right_ref, low_ref, high_ref, total):
    total[...] = mm(left_ref[...], right_ref[...], TN)
    wide = total.shape[0] // len(order)
    for at, slot in enumerate(order):
        block = jnp.bitwise_xor(part_ref[0], slot)
        piece = total[pl.ds(pl.multiple_of(block * wide, wide), wide), :].astype(BF)
        out_ref, row = (low_ref, at) if at < len(order) // 2 else (high_ref, at - len(order) // 2)
        out_ref[row * wide : (row + 1) * wide, :] = piece


def slot_weight_grad(order, part, left, right):
    tokens, model = left.shape
    cols = right.shape[1]
    once = lambda j, i: (0, 0)
    ins = [(left, (tokens, model), once), (right, (tokens, cols), once)]
    half = shaped((model // 2, cols), BF)
    return call(functools.partial(slot_weight_kernel, order), "slot_weight_grad", (1,), ins,
                [(half, half.shape, once)] * 2, [pltpu.VMEM((model, cols), F32)], scalars=part[None])


def weight_halves_kernel(left_ref, right_ref, high_ref, low_ref):
    for half, out_ref in enumerate((high_ref, low_ref)):

        @pl.when(pl.program_id(0) == half)
        def _(out_ref=out_ref):
            out_ref[...] = mm(left_ref[...], right_ref[...], TN).astype(BF)


def weight_halves(left, right):
    tokens, model = left.shape
    cols = right.shape[1]
    once = lambda i: (0, 0)
    ins = [(left, (tokens, model // 2), lambda i: (0, 1 - i)), (right, (tokens, cols), once)]
    half = shaped((model // 2, cols), BF)
    return call(weight_halves_kernel, "weight_halves", (2,), ins, [(half, half.shape, once)] * 2)


def q_back_kernel(heads, dqa_ref, dqb_ref, dqc_ref, lin_ref, gain_ref, cos_ref, sin_ref, w_ref, *refs):
    d_ref, part_ref, gains_ref, dq_ref = refs[-4:]
    step = pl.program_id(0)

    @pl.when(step == 0)
    def _():
        dq_ref[...] = dqa_ref[...]

    @pl.when(step == 1)
    def _():
        dq_ref[...] = dqb_ref[...].astype(F32)

    @pl.when(step > 1)
    def _():
        dq_ref[...] = dqc_ref[...]

    cos, sin = cos_ref[...], sin_ref[...]
    total = jnp.zeros(cos.shape, F32)
    for h in range(heads):
        cols = slice(h * HEAD_SIZE, (h + 1) * HEAD_SIZE)
        grad, summand = head_norm_back(turn_back(dq_ref[:, cols], cos, sin), lin_ref[:, cols], gain_ref[...])
        d_ref[:, cols] = grad.astype(BF)
        total = total + summand
    part_ref[...] = mm(d_ref[...], w_ref[...], NT)
    add_up(gains_ref, total)


def q_back(dq_a, dq_b, dq_c, lin, gain, cos, sin, w):
    rows, cols = lin.shape
    model = w.shape[0]
    size = rows // 4
    here, once = lambda f: (f, 0), lambda f: (0, 0)
    ins = [
        (dq_a, (size, cols), once), (dq_b, (size, cols), once), (dq_c, (size, cols), lambda f: (jnp.maximum(f - 2, 0), 0)),
        (lin, (size, cols), here), (gain, (1, HEAD_SIZE), once),
        (cos, (size, HEAD_SIZE), here), (sin, (size, HEAD_SIZE), here), (w, (model, cols), once),
    ]
    outs = [
        (shaped((rows, cols), BF), (size, cols), here),
        (shaped((rows, model), F32), (size, model), here),
        (shaped((1, HEAD_SIZE), F32), (1, HEAD_SIZE), once),
    ]
    kernel = functools.partial(q_back_kernel, cols // HEAD_SIZE)
    return call(kernel, "q_back", (4,), ins, outs, [pltpu.VMEM((size, cols), F32)])


def kv_back_kernel(heads, n_keys, n_values, lin_ref, gain_ref, cos_ref, sin_ref, w_ref, slots_ref, q_part_ref, *refs):
    key_refs, value_refs = refs[:n_keys], refs[n_keys : n_keys + n_values]
    d_ref, part_ref, gains_ref = refs[-3:]
    cos, sin = cos_ref[...], sin_ref[...]
    width = heads * HEAD_SIZE

    def total(sources, which, cols):
        value = None
        for ref in sources:
            piece = ref[which, :, cols] if len(ref.shape) == 3 else ref[:, cols]
            value = piece.astype(F32) if value is None else value + piece.astype(F32)
        return value

    gains = jnp.zeros(cos.shape, F32)
    for h in range(heads):
        cols = slice(h * HEAD_SIZE, (h + 1) * HEAD_SIZE)
        grad, summand = head_norm_back(
            turn_back(total(key_refs, 0, cols), cos, sin), lin_ref[:, cols], gain_ref[...]
        )
        d_ref[:, cols] = grad.astype(BF)
        gains = gains + summand
    d_ref[:, width:] = total(value_refs, 1, slice(None)).astype(BF)
    part = (q_part_ref[...] + mm(d_ref[...], w_ref[...], NT)).astype(BF)
    part_ref[...] = mm(part, slots_ref[...], NT).astype(BF)
    add_up(gains_ref, gains)


def kv_back(half, keys, values, lin, gain, cos, sin, w, to_slots, q_part, whole=None):
    rows, cols = lin.shape
    model = w.shape[0]
    size, steps = row_blocks(rows)
    mine, here, once = lambda f: (half * steps + f, 0), lambda f: (f, 0), lambda f: (0, 0)
    ins = [
        (lin, (size, cols), here), (gain, (1, HEAD_SIZE), once), (cos, (size, HEAD_SIZE), mine),
        (sin, (size, HEAD_SIZE), mine), (w, (model, 2 * cols), once),
        (to_slots, (model, model), once), (q_part, (size, model), mine),
    ]
    for piece in list(keys) + list(values):
        if piece.ndim == 3:
            ins.append((piece, (2, size, cols), lambda f: (0, f, 0)))
        else:
            ins.append((piece, (size, cols), here))
    keep = {}
    if whole is not None:
        keep = {len(ins): 0}
        ins.append((whole, None, None))
    outs = [
        (shaped((2 * rows, 2 * cols), BF), (size, 2 * cols), mine),
        (shaped((rows, model), BF), (size, model), here),
        (shaped((1, HEAD_SIZE), F32), (1, HEAD_SIZE), once),
    ]
    kernel = functools.partial(kv_back_kernel, cols // HEAD_SIZE, len(keys), len(values))
    return call(kernel, "kv_back", (steps,), ins, outs, keep=keep, us=3 * (1 - half))


def tokens_kernel(own_ref, got_ref, x_ref, gain_ref, d_resid_ref, *refs):
    out_ref, dgain_ref = refs[-2:]
    grad = own_ref[...].astype(F32) + got_ref[...].astype(F32)
    d_norm, summand = norm_back(grad, x_ref[...].astype(F32), gain_ref[...])
    add_up(dgain_ref, summand)
    out_ref[...] = (d_resid_ref[...] + d_norm).astype(BF)


def tokens_back(half, own, got, x, gain, d_resid, whole=None):
    rows, model = own.shape
    size, steps = row_blocks(rows)
    mine, here, once = lambda f: (half * steps + f, 0), lambda f: (f, 0), lambda f: (0, 0)
    block = (size, model)
    ins = [(own, block, here), (got, block, here), (x, block, mine), (gain, (1, model), once), (d_resid, block, here)]
    keep = {}
    if whole is not None:
        keep = {len(ins): 0}
        ins.append((whole, None, None))
    outs = [(shaped((2 * rows, model), BF), block, mine), (shaped((1, model), F32), (1, model), once)]
    return call(tokens_kernel, "tokens_back", (steps,), ins, outs, keep=keep, us=20)


def share_kernel(chunk, ffn_ref, own_ref, got_ref, out_ref, gate_ref, up_ref, down_ref):
    units = gate_ref.shape[1]
    out_ref[...] = own_ref[...].astype(F32) + got_ref[...].astype(F32)
    for at in range(0, units, chunk):
        gate_ref[:, at : at + chunk] = ffn_ref[:, 2 * at : 2 * at + chunk].astype(F32)
        up_ref[:, at : at + chunk] = ffn_ref[:, 2 * at + chunk : 2 * at + 2 * chunk].astype(F32)
    down_ref[...] = ffn_ref[:, 2 * units :].astype(F32)


def unpack(chunk, ffn_share, out_grad):
    wide, units = ffn_share.shape[0], ffn_share.shape[1] // 3
    o_cols = out_grad[0].shape[1]
    whole = lambda f: (0, 0)
    ins = [(ffn_share, ffn_share.shape, whole)] + [(grad, (wide, o_cols), whole) for grad in out_grad]
    outs = [(shaped((wide, cols), F32), (wide, cols), whole) for cols in (o_cols, units, units, units)]
    return call(functools.partial(share_kernel, chunk), "unpack", (1,), ins, outs)


def layer_kernel(resid_ref, own_ref, got_ref, *refs):
    refs[-1][...] = (resid_ref[...] + (own_ref[...].astype(F32) + got_ref[...].astype(F32))).astype(BF)


def add_layer(half, resid, own, got, whole=None):
    rows, model = resid.shape
    size, steps = row_blocks(rows)
    here, mine = lambda f: (f, 0), lambda f: (half * steps + f, 0)
    ins = [(array, (size, model), here) for array in (resid, own, got)]
    keep = {}
    if whole is not None:
        keep = {len(ins): 0}
        ins.append((whole, None, None))
    outs = [(shaped((2 * rows, model), BF), (size, model), mine)]
    return call(layer_kernel, "add_layer", (steps,), ins, outs, keep=keep)[0]


def swap(value, axis, bit):
    size = lax.axis_size(axis)
    return lax.ppermute(value, axis, [(i, i ^ bit) for i in range(size)])


def shift(value, by):
    size = lax.axis_size("ctx")
    return lax.ppermute(value, "ctx", [(i, i + by) for i in range(size) if 0 <= i + by < size])


def add_low(left, right):
    return (left.astype(F32) + right.astype(F32)).astype(BF)


def butterfly(value, axes, gates=()):
    gates = list(gates)
    for axis in axes:
        bit = 1
        while bit < lax.axis_size(axis):
            got = swap(value, axis, bit)
            value = value + (after(got, gates.pop(0)) if gates else got)
            bit *= 2
    return value


def after(value, *others):
    return lax.optimization_barrier((value, *others))[0]


def rotary_tables(position):
    half_dim = HEAD_SIZE // 2
    inverse_freq = jnp.exp(jnp.arange(half_dim, dtype=F32) * (-math.log(ROPE_BASE) / half_dim))
    angles = position.astype(F32)[:, None] * inverse_freq[None, :]
    cosine, sine = jnp.cos(angles), jnp.sin(angles)
    return jnp.concatenate([cosine, cosine], axis=-1), jnp.concatenate([-sine, sine], axis=-1)


def body(
    tokens,
    cont_lengths,
    attn_gain,
    ffn_gain,
    query_gain,
    key_gain,
    w_query,
    key_weight,
    value_weight,
    w_out,
    w_gate,
    w_up,
    w_down,
    cotangent,
):
    ctx_size = lax.axis_size("ctx")
    weight_axes = ("shard", "ctx")
    parts = lax.axis_size("shard") * ctx_size
    me = lax.axis_index("ctx")
    part = lax.axis_index("shard") * ctx_size + me
    rows, model = tokens.shape[0] // 2, tokens.shape[1]
    n_halo = 1 + -(-(LONGEST - 1) // rows)
    lengths = cont_lengths[0]

    bits = [("shard", 1)] + [("ctx", 1 << i) for i in range(1, ctx_size.bit_length() - 1)] + [("ctx", 1)]
    order = [0]
    for axis, bit in bits:
        order += [j ^ (bit * ctx_size if axis == "shard" else bit) for j in order]
    wide, narrow = attn_gain.shape[0], query_gain.shape[0]
    q_cols, k_cols = w_query.shape[1], key_weight.shape[1]
    o_cols, units = w_out.shape[0], w_gate.shape[1]
    heads, kv_heads = q_cols // HEAD_SIZE, k_cols // HEAD_SIZE
    chunk = math.gcd(units, 512)

    def gather_first(piece, *gate):
        return jnp.concatenate([piece, after(swap(piece, "shard", 1), *gate)]) if ctx_size == 8 else piece

    def gather_near(one, *gate):
        if ctx_size != 8:
            for axis, bit in bits:
                one = jnp.concatenate([one, swap(one, axis, bit)])
            return [one]
        return [one] + [after(swap(one, "ctx", bit), *gate) for bit in (2, 4, 6)]

    def gather_far(near, *gate):
        if ctx_size != 8:
            return near
        return near + [after(swap(piece, "ctx", 1), *gate) for piece in near]

    def scatter_rows(low, high, late):
        total = add_low(low, after(swap(high, "ctx", 1), late))
        if ctx_size != 8:
            for axis, bit in bits[-2:0:-1]:
                size = total.shape[0] // 2
                total = add_low(total[:size], swap(total[size:], axis, bit))
            return (total,)
        size = total.shape[0] // 4
        by_x, by_y, far = (total[i * size : (i + 1) * size] for i in (1, 2, 3))
        return total, swap(by_x, "ctx", 2), swap(by_y, "ctx", 4), swap(far, "ctx", 6)

    def scatter_sum(stage, late):
        total = stage[0].astype(F32)[: stage[-1].shape[0]]
        for piece in stage[1:]:
            total = total + after(piece, late).astype(F32)
        total, size = total.astype(BF), total.shape[0] // 2
        return total, swap(total[size:], "shard", 1)

    kv_piece, od_piece, gu_piece = pack(
        chunk, key_weight, value_weight, w_out.T, w_down.T, w_gate, w_up
    )
    kv_one = gather_first(kv_piece)
    kv_near = gather_near(kv_one)
    kv_pieces = gather_far(kv_near)
    q_one = gather_first(after(w_query, kv_one), kv_near[-1])
    w_od = lax.all_gather(od_piece, weight_axes, axis=0, tiled=True)
    gains = jnp.concatenate([attn_gain, ffn_gain, query_gain, key_gain])[None]
    gains = jnp.where(jnp.arange(parts)[:, None] == part, gains, jnp.zeros((), BF))
    gains = gains + after(swap(gains, "ctx", 1), kv_piece)
    for at, (axis, bit) in enumerate(bits[:-1]):
        gains = gains + after(swap(gains, axis, bit), (kv_one, kv_near[-1], kv_near[-1])[min(at, 2)])
    gains = gains.astype(F32)
    gain_one = gains[:, :wide].reshape(1, -1)
    gain_two = gains[:, wide : 2 * wide].reshape(1, -1)
    gain_q = gains[:, 2 * wide : 2 * wide + narrow].reshape(1, -1)
    gain_k = gains[:, 2 * wide + narrow :].reshape(1, -1)
    source = jnp.bitwise_xor(part, jnp.array(order, jnp.int32))[:, None] * wide + jnp.arange(wide, dtype=jnp.int32)
    to_slots = (jnp.arange(model, dtype=jnp.int32)[:, None] == source.reshape(1, -1)).astype(BF)
    tokens_s = mm(after(tokens, q_one), to_slots).astype(BF)
    gain_one_s = mm(gain_one.astype(BF), to_slots)

    cont_at = me * rows + jnp.arange(rows, dtype=jnp.int32)
    cont_ends = jnp.cumsum(lengths)
    starts = cont_ends - lengths
    seg = jnp.sum((cont_ends[None, :] <= cont_at[:, None]).astype(jnp.int32), axis=1)
    numbers = jnp.arange(lengths.shape[0], dtype=jnp.int32)
    first = jnp.sum(jnp.where(numbers[None, :] == seg[:, None], starts[None, :], 0), axis=1)
    position = jnp.concatenate([me * rows + jnp.arange(rows, dtype=jnp.int32), PROMPT + cont_at - first])
    low = first - me * rows
    low_col = jnp.broadcast_to(low[:, None], (rows, 128))
    low_row = jnp.broadcast_to(jnp.concatenate([low, low])[None, :], (8, 2 * rows))
    scalars = jnp.stack([me, low[0]])
    cos, sin = rotary_tables(position)

    once = lambda f: (0, 0)

    def weight_inputs(pieces):
        return [(piece, piece.shape, once) for piece in pieces]

    def keys_values(half, gain, pieces, whole=None):
        mine = lambda f: (half, 0)
        ins = [
            (tokens_s, (rows, model), mine), (gain, (1, model), once), (gain_k, (1, HEAD_SIZE), once),
            (cos, (rows, HEAD_SIZE), mine), (sin, (rows, HEAD_SIZE), mine), *weight_inputs(pieces),
        ]
        keep = {}
        if whole is not None:
            keep = {len(ins): 0}
            ins.append((whole, None, None))
        outs = [
            (shaped((2 * rows, model), BF), (rows, model), mine),
            (shaped((2, rows, k_cols), BF), (2, rows, k_cols), lambda f: (0, 0, 0)),
            (shaped((rows, k_cols), F32), (rows, k_cols), once),
        ]
        if len(pieces) > 1:
            outs.append((shaped((model, 2 * k_cols), BF), (model, 2 * k_cols), once))
        return call(functools.partial(kv_kernel, kv_heads, len(pieces)), "keys_values", (1,), ins, outs, keep=keep)

    q_near = gather_near(q_one, kv_pieces[-1])
    normed, kv_p, k_lin_p, *w_kv = keys_values(0, after(gain_one_s, *q_near[1:]), kv_pieces)
    (w_kv,) = w_kv or kv_pieces
    normed, kv_c, k_lin_c = keys_values(1, after(gain_one_s, kv_p), [w_kv], normed)
    q_pieces = gather_far(q_near, kv_c)

    def queries(half, gain, pieces, whole=None):
        mine = lambda f: (half, 0)
        ins = [
            (normed, (rows, model), mine), (gain, (1, HEAD_SIZE), once),
            (cos, (rows, HEAD_SIZE), mine), (sin, (rows, HEAD_SIZE), mine), *weight_inputs(pieces),
        ]
        keep = {}
        if whole is not None:
            keep = {len(ins): 1}
            ins.append((whole, None, None))
        outs = [
            (shaped((rows, q_cols), BF), (rows, q_cols), once),
            (shaped((2 * rows, q_cols), F32), (rows, q_cols), mine),
        ]
        if len(pieces) > 1:
            outs.append((shaped((model, q_cols), BF), (model, q_cols), once))
        return call(functools.partial(q_kernel, heads, len(pieces)), "queries", (1,), ins, outs, keep=keep)

    q_c, q_lin, *w_q = queries(1, gain_q, q_pieces)
    (w_q,) = w_q or q_pieces
    q_p, q_lin = queries(0, after(gain_q, q_c), [w_q], q_lin)

    def pick(source, wanted):
        return {s: source[s] for s in source if s in wanted}

    near, middle, far = (0, 1), (2, 3, 4, 5), tuple(range(6, ctx_size))
    slots, halos = {0: kv_p}, {0: kv_c}
    odd = (me % 2) == 1
    if ctx_size == 8:
        slots[1], slots[2], slots[4] = (swap(kv_p, "ctx", bit) for bit in (1, 2, 4))
    else:
        both, bit = kv_p[None], 1
        while bit < ctx_size:
            both = jnp.concatenate([both, swap(both, "ctx", bit)])
            bit *= 2
        slots = {s: both[s] for s in range(ctx_size)}
        halos.update({d: shift(kv_c, d) for d in range(1, n_halo)})
    ready = ()
    if ctx_size == 8:
        slots[2], slots[4] = after(slots[2], q_p), after(slots[4], q_p)
        far_k, far_v = swap(slots[4][0], "ctx", 2), swap(slots[2][1], "ctx", 4)
        slots[3], slots[5] = swap(slots[2], "ctx", 1), swap(slots[4], "ctx", 1)
        halos[2] = shift(after(kv_c, slots[2]), 2)
        gu_piece = after(gu_piece, slots[2], slots[4])
        ready = (slots[2], slots[4])
    w_gu = lax.all_gather(after(gu_piece, w_od), weight_axes, axis=0, tiled=True)
    c_state = attention_forward(
        (1,), after(scalars, *ready), (q_c,), low_col, pick(slots, near), pick(halos, (0,))
    )
    if ctx_size == 8:
        slots[6] = after(far_k, c_state[0]), after(far_v, c_state[0])
        slots[7] = tuple(swap(part, "ctx", 1) for part in slots[6])
    attended, lse_p = attention_forward(
        (0,), after(scalars, c_state[0]), (q_p,), low_col, slots, {}, None, (None,)
    )
    part_p = out_projection(0, attended, w_od)
    got_p = swap(part_p, "tensor", 1)
    if ctx_size == 8:
        halos[1] = swap(jnp.where(odd, after(halos[2], part_p), kv_c), "ctx", 1)
    attended, lse_c = attention_forward(
        (1,), after(scalars, part_p), (q_c,), low_col, pick(slots, middle + far), pick(halos, range(1, n_halo)),
        c_state, (attended,),
    )
    part_c = out_projection(1, attended, w_od)
    got_c = swap(part_c, "tensor", 1)

    resid_p, *whole, out_p, back_p = feed_forward(
        0, tokens, part_p, got_p, after(gain_two, part_c), cotangent, w_od, w_gu, chunk
    )
    back_got_p = swap(back_p, "tensor", 1)
    resid_c, *whole, out_c, back_c = feed_forward(
        1, tokens, part_c, got_c, after(gain_two, back_p), cotangent, w_od, w_gu, chunk, whole
    )
    back_got_c = swap(back_c, "tensor", 1)
    normed_ffn, hidden, d_gu = whole
    ffn_grads = weight_grad(normed_ffn, d_gu, 0, 3 * units, 2 * chunk)
    ffn_grads = weight_grad(cotangent, hidden, 2 * units, 3 * units, chunk, ffn_grads)
    ffn_share = lax.psum_scatter(ffn_grads, weight_axes, scatter_dimension=0, tiled=True)
    d_resid_p, d_mixed, d_att_p, delta_p, d_two_p = mixed_back(
        0, back_p, back_got_p, resid_p, after(gain_two, ffn_grads), cotangent, w_od, o_cols, attended
    )

    def mirror(value):
        return lax.ppermute(value, "ctx", [(i, i ^ (ctx_size - 1)) for i in range(ctx_size)])

    half = rows // 2
    q_b, lse_b = mirror(after(q_p, part_c)[half:]), mirror(after(lse_p, part_c)[:, :, half:])
    do_b, delta_b = mirror(d_att_p[half:]), mirror(delta_p[:, :, half:])
    d_resid_c, d_mixed, d_att_c, delta_c, d_two_c = mixed_back(
        1, back_c, back_got_c, resid_c, after(gain_two, d_att_p), cotangent, w_od, o_cols, attended, d_mixed
    )
    out_low, out_high = slot_weight_grad(order, part, d_mixed, attended)
    out_p, out_c = after(out_p, out_low), after(out_c, out_low)
    out_got_p, out_got_c = swap(out_p, "tensor", 1), swap(out_c, "tensor", 1)

    def back_c_rows(deps, slots, halos, carry, prior=None, last=False):
        return attention_backward(
            1, after(scalars, *deps), q_c, d_att_c, lse_c, delta_c, low_row, slots, halos, carry, prior, last
        )

    dq_c, from_c, g_halo = back_c_rows((out_low,), pick(slots, far), halos, None)
    out_grad = scatter_rows(out_low, out_high, dq_c)
    if ctx_size == 8:
        near_one = swap(g_halo[1], "ctx", 1)
    dq_a, dq_b, from_p = prompt_backward(
        after(scalars, dq_c, out_grad[0]), ctx_size, (q_p, d_att_p, lse_p, delta_p),
        (q_b, do_b, lse_b, delta_b), slots, from_c,
    )
    dq_b = mirror(dq_b)
    g = pick(from_p, far)
    zero = jnp.zeros((), BF)
    ready = ()
    if ctx_size == 8:
        got7 = swap(g[7], "ctx", 1)
        near_one = after(near_one, dq_a)
        two_back = add_low(g_halo[2], jnp.where(odd, near_one, zero))
        halo_two = shift(two_back, -2)
        halo_near = jnp.where(odd, zero, near_one)
        ready = (two_back, halo_near)
    dq_c, more, _ = back_c_rows((dq_a, out_grad[0], *ready), pick(slots, middle), {}, dq_c, from_p)
    g.update(more)
    out_grad = scatter_sum(out_grad, dq_c)
    if ctx_size == 8:
        g6 = add_low(g[6], after(got7, dq_c))
        far_k, far_v = swap(g6[0], "ctx", 2), swap(g6[1], "ctx", 4)
        got3, got5 = swap(g[3], "ctx", 1), swap(g[5], "ctx", 1)
        ready = (g6,)
    dq_c, more, _ = back_c_rows(
        (dq_c, out_got_p, out_got_c, out_grad[0], dq_b, *ready), pick(slots, near), {}, dq_c, from_p, True
    )
    g.update(more)
    if ctx_size == 8:
        got1 = swap(g[1], "ctx", 1)
        far_k, far_v, got3, got5 = (after(v, dq_c, halo_two, ffn_share) for v in (far_k, far_v, got3, got5))
        to_x, to_y = merge(g[2], got3, g[4], got5, far_k, far_v)
        ready = (to_x,)
        keys_p = values_p = [g[0], got1, swap(to_x, "ctx", 2), swap(to_y, "ctx", 4)]
        keys_c = values_c = [g_halo[0], halo_near, halo_two]
    else:
        both = jnp.stack([g[s] for s in range(ctx_size)])
        while both.shape[0] > 1:
            size = both.shape[0] // 2
            both = add_low(both[:size], swap(both[size:], "ctx", size))
        keys_p = values_p = [both[0]]
        keys_c = values_c = [g_halo[0]] + [shift(g_halo[d], -d) for d in range(1, n_halo)]

    d_q, q_part, q_heads = q_back(dq_a, dq_b, dq_c, q_lin, after(gain_q, dq_c, *ready), cos, sin, w_q)
    d_kv, into_c, k_heads_c = kv_back(
        1, keys_c, values_c, k_lin_c, after(gain_k, q_part), cos, sin, w_kv, to_slots, q_part
    )
    into_got_c = swap(into_c, "tensor", 1)
    q_high, q_low = weight_halves(normed, after(d_q, into_c))
    d_kv, into_p, k_heads_p = kv_back(
        0, keys_p, values_p, k_lin_p, after(gain_k, q_low), cos, sin, w_kv, to_slots, q_part, d_kv
    )
    into_got_p = swap(into_p, "tensor", 1)
    q_grad = scatter_rows(q_low, q_high, into_p)
    kv_high, kv_low = weight_halves(normed, after(d_kv, q_grad[0]))
    heads = jnp.concatenate([q_heads, k_heads_c + k_heads_p], axis=1)
    heads_got = swap(heads, "tensor", 1)
    grad_tokens, d_one_c = tokens_back(1, into_c, into_got_c, tokens, after(gain_one, kv_low, q_grad[0]), d_resid_c)
    out_share, gate_share, up_share, down_share = unpack(chunk, after(ffn_share, d_one_c), out_grad)
    q_grad = scatter_sum(q_grad, gate_share)
    kv_grad = scatter_rows(kv_low, kv_high, gate_share)
    layer_out = add_layer(0, after(resid_p, kv_grad[0], q_grad[0]), out_p, out_got_p)
    layer_out = add_layer(1, after(resid_c, kv_grad[0]), out_c, out_got_c, layer_out)
    q_share = add_low(q_grad[0][:wide], after(q_grad[1], layer_out)).astype(F32)
    kv_grad = scatter_sum(kv_grad, layer_out)
    grad_tokens, d_one_p = tokens_back(
        0, into_p, into_got_p, tokens, after(gain_one, kv_grad[0], q_share), d_resid_p, grad_tokens
    )
    heads = heads + after(heads_got, d_one_p)
    late = jnp.concatenate([d_one_c + d_one_p, heads, d_two_c + d_two_p], axis=1)
    kv_share = add_low(kv_grad[0][:wide], after(kv_grad[1], d_one_p)).astype(F32)
    late = butterfly(late, ("ctx", "shard"), (d_one_p, kv_share))

    def own_gain(value, size):
        return lax.dynamic_index_in_dim(value.reshape(parts, size), part, 0, keepdims=False)

    return (
        layer_out,
        grad_tokens,
        own_gain(late[:, :model], wide),
        own_gain(late[:, model + 2 * HEAD_SIZE :], wide),
        own_gain(late[:, model : model + HEAD_SIZE], narrow),
        own_gain(late[:, model + HEAD_SIZE : model + 2 * HEAD_SIZE], narrow),
        q_share,
        kv_share[:, :k_cols],
        kv_share[:, k_cols:],
        out_share.T,
        gate_share,
        up_share,
        down_share.T,
    )


def solution(mesh):
    split = ("shard", "ctx")
    rows, gain = P(split, None), P(split)
    into, out_of = P(split, "tensor"), P("tensor", split)
    in_specs = (rows, P("shard", None)) + (gain,) * 4 + (into,) * 3 + (out_of,)
    in_specs += (into, into, out_of, rows)
    out_specs = (rows, rows) + (gain,) * 4 + (into,) * 3 + (out_of, into, into, out_of)
    return jax.shard_map(body, mesh=mesh, in_specs=in_specs, out_specs=out_specs, check_vma=False)
```

```python
import functools
import math

import jax
import jax.numpy as jnp
from jax import lax
from jax.experimental import pallas as pl
from jax.experimental.pallas import tpu as pltpu
from jax.sharding import PartitionSpec as P

HEAD_SIZE = 128
PROMPT = 4096
CONT_TOK = 4096
LONGEST = 1024

EPSILON = 1e-06
ROPE_BASE = 1000000.0
MASKED = -1e30
LOG2E = math.log2(math.e)
LN2 = math.log(2.0)
SCALE = 1.0 / math.sqrt(HEAD_SIZE)

BF = jnp.bfloat16
F32 = jnp.float32
NN = (((1,), (0,)), ((), ()))
NT = (((1,), (1,)), ((), ()))
TN = (((0,), (0,)), ((), ()))
MIB = 2**20
STATED = 3e9


def mm(left, right, dims=NN):
    return lax.dot_general(left, right, dims, preferred_element_type=F32)


def shaped(dims, kind):
    return jax.ShapeDtypeStruct(dims, kind)


def call(kernel, name, grid, ins, outs, scratch=(), vmem=56, scalars=None, keep=None, us=0):
    in_specs, arrays = [], []
    for array, block, index in ins:
        arrays.append(array)
        in_specs.append(pl.BlockSpec(memory_space=pl.ANY) if block is None else pl.BlockSpec(block, index))
    lead = 0 if scalars is None else 1
    return pl.pallas_call(
        kernel,
        grid_spec=pltpu.PrefetchScalarGridSpec(
            num_scalar_prefetch=lead,
            grid=grid,
            in_specs=in_specs,
            out_specs=[pl.BlockSpec(block, index) for _, block, index in outs],
            scratch_shapes=list(scratch),
        ),
        out_shape=[shape for shape, _, _ in outs],
        input_output_aliases={a + lead: b for a, b in (keep or {}).items()},
        compiler_params=pltpu.CompilerParams(vmem_limit_bytes=vmem * MIB),
        cost_estimate=pl.CostEstimate(flops=int(us * STATED), bytes_accessed=0, transcendentals=0),
        name=name,
    )(*([] if scalars is None else [scalars]), *arrays)


def rms(values):
    return lax.rsqrt(jnp.mean(values * values, axis=-1, keepdims=True) + EPSILON)


def turn(values, cos, sin):
    return values * cos + pltpu.roll(values, HEAD_SIZE // 2, 1) * sin


def turn_back(values, cos, sin):
    return values * cos - pltpu.roll(values, HEAD_SIZE // 2, 1) * sin


def put_together(pieces, whole_ref):
    rows = whole_ref.shape[0] // len(pieces)
    for at, piece in enumerate(pieces):
        whole_ref[at * rows : (at + 1) * rows, :] = piece[...]


def kv_kernel(heads, n_pieces, x_ref, gain_ref, hgain_ref, cos_ref, sin_ref, *refs):
    pieces, refs = refs[:n_pieces], refs[n_pieces:]
    if n_pieces == 1:
        w_ref, (normed_ref, kv_ref, lin_ref) = pieces[0], refs[-3:]
    else:
        normed_ref, kv_ref, lin_ref, w_ref = refs[-4:]
        put_together(pieces, w_ref)
    x = x_ref[...].astype(F32)
    normed_ref[...] = (x * rms(x) * gain_ref[...]).astype(BF)
    both = mm(normed_ref[...], w_ref[...])
    width = heads * HEAD_SIZE
    kv_ref[1] = both[:, width:].astype(BF)
    for h in range(heads):
        cols = slice(h * HEAD_SIZE, (h + 1) * HEAD_SIZE)
        lin = both[:, cols]
        lin_ref[:, cols] = lin
        kv_ref[0, :, cols] = turn(lin * rms(lin) * hgain_ref[...], cos_ref[...], sin_ref[...]).astype(BF)


def q_kernel(heads, n_pieces, normed_ref, hgain_ref, cos_ref, sin_ref, *refs):
    pieces, refs = refs[:n_pieces], refs[n_pieces:]
    if n_pieces == 1:
        w_ref, (q_ref, lin_ref) = pieces[0], refs[-2:]
    else:
        q_ref, lin_ref, w_ref = refs[-3:]
        put_together(pieces, w_ref)
    both = mm(normed_ref[...], w_ref[...])
    for h in range(heads):
        cols = slice(h * HEAD_SIZE, (h + 1) * HEAD_SIZE)
        lin = both[:, cols]
        lin_ref[:, cols] = lin
        turned = turn(lin * rms(lin) * hgain_ref[...], cos_ref[...], sin_ref[...])
        q_ref[:, cols] = (turned * (SCALE * LOG2E)).astype(BF)


def pack_kernel(chunk, key_ref, value_ref, out_ref, down_ref, gate_ref, up_ref, kv_ref, od_ref, gu_ref):
    k_cols, o_cols, units = key_ref.shape[1], out_ref.shape[1], gate_ref.shape[1]
    kv_ref[:, :k_cols] = key_ref[...]
    kv_ref[:, k_cols:] = value_ref[...]
    od_ref[:, :o_cols] = out_ref[...]
    od_ref[:, o_cols:] = down_ref[...]
    for at in range(0, units, chunk):
        gu_ref[:, 2 * at : 2 * at + chunk] = gate_ref[:, at : at + chunk]
        gu_ref[:, 2 * at + chunk : 2 * at + 2 * chunk] = up_ref[:, at : at + chunk]


def pack(chunk, *weights):
    cols = [w.shape[1] for w in weights]
    wide = weights[0].shape[0]
    whole = lambda f: (0, 0)
    ins = [(w, w.shape, whole) for w in weights]
    sums = (cols[0] + cols[1], cols[2] + cols[3], cols[4] + cols[5])
    outs = [(shaped((wide, width), BF), (wide, width), whole) for width in sums]
    return call(functools.partial(pack_kernel, chunk), "pack", (1,), ins, outs)


def by_top_bit(slots):
    groups = {}
    for at, s in enumerate(slots):
        if s:
            groups.setdefault(1 << (s.bit_length() - 1), []).append(at)
    return groups


def slot_inputs(kv, rows):
    if isinstance(kv, tuple):
        return [(part, (rows, 128), lambda h, i: (0, h)) for part in kv]
    return [(kv, (2, rows, 128), lambda h, i: (0, 0, h))]


def take_slots(refs, pairs):
    taken = []
    for pair in pairs:
        if pair:
            taken.append((refs.pop(0), refs.pop(0)))
        else:
            ref = refs.pop(0)
            taken.append((ref.at[0], ref.at[1]))
    return taken


def fwd_kernel(plan, idx_ref, lo_ref, *refs):
    halves, slots, halos = plan["halves"], plan["slots"], plan["halos"]
    refs = list(refs)
    q_refs = [refs.pop(0) for _ in halves]
    slot_refs = take_slots(refs, plan["pairs"])
    halo_refs = take_slots(refs, [False] * len(halos))
    prior = [refs.pop(0) for _ in range(2 * len(halves))] if plan["carry"] else None
    if plan["last"]:
        if plan["alias"]:
            refs.pop(0)
        out_ref, lse_ref = refs[:2]
        refs = refs[2:]
    else:
        results, refs = refs[: 2 * len(halves)], refs[2 * len(halves) :]
    me, lo_first = idx_ref[0], idx_ref[1]
    rows = q_refs[0].shape[0]
    row = lax.broadcasted_iota(jnp.int32, (2 * rows, 1), 0)
    row = jnp.where(row >= rows, row - rows, row)
    col = lax.broadcasted_iota(jnp.int32, (1, rows), 1)
    for n, half in enumerate(halves):
        qs, acc, tot = refs[3 * n : 3 * n + 3]
        for g in range(2):
            cols, at = slice(g * HEAD_SIZE, (g + 1) * HEAD_SIZE), slice(g * rows, (g + 1) * rows)
            qs[at, :] = q_refs[n][:, cols]
            if prior is not None:
                acc[at, :] = prior[2 * n][:, cols]
                tot[at, :] = prior[2 * n + 1][:, cols]
        empty = [prior is None]

        def add(kv_ref, mask=None):
            scores = mm(qs[...], kv_ref[0][...], NT)
            if mask is not None:
                scores = jnp.where(mask, scores, MASKED)
            weights = jnp.exp2(scores)
            total = weights[:, :128]
            for at in range(128, weights.shape[1], 128):
                total = total + weights[:, at : at + 128]
            part = mm(weights.astype(BF), kv_ref[1][...])
            if empty[0]:
                acc[...] = part
                tot[...] = total
            else:
                acc[...] += part
                tot[...] += total
            empty[0] = False

        if half == 1:
            for kv_ref in slot_refs:
                add(kv_ref)
            low = jnp.concatenate([lo_ref[:, :1], lo_ref[:, :1]])
            for d, kv_ref in zip(halos, halo_refs):
                if d == 0:
                    add(kv_ref, (col <= row) & (col >= low))
                else:

                    @pl.when(lo_first < -(d - 1) * rows)
                    def _(d=d, kv_ref=kv_ref):
                        add(kv_ref, col - d * rows >= low)

        else:
            if 0 in slots:
                add(slot_refs[slots.index(0)], col <= row)
            for bit, group in by_top_bit(slots).items():

                @pl.when(jnp.bitwise_and(me, bit) != 0)
                def _(group=group):
                    for at in group:
                        add(slot_refs[at])

        if not plan["last"]:
            for g in range(2):
                cols, at = slice(g * HEAD_SIZE, (g + 1) * HEAD_SIZE), slice(g * rows, (g + 1) * rows)
                results[2 * n][:, cols] = acc[at, :]
                results[2 * n + 1][:, cols] = tot[at, :]
    if plan["last"]:
        qs, acc, tot = refs
        for g in range(2):
            cols, at = slice(g * HEAD_SIZE, (g + 1) * HEAD_SIZE), slice(g * rows, (g + 1) * rows)
            total = jnp.sum(tot[at, :], axis=1, keepdims=True)
            out_ref[:, cols] = (acc[at, :] / total).astype(BF)
            lse_ref[0, g : g + 1, :] = jnp.log2(jnp.sum(tot[at, :].T, axis=0, keepdims=True))


def attention_forward(halves, scalars, q, low, slots, halos, carry=None, last=None):
    rows, heads = q[0].shape[0], q[0].shape[1] // 256
    plan = dict(halves=halves, slots=list(slots), pairs=[isinstance(kv, tuple) for kv in slots.values()], halos=list(halos), carry=carry is not None,
                last=last is not None, alias=last is not None and last[0] is not None)
    part = lambda h, i: (0, h)
    ins = [(low, (rows, 128), lambda h, i: (0, 0))]
    ins += [(of_half, (rows, 256), part) for of_half in q]
    for kv in list(slots.values()) + list(halos.values()):
        ins += slot_inputs(kv, rows)
    if carry is not None:
        ins += [(c, (rows, 256), part) for c in carry]
    scratch, keep = [], {}
    for _ in halves:
        scratch += [pltpu.VMEM((2 * rows, 128), BF)] + [pltpu.VMEM((2 * rows, 128), F32)] * 2
    state = shaped((rows, heads * 256), F32)
    if last is None:
        outs = [(state, (rows, 256), part)] * (2 * len(halves))
    else:
        other = last[0]
        if other is not None:
            keep = {len(ins): 0}
            ins.append((other, None, None))
        half = halves[0]
        outs = [
            (shaped((2 * rows, heads * 256), BF), (rows, 256), lambda h, i: (half, h)),
            (shaped((heads, 8, rows), F32), (1, 8, rows), lambda h, i: (h, 0, 0)),
        ]
    return call(functools.partial(fwd_kernel, plan), "attend", (heads,), ins, outs, scratch,
                scalars=scalars, keep=keep)


def out_kernel(att_ref, w_ref, part_ref):
    part_ref[...] = mm(att_ref[...], w_ref[...], NT).astype(BF)


def out_projection(half, attended, w_rest):
    rows, cols = attended.shape[0] // 2, attended.shape[1]
    model = w_rest.shape[0]
    ins = [(attended, (rows, cols), lambda j: (half, 0)), (w_rest, (model // 2, cols), lambda j: (j, 0))]
    outs = [(shaped((rows, model), BF), (rows, model // 2), lambda j: (0, j))]
    return call(out_kernel, "out_projection", (2,), ins, outs)[0]


def bwd_kernel(plan, idx_ref, q_ref, do_ref, lse_ref, delta_ref, lo_ref, *refs):
    half, slots, halos = plan["half"], plan["slots"], plan["halos"]
    refs = list(refs)
    slot_refs = take_slots(refs, plan["pairs"])
    halo_refs = take_slots(refs, [False] * len(halos))
    prior_dq = refs.pop(0) if plan["carry"] else None
    prior = [refs.pop(0) for _ in slots] if plan["sum"] else None
    if plan["alias"]:
        refs.pop(0)
    dq_ref = refs.pop(0)
    slot_outs = [refs.pop(0) for _ in slots]
    halo_outs = [refs.pop(0) for _ in halos]
    qs, dos, lses, deltas, dq = refs
    me, lo_first = idx_ref[0], idx_ref[1]
    rows = q_ref.shape[0]
    for g in range(2):
        cols, at = slice(g * HEAD_SIZE, (g + 1) * HEAD_SIZE), slice(g * rows, (g + 1) * rows)
        qs[at, :] = q_ref[:, cols]
        dos[at, :] = do_ref[:, cols]
        lses[:, at] = lse_ref[0, g : g + 1, :]
        deltas[:, at] = delta_ref[0, g : g + 1, :]
    dq[...] = jnp.zeros_like(dq) if prior_dq is None else prior_dq[...]

    def block(kv_ref, out_ref, mask=None, before=None):
        keys = kv_ref[0][...]
        scores = mm(keys, qs[...], NT)
        dp = mm(kv_ref[1][...], dos[...], NT)
        scores = scores - lses[...]
        if mask is not None:
            scores = jnp.where(mask, scores, MASKED)
        probs = jnp.exp2(scores)
        ds = (probs * (dp - deltas[...])).astype(BF)
        dq[...] += mm(keys.T, ds)
        dk, dv = mm(ds, qs[...]) * LN2, mm(probs.astype(BF), dos[...])
        if before is not None:
            dk, dv = dk + before[0].astype(F32), dv + before[1].astype(F32)
        out_ref[0] = dk.astype(BF)
        out_ref[1] = dv.astype(BF)

    lane = lax.broadcasted_iota(jnp.int32, (1, 2 * rows), 1)
    lane = jnp.where(lane >= rows, lane - rows, lane)
    key = lax.broadcasted_iota(jnp.int32, (rows, 1), 0)

    def when(needed, kv_ref, out_ref, mask=None):
        @pl.when(needed)
        def _():
            block(kv_ref, out_ref, mask)

        @pl.when(jnp.logical_not(needed))
        def _():
            out_ref[...] = jnp.zeros_like(out_ref)

    low = lo_ref[:1, :]
    for d, kv_ref, out_ref in zip(halos, halo_refs, halo_outs):
        if d == 0:
            block(kv_ref, out_ref, (key <= lane) & (key >= low))
        else:
            when(lo_first < -(d - 1) * rows, kv_ref, out_ref, key - d * rows >= low)
    if half == 1:
        for at in range(len(slots)):
            block(slot_refs[at], slot_outs[at], None, prior[at] if prior else None)
    else:
        if 0 in slots:
            at = slots.index(0)
            block(slot_refs[at], slot_outs[at], key <= lane)
        for bit, group in by_top_bit(slots).items():

            @pl.when(jnp.bitwise_and(me, bit) != 0)
            def _(group=group):
                for at in group:
                    block(slot_refs[at], slot_outs[at])

            @pl.when(jnp.bitwise_and(me, bit) == 0)
            def _(group=group):
                for at in group:
                    slot_outs[at][...] = jnp.zeros_like(slot_outs[at])

    if plan["last"]:
        for g in range(2):
            cols = slice(g * HEAD_SIZE, (g + 1) * HEAD_SIZE)
            dq_ref[:, cols] = dq[:, g * rows : (g + 1) * rows].T * SCALE
    else:
        dq_ref[...] = dq[...]


def attention_backward(half, scalars, q, do, lse, delta, low, slots, halos, carry=None, prior=None, last=True, whole=None):
    rows, heads = q.shape[0], q.shape[1] // 256
    plan = dict(half=half, slots=list(slots), pairs=[isinstance(kv, tuple) for kv in slots.values()], halos=list(halos), carry=carry is not None,
                sum=prior is not None, last=last, alias=whole is not None)
    part = lambda h, i: (0, h)
    stat = lambda h, i: (h, 0, 0)
    kv_map = lambda h, i: (0, 0, h)
    ins = [
        (q, (rows, 256), part),
        (do, (rows, 256), part),
        (lse, (1, 8, rows), stat),
        (delta, (1, 8, rows), stat),
        (low, (8, 2 * rows), lambda h, i: (0, 0)),
    ]
    pieces = list(slots.values()) + list(halos.values())
    for kv in pieces:
        ins += slot_inputs(kv, rows)
    if carry is not None:
        ins.append((carry, (128, 2 * rows), lambda h, i: (h, 0)))
    if prior is not None:
        ins += [(prior[s], (2, rows, 128), kv_map) for s in slots]
    keep = {}
    if whole is not None:
        keep = {len(ins): 0}
        ins.append((whole, None, None))
    if last:
        outs = [(shaped((rows, heads * 256), F32), (rows, 256), part)]
    else:
        outs = [(shaped((heads * 128, 2 * rows), F32), (128, 2 * rows), lambda h, i: (h, 0))]
    outs += [(shaped((2, rows, heads * 128), BF), (2, rows, 128), kv_map) for _ in pieces]
    scratch = [
        pltpu.VMEM((2 * rows, 128), BF),
        pltpu.VMEM((2 * rows, 128), BF),
        pltpu.VMEM((1, 2 * rows), F32),
        pltpu.VMEM((1, 2 * rows), F32),
        pltpu.VMEM((128, 2 * rows), F32),
    ]
    us = 4 + 6 * (len(slots) + len(halos)) if carry is not None or halos else 0.1
    results = call(functools.partial(bwd_kernel, plan), "attend_back", (heads,), ins, outs, scratch,
                   scalars=scalars, us=us, keep=keep)
    n = len(slots)
    return results[0], dict(zip(slots, results[1 : 1 + n])), dict(zip(halos, results[1 + n :]))


def prompt_back_kernel(plan, idx_ref, qa_ref, qb_ref, doa_ref, dob_ref, lse_ref, lse_b_ref, delta_ref, delta_b_ref, *refs):
    slots, last = plan["slots"], plan["ctx"] - 1
    refs = list(refs)
    slot_refs = take_slots(refs, plan["pairs"])
    prior = {s: refs.pop(0) for s in plan["prior"]}
    dqa_ref, dqb_ref = refs.pop(0), refs.pop(0)
    outs = [refs.pop(0) for _ in slots]
    qs, dos, lses, deltas, dq = refs
    me = idx_ref[0]
    half = qa_ref.shape[0]
    rows = 2 * half
    for part, (q_ref, do_ref) in enumerate(((qa_ref, doa_ref), (qb_ref, dob_ref))):
        for g in range(2):
            cols = slice(g * HEAD_SIZE, (g + 1) * HEAD_SIZE)
            at = slice(part * rows + g * half, part * rows + (g + 1) * half)
            qs[at, :] = q_ref[:, cols]
            dos[at, :] = do_ref[:, cols]
            for total, own, got in ((lses, lse_ref, lse_b_ref), (deltas, delta_ref, delta_b_ref)):
                total[:, at] = (got if part else own)[0, g : g + 1, :half]
    dq[...] = jnp.zeros_like(dq)
    lane = lax.broadcasted_iota(jnp.int32, (1, rows), 1)
    lane = jnp.where(lane >= half, lane - half, lane)
    key = lax.broadcasted_iota(jnp.int32, (rows, 1), 0)

    def block(s, part, mask=None):
        kv_ref, out_ref = slot_refs[slots.index(s)], outs[slots.index(s)]
        at = slice(part * rows, (part + 1) * rows)
        keys = kv_ref[0][...]
        scores = mm(keys, qs[at, :], NT)
        dp = mm(kv_ref[1][...], dos[at, :], NT)
        scores = scores - lses[:, at]
        if mask is not None:
            scores = jnp.where(mask, scores, MASKED)
        probs = jnp.exp2(scores)
        ds = (probs * (dp - deltas[:, at])).astype(BF)
        dq[:, at] += mm(keys.T, ds)
        before = out_ref if part else prior.get(s)
        for which, value in enumerate((mm(ds, qs[at, :]) * LN2, mm(probs.astype(BF), dos[at, :]))):
            if before is not None:
                value = value + before[which].astype(F32)
            out_ref[which] = value.astype(BF)

    block(0, 0, key <= lane)
    for bit, group in by_top_bit(slots).items():
        group = [slots[at] for at in group]

        @pl.when(jnp.bitwise_and(me, bit) != 0)
        def _(group=group):
            for s in group:
                block(s, 0)

        @pl.when(jnp.bitwise_and(me, bit) == 0)
        def _(group=group):
            for s in group:
                out_ref = outs[slots.index(s)]
                out_ref[...] = prior[s][...] if s in prior else jnp.zeros_like(out_ref)

    block(last, 1, key <= lane + half)
    for bit, group in by_top_bit(slots).items():

        @pl.when(jnp.bitwise_and(me, bit) == 0)
        def _(group=[slots[at] ^ last for at in group]):
            for s in group:
                block(s, 1)

    for part, out_ref in enumerate((dqa_ref, dqb_ref)):
        for g in range(2):
            at = slice(part * rows + g * half, part * rows + (g + 1) * half)
            cols = slice(g * HEAD_SIZE, (g + 1) * HEAD_SIZE)
            out_ref[:, cols] = (dq[:, at].T * SCALE).astype(out_ref.dtype)


def prompt_backward(scalars, ctx, own, got, slots, prior):
    rows, heads = own[0].shape[0], own[0].shape[1] // 256
    half = rows // 2
    plan = dict(slots=list(slots), prior=list(prior), ctx=ctx,
                pairs=[isinstance(kv, tuple) for kv in slots.values()])
    part = lambda h, i: (0, h)
    stat = lambda h, i: (h, 0, 0)
    kv_map = lambda h, i: (0, 0, h)
    ins = []
    for mine, other in zip(own[:2], got[:2]):
        ins += [(mine, (half, 256), part), (other, (half, 256), part)]
    for mine, other in zip(own[2:], got[2:]):
        ins += [(mine, (1, 8, rows), stat), (other, (1, 8, half), stat)]
    for kv in slots.values():
        ins += slot_inputs(kv, rows)
    ins += [(grad, (2, rows, 128), kv_map) for grad in prior.values()]
    outs = [(shaped((half, heads * 256), kind), (half, 256), part) for kind in (F32, BF)]
    outs += [(shaped((2, rows, heads * 128), BF), (2, rows, 128), kv_map) for _ in slots]
    scratch = [
        pltpu.VMEM((2 * rows, 128), BF),
        pltpu.VMEM((2 * rows, 128), BF),
        pltpu.VMEM((1, 2 * rows), F32),
        pltpu.VMEM((1, 2 * rows), F32),
        pltpu.VMEM((128, 2 * rows), F32),
    ]
    results = call(functools.partial(prompt_back_kernel, plan), "prompt_back", (heads,), ins, outs, scratch,
                   scalars=scalars, us=16)
    return results[0], results[1], dict(zip(slots, results[2:]))


def ffn_kernel(x_ref, own_ref, got_ref, gain_ref, dy_ref, gu_ref, down_ref, *refs):
    resid_ref, normed_ref, hidden_ref, dgu_ref, out_ref, back_ref, normed, out_acc, back_acc = refs[-9:]
    step, steps = pl.program_id(0), pl.num_programs(0)

    @pl.when(step == 0)
    def _():
        resid = x_ref[...].astype(F32) + (own_ref[...].astype(F32) + got_ref[...].astype(F32))
        resid_ref[...] = resid
        normed[...] = (resid * rms(resid) * gain_ref[...]).astype(BF)
        normed_ref[...] = normed[...]
        out_acc[...] = jnp.zeros_like(out_acc)
        back_acc[...] = jnp.zeros_like(back_acc)

    wide = down_ref.shape[1]
    both = mm(normed[...], gu_ref[...])
    d_hidden = mm(dy_ref[...], down_ref[...])
    gate, up = both[:, :wide], both[:, wide:]
    sig = 1.0 / (1.0 + jnp.exp(-gate))
    silu = gate * sig
    hidden = (silu * up).astype(BF)
    hidden_ref[...] = hidden
    d_up = (d_hidden * silu).astype(BF)
    d_gate = (d_hidden * up * (sig + silu * (1.0 - sig))).astype(BF)
    dgu_ref[:, :wide] = d_gate
    dgu_ref[:, wide:] = d_up
    out_acc[...] += mm(hidden, down_ref[...], NT)
    back_acc[...] += mm(dgu_ref[...], gu_ref[...], NT)

    @pl.when(step == steps - 1)
    def _():
        out_ref[...] = out_acc[...].astype(BF)
        back_ref[...] = back_acc[...].astype(BF)


def feed_forward(half, x, own, got, gain, dy, w_od, w_gu, chunk, whole=None):
    rows, model = own.shape
    units = w_gu.shape[1] // 2
    steps = units // chunk
    mine, once = lambda f: (half, 0), lambda f: (0, 0)
    at_down = (w_od.shape[1] - units) // chunk
    block = (rows, model)
    ins = [
        (x, block, mine), (own, block, once), (got, block, once), (gain, (1, model), once), (dy, block, mine),
        (w_gu, (model, 2 * chunk), lambda f: (0, f)),
        (w_od, (model, chunk), lambda f: (0, at_down + f)),
    ]
    keep = {}
    if whole is not None:
        keep = {len(ins) + i: 1 + i for i in range(3)}
        ins += [(array, None, None) for array in whole]
    outs = [
        (shaped((rows, model), F32), block, once),
        (shaped((2 * rows, model), BF), block, mine),
        (shaped((2 * rows, units), BF), (rows, chunk), lambda f: (half, f)),
        (shaped((2 * rows, 2 * units), BF), (rows, 2 * chunk), lambda f: (half, f)),
        (shaped((rows, model), BF), block, once),
        (shaped((rows, model), BF), block, once),
    ]
    scratch = [pltpu.VMEM(block, BF), pltpu.VMEM(block, F32), pltpu.VMEM(block, F32)]
    return call(ffn_kernel, "feed_forward", (steps,), ins, outs, scratch, keep=keep)


def norm_back(grad, values, gain):
    scale = rms(values)
    unit = values * scale
    inner = grad * gain
    return scale * (inner - unit * jnp.mean(inner * unit, axis=-1, keepdims=True)), grad * unit


def lane_mean(values):
    width = values.shape[-1]
    ones = jnp.ones((width, width), BF)
    high = values.astype(BF)
    low = (values - high.astype(F32)).astype(BF)
    return (mm(high, ones) + mm(low, ones)) * (1.0 / width)


def head_norm_back(grad, values, gain):
    scale = lax.rsqrt(lane_mean(values * values) + EPSILON)
    unit = values * scale
    inner = grad * gain
    return scale * (inner - unit * lane_mean(inner * unit)), grad * unit


def row_blocks(rows):
    size = rows // 2 if rows % 512 == 0 else rows
    return size, rows // size


def add_up(ref, value):
    total = jnp.sum(value, axis=0, keepdims=True)

    @pl.when(pl.program_id(0) == 0)
    def _():
        ref[...] = total

    @pl.when(pl.program_id(0) > 0)
    def _():
        ref[...] += total


def mixed_kernel(heads, own_ref, got_ref, resid_ref, gain_ref, dy_ref, w_ref, att_ref, *refs):
    d_resid_ref, mixed_ref, datt_ref, delta_ref, dgain_ref = refs[-5:]
    grad = own_ref[...].astype(F32) + got_ref[...].astype(F32)
    d_norm, summand = norm_back(grad, resid_ref[...], gain_ref[...])
    add_up(dgain_ref, summand)
    d_resid = dy_ref[...].astype(F32) + d_norm
    d_resid_ref[...] = d_resid
    mixed_ref[...] = d_resid.astype(BF)
    datt_ref[...] = mm(mixed_ref[...], w_ref[...]).astype(BF)
    for h in range(heads):
        cols = slice(h * HEAD_SIZE, (h + 1) * HEAD_SIZE)
        product = datt_ref[:, cols].astype(F32) * att_ref[:, cols].astype(F32)
        delta_ref[h // 2, h % 2 : h % 2 + 1, :] = jnp.sum(product.T, axis=0, keepdims=True)


def mixed_back(half, own, got, resid, gain, dy, w_rest, o_cols, attended, whole=None):
    rows, model = own.shape
    heads = o_cols // HEAD_SIZE
    size, steps = row_blocks(rows)
    mine, here, once = lambda f: (half * steps + f, 0), lambda f: (f, 0), lambda f: (0, 0)
    block = (size, model)
    ins = [
        (own, block, here), (got, block, here), (resid, block, here), (gain, (1, model), once),
        (dy, block, mine), (w_rest, (model, o_cols), once), (attended, (size, o_cols), mine),
    ]
    keep = {}
    if whole is not None:
        keep = {len(ins): 1}
        ins.append((whole, None, None))
    outs = [
        (shaped((rows, model), F32), block, here),
        (shaped((2 * rows, model), BF), block, mine),
        (shaped((rows, o_cols), BF), (size, o_cols), here),
        (shaped((heads // 2, 8, rows), F32), (heads // 2, 8, size), lambda f: (0, 0, f)),
        (shaped((1, model), F32), (1, model), once),
    ]
    return call(functools.partial(mixed_kernel, heads), "mixed_back", (steps,), ins, outs, keep=keep)


def merge_kernel(two, got3, four, got5, far_k, far_v, to_x, to_y):
    for which in range(2):
        by_x = two[which].astype(F32) + got3[which].astype(F32)
        by_y = four[which].astype(F32) + got5[which].astype(F32)
        to_x[which] = (by_x + far_v[...].astype(F32) if which else by_x).astype(BF)
        to_y[which] = (by_y if which else by_y + far_k[...].astype(F32)).astype(BF)


def merge(*pieces):
    rows, cols = pieces[-1].shape
    size, steps = row_blocks(rows)
    ins = []
    for piece in pieces:
        if piece.ndim == 3:
            ins.append((piece, (2, size, cols), lambda f: (0, f, 0)))
        else:
            ins.append((piece, (size, cols), lambda f: (f, 0)))
    outs = [(shaped((2, rows, cols), BF), (2, size, cols), lambda f: (0, f, 0))] * 2
    return call(merge_kernel, "merge", (steps,), ins, outs)


def weight_kernel(left_ref, right_ref, *refs):
    refs[-1][...] = mm(left_ref[...], right_ref[...], TN).astype(BF)


def weight_grad(left, right, at, width, cols, whole=None):
    tokens, model = left.shape
    n = right.shape[1]
    ins = [(left, (tokens, model), lambda j: (0, 0)), (right, (tokens, cols), lambda j: (0, j))]
    keep = {}
    if whole is not None:
        keep = {len(ins): 0}
        ins.append((whole, None, None))
    outs = [(shaped((model, width), BF), (model, cols), lambda j: (0, at // cols + j))]
    return call(weight_kernel, "weight_grad", (n // cols,), ins, outs, keep=keep)[0]


def slot_weight_kernel(order, part_ref, left_ref, right_ref, low_ref, high_ref, total):
    total[...] = mm(left_ref[...], right_ref[...], TN)
    wide = total.shape[0] // len(order)
    for at, slot in enumerate(order):
        block = jnp.bitwise_xor(part_ref[0], slot)
        piece = total[pl.ds(pl.multiple_of(block * wide, wide), wide), :].astype(BF)
        out_ref, row = (low_ref, at) if at < len(order) // 2 else (high_ref, at - len(order) // 2)
        out_ref[row * wide : (row + 1) * wide, :] = piece


def slot_weight_grad(order, part, left, right):
    tokens, model = left.shape
    cols = right.shape[1]
    once = lambda j, i: (0, 0)
    ins = [(left, (tokens, model), once), (right, (tokens, cols), once)]
    half = shaped((model // 2, cols), BF)
    return call(functools.partial(slot_weight_kernel, order), "slot_weight_grad", (1,), ins,
                [(half, half.shape, once)] * 2, [pltpu.VMEM((model, cols), F32)], scalars=part[None])


def weight_halves_kernel(left_ref, right_ref, high_ref, low_ref):
    for half, out_ref in enumerate((high_ref, low_ref)):

        @pl.when(pl.program_id(0) == half)
        def _(out_ref=out_ref):
            out_ref[...] = mm(left_ref[...], right_ref[...], TN).astype(BF)


def weight_halves(left, right):
    tokens, model = left.shape
    cols = right.shape[1]
    once = lambda i: (0, 0)
    ins = [(left, (tokens, model // 2), lambda i: (0, 1 - i)), (right, (tokens, cols), once)]
    half = shaped((model // 2, cols), BF)
    return call(weight_halves_kernel, "weight_halves", (2,), ins, [(half, half.shape, once)] * 2)


def q_back_kernel(heads, dqa_ref, dqb_ref, dqc_ref, lin_ref, gain_ref, cos_ref, sin_ref, w_ref, *refs):
    d_ref, part_ref, gains_ref, dq_ref = refs[-4:]
    step = pl.program_id(0)

    @pl.when(step == 0)
    def _():
        dq_ref[...] = dqa_ref[...]

    @pl.when(step == 1)
    def _():
        dq_ref[...] = dqb_ref[...].astype(F32)

    @pl.when(step > 1)
    def _():
        dq_ref[...] = dqc_ref[...]

    cos, sin = cos_ref[...], sin_ref[...]
    total = jnp.zeros(cos.shape, F32)
    for h in range(heads):
        cols = slice(h * HEAD_SIZE, (h + 1) * HEAD_SIZE)
        grad, summand = head_norm_back(turn_back(dq_ref[:, cols], cos, sin), lin_ref[:, cols], gain_ref[...])
        d_ref[:, cols] = grad.astype(BF)
        total = total + summand
    part_ref[...] = mm(d_ref[...], w_ref[...], NT)
    add_up(gains_ref, total)


def q_back(dq_a, dq_b, dq_c, lin, gain, cos, sin, w):
    rows, cols = lin.shape
    model = w.shape[0]
    size = rows // 4
    here, once = lambda f: (f, 0), lambda f: (0, 0)
    ins = [
        (dq_a, (size, cols), once), (dq_b, (size, cols), once), (dq_c, (size, cols), lambda f: (jnp.maximum(f - 2, 0), 0)),
        (lin, (size, cols), here), (gain, (1, HEAD_SIZE), once),
        (cos, (size, HEAD_SIZE), here), (sin, (size, HEAD_SIZE), here), (w, (model, cols), once),
    ]
    outs = [
        (shaped((rows, cols), BF), (size, cols), here),
        (shaped((rows, model), F32), (size, model), here),
        (shaped((1, HEAD_SIZE), F32), (1, HEAD_SIZE), once),
    ]
    kernel = functools.partial(q_back_kernel, cols // HEAD_SIZE)
    return call(kernel, "q_back", (4,), ins, outs, [pltpu.VMEM((size, cols), F32)])


def kv_back_kernel(heads, n_keys, n_values, lin_ref, gain_ref, cos_ref, sin_ref, w_ref, slots_ref, q_part_ref, *refs):
    key_refs, value_refs = refs[:n_keys], refs[n_keys : n_keys + n_values]
    d_ref, part_ref, gains_ref = refs[-3:]
    cos, sin = cos_ref[...], sin_ref[...]
    width = heads * HEAD_SIZE

    def total(sources, which, cols):
        value = None
        for ref in sources:
            piece = ref[which, :, cols] if len(ref.shape) == 3 else ref[:, cols]
            value = piece.astype(F32) if value is None else value + piece.astype(F32)
        return value

    gains = jnp.zeros(cos.shape, F32)
    for h in range(heads):
        cols = slice(h * HEAD_SIZE, (h + 1) * HEAD_SIZE)
        grad, summand = head_norm_back(
            turn_back(total(key_refs, 0, cols), cos, sin), lin_ref[:, cols], gain_ref[...]
        )
        d_ref[:, cols] = grad.astype(BF)
        gains = gains + summand
    d_ref[:, width:] = total(value_refs, 1, slice(None)).astype(BF)
    part = (q_part_ref[...] + mm(d_ref[...], w_ref[...], NT)).astype(BF)
    part_ref[...] = mm(part, slots_ref[...], NT).astype(BF)
    add_up(gains_ref, gains)


def kv_back(half, keys, values, lin, gain, cos, sin, w, to_slots, q_part, whole=None):
    rows, cols = lin.shape
    model = w.shape[0]
    size, steps = row_blocks(rows)
    mine, here, once = lambda f: (half * steps + f, 0), lambda f: (f, 0), lambda f: (0, 0)
    ins = [
        (lin, (size, cols), here), (gain, (1, HEAD_SIZE), once), (cos, (size, HEAD_SIZE), mine),
        (sin, (size, HEAD_SIZE), mine), (w, (model, 2 * cols), once),
        (to_slots, (model, model), once), (q_part, (size, model), mine),
    ]
    for piece in list(keys) + list(values):
        if piece.ndim == 3:
            ins.append((piece, (2, size, cols), lambda f: (0, f, 0)))
        else:
            ins.append((piece, (size, cols), here))
    keep = {}
    if whole is not None:
        keep = {len(ins): 0}
        ins.append((whole, None, None))
    outs = [
        (shaped((2 * rows, 2 * cols), BF), (size, 2 * cols), mine),
        (shaped((rows, model), BF), (size, model), here),
        (shaped((1, HEAD_SIZE), F32), (1, HEAD_SIZE), once),
    ]
    kernel = functools.partial(kv_back_kernel, cols // HEAD_SIZE, len(keys), len(values))
    return call(kernel, "kv_back", (steps,), ins, outs, keep=keep, us=3 * (1 - half))


def tokens_kernel(own_ref, got_ref, x_ref, gain_ref, d_resid_ref, *refs):
    out_ref, dgain_ref = refs[-2:]
    grad = own_ref[...].astype(F32) + got_ref[...].astype(F32)
    d_norm, summand = norm_back(grad, x_ref[...].astype(F32), gain_ref[...])
    add_up(dgain_ref, summand)
    out_ref[...] = (d_resid_ref[...] + d_norm).astype(BF)


def tokens_back(half, own, got, x, gain, d_resid, whole=None):
    rows, model = own.shape
    size, steps = row_blocks(rows)
    mine, here, once = lambda f: (half * steps + f, 0), lambda f: (f, 0), lambda f: (0, 0)
    block = (size, model)
    ins = [(own, block, here), (got, block, here), (x, block, mine), (gain, (1, model), once), (d_resid, block, here)]
    keep = {}
    if whole is not None:
        keep = {len(ins): 0}
        ins.append((whole, None, None))
    outs = [(shaped((2 * rows, model), BF), block, mine), (shaped((1, model), F32), (1, model), once)]
    return call(tokens_kernel, "tokens_back", (steps,), ins, outs, keep=keep, us=20)


def share_kernel(chunk, ffn_ref, own_ref, got_ref, out_ref, gate_ref, up_ref, down_ref):
    units = gate_ref.shape[1]
    out_ref[...] = own_ref[...].astype(F32) + got_ref[...].astype(F32)
    for at in range(0, units, chunk):
        gate_ref[:, at : at + chunk] = ffn_ref[:, 2 * at : 2 * at + chunk].astype(F32)
        up_ref[:, at : at + chunk] = ffn_ref[:, 2 * at + chunk : 2 * at + 2 * chunk].astype(F32)
    down_ref[...] = ffn_ref[:, 2 * units :].astype(F32)


def unpack(chunk, ffn_share, out_grad):
    wide, units = ffn_share.shape[0], ffn_share.shape[1] // 3
    o_cols = out_grad[0].shape[1]
    whole = lambda f: (0, 0)
    ins = [(ffn_share, ffn_share.shape, whole)] + [(grad, (wide, o_cols), whole) for grad in out_grad]
    outs = [(shaped((wide, cols), F32), (wide, cols), whole) for cols in (o_cols, units, units, units)]
    return call(functools.partial(share_kernel, chunk), "unpack", (1,), ins, outs)


def layer_kernel(resid_ref, own_ref, got_ref, *refs):
    refs[-1][...] = (resid_ref[...] + (own_ref[...].astype(F32) + got_ref[...].astype(F32))).astype(BF)


def add_layer(half, resid, own, got, whole=None):
    rows, model = resid.shape
    size, steps = row_blocks(rows)
    here, mine = lambda f: (f, 0), lambda f: (half * steps + f, 0)
    ins = [(array, (size, model), here) for array in (resid, own, got)]
    keep = {}
    if whole is not None:
        keep = {len(ins): 0}
        ins.append((whole, None, None))
    outs = [(shaped((2 * rows, model), BF), (size, model), mine)]
    return call(layer_kernel, "add_layer", (steps,), ins, outs, keep=keep)[0]


def swap(value, axis, bit):
    size = lax.axis_size(axis)
    return lax.ppermute(value, axis, [(i, i ^ bit) for i in range(size)])


def shift(value, by):
    size = lax.axis_size("ctx")
    return lax.ppermute(value, "ctx", [(i, i + by) for i in range(size) if 0 <= i + by < size])


def add_low(left, right):
    return (left.astype(F32) + right.astype(F32)).astype(BF)


def butterfly(value, axes, gates=()):
    gates = list(gates)
    for axis in axes:
        bit = 1
        while bit < lax.axis_size(axis):
            got = swap(value, axis, bit)
            value = value + (after(got, gates.pop(0)) if gates else got)
            bit *= 2
    return value


def after(value, *others):
    return lax.optimization_barrier((value, *others))[0]


def rotary_tables(position):
    half_dim = HEAD_SIZE // 2
    inverse_freq = jnp.exp(jnp.arange(half_dim, dtype=F32) * (-math.log(ROPE_BASE) / half_dim))
    angles = position.astype(F32)[:, None] * inverse_freq[None, :]
    cosine, sine = jnp.cos(angles), jnp.sin(angles)
    return jnp.concatenate([cosine, cosine], axis=-1), jnp.concatenate([-sine, sine], axis=-1)


def body(
    tokens,
    cont_lengths,
    attn_gain,
    ffn_gain,
    query_gain,
    key_gain,
    w_query,
    key_weight,
    value_weight,
    w_out,
    w_gate,
    w_up,
    w_down,
    cotangent,
):
    ctx_size = lax.axis_size("ctx")
    weight_axes = ("shard", "ctx")
    parts = lax.axis_size("shard") * ctx_size
    me = lax.axis_index("ctx")
    part = lax.axis_index("shard") * ctx_size + me
    rows, model = tokens.shape[0] // 2, tokens.shape[1]
    n_halo = 1 + -(-(LONGEST - 1) // rows)
    lengths = cont_lengths[0]

    bits = [("shard", 1)] + [("ctx", 1 << i) for i in range(1, ctx_size.bit_length() - 1)] + [("ctx", 1)]
    order = [0]
    for axis, bit in bits:
        order += [j ^ (bit * ctx_size if axis == "shard" else bit) for j in order]
    wide, narrow = attn_gain.shape[0], query_gain.shape[0]
    q_cols, k_cols = w_query.shape[1], key_weight.shape[1]
    o_cols, units = w_out.shape[0], w_gate.shape[1]
    heads, kv_heads = q_cols // HEAD_SIZE, k_cols // HEAD_SIZE
    chunk = math.gcd(units, 512)

    def gather_first(piece, *gate):
        return jnp.concatenate([piece, after(swap(piece, "shard", 1), *gate)]) if ctx_size == 8 else piece

    def gather_near(one, *gate):
        if ctx_size != 8:
            for axis, bit in bits:
                one = jnp.concatenate([one, swap(one, axis, bit)])
            return [one]
        return [one] + [after(swap(one, "ctx", bit), *gate) for bit in (2, 4, 6)]

    def gather_far(near, *gate):
        if ctx_size != 8:
            return near
        return near + [after(swap(piece, "ctx", 1), *gate) for piece in near]

    def scatter_rows(low, high, late):
        total = add_low(low, after(swap(high, "ctx", 1), late))
        if ctx_size != 8:
            for axis, bit in bits[-2:0:-1]:
                size = total.shape[0] // 2
                total = add_low(total[:size], swap(total[size:], axis, bit))
            return (total,)
        size = total.shape[0] // 4
        by_x, by_y, far = (total[i * size : (i + 1) * size] for i in (1, 2, 3))
        return total, swap(by_x, "ctx", 2), swap(by_y, "ctx", 4), swap(far, "ctx", 6)

    def scatter_first(low, high, late):
        if ctx_size != 8:
            return scatter_rows(low, high, late)
        total = add_low(low, after(swap(high, "ctx", 1), late))
        size, cut = total.shape[0] // 4, total.shape[1] // 2
        own, by_x, by_y, far = (total[i * size : (i + 1) * size] for i in range(4))
        left, right = swap(far[:, :cut], "ctx", 2), swap(far[:, cut:], "ctx", 4)
        return own, by_x, by_y, left, right

    def scatter_more(stage, late):
        if ctx_size != 8:
            return stage
        own, by_x, by_y, left, right = stage
        left, right = after(left, late), after(right, late)
        cut = left.shape[1]
        by_x = jnp.concatenate([by_x[:, :cut], add_low(by_x[:, cut:], right)], axis=1)
        by_y = jnp.concatenate([add_low(by_y[:, :cut], left), by_y[:, cut:]], axis=1)
        return lax.optimization_barrier((own, by_x, by_y))[0], swap(by_x, "ctx", 2), swap(by_y, "ctx", 4)

    def scatter_sum(stage, late):
        total = stage[0].astype(F32)[: stage[-1].shape[0]]
        for piece in stage[1:]:
            total = total + after(piece, late).astype(F32)
        total, size = total.astype(BF), total.shape[0] // 2
        return total, swap(total[size:], "shard", 1)

    kv_piece, od_piece, gu_piece = pack(
        chunk, key_weight, value_weight, w_out.T, w_down.T, w_gate, w_up
    )
    kv_one = gather_first(kv_piece)
    kv_near = gather_near(kv_one)
    kv_pieces = gather_far(kv_near)
    q_one = gather_first(after(w_query, kv_one), kv_near[-1])
    w_od = lax.all_gather(od_piece, weight_axes, axis=0, tiled=True)
    gains = jnp.concatenate([attn_gain, ffn_gain, query_gain, key_gain])[None]
    gains = jnp.where(jnp.arange(parts)[:, None] == part, gains, jnp.zeros((), BF))
    gains = gains + after(swap(gains, "ctx", 1), kv_piece)
    for at, (axis, bit) in enumerate(bits[:-1]):
        gains = gains + after(swap(gains, axis, bit), (kv_one, kv_near[-1], kv_near[-1])[min(at, 2)])
    gains = gains.astype(F32)
    gain_one = gains[:, :wide].reshape(1, -1)
    gain_two = gains[:, wide : 2 * wide].reshape(1, -1)
    gain_q = gains[:, 2 * wide : 2 * wide + narrow].reshape(1, -1)
    gain_k = gains[:, 2 * wide + narrow :].reshape(1, -1)
    source = jnp.bitwise_xor(part, jnp.array(order, jnp.int32))[:, None] * wide + jnp.arange(wide, dtype=jnp.int32)
    to_slots = (jnp.arange(model, dtype=jnp.int32)[:, None] == source.reshape(1, -1)).astype(BF)
    tokens_s = mm(after(tokens, q_one), to_slots).astype(BF)
    gain_one_s = mm(gain_one.astype(BF), to_slots)

    cont_at = me * rows + jnp.arange(rows, dtype=jnp.int32)
    cont_ends = jnp.cumsum(lengths)
    starts = cont_ends - lengths
    seg = jnp.sum((cont_ends[None, :] <= cont_at[:, None]).astype(jnp.int32), axis=1)
    numbers = jnp.arange(lengths.shape[0], dtype=jnp.int32)
    first = jnp.sum(jnp.where(numbers[None, :] == seg[:, None], starts[None, :], 0), axis=1)
    position = jnp.concatenate([me * rows + jnp.arange(rows, dtype=jnp.int32), PROMPT + cont_at - first])
    low = first - me * rows
    low_col = jnp.broadcast_to(low[:, None], (rows, 128))
    low_row = jnp.broadcast_to(jnp.concatenate([low, low])[None, :], (8, 2 * rows))
    scalars = jnp.stack([me, low[0]])
    cos, sin = rotary_tables(position)

    once = lambda f: (0, 0)

    def weight_inputs(pieces):
        return [(piece, piece.shape, once) for piece in pieces]

    def keys_values(half, gain, pieces, whole=None):
        mine = lambda f: (half, 0)
        ins = [
            (tokens_s, (rows, model), mine), (gain, (1, model), once), (gain_k, (1, HEAD_SIZE), once),
            (cos, (rows, HEAD_SIZE), mine), (sin, (rows, HEAD_SIZE), mine), *weight_inputs(pieces),
        ]
        keep = {}
        if whole is not None:
            keep = {len(ins): 0}
            ins.append((whole, None, None))
        outs = [
            (shaped((2 * rows, model), BF), (rows, model), mine),
            (shaped((2, rows, k_cols), BF), (2, rows, k_cols), lambda f: (0, 0, 0)),
            (shaped((rows, k_cols), F32), (rows, k_cols), once),
        ]
        if len(pieces) > 1:
            outs.append((shaped((model, 2 * k_cols), BF), (model, 2 * k_cols), once))
        return call(functools.partial(kv_kernel, kv_heads, len(pieces)), "keys_values", (1,), ins, outs, keep=keep)

    q_near = gather_near(q_one, kv_pieces[-1])
    normed, kv_p, k_lin_p, *w_kv = keys_values(0, after(gain_one_s, *q_near[1:]), kv_pieces)
    (w_kv,) = w_kv or kv_pieces
    normed, kv_c, k_lin_c = keys_values(1, after(gain_one_s, kv_p), [w_kv], normed)
    q_pieces = gather_far(q_near, kv_c)

    def queries(half, gain, pieces, whole=None):
        mine = lambda f: (half, 0)
        ins = [
            (normed, (rows, model), mine), (gain, (1, HEAD_SIZE), once),
            (cos, (rows, HEAD_SIZE), mine), (sin, (rows, HEAD_SIZE), mine), *weight_inputs(pieces),
        ]
        keep = {}
        if whole is not None:
            keep = {len(ins): 1}
            ins.append((whole, None, None))
        outs = [
            (shaped((rows, q_cols), BF), (rows, q_cols), once),
            (shaped((2 * rows, q_cols), F32), (rows, q_cols), mine),
        ]
        if len(pieces) > 1:
            outs.append((shaped((model, q_cols), BF), (model, q_cols), once))
        return call(functools.partial(q_kernel, heads, len(pieces)), "queries", (1,), ins, outs, keep=keep)

    q_c, q_lin, *w_q = queries(1, gain_q, q_pieces)
    (w_q,) = w_q or q_pieces
    q_p, q_lin = queries(0, after(gain_q, q_c), [w_q], q_lin)

    def pick(source, wanted):
        return {s: source[s] for s in source if s in wanted}

    near, middle, far = (0, 1), (2, 3, 4, 5), tuple(range(6, ctx_size))
    slots, halos = {0: kv_p}, {0: kv_c}
    odd = (me % 2) == 1
    if ctx_size == 8:
        slots[1], slots[2], slots[4] = (swap(kv_p, "ctx", bit) for bit in (1, 2, 4))
    else:
        both, bit = kv_p[None], 1
        while bit < ctx_size:
            both = jnp.concatenate([both, swap(both, "ctx", bit)])
            bit *= 2
        slots = {s: both[s] for s in range(ctx_size)}
        halos.update({d: shift(kv_c, d) for d in range(1, n_halo)})
    ready = ()
    if ctx_size == 8:
        slots[2], slots[4] = after(slots[2], q_p), after(slots[4], q_p)
        far_k, far_v = swap(slots[4][0], "ctx", 2), swap(slots[2][1], "ctx", 4)
        slots[3], slots[5] = swap(slots[2], "ctx", 1), swap(slots[4], "ctx", 1)
        halos[2] = shift(after(kv_c, slots[2]), 2)
        gu_piece = after(gu_piece, slots[2], slots[4])
        ready = (slots[2], slots[4])
    w_gu = lax.all_gather(after(gu_piece, w_od), weight_axes, axis=0, tiled=True)
    c_state = attention_forward(
        (1,), after(scalars, *ready), (q_c,), low_col, pick(slots, near), pick(halos, (0,))
    )
    if ctx_size == 8:
        slots[6] = after(far_k, c_state[0]), after(far_v, c_state[0])
        slots[7] = tuple(swap(part, "ctx", 1) for part in slots[6])
    attended, lse_p = attention_forward(
        (0,), after(scalars, c_state[0]), (q_p,), low_col, slots, {}, None, (None,)
    )
    part_p = out_projection(0, attended, w_od)
    got_p = swap(part_p, "tensor", 1)
    if ctx_size == 8:
        halos[1] = swap(jnp.where(odd, after(halos[2], part_p), kv_c), "ctx", 1)
    attended, lse_c = attention_forward(
        (1,), after(scalars, part_p), (q_c,), low_col, pick(slots, middle + far), pick(halos, range(1, n_halo)),
        c_state, (attended,),
    )
    part_c = out_projection(1, attended, w_od)
    got_c = swap(part_c, "tensor", 1)

    resid_p, *whole, out_p, back_p = feed_forward(
        0, tokens, part_p, got_p, after(gain_two, part_c), cotangent, w_od, w_gu, chunk
    )
    back_got_p = swap(back_p, "tensor", 1)
    resid_c, *whole, out_c, back_c = feed_forward(
        1, tokens, part_c, got_c, after(gain_two, back_p), cotangent, w_od, w_gu, chunk, whole
    )
    back_got_c = swap(back_c, "tensor", 1)
    normed_ffn, hidden, d_gu = whole
    ffn_grads = weight_grad(normed_ffn, d_gu, 0, 3 * units, 2 * chunk)
    ffn_grads = weight_grad(cotangent, hidden, 2 * units, 3 * units, chunk, ffn_grads)
    ffn_share = lax.psum_scatter(ffn_grads, weight_axes, scatter_dimension=0, tiled=True)
    def mirror(value):
        return lax.ppermute(value, "ctx", [(i, i ^ (ctx_size - 1)) for i in range(ctx_size)])

    half = rows // 2
    q_b, lse_b = mirror(after(q_p, part_c)[half:]), mirror(after(lse_p, part_c)[:, :, half:])
    d_resid_p, d_mixed, d_att_p, delta_p, d_two_p = mixed_back(
        0, back_p, back_got_p, resid_p, after(gain_two, ffn_grads, q_b, lse_b), cotangent, w_od, o_cols, attended
    )

    do_b, delta_b = mirror(d_att_p[half:]), mirror(delta_p[:, :, half:])
    d_resid_c, d_mixed, d_att_c, delta_c, d_two_c = mixed_back(
        1, back_c, back_got_c, resid_c, after(gain_two, d_att_p), cotangent, w_od, o_cols, attended, d_mixed
    )
    out_low, out_high = slot_weight_grad(order, part, d_mixed, attended)
    out_p = after(out_p, out_low)
    out_got_p = swap(out_p, "tensor", 1)

    def back_c_rows(deps, slots, halos, carry, prior=None, last=False):
        return attention_backward(
            1, after(scalars, *deps), q_c, d_att_c, lse_c, delta_c, low_row, slots, halos, carry, prior, last
        )

    dq_c, from_c, g_halo = back_c_rows((out_low,), pick(slots, far), halos, None)
    out_c = after(out_c, dq_c)
    out_got_c = swap(out_c, "tensor", 1)
    out_grad = scatter_rows(out_low, out_high, dq_c)
    if ctx_size == 8:
        near_one = swap(g_halo[1], "ctx", 1)
    dq_a, dq_b, from_p = prompt_backward(
        after(scalars, dq_c, out_got_p, out_grad[0]), ctx_size, (q_p, d_att_p, lse_p, delta_p),
        (q_b, do_b, lse_b, delta_b), slots, from_c,
    )
    g = pick(from_p, far)
    zero = jnp.zeros((), BF)
    ready = ()
    if ctx_size == 8:
        got7 = swap(g[7], "ctx", 1)
        near_one = after(near_one, dq_a)
        two_back = add_low(g_halo[2], jnp.where(odd, near_one, zero))
        halo_two = shift(two_back, -2)
        halo_near = jnp.where(odd, zero, near_one)
        ready = (two_back, halo_near)
    dq_c, more, _ = back_c_rows((dq_a, out_got_c, *ready), pick(slots, middle), {}, dq_c, from_p)
    g.update(more)
    dq_b = mirror(after(dq_b, dq_c))
    out_grad = scatter_sum(out_grad, dq_c)
    if ctx_size == 8:
        g6 = add_low(g[6], after(got7, dq_c))
        far_k, far_v = swap(g6[0], "ctx", 2), swap(g6[1], "ctx", 4)
        got3, got5 = swap(g[3], "ctx", 1), swap(g[5], "ctx", 1)
        ready = (g6, halo_two)
    dq_c, more, _ = back_c_rows(
        (dq_c, out_grad[0], *ready), pick(slots, near), {}, dq_c, from_p, True
    )
    g.update(more)
    if ctx_size == 8:
        got1 = swap(g[1], "ctx", 1)
        far_k, far_v, got3, got5 = (after(v, dq_c, dq_b, ffn_share) for v in (far_k, far_v, got3, got5))
        to_x, to_y = merge(g[2], got3, g[4], got5, far_k, far_v)
        ready = (to_x,)
        keys_p = values_p = [g[0], got1, swap(to_x, "ctx", 2), swap(to_y, "ctx", 4)]
        keys_c = values_c = [g_halo[0], halo_near, halo_two]
    else:
        both = jnp.stack([g[s] for s in range(ctx_size)])
        while both.shape[0] > 1:
            size = both.shape[0] // 2
            both = add_low(both[:size], swap(both[size:], "ctx", size))
        keys_p = values_p = [both[0]]
        keys_c = values_c = [g_halo[0]] + [shift(g_halo[d], -d) for d in range(1, n_halo)]

    d_q, q_part, q_heads = q_back(dq_a, dq_b, dq_c, q_lin, after(gain_q, dq_c, *ready), cos, sin, w_q)
    d_kv, into_c, k_heads_c = kv_back(
        1, keys_c, values_c, k_lin_c, after(gain_k, q_part), cos, sin, w_kv, to_slots, q_part
    )
    into_got_c = swap(into_c, "tensor", 1)
    q_high, q_low = weight_halves(normed, after(d_q, into_c))
    d_kv, into_p, k_heads_p = kv_back(
        0, keys_p, values_p, k_lin_p, after(gain_k, q_low), cos, sin, w_kv, to_slots, q_part, d_kv
    )
    into_got_p = swap(into_p, "tensor", 1)
    q_grad = scatter_first(q_low, q_high, into_p)
    kv_high, kv_low = weight_halves(normed, after(d_kv, q_grad[0]))
    q_grad = scatter_more(q_grad, kv_low)
    heads = jnp.concatenate([q_heads, k_heads_c + k_heads_p], axis=1)
    heads_got = swap(heads, "tensor", 1)
    grad_tokens, d_one_c = tokens_back(1, into_c, into_got_c, tokens, after(gain_one, kv_low, q_grad[0]), d_resid_c)
    out_share, gate_share, up_share, down_share = unpack(chunk, after(ffn_share, d_one_c), out_grad)
    q_grad = scatter_sum(q_grad, gate_share)
    kv_grad = scatter_first(kv_low, kv_high, gate_share)
    layer_out = add_layer(0, after(resid_p, kv_grad[0], q_grad[0]), out_p, out_got_p)
    kv_grad = scatter_more(kv_grad, layer_out)
    layer_out = add_layer(1, after(resid_c, kv_grad[0]), out_c, out_got_c, layer_out)
    q_share = add_low(q_grad[0][:wide], after(q_grad[1], layer_out)).astype(F32)
    kv_grad = scatter_sum(kv_grad, layer_out)
    grad_tokens, d_one_p = tokens_back(
        0, into_p, into_got_p, tokens, after(gain_one, kv_grad[0], q_share), d_resid_p, grad_tokens
    )
    heads = heads + after(heads_got, d_one_p)
    late = jnp.concatenate([d_one_c + d_one_p, heads, d_two_c + d_two_p], axis=1)
    kv_share = add_low(kv_grad[0][:wide], after(kv_grad[1], d_one_p)).astype(F32)
    late = butterfly(late, ("ctx", "shard"), (d_one_p, kv_share))

    def own_gain(value, size):
        return lax.dynamic_index_in_dim(value.reshape(parts, size), part, 0, keepdims=False)

    return (
        layer_out,
        grad_tokens,
        own_gain(late[:, :model], wide),
        own_gain(late[:, model + 2 * HEAD_SIZE :], wide),
        own_gain(late[:, model : model + HEAD_SIZE], narrow),
        own_gain(late[:, model + HEAD_SIZE : model + 2 * HEAD_SIZE], narrow),
        q_share,
        kv_share[:, :k_cols],
        kv_share[:, k_cols:],
        out_share.T,
        gate_share,
        up_share,
        down_share.T,
    )


def solution(mesh):
    split = ("shard", "ctx")
    rows, gain = P(split, None), P(split)
    into, out_of = P(split, "tensor"), P("tensor", split)
    in_specs = (rows, P("shard", None)) + (gain,) * 4 + (into,) * 3 + (out_of,)
    in_specs += (into, into, out_of, rows)
    out_specs = (rows, rows) + (gain,) * 4 + (into,) * 3 + (out_of, into, into, out_of)
    return jax.shard_map(body, mesh=mesh, in_specs=in_specs, out_specs=out_specs, check_vma=False)
```

```python
import functools
import math

import jax
import jax.numpy as jnp
from jax import lax
from jax.experimental import pallas as pl
from jax.experimental.pallas import tpu as pltpu
from jax.sharding import PartitionSpec as P

HEAD_SIZE = 128
PROMPT = 4096
CONT_TOK = 4096
LONGEST = 1024

EPSILON = 1e-06
ROPE_BASE = 1000000.0
MASKED = -1e30
LOG2E = math.log2(math.e)
LN2 = math.log(2.0)
SCALE = 1.0 / math.sqrt(HEAD_SIZE)

BF = jnp.bfloat16
F32 = jnp.float32
NN = (((1,), (0,)), ((), ()))
NT = (((1,), (1,)), ((), ()))
TN = (((0,), (0,)), ((), ()))
MIB = 2**20
STATED = 3e9


def mm(left, right, dims=NN):
    return lax.dot_general(left, right, dims, preferred_element_type=F32)


def shaped(dims, kind):
    return jax.ShapeDtypeStruct(dims, kind)


def call(kernel, name, grid, ins, outs, scratch=(), vmem=56, scalars=None, keep=None, us=0):
    in_specs, arrays = [], []
    for array, block, index in ins:
        arrays.append(array)
        in_specs.append(pl.BlockSpec(memory_space=pl.ANY) if block is None else pl.BlockSpec(block, index))
    lead = 0 if scalars is None else 1
    return pl.pallas_call(
        kernel,
        grid_spec=pltpu.PrefetchScalarGridSpec(
            num_scalar_prefetch=lead,
            grid=grid,
            in_specs=in_specs,
            out_specs=[pl.BlockSpec(block, index) for _, block, index in outs],
            scratch_shapes=list(scratch),
        ),
        out_shape=[shape for shape, _, _ in outs],
        input_output_aliases={a + lead: b for a, b in (keep or {}).items()},
        compiler_params=pltpu.CompilerParams(vmem_limit_bytes=vmem * MIB),
        cost_estimate=pl.CostEstimate(flops=int(us * STATED), bytes_accessed=0, transcendentals=0),
        name=name,
    )(*([] if scalars is None else [scalars]), *arrays)


def rms(values):
    return lax.rsqrt(jnp.mean(values * values, axis=-1, keepdims=True) + EPSILON)


def turn(values, cos, sin):
    return values * cos + pltpu.roll(values, HEAD_SIZE // 2, 1) * sin


def turn_back(values, cos, sin):
    return values * cos - pltpu.roll(values, HEAD_SIZE // 2, 1) * sin


def put_together(pieces, whole_ref):
    rows = whole_ref.shape[0] // len(pieces)
    for at, piece in enumerate(pieces):
        whole_ref[at * rows : (at + 1) * rows, :] = piece[...]


def kv_kernel(heads, n_pieces, x_ref, gain_ref, hgain_ref, cos_ref, sin_ref, *refs):
    pieces, refs = refs[:n_pieces], refs[n_pieces:]
    if n_pieces == 1:
        w_ref, (normed_ref, kv_ref, lin_ref) = pieces[0], refs[-3:]
    else:
        normed_ref, kv_ref, lin_ref, w_ref = refs[-4:]
        put_together(pieces, w_ref)
    x = x_ref[...].astype(F32)
    normed_ref[...] = (x * rms(x) * gain_ref[...]).astype(BF)
    both = mm(normed_ref[...], w_ref[...])
    width = heads * HEAD_SIZE
    kv_ref[1] = both[:, width:].astype(BF)
    for h in range(heads):
        cols = slice(h * HEAD_SIZE, (h + 1) * HEAD_SIZE)
        lin = both[:, cols]
        lin_ref[:, cols] = lin
        kv_ref[0, :, cols] = turn(lin * rms(lin) * hgain_ref[...], cos_ref[...], sin_ref[...]).astype(BF)


def q_kernel(heads, n_pieces, normed_ref, hgain_ref, cos_ref, sin_ref, *refs):
    pieces, refs = refs[:n_pieces], refs[n_pieces:]
    if n_pieces == 1:
        w_ref, (q_ref, lin_ref) = pieces[0], refs[-2:]
    else:
        q_ref, lin_ref, w_ref = refs[-3:]
        put_together(pieces, w_ref)
    both = mm(normed_ref[...], w_ref[...])
    for h in range(heads):
        cols = slice(h * HEAD_SIZE, (h + 1) * HEAD_SIZE)
        lin = both[:, cols]
        lin_ref[:, cols] = lin
        turned = turn(lin * rms(lin) * hgain_ref[...], cos_ref[...], sin_ref[...])
        q_ref[:, cols] = (turned * (SCALE * LOG2E)).astype(BF)


def pack_kernel(chunk, key_ref, value_ref, out_ref, down_ref, gate_ref, up_ref, kv_ref, od_ref, gu_ref):
    k_cols, o_cols, units = key_ref.shape[1], out_ref.shape[1], gate_ref.shape[1]
    kv_ref[:, :k_cols] = key_ref[...]
    kv_ref[:, k_cols:] = value_ref[...]
    od_ref[:, :o_cols] = out_ref[...]
    od_ref[:, o_cols:] = down_ref[...]
    for at in range(0, units, chunk):
        gu_ref[:, 2 * at : 2 * at + chunk] = gate_ref[:, at : at + chunk]
        gu_ref[:, 2 * at + chunk : 2 * at + 2 * chunk] = up_ref[:, at : at + chunk]


def pack(chunk, *weights):
    cols = [w.shape[1] for w in weights]
    wide = weights[0].shape[0]
    whole = lambda f: (0, 0)
    ins = [(w, w.shape, whole) for w in weights]
    sums = (cols[0] + cols[1], cols[2] + cols[3], cols[4] + cols[5])
    outs = [(shaped((wide, width), BF), (wide, width), whole) for width in sums]
    return call(functools.partial(pack_kernel, chunk), "pack", (1,), ins, outs)


def by_top_bit(slots):
    groups = {}
    for at, s in enumerate(slots):
        if s:
            groups.setdefault(1 << (s.bit_length() - 1), []).append(at)
    return groups


def slot_inputs(kv, rows):
    if isinstance(kv, tuple):
        return [(part, (rows, 128), lambda h, i: (0, h)) for part in kv]
    return [(kv, (2, rows, 128), lambda h, i: (0, 0, h))]


def take_slots(refs, pairs):
    taken = []
    for pair in pairs:
        if pair:
            taken.append((refs.pop(0), refs.pop(0)))
        else:
            ref = refs.pop(0)
            taken.append((ref.at[0], ref.at[1]))
    return taken


def fwd_kernel(plan, idx_ref, lo_ref, *refs):
    halves, slots, halos = plan["halves"], plan["slots"], plan["halos"]
    refs = list(refs)
    q_refs = [refs.pop(0) for _ in halves]
    slot_refs = take_slots(refs, plan["pairs"])
    halo_refs = take_slots(refs, [False] * len(halos))
    prior = [refs.pop(0) for _ in range(2 * len(halves))] if plan["carry"] else None
    if plan["last"]:
        if plan["alias"]:
            refs.pop(0)
        out_ref, lse_ref = refs[:2]
        refs = refs[2:]
    else:
        results, refs = refs[: 2 * len(halves)], refs[2 * len(halves) :]
    me, lo_first = idx_ref[0], idx_ref[1]
    rows = q_refs[0].shape[0]
    row = lax.broadcasted_iota(jnp.int32, (2 * rows, 1), 0)
    row = jnp.where(row >= rows, row - rows, row)
    col = lax.broadcasted_iota(jnp.int32, (1, rows), 1)
    for n, half in enumerate(halves):
        qs, acc, tot = refs[3 * n : 3 * n + 3]
        for g in range(2):
            cols, at = slice(g * HEAD_SIZE, (g + 1) * HEAD_SIZE), slice(g * rows, (g + 1) * rows)
            qs[at, :] = q_refs[n][:, cols]
            if prior is not None:
                acc[at, :] = prior[2 * n][:, cols]
                tot[at, :] = prior[2 * n + 1][:, cols]
        empty = [prior is None]

        def add(kv_ref, mask=None):
            scores = mm(qs[...], kv_ref[0][...], NT)
            if mask is not None:
                scores = jnp.where(mask, scores, MASKED)
            weights = jnp.exp2(scores)
            total = weights[:, :128]
            for at in range(128, weights.shape[1], 128):
                total = total + weights[:, at : at + 128]
            part = mm(weights.astype(BF), kv_ref[1][...])
            if empty[0]:
                acc[...] = part
                tot[...] = total
            else:
                acc[...] += part
                tot[...] += total
            empty[0] = False

        if half == 1:
            for kv_ref in slot_refs:
                add(kv_ref)
            low = jnp.concatenate([lo_ref[:, :1], lo_ref[:, :1]])
            for d, kv_ref in zip(halos, halo_refs):
                if d == 0:
                    add(kv_ref, (col <= row) & (col >= low))
                else:

                    @pl.when(lo_first < -(d - 1) * rows)
                    def _(d=d, kv_ref=kv_ref):
                        add(kv_ref, col - d * rows >= low)

        else:
            if 0 in slots:
                add(slot_refs[slots.index(0)], col <= row)
            for bit, group in by_top_bit(slots).items():

                @pl.when(jnp.bitwise_and(me, bit) != 0)
                def _(group=group):
                    for at in group:
                        add(slot_refs[at])

        if not plan["last"]:
            for g in range(2):
                cols, at = slice(g * HEAD_SIZE, (g + 1) * HEAD_SIZE), slice(g * rows, (g + 1) * rows)
                results[2 * n][:, cols] = acc[at, :]
                results[2 * n + 1][:, cols] = tot[at, :]
    if plan["last"]:
        qs, acc, tot = refs
        for g in range(2):
            cols, at = slice(g * HEAD_SIZE, (g + 1) * HEAD_SIZE), slice(g * rows, (g + 1) * rows)
            total = jnp.sum(tot[at, :], axis=1, keepdims=True)
            out_ref[:, cols] = (acc[at, :] / total).astype(BF)
            lse_ref[0, g : g + 1, :] = jnp.log2(jnp.sum(tot[at, :].T, axis=0, keepdims=True))


def attention_forward(halves, scalars, q, low, slots, halos, carry=None, last=None):
    rows, heads = q[0].shape[0], q[0].shape[1] // 256
    plan = dict(halves=halves, slots=list(slots), pairs=[isinstance(kv, tuple) for kv in slots.values()], halos=list(halos), carry=carry is not None,
                last=last is not None, alias=last is not None and last[0] is not None)
    part = lambda h, i: (0, h)
    ins = [(low, (rows, 128), lambda h, i: (0, 0))]
    ins += [(of_half, (rows, 256), part) for of_half in q]
    for kv in list(slots.values()) + list(halos.values()):
        ins += slot_inputs(kv, rows)
    if carry is not None:
        ins += [(c, (rows, 256), part) for c in carry]
    scratch, keep = [], {}
    for _ in halves:
        scratch += [pltpu.VMEM((2 * rows, 128), BF)] + [pltpu.VMEM((2 * rows, 128), F32)] * 2
    state = shaped((rows, heads * 256), F32)
    if last is None:
        outs = [(state, (rows, 256), part)] * (2 * len(halves))
    else:
        other = last[0]
        if other is not None:
            keep = {len(ins): 0}
            ins.append((other, None, None))
        half = halves[0]
        outs = [
            (shaped((2 * rows, heads * 256), BF), (rows, 256), lambda h, i: (half, h)),
            (shaped((heads, 8, rows), F32), (1, 8, rows), lambda h, i: (h, 0, 0)),
        ]
    return call(functools.partial(fwd_kernel, plan), "attend", (heads,), ins, outs, scratch,
                scalars=scalars, keep=keep)


def out_kernel(att_ref, w_ref, part_ref):
    part_ref[...] = mm(att_ref[...], w_ref[...], NT).astype(BF)


def out_projection(half, attended, w_rest):
    rows, cols = attended.shape[0] // 2, attended.shape[1]
    model = w_rest.shape[0]
    ins = [(attended, (rows, cols), lambda j: (half, 0)), (w_rest, (model // 2, cols), lambda j: (j, 0))]
    outs = [(shaped((rows, model), BF), (rows, model // 2), lambda j: (0, j))]
    return call(out_kernel, "out_projection", (2,), ins, outs)[0]


def bwd_kernel(plan, idx_ref, q_ref, do_ref, lse_ref, delta_ref, lo_ref, *refs):
    half, slots, halos = plan["half"], plan["slots"], plan["halos"]
    refs = list(refs)
    slot_refs = take_slots(refs, plan["pairs"])
    halo_refs = take_slots(refs, [False] * len(halos))
    prior_dq = refs.pop(0) if plan["carry"] else None
    prior = [refs.pop(0) for _ in slots] if plan["sum"] else None
    if plan["alias"]:
        refs.pop(0)
    dq_ref = refs.pop(0)
    slot_outs = [refs.pop(0) for _ in slots]
    halo_outs = [refs.pop(0) for _ in halos]
    qs, dos, lses, deltas, dq = refs
    me, lo_first = idx_ref[0], idx_ref[1]
    rows = q_ref.shape[0]
    for g in range(2):
        cols, at = slice(g * HEAD_SIZE, (g + 1) * HEAD_SIZE), slice(g * rows, (g + 1) * rows)
        qs[at, :] = q_ref[:, cols]
        dos[at, :] = do_ref[:, cols]
        lses[:, at] = lse_ref[0, g : g + 1, :]
        deltas[:, at] = delta_ref[0, g : g + 1, :]
    dq[...] = jnp.zeros_like(dq) if prior_dq is None else prior_dq[...]

    def block(kv_ref, out_ref, mask=None, before=None):
        keys = kv_ref[0][...]
        scores = mm(keys, qs[...], NT)
        dp = mm(kv_ref[1][...], dos[...], NT)
        scores = scores - lses[...]
        if mask is not None:
            scores = jnp.where(mask, scores, MASKED)
        probs = jnp.exp2(scores)
        ds = (probs * (dp - deltas[...])).astype(BF)
        dq[...] += mm(keys.T, ds)
        dk, dv = mm(ds, qs[...]) * LN2, mm(probs.astype(BF), dos[...])
        if before is not None:
            dk, dv = dk + before[0].astype(F32), dv + before[1].astype(F32)
        out_ref[0] = dk.astype(BF)
        out_ref[1] = dv.astype(BF)

    lane = lax.broadcasted_iota(jnp.int32, (1, 2 * rows), 1)
    lane = jnp.where(lane >= rows, lane - rows, lane)
    key = lax.broadcasted_iota(jnp.int32, (rows, 1), 0)

    def when(needed, kv_ref, out_ref, mask=None):
        @pl.when(needed)
        def _():
            block(kv_ref, out_ref, mask)

        @pl.when(jnp.logical_not(needed))
        def _():
            out_ref[...] = jnp.zeros_like(out_ref)

    low = lo_ref[:1, :]
    for d, kv_ref, out_ref in zip(halos, halo_refs, halo_outs):
        if d == 0:
            block(kv_ref, out_ref, (key <= lane) & (key >= low))
        else:
            when(lo_first < -(d - 1) * rows, kv_ref, out_ref, key - d * rows >= low)
    if half == 1:
        for at in range(len(slots)):
            block(slot_refs[at], slot_outs[at], None, prior[at] if prior else None)
    else:
        if 0 in slots:
            at = slots.index(0)
            block(slot_refs[at], slot_outs[at], key <= lane)
        for bit, group in by_top_bit(slots).items():

            @pl.when(jnp.bitwise_and(me, bit) != 0)
            def _(group=group):
                for at in group:
                    block(slot_refs[at], slot_outs[at])

            @pl.when(jnp.bitwise_and(me, bit) == 0)
            def _(group=group):
                for at in group:
                    slot_outs[at][...] = jnp.zeros_like(slot_outs[at])

    if plan["last"]:
        for g in range(2):
            cols = slice(g * HEAD_SIZE, (g + 1) * HEAD_SIZE)
            dq_ref[:, cols] = dq[:, g * rows : (g + 1) * rows].T * SCALE
    else:
        dq_ref[...] = dq[...]


def attention_backward(half, scalars, q, do, lse, delta, low, slots, halos, carry=None, prior=None, last=True, whole=None):
    rows, heads = q.shape[0], q.shape[1] // 256
    plan = dict(half=half, slots=list(slots), pairs=[isinstance(kv, tuple) for kv in slots.values()], halos=list(halos), carry=carry is not None,
                sum=prior is not None, last=last, alias=whole is not None)
    part = lambda h, i: (0, h)
    stat = lambda h, i: (h, 0, 0)
    kv_map = lambda h, i: (0, 0, h)
    ins = [
        (q, (rows, 256), part),
        (do, (rows, 256), part),
        (lse, (1, 8, rows), stat),
        (delta, (1, 8, rows), stat),
        (low, (8, 2 * rows), lambda h, i: (0, 0)),
    ]
    pieces = list(slots.values()) + list(halos.values())
    for kv in pieces:
        ins += slot_inputs(kv, rows)
    if carry is not None:
        ins.append((carry, (128, 2 * rows), lambda h, i: (h, 0)))
    if prior is not None:
        ins += [(prior[s], (2, rows, 128), kv_map) for s in slots]
    keep = {}
    if whole is not None:
        keep = {len(ins): 0}
        ins.append((whole, None, None))
    if last:
        outs = [(shaped((2 * rows, heads * 256), F32), (rows, 256), lambda h, i: (half, h))]
    else:
        outs = [(shaped((heads * 128, 2 * rows), F32), (128, 2 * rows), lambda h, i: (h, 0))]
    outs += [(shaped((2, rows, heads * 128), BF), (2, rows, 128), kv_map) for _ in pieces]
    scratch = [
        pltpu.VMEM((2 * rows, 128), BF),
        pltpu.VMEM((2 * rows, 128), BF),
        pltpu.VMEM((1, 2 * rows), F32),
        pltpu.VMEM((1, 2 * rows), F32),
        pltpu.VMEM((128, 2 * rows), F32),
    ]
    us = 4 + 6 * (len(slots) + len(halos)) if carry is not None or halos else 0.1
    results = call(functools.partial(bwd_kernel, plan), "attend_back", (heads,), ins, outs, scratch,
                   scalars=scalars, us=us, keep=keep)
    n = len(slots)
    return results[0], dict(zip(slots, results[1 : 1 + n])), dict(zip(halos, results[1 + n :]))


def ffn_kernel(x_ref, own_ref, got_ref, gain_ref, dy_ref, gu_ref, down_ref, *refs):
    resid_ref, normed_ref, hidden_ref, dgu_ref, out_ref, back_ref, normed, out_acc, back_acc = refs[-9:]
    step, steps = pl.program_id(0), pl.num_programs(0)

    @pl.when(step == 0)
    def _():
        resid = x_ref[...].astype(F32) + (own_ref[...].astype(F32) + got_ref[...].astype(F32))
        resid_ref[...] = resid
        normed[...] = (resid * rms(resid) * gain_ref[...]).astype(BF)
        normed_ref[...] = normed[...]
        out_acc[...] = jnp.zeros_like(out_acc)
        back_acc[...] = jnp.zeros_like(back_acc)

    wide = down_ref.shape[1]
    both = mm(normed[...], gu_ref[...])
    d_hidden = mm(dy_ref[...], down_ref[...])
    gate, up = both[:, :wide], both[:, wide:]
    sig = 1.0 / (1.0 + jnp.exp(-gate))
    silu = gate * sig
    hidden = (silu * up).astype(BF)
    hidden_ref[...] = hidden
    d_up = (d_hidden * silu).astype(BF)
    d_gate = (d_hidden * up * (sig + silu * (1.0 - sig))).astype(BF)
    dgu_ref[:, :wide] = d_gate
    dgu_ref[:, wide:] = d_up
    out_acc[...] += mm(hidden, down_ref[...], NT)
    back_acc[...] += mm(dgu_ref[...], gu_ref[...], NT)

    @pl.when(step == steps - 1)
    def _():
        out_ref[...] = out_acc[...].astype(BF)
        back_ref[...] = back_acc[...].astype(BF)


def feed_forward(half, x, own, got, gain, dy, w_od, w_gu, chunk, whole=None):
    rows, model = own.shape
    units = w_gu.shape[1] // 2
    steps = units // chunk
    mine, once = lambda f: (half, 0), lambda f: (0, 0)
    at_down = (w_od.shape[1] - units) // chunk
    block = (rows, model)
    ins = [
        (x, block, mine), (own, block, once), (got, block, once), (gain, (1, model), once), (dy, block, mine),
        (w_gu, (model, 2 * chunk), lambda f: (0, f)),
        (w_od, (model, chunk), lambda f: (0, at_down + f)),
    ]
    keep = {}
    if whole is not None:
        keep = {len(ins) + i: 1 + i for i in range(3)}
        ins += [(array, None, None) for array in whole]
    outs = [
        (shaped((rows, model), F32), block, once),
        (shaped((2 * rows, model), BF), block, mine),
        (shaped((2 * rows, units), BF), (rows, chunk), lambda f: (half, f)),
        (shaped((2 * rows, 2 * units), BF), (rows, 2 * chunk), lambda f: (half, f)),
        (shaped((rows, model), BF), block, once),
        (shaped((rows, model), BF), block, once),
    ]
    scratch = [pltpu.VMEM(block, BF), pltpu.VMEM(block, F32), pltpu.VMEM(block, F32)]
    return call(ffn_kernel, "feed_forward", (steps,), ins, outs, scratch, keep=keep)


def norm_back(grad, values, gain):
    scale = rms(values)
    unit = values * scale
    inner = grad * gain
    return scale * (inner - unit * jnp.mean(inner * unit, axis=-1, keepdims=True)), grad * unit


def lane_mean(values):
    width = values.shape[-1]
    ones = jnp.ones((width, width), BF)
    high = values.astype(BF)
    low = (values - high.astype(F32)).astype(BF)
    return (mm(high, ones) + mm(low, ones)) * (1.0 / width)


def head_norm_back(grad, values, gain):
    scale = lax.rsqrt(lane_mean(values * values) + EPSILON)
    unit = values * scale
    inner = grad * gain
    return scale * (inner - unit * lane_mean(inner * unit)), grad * unit


def row_blocks(rows):
    size = rows // 2 if rows % 512 == 0 else rows
    return size, rows // size


def add_up(ref, value):
    total = jnp.sum(value, axis=0, keepdims=True)

    @pl.when(pl.program_id(0) == 0)
    def _():
        ref[...] = total

    @pl.when(pl.program_id(0) > 0)
    def _():
        ref[...] += total


def mixed_kernel(heads, own_ref, got_ref, resid_ref, gain_ref, dy_ref, w_ref, att_ref, *refs):
    d_resid_ref, mixed_ref, datt_ref, delta_ref, dgain_ref = refs[-5:]
    grad = own_ref[...].astype(F32) + got_ref[...].astype(F32)
    d_norm, summand = norm_back(grad, resid_ref[...], gain_ref[...])
    add_up(dgain_ref, summand)
    d_resid = dy_ref[...].astype(F32) + d_norm
    d_resid_ref[...] = d_resid
    mixed_ref[...] = d_resid.astype(BF)
    datt_ref[...] = mm(mixed_ref[...], w_ref[...]).astype(BF)
    for h in range(heads):
        cols = slice(h * HEAD_SIZE, (h + 1) * HEAD_SIZE)
        product = datt_ref[:, cols].astype(F32) * att_ref[:, cols].astype(F32)
        delta_ref[h // 2, h % 2 : h % 2 + 1, :] = jnp.sum(product.T, axis=0, keepdims=True)


def mixed_back(half, own, got, resid, gain, dy, w_rest, o_cols, attended, whole=None):
    rows, model = own.shape
    heads = o_cols // HEAD_SIZE
    size, steps = row_blocks(rows)
    mine, here, once = lambda f: (half * steps + f, 0), lambda f: (f, 0), lambda f: (0, 0)
    block = (size, model)
    ins = [
        (own, block, here), (got, block, here), (resid, block, here), (gain, (1, model), once),
        (dy, block, mine), (w_rest, (model, o_cols), once), (attended, (size, o_cols), mine),
    ]
    keep = {}
    if whole is not None:
        keep = {len(ins): 1}
        ins.append((whole, None, None))
    outs = [
        (shaped((rows, model), F32), block, here),
        (shaped((2 * rows, model), BF), block, mine),
        (shaped((rows, o_cols), BF), (size, o_cols), here),
        (shaped((heads // 2, 8, rows), F32), (heads // 2, 8, size), lambda f: (0, 0, f)),
        (shaped((1, model), F32), (1, model), once),
    ]
    return call(functools.partial(mixed_kernel, heads), "mixed_back", (steps,), ins, outs, keep=keep)


def merge_kernel(two, got3, four, got5, far_k, far_v, to_x, to_y):
    for which in range(2):
        by_x = two[which].astype(F32) + got3[which].astype(F32)
        by_y = four[which].astype(F32) + got5[which].astype(F32)
        to_x[which] = (by_x + far_v[...].astype(F32) if which else by_x).astype(BF)
        to_y[which] = (by_y if which else by_y + far_k[...].astype(F32)).astype(BF)


def merge(*pieces):
    rows, cols = pieces[-1].shape
    size, steps = row_blocks(rows)
    ins = []
    for piece in pieces:
        if piece.ndim == 3:
            ins.append((piece, (2, size, cols), lambda f: (0, f, 0)))
        else:
            ins.append((piece, (size, cols), lambda f: (f, 0)))
    outs = [(shaped((2, rows, cols), BF), (2, size, cols), lambda f: (0, f, 0))] * 2
    return call(merge_kernel, "merge", (steps,), ins, outs)


def weight_kernel(left_ref, right_ref, *refs):
    refs[-1][...] = mm(left_ref[...], right_ref[...], TN).astype(BF)


def weight_grad(left, right, at, width, cols, whole=None):
    tokens, model = left.shape
    n = right.shape[1]
    ins = [(left, (tokens, model), lambda j: (0, 0)), (right, (tokens, cols), lambda j: (0, j))]
    keep = {}
    if whole is not None:
        keep = {len(ins): 0}
        ins.append((whole, None, None))
    outs = [(shaped((model, width), BF), (model, cols), lambda j: (0, at // cols + j))]
    return call(weight_kernel, "weight_grad", (n // cols,), ins, outs, keep=keep)[0]


def slot_weight_kernel(order, part_ref, left_ref, right_ref, low_ref, high_ref, total):
    total[...] = mm(left_ref[...], right_ref[...], TN)
    wide = total.shape[0] // len(order)
    for at, slot in enumerate(order):
        block = jnp.bitwise_xor(part_ref[0], slot)
        piece = total[pl.ds(pl.multiple_of(block * wide, wide), wide), :].astype(BF)
        out_ref, row = (low_ref, at) if at < len(order) // 2 else (high_ref, at - len(order) // 2)
        out_ref[row * wide : (row + 1) * wide, :] = piece


def slot_weight_grad(order, part, left, right):
    tokens, model = left.shape
    cols = right.shape[1]
    once = lambda j, i: (0, 0)
    ins = [(left, (tokens, model), once), (right, (tokens, cols), once)]
    half = shaped((model // 2, cols), BF)
    return call(functools.partial(slot_weight_kernel, order), "slot_weight_grad", (1,), ins,
                [(half, half.shape, once)] * 2, [pltpu.VMEM((model, cols), F32)], scalars=part[None])


def weight_halves_kernel(left_ref, right_ref, high_ref, low_ref):
    for half, out_ref in enumerate((high_ref, low_ref)):

        @pl.when(pl.program_id(0) == half)
        def _(out_ref=out_ref):
            out_ref[...] = mm(left_ref[...], right_ref[...], TN).astype(BF)


def weight_halves(left, right):
    tokens, model = left.shape
    cols = right.shape[1]
    once = lambda i: (0, 0)
    ins = [(left, (tokens, model // 2), lambda i: (0, 1 - i)), (right, (tokens, cols), once)]
    half = shaped((model // 2, cols), BF)
    return call(weight_halves_kernel, "weight_halves", (2,), ins, [(half, half.shape, once)] * 2)


def q_back_kernel(heads, dq_ref, lin_ref, gain_ref, cos_ref, sin_ref, w_ref, *refs):
    d_ref, part_ref, gains_ref = refs[-3:]
    cos, sin = cos_ref[...], sin_ref[...]
    total = jnp.zeros(cos.shape, F32)
    for h in range(heads):
        cols = slice(h * HEAD_SIZE, (h + 1) * HEAD_SIZE)
        grad, summand = head_norm_back(turn_back(dq_ref[:, cols], cos, sin), lin_ref[:, cols], gain_ref[...])
        d_ref[:, cols] = grad.astype(BF)
        total = total + summand
    part_ref[...] = mm(d_ref[...], w_ref[...], NT)
    add_up(gains_ref, total)


def q_back(dq, lin, gain, cos, sin, w):
    rows, cols = dq.shape
    model = w.shape[0]
    size, steps = row_blocks(rows)
    here, once = lambda f: (f, 0), lambda f: (0, 0)
    ins = [
        (dq, (size, cols), here), (lin, (size, cols), here), (gain, (1, HEAD_SIZE), once),
        (cos, (size, HEAD_SIZE), here), (sin, (size, HEAD_SIZE), here), (w, (model, cols), once),
    ]
    outs = [
        (shaped((rows, cols), BF), (size, cols), here),
        (shaped((rows, model), F32), (size, model), here),
        (shaped((1, HEAD_SIZE), F32), (1, HEAD_SIZE), once),
    ]
    kernel = functools.partial(q_back_kernel, cols // HEAD_SIZE)
    return call(kernel, "q_back", (steps,), ins, outs)


def kv_back_kernel(heads, n_keys, n_values, lin_ref, gain_ref, cos_ref, sin_ref, w_ref, slots_ref, q_part_ref, *refs):
    key_refs, value_refs = refs[:n_keys], refs[n_keys : n_keys + n_values]
    d_ref, part_ref, gains_ref = refs[-3:]
    cos, sin = cos_ref[...], sin_ref[...]
    width = heads * HEAD_SIZE

    def total(sources, which, cols):
        value = None
        for ref in sources:
            piece = ref[which, :, cols] if len(ref.shape) == 3 else ref[:, cols]
            value = piece.astype(F32) if value is None else value + piece.astype(F32)
        return value

    gains = jnp.zeros(cos.shape, F32)
    for h in range(heads):
        cols = slice(h * HEAD_SIZE, (h + 1) * HEAD_SIZE)
        grad, summand = head_norm_back(
            turn_back(total(key_refs, 0, cols), cos, sin), lin_ref[:, cols], gain_ref[...]
        )
        d_ref[:, cols] = grad.astype(BF)
        gains = gains + summand
    d_ref[:, width:] = total(value_refs, 1, slice(None)).astype(BF)
    part = (q_part_ref[...] + mm(d_ref[...], w_ref[...], NT)).astype(BF)
    part_ref[...] = mm(part, slots_ref[...], NT).astype(BF)
    add_up(gains_ref, gains)


def kv_back(half, keys, values, lin, gain, cos, sin, w, to_slots, q_part, whole=None):
    rows, cols = lin.shape
    model = w.shape[0]
    size, steps = row_blocks(rows)
    mine, here, once = lambda f: (half * steps + f, 0), lambda f: (f, 0), lambda f: (0, 0)
    ins = [
        (lin, (size, cols), here), (gain, (1, HEAD_SIZE), once), (cos, (size, HEAD_SIZE), mine),
        (sin, (size, HEAD_SIZE), mine), (w, (model, 2 * cols), once),
        (to_slots, (model, model), once), (q_part, (size, model), mine),
    ]
    for piece in list(keys) + list(values):
        if piece.ndim == 3:
            ins.append((piece, (2, size, cols), lambda f: (0, f, 0)))
        else:
            ins.append((piece, (size, cols), here))
    keep = {}
    if whole is not None:
        keep = {len(ins): 0}
        ins.append((whole, None, None))
    outs = [
        (shaped((2 * rows, 2 * cols), BF), (size, 2 * cols), mine),
        (shaped((rows, model), BF), (size, model), here),
        (shaped((1, HEAD_SIZE), F32), (1, HEAD_SIZE), once),
    ]
    kernel = functools.partial(kv_back_kernel, cols // HEAD_SIZE, len(keys), len(values))
    return call(kernel, "kv_back", (steps,), ins, outs, keep=keep, us=3 * (1 - half))


def tokens_kernel(own_ref, got_ref, x_ref, gain_ref, d_resid_ref, *refs):
    out_ref, dgain_ref = refs[-2:]
    grad = own_ref[...].astype(F32) + got_ref[...].astype(F32)
    d_norm, summand = norm_back(grad, x_ref[...].astype(F32), gain_ref[...])
    add_up(dgain_ref, summand)
    out_ref[...] = (d_resid_ref[...] + d_norm).astype(BF)


def tokens_back(half, own, got, x, gain, d_resid, whole=None):
    rows, model = own.shape
    size, steps = row_blocks(rows)
    mine, here, once = lambda f: (half * steps + f, 0), lambda f: (f, 0), lambda f: (0, 0)
    block = (size, model)
    ins = [(own, block, here), (got, block, here), (x, block, mine), (gain, (1, model), once), (d_resid, block, here)]
    keep = {}
    if whole is not None:
        keep = {len(ins): 0}
        ins.append((whole, None, None))
    outs = [(shaped((2 * rows, model), BF), block, mine), (shaped((1, model), F32), (1, model), once)]
    return call(tokens_kernel, "tokens_back", (steps,), ins, outs, keep=keep, us=20)


def share_kernel(chunk, ffn_ref, own_ref, got_ref, out_ref, gate_ref, up_ref, down_ref):
    units = gate_ref.shape[1]
    out_ref[...] = own_ref[...].astype(F32) + got_ref[...].astype(F32)
    for at in range(0, units, chunk):
        gate_ref[:, at : at + chunk] = ffn_ref[:, 2 * at : 2 * at + chunk].astype(F32)
        up_ref[:, at : at + chunk] = ffn_ref[:, 2 * at + chunk : 2 * at + 2 * chunk].astype(F32)
    down_ref[...] = ffn_ref[:, 2 * units :].astype(F32)


def unpack(chunk, ffn_share, out_grad):
    wide, units = ffn_share.shape[0], ffn_share.shape[1] // 3
    o_cols = out_grad[0].shape[1]
    whole = lambda f: (0, 0)
    ins = [(ffn_share, ffn_share.shape, whole)] + [(grad, (wide, o_cols), whole) for grad in out_grad]
    outs = [(shaped((wide, cols), F32), (wide, cols), whole) for cols in (o_cols, units, units, units)]
    return call(functools.partial(share_kernel, chunk), "unpack", (1,), ins, outs)


def layer_kernel(resid_ref, own_ref, got_ref, *refs):
    refs[-1][...] = (resid_ref[...] + (own_ref[...].astype(F32) + got_ref[...].astype(F32))).astype(BF)


def add_layer(half, resid, own, got, whole=None):
    rows, model = resid.shape
    size, steps = row_blocks(rows)
    here, mine = lambda f: (f, 0), lambda f: (half * steps + f, 0)
    ins = [(array, (size, model), here) for array in (resid, own, got)]
    keep = {}
    if whole is not None:
        keep = {len(ins): 0}
        ins.append((whole, None, None))
    outs = [(shaped((2 * rows, model), BF), (size, model), mine)]
    return call(layer_kernel, "add_layer", (steps,), ins, outs, keep=keep)[0]


def swap(value, axis, bit):
    size = lax.axis_size(axis)
    return lax.ppermute(value, axis, [(i, i ^ bit) for i in range(size)])


def shift(value, by):
    size = lax.axis_size("ctx")
    return lax.ppermute(value, "ctx", [(i, i + by) for i in range(size) if 0 <= i + by < size])


def add_low(left, right):
    return (left.astype(F32) + right.astype(F32)).astype(BF)


def butterfly(value, axes, gates=()):
    gates = list(gates)
    for axis in axes:
        bit = 1
        while bit < lax.axis_size(axis):
            got = swap(value, axis, bit)
            value = value + (after(got, gates.pop(0)) if gates else got)
            bit *= 2
    return value


def after(value, *others):
    return lax.optimization_barrier((value, *others))[0]


def rotary_tables(position):
    half_dim = HEAD_SIZE // 2
    inverse_freq = jnp.exp(jnp.arange(half_dim, dtype=F32) * (-math.log(ROPE_BASE) / half_dim))
    angles = position.astype(F32)[:, None] * inverse_freq[None, :]
    cosine, sine = jnp.cos(angles), jnp.sin(angles)
    return jnp.concatenate([cosine, cosine], axis=-1), jnp.concatenate([-sine, sine], axis=-1)


def body(
    tokens,
    cont_lengths,
    attn_gain,
    ffn_gain,
    query_gain,
    key_gain,
    w_query,
    key_weight,
    value_weight,
    w_out,
    w_gate,
    w_up,
    w_down,
    cotangent,
):
    ctx_size = lax.axis_size("ctx")
    weight_axes = ("shard", "ctx")
    parts = lax.axis_size("shard") * ctx_size
    me = lax.axis_index("ctx")
    part = lax.axis_index("shard") * ctx_size + me
    rows, model = tokens.shape[0] // 2, tokens.shape[1]
    n_halo = 1 + -(-(LONGEST - 1) // rows)
    lengths = cont_lengths[0]

    bits = [("shard", 1)] + [("ctx", 1 << i) for i in range(1, ctx_size.bit_length() - 1)] + [("ctx", 1)]
    order = [0]
    for axis, bit in bits:
        order += [j ^ (bit * ctx_size if axis == "shard" else bit) for j in order]
    wide, narrow = attn_gain.shape[0], query_gain.shape[0]
    q_cols, k_cols = w_query.shape[1], key_weight.shape[1]
    o_cols, units = w_out.shape[0], w_gate.shape[1]
    heads, kv_heads = q_cols // HEAD_SIZE, k_cols // HEAD_SIZE
    chunk = math.gcd(units, 512)

    def gather_first(piece, *gate):
        return jnp.concatenate([piece, after(swap(piece, "shard", 1), *gate)]) if ctx_size == 8 else piece

    def gather_near(one, *gate):
        if ctx_size != 8:
            for axis, bit in bits:
                one = jnp.concatenate([one, swap(one, axis, bit)])
            return [one]
        return [one] + [after(swap(one, "ctx", bit), *gate) for bit in (2, 4, 6)]

    def gather_far(near, *gate):
        if ctx_size != 8:
            return near
        return near + [after(swap(piece, "ctx", 1), *gate) for piece in near]

    def scatter_rows(low, high, late):
        total = add_low(low, after(swap(high, "ctx", 1), late))
        if ctx_size != 8:
            for axis, bit in bits[-2:0:-1]:
                size = total.shape[0] // 2
                total = add_low(total[:size], swap(total[size:], axis, bit))
            return (total,)
        size, cut = total.shape[0] // 4, total.shape[1] // 2
        own, by_x, by_y, far = (total[i * size : (i + 1) * size] for i in range(4))
        left, right = swap(far[:, :cut], "ctx", 2), swap(far[:, cut:], "ctx", 4)
        return own, by_x, by_y, left, right

    def scatter_more(stage, late):
        if ctx_size != 8:
            return stage
        own, by_x, by_y, left, right = stage
        left, right = after(left, late), after(right, late)
        cut = left.shape[1]
        by_x = jnp.concatenate([by_x[:, :cut], add_low(by_x[:, cut:], right)], axis=1)
        by_y = jnp.concatenate([add_low(by_y[:, :cut], left), by_y[:, cut:]], axis=1)
        return lax.optimization_barrier((own, by_x, by_y))[0], swap(by_x, "ctx", 2), swap(by_y, "ctx", 4)

    def scatter_sum(stage, late):
        total = stage[0].astype(F32)
        for piece in stage[1:]:
            total = total + after(piece, late).astype(F32)
        total, size = total.astype(BF), total.shape[0] // 2
        return total, swap(total[size:], "shard", 1)

    kv_piece, od_piece, gu_piece = pack(
        chunk, key_weight, value_weight, w_out.T, w_down.T, w_gate, w_up
    )
    kv_one = gather_first(kv_piece)
    kv_near = gather_near(kv_one)
    kv_pieces = gather_far(kv_near)
    q_one = gather_first(after(w_query, kv_one), kv_near[-1])
    w_od = lax.all_gather(od_piece, weight_axes, axis=0, tiled=True)
    gains = jnp.concatenate([attn_gain, ffn_gain, query_gain, key_gain])[None]
    gains = jnp.where(jnp.arange(parts)[:, None] == part, gains, jnp.zeros((), BF))
    gains = gains + after(swap(gains, "ctx", 1), kv_piece)
    for at, (axis, bit) in enumerate(bits[:-1]):
        gains = gains + after(swap(gains, axis, bit), (kv_one, kv_near[-1], kv_near[-1])[min(at, 2)])
    gains = gains.astype(F32)
    gain_one = gains[:, :wide].reshape(1, -1)
    gain_two = gains[:, wide : 2 * wide].reshape(1, -1)
    gain_q = gains[:, 2 * wide : 2 * wide + narrow].reshape(1, -1)
    gain_k = gains[:, 2 * wide + narrow :].reshape(1, -1)
    source = jnp.bitwise_xor(part, jnp.array(order, jnp.int32))[:, None] * wide + jnp.arange(wide, dtype=jnp.int32)
    to_slots = (jnp.arange(model, dtype=jnp.int32)[:, None] == source.reshape(1, -1)).astype(BF)
    tokens_s = mm(after(tokens, q_one), to_slots).astype(BF)
    gain_one_s = mm(gain_one.astype(BF), to_slots)

    cont_at = me * rows + jnp.arange(rows, dtype=jnp.int32)
    cont_ends = jnp.cumsum(lengths)
    starts = cont_ends - lengths
    seg = jnp.sum((cont_ends[None, :] <= cont_at[:, None]).astype(jnp.int32), axis=1)
    numbers = jnp.arange(lengths.shape[0], dtype=jnp.int32)
    first = jnp.sum(jnp.where(numbers[None, :] == seg[:, None], starts[None, :], 0), axis=1)
    position = jnp.concatenate([me * rows + jnp.arange(rows, dtype=jnp.int32), PROMPT + cont_at - first])
    low = first - me * rows
    low_col = jnp.broadcast_to(low[:, None], (rows, 128))
    low_row = jnp.broadcast_to(jnp.concatenate([low, low])[None, :], (8, 2 * rows))
    scalars = jnp.stack([me, low[0]])
    cos, sin = rotary_tables(position)

    once = lambda f: (0, 0)

    def weight_inputs(pieces):
        return [(piece, piece.shape, once) for piece in pieces]

    def keys_values(half, gain, pieces, whole=None):
        mine = lambda f: (half, 0)
        ins = [
            (tokens_s, (rows, model), mine), (gain, (1, model), once), (gain_k, (1, HEAD_SIZE), once),
            (cos, (rows, HEAD_SIZE), mine), (sin, (rows, HEAD_SIZE), mine), *weight_inputs(pieces),
        ]
        keep = {}
        if whole is not None:
            keep = {len(ins): 0}
            ins.append((whole, None, None))
        outs = [
            (shaped((2 * rows, model), BF), (rows, model), mine),
            (shaped((2, rows, k_cols), BF), (2, rows, k_cols), lambda f: (0, 0, 0)),
            (shaped((rows, k_cols), F32), (rows, k_cols), once),
        ]
        if len(pieces) > 1:
            outs.append((shaped((model, 2 * k_cols), BF), (model, 2 * k_cols), once))
        return call(functools.partial(kv_kernel, kv_heads, len(pieces)), "keys_values", (1,), ins, outs, keep=keep)

    q_near = gather_near(q_one, kv_pieces[-1])
    normed, kv_p, k_lin_p, *w_kv = keys_values(0, after(gain_one_s, *q_near[1:]), kv_pieces)
    (w_kv,) = w_kv or kv_pieces
    normed, kv_c, k_lin_c = keys_values(1, after(gain_one_s, kv_p), [w_kv], normed)
    q_pieces = gather_far(q_near, kv_c)

    def queries(half, gain, pieces, whole=None):
        mine = lambda f: (half, 0)
        ins = [
            (normed, (rows, model), mine), (gain, (1, HEAD_SIZE), once),
            (cos, (rows, HEAD_SIZE), mine), (sin, (rows, HEAD_SIZE), mine), *weight_inputs(pieces),
        ]
        keep = {}
        if whole is not None:
            keep = {len(ins): 1}
            ins.append((whole, None, None))
        outs = [
            (shaped((rows, q_cols), BF), (rows, q_cols), once),
            (shaped((2 * rows, q_cols), F32), (rows, q_cols), mine),
        ]
        if len(pieces) > 1:
            outs.append((shaped((model, q_cols), BF), (model, q_cols), once))
        return call(functools.partial(q_kernel, heads, len(pieces)), "queries", (1,), ins, outs, keep=keep)

    q_c, q_lin, *w_q = queries(1, gain_q, q_pieces)
    (w_q,) = w_q or q_pieces
    q_p, q_lin = queries(0, after(gain_q, q_c), [w_q], q_lin)

    def pick(source, wanted):
        return {s: source[s] for s in source if s in wanted}

    near, middle, far = (0, 1), (2, 3, 4, 5), tuple(range(6, ctx_size))
    slots, halos = {0: kv_p}, {0: kv_c}
    odd = (me % 2) == 1
    if ctx_size == 8:
        slots[1], slots[2], slots[4] = (swap(kv_p, "ctx", bit) for bit in (1, 2, 4))
    else:
        both, bit = kv_p[None], 1
        while bit < ctx_size:
            both = jnp.concatenate([both, swap(both, "ctx", bit)])
            bit *= 2
        slots = {s: both[s] for s in range(ctx_size)}
        halos.update({d: shift(kv_c, d) for d in range(1, n_halo)})
    ready = ()
    if ctx_size == 8:
        slots[2], slots[4] = after(slots[2], q_p), after(slots[4], q_p)
        far_k, far_v = swap(slots[4][0], "ctx", 2), swap(slots[2][1], "ctx", 4)
        slots[3], slots[5] = swap(slots[2], "ctx", 1), swap(slots[4], "ctx", 1)
        halos[2] = shift(after(kv_c, slots[2]), 2)
        gu_piece = after(gu_piece, slots[2], slots[4])
        ready = (slots[2], slots[4])
    w_gu = lax.all_gather(after(gu_piece, w_od), weight_axes, axis=0, tiled=True)
    c_state = attention_forward(
        (1,), after(scalars, *ready), (q_c,), low_col, pick(slots, near), pick(halos, (0,))
    )
    if ctx_size == 8:
        slots[6] = after(far_k, c_state[0]), after(far_v, c_state[0])
        slots[7] = tuple(swap(part, "ctx", 1) for part in slots[6])
    attended, lse_p = attention_forward(
        (0,), after(scalars, c_state[0]), (q_p,), low_col, slots, {}, None, (None,)
    )
    part_p = out_projection(0, attended, w_od)
    got_p = swap(part_p, "tensor", 1)
    if ctx_size == 8:
        halos[1] = swap(jnp.where(odd, after(halos[2], part_p), kv_c), "ctx", 1)
    attended, lse_c = attention_forward(
        (1,), after(scalars, part_p), (q_c,), low_col, pick(slots, middle + far), pick(halos, range(1, n_halo)),
        c_state, (attended,),
    )
    part_c = out_projection(1, attended, w_od)
    got_c = swap(part_c, "tensor", 1)

    resid_p, *whole, out_p, back_p = feed_forward(
        0, tokens, part_p, got_p, after(gain_two, part_c), cotangent, w_od, w_gu, chunk
    )
    back_got_p = swap(back_p, "tensor", 1)
    resid_c, *whole, out_c, back_c = feed_forward(
        1, tokens, part_c, got_c, after(gain_two, back_p), cotangent, w_od, w_gu, chunk, whole
    )
    back_got_c = swap(back_c, "tensor", 1)
    normed_ffn, hidden, d_gu = whole
    ffn_grads = weight_grad(normed_ffn, d_gu, 0, 3 * units, 2 * chunk)
    ffn_grads = weight_grad(cotangent, hidden, 2 * units, 3 * units, chunk, ffn_grads)
    ffn_share = lax.psum_scatter(ffn_grads, weight_axes, scatter_dimension=0, tiled=True)
    d_resid_p, d_mixed, d_att_p, delta_p, d_two_p = mixed_back(
        0, back_p, back_got_p, resid_p, after(gain_two, ffn_grads), cotangent, w_od, o_cols, attended
    )

    of_rows = [(d_att_p, lse_p, delta_p)]

    def back_rows(half, deps, slots, halos, carry, prior=None, whole=None, last=False):
        do, lse, delta = of_rows[half]
        return attention_backward(
            half, after(scalars, *deps), (q_p, q_c)[half], do, lse, delta, low_row, slots, halos, carry, prior, last, whole
        )

    dq_p, prior, _ = back_rows(0, (d_att_p,), pick(slots, far), {}, None)
    d_resid_c, d_mixed, d_att_c, delta_c, d_two_c = mixed_back(
        1, back_c, back_got_c, resid_c, after(gain_two, dq_p), cotangent, w_od, o_cols, attended, d_mixed
    )
    of_rows.append((d_att_c, lse_c, delta_c))
    out_low, out_high = slot_weight_grad(order, part, d_mixed, attended)
    out_p, out_c = after(out_p, out_low), after(out_c, out_low)
    out_got_p, out_got_c = swap(out_p, "tensor", 1), swap(out_c, "tensor", 1)
    dq_c, g, g_halo = back_rows(1, (out_low,), pick(slots, far), halos, None, prior)
    out_grad = scatter_rows(out_low, out_high, dq_c)
    zero = jnp.zeros((), BF)
    ready = ()
    if ctx_size == 8:
        near_one, got7 = swap(g_halo[1], "ctx", 1), swap(g[7], "ctx", 1)
    dq, prior, _ = back_rows(0, (dq_c, out_got_p, out_grad[0]), pick(slots, near + middle), {}, dq_p, None, None, True)
    out_grad = scatter_more(out_grad, dq)
    if ctx_size == 8:
        g6 = add_low(g[6], after(got7, dq))
        far_k, far_v = swap(g6[0], "ctx", 2), swap(g6[1], "ctx", 4)
        near_one = after(near_one, dq)
        two_back = add_low(g_halo[2], jnp.where(odd, near_one, zero))
        halo_two = shift(two_back, -2)
        halo_near = jnp.where(odd, zero, near_one)
        ready = (g6, two_back, halo_near)
    dq_c, more, _ = back_rows(1, (dq, out_got_p, out_got_c, *ready), pick(slots, middle), {}, dq_c, prior)
    g.update(more)
    out_grad = scatter_sum(out_grad, dq_c)
    ready = (out_grad[0],)
    if ctx_size == 8:
        got3, got5 = swap(g[3], "ctx", 1), swap(g[5], "ctx", 1)
        ready = (out_grad[0], halo_two)
    dq, more, _ = back_rows(1, (dq_c, *ready), pick(slots, near), {}, dq_c, prior, dq, True)
    g.update(more)
    if ctx_size == 8:
        got1 = swap(g[1], "ctx", 1)
        far_k, far_v, got3, got5 = (after(v, dq, out_grad[1], ffn_share) for v in (far_k, far_v, got3, got5))
        to_x, to_y = merge(g[2], got3, g[4], got5, far_k, far_v)
        ready = (to_x,)
        keys_p = values_p = [g[0], got1, swap(to_x, "ctx", 2), swap(to_y, "ctx", 4)]
        keys_c = values_c = [g_halo[0], halo_near, halo_two]
    else:
        both = jnp.stack([g[s] for s in range(ctx_size)])
        while both.shape[0] > 1:
            size = both.shape[0] // 2
            both = add_low(both[:size], swap(both[size:], "ctx", size))
        keys_p = values_p = [both[0]]
        keys_c = values_c = [g_halo[0]] + [shift(g_halo[d], -d) for d in range(1, n_halo)]

    d_q, q_part, q_heads = q_back(dq, q_lin, after(gain_q, dq, *ready), cos, sin, w_q)
    d_kv, into_c, k_heads_c = kv_back(
        1, keys_c, values_c, k_lin_c, after(gain_k, q_part), cos, sin, w_kv, to_slots, q_part
    )
    into_got_c = swap(into_c, "tensor", 1)
    q_high, q_low = weight_halves(normed, after(d_q, into_c))
    d_kv, into_p, k_heads_p = kv_back(
        0, keys_p, values_p, k_lin_p, after(gain_k, q_low), cos, sin, w_kv, to_slots, q_part, d_kv
    )
    into_got_p = swap(into_p, "tensor", 1)
    q_grad = scatter_rows(q_low, q_high, into_p)
    kv_high, kv_low = weight_halves(normed, after(d_kv, q_grad[0]))
    q_grad = scatter_more(q_grad, kv_low)
    heads = jnp.concatenate([q_heads, k_heads_c + k_heads_p], axis=1)
    heads_got = swap(heads, "tensor", 1)
    grad_tokens, d_one_c = tokens_back(1, into_c, into_got_c, tokens, after(gain_one, kv_low, q_grad[0]), d_resid_c)
    out_share, gate_share, up_share, down_share = unpack(chunk, after(ffn_share, d_one_c), out_grad)
    q_grad = scatter_sum(q_grad, gate_share)
    kv_grad = scatter_rows(kv_low, kv_high, gate_share)
    layer_out = add_layer(0, after(resid_p, kv_grad[0], q_grad[0]), out_p, out_got_p)
    kv_grad = scatter_more(kv_grad, layer_out)
    layer_out = add_layer(1, after(resid_c, kv_grad[0]), out_c, out_got_c, layer_out)
    q_share = add_low(q_grad[0][:wide], after(q_grad[1], layer_out)).astype(F32)
    kv_grad = scatter_sum(kv_grad, layer_out)
    grad_tokens, d_one_p = tokens_back(
        0, into_p, into_got_p, tokens, after(gain_one, kv_grad[0], q_share), d_resid_p, grad_tokens
    )
    heads = heads + after(heads_got, d_one_p)
    late = jnp.concatenate([d_one_c + d_one_p, heads, d_two_c + d_two_p], axis=1)
    kv_share = add_low(kv_grad[0][:wide], after(kv_grad[1], d_one_p)).astype(F32)
    late = butterfly(late, ("ctx", "shard"), (d_one_p, kv_share))

    def own_gain(value, size):
        return lax.dynamic_index_in_dim(value.reshape(parts, size), part, 0, keepdims=False)

    return (
        layer_out,
        grad_tokens,
        own_gain(late[:, :model], wide),
        own_gain(late[:, model + 2 * HEAD_SIZE :], wide),
        own_gain(late[:, model : model + HEAD_SIZE], narrow),
        own_gain(late[:, model + HEAD_SIZE : model + 2 * HEAD_SIZE], narrow),
        q_share,
        kv_share[:, :k_cols],
        kv_share[:, k_cols:],
        out_share.T,
        gate_share,
        up_share,
        down_share.T,
    )


def solution(mesh):
    split = ("shard", "ctx")
    rows, gain = P(split, None), P(split)
    into, out_of = P(split, "tensor"), P("tensor", split)
    in_specs = (rows, P("shard", None)) + (gain,) * 4 + (into,) * 3 + (out_of,)
    in_specs += (into, into, out_of, rows)
    out_specs = (rows, rows) + (gain,) * 4 + (into,) * 3 + (out_of, into, into, out_of)
    return jax.shard_map(body, mesh=mesh, in_specs=in_specs, out_specs=out_specs, check_vma=False)
```

```python
import functools
import math

import jax
import jax.numpy as jnp
from jax import lax
from jax.experimental import pallas as pl
from jax.experimental.pallas import tpu as pltpu
from jax.sharding import PartitionSpec as P

HEAD_SIZE = 128
PROMPT = 4096
CONT_TOK = 4096
LONGEST = 1024

EPSILON = 1e-06
ROPE_BASE = 1000000.0
MASKED = -1e30
LOG2E = math.log2(math.e)
LN2 = math.log(2.0)
SCALE = 1.0 / math.sqrt(HEAD_SIZE)

BF = jnp.bfloat16
F32 = jnp.float32
NN = (((1,), (0,)), ((), ()))
NT = (((1,), (1,)), ((), ()))
TN = (((0,), (0,)), ((), ()))
MIB = 2**20
STATED = 3e9


def mm(left, right, dims=NN):
    return lax.dot_general(left, right, dims, preferred_element_type=F32)


def shaped(dims, kind):
    return jax.ShapeDtypeStruct(dims, kind)


def call(kernel, name, grid, ins, outs, scratch=(), vmem=56, scalars=None, keep=None, us=0):
    in_specs, arrays = [], []
    for array, block, index in ins:
        arrays.append(array)
        in_specs.append(pl.BlockSpec(memory_space=pl.ANY) if block is None else pl.BlockSpec(block, index))
    lead = 0 if scalars is None else 1
    return pl.pallas_call(
        kernel,
        grid_spec=pltpu.PrefetchScalarGridSpec(
            num_scalar_prefetch=lead,
            grid=grid,
            in_specs=in_specs,
            out_specs=[pl.BlockSpec(block, index) for _, block, index in outs],
            scratch_shapes=list(scratch),
        ),
        out_shape=[shape for shape, _, _ in outs],
        input_output_aliases={a + lead: b for a, b in (keep or {}).items()},
        compiler_params=pltpu.CompilerParams(vmem_limit_bytes=vmem * MIB),
        cost_estimate=pl.CostEstimate(flops=int(us * STATED), bytes_accessed=0, transcendentals=0),
        name=name,
    )(*([] if scalars is None else [scalars]), *arrays)


def rms(values):
    return lax.rsqrt(jnp.mean(values * values, axis=-1, keepdims=True) + EPSILON)


def turn(values, cos, sin):
    return values * cos + pltpu.roll(values, HEAD_SIZE // 2, 1) * sin


def turn_back(values, cos, sin):
    return values * cos - pltpu.roll(values, HEAD_SIZE // 2, 1) * sin


def put_together(pieces, whole_ref):
    rows = whole_ref.shape[0] // len(pieces)
    for at, piece in enumerate(pieces):
        whole_ref[at * rows : (at + 1) * rows, :] = piece[...]


def kv_kernel(heads, n_pieces, x_ref, gain_ref, hgain_ref, cos_ref, sin_ref, *refs):
    pieces, refs = refs[:n_pieces], refs[n_pieces:]
    if n_pieces == 1:
        w_ref, (normed_ref, kv_ref, lin_ref) = pieces[0], refs[-3:]
    else:
        normed_ref, kv_ref, lin_ref, w_ref = refs[-4:]
        put_together(pieces, w_ref)
    x = x_ref[...].astype(F32)
    normed_ref[...] = (x * rms(x) * gain_ref[...]).astype(BF)
    both = mm(normed_ref[...], w_ref[...])
    width = heads * HEAD_SIZE
    kv_ref[1] = both[:, width:].astype(BF)
    for h in range(heads):
        cols = slice(h * HEAD_SIZE, (h + 1) * HEAD_SIZE)
        lin = both[:, cols]
        lin_ref[:, cols] = lin
        kv_ref[0, :, cols] = turn(lin * rms(lin) * hgain_ref[...], cos_ref[...], sin_ref[...]).astype(BF)


def q_kernel(heads, n_pieces, normed_ref, hgain_ref, cos_ref, sin_ref, *refs):
    pieces, refs = refs[:n_pieces], refs[n_pieces:]
    if n_pieces == 1:
        w_ref, (q_ref, lin_ref) = pieces[0], refs[-2:]
    else:
        q_ref, lin_ref, w_ref = refs[-3:]
        put_together(pieces, w_ref)
    both = mm(normed_ref[...], w_ref[...])
    for h in range(heads):
        cols = slice(h * HEAD_SIZE, (h + 1) * HEAD_SIZE)
        lin = both[:, cols]
        lin_ref[:, cols] = lin
        turned = turn(lin * rms(lin) * hgain_ref[...], cos_ref[...], sin_ref[...])
        q_ref[:, cols] = (turned * (SCALE * LOG2E)).astype(BF)


def pack_kernel(chunk, key_ref, value_ref, out_ref, down_ref, gate_ref, up_ref, kv_ref, od_ref, gu_ref):
    k_cols, o_cols, units = key_ref.shape[1], out_ref.shape[1], gate_ref.shape[1]
    kv_ref[:, :k_cols] = key_ref[...]
    kv_ref[:, k_cols:] = value_ref[...]
    od_ref[:, :o_cols] = out_ref[...]
    od_ref[:, o_cols:] = down_ref[...]
    for at in range(0, units, chunk):
        gu_ref[:, 2 * at : 2 * at + chunk] = gate_ref[:, at : at + chunk]
        gu_ref[:, 2 * at + chunk : 2 * at + 2 * chunk] = up_ref[:, at : at + chunk]


def pack(chunk, *weights):
    cols = [w.shape[1] for w in weights]
    wide = weights[0].shape[0]
    whole = lambda f: (0, 0)
    ins = [(w, w.shape, whole) for w in weights]
    sums = (cols[0] + cols[1], cols[2] + cols[3], cols[4] + cols[5])
    outs = [(shaped((wide, width), BF), (wide, width), whole) for width in sums]
    return call(functools.partial(pack_kernel, chunk), "pack", (1,), ins, outs)


def by_top_bit(slots):
    groups = {}
    for at, s in enumerate(slots):
        if s:
            groups.setdefault(1 << (s.bit_length() - 1), []).append(at)
    return groups


def slot_inputs(kv, rows):
    if isinstance(kv, tuple):
        return [(part, (rows, 128), lambda h, i: (0, h)) for part in kv]
    return [(kv, (2, rows, 128), lambda h, i: (0, 0, h))]


def take_slots(refs, pairs):
    taken = []
    for pair in pairs:
        if pair:
            taken.append((refs.pop(0), refs.pop(0)))
        else:
            ref = refs.pop(0)
            taken.append((ref.at[0], ref.at[1]))
    return taken


def fwd_kernel(plan, idx_ref, lo_ref, *refs):
    halves, slots, halos = plan["halves"], plan["slots"], plan["halos"]
    refs = list(refs)
    q_refs = [refs.pop(0) for _ in halves]
    slot_refs = take_slots(refs, plan["pairs"])
    halo_refs = take_slots(refs, [False] * len(halos))
    prior = [refs.pop(0) for _ in range(2 * len(halves))] if plan["carry"] else None
    if plan["last"]:
        if plan["alias"]:
            refs.pop(0)
        out_ref, lse_ref = refs[:2]
        refs = refs[2:]
    else:
        results, refs = refs[: 2 * len(halves)], refs[2 * len(halves) :]
    me, lo_first = idx_ref[0], idx_ref[1]
    rows = q_refs[0].shape[0]
    row = lax.broadcasted_iota(jnp.int32, (2 * rows, 1), 0)
    row = jnp.where(row >= rows, row - rows, row)
    col = lax.broadcasted_iota(jnp.int32, (1, rows), 1)
    for n, half in enumerate(halves):
        qs, acc, tot = refs[3 * n : 3 * n + 3]
        for g in range(2):
            cols, at = slice(g * HEAD_SIZE, (g + 1) * HEAD_SIZE), slice(g * rows, (g + 1) * rows)
            qs[at, :] = q_refs[n][:, cols]
            if prior is not None:
                acc[at, :] = prior[2 * n][:, cols]
                tot[at, :] = prior[2 * n + 1][:, cols]
        empty = [prior is None]

        def add(kv_ref, mask=None):
            scores = mm(qs[...], kv_ref[0][...], NT)
            if mask is not None:
                scores = jnp.where(mask, scores, MASKED)
            weights = jnp.exp2(scores)
            total = weights[:, :128]
            for at in range(128, weights.shape[1], 128):
                total = total + weights[:, at : at + 128]
            part = mm(weights.astype(BF), kv_ref[1][...])
            if empty[0]:
                acc[...] = part
                tot[...] = total
            else:
                acc[...] += part
                tot[...] += total
            empty[0] = False

        if half == 1:
            for kv_ref in slot_refs:
                add(kv_ref)
            low = jnp.concatenate([lo_ref[:, :1], lo_ref[:, :1]])
            for d, kv_ref in zip(halos, halo_refs):
                if d == 0:
                    add(kv_ref, (col <= row) & (col >= low))
                else:

                    @pl.when(lo_first < -(d - 1) * rows)
                    def _(d=d, kv_ref=kv_ref):
                        add(kv_ref, col - d * rows >= low)

        else:
            if 0 in slots:
                add(slot_refs[slots.index(0)], col <= row)
            for bit, group in by_top_bit(slots).items():

                @pl.when(jnp.bitwise_and(me, bit) != 0)
                def _(group=group):
                    for at in group:
                        add(slot_refs[at])

        if not plan["last"]:
            for g in range(2):
                cols, at = slice(g * HEAD_SIZE, (g + 1) * HEAD_SIZE), slice(g * rows, (g + 1) * rows)
                results[2 * n][:, cols] = acc[at, :]
                results[2 * n + 1][:, cols] = tot[at, :]
    if plan["last"]:
        qs, acc, tot = refs
        for g in range(2):
            cols, at = slice(g * HEAD_SIZE, (g + 1) * HEAD_SIZE), slice(g * rows, (g + 1) * rows)
            total = jnp.sum(tot[at, :], axis=1, keepdims=True)
            out_ref[:, cols] = (acc[at, :] / total).astype(BF)
            lse_ref[0, g : g + 1, :] = jnp.log2(jnp.sum(tot[at, :].T, axis=0, keepdims=True))


def attention_forward(halves, scalars, q, low, slots, halos, carry=None, last=None):
    rows, heads = q[0].shape[0], q[0].shape[1] // 256
    plan = dict(halves=halves, slots=list(slots), pairs=[isinstance(kv, tuple) for kv in slots.values()], halos=list(halos), carry=carry is not None,
                last=last is not None, alias=last is not None and last[0] is not None)
    part = lambda h, i: (0, h)
    ins = [(low, (rows, 128), lambda h, i: (0, 0))]
    ins += [(of_half, (rows, 256), part) for of_half in q]
    for kv in list(slots.values()) + list(halos.values()):
        ins += slot_inputs(kv, rows)
    if carry is not None:
        ins += [(c, (rows, 256), part) for c in carry]
    scratch, keep = [], {}
    for _ in halves:
        scratch += [pltpu.VMEM((2 * rows, 128), BF)] + [pltpu.VMEM((2 * rows, 128), F32)] * 2
    state = shaped((rows, heads * 256), F32)
    if last is None:
        outs = [(state, (rows, 256), part)] * (2 * len(halves))
    else:
        other = last[0]
        if other is not None:
            keep = {len(ins): 0}
            ins.append((other, None, None))
        half = halves[0]
        outs = [
            (shaped((2 * rows, heads * 256), BF), (rows, 256), lambda h, i: (half, h)),
            (shaped((heads, 8, rows), F32), (1, 8, rows), lambda h, i: (h, 0, 0)),
        ]
    return call(functools.partial(fwd_kernel, plan), "attend", (heads,), ins, outs, scratch,
                scalars=scalars, keep=keep)


def out_kernel(att_ref, w_ref, part_ref):
    part_ref[...] = mm(att_ref[...], w_ref[...], NT).astype(BF)


def out_projection(half, attended, w_rest):
    rows, cols = attended.shape[0] // 2, attended.shape[1]
    model = w_rest.shape[0]
    ins = [(attended, (rows, cols), lambda j: (half, 0)), (w_rest, (model // 2, cols), lambda j: (j, 0))]
    outs = [(shaped((rows, model), BF), (rows, model // 2), lambda j: (0, j))]
    return call(out_kernel, "out_projection", (2,), ins, outs)[0]


def bwd_kernel(plan, idx_ref, q_ref, do_ref, lse_ref, delta_ref, lo_ref, *refs):
    half, slots, halos = plan["half"], plan["slots"], plan["halos"]
    refs = list(refs)
    slot_refs = take_slots(refs, plan["pairs"])
    halo_refs = take_slots(refs, [False] * len(halos))
    prior_dq = refs.pop(0) if plan["carry"] else None
    prior = [refs.pop(0) for _ in slots] if plan["sum"] else None
    if plan["alias"]:
        refs.pop(0)
    dq_ref = refs.pop(0)
    slot_outs = [refs.pop(0) for _ in slots]
    halo_outs = [refs.pop(0) for _ in halos]
    qs, dos, lses, deltas, dq = refs
    me, lo_first = idx_ref[0], idx_ref[1]
    rows = q_ref.shape[0]
    for g in range(2):
        cols, at = slice(g * HEAD_SIZE, (g + 1) * HEAD_SIZE), slice(g * rows, (g + 1) * rows)
        qs[at, :] = q_ref[:, cols]
        dos[at, :] = do_ref[:, cols]
        lses[:, at] = lse_ref[0, g : g + 1, :]
        deltas[:, at] = delta_ref[0, g : g + 1, :]
    dq[...] = jnp.zeros_like(dq) if prior_dq is None else prior_dq[...]

    def block(kv_ref, out_ref, mask=None, before=None):
        keys = kv_ref[0][...]
        scores = mm(keys, qs[...], NT)
        dp = mm(kv_ref[1][...], dos[...], NT)
        scores = scores - lses[...]
        if mask is not None:
            scores = jnp.where(mask, scores, MASKED)
        probs = jnp.exp2(scores)
        ds = (probs * (dp - deltas[...])).astype(BF)
        dq[...] += mm(keys.T, ds)
        dk, dv = mm(ds, qs[...]) * LN2, mm(probs.astype(BF), dos[...])
        if before is not None:
            dk, dv = dk + before[0].astype(F32), dv + before[1].astype(F32)
        out_ref[0] = dk.astype(BF)
        out_ref[1] = dv.astype(BF)

    lane = lax.broadcasted_iota(jnp.int32, (1, 2 * rows), 1)
    lane = jnp.where(lane >= rows, lane - rows, lane)
    key = lax.broadcasted_iota(jnp.int32, (rows, 1), 0)

    def when(needed, kv_ref, out_ref, mask=None):
        @pl.when(needed)
        def _():
            block(kv_ref, out_ref, mask)

        @pl.when(jnp.logical_not(needed))
        def _():
            out_ref[...] = jnp.zeros_like(out_ref)

    low = lo_ref[:1, :]
    for d, kv_ref, out_ref in zip(halos, halo_refs, halo_outs):
        if d == 0:
            block(kv_ref, out_ref, (key <= lane) & (key >= low))
        else:
            when(lo_first < -(d - 1) * rows, kv_ref, out_ref, key - d * rows >= low)
    if half == 1:
        for at in range(len(slots)):
            block(slot_refs[at], slot_outs[at], None, prior[at] if prior else None)
    else:
        if 0 in slots:
            at = slots.index(0)
            block(slot_refs[at], slot_outs[at], key <= lane)
        for bit, group in by_top_bit(slots).items():

            @pl.when(jnp.bitwise_and(me, bit) != 0)
            def _(group=group):
                for at in group:
                    block(slot_refs[at], slot_outs[at])

            @pl.when(jnp.bitwise_and(me, bit) == 0)
            def _(group=group):
                for at in group:
                    slot_outs[at][...] = jnp.zeros_like(slot_outs[at])

    if plan["last"]:
        for g in range(2):
            cols = slice(g * HEAD_SIZE, (g + 1) * HEAD_SIZE)
            dq_ref[:, cols] = dq[:, g * rows : (g + 1) * rows].T * SCALE
    else:
        dq_ref[...] = dq[...]


def attention_backward(half, scalars, q, do, lse, delta, low, slots, halos, carry=None, prior=None, last=True, whole=None):
    rows, heads = q.shape[0], q.shape[1] // 256
    plan = dict(half=half, slots=list(slots), pairs=[isinstance(kv, tuple) for kv in slots.values()], halos=list(halos), carry=carry is not None,
                sum=prior is not None, last=last, alias=whole is not None)
    part = lambda h, i: (0, h)
    stat = lambda h, i: (h, 0, 0)
    kv_map = lambda h, i: (0, 0, h)
    ins = [
        (q, (rows, 256), part),
        (do, (rows, 256), part),
        (lse, (1, 8, rows), stat),
        (delta, (1, 8, rows), stat),
        (low, (8, 2 * rows), lambda h, i: (0, 0)),
    ]
    pieces = list(slots.values()) + list(halos.values())
    for kv in pieces:
        ins += slot_inputs(kv, rows)
    if carry is not None:
        ins.append((carry, (128, 2 * rows), lambda h, i: (h, 0)))
    if prior is not None:
        ins += [(prior[s], (2, rows, 128), kv_map) for s in slots]
    keep = {}
    if whole is not None:
        keep = {len(ins): 0}
        ins.append((whole, None, None))
    if last:
        outs = [(shaped((rows, heads * 256), F32), (rows, 256), part)]
    else:
        outs = [(shaped((heads * 128, 2 * rows), F32), (128, 2 * rows), lambda h, i: (h, 0))]
    outs += [(shaped((2, rows, heads * 128), BF), (2, rows, 128), kv_map) for _ in pieces]
    scratch = [
        pltpu.VMEM((2 * rows, 128), BF),
        pltpu.VMEM((2 * rows, 128), BF),
        pltpu.VMEM((1, 2 * rows), F32),
        pltpu.VMEM((1, 2 * rows), F32),
        pltpu.VMEM((128, 2 * rows), F32),
    ]
    us = 4 + 6 * (len(slots) + len(halos)) if carry is not None or halos else 0.1
    results = call(functools.partial(bwd_kernel, plan), "attend_back", (heads,), ins, outs, scratch,
                   scalars=scalars, us=us, keep=keep)
    n = len(slots)
    return results[0], dict(zip(slots, results[1 : 1 + n])), dict(zip(halos, results[1 + n :]))


def prompt_back_kernel(plan, idx_ref, qa_ref, qb_ref, doa_ref, dob_ref, lse_ref, lse_b_ref, delta_ref, delta_b_ref, *refs):
    slots, last = plan["slots"], plan["ctx"] - 1
    refs = list(refs)
    slot_refs = take_slots(refs, plan["pairs"])
    prior = {s: refs.pop(0) for s in plan["prior"]}
    dqa_ref, dqb_ref = refs.pop(0), refs.pop(0)
    outs = [refs.pop(0) for _ in slots]
    qs, dos, lses, deltas, dq = refs
    me = idx_ref[0]
    half = qa_ref.shape[0]
    rows = 2 * half
    for part, (q_ref, do_ref) in enumerate(((qa_ref, doa_ref), (qb_ref, dob_ref))):
        for g in range(2):
            cols = slice(g * HEAD_SIZE, (g + 1) * HEAD_SIZE)
            at = slice(part * rows + g * half, part * rows + (g + 1) * half)
            qs[at, :] = q_ref[:, cols]
            dos[at, :] = do_ref[:, cols]
            for total, own, got in ((lses, lse_ref, lse_b_ref), (deltas, delta_ref, delta_b_ref)):
                total[:, at] = (got if part else own)[0, g : g + 1, :half]
    dq[...] = jnp.zeros_like(dq)
    lane = lax.broadcasted_iota(jnp.int32, (1, rows), 1)
    lane = jnp.where(lane >= half, lane - half, lane)
    key = lax.broadcasted_iota(jnp.int32, (rows, 1), 0)

    def block(s, part, mask=None):
        kv_ref, out_ref = slot_refs[slots.index(s)], outs[slots.index(s)]
        at = slice(part * rows, (part + 1) * rows)
        keys = kv_ref[0][...]
        scores = mm(keys, qs[at, :], NT)
        dp = mm(kv_ref[1][...], dos[at, :], NT)
        scores = scores - lses[:, at]
        if mask is not None:
            scores = jnp.where(mask, scores, MASKED)
        probs = jnp.exp2(scores)
        ds = (probs * (dp - deltas[:, at])).astype(BF)
        dq[:, at] += mm(keys.T, ds)
        before = out_ref if part else prior.get(s)
        for which, value in enumerate((mm(ds, qs[at, :]) * LN2, mm(probs.astype(BF), dos[at, :]))):
            if before is not None:
                value = value + before[which].astype(F32)
            out_ref[which] = value.astype(BF)

    block(0, 0, key <= lane)
    for bit, group in by_top_bit(slots).items():
        group = [slots[at] for at in group]

        @pl.when(jnp.bitwise_and(me, bit) != 0)
        def _(group=group):
            for s in group:
                block(s, 0)

        @pl.when(jnp.bitwise_and(me, bit) == 0)
        def _(group=group):
            for s in group:
                out_ref = outs[slots.index(s)]
                out_ref[...] = prior[s][...] if s in prior else jnp.zeros_like(out_ref)

    block(last, 1, key <= lane + half)
    for bit, group in by_top_bit(slots).items():

        @pl.when(jnp.bitwise_and(me, bit) == 0)
        def _(group=[slots[at] ^ last for at in group]):
            for s in group:
                block(s, 1)

    for part, out_ref in enumerate((dqa_ref, dqb_ref)):
        for g in range(2):
            at = slice(part * rows + g * half, part * rows + (g + 1) * half)
            cols = slice(g * HEAD_SIZE, (g + 1) * HEAD_SIZE)
            out_ref[:, cols] = (dq[:, at].T * SCALE).astype(out_ref.dtype)


def prompt_backward(scalars, ctx, own, got, slots, prior):
    rows, heads = own[0].shape[0], own[0].shape[1] // 256
    half = rows // 2
    plan = dict(slots=list(slots), prior=list(prior), ctx=ctx,
                pairs=[isinstance(kv, tuple) for kv in slots.values()])
    part = lambda h, i: (0, h)
    stat = lambda h, i: (h, 0, 0)
    kv_map = lambda h, i: (0, 0, h)
    ins = []
    for mine, other in zip(own[:2], got[:2]):
        ins += [(mine, (half, 256), part), (other, (half, 256), part)]
    for mine, other in zip(own[2:], got[2:]):
        ins += [(mine, (1, 8, rows), stat), (other, (1, 8, half), stat)]
    for kv in slots.values():
        ins += slot_inputs(kv, rows)
    ins += [(grad, (2, rows, 128), kv_map) for grad in prior.values()]
    outs = [(shaped((half, heads * 256), kind), (half, 256), part) for kind in (F32, BF)]
    outs += [(shaped((2, rows, heads * 128), BF), (2, rows, 128), kv_map) for _ in slots]
    scratch = [
        pltpu.VMEM((2 * rows, 128), BF),
        pltpu.VMEM((2 * rows, 128), BF),
        pltpu.VMEM((1, 2 * rows), F32),
        pltpu.VMEM((1, 2 * rows), F32),
        pltpu.VMEM((128, 2 * rows), F32),
    ]
    results = call(functools.partial(prompt_back_kernel, plan), "prompt_back", (heads,), ins, outs, scratch,
                   scalars=scalars, us=16)
    return results[0], results[1], dict(zip(slots, results[2:]))


def ffn_kernel(x_ref, own_ref, got_ref, gain_ref, dy_ref, gu_ref, down_ref, *refs):
    resid_ref, normed_ref, hidden_ref, dgu_ref, out_ref, back_ref, normed, out_acc, back_acc = refs[-9:]
    step, steps = pl.program_id(0), pl.num_programs(0)

    @pl.when(step == 0)
    def _():
        resid = x_ref[...].astype(F32) + (own_ref[...].astype(F32) + got_ref[...].astype(F32))
        resid_ref[...] = resid
        normed[...] = (resid * rms(resid) * gain_ref[...]).astype(BF)
        normed_ref[...] = normed[...]
        out_acc[...] = jnp.zeros_like(out_acc)
        back_acc[...] = jnp.zeros_like(back_acc)

    wide = down_ref.shape[1]
    both = mm(normed[...], gu_ref[...])
    d_hidden = mm(dy_ref[...], down_ref[...])
    gate, up = both[:, :wide], both[:, wide:]
    sig = 1.0 / (1.0 + jnp.exp(-gate))
    silu = gate * sig
    hidden = (silu * up).astype(BF)
    hidden_ref[...] = hidden
    d_up = (d_hidden * silu).astype(BF)
    d_gate = (d_hidden * up * (sig + silu * (1.0 - sig))).astype(BF)
    dgu_ref[:, :wide] = d_gate
    dgu_ref[:, wide:] = d_up
    out_acc[...] += mm(hidden, down_ref[...], NT)
    back_acc[...] += mm(dgu_ref[...], gu_ref[...], NT)

    @pl.when(step == steps - 1)
    def _():
        out_ref[...] = out_acc[...].astype(BF)
        back_ref[...] = back_acc[...].astype(BF)


def feed_forward(half, x, own, got, gain, dy, w_od, w_gu, chunk, whole=None):
    rows, model = own.shape
    units = w_gu.shape[1] // 2
    steps = units // chunk
    mine, once = lambda f: (half, 0), lambda f: (0, 0)
    at_down = (w_od.shape[1] - units) // chunk
    block = (rows, model)
    ins = [
        (x, block, mine), (own, block, once), (got, block, once), (gain, (1, model), once), (dy, block, mine),
        (w_gu, (model, 2 * chunk), lambda f: (0, f)),
        (w_od, (model, chunk), lambda f: (0, at_down + f)),
    ]
    keep = {}
    if whole is not None:
        keep = {len(ins) + i: 1 + i for i in range(3)}
        ins += [(array, None, None) for array in whole]
    outs = [
        (shaped((rows, model), F32), block, once),
        (shaped((2 * rows, model), BF), block, mine),
        (shaped((2 * rows, units), BF), (rows, chunk), lambda f: (half, f)),
        (shaped((2 * rows, 2 * units), BF), (rows, 2 * chunk), lambda f: (half, f)),
        (shaped((rows, model), BF), block, once),
        (shaped((rows, model), BF), block, once),
    ]
    scratch = [pltpu.VMEM(block, BF), pltpu.VMEM(block, F32), pltpu.VMEM(block, F32)]
    return call(ffn_kernel, "feed_forward", (steps,), ins, outs, scratch, keep=keep)


def norm_back(grad, values, gain):
    scale = rms(values)
    unit = values * scale
    inner = grad * gain
    return scale * (inner - unit * jnp.mean(inner * unit, axis=-1, keepdims=True)), grad * unit


def lane_mean(values):
    width = values.shape[-1]
    ones = jnp.ones((width, width), BF)
    high = values.astype(BF)
    low = (values - high.astype(F32)).astype(BF)
    return (mm(high, ones) + mm(low, ones)) * (1.0 / width)


def head_norm_back(grad, values, gain):
    scale = lax.rsqrt(lane_mean(values * values) + EPSILON)
    unit = values * scale
    inner = grad * gain
    return scale * (inner - unit * lane_mean(inner * unit)), grad * unit


def row_blocks(rows):
    size = rows // 2 if rows % 512 == 0 else rows
    return size, rows // size


def add_up(ref, value):
    total = jnp.sum(value, axis=0, keepdims=True)

    @pl.when(pl.program_id(0) == 0)
    def _():
        ref[...] = total

    @pl.when(pl.program_id(0) > 0)
    def _():
        ref[...] += total


def mixed_kernel(heads, own_ref, got_ref, resid_ref, gain_ref, dy_ref, w_ref, att_ref, *refs):
    d_resid_ref, mixed_ref, datt_ref, delta_ref, dgain_ref = refs[-5:]
    grad = own_ref[...].astype(F32) + got_ref[...].astype(F32)
    d_norm, summand = norm_back(grad, resid_ref[...], gain_ref[...])
    add_up(dgain_ref, summand)
    d_resid = dy_ref[...].astype(F32) + d_norm
    d_resid_ref[...] = d_resid
    mixed_ref[...] = d_resid.astype(BF)
    datt_ref[...] = mm(mixed_ref[...], w_ref[...]).astype(BF)
    for h in range(heads):
        cols = slice(h * HEAD_SIZE, (h + 1) * HEAD_SIZE)
        product = datt_ref[:, cols].astype(F32) * att_ref[:, cols].astype(F32)
        delta_ref[h // 2, h % 2 : h % 2 + 1, :] = jnp.sum(product.T, axis=0, keepdims=True)


def mixed_back(half, own, got, resid, gain, dy, w_rest, o_cols, attended, whole=None):
    rows, model = own.shape
    heads = o_cols // HEAD_SIZE
    size, steps = row_blocks(rows)
    mine, here, once = lambda f: (half * steps + f, 0), lambda f: (f, 0), lambda f: (0, 0)
    block = (size, model)
    ins = [
        (own, block, here), (got, block, here), (resid, block, here), (gain, (1, model), once),
        (dy, block, mine), (w_rest, (model, o_cols), once), (attended, (size, o_cols), mine),
    ]
    keep = {}
    if whole is not None:
        keep = {len(ins): 1}
        ins.append((whole, None, None))
    outs = [
        (shaped((rows, model), F32), block, here),
        (shaped((2 * rows, model), BF), block, mine),
        (shaped((rows, o_cols), BF), (size, o_cols), here),
        (shaped((heads // 2, 8, rows), F32), (heads // 2, 8, size), lambda f: (0, 0, f)),
        (shaped((1, model), F32), (1, model), once),
    ]
    return call(functools.partial(mixed_kernel, heads), "mixed_back", (steps,), ins, outs, keep=keep)


def merge_kernel(two, got3, four, got5, far_k, far_v, to_x, to_y):
    for which in range(2):
        by_x = two[which].astype(F32) + got3[which].astype(F32)
        by_y = four[which].astype(F32) + got5[which].astype(F32)
        to_x[which] = (by_x + far_v[...].astype(F32) if which else by_x).astype(BF)
        to_y[which] = (by_y if which else by_y + far_k[...].astype(F32)).astype(BF)


def merge(*pieces):
    rows, cols = pieces[-1].shape
    size, steps = row_blocks(rows)
    ins = []
    for piece in pieces:
        if piece.ndim == 3:
            ins.append((piece, (2, size, cols), lambda f: (0, f, 0)))
        else:
            ins.append((piece, (size, cols), lambda f: (f, 0)))
    outs = [(shaped((2, rows, cols), BF), (2, size, cols), lambda f: (0, f, 0))] * 2
    return call(merge_kernel, "merge", (steps,), ins, outs)


def weight_kernel(left_ref, right_ref, *refs):
    refs[-1][...] = mm(left_ref[...], right_ref[...], TN).astype(BF)


def weight_grad(left, right, at, width, cols, whole=None):
    tokens, model = left.shape
    n = right.shape[1]
    ins = [(left, (tokens, model), lambda j: (0, 0)), (right, (tokens, cols), lambda j: (0, j))]
    keep = {}
    if whole is not None:
        keep = {len(ins): 0}
        ins.append((whole, None, None))
    outs = [(shaped((model, width), BF), (model, cols), lambda j: (0, at // cols + j))]
    return call(weight_kernel, "weight_grad", (n // cols,), ins, outs, keep=keep)[0]


def slot_weight_kernel(order, part_ref, left_ref, right_ref, low_ref, high_ref, total):
    total[...] = mm(left_ref[...], right_ref[...], TN)
    wide = total.shape[0] // len(order)
    for at, slot in enumerate(order):
        block = jnp.bitwise_xor(part_ref[0], slot)
        piece = total[pl.ds(pl.multiple_of(block * wide, wide), wide), :].astype(BF)
        out_ref, row = (low_ref, at) if at < len(order) // 2 else (high_ref, at - len(order) // 2)
        out_ref[row * wide : (row + 1) * wide, :] = piece


def slot_weight_grad(order, part, left, right):
    tokens, model = left.shape
    cols = right.shape[1]
    once = lambda j, i: (0, 0)
    ins = [(left, (tokens, model), once), (right, (tokens, cols), once)]
    half = shaped((model // 2, cols), BF)
    return call(functools.partial(slot_weight_kernel, order), "slot_weight_grad", (1,), ins,
                [(half, half.shape, once)] * 2, [pltpu.VMEM((model, cols), F32)], scalars=part[None])


def weight_halves_kernel(left_ref, right_ref, high_ref, low_ref):
    for half, out_ref in enumerate((high_ref, low_ref)):

        @pl.when(pl.program_id(0) == half)
        def _(out_ref=out_ref):
            out_ref[...] = mm(left_ref[...], right_ref[...], TN).astype(BF)


def weight_halves(left, right):
    tokens, model = left.shape
    cols = right.shape[1]
    once = lambda i: (0, 0)
    ins = [(left, (tokens, model // 2), lambda i: (0, 1 - i)), (right, (tokens, cols), once)]
    half = shaped((model // 2, cols), BF)
    return call(weight_halves_kernel, "weight_halves", (2,), ins, [(half, half.shape, once)] * 2)


def q_back_kernel(heads, dqa_ref, dqb_ref, dqc_ref, lin_ref, gain_ref, cos_ref, sin_ref, w_ref, *refs):
    d_ref, part_ref, gains_ref, dq_ref = refs[-4:]
    step = pl.program_id(0)

    @pl.when(step == 0)
    def _():
        dq_ref[...] = dqa_ref[...]

    @pl.when(step == 1)
    def _():
        dq_ref[...] = dqb_ref[...].astype(F32)

    @pl.when(step > 1)
    def _():
        dq_ref[...] = dqc_ref[...]

    cos, sin = cos_ref[...], sin_ref[...]
    total = jnp.zeros(cos.shape, F32)
    for h in range(heads):
        cols = slice(h * HEAD_SIZE, (h + 1) * HEAD_SIZE)
        grad, summand = head_norm_back(turn_back(dq_ref[:, cols], cos, sin), lin_ref[:, cols], gain_ref[...])
        d_ref[:, cols] = grad.astype(BF)
        total = total + summand
    part_ref[...] = mm(d_ref[...], w_ref[...], NT)
    add_up(gains_ref, total)


def q_back(dq_a, dq_b, dq_c, lin, gain, cos, sin, w):
    rows, cols = lin.shape
    model = w.shape[0]
    size = rows // 4
    here, once = lambda f: (f, 0), lambda f: (0, 0)
    ins = [
        (dq_a, (size, cols), once), (dq_b, (size, cols), once), (dq_c, (size, cols), lambda f: (jnp.maximum(f - 2, 0), 0)),
        (lin, (size, cols), here), (gain, (1, HEAD_SIZE), once),
        (cos, (size, HEAD_SIZE), here), (sin, (size, HEAD_SIZE), here), (w, (model, cols), once),
    ]
    outs = [
        (shaped((rows, cols), BF), (size, cols), here),
        (shaped((rows, model), F32), (size, model), here),
        (shaped((1, HEAD_SIZE), F32), (1, HEAD_SIZE), once),
    ]
    kernel = functools.partial(q_back_kernel, cols // HEAD_SIZE)
    return call(kernel, "q_back", (4,), ins, outs, [pltpu.VMEM((size, cols), F32)])


def kv_back_kernel(heads, n_keys, n_values, lin_ref, gain_ref, cos_ref, sin_ref, w_ref, slots_ref, q_part_ref, *refs):
    key_refs, value_refs = refs[:n_keys], refs[n_keys : n_keys + n_values]
    d_ref, part_ref, gains_ref = refs[-3:]
    cos, sin = cos_ref[...], sin_ref[...]
    width = heads * HEAD_SIZE

    def total(sources, which, cols):
        value = None
        for ref in sources:
            piece = ref[which, :, cols] if len(ref.shape) == 3 else ref[:, cols]
            value = piece.astype(F32) if value is None else value + piece.astype(F32)
        return value

    gains = jnp.zeros(cos.shape, F32)
    for h in range(heads):
        cols = slice(h * HEAD_SIZE, (h + 1) * HEAD_SIZE)
        grad, summand = head_norm_back(
            turn_back(total(key_refs, 0, cols), cos, sin), lin_ref[:, cols], gain_ref[...]
        )
        d_ref[:, cols] = grad.astype(BF)
        gains = gains + summand
    d_ref[:, width:] = total(value_refs, 1, slice(None)).astype(BF)
    part = (q_part_ref[...] + mm(d_ref[...], w_ref[...], NT)).astype(BF)
    part_ref[...] = mm(part, slots_ref[...], NT).astype(BF)
    add_up(gains_ref, gains)


def kv_back(half, keys, values, lin, gain, cos, sin, w, to_slots, q_part, whole=None):
    rows, cols = lin.shape
    model = w.shape[0]
    size, steps = row_blocks(rows)
    mine, here, once = lambda f: (half * steps + f, 0), lambda f: (f, 0), lambda f: (0, 0)
    ins = [
        (lin, (size, cols), here), (gain, (1, HEAD_SIZE), once), (cos, (size, HEAD_SIZE), mine),
        (sin, (size, HEAD_SIZE), mine), (w, (model, 2 * cols), once),
        (to_slots, (model, model), once), (q_part, (size, model), mine),
    ]
    for piece in list(keys) + list(values):
        if piece.ndim == 3:
            ins.append((piece, (2, size, cols), lambda f: (0, f, 0)))
        else:
            ins.append((piece, (size, cols), here))
    keep = {}
    if whole is not None:
        keep = {len(ins): 0}
        ins.append((whole, None, None))
    outs = [
        (shaped((2 * rows, 2 * cols), BF), (size, 2 * cols), mine),
        (shaped((rows, model), BF), (size, model), here),
        (shaped((1, HEAD_SIZE), F32), (1, HEAD_SIZE), once),
    ]
    kernel = functools.partial(kv_back_kernel, cols // HEAD_SIZE, len(keys), len(values))
    return call(kernel, "kv_back", (steps,), ins, outs, keep=keep, us=3 * (1 - half))


def tokens_kernel(own_ref, got_ref, x_ref, gain_ref, d_resid_ref, *refs):
    out_ref, dgain_ref = refs[-2:]
    grad = own_ref[...].astype(F32) + got_ref[...].astype(F32)
    d_norm, summand = norm_back(grad, x_ref[...].astype(F32), gain_ref[...])
    add_up(dgain_ref, summand)
    out_ref[...] = (d_resid_ref[...] + d_norm).astype(BF)


def tokens_back(half, own, got, x, gain, d_resid, whole=None):
    rows, model = own.shape
    size, steps = row_blocks(rows)
    mine, here, once = lambda f: (half * steps + f, 0), lambda f: (f, 0), lambda f: (0, 0)
    block = (size, model)
    ins = [(own, block, here), (got, block, here), (x, block, mine), (gain, (1, model), once), (d_resid, block, here)]
    keep = {}
    if whole is not None:
        keep = {len(ins): 0}
        ins.append((whole, None, None))
    outs = [(shaped((2 * rows, model), BF), block, mine), (shaped((1, model), F32), (1, model), once)]
    return call(tokens_kernel, "tokens_back", (steps,), ins, outs, keep=keep, us=20)


def share_kernel(chunk, ffn_ref, own_ref, got_ref, out_ref, gate_ref, up_ref, down_ref):
    units = gate_ref.shape[1]
    out_ref[...] = own_ref[...].astype(F32) + got_ref[...].astype(F32)
    for at in range(0, units, chunk):
        gate_ref[:, at : at + chunk] = ffn_ref[:, 2 * at : 2 * at + chunk].astype(F32)
        up_ref[:, at : at + chunk] = ffn_ref[:, 2 * at + chunk : 2 * at + 2 * chunk].astype(F32)
    down_ref[...] = ffn_ref[:, 2 * units :].astype(F32)


def unpack(chunk, ffn_share, out_grad):
    wide, units = ffn_share.shape[0], ffn_share.shape[1] // 3
    o_cols = out_grad[0].shape[1]
    whole = lambda f: (0, 0)
    ins = [(ffn_share, ffn_share.shape, whole)] + [(grad, (wide, o_cols), whole) for grad in out_grad]
    outs = [(shaped((wide, cols), F32), (wide, cols), whole) for cols in (o_cols, units, units, units)]
    return call(functools.partial(share_kernel, chunk), "unpack", (1,), ins, outs)


def layer_kernel(resid_ref, own_ref, got_ref, *refs):
    refs[-1][...] = (resid_ref[...] + (own_ref[...].astype(F32) + got_ref[...].astype(F32))).astype(BF)


def add_layer(half, resid, own, got, whole=None):
    rows, model = resid.shape
    size, steps = row_blocks(rows)
    here, mine = lambda f: (f, 0), lambda f: (half * steps + f, 0)
    ins = [(array, (size, model), here) for array in (resid, own, got)]
    keep = {}
    if whole is not None:
        keep = {len(ins): 0}
        ins.append((whole, None, None))
    outs = [(shaped((2 * rows, model), BF), (size, model), mine)]
    return call(layer_kernel, "add_layer", (steps,), ins, outs, keep=keep)[0]


def swap(value, axis, bit):
    size = lax.axis_size(axis)
    return lax.ppermute(value, axis, [(i, i ^ bit) for i in range(size)])


def shift(value, by):
    size = lax.axis_size("ctx")
    return lax.ppermute(value, "ctx", [(i, i + by) for i in range(size) if 0 <= i + by < size])


def add_low(left, right):
    return (left.astype(F32) + right.astype(F32)).astype(BF)


def butterfly(value, axes, gates=()):
    gates = list(gates)
    for axis in axes:
        bit = 1
        while bit < lax.axis_size(axis):
            got = swap(value, axis, bit)
            value = value + (after(got, gates.pop(0)) if gates else got)
            bit *= 2
    return value


def after(value, *others):
    return lax.optimization_barrier((value, *others))[0]


def rotary_tables(position):
    half_dim = HEAD_SIZE // 2
    inverse_freq = jnp.exp(jnp.arange(half_dim, dtype=F32) * (-math.log(ROPE_BASE) / half_dim))
    angles = position.astype(F32)[:, None] * inverse_freq[None, :]
    cosine, sine = jnp.cos(angles), jnp.sin(angles)
    return jnp.concatenate([cosine, cosine], axis=-1), jnp.concatenate([-sine, sine], axis=-1)


def body(
    tokens,
    cont_lengths,
    attn_gain,
    ffn_gain,
    query_gain,
    key_gain,
    w_query,
    key_weight,
    value_weight,
    w_out,
    w_gate,
    w_up,
    w_down,
    cotangent,
):
    ctx_size = lax.axis_size("ctx")
    weight_axes = ("shard", "ctx")
    parts = lax.axis_size("shard") * ctx_size
    me = lax.axis_index("ctx")
    part = lax.axis_index("shard") * ctx_size + me
    rows, model = tokens.shape[0] // 2, tokens.shape[1]
    n_halo = 1 + -(-(LONGEST - 1) // rows)
    lengths = cont_lengths[0]

    bits = [("shard", 1)] + [("ctx", 1 << i) for i in range(1, ctx_size.bit_length() - 1)] + [("ctx", 1)]
    order = [0]
    for axis, bit in bits:
        order += [j ^ (bit * ctx_size if axis == "shard" else bit) for j in order]
    wide, narrow = attn_gain.shape[0], query_gain.shape[0]
    q_cols, k_cols = w_query.shape[1], key_weight.shape[1]
    o_cols, units = w_out.shape[0], w_gate.shape[1]
    heads, kv_heads = q_cols // HEAD_SIZE, k_cols // HEAD_SIZE
    chunk = math.gcd(units, 512)

    def gather_first(piece, *gate):
        return jnp.concatenate([piece, after(swap(piece, "shard", 1), *gate)]) if ctx_size == 8 else piece

    def gather_near(one, *gate):
        if ctx_size != 8:
            for axis, bit in bits:
                one = jnp.concatenate([one, swap(one, axis, bit)])
            return [one]
        return [one] + [after(swap(one, "ctx", bit), *gate) for bit in (2, 4, 6)]

    def gather_far(near, *gate):
        if ctx_size != 8:
            return near
        return near + [after(swap(piece, "ctx", 1), *gate) for piece in near]

    def scatter_rows(low, high, late):
        total = add_low(low, after(swap(high, "ctx", 1), late))
        if ctx_size != 8:
            for axis, bit in bits[-2:0:-1]:
                size = total.shape[0] // 2
                total = add_low(total[:size], swap(total[size:], axis, bit))
            return (total,)
        size = total.shape[0] // 4
        by_x, by_y, far = (total[i * size : (i + 1) * size] for i in (1, 2, 3))
        return total, swap(by_x, "ctx", 2), swap(by_y, "ctx", 4), swap(far, "ctx", 6)

    def scatter_first(low, high, late):
        if ctx_size != 8:
            return scatter_rows(low, high, late)
        total = add_low(low, after(swap(high, "ctx", 1), late))
        size, cut = total.shape[0] // 4, total.shape[1] // 2
        own, by_x, by_y, far = (total[i * size : (i + 1) * size] for i in range(4))
        left, right = swap(far[:, :cut], "ctx", 2), swap(far[:, cut:], "ctx", 4)
        return own, by_x, by_y, left, right

    def scatter_more(stage, late):
        if ctx_size != 8:
            return stage
        own, by_x, by_y, left, right = stage
        left, right = after(left, late), after(right, late)
        cut = left.shape[1]
        by_x = jnp.concatenate([by_x[:, :cut], add_low(by_x[:, cut:], right)], axis=1)
        by_y = jnp.concatenate([add_low(by_y[:, :cut], left), by_y[:, cut:]], axis=1)
        return lax.optimization_barrier((own, by_x, by_y))[0], swap(by_x, "ctx", 2), swap(by_y, "ctx", 4)

    def scatter_sum(stage, late):
        total = stage[0].astype(F32)[: stage[-1].shape[0]]
        for piece in stage[1:]:
            total = total + after(piece, late).astype(F32)
        total, size = total.astype(BF), total.shape[0] // 2
        return total, swap(total[size:], "shard", 1)

    kv_piece, od_piece, gu_piece = pack(
        chunk, key_weight, value_weight, w_out.T, w_down.T, w_gate, w_up
    )
    kv_one = gather_first(kv_piece)
    kv_near = gather_near(kv_one)
    kv_pieces = gather_far(kv_near)
    q_one = gather_first(after(w_query, kv_one), kv_near[-1])
    w_od = lax.all_gather(od_piece, weight_axes, axis=0, tiled=True)
    gains = jnp.concatenate([attn_gain, ffn_gain, query_gain, key_gain])[None]
    gains = jnp.where(jnp.arange(parts)[:, None] == part, gains, jnp.zeros((), BF))
    gains = gains + after(swap(gains, "ctx", 1), kv_piece)
    for at, (axis, bit) in enumerate(bits[:-1]):
        gains = gains + after(swap(gains, axis, bit), (kv_one, kv_near[-1], kv_near[-1])[min(at, 2)])
    gains = gains.astype(F32)
    gain_one = gains[:, :wide].reshape(1, -1)
    gain_two = gains[:, wide : 2 * wide].reshape(1, -1)
    gain_q = gains[:, 2 * wide : 2 * wide + narrow].reshape(1, -1)
    gain_k = gains[:, 2 * wide + narrow :].reshape(1, -1)
    source = jnp.bitwise_xor(part, jnp.array(order, jnp.int32))[:, None] * wide + jnp.arange(wide, dtype=jnp.int32)
    to_slots = (jnp.arange(model, dtype=jnp.int32)[:, None] == source.reshape(1, -1)).astype(BF)
    tokens_s = mm(after(tokens, q_one), to_slots).astype(BF)
    gain_one_s = mm(gain_one.astype(BF), to_slots)

    cont_at = me * rows + jnp.arange(rows, dtype=jnp.int32)
    cont_ends = jnp.cumsum(lengths)
    starts = cont_ends - lengths
    seg = jnp.sum((cont_ends[None, :] <= cont_at[:, None]).astype(jnp.int32), axis=1)
    numbers = jnp.arange(lengths.shape[0], dtype=jnp.int32)
    first = jnp.sum(jnp.where(numbers[None, :] == seg[:, None], starts[None, :], 0), axis=1)
    position = jnp.concatenate([me * rows + jnp.arange(rows, dtype=jnp.int32), PROMPT + cont_at - first])
    low = first - me * rows
    low_col = jnp.broadcast_to(low[:, None], (rows, 128))
    low_row = jnp.broadcast_to(jnp.concatenate([low, low])[None, :], (8, 2 * rows))
    scalars = jnp.stack([me, low[0]])
    cos, sin = rotary_tables(position)

    once = lambda f: (0, 0)

    def weight_inputs(pieces):
        return [(piece, piece.shape, once) for piece in pieces]

    def keys_values(half, gain, pieces, whole=None):
        mine = lambda f: (half, 0)
        ins = [
            (tokens_s, (rows, model), mine), (gain, (1, model), once), (gain_k, (1, HEAD_SIZE), once),
            (cos, (rows, HEAD_SIZE), mine), (sin, (rows, HEAD_SIZE), mine), *weight_inputs(pieces),
        ]
        keep = {}
        if whole is not None:
            keep = {len(ins): 0}
            ins.append((whole, None, None))
        outs = [
            (shaped((2 * rows, model), BF), (rows, model), mine),
            (shaped((2, rows, k_cols), BF), (2, rows, k_cols), lambda f: (0, 0, 0)),
            (shaped((rows, k_cols), F32), (rows, k_cols), once),
        ]
        if len(pieces) > 1:
            outs.append((shaped((model, 2 * k_cols), BF), (model, 2 * k_cols), once))
        return call(functools.partial(kv_kernel, kv_heads, len(pieces)), "keys_values", (1,), ins, outs, keep=keep)

    q_near = gather_near(q_one, kv_pieces[-1])
    normed, kv_p, k_lin_p, *w_kv = keys_values(0, after(gain_one_s, *q_near[1:]), kv_pieces)
    (w_kv,) = w_kv or kv_pieces
    normed, kv_c, k_lin_c = keys_values(1, after(gain_one_s, kv_p), [w_kv], normed)
    q_pieces = gather_far(q_near, kv_c)

    def queries(half, gain, pieces, whole=None):
        scratch = []
        mine = lambda f: (half, 0)
        ins = [
            (normed, (rows, model), mine), (gain, (1, HEAD_SIZE), once),
            (cos, (rows, HEAD_SIZE), mine), (sin, (rows, HEAD_SIZE), mine), *weight_inputs(pieces),
        ]
        keep = {}
        if whole is not None:
            keep = {len(ins): 1}
            ins.append((whole, None, None))
        outs = [
            (shaped((rows, q_cols), BF), (rows, q_cols), once),
            (shaped((2 * rows, q_cols), F32), (rows, q_cols), mine),
        ]
        if len(pieces) > 1 and whole is not None:
            outs.append((shaped((model, q_cols), BF), (model, q_cols), once))
        elif len(pieces) > 1:
            scratch = [pltpu.VMEM((model, q_cols), BF)]
        kernel = functools.partial(q_kernel, heads, len(pieces))
        return call(kernel, "queries", (1,), ins, outs, scratch, keep=keep)

    q_c, q_lin = queries(1, gain_q, q_pieces)
    q_p, q_lin, *w_q = queries(0, after(gain_q, q_c), q_pieces, q_lin)
    (w_q,) = w_q or q_pieces

    def pick(source, wanted):
        return {s: source[s] for s in source if s in wanted}

    near, middle, far = (0, 1), (2, 3, 4, 5), tuple(range(6, ctx_size))
    slots, halos = {0: kv_p}, {0: kv_c}
    odd = (me % 2) == 1
    if ctx_size == 8:
        slots[1], slots[2], slots[4] = (swap(kv_p, "ctx", bit) for bit in (1, 2, 4))
    else:
        both, bit = kv_p[None], 1
        while bit < ctx_size:
            both = jnp.concatenate([both, swap(both, "ctx", bit)])
            bit *= 2
        slots = {s: both[s] for s in range(ctx_size)}
        halos.update({d: shift(kv_c, d) for d in range(1, n_halo)})
    ready = ()
    if ctx_size == 8:
        slots[2], slots[4] = after(slots[2], q_p), after(slots[4], q_p)
        far_k, far_v = swap(slots[4][0], "ctx", 2), swap(slots[2][1], "ctx", 4)
        slots[3], slots[5] = swap(slots[2], "ctx", 1), swap(slots[4], "ctx", 1)
        halos[2] = shift(after(kv_c, slots[2]), 2)
        gu_piece = after(gu_piece, slots[2], slots[4])
        ready = (slots[2], slots[4])
    w_gu = lax.all_gather(after(gu_piece, w_od), weight_axes, axis=0, tiled=True)
    c_state = attention_forward(
        (1,), after(scalars, *ready), (q_c,), low_col, pick(slots, near), pick(halos, (0,))
    )
    if ctx_size == 8:
        slots[6] = after(far_k, c_state[0]), after(far_v, c_state[0])
        slots[7] = tuple(swap(part, "ctx", 1) for part in slots[6])
    attended, lse_p = attention_forward(
        (0,), after(scalars, c_state[0]), (q_p,), low_col, slots, {}, None, (None,)
    )
    part_p = out_projection(0, attended, w_od)
    got_p = swap(part_p, "tensor", 1)
    if ctx_size == 8:
        halos[1] = swap(jnp.where(odd, after(halos[2], part_p), kv_c), "ctx", 1)
    attended, lse_c = attention_forward(
        (1,), after(scalars, part_p), (q_c,), low_col, pick(slots, middle + far), pick(halos, range(1, n_halo)),
        c_state, (attended,),
    )
    part_c = out_projection(1, attended, w_od)
    got_c = swap(part_c, "tensor", 1)

    resid_p, *whole, out_p, back_p = feed_forward(
        0, tokens, part_p, got_p, after(gain_two, part_c), cotangent, w_od, w_gu, chunk
    )
    back_got_p = swap(back_p, "tensor", 1)
    resid_c, *whole, out_c, back_c = feed_forward(
        1, tokens, part_c, got_c, after(gain_two, back_p), cotangent, w_od, w_gu, chunk, whole
    )
    back_got_c = swap(back_c, "tensor", 1)
    normed_ffn, hidden, d_gu = whole
    ffn_grads = weight_grad(normed_ffn, d_gu, 0, 3 * units, 2 * chunk)
    ffn_grads = weight_grad(cotangent, hidden, 2 * units, 3 * units, chunk, ffn_grads)
    ffn_share = lax.psum_scatter(ffn_grads, weight_axes, scatter_dimension=0, tiled=True)
    def mirror(value):
        return lax.ppermute(value, "ctx", [(i, i ^ (ctx_size - 1)) for i in range(ctx_size)])

    half = rows // 2
    q_b, lse_b = mirror(after(q_p, part_c)[half:]), mirror(after(lse_p, part_c)[:, :, half:])
    d_resid_p, d_mixed, d_att_p, delta_p, d_two_p = mixed_back(
        0, back_p, back_got_p, resid_p, after(gain_two, ffn_grads, q_b, lse_b), cotangent, w_od, o_cols, attended
    )

    do_b, delta_b = mirror(d_att_p[half:]), mirror(delta_p[:, :, half:])
    d_resid_c, d_mixed, d_att_c, delta_c, d_two_c = mixed_back(
        1, back_c, back_got_c, resid_c, after(gain_two, d_att_p), cotangent, w_od, o_cols, attended, d_mixed
    )
    out_low, out_high = slot_weight_grad(order, part, d_mixed, attended)
    out_p = after(out_p, out_low)
    out_got_p = swap(out_p, "tensor", 1)

    def back_c_rows(deps, slots, halos, carry, prior=None, last=False):
        return attention_backward(
            1, after(scalars, *deps), q_c, d_att_c, lse_c, delta_c, low_row, slots, halos, carry, prior, last
        )

    dq_c, from_c, g_halo = back_c_rows((out_low,), pick(slots, far), halos, None)
    out_c = after(out_c, dq_c)
    out_got_c = swap(out_c, "tensor", 1)
    out_grad = scatter_rows(out_low, out_high, dq_c)
    if ctx_size == 8:
        near_one = swap(g_halo[1], "ctx", 1)
    dq_a, dq_b, from_p = prompt_backward(
        after(scalars, dq_c, out_got_p, out_grad[0]), ctx_size, (q_p, d_att_p, lse_p, delta_p),
        (q_b, do_b, lse_b, delta_b), slots, from_c,
    )
    g = pick(from_p, far)
    zero = jnp.zeros((), BF)
    ready = ()
    if ctx_size == 8:
        got7 = swap(g[7], "ctx", 1)
        near_one = after(near_one, dq_a)
        two_back = add_low(g_halo[2], jnp.where(odd, near_one, zero))
        halo_two = shift(two_back, -2)
        halo_near = jnp.where(odd, zero, near_one)
        ready = (two_back, halo_near)
    dq_c, more, _ = back_c_rows((dq_a, out_got_c, *ready), pick(slots, middle), {}, dq_c, from_p)
    g.update(more)
    dq_b = mirror(after(dq_b, dq_c))
    out_grad = scatter_sum(out_grad, dq_c)
    if ctx_size == 8:
        g6 = add_low(g[6], after(got7, dq_c))
        far_k, far_v = swap(g6[0], "ctx", 2), swap(g6[1], "ctx", 4)
        got3, got5 = swap(g[3], "ctx", 1), swap(g[5], "ctx", 1)
        ready = (g6, halo_two)
    dq_c, more, _ = back_c_rows(
        (dq_c, out_grad[0], *ready), pick(slots, near), {}, dq_c, from_p, True
    )
    g.update(more)
    if ctx_size == 8:
        got1 = swap(g[1], "ctx", 1)
        far_k, far_v, got3, got5 = (after(v, dq_c, dq_b, ffn_share) for v in (far_k, far_v, got3, got5))
        to_x, to_y = merge(g[2], got3, g[4], got5, far_k, far_v)
        ready = (to_x,)
        keys_p = values_p = [g[0], got1, swap(to_x, "ctx", 2), swap(to_y, "ctx", 4)]
        keys_c = values_c = [g_halo[0], halo_near, halo_two]
    else:
        both = jnp.stack([g[s] for s in range(ctx_size)])
        while both.shape[0] > 1:
            size = both.shape[0] // 2
            both = add_low(both[:size], swap(both[size:], "ctx", size))
        keys_p = values_p = [both[0]]
        keys_c = values_c = [g_halo[0]] + [shift(g_halo[d], -d) for d in range(1, n_halo)]

    d_q, q_part, q_heads = q_back(dq_a, dq_b, dq_c, q_lin, after(gain_q, dq_c, *ready), cos, sin, w_q)
    d_kv, into_c, k_heads_c = kv_back(
        1, keys_c, values_c, k_lin_c, after(gain_k, q_part), cos, sin, w_kv, to_slots, q_part
    )
    into_got_c = swap(into_c, "tensor", 1)
    q_high, q_low = weight_halves(normed, after(d_q, into_c))
    d_kv, into_p, k_heads_p = kv_back(
        0, keys_p, values_p, k_lin_p, after(gain_k, q_low), cos, sin, w_kv, to_slots, q_part, d_kv
    )
    into_got_p = swap(into_p, "tensor", 1)
    q_grad = scatter_first(q_low, q_high, into_p)
    kv_high, kv_low = weight_halves(normed, after(d_kv, q_grad[0]))
    q_grad = scatter_more(q_grad, kv_low)
    heads = jnp.concatenate([q_heads, k_heads_c + k_heads_p], axis=1)
    heads_got = swap(heads, "tensor", 1)
    grad_tokens, d_one_c = tokens_back(1, into_c, into_got_c, tokens, after(gain_one, kv_low, q_grad[0]), d_resid_c)
    out_share, gate_share, up_share, down_share = unpack(chunk, after(ffn_share, d_one_c), out_grad)
    q_grad = scatter_sum(q_grad, gate_share)
    kv_grad = scatter_first(kv_low, kv_high, gate_share)
    layer_out = add_layer(0, after(resid_p, kv_grad[0], q_grad[0]), out_p, out_got_p)
    kv_grad = scatter_more(kv_grad, layer_out)
    layer_out = add_layer(1, after(resid_c, kv_grad[0]), out_c, out_got_c, layer_out)
    q_share = add_low(q_grad[0][:wide], after(q_grad[1], layer_out)).astype(F32)
    kv_grad = scatter_sum(kv_grad, layer_out)
    grad_tokens, d_one_p = tokens_back(
        0, into_p, into_got_p, tokens, after(gain_one, kv_grad[0], q_share), d_resid_p, grad_tokens
    )
    heads = heads + after(heads_got, d_one_p)
    late = jnp.concatenate([d_one_c + d_one_p, heads, d_two_c + d_two_p], axis=1)
    kv_share = add_low(kv_grad[0][:wide], after(kv_grad[1], d_one_p)).astype(F32)
    late = butterfly(late, ("ctx", "shard"), (d_one_p, kv_share))

    def own_gain(value, size):
        return lax.dynamic_index_in_dim(value.reshape(parts, size), part, 0, keepdims=False)

    return (
        layer_out,
        grad_tokens,
        own_gain(late[:, :model], wide),
        own_gain(late[:, model + 2 * HEAD_SIZE :], wide),
        own_gain(late[:, model : model + HEAD_SIZE], narrow),
        own_gain(late[:, model + HEAD_SIZE : model + 2 * HEAD_SIZE], narrow),
        q_share,
        kv_share[:, :k_cols],
        kv_share[:, k_cols:],
        out_share.T,
        gate_share,
        up_share,
        down_share.T,
    )


def solution(mesh):
    split = ("shard", "ctx")
    rows, gain = P(split, None), P(split)
    into, out_of = P(split, "tensor"), P("tensor", split)
    in_specs = (rows, P("shard", None)) + (gain,) * 4 + (into,) * 3 + (out_of,)
    in_specs += (into, into, out_of, rows)
    out_specs = (rows, rows) + (gain,) * 4 + (into,) * 3 + (out_of, into, into, out_of)
    return jax.shard_map(body, mesh=mesh, in_specs=in_specs, out_specs=out_specs, check_vma=False)
```
